32 devices in a mesh: grp: 16 (over z, y, core), tp: 2 (over x).
Axes of the slice: x: 2, y: 2, z: 4, core: 2. Of those that a mesh axis runs over, the one named last changes fastest.
Arguments:
- tokens: float32 [8192, 1024], P(('grp', 'tp')), may hold values from -6 to 6
- cotangent: float32 [8192, 1024], P(('grp', 'tp')), may hold values from -6 to 6
- lengths: int32 [16, 4], P('grp'), may hold values from 1 to 384, as said below
- order: int32 [16, 4], P('grp'), may hold values from 0 to 3, each once within a row
- weights: float32 [3072, 64, 64], P(('tp', 'grp'))
- momentum: float32 [3072, 64, 64], P(('tp', 'grp')), may hold values from -1.75 to 1.75
- stat_left: float32 [3072, 64, 64], P(('tp', 'grp'))
- stat_right: float32 [3072, 64, 64], P(('tp', 'grp'))
- root_left: float32 [3072, 64, 64], P(('tp', 'grp'))
- root_right: float32 [3072, 64, 64], P(('tp', 'grp'))
- vec_params: float32 [12, 1024], replicated
- vec_momentum: float32 [12, 1024], replicated, may hold values from -3 to 3
- vec_second: float32 [12, 1024], replicated, may hold values from 0.1 to 0.5
Outputs:
- mixed: float32 [8192, 1024], P(('grp', 'tp'))
- input_grad: float32 [8192, 1024], P(('grp', 'tp'))
- weight_grads: float32 [3072, 64, 64], P(('tp', 'grp'))
- stat_left_new: float32 [3072, 64, 64], P(('tp', 'grp'))
- stat_right_new: float32 [3072, 64, 64], P(('tp', 'grp'))
- momentum_new: float32 [3072, 64, 64], P(('tp', 'grp'))
- weights_new: float32 [3072, 64, 64], P(('tp', 'grp'))
- vec_grads: float32 [12, 1024], replicated
- vec_second_new: float32 [12, 1024], replicated
- vec_momentum_new: float32 [12, 1024], replicated
- vec_new: float32 [12, 1024], replicated
The draws below stay inside these ranges and needn't reach their ends.
Inputs may be any that keep to these rules, and one draw needn't show every extreme that they name: `lengths`: packed in their order, each group's articles fill at most 512 positions, and one article of every group is longer than 256.
All inputs are finite; a program needn't handle non-finite values.
Results may differ from the reference program's by a relative error of at most 0.017.
Values may be sent and summed in bfloat16 or wider, within the bound.
A program may use at most 192 MiB of HBM per device.

```python
import math
import jax
import jax.numpy as jnp
from jax import lax

D = 1024
HEADS = 8
HD = 128
FF = 4096
TOK_DEV = 256
ARTS = 4
BLOCK = 64
GROUPS = 16
GROUP_ROWS = 512
TOKENS = 8192
SHORT_MOST = 42
QO = 24
OO = 8
IO = 32
CH = 96
NBLK = 3072
NV = 12
N_GRP = 16
N_TP = 2


OUT_GAIN = 6.0


def symmetric_blocks(key, low_end, high_end, off_scale):
    key_diagonal, key_off = jax.random.split(key)
    diagonal = jnp.exp(jax.random.uniform(key_diagonal, (NBLK, BLOCK), jnp.float32, math.log(low_end), math.log(high_end)))
    gauss_noise = jax.random.normal(key_off, (NBLK, BLOCK, BLOCK), jnp.float32)
    identity = jnp.eye(BLOCK, dtype=jnp.float32)
    paired = (gauss_noise + jnp.swapaxes(gauss_noise, 1, 2)) * (off_scale / math.sqrt(2.0 * BLOCK))
    return (paired * (1.0 - identity) + diagonal[:, :, None] * identity).astype(jnp.float32)


def draw_lengths(key, part):
    key = jax.random.fold_in(key, 11)
    key_short, key_span, key_pick, key_slot = jax.random.split(key, 4)
    longest = GROUP_ROWS - TOK_DEV // 2
    least = GROUP_ROWS - TOK_DEV + 1
    short_lengths = jax.random.randint(key_short, (GROUPS, ARTS), 1, SHORT_MOST + 1)
    long_lengths = jax.random.randint(key_span, (GROUPS, 1), least, longest + 1)
    chosen = jax.random.randint(key_pick, (), 0, GROUPS)
    long_lengths = jnp.where(jnp.arange(GROUPS)[:, None] == chosen, longest, long_lengths)
    slot_index = jax.random.randint(key_slot, (GROUPS, 1), 0, ARTS)
    return jnp.where(jnp.arange(ARTS)[None, :] == slot_index, long_lengths, short_lengths).astype(jnp.int32)


def draw_weights(key, part):
    key = jax.random.fold_in(key, 21)
    within = jnp.arange(NBLK) % CH
    drawn = D ** (-0.5)
    scales = jnp.where(within < QO, drawn, jnp.where(within < QO + OO, OUT_GAIN * drawn, jnp.where(within < QO + OO + IO, drawn, FF ** (-0.5))))
    return (jax.random.normal(key, (NBLK, BLOCK, BLOCK), jnp.float32) * scales[:, None, None]).astype(jnp.float32)


def draw_stat_left(key, part):
    key = jax.random.fold_in(key, 31)
    level = 0.1 / 0.9 * BLOCK * 0.25
    return symmetric_blocks(key, level, 4.0 * level, level)


def draw_stat_right(key, part):
    key = jax.random.fold_in(key, 32)
    level = 0.1 / 0.9 * BLOCK * 0.25
    return symmetric_blocks(key, level, 4.0 * level, level)


def draw_root_left(key, part):
    key = jax.random.fold_in(key, 33)
    return symmetric_blocks(key, 0.5, 2.0, 0.5)


def draw_root_right(key, part):
    key = jax.random.fold_in(key, 34)
    return symmetric_blocks(key, 0.5, 2.0, 0.5)


def draw_vec_params(key, part):
    key = jax.random.fold_in(key, 41)
    gauss_noise = jax.random.normal(key, (NV, D), jnp.float32)
    row_ids = jnp.arange(NV)[:, None]
    gains = (row_ids == 0) | (row_ids == 2)
    return jnp.where(gains, 1.0 + 0.15 * gauss_noise, 0.3 * gauss_noise).astype(jnp.float32)


def block_scale(key, extent, cuts, smallest, largest):
    level = 1.0
    for position, blocks in cuts:
        heights = jax.random.uniform(jax.random.fold_in(jax.random.fold_in(key, 6), position), (blocks,), jnp.float32, smallest / len(cuts), largest / len(cuts))
        level = level * jnp.repeat(jnp.exp(heights), extent[position] // blocks).reshape((-1,) + (1,) * (len(extent) - 1 - position))
    return level


def scatter_about(key, shape, deviation, reach, cuts=(), held_as=jnp.bfloat16):
    level = block_scale(key, shape, cuts, -0.22, 0.18) if cuts else 1.0
    drawn = jax.random.normal(key, shape, jnp.float32) * deviation * level
    return jnp.minimum(jnp.maximum(drawn, -reach), reach).astype(held_as)


def setup_inputs(seed: int = 0) -> dict:
    key_of = jax.random.split(jax.random.key(seed), 14)
    tokens = scatter_about(key_of[0], (TOKENS, D), 1.0, 6.0, ((0, 32),), jnp.float32)
    cotangent = scatter_about(key_of[1], (TOKENS, D), 1.0, 6.0, ((0, 32),), jnp.float32)
    lengths = draw_lengths(jax.random.fold_in(key_of[13], 71), 0)
    order = jax.vmap(lambda own: jax.random.permutation(own, ARTS))(jax.random.split(key_of[3], GROUPS)).reshape((GROUPS, ARTS)).astype(jnp.int32)
    weights = draw_weights(jax.random.fold_in(key_of[13], 71), 0)
    momentum = scatter_about(key_of[5], (NBLK, BLOCK, BLOCK), 0.3, 1.75, ((0, 32),), jnp.float32)
    stat_left = draw_stat_left(jax.random.fold_in(key_of[13], 71), 0)
    stat_right = draw_stat_right(jax.random.fold_in(key_of[13], 71), 0)
    root_left = draw_root_left(jax.random.fold_in(key_of[13], 71), 0)
    root_right = draw_root_right(jax.random.fold_in(key_of[13], 71), 0)
    vec_params = draw_vec_params(jax.random.fold_in(key_of[13], 71), 0)
    vec_momentum = scatter_about(key_of[11], (NV, D), 0.5, 3.0, (), jnp.float32)
    vec_second = jnp.clip(jnp.exp(jax.random.uniform(key_of[12], (NV, D), jnp.float32, math.log(0.1), math.log(0.5))), 0.1, 0.5)
    return dict(tokens=tokens, cotangent=cotangent, lengths=lengths, order=order, weights=weights, momentum=momentum, stat_left=stat_left, stat_right=stat_right, root_left=root_left, root_right=root_right, vec_params=vec_params, vec_momentum=vec_momentum, vec_second=vec_second)


EPS = 1e-05
NEG = -1e+30
DECAY = 0.9
BETA = 0.9
RATE = 0.05
VEC_DECAY = 0.9
VEC_RATE = 0.2
VEC_EPS = 1e-08

@jax.custom_vjp
def low(v):
    return lax.optimization_barrier(v.astype(jnp.bfloat16)).astype(jnp.float32)

@jax.custom_vjp
def low_back(v):
    return v

def low_keep(v):
    return (low(v), None)

def low_pass(kept, grad):
    return (grad,)

def back_keep(v):
    return (v, None)

def back_low(kept, grad):
    return (low(grad),)
low.defvjp(low_keep, low_pass)
low_back.defvjp(back_keep, back_low)

def matmul(left, right):
    return jnp.dot(left, right, precision=lax.Precision.HIGHEST, preferred_element_type=jnp.float32)

def layer_norm(value, gain, shift):
    average = lax.optimization_barrier(jnp.mean(value, -1, keepdims=True))
    centred = value - average
    spread = lax.optimization_barrier(jnp.mean(centred * centred, -1, keepdims=True))
    return centred * lax.rsqrt(spread + EPS) * gain + shift

def segment_ids(lengths_row, order_row):
    slots = jnp.arange(ARTS).astype(jnp.int32)
    picks = (order_row[:, None] == slots[None, :]).astype(jnp.int32)
    packed = lax.optimization_barrier(jnp.sum(picks * lengths_row[None, :], 1)).astype(jnp.int32)
    ends = jnp.cumsum(packed).astype(jnp.int32)
    spots = jnp.arange(GROUP_ROWS).astype(jnp.int32)
    return lax.optimization_barrier(jnp.sum((spots[:, None] >= ends[None, :]).astype(jnp.int32), 1)).astype(jnp.int32)

def allowed_mask(row_ids, row_segs, segments, key_ids):
    causal = key_ids[None, :] <= row_ids[:, None]
    same = segments[None, :] == row_segs[:, None]
    alone = (row_segs[:, None] < ARTS) | (key_ids[None, :] == row_ids[:, None])
    return causal & same & alone

def from_columns(tiles, row_total, col_total):
    return tiles.reshape(col_total // BLOCK, row_total // BLOCK, BLOCK, BLOCK).transpose(1, 2, 0, 3).reshape(row_total, col_total)

def from_rows(tiles, row_total, col_total):
    return tiles.reshape(row_total // BLOCK, col_total // BLOCK, BLOCK, BLOCK).transpose(0, 2, 1, 3).reshape(row_total, col_total)

def to_columns(matrix):
    row_total, col_total = matrix.shape
    return matrix.reshape(row_total // BLOCK, BLOCK, col_total // BLOCK, BLOCK).transpose(2, 0, 1, 3).reshape(-1, BLOCK, BLOCK)

def to_rows(matrix):
    row_total, col_total = matrix.shape
    return matrix.reshape(row_total // BLOCK, BLOCK, col_total // BLOCK, BLOCK).transpose(0, 2, 1, 3).reshape(-1, BLOCK, BLOCK)

def group_forward(inputs, w_qkv, w_out, w_in, w_down, vecs):
    rows_in, segments = inputs
    normed_one = low(layer_norm(rows_in, vecs[0], vecs[1]))
    qv_bias = vecs[6:8].reshape(HEADS, 2, HD)
    bias_qkv = jnp.stack([qv_bias[:, 0], jnp.zeros((HEADS, HD), jnp.float32), qv_bias[:, 1]], 1).reshape(3 * D)
    projected = low(low_back(matmul(normed_one, low(w_qkv)) + bias_qkv)).reshape(GROUP_ROWS, HEADS, 3, HD)
    queries = projected[:, :, 0]
    keys_all = projected[:, :, 1]
    values_all = projected[:, :, 2]
    span = min(512, GROUP_ROWS)
    key_ids = jnp.arange(GROUP_ROWS).astype(jnp.int32)

    def attend(first_row):
        row_ids = first_row + jnp.arange(span).astype(jnp.int32)
        row_segs = lax.dynamic_slice_in_dim(segments, first_row, span, 0)
        allowed = allowed_mask(row_ids, row_segs, segments, key_ids)
        query_rows = lax.dynamic_slice_in_dim(queries, first_row, span, 0)
        scores = low_back(jnp.einsum('qhd,khd->hqk', query_rows, keys_all, precision=lax.Precision.HIGHEST) * HD ** (-0.5))
        scores = jnp.where(allowed[None], scores, NEG)
        row_max = lax.optimization_barrier(jnp.max(scores, -1, keepdims=True))
        expo = jnp.exp(scores - row_max)
        probs = expo / lax.optimization_barrier(jnp.sum(expo, -1, keepdims=True))
        return jnp.einsum('hqk,khd->qhd', low(probs), values_all, precision=lax.Precision.HIGHEST)
    starts = (jnp.arange(GROUP_ROWS // span) * span).astype(jnp.int32)
    context = lax.map(jax.checkpoint(attend), starts).reshape(GROUP_ROWS, D)
    context = low(low_back(context))
    hidden = rows_in + low_back(matmul(context, low(w_out))) + vecs[4]
    normed_two = low(layer_norm(hidden, vecs[2], vecs[3]))
    inner = low_back(matmul(normed_two, low(w_in)) + vecs[8:].reshape(FF))
    activ = low(jax.nn.gelu(inner))
    return hidden + low_back(matmul(activ, low(w_down))) + vecs[5]

def reference(tokens, cotangent, lengths, order, weights, momentum, stat_left, stat_right, root_left, root_right, vec_params, vec_momentum, vec_second):
    owners = N_GRP * N_TP
    segments = jax.vmap(segment_ids)(lengths, order)
    per_owner = weights.reshape(owners, CH, BLOCK, BLOCK)
    marks = [0, QO, QO + OO, QO + OO + IO, CH]
    pieces = [per_owner[:, marks[index]:marks[index + 1]].reshape(-1, BLOCK, BLOCK) for index in range(4)]
    w_qkv = from_columns(pieces[0], D, 3 * D)
    w_out = from_rows(pieces[1], D, D)
    w_in = from_columns(pieces[2], D, FF)
    w_down = from_rows(pieces[3], FF, D)

    def forward(rows_in, wq, wo, wi, wd, vecs):
        grouped = rows_in.reshape(N_GRP, GROUP_ROWS, D)

        def one_group(inputs):
            return group_forward(inputs, wq, wo, wi, wd, vecs)
        return lax.map(jax.checkpoint(one_group), (grouped, segments)).reshape(TOKENS, D)
    mixed, pull = jax.vjp(forward, tokens, w_qkv, w_out, w_in, w_down, vec_params)
    input_grad, g_qkv, g_out, g_in, g_down, vec_grads = pull(cotangent)
    grad_parts = [to_columns(g_qkv), to_rows(g_out), to_columns(g_in), to_rows(g_down)]
    weight_grads = jnp.concatenate([part.reshape(owners, -1, BLOCK, BLOCK) for part in grad_parts], 1).reshape(NBLK, BLOCK, BLOCK)
    scaled = weight_grads * TOKENS ** (-0.5)
    stat_left_new = DECAY * stat_left + (1.0 - DECAY) * jnp.einsum('nij,nkj->nik', scaled, scaled, precision=lax.Precision.HIGHEST)
    stat_right_new = DECAY * stat_right + (1.0 - DECAY) * jnp.einsum('nji,njk->nik', scaled, scaled, precision=lax.Precision.HIGHEST)
    shaped = jnp.einsum('nij,njk->nik', root_left, scaled, precision=lax.Precision.HIGHEST)
    shaped = jnp.einsum('nij,njk->nik', shaped, root_right, precision=lax.Precision.HIGHEST)
    momentum_new = BETA * momentum + shaped
    weights_new = weights - RATE * momentum_new
    vec_scaled = vec_grads * TOKENS ** (-0.5)
    vec_second_new = VEC_DECAY * vec_second + (1.0 - VEC_DECAY) * vec_scaled * vec_scaled
    vec_momentum_new = BETA * vec_momentum + vec_scaled * lax.rsqrt(vec_second_new + VEC_EPS)
    vec_new = vec_params - VEC_RATE * vec_momentum_new
    return (mixed, input_grad, weight_grads, stat_left_new, stat_right_new, momentum_new, weights_new, vec_grads, vec_second_new, vec_momentum_new, vec_new)
```

```python
import functools

import jax
import jax.numpy as jnp
from jax import lax
from jax.experimental import pallas as pl
from jax.experimental.pallas import tpu as pltpu
from jax.sharding import PartitionSpec as P

D = 1024
HEADS = 8
HD = 128
FF = 4096
BLOCK = 64


EPS = 1e-05
NEG = -1e30
DECAY = 0.9
BETA = 0.9
RATE = 0.05
VEC_DECAY = 0.9
VEC_RATE = 0.2
VEC_EPS = 1e-08


def norm_rows(value, gain, shift):
    average = jnp.mean(value, -1, keepdims=True)
    centred = value - average
    inverse = lax.rsqrt(jnp.mean(centred * centred, -1, keepdims=True) + EPS)
    normed = centred * inverse
    return (normed * gain + shift, normed, inverse)


def norm_back(grad_out, normed, inverse, gain):
    scaled = grad_out * gain
    return inverse * (
        scaled
        - jnp.mean(scaled, -1, keepdims=True)
        - normed * jnp.mean(scaled * normed, -1, keepdims=True)
    )


def segment_ids(lengths_row, order_row, group_rows):
    article_count = lengths_row.shape[0]
    slots = jnp.arange(article_count, dtype=jnp.int32)
    picks = (order_row[:, None] == slots[None, :]).astype(jnp.int32)
    packed = jnp.sum(picks * lengths_row[None, :], 1)
    ends = jnp.cumsum(packed)
    spots = jnp.arange(group_rows, dtype=jnp.int32)
    return jnp.sum((spots[:, None] >= ends[None, :]).astype(jnp.int32), 1)


def allowed_mask(row_ids, row_segs, segments, key_ids, article_count):
    causal = key_ids[None, :] <= row_ids[:, None]
    same = segments[None, :] == row_segs[:, None]
    alone = (row_segs[:, None] < article_count) | (key_ids[None, :] == row_ids[:, None])
    return causal & same & alone


def from_columns(tiles, row_total, col_total):
    return (
        tiles.reshape(col_total // BLOCK, row_total // BLOCK, BLOCK, BLOCK)
        .transpose(1, 2, 0, 3)
        .reshape(row_total, col_total)
    )


def from_rows(tiles, row_total, col_total):
    return (
        tiles.reshape(row_total // BLOCK, col_total // BLOCK, BLOCK, BLOCK)
        .transpose(0, 2, 1, 3)
        .reshape(row_total, col_total)
    )


def to_columns(matrix):
    row_total, col_total = matrix.shape
    return (
        matrix.reshape(row_total // BLOCK, BLOCK, col_total // BLOCK, BLOCK)
        .transpose(2, 0, 1, 3)
        .reshape(-1, BLOCK, BLOCK)
    )


def to_rows(matrix):
    row_total, col_total = matrix.shape
    return (
        matrix.reshape(row_total // BLOCK, BLOCK, col_total // BLOCK, BLOCK)
        .transpose(0, 2, 1, 3)
        .reshape(-1, BLOCK, BLOCK)
    )


def per_device_general(
    tokens,
    cotangent,
    lengths,
    order,
    weights,
    momentum,
    stat_left,
    stat_right,
    root_left,
    root_right,
    vec_params,
    vec_momentum,
    vec_second,
):
    groups = lax.axis_size("grp")
    tp_size = lax.axis_size("tp")
    tp_rank = lax.axis_index("tp")
    tok_rows = tokens.shape[0]
    group_rows = tok_rows * tp_size
    article_count = lengths.shape[1]
    owners = groups * tp_size
    block_area = BLOCK * BLOCK * owners
    qkv_count = 3 * D * D // block_area
    out_count = D * D // block_area
    in_count = D * FF // block_area
    owned_blocks = weights.shape[0]
    heads_here = HEADS // tp_size
    qkv_cols = 3 * D // tp_size
    feat_here = D // tp_size
    ff_here = FF // tp_size
    qv_width = 2 * D // tp_size
    token_total = group_rows * groups
    gathered = lax.all_gather(weights.astype(jnp.bfloat16), "grp", axis=0, tiled=True)
    per_owner = gathered.reshape(groups, owned_blocks, BLOCK, BLOCK)
    marks = [0, qkv_count, qkv_count + out_count, qkv_count + out_count + in_count, owned_blocks]
    pieces = [
        per_owner[:, marks[index] : marks[index + 1]].reshape(-1, BLOCK, BLOCK)
        for index in range(4)
    ]
    w_qkv = from_columns(pieces[0], D, qkv_cols)
    w_out = from_rows(pieces[1], feat_here, D)
    w_in = from_columns(pieces[2], D, ff_here)
    w_down = from_rows(pieces[3], ff_here, D)
    w_qkv_heads = w_qkv.reshape(D, heads_here, 3, HD)
    w_out_heads = w_out.reshape(heads_here, HD, D)
    segments = segment_ids(lengths[0], order[0], group_rows)
    gain_one = vec_params[0]
    shift_one = vec_params[1]
    gain_two = vec_params[2]
    shift_two = vec_params[3]
    bias_out = vec_params[4]
    bias_down = vec_params[5]
    qv_here = lax.dynamic_slice_in_dim(
        vec_params[6:8].reshape(2 * D), tp_rank * qv_width, qv_width
    ).reshape(heads_here, 2, HD)
    bias_heads = jnp.stack(
        [qv_here[:, 0], jnp.zeros((heads_here, HD), jnp.float32), qv_here[:, 1]], 0
    )[:, :, None, :]
    bias_in = lax.dynamic_slice_in_dim(vec_params[8:].reshape(FF), tp_rank * ff_here, ff_here)
    normed_one, unit_one, inverse_one = norm_rows(tokens, gain_one, shift_one)
    rows_one = lax.all_gather(normed_one.astype(jnp.bfloat16), "tp", axis=0, tiled=True)
    projected = (
        jnp.einsum("rx,xhcd->chrd", rows_one, w_qkv_heads, preferred_element_type=jnp.float32)
        + bias_heads
    ).astype(jnp.bfloat16)
    queries = projected[0]
    keys_all = projected[1]
    values_all = projected[2]
    span = min(512, group_rows)
    starts = jnp.arange(group_rows // span, dtype=jnp.int32) * span
    key_ids = jnp.arange(group_rows, dtype=jnp.int32)
    score_scale = HD ** (-0.5)

    def masked_scores(first_row):
        row_ids = first_row + jnp.arange(span, dtype=jnp.int32)
        row_segs = lax.dynamic_slice_in_dim(segments, first_row, span, 0)
        allowed = allowed_mask(row_ids, row_segs, segments, key_ids, article_count)
        query_rows = lax.dynamic_slice_in_dim(queries, first_row, span, 1)
        scores = (
            jnp.einsum("hqd,hkd->hqk", query_rows, keys_all, preferred_element_type=jnp.float32)
            * score_scale
        )
        return (jnp.where(allowed[None], scores, NEG), query_rows)

    def attend(context_buf, first_row):
        scores, query_rows = masked_scores(first_row)
        row_max = jnp.max(scores, -1, keepdims=True)
        expo = jnp.exp(scores - row_max)
        expsum = jnp.sum(expo, -1, keepdims=True)
        probs_low = (expo / expsum).astype(jnp.bfloat16)
        context = jnp.einsum(
            "hqk,hkd->hqd", probs_low, values_all, preferred_element_type=jnp.float32
        ).astype(jnp.bfloat16)
        context_buf = lax.dynamic_update_slice_in_dim(context_buf, context, first_row, 1)
        return (context_buf, (row_max + jnp.log(expsum))[:, :, 0])

    context_low, log_norm = lax.scan(
        attend, jnp.zeros((heads_here, group_rows, HD), jnp.bfloat16), starts
    )
    attn_sum = lax.psum_scatter(
        jnp.einsum(
            "hrd,hde->re", context_low, w_out_heads, preferred_element_type=jnp.float32
        ).astype(jnp.bfloat16),
        "tp",
        scatter_dimension=0,
        tiled=True,
    ).astype(jnp.float32)
    hidden = tokens + attn_sum + bias_out
    normed_two, unit_two, inverse_two = norm_rows(hidden, gain_two, shift_two)
    rows_two = lax.all_gather(normed_two.astype(jnp.bfloat16), "tp", axis=0, tiled=True)
    inner = jnp.dot(rows_two, w_in, preferred_element_type=jnp.float32) + bias_in
    activ, gelu_pull = jax.vjp(jax.nn.gelu, inner)
    activ_low = activ.astype(jnp.bfloat16)
    mixed = (
        hidden
        + lax.psum_scatter(
            jnp.dot(activ_low, w_down, preferred_element_type=jnp.float32).astype(jnp.bfloat16),
            "tp",
            scatter_dimension=0,
            tiled=True,
        ).astype(jnp.float32)
        + bias_down
    )
    grad_low = cotangent.astype(jnp.bfloat16)
    grad_rows = lax.all_gather(grad_low, "tp", axis=0, tiled=True)
    g_down = jnp.einsum("rf,rd->fd", activ_low, grad_rows, preferred_element_type=jnp.float32)
    grad_activ = jnp.einsum("rd,fd->rf", grad_rows, w_down, preferred_element_type=jnp.float32)
    grad_inner = gelu_pull(grad_activ)[0].astype(jnp.bfloat16)
    g_in = jnp.einsum("rd,rf->df", rows_two, grad_inner, preferred_element_type=jnp.float32)
    g_bias_in = jnp.sum(grad_inner.astype(jnp.float32), 0)
    ffn_blocks = jnp.concatenate(
        [
            to_columns(g_in).reshape(groups, in_count, BLOCK, BLOCK),
            to_rows(g_down).reshape(groups, in_count, BLOCK, BLOCK),
        ],
        1,
    )
    grad_normed_two = lax.psum_scatter(
        jnp.einsum("rf,df->rd", grad_inner, w_in, preferred_element_type=jnp.float32).astype(
            jnp.bfloat16
        ),
        "tp",
        scatter_dimension=0,
        tiled=True,
    ).astype(jnp.float32)
    grad_hidden = cotangent + norm_back(grad_normed_two, unit_two, inverse_two, gain_two)
    grad_attn_low = grad_hidden.astype(jnp.bfloat16)
    grad_attn_rows = lax.all_gather(grad_attn_low, "tp", axis=0, tiled=True)
    g_out = jnp.einsum(
        "hrd,re->hde", context_low, grad_attn_rows, preferred_element_type=jnp.float32
    ).reshape(feat_here, D)
    grad_context = jnp.einsum(
        "re,hde->hrd", grad_attn_rows, w_out_heads, preferred_element_type=jnp.float32
    ).astype(jnp.bfloat16)
    zero_heads = jnp.zeros((heads_here, group_rows, HD), jnp.float32)

    def attend_back(carry, inputs):
        grad_queries, grad_keys, grad_values = carry
        first_row, log_block = inputs
        scores, query_rows = masked_scores(first_row)
        probs = jnp.exp(scores - log_block[:, :, None])
        grad_ctx_rows = lax.dynamic_slice_in_dim(grad_context, first_row, span, 1)
        grad_probs = jnp.einsum(
            "hqd,hkd->hqk", grad_ctx_rows, values_all, preferred_element_type=jnp.float32
        )
        delta = jnp.sum(probs * grad_probs, -1, keepdims=True)
        grad_scores = (probs * (grad_probs - delta)).astype(jnp.bfloat16)
        query_part = (
            jnp.einsum("hqk,hkd->hqd", grad_scores, keys_all, preferred_element_type=jnp.float32)
            * score_scale
        )
        grad_queries = lax.dynamic_update_slice_in_dim(grad_queries, query_part, first_row, 1)
        grad_keys = (
            grad_keys
            + jnp.einsum(
                "hqk,hqd->hkd", grad_scores, query_rows, preferred_element_type=jnp.float32
            )
            * score_scale
        )
        grad_values = grad_values + jnp.einsum(
            "hqk,hqd->hkd",
            probs.astype(jnp.bfloat16),
            grad_ctx_rows,
            preferred_element_type=jnp.float32,
        )
        return ((grad_queries, grad_keys, grad_values), None)

    (grad_queries, grad_keys, grad_values), unused = lax.scan(
        attend_back, (zero_heads, zero_heads, zero_heads), (starts, log_norm)
    )
    grad_proj = jnp.stack([grad_queries, grad_keys, grad_values], 0).astype(jnp.bfloat16)
    proj_sums = jnp.sum(grad_proj.astype(jnp.float32), 2)
    g_bias_qv = jnp.stack([proj_sums[0], proj_sums[2]], 1).reshape(qv_width)
    g_qkv = jnp.einsum(
        "rx,chrd->xhcd", rows_one, grad_proj, preferred_element_type=jnp.float32
    ).reshape(D, qkv_cols)
    grad_normed_one = lax.psum_scatter(
        jnp.einsum(
            "chrd,xhcd->rx", grad_proj, w_qkv_heads, preferred_element_type=jnp.float32
        ).astype(jnp.bfloat16),
        "tp",
        scatter_dimension=0,
        tiled=True,
    ).astype(jnp.float32)
    input_grad = grad_hidden + norm_back(grad_normed_one, unit_one, inverse_one, gain_one)
    local_rows = jnp.stack(
        [
            jnp.sum(grad_normed_one * unit_one, 0),
            jnp.sum(grad_normed_one, 0),
            jnp.sum(grad_normed_two * unit_two, 0),
            jnp.sum(grad_normed_two, 0),
            jnp.sum(grad_hidden, 0),
            jnp.sum(cotangent, 0),
        ]
    )
    qv_rows = lax.dynamic_update_slice(
        jnp.zeros((2 * D,), jnp.float32), g_bias_qv, (tp_rank * qv_width,)
    ).reshape(2, D)
    in_rows = lax.dynamic_update_slice(
        jnp.zeros((FF,), jnp.float32), g_bias_in, (tp_rank * ff_here,)
    ).reshape(FF // D, D)
    vec_grads = lax.psum(jnp.concatenate([local_rows, qv_rows, in_rows], 0), ("grp", "tp"))
    attn_blocks = jnp.concatenate(
        [
            to_columns(g_qkv).reshape(groups, qkv_count, BLOCK, BLOCK),
            to_rows(g_out).reshape(groups, out_count, BLOCK, BLOCK),
        ],
        1,
    )
    every_block = jnp.concatenate([attn_blocks, ffn_blocks], 1).reshape(-1, BLOCK, BLOCK)
    weight_grads = lax.psum_scatter(
        every_block.astype(jnp.bfloat16), "grp", scatter_dimension=0, tiled=True
    ).astype(jnp.float32)
    scaled = weight_grads * token_total ** (-0.5)
    stat_left_new = DECAY * stat_left + (1.0 - DECAY) * jnp.einsum(
        "nij,nkj->nik", scaled, scaled, precision=lax.Precision.HIGHEST
    )
    stat_right_new = DECAY * stat_right + (1.0 - DECAY) * jnp.einsum(
        "nji,njk->nik", scaled, scaled, precision=lax.Precision.HIGHEST
    )
    shaped = jnp.einsum("nij,njk->nik", root_left, scaled, precision=lax.Precision.HIGHEST)
    shaped = jnp.einsum("nij,njk->nik", shaped, root_right, precision=lax.Precision.HIGHEST)
    momentum_new = BETA * momentum + shaped
    weights_new = weights - RATE * momentum_new
    vec_scaled = vec_grads * token_total ** (-0.5)
    vec_second_new = VEC_DECAY * vec_second + (1.0 - VEC_DECAY) * vec_scaled * vec_scaled
    vec_momentum_new = BETA * vec_momentum + vec_scaled * lax.rsqrt(vec_second_new + VEC_EPS)
    vec_new = vec_params - VEC_RATE * vec_momentum_new
    return (
        mixed,
        input_grad,
        weight_grads,
        stat_left_new,
        stat_right_new,
        momentum_new,
        weights_new,
        vec_grads,
        vec_second_new,
        vec_momentum_new,
        vec_new,
    )


MESH_ID = pl.DeviceIdType.MESH
LANES = 128
HALF = 64
VMEM_LIMIT = 60 * 2**20


def remote(src, dst, send_sem, recv_sem, device):
    return pltpu.make_async_remote_copy(
        src_ref=src,
        dst_ref=dst,
        send_sem=send_sem,
        recv_sem=recv_sem,
        device_id=device,
        device_id_type=MESH_ID,
    )


def place():
    grp = lax.axis_index("grp")
    return lax.div(grp, 4), lax.rem(lax.div(grp, 2), 2), lax.rem(grp, 2), lax.axis_index("tp")


def slot_of(z, y, c):
    return z * 4 + y * 2 + c


def meet(devices):
    barrier = pltpu.get_barrier_semaphore()
    for device in devices:
        pl.semaphore_signal(barrier, inc=1, device_id=device, device_id_type=MESH_ID)
    pl.semaphore_wait(barrier, len(devices))


def lay_blocks(view_ref, stack):
    count = view_ref.shape[2]

    def row(i, carry):
        stack[pl.ds(i, count, stride=BLOCK), 0:HALF] = view_ref[i].T
        return carry

    lax.fori_loop(0, BLOCK, row, 0)


def gather_kernel(
    depth, view, out_q, out_o, out_i, out_d, stack, own_q, own_o, own_i, own_d, recv, send_z, send_y, send_c, local
):
    z, y, c, t = place()
    zs = [(lax.rem(z + step, depth)) for step in range(1, depth)]
    me = slot_of(z, y, c)
    y_peer = (slot_of(z, 1 - y, c), t)
    c_peer = (slot_of(z, y, 1 - c), t)
    z_peers = [(slot_of(zz, y, c), t) for zz in zs]
    meet([y_peer, c_peer] + z_peers)

    lay_blocks(view, stack)
    bf = jnp.bfloat16
    rows = own_q.shape[0]
    own_q[:, 0:HALF] = stack[0:rows, 0:HALF].astype(bf)
    own_q[:, HALF:LANES] = stack[rows : 2 * rows, 0:HALF].astype(bf)
    base = 2 * rows
    for b in range(8):
        own_o[:, b * HALF : (b + 1) * HALF] = stack[base + b * 64 : base + b * 64 + 64, 0:HALF].astype(bf)
    base += 512
    own_i[:, 0:HALF] = stack[base : base + 1024, 0:HALF].astype(bf)
    own_i[:, HALF:LANES] = stack[base + 1024 : base + 2048, 0:HALF].astype(bf)
    base += 2048
    for r in range(2):
        for b in range(16):
            at = base + (r * 16 + b) * 64
            own_d[r * 64 : r * 64 + 64, b * HALF : (b + 1) * HALF] = stack[at : at + 64, 0:HALF].astype(bf)

    outs = (out_q, out_o, out_i, out_d)
    owns = (own_q, own_o, own_i, own_d)
    started = []
    locals_ = []
    for k in range(4):
        own, out = owns[k], outs[k]
        for step in range(depth - 1):
            copy = remote(own, out.at[me], send_z.at[k, step], recv.at[k, me], z_peers[step])
            copy.start()
            started.append(copy)
        copy = remote(own, out.at[me], send_y.at[k, 0], recv.at[k, me], y_peer)
        copy.start()
        started.append(copy)
        copy = remote(own, out.at[me], send_c.at[k, 0], recv.at[k, me], c_peer)
        copy.start()
        started.append(copy)
        mine = pltpu.make_async_copy(own, out.at[me], local.at[k])
        mine.start()
        locals_.append(mine)

    def arrived(k, slot):
        remote(outs[k].at[slot], outs[k].at[slot], send_y.at[k, 0], recv.at[k, slot], y_peer).wait_recv()

    for k in range(4):
        out = outs[k]
        for step in range(depth):
            if step > 0:
                slot = slot_of(zs[step - 1], y, c)
                arrived(k, slot)
                copy = remote(out.at[slot], out.at[slot], send_y.at[k, step], recv.at[k, slot], y_peer)
                copy.start()
                started.append(copy)
                copy = remote(out.at[slot], out.at[slot], send_c.at[k, step], recv.at[k, slot], c_peer)
                copy.start()
                started.append(copy)
        for step in range(depth):
            slot = slot_of(z if step == 0 else zs[step - 1], 1 - y, c)
            arrived(k, slot)
            copy = remote(out.at[slot], out.at[slot], send_c.at[k, depth + step], recv.at[k, slot], c_peer)
            copy.start()
            started.append(copy)
    for k in range(4):
        for zz in range(depth):
            for yy in range(2):
                arrived(k, slot_of(zz, yy, 1 - c))
    for copy in started:
        copy.wait_send()
    for mine in locals_:
        mine.wait()


def piece_shapes():
    return ((768, LANES), (64, 512), (1024, LANES), (LANES, 1024))


def gather_weights(groups, weights):
    depth = groups // 4
    shapes = piece_shapes()
    bf = jnp.bfloat16
    view = jnp.transpose(weights, (1, 2, 0))
    return pl.pallas_call(
        functools.partial(gather_kernel, depth),
        out_shape=[jax.ShapeDtypeStruct((groups,) + s, bf) for s in shapes],
        in_specs=[pl.BlockSpec(memory_space=pltpu.VMEM)],
        out_specs=[pl.BlockSpec(memory_space=pl.ANY)] * 4,
        scratch_shapes=[pltpu.VMEM((weights.shape[0] * BLOCK, LANES), jnp.float32)]
        + [pltpu.VMEM(s, bf) for s in shapes]
        + [
            pltpu.SemaphoreType.DMA((4, groups)),
            pltpu.SemaphoreType.DMA((4, depth - 1)),
            pltpu.SemaphoreType.DMA((4, depth)),
            pltpu.SemaphoreType.DMA((4, 2 * depth)),
            pltpu.SemaphoreType.DMA((4,)),
        ],
        compiler_params=pltpu.CompilerParams(
            collective_id=0, has_side_effects=True, vmem_limit_bytes=VMEM_LIMIT
        ),
        name="gather_weights",
    )(view)


def scatter_kernel(depth, *refs):
    parts, sums = refs[0:4], refs[4:8]
    core_in, y_out, y_in, held, z_out, z_in = (refs[8 + 4 * k : 12 + 4 * k] for k in range(6))
    recv_c, recv_y, recv_z, send_c, send_y, send_z = refs[32:38]
    z, y, c, t = place()
    zs = [z] + [lax.rem(z + step, depth) for step in range(1, depth)]
    y_peer = (slot_of(z, 1 - y, c), t)
    c_peer = (slot_of(z, y, 1 - c), t)
    meet([y_peer, c_peer] + [(slot_of(zz, y, c), t) for zz in zs[1:]])
    started = []

    def go(copy):
        copy.start()
        started.append(copy)

    def add(dst, first, second):
        rows = dst.shape[0]
        step = min(rows, 256 * LANES // dst.shape[1])

        def body(i, carry):
            at = pl.ds(pl.multiple_of(i * step, 16), step)
            total = first[at, :].astype(jnp.float32) + second[at, :].astype(jnp.float32)
            dst[at, :] = total.astype(dst.dtype)
            return carry

        lax.fori_loop(0, rows // step, body, 0)

    order = (2, 3, 1, 0)
    for k in order:
        for far in (1, 0):
            for step in range(depth):
                yy = 1 - y if far else y
                src = parts[k].at[slot_of(zs[step], yy, 1 - c)]
                place_in = zs[step] * 2 + yy
                go(remote(src, core_in[k].at[place_in], send_c.at[k, far * depth + step], recv_c.at[k, place_in], c_peer))
    for k in order:
        for far in (1, 0):
            for step in range(depth):
                yy = 1 - y if far else y
                place_in = zs[step] * 2 + yy
                landed = core_in[k].at[place_in]
                remote(landed, landed, send_c.at[k, 0], recv_c.at[k, place_in], c_peer).wait_recv()
                own = parts[k].at[slot_of(zs[step], yy, c)]
                if far:
                    add(y_out[k].at[step], own, landed)
                    go(remote(y_out[k].at[step], y_in[k].at[step], send_y.at[k, step], recv_y.at[k, step], y_peer))
                else:
                    add(held[k].at[step], own, landed)
    for k in order:
        for step in list(range(1, depth)) + [0]:
            landed = y_in[k].at[step]
            remote(landed, landed, send_y.at[k, 0], recv_y.at[k, step], y_peer).wait_recv()
            if step:
                add(z_out[k].at[step - 1], held[k].at[step], landed)
                go(
                    remote(
                        z_out[k].at[step - 1],
                        z_in[k].at[depth - 1 - step],
                        send_z.at[k, step - 1],
                        recv_z.at[k, depth - 1 - step],
                        (slot_of(zs[step], y, c), t),
                    )
                )
            else:
                add(sums[k], held[k].at[step], landed)
    for k in order:
        for step in range(depth - 1):
            landed = z_in[k].at[step]
            remote(landed, landed, send_z.at[k, 0], recv_z.at[k, step], y_peer).wait_recv()
            add(sums[k], sums[k], landed)
    for copy in started:
        copy.wait_send()


def scatter_grads(groups, parts):
    depth = groups // 4
    shapes = piece_shapes()
    bf = jnp.bfloat16

    def many(count):
        return [pltpu.VMEM((count,) + s, bf) for s in shapes]

    return pl.pallas_call(
        functools.partial(scatter_kernel, depth),
        out_shape=[jax.ShapeDtypeStruct(s, jnp.float32) for s in shapes],
        in_specs=[pl.BlockSpec(memory_space=pltpu.VMEM)] * 4,
        out_specs=[pl.BlockSpec(memory_space=pltpu.VMEM)] * 4,
        scratch_shapes=many(2 * depth)
        + many(depth)
        + many(depth)
        + many(depth)
        + many(depth - 1)
        + many(depth - 1)
        + [
            pltpu.SemaphoreType.DMA((4, 2 * depth)),
            pltpu.SemaphoreType.DMA((4, depth)),
            pltpu.SemaphoreType.DMA((4, depth - 1)),
            pltpu.SemaphoreType.DMA((4, 2 * depth)),
            pltpu.SemaphoreType.DMA((4, depth)),
            pltpu.SemaphoreType.DMA((4, depth - 1)),
        ],
        compiler_params=pltpu.CompilerParams(
            collective_id=1, has_side_effects=True, vmem_limit_bytes=VMEM_LIMIT
        ),
        name="scatter_grads",
    )(*parts)


def fold_tiles(value, mask):
    kept = jnp.where(mask, value, 0.0)
    halves = kept[:, :LANES] + kept[:, LANES:]
    return halves + pltpu.roll(halves, HALF, 1)


def update_kernel(
    scale, sum_q, sum_o, sum_i, sum_d, root_l, root_r, w, m, sl, sr, out_g, out_sl, out_sr, out_m, out_w, first, second
):
    count = root_l.shape[2]
    bf = jnp.bfloat16

    @pl.when(pl.program_id(0) == 0)
    def _():
        rows = sum_q.shape[0]
        first[0:rows, 0:HALF] = sum_q[:, 0:HALF]
        first[rows : 2 * rows, 0:HALF] = sum_q[:, HALF:LANES]
        base = 2 * rows
        for b in range(8):
            first[base + b * 64 : base + b * 64 + 64, 0:HALF] = sum_o[:, b * HALF : (b + 1) * HALF]
        base += 512
        first[base : base + 1024, 0:HALF] = sum_i[:, 0:HALF]
        first[base + 1024 : base + 2048, 0:HALF] = sum_i[:, HALF:LANES]
        base += 2048
        for r in range(2):
            for b in range(16):
                at = base + (r * 16 + b) * 64
                first[at : at + 64, 0:HALF] = sum_d[r * 64 : r * 64 + 64, b * HALF : (b + 1) * HALF]

        def row(i, carry):
            both = jnp.concatenate([root_l[i], root_r[i]], 0)
            second[pl.ds(i, count, stride=BLOCK), :] = both.T
            return carry

        lax.fori_loop(0, BLOCK, row, 0)
        row_id = lax.broadcasted_iota(jnp.int32, (256, 256), 0)
        col_id = lax.broadcasted_iota(jnp.int32, (256, 256), 1)
        mask = lax.shift_right_logical(row_id, 6) == lax.shift_right_logical(col_id, 6)
        zero = jnp.zeros((256, 256), jnp.float32)

        def spread(v):
            return jnp.where(mask, jnp.concatenate([v, v, v, v], 1), zero).astype(bf)

        def four(k, carry):
            at = pl.ds(pl.multiple_of(k * 256, 256), 256)
            s32 = first[at, 0:HALF] * scale
            s = s32.astype(bf)
            left = second[at, 0:HALF]
            right = second[at, HALF:LANES].astype(bf)
            outer = lax.dot_general(s, s, (((1,), (1,)), ((), ())), preferred_element_type=jnp.float32)
            inner = lax.dot_general(spread(s32), s, (((0,), (0,)), ((), ())), preferred_element_type=jnp.float32)
            shaped = jnp.dot(spread(left), s, preferred_element_type=jnp.float32)
            shaped = jnp.dot(spread(shaped), right, preferred_element_type=jnp.float32)
            first[at, HALF:LANES] = fold_tiles(outer, mask)[:, HALF:LANES]
            second[at, 0:HALF] = inner
            second[at, HALF:LANES] = shaped
            return carry

        lax.fori_loop(0, count // 4, four, 0)

    i0 = pl.program_id(0) * w.shape[0]

    def rows_out(ii, carry):
        at = pl.ds(i0 + ii, count, stride=BLOCK)
        one = first[at, :].T
        two = second[at, :].T
        out_g[ii] = one[0:HALF]
        out_sl[ii] = DECAY * sl[ii] + (1.0 - DECAY) * one[HALF:LANES]
        out_sr[ii] = DECAY * sr[ii] + (1.0 - DECAY) * two[0:HALF]
        fresh = BETA * m[ii] + two[HALF:LANES]
        out_m[ii] = fresh
        out_w[ii] = w[ii] - RATE * fresh
        return carry

    lax.fori_loop(0, w.shape[0], rows_out, 0)


def update_blocks(sums, weights, momentum, stat_left, stat_right, root_left, root_right, token_total):
    def view(a):
        return jnp.transpose(a, (1, 2, 0))

    count = weights.shape[0]
    rows = 8
    whole = pl.BlockSpec(memory_space=pltpu.VMEM)
    part = pl.BlockSpec((rows, BLOCK, count), lambda i: (i, 0, 0))
    outs = pl.pallas_call(
        functools.partial(update_kernel, token_total ** (-0.5)),
        grid=(BLOCK // rows,),
        out_shape=[jax.ShapeDtypeStruct((BLOCK, BLOCK, count), jnp.float32)] * 5,
        in_specs=[whole] * 6 + [part] * 4,
        out_specs=[part] * 5,
        scratch_shapes=[
            pltpu.VMEM((count * BLOCK, LANES), jnp.float32),
            pltpu.VMEM((count * BLOCK, LANES), jnp.float32),
        ],
        compiler_params=pltpu.CompilerParams(vmem_limit_bytes=VMEM_LIMIT),
        name="update_blocks",
    )(*sums, view(root_left), view(root_right), view(weights), view(momentum), view(stat_left), view(stat_right))
    return [jnp.transpose(a, (2, 0, 1)) for a in outs]


def per_device(
    grp_count,
    tp_count,
    tokens,
    cotangent,
    lengths,
    order,
    weights,
    momentum,
    stat_left,
    stat_right,
    root_left,
    root_right,
    vec_params,
    vec_momentum,
    vec_second,
):
    if tp_count != 2 or grp_count % 4 or weights.shape[0] != 96:
        return per_device_general(
            tokens,
            cotangent,
            lengths,
            order,
            weights,
            momentum,
            stat_left,
            stat_right,
            root_left,
            root_right,
            vec_params,
            vec_momentum,
            vec_second,
        )
    groups = grp_count
    tp_size = lax.axis_size("tp")
    tp_rank = lax.axis_index("tp")
    tok_rows = tokens.shape[0]
    group_rows = tok_rows * tp_size
    article_count = lengths.shape[1]
    owners = groups * tp_size
    block_area = BLOCK * BLOCK * owners
    qkv_count = 3 * D * D // block_area
    out_count = D * D // block_area
    in_count = D * FF // block_area
    owned_blocks = weights.shape[0]
    heads_here = HEADS // tp_size
    qkv_cols = 3 * D // tp_size
    feat_here = D // tp_size
    ff_here = FF // tp_size
    qv_width = 2 * D // tp_size
    token_total = group_rows * groups
    got_q, got_o, got_i, got_d = gather_weights(groups, weights)
    tiles_q = jnp.concatenate(
        [
            got_q[:, :, :HALF].reshape(groups, 12, BLOCK, BLOCK),
            got_q[:, :, HALF:].reshape(groups, 12, BLOCK, BLOCK),
        ],
        1,
    ).reshape(-1, BLOCK, BLOCK)
    w_qkv = from_columns(tiles_q, D, qkv_cols)
    w_out = got_o.reshape(groups // 2, 2, BLOCK, 512).transpose(0, 2, 1, 3).reshape(feat_here, D)
    w_in = got_i.transpose(1, 0, 2).reshape(D, ff_here)
    w_down = got_d.reshape(ff_here, D)
    w_qkv_heads = w_qkv.reshape(D, heads_here, 3, HD)
    w_out_heads = w_out.reshape(heads_here, HD, D)
    segments = segment_ids(lengths[0], order[0], group_rows)
    gain_one = vec_params[0]
    shift_one = vec_params[1]
    gain_two = vec_params[2]
    shift_two = vec_params[3]
    bias_out = vec_params[4]
    bias_down = vec_params[5]
    qv_here = lax.dynamic_slice_in_dim(
        vec_params[6:8].reshape(2 * D), tp_rank * qv_width, qv_width
    ).reshape(heads_here, 2, HD)
    bias_heads = jnp.stack(
        [qv_here[:, 0], jnp.zeros((heads_here, HD), jnp.float32), qv_here[:, 1]], 0
    )[:, :, None, :]
    bias_in = lax.dynamic_slice_in_dim(vec_params[8:].reshape(FF), tp_rank * ff_here, ff_here)
    normed_one, unit_one, inverse_one = norm_rows(tokens, gain_one, shift_one)
    rows_one = lax.all_gather(normed_one.astype(jnp.bfloat16), "tp", axis=0, tiled=True)
    projected = (
        jnp.einsum("rx,xhcd->chrd", rows_one, w_qkv_heads, preferred_element_type=jnp.float32)
        + bias_heads
    ).astype(jnp.bfloat16)
    queries = projected[0]
    keys_all = projected[1]
    values_all = projected[2]
    span = min(512, group_rows)
    starts = jnp.arange(group_rows // span, dtype=jnp.int32) * span
    key_ids = jnp.arange(group_rows, dtype=jnp.int32)
    score_scale = HD ** (-0.5)

    def masked_scores(first_row):
        row_ids = first_row + jnp.arange(span, dtype=jnp.int32)
        row_segs = lax.dynamic_slice_in_dim(segments, first_row, span, 0)
        allowed = allowed_mask(row_ids, row_segs, segments, key_ids, article_count)
        query_rows = lax.dynamic_slice_in_dim(queries, first_row, span, 1)
        scores = (
            jnp.einsum("hqd,hkd->hqk", query_rows, keys_all, preferred_element_type=jnp.float32)
            * score_scale
        )
        return (jnp.where(allowed[None], scores, NEG), query_rows)

    def attend(context_buf, first_row):
        scores, query_rows = masked_scores(first_row)
        row_max = jnp.max(scores, -1, keepdims=True)
        expo = jnp.exp(scores - row_max)
        expsum = jnp.sum(expo, -1, keepdims=True)
        probs_low = (expo / expsum).astype(jnp.bfloat16)
        context = jnp.einsum(
            "hqk,hkd->hqd", probs_low, values_all, preferred_element_type=jnp.float32
        ).astype(jnp.bfloat16)
        context_buf = lax.dynamic_update_slice_in_dim(context_buf, context, first_row, 1)
        return (context_buf, (row_max + jnp.log(expsum))[:, :, 0])

    context_low, log_norm = lax.scan(
        attend, jnp.zeros((heads_here, group_rows, HD), jnp.bfloat16), starts
    )
    attn_sum = lax.psum_scatter(
        jnp.einsum(
            "hrd,hde->re", context_low, w_out_heads, preferred_element_type=jnp.float32
        ).astype(jnp.bfloat16),
        "tp",
        scatter_dimension=0,
        tiled=True,
    ).astype(jnp.float32)
    hidden = tokens + attn_sum + bias_out
    normed_two, unit_two, inverse_two = norm_rows(hidden, gain_two, shift_two)
    rows_two = lax.all_gather(normed_two.astype(jnp.bfloat16), "tp", axis=0, tiled=True)
    inner = jnp.dot(rows_two, w_in, preferred_element_type=jnp.float32) + bias_in
    activ, gelu_pull = jax.vjp(jax.nn.gelu, inner)
    activ_low = activ.astype(jnp.bfloat16)
    mixed = (
        hidden
        + lax.psum_scatter(
            jnp.dot(activ_low, w_down, preferred_element_type=jnp.float32).astype(jnp.bfloat16),
            "tp",
            scatter_dimension=0,
            tiled=True,
        ).astype(jnp.float32)
        + bias_down
    )
    grad_low = cotangent.astype(jnp.bfloat16)
    grad_rows = lax.all_gather(grad_low, "tp", axis=0, tiled=True)
    g_down = jnp.einsum("rf,rd->fd", activ_low, grad_rows, preferred_element_type=jnp.float32)
    grad_activ = jnp.einsum("rd,fd->rf", grad_rows, w_down, preferred_element_type=jnp.float32)
    grad_inner = gelu_pull(grad_activ)[0].astype(jnp.bfloat16)
    g_in = jnp.einsum("rd,rf->df", rows_two, grad_inner, preferred_element_type=jnp.float32)
    g_bias_in = jnp.sum(grad_inner.astype(jnp.float32), 0)
    grad_normed_two = lax.psum_scatter(
        jnp.einsum("rf,df->rd", grad_inner, w_in, preferred_element_type=jnp.float32).astype(
            jnp.bfloat16
        ),
        "tp",
        scatter_dimension=0,
        tiled=True,
    ).astype(jnp.float32)
    grad_hidden = cotangent + norm_back(grad_normed_two, unit_two, inverse_two, gain_two)
    grad_attn_low = grad_hidden.astype(jnp.bfloat16)
    grad_attn_rows = lax.all_gather(grad_attn_low, "tp", axis=0, tiled=True)
    g_out = jnp.einsum(
        "hrd,re->hde", context_low, grad_attn_rows, preferred_element_type=jnp.float32
    ).reshape(feat_here, D)
    grad_context = jnp.einsum(
        "re,hde->hrd", grad_attn_rows, w_out_heads, preferred_element_type=jnp.float32
    ).astype(jnp.bfloat16)
    zero_heads = jnp.zeros((heads_here, group_rows, HD), jnp.float32)

    def attend_back(carry, inputs):
        grad_queries, grad_keys, grad_values = carry
        first_row, log_block = inputs
        scores, query_rows = masked_scores(first_row)
        probs = jnp.exp(scores - log_block[:, :, None])
        grad_ctx_rows = lax.dynamic_slice_in_dim(grad_context, first_row, span, 1)
        grad_probs = jnp.einsum(
            "hqd,hkd->hqk", grad_ctx_rows, values_all, preferred_element_type=jnp.float32
        )
        delta = jnp.sum(probs * grad_probs, -1, keepdims=True)
        grad_scores = (probs * (grad_probs - delta)).astype(jnp.bfloat16)
        query_part = (
            jnp.einsum("hqk,hkd->hqd", grad_scores, keys_all, preferred_element_type=jnp.float32)
            * score_scale
        )
        grad_queries = lax.dynamic_update_slice_in_dim(grad_queries, query_part, first_row, 1)
        grad_keys = (
            grad_keys
            + jnp.einsum(
                "hqk,hqd->hkd", grad_scores, query_rows, preferred_element_type=jnp.float32
            )
            * score_scale
        )
        grad_values = grad_values + jnp.einsum(
            "hqk,hqd->hkd",
            probs.astype(jnp.bfloat16),
            grad_ctx_rows,
            preferred_element_type=jnp.float32,
        )
        return ((grad_queries, grad_keys, grad_values), None)

    (grad_queries, grad_keys, grad_values), unused = lax.scan(
        attend_back, (zero_heads, zero_heads, zero_heads), (starts, log_norm)
    )
    grad_proj = jnp.stack([grad_queries, grad_keys, grad_values], 0).astype(jnp.bfloat16)
    proj_sums = jnp.sum(grad_proj.astype(jnp.float32), 2)
    g_bias_qv = jnp.stack([proj_sums[0], proj_sums[2]], 1).reshape(qv_width)
    g_qkv = jnp.einsum(
        "rx,chrd->xhcd", rows_one, grad_proj, preferred_element_type=jnp.float32
    ).reshape(D, qkv_cols)
    grad_normed_one = lax.psum_scatter(
        jnp.einsum(
            "chrd,xhcd->rx", grad_proj, w_qkv_heads, preferred_element_type=jnp.float32
        ).astype(jnp.bfloat16),
        "tp",
        scatter_dimension=0,
        tiled=True,
    ).astype(jnp.float32)
    input_grad = grad_hidden + norm_back(grad_normed_one, unit_one, inverse_one, gain_one)
    local_rows = jnp.stack(
        [
            jnp.sum(grad_normed_one * unit_one, 0),
            jnp.sum(grad_normed_one, 0),
            jnp.sum(grad_normed_two * unit_two, 0),
            jnp.sum(grad_normed_two, 0),
            jnp.sum(grad_hidden, 0),
            jnp.sum(cotangent, 0),
        ]
    )
    qv_rows = lax.dynamic_update_slice(
        jnp.zeros((2 * D,), jnp.float32), g_bias_qv, (tp_rank * qv_width,)
    ).reshape(2, D)
    in_rows = lax.dynamic_update_slice(
        jnp.zeros((FF,), jnp.float32), g_bias_in, (tp_rank * ff_here,)
    ).reshape(FF // D, D)
    vec_grads = lax.psum(jnp.concatenate([local_rows, qv_rows, in_rows], 0), ("grp", "tp"))
    bf = jnp.bfloat16
    tiles_q = to_columns(g_qkv.astype(bf)).reshape(groups, 2, 12 * BLOCK, BLOCK)
    part_q = jnp.concatenate([tiles_q[:, 0], tiles_q[:, 1]], 2)
    part_o = g_out.astype(bf).reshape(groups // 2, BLOCK, 2, 512).transpose(0, 2, 1, 3).reshape(groups, BLOCK, 512)
    part_i = g_in.astype(bf).reshape(D, groups, LANES).transpose(1, 0, 2)
    part_d = g_down.astype(bf).reshape(groups, LANES, D)
    sums = scatter_grads(groups, (part_q, part_o, part_i, part_d))
    weight_grads, stat_left_new, stat_right_new, momentum_new, weights_new = update_blocks(
        sums, weights, momentum, stat_left, stat_right, root_left, root_right, token_total
    )
    vec_scaled = vec_grads * token_total ** (-0.5)
    vec_second_new = VEC_DECAY * vec_second + (1.0 - VEC_DECAY) * vec_scaled * vec_scaled
    vec_momentum_new = BETA * vec_momentum + vec_scaled * lax.rsqrt(vec_second_new + VEC_EPS)
    vec_new = vec_params - VEC_RATE * vec_momentum_new
    return (
        mixed,
        input_grad,
        weight_grads,
        stat_left_new,
        stat_right_new,
        momentum_new,
        weights_new,
        vec_grads,
        vec_second_new,
        vec_momentum_new,
        vec_new,
    )


def solution(mesh):
    placed = (
        P(("grp", "tp"), None),
        P(("grp", "tp"), None),
        P("grp", None),
        P("grp", None),
        P(("tp", "grp"), None, None),
        P(("tp", "grp"), None, None),
        P(("tp", "grp"), None, None),
        P(("tp", "grp"), None, None),
        P(("tp", "grp"), None, None),
        P(("tp", "grp"), None, None),
        P(),
        P(),
        P(),
    )
    return jax.shard_map(
        functools.partial(per_device, mesh.shape["grp"], mesh.shape["tp"]),
        mesh=mesh,
        in_specs=placed,
        out_specs=(
            P(("grp", "tp"), None),
            P(("grp", "tp"), None),
            P(("tp", "grp"), None, None),
            P(("tp", "grp"), None, None),
            P(("tp", "grp"), None, None),
            P(("tp", "grp"), None, None),
            P(("tp", "grp"), None, None),
            P(),
            P(),
            P(),
            P(),
        ),
        check_vma=False,
    )
```

```python
import functools

import jax
import jax.numpy as jnp
from jax import lax
from jax.experimental import pallas as pl
from jax.experimental.pallas import tpu as pltpu
from jax.sharding import PartitionSpec as P

D = 1024
HEADS = 8
HD = 128
FF = 4096
BLOCK = 64


EPS = 1e-05
NEG = -1e30
DECAY = 0.9
BETA = 0.9
RATE = 0.05
VEC_DECAY = 0.9
VEC_RATE = 0.2
VEC_EPS = 1e-08


def norm_rows(value, gain, shift):
    average = jnp.mean(value, -1, keepdims=True)
    centred = value - average
    inverse = lax.rsqrt(jnp.mean(centred * centred, -1, keepdims=True) + EPS)
    normed = centred * inverse
    return (normed * gain + shift, normed, inverse)


def norm_back(grad_out, normed, inverse, gain):
    scaled = grad_out * gain
    return inverse * (
        scaled
        - jnp.mean(scaled, -1, keepdims=True)
        - normed * jnp.mean(scaled * normed, -1, keepdims=True)
    )


def segment_ids(lengths_row, order_row, group_rows):
    article_count = lengths_row.shape[0]
    slots = jnp.arange(article_count, dtype=jnp.int32)
    picks = (order_row[:, None] == slots[None, :]).astype(jnp.int32)
    packed = jnp.sum(picks * lengths_row[None, :], 1)
    ends = jnp.cumsum(packed)
    spots = jnp.arange(group_rows, dtype=jnp.int32)
    return jnp.sum((spots[:, None] >= ends[None, :]).astype(jnp.int32), 1)


def allowed_mask(row_ids, row_segs, segments, key_ids, article_count):
    causal = key_ids[None, :] <= row_ids[:, None]
    same = segments[None, :] == row_segs[:, None]
    alone = (row_segs[:, None] < article_count) | (key_ids[None, :] == row_ids[:, None])
    return causal & same & alone


def from_columns(tiles, row_total, col_total):
    return (
        tiles.reshape(col_total // BLOCK, row_total // BLOCK, BLOCK, BLOCK)
        .transpose(1, 2, 0, 3)
        .reshape(row_total, col_total)
    )


def from_rows(tiles, row_total, col_total):
    return (
        tiles.reshape(row_total // BLOCK, col_total // BLOCK, BLOCK, BLOCK)
        .transpose(0, 2, 1, 3)
        .reshape(row_total, col_total)
    )


def to_columns(matrix):
    row_total, col_total = matrix.shape
    return (
        matrix.reshape(row_total // BLOCK, BLOCK, col_total // BLOCK, BLOCK)
        .transpose(2, 0, 1, 3)
        .reshape(-1, BLOCK, BLOCK)
    )


def to_rows(matrix):
    row_total, col_total = matrix.shape
    return (
        matrix.reshape(row_total // BLOCK, BLOCK, col_total // BLOCK, BLOCK)
        .transpose(0, 2, 1, 3)
        .reshape(-1, BLOCK, BLOCK)
    )


def per_device_general(
    tokens,
    cotangent,
    lengths,
    order,
    weights,
    momentum,
    stat_left,
    stat_right,
    root_left,
    root_right,
    vec_params,
    vec_momentum,
    vec_second,
):
    groups = lax.axis_size("grp")
    tp_size = lax.axis_size("tp")
    tp_rank = lax.axis_index("tp")
    tok_rows = tokens.shape[0]
    group_rows = tok_rows * tp_size
    article_count = lengths.shape[1]
    owners = groups * tp_size
    block_area = BLOCK * BLOCK * owners
    qkv_count = 3 * D * D // block_area
    out_count = D * D // block_area
    in_count = D * FF // block_area
    owned_blocks = weights.shape[0]
    heads_here = HEADS // tp_size
    qkv_cols = 3 * D // tp_size
    feat_here = D // tp_size
    ff_here = FF // tp_size
    qv_width = 2 * D // tp_size
    token_total = group_rows * groups
    gathered = lax.all_gather(weights.astype(jnp.bfloat16), "grp", axis=0, tiled=True)
    per_owner = gathered.reshape(groups, owned_blocks, BLOCK, BLOCK)
    marks = [0, qkv_count, qkv_count + out_count, qkv_count + out_count + in_count, owned_blocks]
    pieces = [
        per_owner[:, marks[index] : marks[index + 1]].reshape(-1, BLOCK, BLOCK)
        for index in range(4)
    ]
    w_qkv = from_columns(pieces[0], D, qkv_cols)
    w_out = from_rows(pieces[1], feat_here, D)
    w_in = from_columns(pieces[2], D, ff_here)
    w_down = from_rows(pieces[3], ff_here, D)
    w_qkv_heads = w_qkv.reshape(D, heads_here, 3, HD)
    w_out_heads = w_out.reshape(heads_here, HD, D)
    segments = segment_ids(lengths[0], order[0], group_rows)
    gain_one = vec_params[0]
    shift_one = vec_params[1]
    gain_two = vec_params[2]
    shift_two = vec_params[3]
    bias_out = vec_params[4]
    bias_down = vec_params[5]
    qv_here = lax.dynamic_slice_in_dim(
        vec_params[6:8].reshape(2 * D), tp_rank * qv_width, qv_width
    ).reshape(heads_here, 2, HD)
    bias_heads = jnp.stack(
        [qv_here[:, 0], jnp.zeros((heads_here, HD), jnp.float32), qv_here[:, 1]], 0
    )[:, :, None, :]
    bias_in = lax.dynamic_slice_in_dim(vec_params[8:].reshape(FF), tp_rank * ff_here, ff_here)
    normed_one, unit_one, inverse_one = norm_rows(tokens, gain_one, shift_one)
    rows_one = lax.all_gather(normed_one.astype(jnp.bfloat16), "tp", axis=0, tiled=True)
    projected = (
        jnp.einsum("rx,xhcd->chrd", rows_one, w_qkv_heads, preferred_element_type=jnp.float32)
        + bias_heads
    ).astype(jnp.bfloat16)
    queries = projected[0]
    keys_all = projected[1]
    values_all = projected[2]
    span = min(512, group_rows)
    starts = jnp.arange(group_rows // span, dtype=jnp.int32) * span
    key_ids = jnp.arange(group_rows, dtype=jnp.int32)
    score_scale = HD ** (-0.5)

    def masked_scores(first_row):
        row_ids = first_row + jnp.arange(span, dtype=jnp.int32)
        row_segs = lax.dynamic_slice_in_dim(segments, first_row, span, 0)
        allowed = allowed_mask(row_ids, row_segs, segments, key_ids, article_count)
        query_rows = lax.dynamic_slice_in_dim(queries, first_row, span, 1)
        scores = (
            jnp.einsum("hqd,hkd->hqk", query_rows, keys_all, preferred_element_type=jnp.float32)
            * score_scale
        )
        return (jnp.where(allowed[None], scores, NEG), query_rows)

    def attend(context_buf, first_row):
        scores, query_rows = masked_scores(first_row)
        row_max = jnp.max(scores, -1, keepdims=True)
        expo = jnp.exp(scores - row_max)
        expsum = jnp.sum(expo, -1, keepdims=True)
        probs_low = (expo / expsum).astype(jnp.bfloat16)
        context = jnp.einsum(
            "hqk,hkd->hqd", probs_low, values_all, preferred_element_type=jnp.float32
        ).astype(jnp.bfloat16)
        context_buf = lax.dynamic_update_slice_in_dim(context_buf, context, first_row, 1)
        return (context_buf, (row_max + jnp.log(expsum))[:, :, 0])

    context_low, log_norm = lax.scan(
        attend, jnp.zeros((heads_here, group_rows, HD), jnp.bfloat16), starts
    )
    attn_sum = lax.psum_scatter(
        jnp.einsum(
            "hrd,hde->re", context_low, w_out_heads, preferred_element_type=jnp.float32
        ).astype(jnp.bfloat16),
        "tp",
        scatter_dimension=0,
        tiled=True,
    ).astype(jnp.float32)
    hidden = tokens + attn_sum + bias_out
    normed_two, unit_two, inverse_two = norm_rows(hidden, gain_two, shift_two)
    rows_two = lax.all_gather(normed_two.astype(jnp.bfloat16), "tp", axis=0, tiled=True)
    inner = jnp.dot(rows_two, w_in, preferred_element_type=jnp.float32) + bias_in
    activ, gelu_pull = jax.vjp(jax.nn.gelu, inner)
    activ_low = activ.astype(jnp.bfloat16)
    mixed = (
        hidden
        + lax.psum_scatter(
            jnp.dot(activ_low, w_down, preferred_element_type=jnp.float32).astype(jnp.bfloat16),
            "tp",
            scatter_dimension=0,
            tiled=True,
        ).astype(jnp.float32)
        + bias_down
    )
    grad_low = cotangent.astype(jnp.bfloat16)
    grad_rows = lax.all_gather(grad_low, "tp", axis=0, tiled=True)
    g_down = jnp.einsum("rf,rd->fd", activ_low, grad_rows, preferred_element_type=jnp.float32)
    grad_activ = jnp.einsum("rd,fd->rf", grad_rows, w_down, preferred_element_type=jnp.float32)
    grad_inner = gelu_pull(grad_activ)[0].astype(jnp.bfloat16)
    g_in = jnp.einsum("rd,rf->df", rows_two, grad_inner, preferred_element_type=jnp.float32)
    g_bias_in = jnp.sum(grad_inner.astype(jnp.float32), 0)
    ffn_blocks = jnp.concatenate(
        [
            to_columns(g_in).reshape(groups, in_count, BLOCK, BLOCK),
            to_rows(g_down).reshape(groups, in_count, BLOCK, BLOCK),
        ],
        1,
    )
    grad_normed_two = lax.psum_scatter(
        jnp.einsum("rf,df->rd", grad_inner, w_in, preferred_element_type=jnp.float32).astype(
            jnp.bfloat16
        ),
        "tp",
        scatter_dimension=0,
        tiled=True,
    ).astype(jnp.float32)
    grad_hidden = cotangent + norm_back(grad_normed_two, unit_two, inverse_two, gain_two)
    grad_attn_low = grad_hidden.astype(jnp.bfloat16)
    grad_attn_rows = lax.all_gather(grad_attn_low, "tp", axis=0, tiled=True)
    g_out = jnp.einsum(
        "hrd,re->hde", context_low, grad_attn_rows, preferred_element_type=jnp.float32
    ).reshape(feat_here, D)
    grad_context = jnp.einsum(
        "re,hde->hrd", grad_attn_rows, w_out_heads, preferred_element_type=jnp.float32
    ).astype(jnp.bfloat16)
    zero_heads = jnp.zeros((heads_here, group_rows, HD), jnp.float32)

    def attend_back(carry, inputs):
        grad_queries, grad_keys, grad_values = carry
        first_row, log_block = inputs
        scores, query_rows = masked_scores(first_row)
        probs = jnp.exp(scores - log_block[:, :, None])
        grad_ctx_rows = lax.dynamic_slice_in_dim(grad_context, first_row, span, 1)
        grad_probs = jnp.einsum(
            "hqd,hkd->hqk", grad_ctx_rows, values_all, preferred_element_type=jnp.float32
        )
        delta = jnp.sum(probs * grad_probs, -1, keepdims=True)
        grad_scores = (probs * (grad_probs - delta)).astype(jnp.bfloat16)
        query_part = (
            jnp.einsum("hqk,hkd->hqd", grad_scores, keys_all, preferred_element_type=jnp.float32)
            * score_scale
        )
        grad_queries = lax.dynamic_update_slice_in_dim(grad_queries, query_part, first_row, 1)
        grad_keys = (
            grad_keys
            + jnp.einsum(
                "hqk,hqd->hkd", grad_scores, query_rows, preferred_element_type=jnp.float32
            )
            * score_scale
        )
        grad_values = grad_values + jnp.einsum(
            "hqk,hqd->hkd",
            probs.astype(jnp.bfloat16),
            grad_ctx_rows,
            preferred_element_type=jnp.float32,
        )
        return ((grad_queries, grad_keys, grad_values), None)

    (grad_queries, grad_keys, grad_values), unused = lax.scan(
        attend_back, (zero_heads, zero_heads, zero_heads), (starts, log_norm)
    )
    grad_proj = jnp.stack([grad_queries, grad_keys, grad_values], 0).astype(jnp.bfloat16)
    proj_sums = jnp.sum(grad_proj.astype(jnp.float32), 2)
    g_bias_qv = jnp.stack([proj_sums[0], proj_sums[2]], 1).reshape(qv_width)
    g_qkv = jnp.einsum(
        "rx,chrd->xhcd", rows_one, grad_proj, preferred_element_type=jnp.float32
    ).reshape(D, qkv_cols)
    grad_normed_one = lax.psum_scatter(
        jnp.einsum(
            "chrd,xhcd->rx", grad_proj, w_qkv_heads, preferred_element_type=jnp.float32
        ).astype(jnp.bfloat16),
        "tp",
        scatter_dimension=0,
        tiled=True,
    ).astype(jnp.float32)
    input_grad = grad_hidden + norm_back(grad_normed_one, unit_one, inverse_one, gain_one)
    local_rows = jnp.stack(
        [
            jnp.sum(grad_normed_one * unit_one, 0),
            jnp.sum(grad_normed_one, 0),
            jnp.sum(grad_normed_two * unit_two, 0),
            jnp.sum(grad_normed_two, 0),
            jnp.sum(grad_hidden, 0),
            jnp.sum(cotangent, 0),
        ]
    )
    qv_rows = lax.dynamic_update_slice(
        jnp.zeros((2 * D,), jnp.float32), g_bias_qv, (tp_rank * qv_width,)
    ).reshape(2, D)
    in_rows = lax.dynamic_update_slice(
        jnp.zeros((FF,), jnp.float32), g_bias_in, (tp_rank * ff_here,)
    ).reshape(FF // D, D)
    vec_grads = lax.psum(jnp.concatenate([local_rows, qv_rows, in_rows], 0), ("grp", "tp"))
    attn_blocks = jnp.concatenate(
        [
            to_columns(g_qkv).reshape(groups, qkv_count, BLOCK, BLOCK),
            to_rows(g_out).reshape(groups, out_count, BLOCK, BLOCK),
        ],
        1,
    )
    every_block = jnp.concatenate([attn_blocks, ffn_blocks], 1).reshape(-1, BLOCK, BLOCK)
    weight_grads = lax.psum_scatter(
        every_block.astype(jnp.bfloat16), "grp", scatter_dimension=0, tiled=True
    ).astype(jnp.float32)
    scaled = weight_grads * token_total ** (-0.5)
    stat_left_new = DECAY * stat_left + (1.0 - DECAY) * jnp.einsum(
        "nij,nkj->nik", scaled, scaled, precision=lax.Precision.HIGHEST
    )
    stat_right_new = DECAY * stat_right + (1.0 - DECAY) * jnp.einsum(
        "nji,njk->nik", scaled, scaled, precision=lax.Precision.HIGHEST
    )
    shaped = jnp.einsum("nij,njk->nik", root_left, scaled, precision=lax.Precision.HIGHEST)
    shaped = jnp.einsum("nij,njk->nik", shaped, root_right, precision=lax.Precision.HIGHEST)
    momentum_new = BETA * momentum + shaped
    weights_new = weights - RATE * momentum_new
    vec_scaled = vec_grads * token_total ** (-0.5)
    vec_second_new = VEC_DECAY * vec_second + (1.0 - VEC_DECAY) * vec_scaled * vec_scaled
    vec_momentum_new = BETA * vec_momentum + vec_scaled * lax.rsqrt(vec_second_new + VEC_EPS)
    vec_new = vec_params - VEC_RATE * vec_momentum_new
    return (
        mixed,
        input_grad,
        weight_grads,
        stat_left_new,
        stat_right_new,
        momentum_new,
        weights_new,
        vec_grads,
        vec_second_new,
        vec_momentum_new,
        vec_new,
    )


MESH_ID = pl.DeviceIdType.MESH
LANES = 128
HALF = 64
VMEM_LIMIT = 62 * 2**20
ARTICLES = 4
GELU_A = (2.0 / 3.141592653589793) ** 0.5
GELU_B = 0.044715


def remote(src, dst, send_sem, recv_sem, device):
    return pltpu.make_async_remote_copy(
        src_ref=src,
        dst_ref=dst,
        send_sem=send_sem,
        recv_sem=recv_sem,
        device_id=device,
        device_id_type=MESH_ID,
    )


def place():
    grp = lax.axis_index("grp")
    return lax.div(grp, 4), lax.rem(lax.div(grp, 2), 2), lax.rem(grp, 2), lax.axis_index("tp")


def slot_of(z, y, c):
    return z * 4 + y * 2 + c


def lay_blocks(view_ref, stack):
    count = view_ref.shape[2]

    def row(i, carry):
        stack[pl.ds(i, count, stride=BLOCK), 0:HALF] = view_ref[i].T
        return carry

    lax.fori_loop(0, BLOCK, row, 0)


def piece_shapes():
    return ((768, LANES), (64, 512), (1024, LANES), (LANES, 1024))


def fold_tiles(value, mask):
    kept = jnp.where(mask, value, 0.0)
    halves = kept[:, :LANES] + kept[:, LANES:]
    return halves + pltpu.roll(halves, HALF, 1)


def update_kernel(
    scale, sum_q, sum_o, sum_i, sum_d, root_l, root_r, w, m, sl, sr, out_g, out_sl, out_sr, out_m, out_w, first, second
):
    count = root_l.shape[2]
    bf = jnp.bfloat16

    @pl.when(pl.program_id(0) == 0)
    def _():
        rows = sum_q.shape[0]
        first[0:rows, 0:HALF] = sum_q[:, 0:HALF]
        first[rows : 2 * rows, 0:HALF] = sum_q[:, HALF:LANES]
        base = 2 * rows
        for b in range(8):
            first[base + b * 64 : base + b * 64 + 64, 0:HALF] = sum_o[:, b * HALF : (b + 1) * HALF]
        base += 512
        first[base : base + 1024, 0:HALF] = sum_i[:, 0:HALF]
        first[base + 1024 : base + 2048, 0:HALF] = sum_i[:, HALF:LANES]
        base += 2048
        for r in range(2):
            for b in range(16):
                at = base + (r * 16 + b) * 64
                first[at : at + 64, 0:HALF] = sum_d[r * 64 : r * 64 + 64, b * HALF : (b + 1) * HALF]

        def row(i, carry):
            both = jnp.concatenate([root_l[i], root_r[i]], 0)
            second[pl.ds(i, count, stride=BLOCK), :] = both.T
            return carry

        lax.fori_loop(0, BLOCK, row, 0)
        row_id = lax.broadcasted_iota(jnp.int32, (256, 256), 0)
        col_id = lax.broadcasted_iota(jnp.int32, (256, 256), 1)
        mask = lax.shift_right_logical(row_id, 6) == lax.shift_right_logical(col_id, 6)
        zero = jnp.zeros((256, 256), jnp.float32)

        def spread(v):
            return jnp.where(mask, jnp.concatenate([v, v, v, v], 1), zero).astype(bf)

        def four(k, carry):
            at = pl.ds(pl.multiple_of(k * 256, 256), 256)
            s32 = first[at, 0:HALF] * scale
            s = s32.astype(bf)
            left = second[at, 0:HALF]
            right = second[at, HALF:LANES].astype(bf)
            outer = lax.dot_general(s, s, (((1,), (1,)), ((), ())), preferred_element_type=jnp.float32)
            inner = lax.dot_general(spread(s32), s, (((0,), (0,)), ((), ())), preferred_element_type=jnp.float32)
            shaped = jnp.dot(spread(left), s, preferred_element_type=jnp.float32)
            shaped = jnp.dot(spread(shaped), right, preferred_element_type=jnp.float32)
            first[at, HALF:LANES] = fold_tiles(outer, mask)[:, HALF:LANES]
            second[at, 0:HALF] = inner
            second[at, HALF:LANES] = shaped
            return carry

        lax.fori_loop(0, count // 4, four, 0)

    i0 = pl.program_id(0) * w.shape[0]

    def rows_out(ii, carry):
        at = pl.ds(i0 + ii, count, stride=BLOCK)
        one = first[at, :].T
        two = second[at, :].T
        out_g[ii] = one[0:HALF]
        out_sl[ii] = DECAY * sl[ii] + (1.0 - DECAY) * one[HALF:LANES]
        out_sr[ii] = DECAY * sr[ii] + (1.0 - DECAY) * two[0:HALF]
        fresh = BETA * m[ii] + two[HALF:LANES]
        out_m[ii] = fresh
        out_w[ii] = w[ii] - RATE * fresh
        return carry

    lax.fori_loop(0, w.shape[0], rows_out, 0)


def update_blocks(sums, weights, momentum, stat_left, stat_right, root_left, root_right, token_total):
    def view(a):
        return jnp.transpose(a, (1, 2, 0))

    count = weights.shape[0]
    rows = 8
    whole = pl.BlockSpec(memory_space=pltpu.VMEM)
    part = pl.BlockSpec((rows, BLOCK, count), lambda i: (i, 0, 0))
    outs = pl.pallas_call(
        functools.partial(update_kernel, token_total ** (-0.5)),
        grid=(BLOCK // rows,),
        out_shape=[jax.ShapeDtypeStruct((BLOCK, BLOCK, count), jnp.float32)] * 5,
        in_specs=[whole] * 6 + [part] * 4,
        out_specs=[part] * 5,
        scratch_shapes=[
            pltpu.VMEM((count * BLOCK, LANES), jnp.float32),
            pltpu.VMEM((count * BLOCK, LANES), jnp.float32),
        ],
        compiler_params=pltpu.CompilerParams(vmem_limit_bytes=VMEM_LIMIT),
        name="update_blocks",
    )(*sums, view(root_left), view(root_right), view(weights), view(momentum), view(stat_left), view(stat_right))
    return [jnp.transpose(a, (2, 0, 1)) for a in outs]


DEPTH = 4


def layer_kernel(
    token_total,
    lengths,
    order,
    view,
    tokens,
    cot,
    vecs,
    vec_m,
    vec_s,
    mixed,
    input_grad,
    sum_q,
    sum_o,
    sum_i,
    sum_d,
    vec_grads,
    vec_s_new,
    vec_m_new,
    vec_new,
    gq,
    go,
    gi,
    gd,
    wqkv,
    cq,
    co,
    ci,
    cd,
    yq,
    yo,
    yi,
    yd,
    zq,
    zo,
    zi,
    zd,
    rows_one,
    rows_two,
    rows_t,
    grad_rows,
    probs,
    qkv,
    ctx,
    gctx,
    hidden,
    ghid,
    far,
    inx,
    macc,
    nacc,
    act,
    gin,
    bias_sum,
    vin,
    vout,
    recv,
    send_y,
    send_c,
    send_z,
    rc_recv,
    rc_send,
    ry_recv,
    ry_send,
    rz_recv,
    rz_send,
    x_send,
    x_recv,
    v_send,
    v_recv,
    copy_sem,
):
    bf, f32 = jnp.bfloat16, jnp.float32
    z, y, c, t = place()
    me = slot_of(z, y, c)
    x_peer = (me, 1 - t)
    y_peer = (slot_of(z, 1 - y, c), t)
    c_peer = (slot_of(z, y, 1 - c), t)
    rows = tokens.shape[0]
    own = pl.ds(pl.multiple_of(t * rows, rows), rows)
    other = pl.ds(pl.multiple_of((1 - t) * rows, rows), rows)
    gathered, core_in, y_in, z_in = (gq, go, gi, gd), (cq, co, ci, cd), (yq, yo, yi, yd), (zq, zo, zi, zd)
    sums = (sum_q, sum_o, sum_i, sum_d)
    Q, O, I, W = range(4)

    def dot(a, b):
        return jnp.dot(a, b, preferred_element_type=f32)

    def dot_nt(a, b):
        return lax.dot_general(a, b, (((1,), (1,)), ((), ())), preferred_element_type=f32)

    def dot_tn(a, b):
        return lax.dot_general(a, b, (((0,), (0,)), ((), ())), preferred_element_type=f32)

    def piece(k, zz, yy, cc):
        if k == O:
            return go.at[zz * 2 + yy, :, pl.ds(pl.multiple_of(cc * 512, 512), 512)]
        return gathered[k].at[slot_of(zz, yy, cc)]

    def near(s):
        return lax.rem(z + (1 - 2 * lax.div(z, 2)) * s + DEPTH, DEPTH)

    def ag_copy(k, zz, yy, way):
        src = piece(k, zz, yy, c)
        sem = recv.at[k, slot_of(zz, yy, c)]
        if way == "up":
            return remote(src, src, send_z.at[k, 0, zz], sem, (slot_of(z + 1, y, c), t))
        if way == "down":
            return remote(src, src, send_z.at[k, 1, zz], sem, (slot_of(z - 1, y, c), t))
        if way == "y":
            return remote(src, src, send_y.at[k, zz], sem, y_peer)
        return remote(src, src, send_c.at[k, yy * DEPTH + zz], sem, c_peer)

    def ag_wait(k, zz, yy, cc):
        ref = piece(k, zz, yy, cc)
        remote(ref, ref, send_y.at[k, 0], recv.at[k, slot_of(zz, yy, cc)], y_peer).wait_recv()

    def own_sends(k):
        @pl.when(z < DEPTH - 1)
        def _():
            ag_copy(k, z, y, "up").start()

        @pl.when(z > 0)
        def _():
            ag_copy(k, z, y, "down").start()

        ag_copy(k, z, y, "y").start()
        ag_copy(k, z, y, "core").start()

    def z_arrival(kinds, dist):
        @pl.when(z >= dist)
        def _():
            for k in kinds:
                ag_wait(k, z - dist, y, c)

                @pl.when(z < DEPTH - 1)
                def _():
                    ag_copy(k, z - dist, y, "up").start()

                ag_copy(k, z - dist, y, "y").start()
                ag_copy(k, z - dist, y, "core").start()

        @pl.when(z + dist < DEPTH)
        def _():
            for k in kinds:
                ag_wait(k, z + dist, y, c)

                @pl.when(z > 0)
                def _():
                    ag_copy(k, z + dist, y, "down").start()

                ag_copy(k, z + dist, y, "y").start()
                ag_copy(k, z + dist, y, "core").start()

    def y_arrival(kinds, dist):
        def one(zz):
            for k in kinds:
                ag_wait(k, zz, 1 - y, c)
                ag_copy(k, zz, 1 - y, "core").start()

        if dist == 0:
            one(z)
            return

        @pl.when(z >= dist)
        def _():
            one(z - dist)

        @pl.when(z + dist < DEPTH)
        def _():
            one(z + dist)

    def drain(k, zz, yy):
        ag_copy(k, zz, yy, "core").wait_send()

        @pl.when(yy == y)
        def _():
            ag_copy(k, zz, y, "y").wait_send()

            @pl.when((zz <= z) & (z < DEPTH - 1))
            def _():
                ag_copy(k, zz, y, "up").wait_send()

            @pl.when((zz >= z) & (z > 0))
            def _():
                ag_copy(k, zz, y, "down").wait_send()

    def add(dst, first, second):
        count, width = dst.shape
        step = min(count, 256 * LANES // width)

        def body(i, carry):
            at = pl.ds(pl.multiple_of(i * step, 16), step)
            dst[at, :] = (first[at, :].astype(f32) + second[at, :].astype(f32)).astype(dst.dtype)
            return carry

        lax.fori_loop(0, count // step, body, 0)

    def rc_copy(k, zz, yy):
        at = zz * 2 + yy
        return remote(piece(k, zz, yy, 1 - c), core_in[k].at[at], rc_send.at[k, at], rc_recv.at[k, at], c_peer)

    def ry_copy(k, zz):
        return remote(piece(k, zz, 1 - y, c), y_in[k].at[zz], ry_send.at[k, zz], ry_recv.at[k, zz], y_peer)

    def rz_copy(k, zz):
        step = lax.rem(zz - z + DEPTH, DEPTH)
        at = DEPTH - 1 - step
        return remote(
            piece(k, zz, y, c), z_in[k].at[at], rz_send.at[k, step - 1], rz_recv.at[k, at], (slot_of(zz, y, c), t)
        )

    def rc_add(k, zz, yy):
        at = zz * 2 + yy
        remote(core_in[k].at[at], core_in[k].at[at], rc_send.at[k, 0], rc_recv.at[k, at], c_peer).wait_recv()
        mine = piece(k, zz, yy, c)
        add(mine, mine, core_in[k].at[at])

        @pl.when(yy != y)
        def _():
            ry_copy(k, zz).start()

    def ry_add(k, s):
        zz = near(s)
        remote(y_in[k].at[zz], y_in[k].at[zz], ry_send.at[k, 0], ry_recv.at[k, zz], y_peer).wait_recv()
        mine = piece(k, zz, y, c)
        if s == 0:
            add(sums[k], mine, y_in[k].at[zz])
        else:
            add(mine, mine, y_in[k].at[zz])
            rz_copy(k, zz).start()

    def rz_add(k):
        for at in range(DEPTH - 1):
            remote(z_in[k].at[at], z_in[k].at[at], rz_send.at[k, 0], rz_recv.at[k, at], y_peer).wait_recv()
            add(sums[k], sums[k], z_in[k].at[at])

    def x_rows(ref, index):
        return remote(ref.at[own], ref.at[own], x_send.at[index], x_recv.at[index], x_peer)

    def x_rows_wait(ref, index):
        remote(ref.at[other], ref.at[other], x_send.at[index], x_recv.at[index], x_peer).wait_recv()

    def x_part(index):
        return remote(far.at[index], inx.at[index], x_send.at[4 + index], x_recv.at[4 + index], x_peer)

    def by_rows(body, step=64):
        def run(i, carry):
            body(pl.multiple_of(i * step, step), step)
            return carry

        lax.fori_loop(0, rows // step, run, 0)

    def norm(value):
        average = jnp.mean(value, -1, keepdims=True)
        centred = value - average
        inverse = lax.rsqrt(jnp.mean(centred * centred, -1, keepdims=True) + EPS)
        return centred * inverse, inverse

    def norm_grad(grad, unit, inverse, gain):
        scaled = grad * gain
        return inverse * (
            scaled - jnp.mean(scaled, -1, keepdims=True) - unit * jnp.mean(scaled * unit, -1, keepdims=True)
        )

    barrier = pltpu.get_barrier_semaphore()
    z_peers = [(slot_of(lax.rem(z + step, DEPTH), y, c), t) for step in range(1, DEPTH)]
    everyone = [x_peer, y_peer, c_peer] + z_peers
    for device in everyone:
        pl.semaphore_signal(barrier, inc=1, device_id=device, device_id_type=MESH_ID)

    def prepare(held, stack):
        load = pltpu.make_async_copy(view, held, copy_sem.at[0])
        load.start()

        def first_norm(at, step):
            unit, inverse = norm(tokens[pl.ds(at, step), :])
            to = pl.ds(pl.multiple_of(t * rows + at, step), step)
            rows_one[to, :] = (unit * vecs[0:1, :] + vecs[1:2, :]).astype(bf)
            grad_rows[to, :] = cot[pl.ds(at, step), :].astype(bf)

        by_rows(first_norm)
        pl.semaphore_wait(barrier, len(everyone))
        x_rows(rows_one, 0).start()
        load.wait()
        lay_blocks(held, stack)
        n = gq.shape[1]
        gq[me, :, 0:HALF] = stack[0:n, 0:HALF].astype(bf)
        gq[me, :, HALF:LANES] = stack[n : 2 * n, 0:HALF].astype(bf)
        own_sends(Q)
        base = 2 * n
        wide = [stack[base + b * 64 : base + b * 64 + 64, 0:HALF] for b in range(8)]
        go[z * 2 + y, :, pl.ds(pl.multiple_of(c * 512, 512), 512)] = jnp.concatenate(wide, 1).astype(bf)
        own_sends(O)
        base += 512
        gi[me, :, 0:HALF] = stack[base : base + 1024, 0:HALF].astype(bf)
        gi[me, :, HALF:LANES] = stack[base + 1024 : base + 2048, 0:HALF].astype(bf)
        base += 2048
        for r in range(2):
            for b in range(16):
                at = base + (r * 16 + b) * 64
                gd[me, r * 64 : r * 64 + 64, b * HALF : (b + 1) * HALF] = stack[at : at + 64, 0:HALF].astype(bf)

    pl.run_scoped(
        prepare,
        pltpu.VMEM(view.shape, f32),
        pltpu.VMEM((view.shape[2] * BLOCK, LANES), f32),
    )
    for dist in range(1, DEPTH):
        z_arrival((Q,), dist)
    x_rows(grad_rows, 1).start()
    own_sends(I)
    own_sends(W)
    for dist in range(DEPTH):
        y_arrival((Q,), dist)
    for dist in range(1, DEPTH):
        z_arrival((O,), dist)
    for zz in range(DEPTH):
        for yy in range(2):
            ag_wait(Q, zz, yy, 1 - c)
    x_rows_wait(rows_one, 0)

    ends = []
    for p in range(ARTICLES):
        length = 0
        for a in range(ARTICLES):
            length = length + jnp.where(order[0, p] == a, lengths[0, a], 0)
        ends.append(length + ends[-1] if p else length)

    def allowed(first, count):
        ids = lax.broadcasted_iota(jnp.int32, (rows, 1), 0) + first
        start = jnp.zeros((rows, 1), jnp.int32)
        for end in ends:
            start = jnp.where(ids >= end, end, start)
        start = jnp.where(ids >= ends[-1], ids, start)
        keys = lax.broadcasted_iota(jnp.int32, (rows, count), 1)
        return (keys <= ids) & (keys >= start)

    scale = HD ** (-0.5)
    strip = 1024

    def assemble(h):
        for yy in range(2):
            even, odd = gq.at[slot_of(h, yy, 0)], gq.at[slot_of(h, yy, 1)]
            at = yy * 192
            wqkv[h, 0:768, at : at + 64] = even[:, 0:64]
            wqkv[h, 768:1024, at : at + 64] = even[0:256, 64:128]
            wqkv[h, 0:512, at + 64 : at + 128] = even[256:768, 64:128]
            wqkv[h, 512:1024, at + 64 : at + 128] = odd[0:512, 0:64]
            wqkv[h, 0:256, at + 128 : at + 192] = odd[512:768, 0:64]
            wqkv[h, 256:1024, at + 128 : at + 192] = odd[:, 64:128]

    def disassemble(h, value):
        for yy in range(2):
            even, odd = gq.at[slot_of(h, yy, 0)], gq.at[slot_of(h, yy, 1)]
            at = yy * 192
            even[:, 0:64] = value[0:768, at : at + 64]
            even[0:256, 64:128] = value[768:1024, at : at + 64]
            even[256:768, 64:128] = value[0:512, at + 64 : at + 128]
            odd[0:512, 0:64] = value[512:1024, at + 64 : at + 128]
            odd[512:768, 0:64] = value[0:256, at + 128 : at + 192]
            odd[:, 64:128] = value[256:1024, at + 128 : at + 192]

    qv = vecs[pl.ds(6 + t, 1), :]

    def head(h):
        assemble(h)
        none = jnp.zeros((1, HD), f32)
        bias = jnp.concatenate([qv[:, h * 256 : h * 256 + 128], none, qv[:, h * 256 + 128 : h * 256 + 256]], 1)
        qkv[h] = (dot(rows_one[...], wqkv[h]) + bias).astype(bf)
        for block in range(2):
            at, seen = slice(block * rows, (block + 1) * rows), (block + 1) * rows
            scores = dot_nt(qkv[h, at, 0:128], qkv[h, 0:seen, 128:256]) * scale
            scores = jnp.where(allowed(block * rows, seen), scores, NEG)
            expo = jnp.exp(scores - jnp.max(scores, -1, keepdims=True))
            low = (expo / jnp.sum(expo, -1, keepdims=True)).astype(bf)
            probs[h, at, 0:seen] = low
            ctx[at, h * 128 : h * 128 + 128] = dot(low, qkv[h, 0:seen, 256:384]).astype(bf)

    head(0)
    for dist in range(DEPTH):
        y_arrival((O,), dist)
    head(1)
    z_arrival((I, W), 1)
    head(2)
    y_arrival((I, W), 0)
    head(3)
    for zz in range(DEPTH):
        for yy in range(2):
            ag_wait(O, zz, yy, 1 - c)

    def w_out(at, count):
        return go[at : at + count].reshape(count * 64, 1024)

    far[0] = dot(ctx[other, :], w_out(0, 8)).astype(bf)
    x_part(0).start()
    hidden[...] = tokens[...] + dot(ctx[own, :], w_out(0, 8)) + vecs[4:5, :]
    z_arrival((I, W), 2)
    y_arrival((I, W), 1)
    x_part(0).wait_recv()

    def second_norm(at, step):
        value = hidden[pl.ds(at, step), :] + inx[0, pl.ds(at, step), :].astype(f32)
        hidden[pl.ds(at, step), :] = value
        unit, inverse = norm(value)
        to = pl.ds(pl.multiple_of(t * rows + at, step), step)
        rows_two[to, :] = (unit * vecs[2:3, :] + vecs[3:4, :]).astype(bf)

    by_rows(second_norm)
    x_rows(rows_two, 2).start()
    z_arrival((I, W), 3)
    y_arrival((I, W), 2)
    macc[...] = jnp.zeros_like(macc)
    nacc[...] = jnp.zeros_like(nacc)
    vout[...] = jnp.zeros_like(vout)
    x_rows_wait(grad_rows, 1)
    x_rows_wait(rows_two, 2)
    rows_t[...] = rows_two[...].T

    def ffn(e, carry):
        s, sub = lax.div(e, 2), lax.rem(e, 2)
        zz, yy = near(s), lax.rem(y + sub, 2)

        @pl.when(e == 5)
        def _():
            y_arrival((I, W), 3)

        for k in (I, W):
            ag_wait(k, zz, yy, 1 - c)
        m = zz * 2 + yy
        first = 2 * m
        bias_row = vecs[pl.ds(8 + 2 * t + lax.div(m, 4), 1), pl.ds(pl.multiple_of(lax.rem(m, 4) * 256, 256), 256)]

        def w_in(at, count):
            return jnp.concatenate([gi[first, at : at + count, :], gi[first + 1, at : at + count, :]], 1)

        def w_down(at, count):
            return gd[pl.ds(first, 2), :, at : at + count].reshape(256, count)

        for block in range(2):
            at = slice(block * rows, (block + 1) * rows)
            inner = dot(rows_two[at, :], w_in(0, 1024)) + bias_row
            cube = inner * inner
            bent = jnp.tanh(GELU_A * inner * (1.0 + GELU_B * cube))
            act[at, :] = (0.5 * inner * (1.0 + bent)).astype(bf)
            slope = 0.5 * (1.0 + bent) + 0.5 * inner * (1.0 - bent * bent) * (GELU_A * (1.0 + 3.0 * GELU_B * cube))
            gin[at, :] = (dot_nt(grad_rows[at, :], w_down(0, 1024)) * slope).astype(bf)
        for nb in range(4):
            at = slice(nb * 256, nb * 256 + 256)
            nacc[:, at] += dot_nt(gin[...], w_in(nb * 256, 256))
            macc[:, at] += dot(act[...], w_down(nb * 256, 256))
        bias_sum[m] = jnp.sum(gin[...].astype(f32), 0, keepdims=True)
        for k in (I, W):
            drain(k, zz, yy)
        for nb in range(4):
            at = slice(nb * 256, nb * 256 + 256)
            part = dot(rows_t[at, :], gin[...]).astype(bf)
            gi[first, at, :] = part[:, 0:LANES]
            gi[first + 1, at, :] = part[:, LANES:]
        act_t = act[...].T
        for nb in range(4):
            at = slice(nb * 256, nb * 256 + 256)
            part = dot(act_t, grad_rows[:, at]).astype(bf)
            gd[pl.ds(first, 2), :, at] = part.reshape(2, LANES, 256)
        for k in (I, W):
            rc_copy(k, zz, yy).start()

        @pl.when(e > 0)
        def _():
            before = e - 1
            for k in (I, W):
                rc_add(k, near(lax.div(before, 2)), lax.rem(y + lax.rem(before, 2), 2))

        return carry

    lax.fori_loop(0, 2 * DEPTH, ffn, 0)
    far[1] = nacc[other, :].astype(bf)
    x_part(1).start()
    for m in range(8):
        for side in range(2):
            row = 8 + 2 * side + m // 4
            vout[0, row : row + 1, m % 4 * 256 : m % 4 * 256 + 256] = jnp.where(t == side, bias_sum[m], 0.0)
    far[2] = macc[other, :].astype(bf)
    x_part(2).start()
    for k in (I, W):
        rc_add(k, near(DEPTH - 1), 1 - y)
    rows_t[...] = rows_one[...].T
    x_part(1).wait_recv()

    def row_sum(row, value):
        vout[0, row : row + 1, :] += jnp.sum(value, 0, keepdims=True)

    def second_back(at, step):
        here = pl.ds(at, step)
        in_group = pl.ds(pl.multiple_of(t * rows + at, step), step)
        grad = nacc[in_group, :] + inx[1, here, :].astype(f32)
        unit, inverse = norm(hidden[here, :])
        back = cot[here, :] + norm_grad(grad, unit, inverse, vecs[2:3, :])
        ghid[here, :] = back
        rows_two[in_group, :] = back.astype(bf)
        row_sum(2, grad * unit)
        row_sum(3, grad)
        row_sum(4, back)
        row_sum(5, cot[here, :])

    x_rows(rows_two, 2).wait_send()
    by_rows(second_back)
    x_rows(rows_two, 3).start()
    for s in range(1, 3):
        for k in (I, W):
            ry_add(k, s)
    x_part(2).wait_recv()

    def mixed_out(at, step):
        here = pl.ds(at, step)
        in_group = pl.ds(pl.multiple_of(t * rows + at, step), step)
        mixed[here, :] = hidden[here, :] + macc[in_group, :] + inx[2, here, :].astype(f32) + vecs[5:6, :]

    by_rows(mixed_out)
    for zz in range(DEPTH):
        for yy in range(2):
            drain(O, zz, yy)
            drain(Q, zz, yy)
    x_rows_wait(rows_two, 3)
    gctx[...] = dot_nt(rows_two[...], w_out(0, 8)).astype(bf)
    for nb in range(4):
        at = slice(nb * 256, nb * 256 + 256)
        go[:, :, at] = dot_tn(ctx[...], rows_two[:, at]).astype(bf).reshape(8, 64, 256)
    for zz in range(DEPTH):
        for yy in range(2):
            rc_copy(O, zz, yy).start()

    def head_back(h):
        q0, q1 = qkv[h, 0:rows, 0:128], qkv[h, rows : 2 * rows, 0:128]
        grads = []
        for block in range(2):
            at, seen = slice(block * rows, (block + 1) * rows), (block + 1) * rows
            low = probs[h, at, 0:seen]
            given = gctx[at, h * 128 : h * 128 + 128]
            prob = low.astype(f32)
            grad_probs = dot_nt(given, qkv[h, 0:seen, 256:384])
            delta = jnp.sum(prob * grad_probs, -1, keepdims=True)
            grad_scores = (prob * (grad_probs - delta)).astype(bf)
            grad_q = dot(grad_scores, qkv[h, 0:seen, 128:256]) * scale
            grad_k = dot_tn(grad_scores, q1 if block else q0) * scale
            grad_v = dot_tn(low, given)
            grads.append((grad_q, grad_k, grad_v))
        (gq0, gk0, gv0), (gq1, gk1, gv1) = grads
        top = jnp.concatenate([gq0, gk0 + gk1[0:rows], gv0 + gv1[0:rows]], 1).astype(bf)
        low_half = jnp.concatenate([gq1, gk1[rows:], gv1[rows:]], 1).astype(bf)
        qkv[h, 0:rows, :] = top
        qkv[h, rows : 2 * rows, :] = low_half
        total = jnp.sum(top.astype(f32), 0, keepdims=True) + jnp.sum(low_half.astype(f32), 0, keepdims=True)
        for side in range(2):
            vout[0, 6 + side : 7 + side, h * 256 : h * 256 + 128] = jnp.where(t == side, total[:, 0:128], 0.0)
            vout[0, 6 + side : 7 + side, h * 256 + 128 : h * 256 + 256] = jnp.where(t == side, total[:, 256:384], 0.0)
        part = dot(rows_t[...], qkv[h]).astype(bf)
        disassemble(h, part)
        for yy in range(2):
            rc_copy(Q, h, yy).start()
        product = dot_nt(qkv[h], wqkv[h])
        if h == 0:
            nacc[...] = product
        else:
            nacc[...] += product

    for h in range(DEPTH):
        head_back(h)
    far[3] = nacc[other, :].astype(bf)
    x_part(3).start()
    for k in (O, Q):
        for s in range(DEPTH):
            rc_add(k, near(s), 1 - y)
    for k in (I, W):
        ry_add(k, 3)
    for k in (O, Q):
        for s in range(DEPTH):
            rc_add(k, near(s), y)
    for k in (I, W):
        ry_add(k, 0)
    x_part(3).wait_recv()

    def first_back(at, step):
        here = pl.ds(at, step)
        in_group = pl.ds(pl.multiple_of(t * rows + at, step), step)
        grad = nacc[in_group, :] + inx[3, here, :].astype(f32)
        unit, inverse = norm(tokens[here, :])
        input_grad[here, :] = ghid[here, :] + norm_grad(grad, unit, inverse, vecs[0:1, :])
        row_sum(0, grad * unit)
        row_sum(1, grad)

    by_rows(first_back)

    stages = (x_peer, c_peer, y_peer)

    def v_copy(stage):
        return remote(vout.at[stage], vin.at[stage], v_send.at[stage], v_recv.at[stage], stages[stage])

    def vz_copy(step):
        peer = (slot_of(lax.rem(z + step, DEPTH), y, c), t)
        return remote(vout.at[3], vin.at[3 + z], v_send.at[2 + step], v_recv.at[3 + z], peer)

    v_copy(0).start()
    for k in (O, Q):
        for s in range(1, DEPTH):
            ry_add(k, s)
        if k == O:
            v_copy(0).wait_recv()
            vout[1] = vout[0] + vin[0]
            v_copy(1).start()
            ry_add(k, 0)
    v_copy(1).wait_recv()
    vout[2] = vout[1] + vin[1]
    v_copy(2).start()
    ry_add(Q, 0)
    for k in (I, W, O):
        rz_add(k)
    v_copy(2).wait_recv()
    vout[3] = vout[2] + vin[2]
    for step in range(1, DEPTH):
        vz_copy(step).start()
    vin[3 + z] = vout[3]
    rz_add(Q)
    for step in range(1, DEPTH):
        zz = lax.rem(z + step, DEPTH)
        remote(vin.at[3 + zz], vin.at[3 + zz], v_send.at[0], v_recv.at[3 + zz], y_peer).wait_recv()
    count = vec_grads.shape[0]
    total = ((vin[3] + vin[4]) + vin[5]) + vin[6]
    total = total[0:count]
    vec_grads[...] = total
    scaled = total * token_total ** (-0.5)
    fresh = VEC_DECAY * vec_s[...] + (1.0 - VEC_DECAY) * scaled * scaled
    vec_s_new[...] = fresh
    momentum = BETA * vec_m[...] + scaled * lax.rsqrt(fresh + VEC_EPS)
    vec_m_new[...] = momentum
    vec_new[...] = vecs[...] - VEC_RATE * momentum

    for stage in range(3):
        v_copy(stage).wait_send()
    for step in range(1, DEPTH):
        vz_copy(step).wait_send()
    for index, ref in ((0, rows_one), (1, grad_rows), (3, rows_two)):
        x_rows(ref, index).wait_send()
    for index in range(4):
        x_part(index).wait_send()
    for k in range(4):
        for zz in range(DEPTH):
            for yy in range(2):
                rc_copy(k, zz, yy).wait_send()
            ry_copy(k, zz).wait_send()
        for s in range(1, DEPTH):
            rz_copy(k, near(s)).wait_send()


def run_layer(tokens, cotangent, lengths, order, weights, vec_params, vec_momentum, vec_second, token_total):
    bf, f32 = jnp.bfloat16, jnp.float32
    rows = tokens.shape[0]
    group = 2 * rows
    owners = 16
    shapes = piece_shapes()
    vec_shape = vec_params.shape
    view = jnp.transpose(weights, (1, 2, 0))
    vmem = pl.BlockSpec(memory_space=pltpu.VMEM)
    smem = pl.BlockSpec(memory_space=pltpu.SMEM)

    def many(count):
        return [pltpu.VMEM((count,) + s, bf) for s in shapes]

    full = pltpu.VMEM((group, D), bf)
    dma = pltpu.SemaphoreType.DMA
    return pl.pallas_call(
        functools.partial(layer_kernel, token_total),
        out_shape=[jax.ShapeDtypeStruct((rows, D), f32)] * 2
        + [jax.ShapeDtypeStruct(s, f32) for s in shapes]
        + [jax.ShapeDtypeStruct(vec_shape, f32)] * 4,
        in_specs=[smem, smem, pl.BlockSpec(memory_space=pl.ANY)] + [vmem] * 5,
        out_specs=[vmem] * 10,
        scratch_shapes=[
            pltpu.VMEM((owners,) + shapes[0], bf),
            pltpu.VMEM((owners // 2, BLOCK, D), bf),
            pltpu.VMEM((owners,) + shapes[2], bf),
            pltpu.VMEM((owners,) + shapes[3], bf),
            pltpu.VMEM((DEPTH, D, 3 * HD), bf),
        ]
        + many(2 * DEPTH)
        + many(DEPTH)
        + many(DEPTH - 1)
        + [
            full,
            full,
            pltpu.VMEM((D, group), bf),
            full,
            pltpu.VMEM((DEPTH, group, group), bf),
            pltpu.VMEM((DEPTH, group, 3 * HD), bf),
            pltpu.VMEM((group, DEPTH * HD), bf),
            pltpu.VMEM((group, DEPTH * HD), bf),
            pltpu.VMEM((rows, D), f32),
            pltpu.VMEM((rows, D), f32),
            pltpu.VMEM((4, rows, D), bf),
            pltpu.VMEM((4, rows, D), bf),
            pltpu.VMEM((group, D), f32),
            pltpu.VMEM((group, D), f32),
            pltpu.VMEM((group, 256), bf),
            pltpu.VMEM((group, 256), bf),
            pltpu.VMEM((8, 1, 256), f32),
            pltpu.VMEM((7, 16, D), f32),
            pltpu.VMEM((4, 16, D), f32),
            dma((4, owners)),
            dma((4, DEPTH)),
            dma((4, 2 * DEPTH)),
            dma((4, 2, DEPTH)),
            dma((4, 2 * DEPTH)),
            dma((4, 2 * DEPTH)),
            dma((4, DEPTH)),
            dma((4, DEPTH)),
            dma((4, DEPTH - 1)),
            dma((4, DEPTH - 1)),
            dma((8,)),
            dma((8,)),
            dma((6,)),
            dma((7,)),
            dma((1,)),
        ],
        compiler_params=pltpu.CompilerParams(
            collective_id=0, has_side_effects=True, vmem_limit_bytes=VMEM_LIMIT
        ),
        name="layer",
    )(lengths, order, view, tokens, cotangent, vec_params, vec_momentum, vec_second)


def per_device(
    grp_count,
    tp_count,
    tokens,
    cotangent,
    lengths,
    order,
    weights,
    momentum,
    stat_left,
    stat_right,
    root_left,
    root_right,
    vec_params,
    vec_momentum,
    vec_second,
):
    fits = grp_count == 4 * DEPTH and tp_count == 2 and tokens.shape[0] == 256
    if not fits or lengths.shape[1] != ARTICLES:
        return per_device_general(
            tokens,
            cotangent,
            lengths,
            order,
            weights,
            momentum,
            stat_left,
            stat_right,
            root_left,
            root_right,
            vec_params,
            vec_momentum,
            vec_second,
        )
    token_total = tokens.shape[0] * tp_count * grp_count
    mixed, input_grad, *rest = run_layer(
        tokens, cotangent, lengths, order, weights, vec_params, vec_momentum, vec_second, token_total
    )
    sums, vecs = rest[:4], rest[4:]
    blocks = update_blocks(
        sums, weights, momentum, stat_left, stat_right, root_left, root_right, token_total
    )
    vec_grads, vec_second_new, vec_momentum_new, vec_new = vecs
    return (mixed, input_grad, *blocks, vec_grads, vec_second_new, vec_momentum_new, vec_new)


def solution(mesh):
    placed = (
        P(("grp", "tp"), None),
        P(("grp", "tp"), None),
        P("grp", None),
        P("grp", None),
        P(("tp", "grp"), None, None),
        P(("tp", "grp"), None, None),
        P(("tp", "grp"), None, None),
        P(("tp", "grp"), None, None),
        P(("tp", "grp"), None, None),
        P(("tp", "grp"), None, None),
        P(),
        P(),
        P(),
    )
    return jax.shard_map(
        functools.partial(per_device, mesh.shape["grp"], mesh.shape["tp"]),
        mesh=mesh,
        in_specs=placed,
        out_specs=(
            P(("grp", "tp"), None),
            P(("grp", "tp"), None),
            P(("tp", "grp"), None, None),
            P(("tp", "grp"), None, None),
            P(("tp", "grp"), None, None),
            P(("tp", "grp"), None, None),
            P(("tp", "grp"), None, None),
            P(),
            P(),
            P(),
            P(),
        ),
        check_vma=False,
    )
```

```python
import functools

import jax
import jax.numpy as jnp
from jax import lax
from jax.experimental import pallas as pl
from jax.experimental.pallas import tpu as pltpu
from jax.sharding import PartitionSpec as P

D = 1024
HEADS = 8
HD = 128
FF = 4096
BLOCK = 64


EPS = 1e-05
NEG = -1e30
DECAY = 0.9
BETA = 0.9
RATE = 0.05
VEC_DECAY = 0.9
VEC_RATE = 0.2
VEC_EPS = 1e-08


def norm_rows(value, gain, shift):
    average = jnp.mean(value, -1, keepdims=True)
    centred = value - average
    inverse = lax.rsqrt(jnp.mean(centred * centred, -1, keepdims=True) + EPS)
    normed = centred * inverse
    return (normed * gain + shift, normed, inverse)


def norm_back(grad_out, normed, inverse, gain):
    scaled = grad_out * gain
    return inverse * (
        scaled
        - jnp.mean(scaled, -1, keepdims=True)
        - normed * jnp.mean(scaled * normed, -1, keepdims=True)
    )


def segment_ids(lengths_row, order_row, group_rows):
    article_count = lengths_row.shape[0]
    slots = jnp.arange(article_count, dtype=jnp.int32)
    picks = (order_row[:, None] == slots[None, :]).astype(jnp.int32)
    packed = jnp.sum(picks * lengths_row[None, :], 1)
    ends = jnp.cumsum(packed)
    spots = jnp.arange(group_rows, dtype=jnp.int32)
    return jnp.sum((spots[:, None] >= ends[None, :]).astype(jnp.int32), 1)


def allowed_mask(row_ids, row_segs, segments, key_ids, article_count):
    causal = key_ids[None, :] <= row_ids[:, None]
    same = segments[None, :] == row_segs[:, None]
    alone = (row_segs[:, None] < article_count) | (key_ids[None, :] == row_ids[:, None])
    return causal & same & alone


def from_columns(tiles, row_total, col_total):
    return (
        tiles.reshape(col_total // BLOCK, row_total // BLOCK, BLOCK, BLOCK)
        .transpose(1, 2, 0, 3)
        .reshape(row_total, col_total)
    )


def from_rows(tiles, row_total, col_total):
    return (
        tiles.reshape(row_total // BLOCK, col_total // BLOCK, BLOCK, BLOCK)
        .transpose(0, 2, 1, 3)
        .reshape(row_total, col_total)
    )


def to_columns(matrix):
    row_total, col_total = matrix.shape
    return (
        matrix.reshape(row_total // BLOCK, BLOCK, col_total // BLOCK, BLOCK)
        .transpose(2, 0, 1, 3)
        .reshape(-1, BLOCK, BLOCK)
    )


def to_rows(matrix):
    row_total, col_total = matrix.shape
    return (
        matrix.reshape(row_total // BLOCK, BLOCK, col_total // BLOCK, BLOCK)
        .transpose(0, 2, 1, 3)
        .reshape(-1, BLOCK, BLOCK)
    )


def per_device_general(
    tokens,
    cotangent,
    lengths,
    order,
    weights,
    momentum,
    stat_left,
    stat_right,
    root_left,
    root_right,
    vec_params,
    vec_momentum,
    vec_second,
):
    groups = lax.axis_size("grp")
    tp_size = lax.axis_size("tp")
    tp_rank = lax.axis_index("tp")
    tok_rows = tokens.shape[0]
    group_rows = tok_rows * tp_size
    article_count = lengths.shape[1]
    owners = groups * tp_size
    block_area = BLOCK * BLOCK * owners
    qkv_count = 3 * D * D // block_area
    out_count = D * D // block_area
    in_count = D * FF // block_area
    owned_blocks = weights.shape[0]
    heads_here = HEADS // tp_size
    qkv_cols = 3 * D // tp_size
    feat_here = D // tp_size
    ff_here = FF // tp_size
    qv_width = 2 * D // tp_size
    token_total = group_rows * groups
    gathered = lax.all_gather(weights.astype(jnp.bfloat16), "grp", axis=0, tiled=True)
    per_owner = gathered.reshape(groups, owned_blocks, BLOCK, BLOCK)
    marks = [0, qkv_count, qkv_count + out_count, qkv_count + out_count + in_count, owned_blocks]
    pieces = [
        per_owner[:, marks[index] : marks[index + 1]].reshape(-1, BLOCK, BLOCK)
        for index in range(4)
    ]
    w_qkv = from_columns(pieces[0], D, qkv_cols)
    w_out = from_rows(pieces[1], feat_here, D)
    w_in = from_columns(pieces[2], D, ff_here)
    w_down = from_rows(pieces[3], ff_here, D)
    w_qkv_heads = w_qkv.reshape(D, heads_here, 3, HD)
    w_out_heads = w_out.reshape(heads_here, HD, D)
    segments = segment_ids(lengths[0], order[0], group_rows)
    gain_one = vec_params[0]
    shift_one = vec_params[1]
    gain_two = vec_params[2]
    shift_two = vec_params[3]
    bias_out = vec_params[4]
    bias_down = vec_params[5]
    qv_here = lax.dynamic_slice_in_dim(
        vec_params[6:8].reshape(2 * D), tp_rank * qv_width, qv_width
    ).reshape(heads_here, 2, HD)
    bias_heads = jnp.stack(
        [qv_here[:, 0], jnp.zeros((heads_here, HD), jnp.float32), qv_here[:, 1]], 0
    )[:, :, None, :]
    bias_in = lax.dynamic_slice_in_dim(vec_params[8:].reshape(FF), tp_rank * ff_here, ff_here)
    normed_one, unit_one, inverse_one = norm_rows(tokens, gain_one, shift_one)
    rows_one = lax.all_gather(normed_one.astype(jnp.bfloat16), "tp", axis=0, tiled=True)
    projected = (
        jnp.einsum("rx,xhcd->chrd", rows_one, w_qkv_heads, preferred_element_type=jnp.float32)
        + bias_heads
    ).astype(jnp.bfloat16)
    queries = projected[0]
    keys_all = projected[1]
    values_all = projected[2]
    span = min(512, group_rows)
    starts = jnp.arange(group_rows // span, dtype=jnp.int32) * span
    key_ids = jnp.arange(group_rows, dtype=jnp.int32)
    score_scale = HD ** (-0.5)

    def masked_scores(first_row):
        row_ids = first_row + jnp.arange(span, dtype=jnp.int32)
        row_segs = lax.dynamic_slice_in_dim(segments, first_row, span, 0)
        allowed = allowed_mask(row_ids, row_segs, segments, key_ids, article_count)
        query_rows = lax.dynamic_slice_in_dim(queries, first_row, span, 1)
        scores = (
            jnp.einsum("hqd,hkd->hqk", query_rows, keys_all, preferred_element_type=jnp.float32)
            * score_scale
        )
        return (jnp.where(allowed[None], scores, NEG), query_rows)

    def attend(context_buf, first_row):
        scores, query_rows = masked_scores(first_row)
        row_max = jnp.max(scores, -1, keepdims=True)
        expo = jnp.exp(scores - row_max)
        expsum = jnp.sum(expo, -1, keepdims=True)
        probs_low = (expo / expsum).astype(jnp.bfloat16)
        context = jnp.einsum(
            "hqk,hkd->hqd", probs_low, values_all, preferred_element_type=jnp.float32
        ).astype(jnp.bfloat16)
        context_buf = lax.dynamic_update_slice_in_dim(context_buf, context, first_row, 1)
        return (context_buf, (row_max + jnp.log(expsum))[:, :, 0])

    context_low, log_norm = lax.scan(
        attend, jnp.zeros((heads_here, group_rows, HD), jnp.bfloat16), starts
    )
    attn_sum = lax.psum_scatter(
        jnp.einsum(
            "hrd,hde->re", context_low, w_out_heads, preferred_element_type=jnp.float32
        ).astype(jnp.bfloat16),
        "tp",
        scatter_dimension=0,
        tiled=True,
    ).astype(jnp.float32)
    hidden = tokens + attn_sum + bias_out
    normed_two, unit_two, inverse_two = norm_rows(hidden, gain_two, shift_two)
    rows_two = lax.all_gather(normed_two.astype(jnp.bfloat16), "tp", axis=0, tiled=True)
    inner = jnp.dot(rows_two, w_in, preferred_element_type=jnp.float32) + bias_in
    activ, gelu_pull = jax.vjp(jax.nn.gelu, inner)
    activ_low = activ.astype(jnp.bfloat16)
    mixed = (
        hidden
        + lax.psum_scatter(
            jnp.dot(activ_low, w_down, preferred_element_type=jnp.float32).astype(jnp.bfloat16),
            "tp",
            scatter_dimension=0,
            tiled=True,
        ).astype(jnp.float32)
        + bias_down
    )
    grad_low = cotangent.astype(jnp.bfloat16)
    grad_rows = lax.all_gather(grad_low, "tp", axis=0, tiled=True)
    g_down = jnp.einsum("rf,rd->fd", activ_low, grad_rows, preferred_element_type=jnp.float32)
    grad_activ = jnp.einsum("rd,fd->rf", grad_rows, w_down, preferred_element_type=jnp.float32)
    grad_inner = gelu_pull(grad_activ)[0].astype(jnp.bfloat16)
    g_in = jnp.einsum("rd,rf->df", rows_two, grad_inner, preferred_element_type=jnp.float32)
    g_bias_in = jnp.sum(grad_inner.astype(jnp.float32), 0)
    ffn_blocks = jnp.concatenate(
        [
            to_columns(g_in).reshape(groups, in_count, BLOCK, BLOCK),
            to_rows(g_down).reshape(groups, in_count, BLOCK, BLOCK),
        ],
        1,
    )
    grad_normed_two = lax.psum_scatter(
        jnp.einsum("rf,df->rd", grad_inner, w_in, preferred_element_type=jnp.float32).astype(
            jnp.bfloat16
        ),
        "tp",
        scatter_dimension=0,
        tiled=True,
    ).astype(jnp.float32)
    grad_hidden = cotangent + norm_back(grad_normed_two, unit_two, inverse_two, gain_two)
    grad_attn_low = grad_hidden.astype(jnp.bfloat16)
    grad_attn_rows = lax.all_gather(grad_attn_low, "tp", axis=0, tiled=True)
    g_out = jnp.einsum(
        "hrd,re->hde", context_low, grad_attn_rows, preferred_element_type=jnp.float32
    ).reshape(feat_here, D)
    grad_context = jnp.einsum(
        "re,hde->hrd", grad_attn_rows, w_out_heads, preferred_element_type=jnp.float32
    ).astype(jnp.bfloat16)
    zero_heads = jnp.zeros((heads_here, group_rows, HD), jnp.float32)

    def attend_back(carry, inputs):
        grad_queries, grad_keys, grad_values = carry
        first_row, log_block = inputs
        scores, query_rows = masked_scores(first_row)
        probs = jnp.exp(scores - log_block[:, :, None])
        grad_ctx_rows = lax.dynamic_slice_in_dim(grad_context, first_row, span, 1)
        grad_probs = jnp.einsum(
            "hqd,hkd->hqk", grad_ctx_rows, values_all, preferred_element_type=jnp.float32
        )
        delta = jnp.sum(probs * grad_probs, -1, keepdims=True)
        grad_scores = (probs * (grad_probs - delta)).astype(jnp.bfloat16)
        query_part = (
            jnp.einsum("hqk,hkd->hqd", grad_scores, keys_all, preferred_element_type=jnp.float32)
            * score_scale
        )
        grad_queries = lax.dynamic_update_slice_in_dim(grad_queries, query_part, first_row, 1)
        grad_keys = (
            grad_keys
            + jnp.einsum(
                "hqk,hqd->hkd", grad_scores, query_rows, preferred_element_type=jnp.float32
            )
            * score_scale
        )
        grad_values = grad_values + jnp.einsum(
            "hqk,hqd->hkd",
            probs.astype(jnp.bfloat16),
            grad_ctx_rows,
            preferred_element_type=jnp.float32,
        )
        return ((grad_queries, grad_keys, grad_values), None)

    (grad_queries, grad_keys, grad_values), unused = lax.scan(
        attend_back, (zero_heads, zero_heads, zero_heads), (starts, log_norm)
    )
    grad_proj = jnp.stack([grad_queries, grad_keys, grad_values], 0).astype(jnp.bfloat16)
    proj_sums = jnp.sum(grad_proj.astype(jnp.float32), 2)
    g_bias_qv = jnp.stack([proj_sums[0], proj_sums[2]], 1).reshape(qv_width)
    g_qkv = jnp.einsum(
        "rx,chrd->xhcd", rows_one, grad_proj, preferred_element_type=jnp.float32
    ).reshape(D, qkv_cols)
    grad_normed_one = lax.psum_scatter(
        jnp.einsum(
            "chrd,xhcd->rx", grad_proj, w_qkv_heads, preferred_element_type=jnp.float32
        ).astype(jnp.bfloat16),
        "tp",
        scatter_dimension=0,
        tiled=True,
    ).astype(jnp.float32)
    input_grad = grad_hidden + norm_back(grad_normed_one, unit_one, inverse_one, gain_one)
    local_rows = jnp.stack(
        [
            jnp.sum(grad_normed_one * unit_one, 0),
            jnp.sum(grad_normed_one, 0),
            jnp.sum(grad_normed_two * unit_two, 0),
            jnp.sum(grad_normed_two, 0),
            jnp.sum(grad_hidden, 0),
            jnp.sum(cotangent, 0),
        ]
    )
    qv_rows = lax.dynamic_update_slice(
        jnp.zeros((2 * D,), jnp.float32), g_bias_qv, (tp_rank * qv_width,)
    ).reshape(2, D)
    in_rows = lax.dynamic_update_slice(
        jnp.zeros((FF,), jnp.float32), g_bias_in, (tp_rank * ff_here,)
    ).reshape(FF // D, D)
    vec_grads = lax.psum(jnp.concatenate([local_rows, qv_rows, in_rows], 0), ("grp", "tp"))
    attn_blocks = jnp.concatenate(
        [
            to_columns(g_qkv).reshape(groups, qkv_count, BLOCK, BLOCK),
            to_rows(g_out).reshape(groups, out_count, BLOCK, BLOCK),
        ],
        1,
    )
    every_block = jnp.concatenate([attn_blocks, ffn_blocks], 1).reshape(-1, BLOCK, BLOCK)
    weight_grads = lax.psum_scatter(
        every_block.astype(jnp.bfloat16), "grp", scatter_dimension=0, tiled=True
    ).astype(jnp.float32)
    scaled = weight_grads * token_total ** (-0.5)
    stat_left_new = DECAY * stat_left + (1.0 - DECAY) * jnp.einsum(
        "nij,nkj->nik", scaled, scaled, precision=lax.Precision.HIGHEST
    )
    stat_right_new = DECAY * stat_right + (1.0 - DECAY) * jnp.einsum(
        "nji,njk->nik", scaled, scaled, precision=lax.Precision.HIGHEST
    )
    shaped = jnp.einsum("nij,njk->nik", root_left, scaled, precision=lax.Precision.HIGHEST)
    shaped = jnp.einsum("nij,njk->nik", shaped, root_right, precision=lax.Precision.HIGHEST)
    momentum_new = BETA * momentum + shaped
    weights_new = weights - RATE * momentum_new
    vec_scaled = vec_grads * token_total ** (-0.5)
    vec_second_new = VEC_DECAY * vec_second + (1.0 - VEC_DECAY) * vec_scaled * vec_scaled
    vec_momentum_new = BETA * vec_momentum + vec_scaled * lax.rsqrt(vec_second_new + VEC_EPS)
    vec_new = vec_params - VEC_RATE * vec_momentum_new
    return (
        mixed,
        input_grad,
        weight_grads,
        stat_left_new,
        stat_right_new,
        momentum_new,
        weights_new,
        vec_grads,
        vec_second_new,
        vec_momentum_new,
        vec_new,
    )


MESH_ID = pl.DeviceIdType.MESH
LANES = 128
HALF = 64
VMEM_LIMIT = 62 * 2**20
ARTICLES = 4
GELU_A = (2.0 / 3.141592653589793) ** 0.5
GELU_B = 0.044715


def remote(src, dst, send_sem, recv_sem, device):
    return pltpu.make_async_remote_copy(
        src_ref=src,
        dst_ref=dst,
        send_sem=send_sem,
        recv_sem=recv_sem,
        device_id=device,
        device_id_type=MESH_ID,
    )


def place():
    grp = lax.axis_index("grp")
    return lax.div(grp, 4), lax.rem(lax.div(grp, 2), 2), lax.rem(grp, 2), lax.axis_index("tp")


def slot_of(z, y, c):
    return z * 4 + y * 2 + c


def lay_blocks(view_ref, stack):
    count = view_ref.shape[2]

    def row(i, carry):
        stack[pl.ds(i, count, stride=BLOCK), 0:HALF] = view_ref[i].T
        return carry

    lax.fori_loop(0, BLOCK, row, 0, unroll=8)


def piece_shapes():
    return ((768, LANES), (64, 512), (1024, LANES), (LANES, 1024))


def fold_tiles(value, mask):
    kept = jnp.where(mask, value, 0.0)
    halves = kept[:, :LANES] + kept[:, LANES:]
    return halves + pltpu.roll(halves, HALF, 1)


def update_kernel(
    scale,
    sum_q,
    sum_o,
    sum_i,
    sum_d,
    root_l,
    root_r,
    vec_g,
    vecs,
    vec_m,
    vec_s,
    mixed,
    input_grad,
    w,
    m,
    sl,
    sr,
    out_g,
    out_sl,
    out_sr,
    out_m,
    out_w,
    out_vg,
    out_vs,
    out_vm,
    out_v,
    out_mixed,
    out_input_grad,
    first,
    second,
    sems,
):
    count = root_l.shape[2]
    bf = jnp.bfloat16
    passed = [
        pltpu.make_async_copy(mixed, out_mixed, sems.at[0]),
        pltpu.make_async_copy(input_grad, out_input_grad, sems.at[1]),
    ]

    @pl.when(pl.program_id(0) == 0)
    def _():
        for copy in passed:
            copy.start()
        total = vec_g[...]
        out_vg[...] = total
        scaled = total * scale
        fresh = VEC_DECAY * vec_s[...] + (1.0 - VEC_DECAY) * scaled * scaled
        out_vs[...] = fresh
        momentum = BETA * vec_m[...] + scaled * lax.rsqrt(fresh + VEC_EPS)
        out_vm[...] = momentum
        out_v[...] = vecs[...] - VEC_RATE * momentum
        rows = sum_q.shape[0]
        first[0:rows, 0:HALF] = sum_q[:, 0:HALF]
        first[rows : 2 * rows, 0:HALF] = sum_q[:, HALF:LANES]
        base = 2 * rows
        for b in range(8):
            first[base + b * 64 : base + b * 64 + 64, 0:HALF] = sum_o[:, b * HALF : (b + 1) * HALF]
        base += 512
        first[base : base + 1024, 0:HALF] = sum_i[:, 0:HALF]
        first[base + 1024 : base + 2048, 0:HALF] = sum_i[:, HALF:LANES]
        base += 2048
        for r in range(2):
            for b in range(16):
                at = base + (r * 16 + b) * 64
                first[at : at + 64, 0:HALF] = sum_d[r * 64 : r * 64 + 64, b * HALF : (b + 1) * HALF]

        def row(i, carry):
            both = jnp.concatenate([root_l[i], root_r[i]], 0)
            second[pl.ds(i, count, stride=BLOCK), :] = both.T
            return carry

        lax.fori_loop(0, BLOCK, row, 0, unroll=8)
        row_id = lax.broadcasted_iota(jnp.int32, (256, 256), 0)
        col_id = lax.broadcasted_iota(jnp.int32, (256, 256), 1)
        mask = lax.shift_right_logical(row_id, 6) == lax.shift_right_logical(col_id, 6)
        zero = jnp.zeros((256, 256), jnp.float32)

        def spread(v):
            return jnp.where(mask, jnp.concatenate([v, v, v, v], 1), zero).astype(bf)

        def four(k, carry):
            at = pl.ds(pl.multiple_of(k * 256, 256), 256)
            s32 = first[at, 0:HALF] * scale
            s = s32.astype(bf)
            left = second[at, 0:HALF]
            right = second[at, HALF:LANES].astype(bf)
            outer = lax.dot_general(s, s, (((1,), (1,)), ((), ())), preferred_element_type=jnp.float32)
            inner = lax.dot_general(spread(s32), s, (((0,), (0,)), ((), ())), preferred_element_type=jnp.float32)
            shaped = jnp.dot(spread(left), s, preferred_element_type=jnp.float32)
            shaped = jnp.dot(spread(shaped), right, preferred_element_type=jnp.float32)
            first[at, HALF:LANES] = fold_tiles(outer, mask)[:, HALF:LANES]
            second[at, 0:HALF] = inner
            second[at, HALF:LANES] = shaped
            return carry

        lax.fori_loop(0, count // 4, four, 0, unroll=4)

    i0 = pl.program_id(0) * w.shape[0]

    def rows_out(ii, carry):
        at = pl.ds(i0 + ii, count, stride=BLOCK)
        one = first[at, :].T
        two = second[at, :].T
        out_g[ii] = one[0:HALF]
        out_sl[ii] = DECAY * sl[ii] + (1.0 - DECAY) * one[HALF:LANES]
        out_sr[ii] = DECAY * sr[ii] + (1.0 - DECAY) * two[0:HALF]
        fresh = BETA * m[ii] + two[HALF:LANES]
        out_m[ii] = fresh
        out_w[ii] = w[ii] - RATE * fresh
        return carry

    lax.fori_loop(0, w.shape[0], rows_out, 0, unroll=True)

    @pl.when(pl.program_id(0) == pl.num_programs(0) - 1)
    def _():
        for copy in passed:
            copy.wait()


def update_blocks(sums, blocks, vec_grads, vecs, results, token_total):
    views = [jnp.transpose(a, (1, 2, 0)) for a in blocks]
    count = blocks[0].shape[0]
    rows = 8
    whole = pl.BlockSpec(memory_space=pltpu.VMEM)
    there = pl.BlockSpec(memory_space=pl.ANY)
    part = pl.BlockSpec((rows, BLOCK, count), lambda i: (i, 0, 0))
    vec = jax.ShapeDtypeStruct(vec_grads.shape, jnp.float32)
    outs = pl.pallas_call(
        functools.partial(update_kernel, token_total ** (-0.5)),
        grid=(BLOCK // rows,),
        out_shape=[jax.ShapeDtypeStruct((BLOCK, BLOCK, count), jnp.float32)] * 5
        + [vec] * 4
        + [jax.ShapeDtypeStruct(a.shape, a.dtype) for a in results],
        in_specs=[whole] * 10 + [there] * 2 + [part] * 4,
        out_specs=[part] * 5 + [whole] * 4 + [there] * 2,
        scratch_shapes=[
            pltpu.VMEM((count * BLOCK, LANES), jnp.float32),
            pltpu.VMEM((count * BLOCK, LANES), jnp.float32),
            pltpu.SemaphoreType.DMA((2,)),
        ],
        compiler_params=pltpu.CompilerParams(vmem_limit_bytes=VMEM_LIMIT),
        name="update_blocks",
    )(*sums, *views[4:], vec_grads, *vecs, *results, *views[:4])
    return [jnp.transpose(a, (2, 0, 1)) for a in outs[:5]], outs[5:9], outs[9:]


DEPTH = 4


def layer_kernel(
    lengths,
    order,
    view,
    tokens,
    cot,
    vecs,
    mixed,
    input_grad,
    sum_q,
    sum_o,
    sum_i,
    sum_d,
    vec_grads,
    gq,
    go,
    gi,
    gd,
    wqkv,
    cq,
    co,
    ci,
    cd,
    yq,
    yo,
    yi,
    yd,
    zq,
    zo,
    zi,
    zd,
    rows_one,
    rows_two,
    rows_t,
    grad_rows,
    probs,
    qkv,
    ctx,
    gctx,
    hidden,
    ghid,
    far,
    inx,
    macc,
    nacc,
    act,
    gin,
    bias_sum,
    vin,
    vout,
    recv,
    send_y,
    send_c,
    send_z,
    rc_recv,
    rc_send,
    ry_recv,
    ry_send,
    rz_recv,
    rz_send,
    x_send,
    x_recv,
    v_send,
    v_recv,
    copy_sem,
):
    bf, f32 = jnp.bfloat16, jnp.float32
    z, y, c, t = place()
    me = slot_of(z, y, c)
    x_peer = (me, 1 - t)
    y_peer = (slot_of(z, 1 - y, c), t)
    c_peer = (slot_of(z, y, 1 - c), t)
    rows = tokens.shape[0]
    own = pl.ds(pl.multiple_of(t * rows, rows), rows)
    other = pl.ds(pl.multiple_of((1 - t) * rows, rows), rows)
    gathered, core_in, y_in, z_in = (gq, go, gi, gd), (cq, co, ci, cd), (yq, yo, yi, yd), (zq, zo, zi, zd)
    sums = (sum_q, sum_o, sum_i, sum_d)
    Q, O, I, W = range(4)

    def dot(a, b):
        return jnp.dot(a, b, preferred_element_type=f32)

    def dot_nt(a, b):
        return lax.dot_general(a, b, (((1,), (1,)), ((), ())), preferred_element_type=f32)

    def dot_tn(a, b):
        return lax.dot_general(a, b, (((0,), (0,)), ((), ())), preferred_element_type=f32)

    def piece(k, zz, yy, cc):
        if k == O:
            return go.at[zz * 2 + yy, :, pl.ds(pl.multiple_of(cc * 512, 512), 512)]
        return gathered[k].at[slot_of(zz, yy, cc)]

    def near(s):
        return lax.rem(z + (1 - 2 * lax.div(z, 2)) * s + DEPTH, DEPTH)

    def ag_copy(k, zz, yy, way):
        src = piece(k, zz, yy, c)
        sem = recv.at[k, slot_of(zz, yy, c)]
        if way == "up":
            return remote(src, src, send_z.at[k, 0, zz], sem, (slot_of(z + 1, y, c), t))
        if way == "down":
            return remote(src, src, send_z.at[k, 1, zz], sem, (slot_of(z - 1, y, c), t))
        if way == "y":
            return remote(src, src, send_y.at[k, zz], sem, y_peer)
        return remote(src, src, send_c.at[k, yy * DEPTH + zz], sem, c_peer)

    def ag_wait(k, zz, yy, cc):
        ref = piece(k, zz, yy, cc)
        remote(ref, ref, send_y.at[k, 0], recv.at[k, slot_of(zz, yy, cc)], y_peer).wait_recv()

    def own_sends(k):
        @pl.when(z < DEPTH - 1)
        def _():
            ag_copy(k, z, y, "up").start()

        @pl.when(z > 0)
        def _():
            ag_copy(k, z, y, "down").start()

        ag_copy(k, z, y, "y").start()
        ag_copy(k, z, y, "core").start()

    def z_arrival(kinds, dist):
        @pl.when(z >= dist)
        def _():
            for k in kinds:
                ag_wait(k, z - dist, y, c)

                @pl.when(z < DEPTH - 1)
                def _():
                    ag_copy(k, z - dist, y, "up").start()

                ag_copy(k, z - dist, y, "y").start()
                ag_copy(k, z - dist, y, "core").start()

        @pl.when(z + dist < DEPTH)
        def _():
            for k in kinds:
                ag_wait(k, z + dist, y, c)

                @pl.when(z > 0)
                def _():
                    ag_copy(k, z + dist, y, "down").start()

                ag_copy(k, z + dist, y, "y").start()
                ag_copy(k, z + dist, y, "core").start()

    def y_arrival(kinds, dist):
        def one(zz):
            for k in kinds:
                ag_wait(k, zz, 1 - y, c)
                ag_copy(k, zz, 1 - y, "core").start()

        if dist == 0:
            one(z)
            return

        @pl.when(z >= dist)
        def _():
            one(z - dist)

        @pl.when(z + dist < DEPTH)
        def _():
            one(z + dist)

    def drain(k, zz, yy):
        ag_copy(k, zz, yy, "core").wait_send()

        @pl.when(yy == y)
        def _():
            ag_copy(k, zz, y, "y").wait_send()

            @pl.when((zz <= z) & (z < DEPTH - 1))
            def _():
                ag_copy(k, zz, y, "up").wait_send()

            @pl.when((zz >= z) & (z > 0))
            def _():
                ag_copy(k, zz, y, "down").wait_send()

    def add(dst, first, second):
        count, width = dst.shape
        step = min(count, 256 * LANES // width)

        def body(i, carry):
            at = pl.ds(pl.multiple_of(i * step, 16), step)
            dst[at, :] = (first[at, :].astype(f32) + second[at, :].astype(f32)).astype(dst.dtype)
            return carry

        lax.fori_loop(0, count // step, body, 0)

    def rc_copy(k, zz, yy):
        at = zz * 2 + yy
        return remote(piece(k, zz, yy, 1 - c), core_in[k].at[at], rc_send.at[k, at], rc_recv.at[k, at], c_peer)

    def ry_copy(k, zz):
        return remote(piece(k, zz, 1 - y, c), y_in[k].at[zz], ry_send.at[k, zz], ry_recv.at[k, zz], y_peer)

    def rz_copy(k, zz):
        step = lax.rem(zz - z + DEPTH, DEPTH)
        at = DEPTH - 1 - step
        return remote(
            piece(k, zz, y, c), z_in[k].at[at], rz_send.at[k, step - 1], rz_recv.at[k, at], (slot_of(zz, y, c), t)
        )

    def rc_add(k, zz, yy):
        at = zz * 2 + yy
        remote(core_in[k].at[at], core_in[k].at[at], rc_send.at[k, 0], rc_recv.at[k, at], c_peer).wait_recv()
        mine = piece(k, zz, yy, c)
        add(mine, mine, core_in[k].at[at])

        @pl.when(yy != y)
        def _():
            ry_copy(k, zz).start()

    def ry_add(k, s):
        zz = near(s)
        remote(y_in[k].at[zz], y_in[k].at[zz], ry_send.at[k, 0], ry_recv.at[k, zz], y_peer).wait_recv()
        mine = piece(k, zz, y, c)
        if s == 0:
            add(sums[k], mine, y_in[k].at[zz])
        else:
            add(mine, mine, y_in[k].at[zz])
            rz_copy(k, zz).start()

    def rz_add(k):
        for at in range(DEPTH - 1):
            remote(z_in[k].at[at], z_in[k].at[at], rz_send.at[k, 0], rz_recv.at[k, at], y_peer).wait_recv()
            add(sums[k], sums[k], z_in[k].at[at])

    def x_rows(ref, index):
        return remote(ref.at[own], ref.at[own], x_send.at[index], x_recv.at[index], x_peer)

    def x_rows_wait(ref, index):
        remote(ref.at[other], ref.at[other], x_send.at[index], x_recv.at[index], x_peer).wait_recv()

    def x_part(index):
        return remote(far.at[index], inx.at[index], x_send.at[4 + index], x_recv.at[4 + index], x_peer)

    def by_rows(body, step=64):
        def run(i, carry):
            body(pl.multiple_of(i * step, step), step)
            return carry

        lax.fori_loop(0, rows // step, run, 0)

    def norm(value):
        average = jnp.mean(value, -1, keepdims=True)
        centred = value - average
        inverse = lax.rsqrt(jnp.mean(centred * centred, -1, keepdims=True) + EPS)
        return centred * inverse, inverse

    def norm_grad(grad, unit, inverse, gain):
        scaled = grad * gain
        return inverse * (
            scaled - jnp.mean(scaled, -1, keepdims=True) - unit * jnp.mean(scaled * unit, -1, keepdims=True)
        )

    barrier = pltpu.get_barrier_semaphore()
    z_peers = [(slot_of(lax.rem(z + step, DEPTH), y, c), t) for step in range(1, DEPTH)]
    everyone = [x_peer, y_peer, c_peer] + z_peers
    for device in everyone:
        pl.semaphore_signal(barrier, inc=1, device_id=device, device_id_type=MESH_ID)

    def prepare(held, stack):
        load = pltpu.make_async_copy(view, held, copy_sem.at[0])
        load.start()

        def first_norm(at, step):
            unit, inverse = norm(tokens[pl.ds(at, step), :])
            to = pl.ds(pl.multiple_of(t * rows + at, step), step)
            rows_one[to, :] = (unit * vecs[0:1, :] + vecs[1:2, :]).astype(bf)
            grad_rows[to, :] = cot[pl.ds(at, step), :].astype(bf)

        by_rows(first_norm)
        pl.semaphore_wait(barrier, len(everyone))
        x_rows(rows_one, 0).start()
        load.wait()
        lay_blocks(held, stack)
        n = gq.shape[1]
        gq[me, :, 0:HALF] = stack[0:n, 0:HALF].astype(bf)
        gq[me, :, HALF:LANES] = stack[n : 2 * n, 0:HALF].astype(bf)
        own_sends(Q)
        base = 2 * n
        wide = [stack[base + b * 64 : base + b * 64 + 64, 0:HALF] for b in range(8)]
        go[z * 2 + y, :, pl.ds(pl.multiple_of(c * 512, 512), 512)] = jnp.concatenate(wide, 1).astype(bf)
        own_sends(O)
        base += 512
        gi[me, :, 0:HALF] = stack[base : base + 1024, 0:HALF].astype(bf)
        gi[me, :, HALF:LANES] = stack[base + 1024 : base + 2048, 0:HALF].astype(bf)
        base += 2048
        for r in range(2):
            for b in range(16):
                at = base + (r * 16 + b) * 64
                gd[me, r * 64 : r * 64 + 64, b * HALF : (b + 1) * HALF] = stack[at : at + 64, 0:HALF].astype(bf)

    pl.run_scoped(
        prepare,
        pltpu.VMEM(view.shape, f32),
        pltpu.VMEM((view.shape[2] * BLOCK, LANES), f32),
    )
    for dist in range(1, DEPTH):
        z_arrival((Q,), dist)
    x_rows(grad_rows, 1).start()
    own_sends(I)
    own_sends(W)
    for dist in range(DEPTH):
        y_arrival((Q,), dist)
    for dist in range(1, DEPTH):
        z_arrival((O,), dist)
    for zz in range(DEPTH):
        for yy in range(2):
            ag_wait(Q, zz, yy, 1 - c)
    x_rows_wait(rows_one, 0)

    ends = []
    for p in range(ARTICLES):
        length = 0
        for a in range(ARTICLES):
            length = length + jnp.where(order[0, p] == a, lengths[0, a], 0)
        ends.append(length + ends[-1] if p else length)

    def allowed(first, count):
        ids = lax.broadcasted_iota(jnp.int32, (rows, 1), 0) + first
        start = jnp.zeros((rows, 1), jnp.int32)
        for end in ends:
            start = jnp.where(ids >= end, end, start)
        start = jnp.where(ids >= ends[-1], ids, start)
        keys = lax.broadcasted_iota(jnp.int32, (rows, count), 1)
        return (keys <= ids) & (keys >= start)

    scale = HD ** (-0.5)
    strip = 1024

    def assemble(h):
        for yy in range(2):
            even, odd = gq.at[slot_of(h, yy, 0)], gq.at[slot_of(h, yy, 1)]
            at = yy * 192
            wqkv[h, 0:768, at : at + 64] = even[:, 0:64]
            wqkv[h, 768:1024, at : at + 64] = even[0:256, 64:128]
            wqkv[h, 0:512, at + 64 : at + 128] = even[256:768, 64:128]
            wqkv[h, 512:1024, at + 64 : at + 128] = odd[0:512, 0:64]
            wqkv[h, 0:256, at + 128 : at + 192] = odd[512:768, 0:64]
            wqkv[h, 256:1024, at + 128 : at + 192] = odd[:, 64:128]

    def disassemble(h, value):
        for yy in range(2):
            even, odd = gq.at[slot_of(h, yy, 0)], gq.at[slot_of(h, yy, 1)]
            at = yy * 192
            even[:, 0:64] = value[0:768, at : at + 64]
            even[0:256, 64:128] = value[768:1024, at : at + 64]
            even[256:768, 64:128] = value[0:512, at + 64 : at + 128]
            odd[0:512, 0:64] = value[512:1024, at + 64 : at + 128]
            odd[512:768, 0:64] = value[0:256, at + 128 : at + 192]
            odd[:, 64:128] = value[256:1024, at + 128 : at + 192]

    qv = vecs[pl.ds(6 + t, 1), :]

    def head(h):
        assemble(h)
        none = jnp.zeros((1, HD), f32)
        bias = jnp.concatenate([qv[:, h * 256 : h * 256 + 128], none, qv[:, h * 256 + 128 : h * 256 + 256]], 1)
        qkv[h] = (dot(rows_one[...], wqkv[h]) + bias).astype(bf)
        for block in range(2):
            at, seen = slice(block * rows, (block + 1) * rows), (block + 1) * rows
            scores = dot_nt(qkv[h, at, 0:128], qkv[h, 0:seen, 128:256]) * scale
            scores = jnp.where(allowed(block * rows, seen), scores, NEG)
            expo = jnp.exp(scores - jnp.max(scores, -1, keepdims=True))
            low = (expo / jnp.sum(expo, -1, keepdims=True)).astype(bf)
            probs[h, at, 0:seen] = low
            ctx[at, h * 128 : h * 128 + 128] = dot(low, qkv[h, 0:seen, 256:384]).astype(bf)

    head(0)
    for dist in range(DEPTH):
        y_arrival((O,), dist)
    head(1)
    z_arrival((I, W), 1)
    head(2)
    y_arrival((I, W), 0)
    head(3)
    for zz in range(DEPTH):
        for yy in range(2):
            ag_wait(O, zz, yy, 1 - c)

    def w_out(at, count):
        return go[at : at + count].reshape(count * 64, 1024)

    far[0] = dot(ctx[other, :], w_out(0, 8)).astype(bf)
    x_part(0).start()
    hidden[...] = tokens[...] + dot(ctx[own, :], w_out(0, 8)) + vecs[4:5, :]
    z_arrival((I, W), 2)
    y_arrival((I, W), 1)
    x_part(0).wait_recv()

    def second_norm(at, step):
        value = hidden[pl.ds(at, step), :] + inx[0, pl.ds(at, step), :].astype(f32)
        hidden[pl.ds(at, step), :] = value
        unit, inverse = norm(value)
        to = pl.ds(pl.multiple_of(t * rows + at, step), step)
        rows_two[to, :] = (unit * vecs[2:3, :] + vecs[3:4, :]).astype(bf)

    by_rows(second_norm)
    x_rows(rows_two, 2).start()
    z_arrival((I, W), 3)
    y_arrival((I, W), 2)
    macc[...] = jnp.zeros_like(macc)
    nacc[...] = jnp.zeros_like(nacc)
    vout[...] = jnp.zeros_like(vout)
    x_rows_wait(grad_rows, 1)
    x_rows_wait(rows_two, 2)
    rows_t[...] = rows_two[...].T

    def ffn(e, carry):
        s, sub = lax.div(e, 2), lax.rem(e, 2)
        zz, yy = near(s), lax.rem(y + sub, 2)

        @pl.when(e == 5)
        def _():
            y_arrival((I, W), 3)

        for k in (I, W):
            ag_wait(k, zz, yy, 1 - c)
        m = zz * 2 + yy
        first = 2 * m
        bias_row = vecs[pl.ds(8 + 2 * t + lax.div(m, 4), 1), pl.ds(pl.multiple_of(lax.rem(m, 4) * 256, 256), 256)]

        def w_in(at, count):
            return jnp.concatenate([gi[first, at : at + count, :], gi[first + 1, at : at + count, :]], 1)

        def w_down(at, count):
            return gd[pl.ds(first, 2), :, at : at + count].reshape(256, count)

        for block in range(2):
            at = slice(block * rows, (block + 1) * rows)
            inner = dot(rows_two[at, :], w_in(0, 1024)) + bias_row
            cube = inner * inner
            bent = jnp.tanh(GELU_A * inner * (1.0 + GELU_B * cube))
            act[at, :] = (0.5 * inner * (1.0 + bent)).astype(bf)
            slope = 0.5 * (1.0 + bent) + 0.5 * inner * (1.0 - bent * bent) * (GELU_A * (1.0 + 3.0 * GELU_B * cube))
            gin[at, :] = (dot_nt(grad_rows[at, :], w_down(0, 1024)) * slope).astype(bf)
        for nb in range(4):
            at = slice(nb * 256, nb * 256 + 256)
            nacc[:, at] += dot_nt(gin[...], w_in(nb * 256, 256))
            macc[:, at] += dot(act[...], w_down(nb * 256, 256))
        bias_sum[m] = jnp.sum(gin[...].astype(f32), 0, keepdims=True)
        for k in (I, W):
            drain(k, zz, yy)
        for nb in range(4):
            at = slice(nb * 256, nb * 256 + 256)
            part = dot(rows_t[at, :], gin[...]).astype(bf)
            gi[first, at, :] = part[:, 0:LANES]
            gi[first + 1, at, :] = part[:, LANES:]
        act_t = act[...].T
        for nb in range(4):
            at = slice(nb * 256, nb * 256 + 256)
            part = dot(act_t, grad_rows[:, at]).astype(bf)
            gd[pl.ds(first, 2), :, at] = part.reshape(2, LANES, 256)
        for k in (I, W):
            rc_copy(k, zz, yy).start()

        @pl.when(e > 0)
        def _():
            before = e - 1
            for k in (I, W):
                rc_add(k, near(lax.div(before, 2)), lax.rem(y + lax.rem(before, 2), 2))

        return carry

    lax.fori_loop(0, 2 * DEPTH, ffn, 0)
    far[1] = nacc[other, :].astype(bf)
    x_part(1).start()
    for m in range(8):
        for side in range(2):
            row = 8 + 2 * side + m // 4
            vout[0, row : row + 1, m % 4 * 256 : m % 4 * 256 + 256] = jnp.where(t == side, bias_sum[m], 0.0)
    far[2] = macc[other, :].astype(bf)
    x_part(2).start()
    for k in (I, W):
        rc_add(k, near(DEPTH - 1), 1 - y)
    rows_t[...] = rows_one[...].T
    x_part(1).wait_recv()

    def row_sum(row, value):
        vout[0, row : row + 1, :] += jnp.sum(value, 0, keepdims=True)

    def second_back(at, step):
        here = pl.ds(at, step)
        in_group = pl.ds(pl.multiple_of(t * rows + at, step), step)
        grad = nacc[in_group, :] + inx[1, here, :].astype(f32)
        unit, inverse = norm(hidden[here, :])
        back = cot[here, :] + norm_grad(grad, unit, inverse, vecs[2:3, :])
        ghid[here, :] = back
        rows_two[in_group, :] = back.astype(bf)
        row_sum(2, grad * unit)
        row_sum(3, grad)
        row_sum(4, back)
        row_sum(5, cot[here, :])

    x_rows(rows_two, 2).wait_send()
    by_rows(second_back)
    x_rows(rows_two, 3).start()
    for s in range(1, 3):
        for k in (I, W):
            ry_add(k, s)
    x_part(2).wait_recv()

    def mixed_out(at, step):
        here = pl.ds(at, step)
        in_group = pl.ds(pl.multiple_of(t * rows + at, step), step)
        mixed[here, :] = hidden[here, :] + macc[in_group, :] + inx[2, here, :].astype(f32) + vecs[5:6, :]

    by_rows(mixed_out)
    for zz in range(DEPTH):
        for yy in range(2):
            drain(O, zz, yy)
            drain(Q, zz, yy)
    x_rows_wait(rows_two, 3)
    gctx[...] = dot_nt(rows_two[...], w_out(0, 8)).astype(bf)
    for nb in range(4):
        at = slice(nb * 256, nb * 256 + 256)
        go[:, :, at] = dot_tn(ctx[...], rows_two[:, at]).astype(bf).reshape(8, 64, 256)
    for zz in range(DEPTH):
        for yy in range(2):
            rc_copy(O, zz, yy).start()

    def head_back(h):
        q0, q1 = qkv[h, 0:rows, 0:128], qkv[h, rows : 2 * rows, 0:128]
        grads = []
        for block in range(2):
            at, seen = slice(block * rows, (block + 1) * rows), (block + 1) * rows
            low = probs[h, at, 0:seen]
            given = gctx[at, h * 128 : h * 128 + 128]
            prob = low.astype(f32)
            grad_probs = dot_nt(given, qkv[h, 0:seen, 256:384])
            delta = jnp.sum(prob * grad_probs, -1, keepdims=True)
            grad_scores = (prob * (grad_probs - delta)).astype(bf)
            grad_q = dot(grad_scores, qkv[h, 0:seen, 128:256]) * scale
            grad_k = dot_tn(grad_scores, q1 if block else q0) * scale
            grad_v = dot_tn(low, given)
            grads.append((grad_q, grad_k, grad_v))
        (gq0, gk0, gv0), (gq1, gk1, gv1) = grads
        top = jnp.concatenate([gq0, gk0 + gk1[0:rows], gv0 + gv1[0:rows]], 1).astype(bf)
        low_half = jnp.concatenate([gq1, gk1[rows:], gv1[rows:]], 1).astype(bf)
        qkv[h, 0:rows, :] = top
        qkv[h, rows : 2 * rows, :] = low_half
        total = jnp.sum(top.astype(f32), 0, keepdims=True) + jnp.sum(low_half.astype(f32), 0, keepdims=True)
        for side in range(2):
            vout[0, 6 + side : 7 + side, h * 256 : h * 256 + 128] = jnp.where(t == side, total[:, 0:128], 0.0)
            vout[0, 6 + side : 7 + side, h * 256 + 128 : h * 256 + 256] = jnp.where(t == side, total[:, 256:384], 0.0)
        part = dot(rows_t[...], qkv[h]).astype(bf)
        disassemble(h, part)
        for yy in range(2):
            rc_copy(Q, h, yy).start()
        product = dot_nt(qkv[h], wqkv[h])
        if h == 0:
            nacc[...] = product
        else:
            nacc[...] += product

    for h in range(DEPTH):
        head_back(h)
    far[3] = nacc[other, :].astype(bf)
    x_part(3).start()
    for k in (O, Q):
        for s in range(DEPTH):
            rc_add(k, near(s), 1 - y)
    for k in (I, W):
        ry_add(k, 3)
    for k in (O, Q):
        for s in range(DEPTH):
            rc_add(k, near(s), y)
    for k in (I, W):
        ry_add(k, 0)
    x_part(3).wait_recv()

    def first_back(at, step):
        here = pl.ds(at, step)
        in_group = pl.ds(pl.multiple_of(t * rows + at, step), step)
        grad = nacc[in_group, :] + inx[3, here, :].astype(f32)
        unit, inverse = norm(tokens[here, :])
        input_grad[here, :] = ghid[here, :] + norm_grad(grad, unit, inverse, vecs[0:1, :])
        row_sum(0, grad * unit)
        row_sum(1, grad)

    by_rows(first_back)

    stages = (x_peer, c_peer, y_peer)

    def v_copy(stage):
        return remote(vout.at[stage], vin.at[stage], v_send.at[stage], v_recv.at[stage], stages[stage])

    def vz_copy(step):
        peer = (slot_of(lax.rem(z + step, DEPTH), y, c), t)
        return remote(vout.at[3], vin.at[3 + z], v_send.at[2 + step], v_recv.at[3 + z], peer)

    v_copy(0).start()
    for k in (O, Q):
        for s in range(1, DEPTH):
            ry_add(k, s)
        if k == O:
            v_copy(0).wait_recv()
            vout[1] = vout[0] + vin[0]
            v_copy(1).start()
            ry_add(k, 0)
    v_copy(1).wait_recv()
    vout[2] = vout[1] + vin[1]
    v_copy(2).start()
    ry_add(Q, 0)
    for k in (I, W, O):
        rz_add(k)
    v_copy(2).wait_recv()
    vout[3] = vout[2] + vin[2]
    for step in range(1, DEPTH):
        vz_copy(step).start()
    vin[3 + z] = vout[3]
    rz_add(Q)
    for step in range(1, DEPTH):
        zz = lax.rem(z + step, DEPTH)
        remote(vin.at[3 + zz], vin.at[3 + zz], v_send.at[0], v_recv.at[3 + zz], y_peer).wait_recv()
    count = vec_grads.shape[0]
    total = ((vin[3] + vin[4]) + vin[5]) + vin[6]
    vec_grads[...] = total[0:count]

    for stage in range(3):
        v_copy(stage).wait_send()
    for step in range(1, DEPTH):
        vz_copy(step).wait_send()
    for index, ref in ((0, rows_one), (1, grad_rows), (3, rows_two)):
        x_rows(ref, index).wait_send()
    for index in range(4):
        x_part(index).wait_send()
    for k in range(4):
        for zz in range(DEPTH):
            for yy in range(2):
                rc_copy(k, zz, yy).wait_send()
            ry_copy(k, zz).wait_send()
        for s in range(1, DEPTH):
            rz_copy(k, near(s)).wait_send()


def run_layer(tokens, cotangent, lengths, order, weights, vec_params):
    bf, f32 = jnp.bfloat16, jnp.float32
    rows = tokens.shape[0]
    group = 2 * rows
    owners = 16
    shapes = piece_shapes()
    view = jnp.transpose(weights, (1, 2, 0))
    vmem = pl.BlockSpec(memory_space=pltpu.VMEM)
    smem = pl.BlockSpec(memory_space=pltpu.SMEM)

    def many(count):
        return [pltpu.VMEM((count,) + s, bf) for s in shapes]

    full = pltpu.VMEM((group, D), bf)
    dma = pltpu.SemaphoreType.DMA
    return pl.pallas_call(
        layer_kernel,
        out_shape=[jax.ShapeDtypeStruct((rows, D), f32)] * 2
        + [jax.ShapeDtypeStruct(s, f32) for s in shapes]
        + [jax.ShapeDtypeStruct(vec_params.shape, f32)],
        in_specs=[smem, smem, pl.BlockSpec(memory_space=pl.ANY)] + [vmem] * 3,
        out_specs=[vmem] * 7,
        scratch_shapes=[
            pltpu.VMEM((owners,) + shapes[0], bf),
            pltpu.VMEM((owners // 2, BLOCK, D), bf),
            pltpu.VMEM((owners,) + shapes[2], bf),
            pltpu.VMEM((owners,) + shapes[3], bf),
            pltpu.VMEM((DEPTH, D, 3 * HD), bf),
        ]
        + many(2 * DEPTH)
        + many(DEPTH)
        + many(DEPTH - 1)
        + [
            full,
            full,
            pltpu.VMEM((D, group), bf),
            full,
            pltpu.VMEM((DEPTH, group, group), bf),
            pltpu.VMEM((DEPTH, group, 3 * HD), bf),
            pltpu.VMEM((group, DEPTH * HD), bf),
            pltpu.VMEM((group, DEPTH * HD), bf),
            pltpu.VMEM((rows, D), f32),
            pltpu.VMEM((rows, D), f32),
            pltpu.VMEM((4, rows, D), bf),
            pltpu.VMEM((4, rows, D), bf),
            pltpu.VMEM((group, D), f32),
            pltpu.VMEM((group, D), f32),
            pltpu.VMEM((group, 256), bf),
            pltpu.VMEM((group, 256), bf),
            pltpu.VMEM((8, 1, 256), f32),
            pltpu.VMEM((7, 16, D), f32),
            pltpu.VMEM((4, 16, D), f32),
            dma((4, owners)),
            dma((4, DEPTH)),
            dma((4, 2 * DEPTH)),
            dma((4, 2, DEPTH)),
            dma((4, 2 * DEPTH)),
            dma((4, 2 * DEPTH)),
            dma((4, DEPTH)),
            dma((4, DEPTH)),
            dma((4, DEPTH - 1)),
            dma((4, DEPTH - 1)),
            dma((8,)),
            dma((8,)),
            dma((6,)),
            dma((7,)),
            dma((1,)),
        ],
        compiler_params=pltpu.CompilerParams(
            collective_id=0, has_side_effects=True, vmem_limit_bytes=VMEM_LIMIT
        ),
        name="layer",
    )(lengths, order, view, tokens, cotangent, vec_params)


def per_device(
    grp_count,
    tp_count,
    tokens,
    cotangent,
    lengths,
    order,
    weights,
    momentum,
    stat_left,
    stat_right,
    root_left,
    root_right,
    vec_params,
    vec_momentum,
    vec_second,
):
    fits = grp_count == 4 * DEPTH and tp_count == 2 and tokens.shape[0] == 256
    if not fits or lengths.shape[1] != ARTICLES:
        return per_device_general(
            tokens,
            cotangent,
            lengths,
            order,
            weights,
            momentum,
            stat_left,
            stat_right,
            root_left,
            root_right,
            vec_params,
            vec_momentum,
            vec_second,
        )
    token_total = tokens.shape[0] * tp_count * grp_count
    mixed, input_grad, *sums, vec_grads = run_layer(tokens, cotangent, lengths, order, weights, vec_params)
    blocks, vecs, results = update_blocks(
        sums,
        (weights, momentum, stat_left, stat_right, root_left, root_right),
        vec_grads,
        (vec_params, vec_momentum, vec_second),
        (mixed, input_grad),
        token_total,
    )
    return (*results, *blocks, *vecs)


def solution(mesh):
    placed = (
        P(("grp", "tp"), None),
        P(("grp", "tp"), None),
        P("grp", None),
        P("grp", None),
        P(("tp", "grp"), None, None),
        P(("tp", "grp"), None, None),
        P(("tp", "grp"), None, None),
        P(("tp", "grp"), None, None),
        P(("tp", "grp"), None, None),
        P(("tp", "grp"), None, None),
        P(),
        P(),
        P(),
    )
    return jax.shard_map(
        functools.partial(per_device, mesh.shape["grp"], mesh.shape["tp"]),
        mesh=mesh,
        in_specs=placed,
        out_specs=(
            P(("grp", "tp"), None),
            P(("grp", "tp"), None),
            P(("tp", "grp"), None, None),
            P(("tp", "grp"), None, None),
            P(("tp", "grp"), None, None),
            P(("tp", "grp"), None, None),
            P(("tp", "grp"), None, None),
            P(),
            P(),
            P(),
            P(),
        ),
        check_vma=False,
    )
```

```python
import functools

import jax
import jax.numpy as jnp
from jax import lax
from jax.experimental import pallas as pl
from jax.experimental.pallas import tpu as pltpu
from jax.sharding import PartitionSpec as P

D = 1024
HEADS = 8
HD = 128
FF = 4096
BLOCK = 64


EPS = 1e-05
NEG = -1e30
DECAY = 0.9
BETA = 0.9
RATE = 0.05
VEC_DECAY = 0.9
VEC_RATE = 0.2
VEC_EPS = 1e-08


def norm_rows(value, gain, shift):
    average = jnp.mean(value, -1, keepdims=True)
    centred = value - average
    inverse = lax.rsqrt(jnp.mean(centred * centred, -1, keepdims=True) + EPS)
    normed = centred * inverse
    return (normed * gain + shift, normed, inverse)


def norm_back(grad_out, normed, inverse, gain):
    scaled = grad_out * gain
    return inverse * (
        scaled
        - jnp.mean(scaled, -1, keepdims=True)
        - normed * jnp.mean(scaled * normed, -1, keepdims=True)
    )


def segment_ids(lengths_row, order_row, group_rows):
    article_count = lengths_row.shape[0]
    slots = jnp.arange(article_count, dtype=jnp.int32)
    picks = (order_row[:, None] == slots[None, :]).astype(jnp.int32)
    packed = jnp.sum(picks * lengths_row[None, :], 1)
    ends = jnp.cumsum(packed)
    spots = jnp.arange(group_rows, dtype=jnp.int32)
    return jnp.sum((spots[:, None] >= ends[None, :]).astype(jnp.int32), 1)


def allowed_mask(row_ids, row_segs, segments, key_ids, article_count):
    causal = key_ids[None, :] <= row_ids[:, None]
    same = segments[None, :] == row_segs[:, None]
    alone = (row_segs[:, None] < article_count) | (key_ids[None, :] == row_ids[:, None])
    return causal & same & alone


def from_columns(tiles, row_total, col_total):
    return (
        tiles.reshape(col_total // BLOCK, row_total // BLOCK, BLOCK, BLOCK)
        .transpose(1, 2, 0, 3)
        .reshape(row_total, col_total)
    )


def from_rows(tiles, row_total, col_total):
    return (
        tiles.reshape(row_total // BLOCK, col_total // BLOCK, BLOCK, BLOCK)
        .transpose(0, 2, 1, 3)
        .reshape(row_total, col_total)
    )


def to_columns(matrix):
    row_total, col_total = matrix.shape
    return (
        matrix.reshape(row_total // BLOCK, BLOCK, col_total // BLOCK, BLOCK)
        .transpose(2, 0, 1, 3)
        .reshape(-1, BLOCK, BLOCK)
    )


def to_rows(matrix):
    row_total, col_total = matrix.shape
    return (
        matrix.reshape(row_total // BLOCK, BLOCK, col_total // BLOCK, BLOCK)
        .transpose(0, 2, 1, 3)
        .reshape(-1, BLOCK, BLOCK)
    )


def per_device_general(
    tokens,
    cotangent,
    lengths,
    order,
    weights,
    momentum,
    stat_left,
    stat_right,
    root_left,
    root_right,
    vec_params,
    vec_momentum,
    vec_second,
):
    groups = lax.axis_size("grp")
    tp_size = lax.axis_size("tp")
    tp_rank = lax.axis_index("tp")
    tok_rows = tokens.shape[0]
    group_rows = tok_rows * tp_size
    article_count = lengths.shape[1]
    owners = groups * tp_size
    block_area = BLOCK * BLOCK * owners
    qkv_count = 3 * D * D // block_area
    out_count = D * D // block_area
    in_count = D * FF // block_area
    owned_blocks = weights.shape[0]
    heads_here = HEADS // tp_size
    qkv_cols = 3 * D // tp_size
    feat_here = D // tp_size
    ff_here = FF // tp_size
    qv_width = 2 * D // tp_size
    token_total = group_rows * groups
    gathered = lax.all_gather(weights.astype(jnp.bfloat16), "grp", axis=0, tiled=True)
    per_owner = gathered.reshape(groups, owned_blocks, BLOCK, BLOCK)
    marks = [0, qkv_count, qkv_count + out_count, qkv_count + out_count + in_count, owned_blocks]
    pieces = [
        per_owner[:, marks[index] : marks[index + 1]].reshape(-1, BLOCK, BLOCK)
        for index in range(4)
    ]
    w_qkv = from_columns(pieces[0], D, qkv_cols)
    w_out = from_rows(pieces[1], feat_here, D)
    w_in = from_columns(pieces[2], D, ff_here)
    w_down = from_rows(pieces[3], ff_here, D)
    w_qkv_heads = w_qkv.reshape(D, heads_here, 3, HD)
    w_out_heads = w_out.reshape(heads_here, HD, D)
    segments = segment_ids(lengths[0], order[0], group_rows)
    gain_one = vec_params[0]
    shift_one = vec_params[1]
    gain_two = vec_params[2]
    shift_two = vec_params[3]
    bias_out = vec_params[4]
    bias_down = vec_params[5]
    qv_here = lax.dynamic_slice_in_dim(
        vec_params[6:8].reshape(2 * D), tp_rank * qv_width, qv_width
    ).reshape(heads_here, 2, HD)
    bias_heads = jnp.stack(
        [qv_here[:, 0], jnp.zeros((heads_here, HD), jnp.float32), qv_here[:, 1]], 0
    )[:, :, None, :]
    bias_in = lax.dynamic_slice_in_dim(vec_params[8:].reshape(FF), tp_rank * ff_here, ff_here)
    normed_one, unit_one, inverse_one = norm_rows(tokens, gain_one, shift_one)
    rows_one = lax.all_gather(normed_one.astype(jnp.bfloat16), "tp", axis=0, tiled=True)
    projected = (
        jnp.einsum("rx,xhcd->chrd", rows_one, w_qkv_heads, preferred_element_type=jnp.float32)
        + bias_heads
    ).astype(jnp.bfloat16)
    queries = projected[0]
    keys_all = projected[1]
    values_all = projected[2]
    span = min(512, group_rows)
    starts = jnp.arange(group_rows // span, dtype=jnp.int32) * span
    key_ids = jnp.arange(group_rows, dtype=jnp.int32)
    score_scale = HD ** (-0.5)

    def masked_scores(first_row):
        row_ids = first_row + jnp.arange(span, dtype=jnp.int32)
        row_segs = lax.dynamic_slice_in_dim(segments, first_row, span, 0)
        allowed = allowed_mask(row_ids, row_segs, segments, key_ids, article_count)
        query_rows = lax.dynamic_slice_in_dim(queries, first_row, span, 1)
        scores = (
            jnp.einsum("hqd,hkd->hqk", query_rows, keys_all, preferred_element_type=jnp.float32)
            * score_scale
        )
        return (jnp.where(allowed[None], scores, NEG), query_rows)

    def attend(context_buf, first_row):
        scores, query_rows = masked_scores(first_row)
        row_max = jnp.max(scores, -1, keepdims=True)
        expo = jnp.exp(scores - row_max)
        expsum = jnp.sum(expo, -1, keepdims=True)
        probs_low = (expo / expsum).astype(jnp.bfloat16)
        context = jnp.einsum(
            "hqk,hkd->hqd", probs_low, values_all, preferred_element_type=jnp.float32
        ).astype(jnp.bfloat16)
        context_buf = lax.dynamic_update_slice_in_dim(context_buf, context, first_row, 1)
        return (context_buf, (row_max + jnp.log(expsum))[:, :, 0])

    context_low, log_norm = lax.scan(
        attend, jnp.zeros((heads_here, group_rows, HD), jnp.bfloat16), starts
    )
    attn_sum = lax.psum_scatter(
        jnp.einsum(
            "hrd,hde->re", context_low, w_out_heads, preferred_element_type=jnp.float32
        ).astype(jnp.bfloat16),
        "tp",
        scatter_dimension=0,
        tiled=True,
    ).astype(jnp.float32)
    hidden = tokens + attn_sum + bias_out
    normed_two, unit_two, inverse_two = norm_rows(hidden, gain_two, shift_two)
    rows_two = lax.all_gather(normed_two.astype(jnp.bfloat16), "tp", axis=0, tiled=True)
    inner = jnp.dot(rows_two, w_in, preferred_element_type=jnp.float32) + bias_in
    activ, gelu_pull = jax.vjp(jax.nn.gelu, inner)
    activ_low = activ.astype(jnp.bfloat16)
    mixed = (
        hidden
        + lax.psum_scatter(
            jnp.dot(activ_low, w_down, preferred_element_type=jnp.float32).astype(jnp.bfloat16),
            "tp",
            scatter_dimension=0,
            tiled=True,
        ).astype(jnp.float32)
        + bias_down
    )
    grad_low = cotangent.astype(jnp.bfloat16)
    grad_rows = lax.all_gather(grad_low, "tp", axis=0, tiled=True)
    g_down = jnp.einsum("rf,rd->fd", activ_low, grad_rows, preferred_element_type=jnp.float32)
    grad_activ = jnp.einsum("rd,fd->rf", grad_rows, w_down, preferred_element_type=jnp.float32)
    grad_inner = gelu_pull(grad_activ)[0].astype(jnp.bfloat16)
    g_in = jnp.einsum("rd,rf->df", rows_two, grad_inner, preferred_element_type=jnp.float32)
    g_bias_in = jnp.sum(grad_inner.astype(jnp.float32), 0)
    ffn_blocks = jnp.concatenate(
        [
            to_columns(g_in).reshape(groups, in_count, BLOCK, BLOCK),
            to_rows(g_down).reshape(groups, in_count, BLOCK, BLOCK),
        ],
        1,
    )
    grad_normed_two = lax.psum_scatter(
        jnp.einsum("rf,df->rd", grad_inner, w_in, preferred_element_type=jnp.float32).astype(
            jnp.bfloat16
        ),
        "tp",
        scatter_dimension=0,
        tiled=True,
    ).astype(jnp.float32)
    grad_hidden = cotangent + norm_back(grad_normed_two, unit_two, inverse_two, gain_two)
    grad_attn_low = grad_hidden.astype(jnp.bfloat16)
    grad_attn_rows = lax.all_gather(grad_attn_low, "tp", axis=0, tiled=True)
    g_out = jnp.einsum(
        "hrd,re->hde", context_low, grad_attn_rows, preferred_element_type=jnp.float32
    ).reshape(feat_here, D)
    grad_context = jnp.einsum(
        "re,hde->hrd", grad_attn_rows, w_out_heads, preferred_element_type=jnp.float32
    ).astype(jnp.bfloat16)
    zero_heads = jnp.zeros((heads_here, group_rows, HD), jnp.float32)

    def attend_back(carry, inputs):
        grad_queries, grad_keys, grad_values = carry
        first_row, log_block = inputs
        scores, query_rows = masked_scores(first_row)
        probs = jnp.exp(scores - log_block[:, :, None])
        grad_ctx_rows = lax.dynamic_slice_in_dim(grad_context, first_row, span, 1)
        grad_probs = jnp.einsum(
            "hqd,hkd->hqk", grad_ctx_rows, values_all, preferred_element_type=jnp.float32
        )
        delta = jnp.sum(probs * grad_probs, -1, keepdims=True)
        grad_scores = (probs * (grad_probs - delta)).astype(jnp.bfloat16)
        query_part = (
            jnp.einsum("hqk,hkd->hqd", grad_scores, keys_all, preferred_element_type=jnp.float32)
            * score_scale
        )
        grad_queries = lax.dynamic_update_slice_in_dim(grad_queries, query_part, first_row, 1)
        grad_keys = (
            grad_keys
            + jnp.einsum(
                "hqk,hqd->hkd", grad_scores, query_rows, preferred_element_type=jnp.float32
            )
            * score_scale
        )
        grad_values = grad_values + jnp.einsum(
            "hqk,hqd->hkd",
            probs.astype(jnp.bfloat16),
            grad_ctx_rows,
            preferred_element_type=jnp.float32,
        )
        return ((grad_queries, grad_keys, grad_values), None)

    (grad_queries, grad_keys, grad_values), unused = lax.scan(
        attend_back, (zero_heads, zero_heads, zero_heads), (starts, log_norm)
    )
    grad_proj = jnp.stack([grad_queries, grad_keys, grad_values], 0).astype(jnp.bfloat16)
    proj_sums = jnp.sum(grad_proj.astype(jnp.float32), 2)
    g_bias_qv = jnp.stack([proj_sums[0], proj_sums[2]], 1).reshape(qv_width)
    g_qkv = jnp.einsum(
        "rx,chrd->xhcd", rows_one, grad_proj, preferred_element_type=jnp.float32
    ).reshape(D, qkv_cols)
    grad_normed_one = lax.psum_scatter(
        jnp.einsum(
            "chrd,xhcd->rx", grad_proj, w_qkv_heads, preferred_element_type=jnp.float32
        ).astype(jnp.bfloat16),
        "tp",
        scatter_dimension=0,
        tiled=True,
    ).astype(jnp.float32)
    input_grad = grad_hidden + norm_back(grad_normed_one, unit_one, inverse_one, gain_one)
    local_rows = jnp.stack(
        [
            jnp.sum(grad_normed_one * unit_one, 0),
            jnp.sum(grad_normed_one, 0),
            jnp.sum(grad_normed_two * unit_two, 0),
            jnp.sum(grad_normed_two, 0),
            jnp.sum(grad_hidden, 0),
            jnp.sum(cotangent, 0),
        ]
    )
    qv_rows = lax.dynamic_update_slice(
        jnp.zeros((2 * D,), jnp.float32), g_bias_qv, (tp_rank * qv_width,)
    ).reshape(2, D)
    in_rows = lax.dynamic_update_slice(
        jnp.zeros((FF,), jnp.float32), g_bias_in, (tp_rank * ff_here,)
    ).reshape(FF // D, D)
    vec_grads = lax.psum(jnp.concatenate([local_rows, qv_rows, in_rows], 0), ("grp", "tp"))
    attn_blocks = jnp.concatenate(
        [
            to_columns(g_qkv).reshape(groups, qkv_count, BLOCK, BLOCK),
            to_rows(g_out).reshape(groups, out_count, BLOCK, BLOCK),
        ],
        1,
    )
    every_block = jnp.concatenate([attn_blocks, ffn_blocks], 1).reshape(-1, BLOCK, BLOCK)
    weight_grads = lax.psum_scatter(
        every_block.astype(jnp.bfloat16), "grp", scatter_dimension=0, tiled=True
    ).astype(jnp.float32)
    scaled = weight_grads * token_total ** (-0.5)
    stat_left_new = DECAY * stat_left + (1.0 - DECAY) * jnp.einsum(
        "nij,nkj->nik", scaled, scaled, precision=lax.Precision.HIGHEST
    )
    stat_right_new = DECAY * stat_right + (1.0 - DECAY) * jnp.einsum(
        "nji,njk->nik", scaled, scaled, precision=lax.Precision.HIGHEST
    )
    shaped = jnp.einsum("nij,njk->nik", root_left, scaled, precision=lax.Precision.HIGHEST)
    shaped = jnp.einsum("nij,njk->nik", shaped, root_right, precision=lax.Precision.HIGHEST)
    momentum_new = BETA * momentum + shaped
    weights_new = weights - RATE * momentum_new
    vec_scaled = vec_grads * token_total ** (-0.5)
    vec_second_new = VEC_DECAY * vec_second + (1.0 - VEC_DECAY) * vec_scaled * vec_scaled
    vec_momentum_new = BETA * vec_momentum + vec_scaled * lax.rsqrt(vec_second_new + VEC_EPS)
    vec_new = vec_params - VEC_RATE * vec_momentum_new
    return (
        mixed,
        input_grad,
        weight_grads,
        stat_left_new,
        stat_right_new,
        momentum_new,
        weights_new,
        vec_grads,
        vec_second_new,
        vec_momentum_new,
        vec_new,
    )


MESH_ID = pl.DeviceIdType.MESH
LANES = 128
HALF = 64
VMEM_LIMIT = 62 * 2**20
ARTICLES = 4
GELU_A = (2.0 / 3.141592653589793) ** 0.5
GELU_B = 0.044715


def remote(src, dst, send_sem, recv_sem, device):
    return pltpu.make_async_remote_copy(
        src_ref=src,
        dst_ref=dst,
        send_sem=send_sem,
        recv_sem=recv_sem,
        device_id=device,
        device_id_type=MESH_ID,
    )


def place():
    grp = lax.axis_index("grp")
    return lax.div(grp, 4), lax.rem(lax.div(grp, 2), 2), lax.rem(grp, 2), lax.axis_index("tp")


def slot_of(z, y, c):
    return z * 4 + y * 2 + c


def lay_blocks(view_ref, stack):
    count = view_ref.shape[2]

    def row(i, carry):
        stack[pl.ds(i, count, stride=BLOCK), 0:HALF] = view_ref[i].T
        return carry

    lax.fori_loop(0, BLOCK, row, 0, unroll=8)


def piece_shapes():
    return ((768, LANES), (64, 512), (1024, LANES), (LANES, 1024))


def fold_tiles(value, mask):
    kept = jnp.where(mask, value, 0.0)
    halves = kept[:, :LANES] + kept[:, LANES:]
    return halves + pltpu.roll(halves, HALF, 1)


def update_kernel(
    scale,
    sum_q,
    sum_o,
    sum_i,
    sum_d,
    root_l,
    root_r,
    vec_g,
    vecs,
    vec_m,
    vec_s,
    mixed,
    input_grad,
    w,
    m,
    sl,
    sr,
    out_g,
    out_sl,
    out_sr,
    out_m,
    out_w,
    out_vg,
    out_vs,
    out_vm,
    out_v,
    out_mixed,
    out_input_grad,
    first,
    second,
):
    count = root_l.shape[2]
    bf = jnp.bfloat16
    out_mixed[...] = mixed[...]
    out_input_grad[...] = input_grad[...]

    @pl.when(pl.program_id(0) == 0)
    def _():
        total = vec_g[...]
        out_vg[...] = total
        scaled = total * scale
        fresh = VEC_DECAY * vec_s[...] + (1.0 - VEC_DECAY) * scaled * scaled
        out_vs[...] = fresh
        momentum = BETA * vec_m[...] + scaled * lax.rsqrt(fresh + VEC_EPS)
        out_vm[...] = momentum
        out_v[...] = vecs[...] - VEC_RATE * momentum
        rows = sum_q.shape[0]
        first[0:rows, 0:HALF] = sum_q[:, 0:HALF]
        first[rows : 2 * rows, 0:HALF] = sum_q[:, HALF:LANES]
        base = 2 * rows
        for b in range(8):
            first[base + b * 64 : base + b * 64 + 64, 0:HALF] = sum_o[:, b * HALF : (b + 1) * HALF]
        base += 512
        first[base : base + 1024, 0:HALF] = sum_i[:, 0:HALF]
        first[base + 1024 : base + 2048, 0:HALF] = sum_i[:, HALF:LANES]
        base += 2048
        for r in range(2):
            for b in range(16):
                at = base + (r * 16 + b) * 64
                first[at : at + 64, 0:HALF] = sum_d[r * 64 : r * 64 + 64, b * HALF : (b + 1) * HALF]

        def row(i, carry):
            both = jnp.concatenate([root_l[i], root_r[i]], 0)
            second[pl.ds(i, count, stride=BLOCK), :] = both.T
            return carry

        lax.fori_loop(0, BLOCK, row, 0, unroll=8)
        row_id = lax.broadcasted_iota(jnp.int32, (256, 256), 0)
        col_id = lax.broadcasted_iota(jnp.int32, (256, 256), 1)
        mask = lax.shift_right_logical(row_id, 6) == lax.shift_right_logical(col_id, 6)
        zero = jnp.zeros((256, 256), jnp.float32)

        def spread(v):
            return jnp.where(mask, jnp.concatenate([v, v, v, v], 1), zero).astype(bf)

        def four(k, carry):
            at = pl.ds(pl.multiple_of(k * 256, 256), 256)
            s32 = first[at, 0:HALF] * scale
            s = s32.astype(bf)
            left = second[at, 0:HALF]
            right = second[at, HALF:LANES].astype(bf)
            outer = lax.dot_general(s, s, (((1,), (1,)), ((), ())), preferred_element_type=jnp.float32)
            inner = lax.dot_general(spread(s32), s, (((0,), (0,)), ((), ())), preferred_element_type=jnp.float32)
            shaped = jnp.dot(spread(left), s, preferred_element_type=jnp.float32)
            shaped = jnp.dot(spread(shaped), right, preferred_element_type=jnp.float32)
            first[at, HALF:LANES] = fold_tiles(outer, mask)[:, HALF:LANES]
            second[at, 0:HALF] = inner
            second[at, HALF:LANES] = shaped
            return carry

        lax.fori_loop(0, count // 4, four, 0, unroll=4)

    i0 = pl.program_id(0) * w.shape[0]

    def rows_out(ii, carry):
        at = pl.ds(i0 + ii, count, stride=BLOCK)
        one = first[at, :].T
        two = second[at, :].T
        out_g[ii] = one[0:HALF]
        out_sl[ii] = DECAY * sl[ii] + (1.0 - DECAY) * one[HALF:LANES]
        out_sr[ii] = DECAY * sr[ii] + (1.0 - DECAY) * two[0:HALF]
        fresh = BETA * m[ii] + two[HALF:LANES]
        out_m[ii] = fresh
        out_w[ii] = w[ii] - RATE * fresh
        return carry

    lax.fori_loop(0, w.shape[0], rows_out, 0, unroll=True)


def update_blocks(sums, blocks, vec_grads, vecs, results, token_total):
    views = [jnp.transpose(a, (1, 2, 0)) for a in blocks]
    count = blocks[0].shape[0]
    rows = 8
    whole = pl.BlockSpec(memory_space=pltpu.VMEM)
    steps = BLOCK // rows
    some = pl.BlockSpec((results[0].shape[0] // steps, results[0].shape[1]), lambda i: (i, 0))
    part = pl.BlockSpec((rows, BLOCK, count), lambda i: (i, 0, 0))
    vec = jax.ShapeDtypeStruct(vec_grads.shape, jnp.float32)
    outs = pl.pallas_call(
        functools.partial(update_kernel, token_total ** (-0.5)),
        grid=(steps,),
        out_shape=[jax.ShapeDtypeStruct((BLOCK, BLOCK, count), jnp.float32)] * 5
        + [vec] * 4
        + [jax.ShapeDtypeStruct(a.shape, a.dtype) for a in results],
        in_specs=[whole] * 10 + [some] * 2 + [part] * 4,
        out_specs=[part] * 5 + [whole] * 4 + [some] * 2,
        scratch_shapes=[
            pltpu.VMEM((count * BLOCK, LANES), jnp.float32),
            pltpu.VMEM((count * BLOCK, LANES), jnp.float32),
        ],
        compiler_params=pltpu.CompilerParams(vmem_limit_bytes=VMEM_LIMIT),
        name="update_blocks",
    )(*sums, *views[4:], vec_grads, *vecs, *results, *views[:4])
    return [jnp.transpose(a, (2, 0, 1)) for a in outs[:5]], outs[5:9], outs[9:]


DEPTH = 4


def layer_kernel(
    lengths,
    order,
    view,
    tokens,
    cot,
    vecs,
    mixed,
    input_grad,
    sum_q,
    sum_o,
    sum_i,
    sum_d,
    vec_grads,
    gq,
    go,
    gi,
    gd,
    wqkv,
    cq,
    co,
    ci,
    cd,
    yq,
    yo,
    yi,
    yd,
    zq,
    zo,
    zi,
    zd,
    rows_one,
    rows_two,
    rows_t,
    grad_rows,
    probs,
    qkv,
    ctx,
    gctx,
    hidden,
    ghid,
    far,
    inx,
    macc,
    nacc,
    act,
    gin,
    bias_sum,
    vin,
    vout,
    recv,
    send_y,
    send_c,
    send_z,
    rc_recv,
    rc_send,
    ry_recv,
    ry_send,
    rz_recv,
    rz_send,
    x_send,
    x_recv,
    v_send,
    v_recv,
    copy_sem,
):
    bf, f32 = jnp.bfloat16, jnp.float32
    z, y, c, t = place()
    me = slot_of(z, y, c)
    x_peer = (me, 1 - t)
    y_peer = (slot_of(z, 1 - y, c), t)
    c_peer = (slot_of(z, y, 1 - c), t)
    rows = tokens.shape[0]
    own = pl.ds(pl.multiple_of(t * rows, rows), rows)
    other = pl.ds(pl.multiple_of((1 - t) * rows, rows), rows)
    gathered, core_in, y_in, z_in = (gq, go, gi, gd), (cq, co, ci, cd), (yq, yo, yi, yd), (zq, zo, zi, zd)
    sums = (sum_q, sum_o, sum_i, sum_d)
    Q, O, I, W = range(4)

    def dot(a, b):
        return jnp.dot(a, b, preferred_element_type=f32)

    def dot_nt(a, b):
        return lax.dot_general(a, b, (((1,), (1,)), ((), ())), preferred_element_type=f32)

    def dot_tn(a, b):
        return lax.dot_general(a, b, (((0,), (0,)), ((), ())), preferred_element_type=f32)

    def piece(k, zz, yy, cc):
        if k == O:
            return go.at[zz * 2 + yy, :, pl.ds(pl.multiple_of(cc * 512, 512), 512)]
        return gathered[k].at[slot_of(zz, yy, cc)]

    def near(s):
        return lax.rem(z + (1 - 2 * lax.div(z, 2)) * s + DEPTH, DEPTH)

    def ag_copy(k, zz, yy, way):
        src = piece(k, zz, yy, c)
        sem = recv.at[k, slot_of(zz, yy, c)]
        if way == "up":
            return remote(src, src, send_z.at[k, 0, zz], sem, (slot_of(z + 1, y, c), t))
        if way == "down":
            return remote(src, src, send_z.at[k, 1, zz], sem, (slot_of(z - 1, y, c), t))
        if way == "y":
            return remote(src, src, send_y.at[k, zz], sem, y_peer)
        return remote(src, src, send_c.at[k, yy * DEPTH + zz], sem, c_peer)

    def ag_wait(k, zz, yy, cc):
        ref = piece(k, zz, yy, cc)
        remote(ref, ref, send_y.at[k, 0], recv.at[k, slot_of(zz, yy, cc)], y_peer).wait_recv()

    def own_sends(k):
        @pl.when(z < DEPTH - 1)
        def _():
            ag_copy(k, z, y, "up").start()

        @pl.when(z > 0)
        def _():
            ag_copy(k, z, y, "down").start()

        ag_copy(k, z, y, "y").start()
        ag_copy(k, z, y, "core").start()

    def z_arrival(kinds, dist):
        @pl.when(z >= dist)
        def _():
            for k in kinds:
                ag_wait(k, z - dist, y, c)

                @pl.when(z < DEPTH - 1)
                def _():
                    ag_copy(k, z - dist, y, "up").start()

                ag_copy(k, z - dist, y, "y").start()
                ag_copy(k, z - dist, y, "core").start()

        @pl.when(z + dist < DEPTH)
        def _():
            for k in kinds:
                ag_wait(k, z + dist, y, c)

                @pl.when(z > 0)
                def _():
                    ag_copy(k, z + dist, y, "down").start()

                ag_copy(k, z + dist, y, "y").start()
                ag_copy(k, z + dist, y, "core").start()

    def y_arrival(kinds, dist):
        def one(zz):
            for k in kinds:
                ag_wait(k, zz, 1 - y, c)
                ag_copy(k, zz, 1 - y, "core").start()

        if dist == 0:
            one(z)
            return

        @pl.when(z >= dist)
        def _():
            one(z - dist)

        @pl.when(z + dist < DEPTH)
        def _():
            one(z + dist)

    def drain(k, zz, yy):
        ag_copy(k, zz, yy, "core").wait_send()

        @pl.when(yy == y)
        def _():
            ag_copy(k, zz, y, "y").wait_send()

            @pl.when((zz <= z) & (z < DEPTH - 1))
            def _():
                ag_copy(k, zz, y, "up").wait_send()

            @pl.when((zz >= z) & (z > 0))
            def _():
                ag_copy(k, zz, y, "down").wait_send()

    def add(dst, first, second):
        count, width = dst.shape
        step = min(count, 256 * LANES // width)

        def body(i, carry):
            at = pl.ds(pl.multiple_of(i * step, 16), step)
            dst[at, :] = (first[at, :].astype(f32) + second[at, :].astype(f32)).astype(dst.dtype)
            return carry

        lax.fori_loop(0, count // step, body, 0)

    def rc_copy(k, zz, yy):
        at = zz * 2 + yy
        return remote(piece(k, zz, yy, 1 - c), core_in[k].at[at], rc_send.at[k, at], rc_recv.at[k, at], c_peer)

    def ry_copy(k, zz):
        return remote(piece(k, zz, 1 - y, c), y_in[k].at[zz], ry_send.at[k, zz], ry_recv.at[k, zz], y_peer)

    def rz_copy(k, zz):
        step = lax.rem(zz - z + DEPTH, DEPTH)
        at = DEPTH - 1 - step
        return remote(
            piece(k, zz, y, c), z_in[k].at[at], rz_send.at[k, step - 1], rz_recv.at[k, at], (slot_of(zz, y, c), t)
        )

    def rc_add(k, zz, yy):
        at = zz * 2 + yy
        remote(core_in[k].at[at], core_in[k].at[at], rc_send.at[k, 0], rc_recv.at[k, at], c_peer).wait_recv()
        mine = piece(k, zz, yy, c)
        add(mine, mine, core_in[k].at[at])

        @pl.when(yy != y)
        def _():
            ry_copy(k, zz).start()

    def ry_add(k, s):
        zz = near(s)
        remote(y_in[k].at[zz], y_in[k].at[zz], ry_send.at[k, 0], ry_recv.at[k, zz], y_peer).wait_recv()
        mine = piece(k, zz, y, c)
        if s == 0:
            add(sums[k], mine, y_in[k].at[zz])
        else:
            add(mine, mine, y_in[k].at[zz])
            rz_copy(k, zz).start()

    def rz_add(k):
        for at in range(DEPTH - 1):
            remote(z_in[k].at[at], z_in[k].at[at], rz_send.at[k, 0], rz_recv.at[k, at], y_peer).wait_recv()
            add(sums[k], sums[k], z_in[k].at[at])

    def x_rows(ref, index):
        return remote(ref.at[own], ref.at[own], x_send.at[index], x_recv.at[index], x_peer)

    def x_rows_wait(ref, index):
        remote(ref.at[other], ref.at[other], x_send.at[index], x_recv.at[index], x_peer).wait_recv()

    def x_part(index):
        return remote(far.at[index], inx.at[index], x_send.at[4 + index], x_recv.at[4 + index], x_peer)

    def by_rows(body, step=64):
        def run(i, carry):
            body(pl.multiple_of(i * step, step), step)
            return carry

        lax.fori_loop(0, rows // step, run, 0)

    def norm(value):
        average = jnp.mean(value, -1, keepdims=True)
        centred = value - average
        inverse = lax.rsqrt(jnp.mean(centred * centred, -1, keepdims=True) + EPS)
        return centred * inverse, inverse

    def norm_grad(grad, unit, inverse, gain):
        scaled = grad * gain
        return inverse * (
            scaled - jnp.mean(scaled, -1, keepdims=True) - unit * jnp.mean(scaled * unit, -1, keepdims=True)
        )

    barrier = pltpu.get_barrier_semaphore()
    z_peers = [(slot_of(lax.rem(z + step, DEPTH), y, c), t) for step in range(1, DEPTH)]
    everyone = [x_peer, y_peer, c_peer] + z_peers
    for device in everyone:
        pl.semaphore_signal(barrier, inc=1, device_id=device, device_id_type=MESH_ID)

    def prepare(held, stack):
        load = pltpu.make_async_copy(view, held, copy_sem.at[0])
        load.start()

        def first_norm(at, step):
            unit, inverse = norm(tokens[pl.ds(at, step), :])
            to = pl.ds(pl.multiple_of(t * rows + at, step), step)
            rows_one[to, :] = (unit * vecs[0:1, :] + vecs[1:2, :]).astype(bf)
            grad_rows[to, :] = cot[pl.ds(at, step), :].astype(bf)

        by_rows(first_norm)
        pl.semaphore_wait(barrier, len(everyone))
        x_rows(rows_one, 0).start()
        load.wait()
        lay_blocks(held, stack)
        n = gq.shape[1]
        gq[me, :, 0:HALF] = stack[0:n, 0:HALF].astype(bf)
        gq[me, :, HALF:LANES] = stack[n : 2 * n, 0:HALF].astype(bf)
        own_sends(Q)
        base = 2 * n
        wide = [stack[base + b * 64 : base + b * 64 + 64, 0:HALF] for b in range(8)]
        go[z * 2 + y, :, pl.ds(pl.multiple_of(c * 512, 512), 512)] = jnp.concatenate(wide, 1).astype(bf)
        own_sends(O)
        base += 512
        gi[me, :, 0:HALF] = stack[base : base + 1024, 0:HALF].astype(bf)
        gi[me, :, HALF:LANES] = stack[base + 1024 : base + 2048, 0:HALF].astype(bf)
        base += 2048
        for r in range(2):
            for b in range(16):
                at = base + (r * 16 + b) * 64
                gd[me, r * 64 : r * 64 + 64, b * HALF : (b + 1) * HALF] = stack[at : at + 64, 0:HALF].astype(bf)

    pl.run_scoped(
        prepare,
        pltpu.VMEM(view.shape, f32),
        pltpu.VMEM((view.shape[2] * BLOCK, LANES), f32),
    )
    for dist in range(1, DEPTH):
        z_arrival((Q,), dist)
    x_rows(grad_rows, 1).start()
    own_sends(I)
    own_sends(W)
    for dist in range(DEPTH):
        y_arrival((Q,), dist)
    for dist in range(1, DEPTH):
        z_arrival((O,), dist)
    for zz in range(DEPTH):
        for yy in range(2):
            ag_wait(Q, zz, yy, 1 - c)
    x_rows_wait(rows_one, 0)

    ends = []
    for p in range(ARTICLES):
        length = 0
        for a in range(ARTICLES):
            length = length + jnp.where(order[0, p] == a, lengths[0, a], 0)
        ends.append(length + ends[-1] if p else length)

    def allowed(first, count):
        ids = lax.broadcasted_iota(jnp.int32, (rows, 1), 0) + first
        start = jnp.zeros((rows, 1), jnp.int32)
        for end in ends:
            start = jnp.where(ids >= end, end, start)
        start = jnp.where(ids >= ends[-1], ids, start)
        keys = lax.broadcasted_iota(jnp.int32, (rows, count), 1)
        return (keys <= ids) & (keys >= start)

    scale = HD ** (-0.5)
    strip = 1024

    def assemble(h):
        for yy in range(2):
            even, odd = gq.at[slot_of(h, yy, 0)], gq.at[slot_of(h, yy, 1)]
            at = yy * 192
            wqkv[h, 0:768, at : at + 64] = even[:, 0:64]
            wqkv[h, 768:1024, at : at + 64] = even[0:256, 64:128]
            wqkv[h, 0:512, at + 64 : at + 128] = even[256:768, 64:128]
            wqkv[h, 512:1024, at + 64 : at + 128] = odd[0:512, 0:64]
            wqkv[h, 0:256, at + 128 : at + 192] = odd[512:768, 0:64]
            wqkv[h, 256:1024, at + 128 : at + 192] = odd[:, 64:128]

    def disassemble(h, value):
        for yy in range(2):
            even, odd = gq.at[slot_of(h, yy, 0)], gq.at[slot_of(h, yy, 1)]
            at = yy * 192
            even[:, 0:64] = value[0:768, at : at + 64]
            even[0:256, 64:128] = value[768:1024, at : at + 64]
            even[256:768, 64:128] = value[0:512, at + 64 : at + 128]
            odd[0:512, 0:64] = value[512:1024, at + 64 : at + 128]
            odd[512:768, 0:64] = value[0:256, at + 128 : at + 192]
            odd[:, 64:128] = value[256:1024, at + 128 : at + 192]

    qv = vecs[pl.ds(6 + t, 1), :]

    def head(h):
        assemble(h)
        none = jnp.zeros((1, HD), f32)
        bias = jnp.concatenate([qv[:, h * 256 : h * 256 + 128], none, qv[:, h * 256 + 128 : h * 256 + 256]], 1)
        qkv[h] = (dot(rows_one[...], wqkv[h]) + bias).astype(bf)
        for block in range(2):
            at, seen = slice(block * rows, (block + 1) * rows), (block + 1) * rows
            scores = dot_nt(qkv[h, at, 0:128], qkv[h, 0:seen, 128:256]) * scale
            scores = jnp.where(allowed(block * rows, seen), scores, NEG)
            expo = jnp.exp(scores - jnp.max(scores, -1, keepdims=True))
            low = (expo / jnp.sum(expo, -1, keepdims=True)).astype(bf)
            probs[h, at, 0:seen] = low
            ctx[at, h * 128 : h * 128 + 128] = dot(low, qkv[h, 0:seen, 256:384]).astype(bf)

    head(0)
    for dist in range(DEPTH):
        y_arrival((O,), dist)
    head(1)
    z_arrival((I, W), 1)
    head(2)
    y_arrival((I, W), 0)
    head(3)
    for zz in range(DEPTH):
        for yy in range(2):
            ag_wait(O, zz, yy, 1 - c)

    def w_out(at, count):
        return go[at : at + count].reshape(count * 64, 1024)

    far[0] = dot(ctx[other, :], w_out(0, 8)).astype(bf)
    x_part(0).start()
    hidden[...] = tokens[...] + dot(ctx[own, :], w_out(0, 8)) + vecs[4:5, :]
    z_arrival((I, W), 2)
    y_arrival((I, W), 1)
    x_part(0).wait_recv()

    def second_norm(at, step):
        value = hidden[pl.ds(at, step), :] + inx[0, pl.ds(at, step), :].astype(f32)
        hidden[pl.ds(at, step), :] = value
        unit, inverse = norm(value)
        to = pl.ds(pl.multiple_of(t * rows + at, step), step)
        rows_two[to, :] = (unit * vecs[2:3, :] + vecs[3:4, :]).astype(bf)

    by_rows(second_norm)
    x_rows(rows_two, 2).start()
    z_arrival((I, W), 3)
    y_arrival((I, W), 2)
    macc[...] = jnp.zeros_like(macc)
    nacc[...] = jnp.zeros_like(nacc)
    vout[...] = jnp.zeros_like(vout)
    x_rows_wait(grad_rows, 1)
    x_rows_wait(rows_two, 2)
    rows_t[...] = rows_two[...].T

    def ffn(e, carry):
        s, sub = lax.div(e, 2), lax.rem(e, 2)
        zz, yy = near(s), lax.rem(y + sub, 2)

        @pl.when(e == 5)
        def _():
            y_arrival((I, W), 3)

        for k in (I, W):
            ag_wait(k, zz, yy, 1 - c)
        m = zz * 2 + yy
        first = 2 * m
        bias_row = vecs[pl.ds(8 + 2 * t + lax.div(m, 4), 1), pl.ds(pl.multiple_of(lax.rem(m, 4) * 256, 256), 256)]

        def w_in(at, count):
            return jnp.concatenate([gi[first, at : at + count, :], gi[first + 1, at : at + count, :]], 1)

        def w_down(at, count):
            return gd[pl.ds(first, 2), :, at : at + count].reshape(256, count)

        for block in range(2):
            at = slice(block * rows, (block + 1) * rows)
            inner = dot(rows_two[at, :], w_in(0, 1024)) + bias_row
            cube = inner * inner
            bent = jnp.tanh(GELU_A * inner * (1.0 + GELU_B * cube))
            act[at, :] = (0.5 * inner * (1.0 + bent)).astype(bf)
            slope = 0.5 * (1.0 + bent) + 0.5 * inner * (1.0 - bent * bent) * (GELU_A * (1.0 + 3.0 * GELU_B * cube))
            gin[at, :] = (dot_nt(grad_rows[at, :], w_down(0, 1024)) * slope).astype(bf)
        for nb in range(4):
            at = slice(nb * 256, nb * 256 + 256)
            nacc[:, at] += dot_nt(gin[...], w_in(nb * 256, 256))
            macc[:, at] += dot(act[...], w_down(nb * 256, 256))
        bias_sum[m] = jnp.sum(gin[...].astype(f32), 0, keepdims=True)
        for k in (I, W):
            drain(k, zz, yy)
        for nb in range(4):
            at = slice(nb * 256, nb * 256 + 256)
            part = dot(rows_t[at, :], gin[...]).astype(bf)
            gi[first, at, :] = part[:, 0:LANES]
            gi[first + 1, at, :] = part[:, LANES:]
        act_t = act[...].T
        for nb in range(4):
            at = slice(nb * 256, nb * 256 + 256)
            part = dot(act_t, grad_rows[:, at]).astype(bf)
            gd[pl.ds(first, 2), :, at] = part.reshape(2, LANES, 256)
        for k in (I, W):
            rc_copy(k, zz, yy).start()

        @pl.when(e > 0)
        def _():
            before = e - 1
            for k in (I, W):
                rc_add(k, near(lax.div(before, 2)), lax.rem(y + lax.rem(before, 2), 2))

        return carry

    lax.fori_loop(0, 2 * DEPTH, ffn, 0)
    far[1] = nacc[other, :].astype(bf)
    x_part(1).start()
    for m in range(8):
        for side in range(2):
            row = 8 + 2 * side + m // 4
            vout[0, row : row + 1, m % 4 * 256 : m % 4 * 256 + 256] = jnp.where(t == side, bias_sum[m], 0.0)
    far[2] = macc[other, :].astype(bf)
    x_part(2).start()
    for k in (I, W):
        rc_add(k, near(DEPTH - 1), 1 - y)
    rows_t[...] = rows_one[...].T
    x_part(1).wait_recv()

    def row_sum(row, value):
        vout[0, row : row + 1, :] += jnp.sum(value, 0, keepdims=True)

    def second_back(at, step):
        here = pl.ds(at, step)
        in_group = pl.ds(pl.multiple_of(t * rows + at, step), step)
        grad = nacc[in_group, :] + inx[1, here, :].astype(f32)
        unit, inverse = norm(hidden[here, :])
        back = cot[here, :] + norm_grad(grad, unit, inverse, vecs[2:3, :])
        ghid[here, :] = back
        rows_two[in_group, :] = back.astype(bf)
        row_sum(2, grad * unit)
        row_sum(3, grad)
        row_sum(4, back)
        row_sum(5, cot[here, :])

    x_rows(rows_two, 2).wait_send()
    by_rows(second_back)
    x_rows(rows_two, 3).start()
    for s in range(1, 3):
        for k in (I, W):
            ry_add(k, s)
    x_part(2).wait_recv()

    def mixed_out(at, step):
        here = pl.ds(at, step)
        in_group = pl.ds(pl.multiple_of(t * rows + at, step), step)
        mixed[here, :] = hidden[here, :] + macc[in_group, :] + inx[2, here, :].astype(f32) + vecs[5:6, :]

    by_rows(mixed_out)
    for zz in range(DEPTH):
        for yy in range(2):
            drain(O, zz, yy)
            drain(Q, zz, yy)
    x_rows_wait(rows_two, 3)
    gctx[...] = dot_nt(rows_two[...], w_out(0, 8)).astype(bf)
    for nb in range(4):
        at = slice(nb * 256, nb * 256 + 256)
        go[:, :, at] = dot_tn(ctx[...], rows_two[:, at]).astype(bf).reshape(8, 64, 256)
    for zz in range(DEPTH):
        for yy in range(2):
            rc_copy(O, zz, yy).start()

    def head_back(h):
        q0, q1 = qkv[h, 0:rows, 0:128], qkv[h, rows : 2 * rows, 0:128]
        grads = []
        for block in range(2):
            at, seen = slice(block * rows, (block + 1) * rows), (block + 1) * rows
            low = probs[h, at, 0:seen]
            given = gctx[at, h * 128 : h * 128 + 128]
            prob = low.astype(f32)
            grad_probs = dot_nt(given, qkv[h, 0:seen, 256:384])
            delta = jnp.sum(prob * grad_probs, -1, keepdims=True)
            grad_scores = (prob * (grad_probs - delta)).astype(bf)
            grad_q = dot(grad_scores, qkv[h, 0:seen, 128:256]) * scale
            grad_k = dot_tn(grad_scores, q1 if block else q0) * scale
            grad_v = dot_tn(low, given)
            grads.append((grad_q, grad_k, grad_v))
        (gq0, gk0, gv0), (gq1, gk1, gv1) = grads
        top = jnp.concatenate([gq0, gk0 + gk1[0:rows], gv0 + gv1[0:rows]], 1).astype(bf)
        low_half = jnp.concatenate([gq1, gk1[rows:], gv1[rows:]], 1).astype(bf)
        qkv[h, 0:rows, :] = top
        qkv[h, rows : 2 * rows, :] = low_half
        total = jnp.sum(top.astype(f32), 0, keepdims=True) + jnp.sum(low_half.astype(f32), 0, keepdims=True)
        for side in range(2):
            vout[0, 6 + side : 7 + side, h * 256 : h * 256 + 128] = jnp.where(t == side, total[:, 0:128], 0.0)
            vout[0, 6 + side : 7 + side, h * 256 + 128 : h * 256 + 256] = jnp.where(t == side, total[:, 256:384], 0.0)
        part = dot(rows_t[...], qkv[h]).astype(bf)
        disassemble(h, part)
        for yy in range(2):
            rc_copy(Q, h, yy).start()
        product = dot_nt(qkv[h], wqkv[h])
        if h == 0:
            nacc[...] = product
        else:
            nacc[...] += product

    for h in range(DEPTH):
        head_back(h)
    far[3] = nacc[other, :].astype(bf)
    x_part(3).start()
    for k in (O, Q):
        for s in range(DEPTH):
            rc_add(k, near(s), 1 - y)
    for k in (I, W):
        ry_add(k, 3)
    for k in (O, Q):
        for s in range(DEPTH):
            rc_add(k, near(s), y)
    for k in (I, W):
        ry_add(k, 0)
    x_part(3).wait_recv()

    def first_back(at, step):
        here = pl.ds(at, step)
        in_group = pl.ds(pl.multiple_of(t * rows + at, step), step)
        grad = nacc[in_group, :] + inx[3, here, :].astype(f32)
        unit, inverse = norm(tokens[here, :])
        input_grad[here, :] = ghid[here, :] + norm_grad(grad, unit, inverse, vecs[0:1, :])
        row_sum(0, grad * unit)
        row_sum(1, grad)

    by_rows(first_back)

    stages = (x_peer, c_peer, y_peer)

    def v_copy(stage):
        return remote(vout.at[stage], vin.at[stage], v_send.at[stage], v_recv.at[stage], stages[stage])

    def vz_copy(step):
        peer = (slot_of(lax.rem(z + step, DEPTH), y, c), t)
        return remote(vout.at[3], vin.at[3 + z], v_send.at[2 + step], v_recv.at[3 + z], peer)

    v_copy(0).start()
    for k in (O, Q):
        for s in range(1, DEPTH):
            ry_add(k, s)
        if k == O:
            v_copy(0).wait_recv()
            vout[1] = vout[0] + vin[0]
            v_copy(1).start()
            ry_add(k, 0)
    v_copy(1).wait_recv()
    vout[2] = vout[1] + vin[1]
    v_copy(2).start()
    ry_add(Q, 0)
    for k in (I, W, O):
        rz_add(k)
    v_copy(2).wait_recv()
    vout[3] = vout[2] + vin[2]
    for step in range(1, DEPTH):
        vz_copy(step).start()
    vin[3 + z] = vout[3]
    rz_add(Q)
    for step in range(1, DEPTH):
        zz = lax.rem(z + step, DEPTH)
        remote(vin.at[3 + zz], vin.at[3 + zz], v_send.at[0], v_recv.at[3 + zz], y_peer).wait_recv()
    count = vec_grads.shape[0]
    total = ((vin[3] + vin[4]) + vin[5]) + vin[6]
    vec_grads[...] = total[0:count]

    for stage in range(3):
        v_copy(stage).wait_send()
    for step in range(1, DEPTH):
        vz_copy(step).wait_send()
    for index, ref in ((0, rows_one), (1, grad_rows), (3, rows_two)):
        x_rows(ref, index).wait_send()
    for index in range(4):
        x_part(index).wait_send()
    for k in range(4):
        for zz in range(DEPTH):
            for yy in range(2):
                rc_copy(k, zz, yy).wait_send()
            ry_copy(k, zz).wait_send()
        for s in range(1, DEPTH):
            rz_copy(k, near(s)).wait_send()


def run_layer(tokens, cotangent, lengths, order, weights, vec_params):
    bf, f32 = jnp.bfloat16, jnp.float32
    rows = tokens.shape[0]
    group = 2 * rows
    owners = 16
    shapes = piece_shapes()
    view = jnp.transpose(weights, (1, 2, 0))
    vmem = pl.BlockSpec(memory_space=pltpu.VMEM)
    smem = pl.BlockSpec(memory_space=pltpu.SMEM)

    def many(count):
        return [pltpu.VMEM((count,) + s, bf) for s in shapes]

    full = pltpu.VMEM((group, D), bf)
    dma = pltpu.SemaphoreType.DMA
    return pl.pallas_call(
        layer_kernel,
        out_shape=[jax.ShapeDtypeStruct((rows, D), f32)] * 2
        + [jax.ShapeDtypeStruct(s, f32) for s in shapes]
        + [jax.ShapeDtypeStruct(vec_params.shape, f32)],
        in_specs=[smem, smem, pl.BlockSpec(memory_space=pl.ANY)] + [vmem] * 3,
        out_specs=[vmem] * 7,
        scratch_shapes=[
            pltpu.VMEM((owners,) + shapes[0], bf),
            pltpu.VMEM((owners // 2, BLOCK, D), bf),
            pltpu.VMEM((owners,) + shapes[2], bf),
            pltpu.VMEM((owners,) + shapes[3], bf),
            pltpu.VMEM((DEPTH, D, 3 * HD), bf),
        ]
        + many(2 * DEPTH)
        + many(DEPTH)
        + many(DEPTH - 1)
        + [
            full,
            full,
            pltpu.VMEM((D, group), bf),
            full,
            pltpu.VMEM((DEPTH, group, group), bf),
            pltpu.VMEM((DEPTH, group, 3 * HD), bf),
            pltpu.VMEM((group, DEPTH * HD), bf),
            pltpu.VMEM((group, DEPTH * HD), bf),
            pltpu.VMEM((rows, D), f32),
            pltpu.VMEM((rows, D), f32),
            pltpu.VMEM((4, rows, D), bf),
            pltpu.VMEM((4, rows, D), bf),
            pltpu.VMEM((group, D), f32),
            pltpu.VMEM((group, D), f32),
            pltpu.VMEM((group, 256), bf),
            pltpu.VMEM((group, 256), bf),
            pltpu.VMEM((8, 1, 256), f32),
            pltpu.VMEM((7, 16, D), f32),
            pltpu.VMEM((4, 16, D), f32),
            dma((4, owners)),
            dma((4, DEPTH)),
            dma((4, 2 * DEPTH)),
            dma((4, 2, DEPTH)),
            dma((4, 2 * DEPTH)),
            dma((4, 2 * DEPTH)),
            dma((4, DEPTH)),
            dma((4, DEPTH)),
            dma((4, DEPTH - 1)),
            dma((4, DEPTH - 1)),
            dma((8,)),
            dma((8,)),
            dma((6,)),
            dma((7,)),
            dma((1,)),
        ],
        compiler_params=pltpu.CompilerParams(
            collective_id=0, has_side_effects=True, vmem_limit_bytes=VMEM_LIMIT
        ),
        name="layer",
    )(lengths, order, view, tokens, cotangent, vec_params)


def per_device(
    grp_count,
    tp_count,
    tokens,
    cotangent,
    lengths,
    order,
    weights,
    momentum,
    stat_left,
    stat_right,
    root_left,
    root_right,
    vec_params,
    vec_momentum,
    vec_second,
):
    fits = grp_count == 4 * DEPTH and tp_count == 2 and tokens.shape[0] == 256
    if not fits or lengths.shape[1] != ARTICLES:
        return per_device_general(
            tokens,
            cotangent,
            lengths,
            order,
            weights,
            momentum,
            stat_left,
            stat_right,
            root_left,
            root_right,
            vec_params,
            vec_momentum,
            vec_second,
        )
    token_total = tokens.shape[0] * tp_count * grp_count
    mixed, input_grad, *sums, vec_grads = run_layer(tokens, cotangent, lengths, order, weights, vec_params)
    blocks, vecs, results = update_blocks(
        sums,
        (weights, momentum, stat_left, stat_right, root_left, root_right),
        vec_grads,
        (vec_params, vec_momentum, vec_second),
        (mixed, input_grad),
        token_total,
    )
    return (*results, *blocks, *vecs)


def solution(mesh):
    placed = (
        P(("grp", "tp"), None),
        P(("grp", "tp"), None),
        P("grp", None),
        P("grp", None),
        P(("tp", "grp"), None, None),
        P(("tp", "grp"), None, None),
        P(("tp", "grp"), None, None),
        P(("tp", "grp"), None, None),
        P(("tp", "grp"), None, None),
        P(("tp", "grp"), None, None),
        P(),
        P(),
        P(),
    )
    return jax.shard_map(
        functools.partial(per_device, mesh.shape["grp"], mesh.shape["tp"]),
        mesh=mesh,
        in_specs=placed,
        out_specs=(
            P(("grp", "tp"), None),
            P(("grp", "tp"), None),
            P(("tp", "grp"), None, None),
            P(("tp", "grp"), None, None),
            P(("tp", "grp"), None, None),
            P(("tp", "grp"), None, None),
            P(("tp", "grp"), None, None),
            P(),
            P(),
            P(),
            P(),
        ),
        check_vma=False,
    )
```

```python
import functools

import jax
import jax.numpy as jnp
from jax import lax
from jax.experimental import pallas as pl
from jax.experimental.pallas import tpu as pltpu
from jax.sharding import PartitionSpec as P

D = 1024
HEADS = 8
HD = 128
FF = 4096
BLOCK = 64


EPS = 1e-05
NEG = -1e30
DECAY = 0.9
BETA = 0.9
RATE = 0.05
VEC_DECAY = 0.9
VEC_RATE = 0.2
VEC_EPS = 1e-08


def norm_rows(value, gain, shift):
    average = jnp.mean(value, -1, keepdims=True)
    centred = value - average
    inverse = lax.rsqrt(jnp.mean(centred * centred, -1, keepdims=True) + EPS)
    normed = centred * inverse
    return (normed * gain + shift, normed, inverse)


def norm_back(grad_out, normed, inverse, gain):
    scaled = grad_out * gain
    return inverse * (
        scaled
        - jnp.mean(scaled, -1, keepdims=True)
        - normed * jnp.mean(scaled * normed, -1, keepdims=True)
    )


def segment_ids(lengths_row, order_row, group_rows):
    article_count = lengths_row.shape[0]
    slots = jnp.arange(article_count, dtype=jnp.int32)
    picks = (order_row[:, None] == slots[None, :]).astype(jnp.int32)
    packed = jnp.sum(picks * lengths_row[None, :], 1)
    ends = jnp.cumsum(packed)
    spots = jnp.arange(group_rows, dtype=jnp.int32)
    return jnp.sum((spots[:, None] >= ends[None, :]).astype(jnp.int32), 1)


def allowed_mask(row_ids, row_segs, segments, key_ids, article_count):
    causal = key_ids[None, :] <= row_ids[:, None]
    same = segments[None, :] == row_segs[:, None]
    alone = (row_segs[:, None] < article_count) | (key_ids[None, :] == row_ids[:, None])
    return causal & same & alone


def from_columns(tiles, row_total, col_total):
    return (
        tiles.reshape(col_total // BLOCK, row_total // BLOCK, BLOCK, BLOCK)
        .transpose(1, 2, 0, 3)
        .reshape(row_total, col_total)
    )


def from_rows(tiles, row_total, col_total):
    return (
        tiles.reshape(row_total // BLOCK, col_total // BLOCK, BLOCK, BLOCK)
        .transpose(0, 2, 1, 3)
        .reshape(row_total, col_total)
    )


def to_columns(matrix):
    row_total, col_total = matrix.shape
    return (
        matrix.reshape(row_total // BLOCK, BLOCK, col_total // BLOCK, BLOCK)
        .transpose(2, 0, 1, 3)
        .reshape(-1, BLOCK, BLOCK)
    )


def to_rows(matrix):
    row_total, col_total = matrix.shape
    return (
        matrix.reshape(row_total // BLOCK, BLOCK, col_total // BLOCK, BLOCK)
        .transpose(0, 2, 1, 3)
        .reshape(-1, BLOCK, BLOCK)
    )


def per_device_general(
    tokens,
    cotangent,
    lengths,
    order,
    weights,
    momentum,
    stat_left,
    stat_right,
    root_left,
    root_right,
    vec_params,
    vec_momentum,
    vec_second,
):
    groups = lax.axis_size("grp")
    tp_size = lax.axis_size("tp")
    tp_rank = lax.axis_index("tp")
    tok_rows = tokens.shape[0]
    group_rows = tok_rows * tp_size
    article_count = lengths.shape[1]
    owners = groups * tp_size
    block_area = BLOCK * BLOCK * owners
    qkv_count = 3 * D * D // block_area
    out_count = D * D // block_area
    in_count = D * FF // block_area
    owned_blocks = weights.shape[0]
    heads_here = HEADS // tp_size
    qkv_cols = 3 * D // tp_size
    feat_here = D // tp_size
    ff_here = FF // tp_size
    qv_width = 2 * D // tp_size
    token_total = group_rows * groups
    gathered = lax.all_gather(weights.astype(jnp.bfloat16), "grp", axis=0, tiled=True)
    per_owner = gathered.reshape(groups, owned_blocks, BLOCK, BLOCK)
    marks = [0, qkv_count, qkv_count + out_count, qkv_count + out_count + in_count, owned_blocks]
    pieces = [
        per_owner[:, marks[index] : marks[index + 1]].reshape(-1, BLOCK, BLOCK)
        for index in range(4)
    ]
    w_qkv = from_columns(pieces[0], D, qkv_cols)
    w_out = from_rows(pieces[1], feat_here, D)
    w_in = from_columns(pieces[2], D, ff_here)
    w_down = from_rows(pieces[3], ff_here, D)
    w_qkv_heads = w_qkv.reshape(D, heads_here, 3, HD)
    w_out_heads = w_out.reshape(heads_here, HD, D)
    segments = segment_ids(lengths[0], order[0], group_rows)
    gain_one = vec_params[0]
    shift_one = vec_params[1]
    gain_two = vec_params[2]
    shift_two = vec_params[3]
    bias_out = vec_params[4]
    bias_down = vec_params[5]
    qv_here = lax.dynamic_slice_in_dim(
        vec_params[6:8].reshape(2 * D), tp_rank * qv_width, qv_width
    ).reshape(heads_here, 2, HD)
    bias_heads = jnp.stack(
        [qv_here[:, 0], jnp.zeros((heads_here, HD), jnp.float32), qv_here[:, 1]], 0
    )[:, :, None, :]
    bias_in = lax.dynamic_slice_in_dim(vec_params[8:].reshape(FF), tp_rank * ff_here, ff_here)
    normed_one, unit_one, inverse_one = norm_rows(tokens, gain_one, shift_one)
    rows_one = lax.all_gather(normed_one.astype(jnp.bfloat16), "tp", axis=0, tiled=True)
    projected = (
        jnp.einsum("rx,xhcd->chrd", rows_one, w_qkv_heads, preferred_element_type=jnp.float32)
        + bias_heads
    ).astype(jnp.bfloat16)
    queries = projected[0]
    keys_all = projected[1]
    values_all = projected[2]
    span = min(512, group_rows)
    starts = jnp.arange(group_rows // span, dtype=jnp.int32) * span
    key_ids = jnp.arange(group_rows, dtype=jnp.int32)
    score_scale = HD ** (-0.5)

    def masked_scores(first_row):
        row_ids = first_row + jnp.arange(span, dtype=jnp.int32)
        row_segs = lax.dynamic_slice_in_dim(segments, first_row, span, 0)
        allowed = allowed_mask(row_ids, row_segs, segments, key_ids, article_count)
        query_rows = lax.dynamic_slice_in_dim(queries, first_row, span, 1)
        scores = (
            jnp.einsum("hqd,hkd->hqk", query_rows, keys_all, preferred_element_type=jnp.float32)
            * score_scale
        )
        return (jnp.where(allowed[None], scores, NEG), query_rows)

    def attend(context_buf, first_row):
        scores, query_rows = masked_scores(first_row)
        row_max = jnp.max(scores, -1, keepdims=True)
        expo = jnp.exp(scores - row_max)
        expsum = jnp.sum(expo, -1, keepdims=True)
        probs_low = (expo / expsum).astype(jnp.bfloat16)
        context = jnp.einsum(
            "hqk,hkd->hqd", probs_low, values_all, preferred_element_type=jnp.float32
        ).astype(jnp.bfloat16)
        context_buf = lax.dynamic_update_slice_in_dim(context_buf, context, first_row, 1)
        return (context_buf, (row_max + jnp.log(expsum))[:, :, 0])

    context_low, log_norm = lax.scan(
        attend, jnp.zeros((heads_here, group_rows, HD), jnp.bfloat16), starts
    )
    attn_sum = lax.psum_scatter(
        jnp.einsum(
            "hrd,hde->re", context_low, w_out_heads, preferred_element_type=jnp.float32
        ).astype(jnp.bfloat16),
        "tp",
        scatter_dimension=0,
        tiled=True,
    ).astype(jnp.float32)
    hidden = tokens + attn_sum + bias_out
    normed_two, unit_two, inverse_two = norm_rows(hidden, gain_two, shift_two)
    rows_two = lax.all_gather(normed_two.astype(jnp.bfloat16), "tp", axis=0, tiled=True)
    inner = jnp.dot(rows_two, w_in, preferred_element_type=jnp.float32) + bias_in
    activ, gelu_pull = jax.vjp(jax.nn.gelu, inner)
    activ_low = activ.astype(jnp.bfloat16)
    mixed = (
        hidden
        + lax.psum_scatter(
            jnp.dot(activ_low, w_down, preferred_element_type=jnp.float32).astype(jnp.bfloat16),
            "tp",
            scatter_dimension=0,
            tiled=True,
        ).astype(jnp.float32)
        + bias_down
    )
    grad_low = cotangent.astype(jnp.bfloat16)
    grad_rows = lax.all_gather(grad_low, "tp", axis=0, tiled=True)
    g_down = jnp.einsum("rf,rd->fd", activ_low, grad_rows, preferred_element_type=jnp.float32)
    grad_activ = jnp.einsum("rd,fd->rf", grad_rows, w_down, preferred_element_type=jnp.float32)
    grad_inner = gelu_pull(grad_activ)[0].astype(jnp.bfloat16)
    g_in = jnp.einsum("rd,rf->df", rows_two, grad_inner, preferred_element_type=jnp.float32)
    g_bias_in = jnp.sum(grad_inner.astype(jnp.float32), 0)
    ffn_blocks = jnp.concatenate(
        [
            to_columns(g_in).reshape(groups, in_count, BLOCK, BLOCK),
            to_rows(g_down).reshape(groups, in_count, BLOCK, BLOCK),
        ],
        1,
    )
    grad_normed_two = lax.psum_scatter(
        jnp.einsum("rf,df->rd", grad_inner, w_in, preferred_element_type=jnp.float32).astype(
            jnp.bfloat16
        ),
        "tp",
        scatter_dimension=0,
        tiled=True,
    ).astype(jnp.float32)
    grad_hidden = cotangent + norm_back(grad_normed_two, unit_two, inverse_two, gain_two)
    grad_attn_low = grad_hidden.astype(jnp.bfloat16)
    grad_attn_rows = lax.all_gather(grad_attn_low, "tp", axis=0, tiled=True)
    g_out = jnp.einsum(
        "hrd,re->hde", context_low, grad_attn_rows, preferred_element_type=jnp.float32
    ).reshape(feat_here, D)
    grad_context = jnp.einsum(
        "re,hde->hrd", grad_attn_rows, w_out_heads, preferred_element_type=jnp.float32
    ).astype(jnp.bfloat16)
    zero_heads = jnp.zeros((heads_here, group_rows, HD), jnp.float32)

    def attend_back(carry, inputs):
        grad_queries, grad_keys, grad_values = carry
        first_row, log_block = inputs
        scores, query_rows = masked_scores(first_row)
        probs = jnp.exp(scores - log_block[:, :, None])
        grad_ctx_rows = lax.dynamic_slice_in_dim(grad_context, first_row, span, 1)
        grad_probs = jnp.einsum(
            "hqd,hkd->hqk", grad_ctx_rows, values_all, preferred_element_type=jnp.float32
        )
        delta = jnp.sum(probs * grad_probs, -1, keepdims=True)
        grad_scores = (probs * (grad_probs - delta)).astype(jnp.bfloat16)
        query_part = (
            jnp.einsum("hqk,hkd->hqd", grad_scores, keys_all, preferred_element_type=jnp.float32)
            * score_scale
        )
        grad_queries = lax.dynamic_update_slice_in_dim(grad_queries, query_part, first_row, 1)
        grad_keys = (
            grad_keys
            + jnp.einsum(
                "hqk,hqd->hkd", grad_scores, query_rows, preferred_element_type=jnp.float32
            )
            * score_scale
        )
        grad_values = grad_values + jnp.einsum(
            "hqk,hqd->hkd",
            probs.astype(jnp.bfloat16),
            grad_ctx_rows,
            preferred_element_type=jnp.float32,
        )
        return ((grad_queries, grad_keys, grad_values), None)

    (grad_queries, grad_keys, grad_values), unused = lax.scan(
        attend_back, (zero_heads, zero_heads, zero_heads), (starts, log_norm)
    )
    grad_proj = jnp.stack([grad_queries, grad_keys, grad_values], 0).astype(jnp.bfloat16)
    proj_sums = jnp.sum(grad_proj.astype(jnp.float32), 2)
    g_bias_qv = jnp.stack([proj_sums[0], proj_sums[2]], 1).reshape(qv_width)
    g_qkv = jnp.einsum(
        "rx,chrd->xhcd", rows_one, grad_proj, preferred_element_type=jnp.float32
    ).reshape(D, qkv_cols)
    grad_normed_one = lax.psum_scatter(
        jnp.einsum(
            "chrd,xhcd->rx", grad_proj, w_qkv_heads, preferred_element_type=jnp.float32
        ).astype(jnp.bfloat16),
        "tp",
        scatter_dimension=0,
        tiled=True,
    ).astype(jnp.float32)
    input_grad = grad_hidden + norm_back(grad_normed_one, unit_one, inverse_one, gain_one)
    local_rows = jnp.stack(
        [
            jnp.sum(grad_normed_one * unit_one, 0),
            jnp.sum(grad_normed_one, 0),
            jnp.sum(grad_normed_two * unit_two, 0),
            jnp.sum(grad_normed_two, 0),
            jnp.sum(grad_hidden, 0),
            jnp.sum(cotangent, 0),
        ]
    )
    qv_rows = lax.dynamic_update_slice(
        jnp.zeros((2 * D,), jnp.float32), g_bias_qv, (tp_rank * qv_width,)
    ).reshape(2, D)
    in_rows = lax.dynamic_update_slice(
        jnp.zeros((FF,), jnp.float32), g_bias_in, (tp_rank * ff_here,)
    ).reshape(FF // D, D)
    vec_grads = lax.psum(jnp.concatenate([local_rows, qv_rows, in_rows], 0), ("grp", "tp"))
    attn_blocks = jnp.concatenate(
        [
            to_columns(g_qkv).reshape(groups, qkv_count, BLOCK, BLOCK),
            to_rows(g_out).reshape(groups, out_count, BLOCK, BLOCK),
        ],
        1,
    )
    every_block = jnp.concatenate([attn_blocks, ffn_blocks], 1).reshape(-1, BLOCK, BLOCK)
    weight_grads = lax.psum_scatter(
        every_block.astype(jnp.bfloat16), "grp", scatter_dimension=0, tiled=True
    ).astype(jnp.float32)
    scaled = weight_grads * token_total ** (-0.5)
    stat_left_new = DECAY * stat_left + (1.0 - DECAY) * jnp.einsum(
        "nij,nkj->nik", scaled, scaled, precision=lax.Precision.HIGHEST
    )
    stat_right_new = DECAY * stat_right + (1.0 - DECAY) * jnp.einsum(
        "nji,njk->nik", scaled, scaled, precision=lax.Precision.HIGHEST
    )
    shaped = jnp.einsum("nij,njk->nik", root_left, scaled, precision=lax.Precision.HIGHEST)
    shaped = jnp.einsum("nij,njk->nik", shaped, root_right, precision=lax.Precision.HIGHEST)
    momentum_new = BETA * momentum + shaped
    weights_new = weights - RATE * momentum_new
    vec_scaled = vec_grads * token_total ** (-0.5)
    vec_second_new = VEC_DECAY * vec_second + (1.0 - VEC_DECAY) * vec_scaled * vec_scaled
    vec_momentum_new = BETA * vec_momentum + vec_scaled * lax.rsqrt(vec_second_new + VEC_EPS)
    vec_new = vec_params - VEC_RATE * vec_momentum_new
    return (
        mixed,
        input_grad,
        weight_grads,
        stat_left_new,
        stat_right_new,
        momentum_new,
        weights_new,
        vec_grads,
        vec_second_new,
        vec_momentum_new,
        vec_new,
    )


MESH_ID = pl.DeviceIdType.MESH
LANES = 128
HALF = 64
VMEM_LIMIT = 62 * 2**20
ARTICLES = 4
GELU_A = (2.0 / 3.141592653589793) ** 0.5
GELU_B = 0.044715


def remote(src, dst, send_sem, recv_sem, device):
    return pltpu.make_async_remote_copy(
        src_ref=src,
        dst_ref=dst,
        send_sem=send_sem,
        recv_sem=recv_sem,
        device_id=device,
        device_id_type=MESH_ID,
    )


def place():
    grp = lax.axis_index("grp")
    return lax.div(grp, 4), lax.rem(lax.div(grp, 2), 2), lax.rem(grp, 2), lax.axis_index("tp")


def slot_of(z, y, c):
    return z * 4 + y * 2 + c


def lay_blocks(view_ref, stack):
    count = view_ref.shape[2]

    def row(i, carry):
        stack[pl.ds(i, count, stride=BLOCK), 0:HALF] = view_ref[i].T
        return carry

    lax.fori_loop(0, BLOCK, row, 0, unroll=8)


def piece_shapes():
    return ((768, LANES), (64, 512), (1024, LANES), (LANES, 1024))


def fold_tiles(value, mask):
    kept = jnp.where(mask, value, 0.0)
    halves = kept[:, :LANES] + kept[:, LANES:]
    return halves + pltpu.roll(halves, HALF, 1)


def update_kernel(
    scale,
    sum_q,
    sum_o,
    sum_i,
    sum_d,
    root_l,
    root_r,
    vec_g,
    vecs,
    vec_m,
    vec_s,
    mixed,
    input_grad,
    w,
    m,
    sl,
    sr,
    out_g,
    out_sl,
    out_sr,
    out_m,
    out_w,
    out_vg,
    out_vs,
    out_vm,
    out_v,
    out_mixed,
    out_input_grad,
    first,
    second,
):
    count = root_l.shape[2]
    bf = jnp.bfloat16
    out_mixed[...] = mixed[...]
    out_input_grad[...] = input_grad[...]

    @pl.when(pl.program_id(0) == 0)
    def _():
        total = vec_g[...]
        out_vg[...] = total
        scaled = total * scale
        fresh = VEC_DECAY * vec_s[...] + (1.0 - VEC_DECAY) * scaled * scaled
        out_vs[...] = fresh
        momentum = BETA * vec_m[...] + scaled * lax.rsqrt(fresh + VEC_EPS)
        out_vm[...] = momentum
        out_v[...] = vecs[...] - VEC_RATE * momentum
        rows = sum_q.shape[0]
        first[0:rows, 0:HALF] = sum_q[:, 0:HALF]
        first[rows : 2 * rows, 0:HALF] = sum_q[:, HALF:LANES]
        base = 2 * rows
        for b in range(8):
            first[base + b * 64 : base + b * 64 + 64, 0:HALF] = sum_o[:, b * HALF : (b + 1) * HALF]
        base += 512
        first[base : base + 1024, 0:HALF] = sum_i[:, 0:HALF]
        first[base + 1024 : base + 2048, 0:HALF] = sum_i[:, HALF:LANES]
        base += 2048
        for r in range(2):
            for b in range(16):
                at = base + (r * 16 + b) * 64
                first[at : at + 64, 0:HALF] = sum_d[r * 64 : r * 64 + 64, b * HALF : (b + 1) * HALF]

        def row(i, carry):
            both = jnp.concatenate([root_l[i], root_r[i]], 0)
            second[pl.ds(i, count, stride=BLOCK), :] = both.T
            return carry

        lax.fori_loop(0, BLOCK, row, 0, unroll=8)
        row_id = lax.broadcasted_iota(jnp.int32, (256, 256), 0)
        col_id = lax.broadcasted_iota(jnp.int32, (256, 256), 1)
        mask = lax.shift_right_logical(row_id, 6) == lax.shift_right_logical(col_id, 6)
        zero = jnp.zeros((256, 256), jnp.float32)

        def spread(v):
            return jnp.where(mask, jnp.concatenate([v, v, v, v], 1), zero).astype(bf)

        def four(k, carry):
            at = pl.ds(pl.multiple_of(k * 256, 256), 256)
            s32 = first[at, 0:HALF] * scale
            s = s32.astype(bf)
            left = second[at, 0:HALF]
            right = second[at, HALF:LANES].astype(bf)
            outer = lax.dot_general(s, s, (((1,), (1,)), ((), ())), preferred_element_type=jnp.float32)
            inner = lax.dot_general(spread(s32), s, (((0,), (0,)), ((), ())), preferred_element_type=jnp.float32)
            shaped = jnp.dot(spread(left), s, preferred_element_type=jnp.float32)
            shaped = jnp.dot(spread(shaped), right, preferred_element_type=jnp.float32)
            first[at, HALF:LANES] = fold_tiles(outer, mask)[:, HALF:LANES]
            second[at, 0:HALF] = inner
            second[at, HALF:LANES] = shaped
            return carry

        lax.fori_loop(0, count // 4, four, 0, unroll=4)

    i0 = pl.program_id(0) * w.shape[0]

    def rows_out(ii, carry):
        at = pl.ds(i0 + ii, count, stride=BLOCK)
        one = first[at, :].T
        two = second[at, :].T
        out_g[ii] = one[0:HALF]
        out_sl[ii] = DECAY * sl[ii] + (1.0 - DECAY) * one[HALF:LANES]
        out_sr[ii] = DECAY * sr[ii] + (1.0 - DECAY) * two[0:HALF]
        fresh = BETA * m[ii] + two[HALF:LANES]
        out_m[ii] = fresh
        out_w[ii] = w[ii] - RATE * fresh
        return carry

    lax.fori_loop(0, w.shape[0], rows_out, 0, unroll=True)


def update_blocks(sums, blocks, vec_grads, vecs, results, token_total):
    views = [jnp.transpose(a, (1, 2, 0)) for a in blocks]
    count = blocks[0].shape[0]
    rows = 8
    whole = pl.BlockSpec(memory_space=pltpu.VMEM)
    steps = BLOCK // rows
    some = pl.BlockSpec((results[0].shape[0] // steps, results[0].shape[1]), lambda i: (i, 0))
    part = pl.BlockSpec((rows, BLOCK, count), lambda i: (i, 0, 0))
    vec = jax.ShapeDtypeStruct(vec_grads.shape, jnp.float32)
    outs = pl.pallas_call(
        functools.partial(update_kernel, token_total ** (-0.5)),
        grid=(steps,),
        out_shape=[jax.ShapeDtypeStruct((BLOCK, BLOCK, count), jnp.float32)] * 5
        + [vec] * 4
        + [jax.ShapeDtypeStruct(a.shape, a.dtype) for a in results],
        in_specs=[whole] * 10 + [some] * 2 + [part] * 4,
        out_specs=[part] * 5 + [whole] * 4 + [some] * 2,
        scratch_shapes=[
            pltpu.VMEM((count * BLOCK, LANES), jnp.float32),
            pltpu.VMEM((count * BLOCK, LANES), jnp.float32),
        ],
        compiler_params=pltpu.CompilerParams(vmem_limit_bytes=VMEM_LIMIT),
        name="update_blocks",
    )(*sums, *views[4:], vec_grads, *vecs, *results, *views[:4])
    return [jnp.transpose(a, (2, 0, 1)) for a in outs[:5]], outs[5:9], outs[9:]


DEPTH = 4


def layer_kernel(
    lengths,
    order,
    view,
    tokens,
    cot,
    vecs,
    mixed,
    input_grad,
    sum_q,
    sum_o,
    sum_i,
    sum_d,
    vec_grads,
    gq,
    go,
    gi,
    gd,
    wqkv,
    cq,
    co,
    ci,
    cd,
    yq,
    yo,
    yi,
    yd,
    zq,
    zo,
    zi,
    zd,
    rows_one,
    rows_two,
    rows_t,
    grad_rows,
    grad_attn,
    probs,
    qkv,
    ctx,
    gctx,
    far,
    inx,
    macc,
    nacc,
    act,
    gin,
    bias_sum,
    qkv_bias,
    vin,
    vout,
    recv,
    send_y,
    send_c,
    send_z,
    rc_recv,
    rc_send,
    ry_recv,
    ry_send,
    rz_recv,
    rz_send,
    x_send,
    x_recv,
    v_send,
    v_recv,
    copy_sem,
):
    bf, f32 = jnp.bfloat16, jnp.float32
    z, y, c, t = place()
    me = slot_of(z, y, c)
    x_peer = (me, 1 - t)
    y_peer = (slot_of(z, 1 - y, c), t)
    c_peer = (slot_of(z, y, 1 - c), t)
    rows = tokens.shape[0]
    own = pl.ds(pl.multiple_of(t * rows, rows), rows)
    other = pl.ds(pl.multiple_of((1 - t) * rows, rows), rows)
    gathered, core_in, y_in, z_in = (gq, go, gi, gd), (cq, co, ci, cd), (yq, yo, yi, yd), (zq, zo, zi, zd)
    sums = (sum_q, sum_o, sum_i, sum_d)
    Q, O, I, W = range(4)

    def dot(a, b):
        return jnp.dot(a, b, preferred_element_type=f32)

    def dot_nt(a, b):
        return lax.dot_general(a, b, (((1,), (1,)), ((), ())), preferred_element_type=f32)

    def dot_tn(a, b):
        return lax.dot_general(a, b, (((0,), (0,)), ((), ())), preferred_element_type=f32)

    def piece(k, zz, yy, cc):
        if k == O:
            return go.at[zz * 2 + yy, :, pl.ds(pl.multiple_of(cc * 512, 512), 512)]
        return gathered[k].at[slot_of(zz, yy, cc)]

    def near(s):
        return lax.rem(z + (1 - 2 * lax.div(z, 2)) * s + DEPTH, DEPTH)

    def ag_copy(k, zz, yy, way):
        src = piece(k, zz, yy, c)
        sem = recv.at[k, slot_of(zz, yy, c)]
        if way == "up":
            return remote(src, src, send_z.at[k, 0, zz], sem, (slot_of(z + 1, y, c), t))
        if way == "down":
            return remote(src, src, send_z.at[k, 1, zz], sem, (slot_of(z - 1, y, c), t))
        if way == "y":
            return remote(src, src, send_y.at[k, zz], sem, y_peer)
        return remote(src, src, send_c.at[k, yy * DEPTH + zz], sem, c_peer)

    def ag_wait(k, zz, yy, cc):
        ref = piece(k, zz, yy, cc)
        remote(ref, ref, send_y.at[k, 0], recv.at[k, slot_of(zz, yy, cc)], y_peer).wait_recv()

    def own_sends_z(k):
        @pl.when(z < DEPTH - 1)
        def _():
            ag_copy(k, z, y, "up").start()

        @pl.when(z > 0)
        def _():
            ag_copy(k, z, y, "down").start()

        ag_copy(k, z, y, "core").start()

    def own_sends_y(k):
        ag_copy(k, z, y, "y").start()

    def z_arrival(kinds, dist):
        @pl.when(z >= dist)
        def _():
            for k in kinds:
                ag_wait(k, z - dist, y, c)

                @pl.when(z < DEPTH - 1)
                def _():
                    ag_copy(k, z - dist, y, "up").start()

                ag_copy(k, z - dist, y, "y").start()
                ag_copy(k, z - dist, y, "core").start()

        @pl.when(z + dist < DEPTH)
        def _():
            for k in kinds:
                ag_wait(k, z + dist, y, c)

                @pl.when(z > 0)
                def _():
                    ag_copy(k, z + dist, y, "down").start()

                ag_copy(k, z + dist, y, "y").start()
                ag_copy(k, z + dist, y, "core").start()

    def y_arrival(kinds, dist):
        def one(zz):
            for k in kinds:
                ag_wait(k, zz, 1 - y, c)
                ag_copy(k, zz, 1 - y, "core").start()

        if dist == 0:
            one(z)
            return

        @pl.when(z >= dist)
        def _():
            one(z - dist)

        @pl.when(z + dist < DEPTH)
        def _():
            one(z + dist)

    def drain(k, zz, yy):
        ag_copy(k, zz, yy, "core").wait_send()

        @pl.when(yy == y)
        def _():
            ag_copy(k, zz, y, "y").wait_send()

            @pl.when((zz <= z) & (z < DEPTH - 1))
            def _():
                ag_copy(k, zz, y, "up").wait_send()

            @pl.when((zz >= z) & (z > 0))
            def _():
                ag_copy(k, zz, y, "down").wait_send()

    def add(dst, first, second):
        count, width = dst.shape
        step = min(count, 256 * LANES // width)

        def body(i, carry):
            at = pl.ds(pl.multiple_of(i * step, 16), step)
            dst[at, :] = (first[at, :].astype(f32) + second[at, :].astype(f32)).astype(dst.dtype)
            return carry

        lax.fori_loop(0, count // step, body, 0)

    def rc_copy(k, zz, yy):
        at = zz * 2 + yy
        return remote(piece(k, zz, yy, 1 - c), core_in[k].at[at], rc_send.at[k, at], rc_recv.at[k, at], c_peer)

    def ry_copy(k, zz):
        return remote(piece(k, zz, 1 - y, c), y_in[k].at[zz], ry_send.at[k, zz], ry_recv.at[k, zz], y_peer)

    def rz_copy(k, zz):
        step = lax.rem(zz - z + DEPTH, DEPTH)
        at = DEPTH - 1 - step
        return remote(
            piece(k, zz, y, c), z_in[k].at[at], rz_send.at[k, step - 1], rz_recv.at[k, at], (slot_of(zz, y, c), t)
        )

    def rc_add(k, zz, yy):
        at = zz * 2 + yy
        remote(core_in[k].at[at], core_in[k].at[at], rc_send.at[k, 0], rc_recv.at[k, at], c_peer).wait_recv()
        mine = piece(k, zz, yy, c)
        add(mine, mine, core_in[k].at[at])

        @pl.when(yy != y)
        def _():
            ry_copy(k, zz).start()

    def ry_add(k, s):
        zz = near(s)
        remote(y_in[k].at[zz], y_in[k].at[zz], ry_send.at[k, 0], ry_recv.at[k, zz], y_peer).wait_recv()
        mine = piece(k, zz, y, c)
        if s == 0:
            add(sums[k], mine, y_in[k].at[zz])
        else:
            add(mine, mine, y_in[k].at[zz])
            rz_copy(k, zz).start()

    def rz_add(k):
        for at in range(DEPTH - 1):
            remote(z_in[k].at[at], z_in[k].at[at], rz_send.at[k, 0], rz_recv.at[k, at], y_peer).wait_recv()
            add(sums[k], sums[k], z_in[k].at[at])

    def x_rows(ref, index):
        return remote(ref.at[own], ref.at[own], x_send.at[index], x_recv.at[index], x_peer)

    def x_rows_wait(ref, index):
        remote(ref.at[other], ref.at[other], x_send.at[index], x_recv.at[index], x_peer).wait_recv()

    def x_part(index):
        return remote(far.at[index], inx.at[index], x_send.at[4 + index], x_recv.at[4 + index], x_peer)

    def by_rows(body, step=64):
        def run(i, carry):
            body(pl.multiple_of(i * step, step), step)
            return carry

        lax.fori_loop(0, rows // step, run, 0)

    def norm(value):
        average = jnp.mean(value, -1, keepdims=True)
        centred = value - average
        inverse = lax.rsqrt(jnp.mean(centred * centred, -1, keepdims=True) + EPS)
        return centred * inverse, inverse

    def norm_grad(grad, unit, inverse, gain):
        scaled = grad * gain
        return inverse * (
            scaled - jnp.mean(scaled, -1, keepdims=True) - unit * jnp.mean(scaled * unit, -1, keepdims=True)
        )

    barrier = pltpu.get_barrier_semaphore()
    z_peers = [(slot_of(lax.rem(z + step, DEPTH), y, c), t) for step in range(1, DEPTH)]
    everyone = [x_peer, y_peer, c_peer] + z_peers
    for device in everyone:
        pl.semaphore_signal(barrier, inc=1, device_id=device, device_id_type=MESH_ID)

    def prepare(held, stack):
        load = pltpu.make_async_copy(view, held, copy_sem.at[0])
        load.start()

        def first_norm(at, step):
            unit, inverse = norm(tokens[pl.ds(at, step), :])
            to = pl.ds(pl.multiple_of(t * rows + at, step), step)
            rows_one[to, :] = (unit * vecs[0:1, :] + vecs[1:2, :]).astype(bf)
            grad_rows[to, :] = cot[pl.ds(at, step), :].astype(bf)

        by_rows(first_norm)
        pl.semaphore_wait(barrier, len(everyone))
        x_rows(rows_one, 0).start()
        load.wait()
        lay_blocks(held, stack)
        n = gq.shape[1]
        gq[me, :, 0:HALF] = stack[0:n, 0:HALF].astype(bf)
        gq[me, :, HALF:LANES] = stack[n : 2 * n, 0:HALF].astype(bf)
        own_sends_y(Q)
        own_sends_z(Q)
        base = 2 * n
        wide = [stack[base + b * 64 : base + b * 64 + 64, 0:HALF] for b in range(8)]
        go[z * 2 + y, :, pl.ds(pl.multiple_of(c * 512, 512), 512)] = jnp.concatenate(wide, 1).astype(bf)
        own_sends_y(O)
        own_sends_z(O)
        base += 512
        gi[me, :, 0:HALF] = stack[base : base + 1024, 0:HALF].astype(bf)
        gi[me, :, HALF:LANES] = stack[base + 1024 : base + 2048, 0:HALF].astype(bf)
        base += 2048
        for r in range(2):
            for b in range(16):
                at = base + (r * 16 + b) * 64
                gd[me, r * 64 : r * 64 + 64, b * HALF : (b + 1) * HALF] = stack[at : at + 64, 0:HALF].astype(bf)

    pl.run_scoped(
        prepare,
        pltpu.VMEM(view.shape, f32),
        pltpu.VMEM((view.shape[2] * BLOCK, LANES), f32),
    )
    x_rows(grad_rows, 1).start()
    z_arrival((Q, O), 1)
    y_arrival((Q, O), 0)
    own_sends_z(I)
    own_sends_z(W)
    z_arrival((Q, O), 2)
    y_arrival((Q, O), 1)
    z_arrival((Q, O), 3)
    own_sends_y(I)
    own_sends_y(W)

    def core_waits(kinds, zz):
        for k in kinds:
            for yy in (y, 1 - y):
                ag_wait(k, zz, yy, 1 - c)

    x_rows_wait(rows_one, 0)

    ends = []
    for p in range(ARTICLES):
        length = 0
        for a in range(ARTICLES):
            length = length + jnp.where(order[0, p] == a, lengths[0, a], 0)
        ends.append(length + ends[-1] if p else length)

    def allowed(first, count):
        ids = lax.broadcasted_iota(jnp.int32, (rows, 1), 0) + first
        start = jnp.zeros((rows, 1), jnp.int32)
        for end in ends:
            start = jnp.where(ids >= end, end, start)
        start = jnp.where(ids >= ends[-1], ids, start)
        keys = lax.broadcasted_iota(jnp.int32, (rows, count), 1)
        return (keys <= ids) & (keys >= start)

    scale = HD ** (-0.5)
    strip = 1024

    def assemble(h):
        for yy in range(2):
            even, odd = gq.at[slot_of(h, yy, 0)], gq.at[slot_of(h, yy, 1)]
            at = yy * 192
            wqkv[h, 0:768, at : at + 64] = even[:, 0:64]
            wqkv[h, 768:1024, at : at + 64] = even[0:256, 64:128]
            wqkv[h, 0:512, at + 64 : at + 128] = even[256:768, 64:128]
            wqkv[h, 512:1024, at + 64 : at + 128] = odd[0:512, 0:64]
            wqkv[h, 0:256, at + 128 : at + 192] = odd[512:768, 0:64]
            wqkv[h, 256:1024, at + 128 : at + 192] = odd[:, 64:128]

    def disassemble(h, value):
        for yy in range(2):
            even, odd = gq.at[slot_of(h, yy, 0)], gq.at[slot_of(h, yy, 1)]
            at = yy * 192
            even[:, 0:64] = value[0:768, at : at + 64]
            even[0:256, 64:128] = value[768:1024, at : at + 64]
            even[256:768, 64:128] = value[0:512, at + 64 : at + 128]
            odd[0:512, 0:64] = value[512:1024, at + 64 : at + 128]
            odd[512:768, 0:64] = value[0:256, at + 128 : at + 192]
            odd[:, 64:128] = value[256:1024, at + 128 : at + 192]

    def lanes(start, size, unit):
        return pl.ds(pl.multiple_of(start, unit), size)

    qv = vecs[pl.ds(6 + t, 1), :]
    for h in range(DEPTH):
        none = jnp.zeros((1, HD), f32)
        qkv_bias[h] = jnp.concatenate([qv[:, h * 256 : h * 256 + 128], none, qv[:, h * 256 + 128 : h * 256 + 256]], 1)

    def head(h):
        core_waits((Q,), h)
        assemble(h)
        qkv[h] = (dot(rows_one[...], wqkv[h]) + qkv_bias[h]).astype(bf)
        for block in range(2):
            at, seen = slice(block * rows, (block + 1) * rows), (block + 1) * rows
            scores = dot_nt(qkv[h, at, 0:128], qkv[h, 0:seen, 128:256]) * scale
            scores = jnp.where(allowed(block * rows, seen), scores, NEG)
            expo = jnp.exp(scores - jnp.max(scores, -1, keepdims=True))
            low = (expo / jnp.sum(expo, -1, keepdims=True)).astype(bf)
            probs[h, at, 0:seen] = low
            ctx[at, lanes(h * HD, HD, HD)] = dot(low, qkv[h, 0:seen, 256:384]).astype(bf)

    head(near(0))
    y_arrival((Q, O), 2)
    head(near(1))
    y_arrival((Q, O), 3)
    head(near(2))
    z_arrival((I, W), 1)
    head(near(3))
    y_arrival((I, W), 0)
    for zz in range(DEPTH):
        core_waits((O,), zz)

    def w_out(at, count):
        return go[at : at + count].reshape(count * 64, 1024)

    far[0] = dot(ctx[other, :], w_out(0, 8)).astype(bf)
    x_part(0).start()
    mixed[...] = tokens[...] + dot(ctx[own, :], w_out(0, 8)) + vecs[4:5, :]
    z_arrival((I, W), 2)
    y_arrival((I, W), 1)
    x_part(0).wait_recv()

    def second_norm(at, step):
        value = mixed[pl.ds(at, step), :] + inx[0, pl.ds(at, step), :].astype(f32)
        mixed[pl.ds(at, step), :] = value
        unit, inverse = norm(value)
        to = pl.ds(pl.multiple_of(t * rows + at, step), step)
        rows_two[to, :] = (unit * vecs[2:3, :] + vecs[3:4, :]).astype(bf)

    by_rows(second_norm)
    x_rows(rows_two, 2).start()
    z_arrival((I, W), 3)
    macc[...] = jnp.zeros_like(macc)
    nacc[...] = jnp.zeros_like(nacc)
    vout[...] = jnp.zeros_like(vout)
    x_rows_wait(grad_rows, 1)

    def ffn(i, carry):
        half, s = lax.div(i, DEPTH), lax.rem(i, DEPTH)
        zz = near(s)

        @pl.when(i == 2)
        def _():
            y_arrival((I, W), 2)

        @pl.when(i == 3)
        def _():
            y_arrival((I, W), 3)

        @pl.when(half == 0)
        def _():
            core_waits((I, W), zz)

        @pl.when(i == DEPTH)
        def _():
            x_rows_wait(rows_two, 2)

        first = 4 * zz
        at = pl.ds(pl.multiple_of(lax.rem(t + half, 2) * rows, rows), rows)
        units = lanes(zz * 512, 512, 512)
        bias_row = vecs[pl.ds(8 + 2 * t + lax.div(zz, 2), 1), lanes(lax.rem(zz, 2) * 512, 512, 512)]

        def w_in(start, count):
            return jnp.concatenate([gi[first + j, start : start + count, :] for j in range(4)], 1)

        def w_down(start, count):
            return gd[pl.ds(first, 4), :, start : start + count].reshape(512, count)

        inner = dot(rows_two[at, :], w_in(0, D)) + bias_row
        square = inner * inner
        bent = jnp.tanh(GELU_A * inner * (1.0 + GELU_B * square))
        act[at, units] = (0.5 * inner * (1.0 + bent)).astype(bf)
        slope = 0.5 * (1.0 + bent) + 0.5 * inner * (1.0 - bent * bent) * (GELU_A * (1.0 + 3.0 * GELU_B * square))
        gin[at, units] = (dot_nt(grad_rows[at, :], w_down(0, D)) * slope).astype(bf)
        for nb in range(4):
            out = slice(nb * 256, nb * 256 + 256)
            nacc[at, out] += dot_nt(gin[at, units], w_in(nb * 256, 256))
            macc[at, out] += dot(act[at, units], w_down(nb * 256, 256))
        return carry

    lax.fori_loop(0, 2 * DEPTH, ffn, 0)
    far[1] = nacc[other, :].astype(bf)
    x_part(1).start()
    far[2] = macc[other, :].astype(bf)
    x_part(2).start()

    rows_t[...] = rows_two[...].T

    def ffn_grads(i, carry):
        zz = near(DEPTH - 1 - i)
        first = 4 * zz
        units = lanes(zz * 512, 512, 512)
        for k in (I, W):
            for yy in range(2):
                drain(k, zz, yy)
        bias_sum[zz] = jnp.sum(gin[:, units].astype(f32), 0, keepdims=True)
        for nb in range(4):
            out = slice(nb * 256, nb * 256 + 256)
            part = dot(rows_t[out, :], gin[:, units]).astype(bf)
            for j in range(4):
                gi[first + j, out, :] = part[:, j * LANES : (j + 1) * LANES]
        for yy in (1 - y, y):
            rc_copy(I, zz, yy).start()
        act_t = act[:, units].T
        for nb in range(4):
            out = slice(nb * 256, nb * 256 + 256)
            part = dot(act_t, grad_rows[:, out]).astype(bf)
            gd[pl.ds(first, 4), :, out] = part.reshape(4, LANES, 256)
        for yy in (1 - y, y):
            rc_copy(W, zz, yy).start()

        @pl.when(i > 0)
        def _():
            before = near(DEPTH - i)
            for yy in (1 - y, y):
                for k in (I, W):
                    rc_add(k, before, yy)

        return carry

    lax.fori_loop(0, DEPTH, ffn_grads, 0)
    for yy in (1 - y, y):
        for k in (I, W):
            rc_add(k, near(0), yy)
    for zz in range(DEPTH):
        for side in range(2):
            row, start = 8 + 2 * side + zz // 2, zz % 2 * 512
            vout[0, row : row + 1, start : start + 512] = jnp.where(t == side, bias_sum[zz], 0.0)
    rows_t[...] = rows_one[...].T
    x_part(1).wait_recv()

    def row_sum(row, value):
        vout[0, row : row + 1, :] += jnp.sum(value, 0, keepdims=True)

    def second_back(at, step):
        here = pl.ds(at, step)
        in_group = pl.ds(pl.multiple_of(t * rows + at, step), step)
        grad = nacc[in_group, :] + inx[1, here, :].astype(f32)
        unit, inverse = norm(mixed[here, :])
        back = cot[here, :] + norm_grad(grad, unit, inverse, vecs[2:3, :])
        input_grad[here, :] = back
        grad_attn[in_group, :] = back.astype(bf)
        row_sum(2, grad * unit)
        row_sum(3, grad)
        row_sum(4, back)
        row_sum(5, cot[here, :])

    by_rows(second_back)
    x_rows(grad_attn, 3).start()
    for s in (3, 2):
        for k in (I, W):
            ry_add(k, s)
    x_part(2).wait_recv()

    def mixed_out(at, step):
        here = pl.ds(at, step)
        in_group = pl.ds(pl.multiple_of(t * rows + at, step), step)
        mixed[here, :] = mixed[here, :] + macc[in_group, :] + inx[2, here, :].astype(f32) + vecs[5:6, :]

    by_rows(mixed_out)
    for zz in range(DEPTH):
        for yy in range(2):
            drain(O, zz, yy)
            drain(Q, zz, yy)
    x_rows_wait(grad_attn, 3)
    gctx[...] = dot_nt(grad_attn[...], w_out(0, 8)).astype(bf)
    ctx_t = ctx[...].T
    for nb in range(4):
        at = slice(nb * 256, nb * 256 + 256)
        go[:, :, at] = dot(ctx_t, grad_attn[:, at]).astype(bf).reshape(8, 64, 256)
    for zz in range(DEPTH):
        for yy in range(2):
            rc_copy(O, zz, yy).start()

    def head_back(h):
        q0, q1 = qkv[h, 0:rows, 0:128], qkv[h, rows : 2 * rows, 0:128]
        grads = []
        for block in range(2):
            at, seen = slice(block * rows, (block + 1) * rows), (block + 1) * rows
            low = probs[h, at, 0:seen]
            given = gctx[at, h * 128 : h * 128 + 128]
            prob = low.astype(f32)
            grad_probs = dot_nt(given, qkv[h, 0:seen, 256:384])
            delta = jnp.sum(prob * grad_probs, -1, keepdims=True)
            grad_scores = (prob * (grad_probs - delta)).astype(bf)
            grad_q = dot(grad_scores, qkv[h, 0:seen, 128:256]) * scale
            grad_k = dot_tn(grad_scores, q1 if block else q0) * scale
            grad_v = dot_tn(low, given)
            grads.append((grad_q, grad_k, grad_v))
        (gq0, gk0, gv0), (gq1, gk1, gv1) = grads
        top = jnp.concatenate([gq0, gk0 + gk1[0:rows], gv0 + gv1[0:rows]], 1).astype(bf)
        low_half = jnp.concatenate([gq1, gk1[rows:], gv1[rows:]], 1).astype(bf)
        qkv[h, 0:rows, :] = top
        qkv[h, rows : 2 * rows, :] = low_half
        total = jnp.sum(top.astype(f32), 0, keepdims=True) + jnp.sum(low_half.astype(f32), 0, keepdims=True)
        for side in range(2):
            vout[0, 6 + side : 7 + side, h * 256 : h * 256 + 128] = jnp.where(t == side, total[:, 0:128], 0.0)
            vout[0, 6 + side : 7 + side, h * 256 + 128 : h * 256 + 256] = jnp.where(t == side, total[:, 256:384], 0.0)
        part = dot(rows_t[...], qkv[h]).astype(bf)
        disassemble(h, part)
        for yy in (1 - y, y):
            rc_copy(Q, h, yy).start()
        product = dot_nt(qkv[h], wqkv[h])
        if h == 0:
            nacc[...] = product
        else:
            nacc[...] += product

    for h in range(DEPTH):
        head_back(h)
        if h == 0:
            for yy in (1 - y, y):
                for s in range(DEPTH):
                    rc_add(O, near(s), yy)
        else:
            for yy in (1 - y, y):
                rc_add(Q, h - 1, yy)
    far[3] = nacc[other, :].astype(bf)
    x_part(3).start()
    for yy in (1 - y, y):
        rc_add(Q, DEPTH - 1, yy)
    for s in (1, 0):
        for k in (I, W):
            ry_add(k, s)
    x_part(3).wait_recv()

    def first_back(at, step):
        here = pl.ds(at, step)
        in_group = pl.ds(pl.multiple_of(t * rows + at, step), step)
        grad = nacc[in_group, :] + inx[3, here, :].astype(f32)
        unit, inverse = norm(tokens[here, :])
        input_grad[here, :] = input_grad[here, :] + norm_grad(grad, unit, inverse, vecs[0:1, :])
        row_sum(0, grad * unit)
        row_sum(1, grad)

    by_rows(first_back)

    stages = (x_peer, c_peer, y_peer)

    def v_copy(stage):
        return remote(vout.at[stage], vin.at[stage], v_send.at[stage], v_recv.at[stage], stages[stage])

    def vz_copy(step):
        peer = (slot_of(lax.rem(z + step, DEPTH), y, c), t)
        return remote(vout.at[3], vin.at[3 + z], v_send.at[2 + step], v_recv.at[3 + z], peer)

    v_copy(0).start()
    for k in (O, Q):
        for s in range(1, DEPTH):
            ry_add(k, s)
        if k == O:
            v_copy(0).wait_recv()
            vout[1] = vout[0] + vin[0]
            v_copy(1).start()
            ry_add(k, 0)
    v_copy(1).wait_recv()
    vout[2] = vout[1] + vin[1]
    v_copy(2).start()
    ry_add(Q, 0)
    for k in (I, W, O):
        rz_add(k)
    v_copy(2).wait_recv()
    vout[3] = vout[2] + vin[2]
    for step in range(1, DEPTH):
        vz_copy(step).start()
    vin[3 + z] = vout[3]
    rz_add(Q)
    for step in range(1, DEPTH):
        zz = lax.rem(z + step, DEPTH)
        remote(vin.at[3 + zz], vin.at[3 + zz], v_send.at[0], v_recv.at[3 + zz], y_peer).wait_recv()
    count = vec_grads.shape[0]
    total = ((vin[3] + vin[4]) + vin[5]) + vin[6]
    vec_grads[...] = total[0:count]

    for stage in range(3):
        v_copy(stage).wait_send()
    for step in range(1, DEPTH):
        vz_copy(step).wait_send()
    for index, ref in enumerate((rows_one, grad_rows, rows_two, grad_attn)):
        x_rows(ref, index).wait_send()
    for index in range(4):
        x_part(index).wait_send()
    for k in range(4):
        for zz in range(DEPTH):
            for yy in range(2):
                rc_copy(k, zz, yy).wait_send()
            ry_copy(k, zz).wait_send()
        for s in range(1, DEPTH):
            rz_copy(k, near(s)).wait_send()


def run_layer(tokens, cotangent, lengths, order, weights, vec_params):
    bf, f32 = jnp.bfloat16, jnp.float32
    rows = tokens.shape[0]
    group = 2 * rows
    owners = 16
    shapes = piece_shapes()
    view = jnp.transpose(weights, (1, 2, 0))
    vmem = pl.BlockSpec(memory_space=pltpu.VMEM)
    smem = pl.BlockSpec(memory_space=pltpu.SMEM)

    def many(count):
        return [pltpu.VMEM((count,) + s, bf) for s in shapes]

    full = pltpu.VMEM((group, D), bf)
    dma = pltpu.SemaphoreType.DMA
    return pl.pallas_call(
        layer_kernel,
        out_shape=[jax.ShapeDtypeStruct((rows, D), f32)] * 2
        + [jax.ShapeDtypeStruct(s, f32) for s in shapes]
        + [jax.ShapeDtypeStruct(vec_params.shape, f32)],
        in_specs=[smem, smem, pl.BlockSpec(memory_space=pl.ANY)] + [vmem] * 3,
        out_specs=[vmem] * 7,
        scratch_shapes=[
            pltpu.VMEM((owners,) + shapes[0], bf),
            pltpu.VMEM((owners // 2, BLOCK, D), bf),
            pltpu.VMEM((owners,) + shapes[2], bf),
            pltpu.VMEM((owners,) + shapes[3], bf),
            pltpu.VMEM((DEPTH, D, 3 * HD), bf),
        ]
        + many(2 * DEPTH)
        + many(DEPTH)
        + many(DEPTH - 1)
        + [
            full,
            full,
            pltpu.VMEM((D, group), bf),
            full,
            full,
            pltpu.VMEM((DEPTH, group, group), bf),
            pltpu.VMEM((DEPTH, group, 3 * HD), bf),
            pltpu.VMEM((group, DEPTH * HD), bf),
            pltpu.VMEM((group, DEPTH * HD), bf),
            pltpu.VMEM((4, rows, D), bf),
            pltpu.VMEM((4, rows, D), bf),
            pltpu.VMEM((group, D), f32),
            pltpu.VMEM((group, D), f32),
            pltpu.VMEM((group, 2 * D), bf),
            pltpu.VMEM((group, 2 * D), bf),
            pltpu.VMEM((DEPTH, 1, 512), f32),
            pltpu.VMEM((DEPTH, 1, 3 * HD), f32),
            pltpu.VMEM((7, 16, D), f32),
            pltpu.VMEM((4, 16, D), f32),
            dma((4, owners)),
            dma((4, DEPTH)),
            dma((4, 2 * DEPTH)),
            dma((4, 2, DEPTH)),
            dma((4, 2 * DEPTH)),
            dma((4, 2 * DEPTH)),
            dma((4, DEPTH)),
            dma((4, DEPTH)),
            dma((4, DEPTH - 1)),
            dma((4, DEPTH - 1)),
            dma((8,)),
            dma((8,)),
            dma((6,)),
            dma((7,)),
            dma((1,)),
        ],
        compiler_params=pltpu.CompilerParams(
            collective_id=0, has_side_effects=True, vmem_limit_bytes=VMEM_LIMIT
        ),
        name="layer",
    )(lengths, order, view, tokens, cotangent, vec_params)


def per_device(
    grp_count,
    tp_count,
    tokens,
    cotangent,
    lengths,
    order,
    weights,
    momentum,
    stat_left,
    stat_right,
    root_left,
    root_right,
    vec_params,
    vec_momentum,
    vec_second,
):
    fits = grp_count == 4 * DEPTH and tp_count == 2 and tokens.shape[0] == 256
    if not fits or lengths.shape[1] != ARTICLES:
        return per_device_general(
            tokens,
            cotangent,
            lengths,
            order,
            weights,
            momentum,
            stat_left,
            stat_right,
            root_left,
            root_right,
            vec_params,
            vec_momentum,
            vec_second,
        )
    token_total = tokens.shape[0] * tp_count * grp_count
    mixed, input_grad, *sums, vec_grads = run_layer(tokens, cotangent, lengths, order, weights, vec_params)
    blocks, vecs, results = update_blocks(
        sums,
        (weights, momentum, stat_left, stat_right, root_left, root_right),
        vec_grads,
        (vec_params, vec_momentum, vec_second),
        (mixed, input_grad),
        token_total,
    )
    return (*results, *blocks, *vecs)


def solution(mesh):
    placed = (
        P(("grp", "tp"), None),
        P(("grp", "tp"), None),
        P("grp", None),
        P("grp", None),
        P(("tp", "grp"), None, None),
        P(("tp", "grp"), None, None),
        P(("tp", "grp"), None, None),
        P(("tp", "grp"), None, None),
        P(("tp", "grp"), None, None),
        P(("tp", "grp"), None, None),
        P(),
        P(),
        P(),
    )
    return jax.shard_map(
        functools.partial(per_device, mesh.shape["grp"], mesh.shape["tp"]),
        mesh=mesh,
        in_specs=placed,
        out_specs=(
            P(("grp", "tp"), None),
            P(("grp", "tp"), None),
            P(("tp", "grp"), None, None),
            P(("tp", "grp"), None, None),
            P(("tp", "grp"), None, None),
            P(("tp", "grp"), None, None),
            P(("tp", "grp"), None, None),
            P(),
            P(),
            P(),
            P(),
        ),
        check_vma=False,
    )
```

```python
import functools

import jax
import jax.numpy as jnp
from jax import lax
from jax.experimental import pallas as pl
from jax.experimental.pallas import tpu as pltpu
from jax.sharding import PartitionSpec as P

D = 1024
HEADS = 8
HD = 128
FF = 4096
BLOCK = 64


EPS = 1e-05
NEG = -1e30
DECAY = 0.9
BETA = 0.9
RATE = 0.05
VEC_DECAY = 0.9
VEC_RATE = 0.2
VEC_EPS = 1e-08


def norm_rows(value, gain, shift):
    average = jnp.mean(value, -1, keepdims=True)
    centred = value - average
    inverse = lax.rsqrt(jnp.mean(centred * centred, -1, keepdims=True) + EPS)
    normed = centred * inverse
    return (normed * gain + shift, normed, inverse)


def norm_back(grad_out, normed, inverse, gain):
    scaled = grad_out * gain
    return inverse * (
        scaled
        - jnp.mean(scaled, -1, keepdims=True)
        - normed * jnp.mean(scaled * normed, -1, keepdims=True)
    )


def segment_ids(lengths_row, order_row, group_rows):
    article_count = lengths_row.shape[0]
    slots = jnp.arange(article_count, dtype=jnp.int32)
    picks = (order_row[:, None] == slots[None, :]).astype(jnp.int32)
    packed = jnp.sum(picks * lengths_row[None, :], 1)
    ends = jnp.cumsum(packed)
    spots = jnp.arange(group_rows, dtype=jnp.int32)
    return jnp.sum((spots[:, None] >= ends[None, :]).astype(jnp.int32), 1)


def allowed_mask(row_ids, row_segs, segments, key_ids, article_count):
    causal = key_ids[None, :] <= row_ids[:, None]
    same = segments[None, :] == row_segs[:, None]
    alone = (row_segs[:, None] < article_count) | (key_ids[None, :] == row_ids[:, None])
    return causal & same & alone


def from_columns(tiles, row_total, col_total):
    return (
        tiles.reshape(col_total // BLOCK, row_total // BLOCK, BLOCK, BLOCK)
        .transpose(1, 2, 0, 3)
        .reshape(row_total, col_total)
    )


def from_rows(tiles, row_total, col_total):
    return (
        tiles.reshape(row_total // BLOCK, col_total // BLOCK, BLOCK, BLOCK)
        .transpose(0, 2, 1, 3)
        .reshape(row_total, col_total)
    )


def to_columns(matrix):
    row_total, col_total = matrix.shape
    return (
        matrix.reshape(row_total // BLOCK, BLOCK, col_total // BLOCK, BLOCK)
        .transpose(2, 0, 1, 3)
        .reshape(-1, BLOCK, BLOCK)
    )


def to_rows(matrix):
    row_total, col_total = matrix.shape
    return (
        matrix.reshape(row_total // BLOCK, BLOCK, col_total // BLOCK, BLOCK)
        .transpose(0, 2, 1, 3)
        .reshape(-1, BLOCK, BLOCK)
    )


def per_device_general(
    tokens,
    cotangent,
    lengths,
    order,
    weights,
    momentum,
    stat_left,
    stat_right,
    root_left,
    root_right,
    vec_params,
    vec_momentum,
    vec_second,
):
    groups = lax.axis_size("grp")
    tp_size = lax.axis_size("tp")
    tp_rank = lax.axis_index("tp")
    tok_rows = tokens.shape[0]
    group_rows = tok_rows * tp_size
    article_count = lengths.shape[1]
    owners = groups * tp_size
    block_area = BLOCK * BLOCK * owners
    qkv_count = 3 * D * D // block_area
    out_count = D * D // block_area
    in_count = D * FF // block_area
    owned_blocks = weights.shape[0]
    heads_here = HEADS // tp_size
    qkv_cols = 3 * D // tp_size
    feat_here = D // tp_size
    ff_here = FF // tp_size
    qv_width = 2 * D // tp_size
    token_total = group_rows * groups
    gathered = lax.all_gather(weights.astype(jnp.bfloat16), "grp", axis=0, tiled=True)
    per_owner = gathered.reshape(groups, owned_blocks, BLOCK, BLOCK)
    marks = [0, qkv_count, qkv_count + out_count, qkv_count + out_count + in_count, owned_blocks]
    pieces = [
        per_owner[:, marks[index] : marks[index + 1]].reshape(-1, BLOCK, BLOCK)
        for index in range(4)
    ]
    w_qkv = from_columns(pieces[0], D, qkv_cols)
    w_out = from_rows(pieces[1], feat_here, D)
    w_in = from_columns(pieces[2], D, ff_here)
    w_down = from_rows(pieces[3], ff_here, D)
    w_qkv_heads = w_qkv.reshape(D, heads_here, 3, HD)
    w_out_heads = w_out.reshape(heads_here, HD, D)
    segments = segment_ids(lengths[0], order[0], group_rows)
    gain_one = vec_params[0]
    shift_one = vec_params[1]
    gain_two = vec_params[2]
    shift_two = vec_params[3]
    bias_out = vec_params[4]
    bias_down = vec_params[5]
    qv_here = lax.dynamic_slice_in_dim(
        vec_params[6:8].reshape(2 * D), tp_rank * qv_width, qv_width
    ).reshape(heads_here, 2, HD)
    bias_heads = jnp.stack(
        [qv_here[:, 0], jnp.zeros((heads_here, HD), jnp.float32), qv_here[:, 1]], 0
    )[:, :, None, :]
    bias_in = lax.dynamic_slice_in_dim(vec_params[8:].reshape(FF), tp_rank * ff_here, ff_here)
    normed_one, unit_one, inverse_one = norm_rows(tokens, gain_one, shift_one)
    rows_one = lax.all_gather(normed_one.astype(jnp.bfloat16), "tp", axis=0, tiled=True)
    projected = (
        jnp.einsum("rx,xhcd->chrd", rows_one, w_qkv_heads, preferred_element_type=jnp.float32)
        + bias_heads
    ).astype(jnp.bfloat16)
    queries = projected[0]
    keys_all = projected[1]
    values_all = projected[2]
    span = min(512, group_rows)
    starts = jnp.arange(group_rows // span, dtype=jnp.int32) * span
    key_ids = jnp.arange(group_rows, dtype=jnp.int32)
    score_scale = HD ** (-0.5)

    def masked_scores(first_row):
        row_ids = first_row + jnp.arange(span, dtype=jnp.int32)
        row_segs = lax.dynamic_slice_in_dim(segments, first_row, span, 0)
        allowed = allowed_mask(row_ids, row_segs, segments, key_ids, article_count)
        query_rows = lax.dynamic_slice_in_dim(queries, first_row, span, 1)
        scores = (
            jnp.einsum("hqd,hkd->hqk", query_rows, keys_all, preferred_element_type=jnp.float32)
            * score_scale
        )
        return (jnp.where(allowed[None], scores, NEG), query_rows)

    def attend(context_buf, first_row):
        scores, query_rows = masked_scores(first_row)
        row_max = jnp.max(scores, -1, keepdims=True)
        expo = jnp.exp(scores - row_max)
        expsum = jnp.sum(expo, -1, keepdims=True)
        probs_low = (expo / expsum).astype(jnp.bfloat16)
        context = jnp.einsum(
            "hqk,hkd->hqd", probs_low, values_all, preferred_element_type=jnp.float32
        ).astype(jnp.bfloat16)
        context_buf = lax.dynamic_update_slice_in_dim(context_buf, context, first_row, 1)
        return (context_buf, (row_max + jnp.log(expsum))[:, :, 0])

    context_low, log_norm = lax.scan(
        attend, jnp.zeros((heads_here, group_rows, HD), jnp.bfloat16), starts
    )
    attn_sum = lax.psum_scatter(
        jnp.einsum(
            "hrd,hde->re", context_low, w_out_heads, preferred_element_type=jnp.float32
        ).astype(jnp.bfloat16),
        "tp",
        scatter_dimension=0,
        tiled=True,
    ).astype(jnp.float32)
    hidden = tokens + attn_sum + bias_out
    normed_two, unit_two, inverse_two = norm_rows(hidden, gain_two, shift_two)
    rows_two = lax.all_gather(normed_two.astype(jnp.bfloat16), "tp", axis=0, tiled=True)
    inner = jnp.dot(rows_two, w_in, preferred_element_type=jnp.float32) + bias_in
    activ, gelu_pull = jax.vjp(jax.nn.gelu, inner)
    activ_low = activ.astype(jnp.bfloat16)
    mixed = (
        hidden
        + lax.psum_scatter(
            jnp.dot(activ_low, w_down, preferred_element_type=jnp.float32).astype(jnp.bfloat16),
            "tp",
            scatter_dimension=0,
            tiled=True,
        ).astype(jnp.float32)
        + bias_down
    )
    grad_low = cotangent.astype(jnp.bfloat16)
    grad_rows = lax.all_gather(grad_low, "tp", axis=0, tiled=True)
    g_down = jnp.einsum("rf,rd->fd", activ_low, grad_rows, preferred_element_type=jnp.float32)
    grad_activ = jnp.einsum("rd,fd->rf", grad_rows, w_down, preferred_element_type=jnp.float32)
    grad_inner = gelu_pull(grad_activ)[0].astype(jnp.bfloat16)
    g_in = jnp.einsum("rd,rf->df", rows_two, grad_inner, preferred_element_type=jnp.float32)
    g_bias_in = jnp.sum(grad_inner.astype(jnp.float32), 0)
    ffn_blocks = jnp.concatenate(
        [
            to_columns(g_in).reshape(groups, in_count, BLOCK, BLOCK),
            to_rows(g_down).reshape(groups, in_count, BLOCK, BLOCK),
        ],
        1,
    )
    grad_normed_two = lax.psum_scatter(
        jnp.einsum("rf,df->rd", grad_inner, w_in, preferred_element_type=jnp.float32).astype(
            jnp.bfloat16
        ),
        "tp",
        scatter_dimension=0,
        tiled=True,
    ).astype(jnp.float32)
    grad_hidden = cotangent + norm_back(grad_normed_two, unit_two, inverse_two, gain_two)
    grad_attn_low = grad_hidden.astype(jnp.bfloat16)
    grad_attn_rows = lax.all_gather(grad_attn_low, "tp", axis=0, tiled=True)
    g_out = jnp.einsum(
        "hrd,re->hde", context_low, grad_attn_rows, preferred_element_type=jnp.float32
    ).reshape(feat_here, D)
    grad_context = jnp.einsum(
        "re,hde->hrd", grad_attn_rows, w_out_heads, preferred_element_type=jnp.float32
    ).astype(jnp.bfloat16)
    zero_heads = jnp.zeros((heads_here, group_rows, HD), jnp.float32)

    def attend_back(carry, inputs):
        grad_queries, grad_keys, grad_values = carry
        first_row, log_block = inputs
        scores, query_rows = masked_scores(first_row)
        probs = jnp.exp(scores - log_block[:, :, None])
        grad_ctx_rows = lax.dynamic_slice_in_dim(grad_context, first_row, span, 1)
        grad_probs = jnp.einsum(
            "hqd,hkd->hqk", grad_ctx_rows, values_all, preferred_element_type=jnp.float32
        )
        delta = jnp.sum(probs * grad_probs, -1, keepdims=True)
        grad_scores = (probs * (grad_probs - delta)).astype(jnp.bfloat16)
        query_part = (
            jnp.einsum("hqk,hkd->hqd", grad_scores, keys_all, preferred_element_type=jnp.float32)
            * score_scale
        )
        grad_queries = lax.dynamic_update_slice_in_dim(grad_queries, query_part, first_row, 1)
        grad_keys = (
            grad_keys
            + jnp.einsum(
                "hqk,hqd->hkd", grad_scores, query_rows, preferred_element_type=jnp.float32
            )
            * score_scale
        )
        grad_values = grad_values + jnp.einsum(
            "hqk,hqd->hkd",
            probs.astype(jnp.bfloat16),
            grad_ctx_rows,
            preferred_element_type=jnp.float32,
        )
        return ((grad_queries, grad_keys, grad_values), None)

    (grad_queries, grad_keys, grad_values), unused = lax.scan(
        attend_back, (zero_heads, zero_heads, zero_heads), (starts, log_norm)
    )
    grad_proj = jnp.stack([grad_queries, grad_keys, grad_values], 0).astype(jnp.bfloat16)
    proj_sums = jnp.sum(grad_proj.astype(jnp.float32), 2)
    g_bias_qv = jnp.stack([proj_sums[0], proj_sums[2]], 1).reshape(qv_width)
    g_qkv = jnp.einsum(
        "rx,chrd->xhcd", rows_one, grad_proj, preferred_element_type=jnp.float32
    ).reshape(D, qkv_cols)
    grad_normed_one = lax.psum_scatter(
        jnp.einsum(
            "chrd,xhcd->rx", grad_proj, w_qkv_heads, preferred_element_type=jnp.float32
        ).astype(jnp.bfloat16),
        "tp",
        scatter_dimension=0,
        tiled=True,
    ).astype(jnp.float32)
    input_grad = grad_hidden + norm_back(grad_normed_one, unit_one, inverse_one, gain_one)
    local_rows = jnp.stack(
        [
            jnp.sum(grad_normed_one * unit_one, 0),
            jnp.sum(grad_normed_one, 0),
            jnp.sum(grad_normed_two * unit_two, 0),
            jnp.sum(grad_normed_two, 0),
            jnp.sum(grad_hidden, 0),
            jnp.sum(cotangent, 0),
        ]
    )
    qv_rows = lax.dynamic_update_slice(
        jnp.zeros((2 * D,), jnp.float32), g_bias_qv, (tp_rank * qv_width,)
    ).reshape(2, D)
    in_rows = lax.dynamic_update_slice(
        jnp.zeros((FF,), jnp.float32), g_bias_in, (tp_rank * ff_here,)
    ).reshape(FF // D, D)
    vec_grads = lax.psum(jnp.concatenate([local_rows, qv_rows, in_rows], 0), ("grp", "tp"))
    attn_blocks = jnp.concatenate(
        [
            to_columns(g_qkv).reshape(groups, qkv_count, BLOCK, BLOCK),
            to_rows(g_out).reshape(groups, out_count, BLOCK, BLOCK),
        ],
        1,
    )
    every_block = jnp.concatenate([attn_blocks, ffn_blocks], 1).reshape(-1, BLOCK, BLOCK)
    weight_grads = lax.psum_scatter(
        every_block.astype(jnp.bfloat16), "grp", scatter_dimension=0, tiled=True
    ).astype(jnp.float32)
    scaled = weight_grads * token_total ** (-0.5)
    stat_left_new = DECAY * stat_left + (1.0 - DECAY) * jnp.einsum(
        "nij,nkj->nik", scaled, scaled, precision=lax.Precision.HIGHEST
    )
    stat_right_new = DECAY * stat_right + (1.0 - DECAY) * jnp.einsum(
        "nji,njk->nik", scaled, scaled, precision=lax.Precision.HIGHEST
    )
    shaped = jnp.einsum("nij,njk->nik", root_left, scaled, precision=lax.Precision.HIGHEST)
    shaped = jnp.einsum("nij,njk->nik", shaped, root_right, precision=lax.Precision.HIGHEST)
    momentum_new = BETA * momentum + shaped
    weights_new = weights - RATE * momentum_new
    vec_scaled = vec_grads * token_total ** (-0.5)
    vec_second_new = VEC_DECAY * vec_second + (1.0 - VEC_DECAY) * vec_scaled * vec_scaled
    vec_momentum_new = BETA * vec_momentum + vec_scaled * lax.rsqrt(vec_second_new + VEC_EPS)
    vec_new = vec_params - VEC_RATE * vec_momentum_new
    return (
        mixed,
        input_grad,
        weight_grads,
        stat_left_new,
        stat_right_new,
        momentum_new,
        weights_new,
        vec_grads,
        vec_second_new,
        vec_momentum_new,
        vec_new,
    )


MESH_ID = pl.DeviceIdType.MESH
LANES = 128
HALF = 64
VMEM_LIMIT = 62 * 2**20
ARTICLES = 4
GELU_A = (2.0 / 3.141592653589793) ** 0.5
GELU_B = 0.044715


def remote(src, dst, send_sem, recv_sem, device):
    return pltpu.make_async_remote_copy(
        src_ref=src,
        dst_ref=dst,
        send_sem=send_sem,
        recv_sem=recv_sem,
        device_id=device,
        device_id_type=MESH_ID,
    )


def place():
    grp = lax.axis_index("grp")
    return lax.div(grp, 4), lax.rem(lax.div(grp, 2), 2), lax.rem(grp, 2), lax.axis_index("tp")


def slot_of(z, y, c):
    return z * 4 + y * 2 + c


def lay_blocks(view_ref, stack):
    count = view_ref.shape[2]

    def row(i, carry):
        stack[pl.ds(i, count, stride=BLOCK), 0:HALF] = view_ref[i].T
        return carry

    lax.fori_loop(0, BLOCK, row, 0, unroll=8)


def piece_shapes():
    return ((768, LANES), (64, 512), (1024, LANES), (LANES, 1024))


def fold_tiles(value, mask):
    kept = jnp.where(mask, value, 0.0)
    halves = kept[:, :LANES] + kept[:, LANES:]
    return halves + pltpu.roll(halves, HALF, 1)


def update_kernel(
    scale,
    sum_q,
    sum_o,
    sum_i,
    sum_d,
    root_l,
    root_r,
    vec_g,
    vecs,
    vec_m,
    vec_s,
    mixed,
    input_grad,
    w,
    m,
    sl,
    sr,
    out_g,
    out_sl,
    out_sr,
    out_m,
    out_w,
    out_vg,
    out_vs,
    out_vm,
    out_v,
    out_mixed,
    out_input_grad,
    first,
    second,
):
    count = root_l.shape[2]
    bf = jnp.bfloat16
    out_mixed[...] = mixed[...]
    out_input_grad[...] = input_grad[...]

    @pl.when(pl.program_id(0) == 0)
    def _():
        total = vec_g[...]
        out_vg[...] = total
        scaled = total * scale
        fresh = VEC_DECAY * vec_s[...] + (1.0 - VEC_DECAY) * scaled * scaled
        out_vs[...] = fresh
        momentum = BETA * vec_m[...] + scaled * lax.rsqrt(fresh + VEC_EPS)
        out_vm[...] = momentum
        out_v[...] = vecs[...] - VEC_RATE * momentum
        rows = sum_q.shape[0]
        first[0:rows, 0:HALF] = sum_q[:, 0:HALF]
        first[rows : 2 * rows, 0:HALF] = sum_q[:, HALF:LANES]
        base = 2 * rows
        for b in range(8):
            first[base + b * 64 : base + b * 64 + 64, 0:HALF] = sum_o[:, b * HALF : (b + 1) * HALF]
        base += 512
        first[base : base + 1024, 0:HALF] = sum_i[:, 0:HALF]
        first[base + 1024 : base + 2048, 0:HALF] = sum_i[:, HALF:LANES]
        base += 2048
        for r in range(2):
            for b in range(16):
                at = base + (r * 16 + b) * 64
                first[at : at + 64, 0:HALF] = sum_d[r * 64 : r * 64 + 64, b * HALF : (b + 1) * HALF]

        def row(i, carry):
            both = jnp.concatenate([root_l[i], root_r[i]], 0)
            second[pl.ds(i, count, stride=BLOCK), :] = both.T
            return carry

        lax.fori_loop(0, BLOCK, row, 0, unroll=8)
        row_id = lax.broadcasted_iota(jnp.int32, (256, 256), 0)
        col_id = lax.broadcasted_iota(jnp.int32, (256, 256), 1)
        mask = lax.shift_right_logical(row_id, 6) == lax.shift_right_logical(col_id, 6)
        zero = jnp.zeros((256, 256), jnp.float32)

        def spread(v):
            return jnp.where(mask, jnp.concatenate([v, v, v, v], 1), zero).astype(bf)

        def four(k, carry):
            at = pl.ds(pl.multiple_of(k * 256, 256), 256)
            s32 = first[at, 0:HALF] * scale
            s = s32.astype(bf)
            left = second[at, 0:HALF]
            right = second[at, HALF:LANES].astype(bf)
            outer = lax.dot_general(s, s, (((1,), (1,)), ((), ())), preferred_element_type=jnp.float32)
            inner = lax.dot_general(spread(s32), s, (((0,), (0,)), ((), ())), preferred_element_type=jnp.float32)
            shaped = jnp.dot(spread(left), s, preferred_element_type=jnp.float32)
            shaped = jnp.dot(spread(shaped), right, preferred_element_type=jnp.float32)
            first[at, HALF:LANES] = fold_tiles(outer, mask)[:, HALF:LANES]
            second[at, 0:HALF] = inner
            second[at, HALF:LANES] = shaped
            return carry

        lax.fori_loop(0, count // 4, four, 0, unroll=4)

    i0 = pl.program_id(0) * w.shape[0]

    def rows_out(ii, carry):
        at = pl.ds(i0 + ii, count, stride=BLOCK)
        one = first[at, :].T
        two = second[at, :].T
        out_g[ii] = one[0:HALF]
        out_sl[ii] = DECAY * sl[ii] + (1.0 - DECAY) * one[HALF:LANES]
        out_sr[ii] = DECAY * sr[ii] + (1.0 - DECAY) * two[0:HALF]
        fresh = BETA * m[ii] + two[HALF:LANES]
        out_m[ii] = fresh
        out_w[ii] = w[ii] - RATE * fresh
        return carry

    lax.fori_loop(0, w.shape[0], rows_out, 0, unroll=True)


def update_blocks(sums, blocks, vec_grads, vecs, results, token_total):
    views = [jnp.transpose(a, (1, 2, 0)) for a in blocks]
    count = blocks[0].shape[0]
    rows = 8
    whole = pl.BlockSpec(memory_space=pltpu.VMEM)
    steps = BLOCK // rows
    some = pl.BlockSpec((results[0].shape[0] // steps, results[0].shape[1]), lambda i: (i, 0))
    part = pl.BlockSpec((rows, BLOCK, count), lambda i: (i, 0, 0))
    vec = jax.ShapeDtypeStruct(vec_grads.shape, jnp.float32)
    outs = pl.pallas_call(
        functools.partial(update_kernel, token_total ** (-0.5)),
        grid=(steps,),
        out_shape=[jax.ShapeDtypeStruct((BLOCK, BLOCK, count), jnp.float32)] * 5
        + [vec] * 4
        + [jax.ShapeDtypeStruct(a.shape, a.dtype) for a in results],
        in_specs=[whole] * 10 + [some] * 2 + [part] * 4,
        out_specs=[part] * 5 + [whole] * 4 + [some] * 2,
        scratch_shapes=[
            pltpu.VMEM((count * BLOCK, LANES), jnp.float32),
            pltpu.VMEM((count * BLOCK, LANES), jnp.float32),
        ],
        compiler_params=pltpu.CompilerParams(vmem_limit_bytes=VMEM_LIMIT),
        name="update_blocks",
    )(*sums, *views[4:], vec_grads, *vecs, *results, *views[:4])
    return [jnp.transpose(a, (2, 0, 1)) for a in outs[:5]], outs[5:9], outs[9:]


DEPTH = 4


def layer_kernel(
    lengths,
    order,
    view,
    tokens,
    cot,
    vecs,
    mixed,
    input_grad,
    sum_q,
    sum_o,
    sum_i,
    sum_d,
    vec_grads,
    gq,
    go,
    gi,
    gd,
    wqkv,
    cq,
    co,
    ci,
    cd,
    yq,
    yo,
    yi,
    yd,
    zq,
    zo,
    zi,
    zd,
    rows_one,
    rows_two,
    rows_t,
    grad_rows,
    grad_attn,
    probs,
    qkv,
    ctx,
    gctx,
    far,
    inx,
    macc,
    nacc,
    act,
    gin,
    bias_sum,
    qkv_bias,
    vin,
    vout,
    recv,
    send_y,
    send_c,
    send_z,
    rc_recv,
    rc_send,
    ry_recv,
    ry_send,
    rz_recv,
    rz_send,
    x_send,
    x_recv,
    v_send,
    v_recv,
    copy_sem,
):
    bf, f32 = jnp.bfloat16, jnp.float32
    z, y, c, t = place()
    me = slot_of(z, y, c)
    x_peer = (me, 1 - t)
    y_peer = (slot_of(z, 1 - y, c), t)
    c_peer = (slot_of(z, y, 1 - c), t)
    rows = tokens.shape[0]
    own = pl.ds(pl.multiple_of(t * rows, rows), rows)
    other = pl.ds(pl.multiple_of((1 - t) * rows, rows), rows)
    gathered, core_in, y_in, z_in = (gq, go, gi, gd), (cq, co, ci, cd), (yq, yo, yi, yd), (zq, zo, zi, zd)
    sums = (sum_q, sum_o, sum_i, sum_d)
    Q, O, I, W, V = range(5)

    def dot(a, b):
        return jnp.dot(a, b, preferred_element_type=f32)

    def dot_nt(a, b):
        return lax.dot_general(a, b, (((1,), (1,)), ((), ())), preferred_element_type=f32)

    def dot_tn(a, b):
        return lax.dot_general(a, b, (((0,), (0,)), ((), ())), preferred_element_type=f32)

    def piece(k, zz, yy, cc):
        if k == O:
            return go.at[zz * 2 + yy, :, pl.ds(pl.multiple_of(cc * 512, 512), 512)]
        return gathered[k].at[slot_of(zz, yy, cc)]

    def near(s):
        return lax.rem(z + (1 - 2 * lax.div(z, 2)) * s + DEPTH, DEPTH)

    def ag_piece(k, zz, yy, cc):
        if k == W:
            return gd.at[slot_of(zz, yy, cc), 0:HALF]
        if k == V:
            return gd.at[slot_of(zz, yy, cc), HALF:LANES]
        return piece(k, zz, yy, cc)

    def ag_copy(k, zz, yy, way):
        src = ag_piece(k, zz, yy, c)
        sem = recv.at[k, slot_of(zz, yy, c)]
        if way == "up":
            return remote(src, src, send_z.at[k, 0, yy * DEPTH + zz], sem, (slot_of(z + 1, y, c), t))
        if way == "down":
            return remote(src, src, send_z.at[k, 1, yy * DEPTH + zz], sem, (slot_of(z - 1, y, c), t))
        if way == "y":
            return remote(src, src, send_y.at[k, zz], sem, y_peer)
        return remote(src, src, send_c.at[k, yy * DEPTH + zz], sem, c_peer)

    def ag_wait(k, zz, yy, cc):
        ref = ag_piece(k, zz, yy, cc)
        remote(ref, ref, send_y.at[k, 0], recv.at[k, slot_of(zz, yy, cc)], y_peer).wait_recv()

    def own_sends_z(k):
        @pl.when(z < DEPTH - 1)
        def _():
            ag_copy(k, z, y, "up").start()

        @pl.when(z > 0)
        def _():
            ag_copy(k, z, y, "down").start()

        ag_copy(k, z, y, "core").start()

    def own_sends_y(k):
        ag_copy(k, z, y, "y").start()

    def z_arrival(kinds, dist):
        @pl.when(z >= dist)
        def _():
            for k in kinds:
                ag_wait(k, z - dist, y, c)

                @pl.when(z < DEPTH - 1)
                def _():
                    ag_copy(k, z - dist, y, "up").start()

                ag_copy(k, z - dist, y, "y").start()
                ag_copy(k, z - dist, y, "core").start()

        @pl.when(z + dist < DEPTH)
        def _():
            for k in kinds:
                ag_wait(k, z + dist, y, c)

                @pl.when(z > 0)
                def _():
                    ag_copy(k, z + dist, y, "down").start()

                ag_copy(k, z + dist, y, "y").start()
                ag_copy(k, z + dist, y, "core").start()

    def y_arrival(kinds, dist):
        def one(zz):
            for k in kinds:
                ag_wait(k, zz, 1 - y, c)
                ag_copy(k, zz, 1 - y, "core").start()

        if dist == 0:
            one(z)
            return

        @pl.when(z >= dist)
        def _():
            one(z - dist)

        @pl.when(z + dist < DEPTH)
        def _():
            one(z + dist)

    def v_forward(zz, yy):
        ag_wait(V, zz, yy, c)

        @pl.when((zz <= z) & (z < DEPTH - 1))
        def _():
            ag_copy(V, zz, yy, "up").start()

        @pl.when((zz >= z) & (z > 0))
        def _():
            ag_copy(V, zz, yy, "down").start()

        ag_copy(V, zz, yy, "core").start()

    def v_arrival(dist):
        for yy in (y, 1 - y):

            @pl.when(z >= dist)
            def _():
                v_forward(z - dist, yy)

            @pl.when(z + dist < DEPTH)
            def _():
                v_forward(z + dist, yy)

    def drain(k, zz, yy):
        ag_copy(k, zz, yy, "core").wait_send()
        if k == V:

            @pl.when((yy == y) & (zz == z))
            def _():
                ag_copy(k, zz, yy, "y").wait_send()

            @pl.when((zz <= z) & (z < DEPTH - 1))
            def _():
                ag_copy(k, zz, yy, "up").wait_send()

            @pl.when((zz >= z) & (z > 0))
            def _():
                ag_copy(k, zz, yy, "down").wait_send()

            return

        @pl.when(yy == y)
        def _():
            ag_copy(k, zz, y, "y").wait_send()

            @pl.when((zz <= z) & (z < DEPTH - 1))
            def _():
                ag_copy(k, zz, y, "up").wait_send()

            @pl.when((zz >= z) & (z > 0))
            def _():
                ag_copy(k, zz, y, "down").wait_send()

    def add(dst, first, second):
        count, width = dst.shape
        step = min(count, 256 * LANES // width)

        def body(i, carry):
            at = pl.ds(pl.multiple_of(i * step, 16), step)
            dst[at, :] = (first[at, :].astype(f32) + second[at, :].astype(f32)).astype(dst.dtype)
            return carry

        lax.fori_loop(0, count // step, body, 0)

    def rc_copy(k, zz, yy):
        at = zz * 2 + yy
        return remote(piece(k, zz, yy, 1 - c), core_in[k].at[at], rc_send.at[k, at], rc_recv.at[k, at], c_peer)

    def ry_copy(k, zz):
        return remote(piece(k, zz, 1 - y, c), y_in[k].at[zz], ry_send.at[k, zz], ry_recv.at[k, zz], y_peer)

    def rz_copy(k, zz):
        step = lax.rem(zz - z + DEPTH, DEPTH)
        at = DEPTH - 1 - step
        return remote(
            piece(k, zz, y, c), z_in[k].at[at], rz_send.at[k, step - 1], rz_recv.at[k, at], (slot_of(zz, y, c), t)
        )

    def rc_add(k, zz, yy):
        at = zz * 2 + yy
        remote(core_in[k].at[at], core_in[k].at[at], rc_send.at[k, 0], rc_recv.at[k, at], c_peer).wait_recv()
        mine = piece(k, zz, yy, c)
        add(mine, mine, core_in[k].at[at])

        @pl.when(yy != y)
        def _():
            ry_copy(k, zz).start()

    def ry_add(k, s):
        zz = near(s)
        remote(y_in[k].at[zz], y_in[k].at[zz], ry_send.at[k, 0], ry_recv.at[k, zz], y_peer).wait_recv()
        mine = piece(k, zz, y, c)
        if s == 0:
            add(sums[k], mine, y_in[k].at[zz])
        else:
            add(mine, mine, y_in[k].at[zz])
            rz_copy(k, zz).start()

    def rz_add(k):
        for at in range(DEPTH - 1):
            remote(z_in[k].at[at], z_in[k].at[at], rz_send.at[k, 0], rz_recv.at[k, at], y_peer).wait_recv()
            add(sums[k], sums[k], z_in[k].at[at])

    def x_rows(ref, index):
        return remote(ref.at[own], ref.at[own], x_send.at[index], x_recv.at[index], x_peer)

    def x_rows_wait(ref, index):
        remote(ref.at[other], ref.at[other], x_send.at[index], x_recv.at[index], x_peer).wait_recv()

    def x_part(index):
        return remote(far.at[index], inx.at[index], x_send.at[4 + index], x_recv.at[4 + index], x_peer)

    def by_rows(body, step=64):
        def run(i, carry):
            body(pl.multiple_of(i * step, step), step)
            return carry

        lax.fori_loop(0, rows // step, run, 0)

    def norm(value):
        average = jnp.mean(value, -1, keepdims=True)
        centred = value - average
        inverse = lax.rsqrt(jnp.mean(centred * centred, -1, keepdims=True) + EPS)
        return centred * inverse, inverse

    def norm_grad(grad, unit, inverse, gain):
        scaled = grad * gain
        return inverse * (
            scaled - jnp.mean(scaled, -1, keepdims=True) - unit * jnp.mean(scaled * unit, -1, keepdims=True)
        )

    barrier = pltpu.get_barrier_semaphore()
    z_peers = [(slot_of(lax.rem(z + step, DEPTH), y, c), t) for step in range(1, DEPTH)]
    everyone = [x_peer, y_peer, c_peer] + z_peers
    for device in everyone:
        pl.semaphore_signal(barrier, inc=1, device_id=device, device_id_type=MESH_ID)

    def prepare(held, stack):
        load = pltpu.make_async_copy(view, held, copy_sem.at[0])
        load.start()

        def first_norm(at, step):
            unit, inverse = norm(tokens[pl.ds(at, step), :])
            to = pl.ds(pl.multiple_of(t * rows + at, step), step)
            rows_one[to, :] = (unit * vecs[0:1, :] + vecs[1:2, :]).astype(bf)
            grad_rows[to, :] = cot[pl.ds(at, step), :].astype(bf)

        by_rows(first_norm)
        pl.semaphore_wait(barrier, len(everyone))
        x_rows(rows_one, 0).start()
        load.wait()
        lay_blocks(held, stack)
        n = gq.shape[1]
        gq[me, :, 0:HALF] = stack[0:n, 0:HALF].astype(bf)
        gq[me, :, HALF:LANES] = stack[n : 2 * n, 0:HALF].astype(bf)
        own_sends_y(Q)
        own_sends_z(Q)
        base = 2 * n
        wide = [stack[base + b * 64 : base + b * 64 + 64, 0:HALF] for b in range(8)]
        go[z * 2 + y, :, pl.ds(pl.multiple_of(c * 512, 512), 512)] = jnp.concatenate(wide, 1).astype(bf)
        own_sends_y(O)
        own_sends_z(O)
        base += 512
        gi[me, :, 0:HALF] = stack[base : base + 1024, 0:HALF].astype(bf)
        gi[me, :, HALF:LANES] = stack[base + 1024 : base + 2048, 0:HALF].astype(bf)
        base += 2048
        for r in range(2):
            for b in range(16):
                at = base + (r * 16 + b) * 64
                gd[me, r * 64 : r * 64 + 64, b * HALF : (b + 1) * HALF] = stack[at : at + 64, 0:HALF].astype(bf)

    pl.run_scoped(
        prepare,
        pltpu.VMEM(view.shape, f32),
        pltpu.VMEM((view.shape[2] * BLOCK, LANES), f32),
    )
    x_rows(grad_rows, 1).start()
    z_arrival((Q, O), 1)
    y_arrival((Q, O), 0)
    for k in (I, W, V):
        own_sends_z(k)
    z_arrival((Q, O), 2)
    y_arrival((Q, O), 1)
    z_arrival((Q, O), 3)
    for k in (I, W, V):
        own_sends_y(k)

    def core_waits(kinds, zz):
        for k in kinds:
            for yy in (y, 1 - y):
                ag_wait(k, zz, yy, 1 - c)

    x_rows_wait(rows_one, 0)

    ends = []
    for p in range(ARTICLES):
        length = 0
        for a in range(ARTICLES):
            length = length + jnp.where(order[0, p] == a, lengths[0, a], 0)
        ends.append(length + ends[-1] if p else length)

    def allowed(first, count):
        ids = lax.broadcasted_iota(jnp.int32, (rows, 1), 0) + first
        start = jnp.zeros((rows, 1), jnp.int32)
        for end in ends:
            start = jnp.where(ids >= end, end, start)
        start = jnp.where(ids >= ends[-1], ids, start)
        keys = lax.broadcasted_iota(jnp.int32, (rows, count), 1)
        return (keys <= ids) & (keys >= start)

    scale = HD ** (-0.5)
    strip = 1024

    def assemble(h):
        for yy in range(2):
            even, odd = gq.at[slot_of(h, yy, 0)], gq.at[slot_of(h, yy, 1)]
            at = yy * 192
            wqkv[h, 0:768, at : at + 64] = even[:, 0:64]
            wqkv[h, 768:1024, at : at + 64] = even[0:256, 64:128]
            wqkv[h, 0:512, at + 64 : at + 128] = even[256:768, 64:128]
            wqkv[h, 512:1024, at + 64 : at + 128] = odd[0:512, 0:64]
            wqkv[h, 0:256, at + 128 : at + 192] = odd[512:768, 0:64]
            wqkv[h, 256:1024, at + 128 : at + 192] = odd[:, 64:128]

    def disassemble(h, value):
        for yy in range(2):
            even, odd = gq.at[slot_of(h, yy, 0)], gq.at[slot_of(h, yy, 1)]
            at = yy * 192
            even[:, 0:64] = value[0:768, at : at + 64]
            even[0:256, 64:128] = value[768:1024, at : at + 64]
            even[256:768, 64:128] = value[0:512, at + 64 : at + 128]
            odd[0:512, 0:64] = value[512:1024, at + 64 : at + 128]
            odd[512:768, 0:64] = value[0:256, at + 128 : at + 192]
            odd[:, 64:128] = value[256:1024, at + 128 : at + 192]

    def lanes(start, size, unit):
        return pl.ds(pl.multiple_of(start, unit), size)

    qv = vecs[pl.ds(6 + t, 1), :]
    for h in range(DEPTH):
        none = jnp.zeros((1, HD), f32)
        qkv_bias[h] = jnp.concatenate([qv[:, h * 256 : h * 256 + 128], none, qv[:, h * 256 + 128 : h * 256 + 256]], 1)

    def head(h):
        core_waits((Q,), h)
        assemble(h)
        qkv[h] = (dot(rows_one[...], wqkv[h]) + qkv_bias[h]).astype(bf)
        for block in range(2):
            at, seen = slice(block * rows, (block + 1) * rows), (block + 1) * rows
            scores = dot_nt(qkv[h, at, 0:128], qkv[h, 0:seen, 128:256]) * scale
            scores = jnp.where(allowed(block * rows, seen), scores, NEG)
            expo = jnp.exp(scores - jnp.max(scores, -1, keepdims=True))
            low = (expo / jnp.sum(expo, -1, keepdims=True)).astype(bf)
            probs[h, at, 0:seen] = low
            ctx[at, lanes(h * HD, HD, HD)] = dot(low, qkv[h, 0:seen, 256:384]).astype(bf)

    head(near(0))
    y_arrival((Q, O), 2)
    head(near(1))
    y_arrival((Q, O), 3)
    head(near(2))
    z_arrival((I, W), 1)
    head(near(3))
    y_arrival((I, W), 0)
    v_forward(z, 1 - y)
    for zz in range(DEPTH):
        core_waits((O,), zz)

    def w_out(at, count):
        return go[at : at + count].reshape(count * 64, 1024)

    far[0] = dot(ctx[other, :], w_out(0, 8)).astype(bf)
    x_part(0).start()
    mixed[...] = tokens[...] + dot(ctx[own, :], w_out(0, 8)) + vecs[4:5, :]
    z_arrival((I, W), 2)
    v_arrival(1)
    y_arrival((I, W), 1)
    x_part(0).wait_recv()

    def second_norm(at, step):
        value = mixed[pl.ds(at, step), :] + inx[0, pl.ds(at, step), :].astype(f32)
        mixed[pl.ds(at, step), :] = value
        unit, inverse = norm(value)
        to = pl.ds(pl.multiple_of(t * rows + at, step), step)
        rows_two[to, :] = (unit * vecs[2:3, :] + vecs[3:4, :]).astype(bf)

    by_rows(second_norm)
    x_rows(rows_two, 2).start()
    z_arrival((I, W), 3)
    v_arrival(2)
    macc[...] = jnp.zeros_like(macc)
    nacc[...] = jnp.zeros_like(nacc)
    vout[...] = jnp.zeros_like(vout)
    x_rows_wait(grad_rows, 1)

    def ffn(half, zz):
        first = 4 * zz
        at = pl.ds(pl.multiple_of(lax.rem(t + half, 2) * rows, rows), rows)
        units = lanes(zz * 512, 512, 512)
        bias_row = vecs[pl.ds(8 + 2 * t + lax.div(zz, 2), 1), lanes(lax.rem(zz, 2) * 512, 512, 512)]

        def w_in(start, count):
            return jnp.concatenate([gi[first + j, start : start + count, :] for j in range(4)], 1)

        def w_down(start, count):
            return gd[pl.ds(first, 4), :, start : start + count].reshape(512, count)

        inner = dot(rows_two[at, :], w_in(0, D)) + bias_row
        square = inner * inner
        bent = jnp.tanh(GELU_A * inner * (1.0 + GELU_B * square))
        act[at, units] = (0.5 * inner * (1.0 + bent)).astype(bf)
        slope = 0.5 * (1.0 + bent) + 0.5 * inner * (1.0 - bent * bent) * (GELU_A * (1.0 + 3.0 * GELU_B * square))
        gin[at, units] = (dot_nt(grad_rows[at, :], w_down(0, D)) * slope).astype(bf)
        for nb in range(4):
            out = slice(nb * 256, nb * 256 + 256)
            nacc[at, out] += dot_nt(gin[at, units], w_in(nb * 256, 256))
            macc[at, out] += dot(act[at, units], w_down(nb * 256, 256))

    def own_rows(i, carry):
        @pl.when(i == 2)
        def _():
            y_arrival((I, W), 2)

        @pl.when(i == 3)
        def _():
            v_arrival(3)
            y_arrival((I, W), 3)

        core_waits((I, W, V), near(i))
        ffn(0, near(i))
        return carry

    lax.fori_loop(0, DEPTH, own_rows, 0)
    x_rows_wait(rows_two, 2)
    rows_t[...] = rows_two[...].T

    def ffn_grads(zz):
        first = 4 * zz
        units = lanes(zz * 512, 512, 512)
        for k in (I, W, V):
            for yy in range(2):
                drain(k, zz, yy)
        bias_sum[zz] = jnp.sum(gin[:, units].astype(f32), 0, keepdims=True)
        for nb in range(4):
            out = slice(nb * 256, nb * 256 + 256)
            part = dot(rows_t[out, :], gin[:, units]).astype(bf)
            for j in range(4):
                gi[first + j, out, :] = part[:, j * LANES : (j + 1) * LANES]
        for yy in (1 - y, y):
            rc_copy(I, zz, yy).start()
        act_t = act[:, units].T
        for nb in range(4):
            out = slice(nb * 256, nb * 256 + 256)
            part = dot(act_t, grad_rows[:, out]).astype(bf)
            gd[pl.ds(first, 4), :, out] = part.reshape(4, LANES, 256)
        for yy in (1 - y, y):
            rc_copy(W, zz, yy).start()

    def reduce_core(zz):
        for yy in (1 - y, y):
            for k in (I, W):
                rc_add(k, zz, yy)

    def other_rows(i, carry):
        @pl.when(i == DEPTH)
        def _():
            far[1] = nacc[other, :].astype(bf)
            x_part(1).start()
            far[2] = macc[other, :].astype(bf)
            x_part(2).start()

        @pl.when(i > 0)
        def _():
            ffn_grads(near(DEPTH - i))

        @pl.when(i > 1)
        def _():
            reduce_core(near(DEPTH + 1 - i))

        @pl.when(i < DEPTH)
        def _():
            ffn(1, near(DEPTH - 1 - i))

        return carry

    lax.fori_loop(0, DEPTH + 1, other_rows, 0)
    reduce_core(near(0))
    for zz in range(DEPTH):
        for side in range(2):
            row, start = 8 + 2 * side + zz // 2, zz % 2 * 512
            vout[0, row : row + 1, start : start + 512] = jnp.where(t == side, bias_sum[zz], 0.0)
    rows_t[...] = rows_one[...].T
    x_part(1).wait_recv()

    def row_sum(row, value):
        vout[0, row : row + 1, :] += jnp.sum(value, 0, keepdims=True)

    def second_back(at, step):
        here = pl.ds(at, step)
        in_group = pl.ds(pl.multiple_of(t * rows + at, step), step)
        grad = nacc[in_group, :] + inx[1, here, :].astype(f32)
        unit, inverse = norm(mixed[here, :])
        back = cot[here, :] + norm_grad(grad, unit, inverse, vecs[2:3, :])
        input_grad[here, :] = back
        grad_attn[in_group, :] = back.astype(bf)
        row_sum(2, grad * unit)
        row_sum(3, grad)
        row_sum(4, back)
        row_sum(5, cot[here, :])

    by_rows(second_back)
    x_rows(grad_attn, 3).start()
    for s in (3, 2):
        for k in (I, W):
            ry_add(k, s)
    x_part(2).wait_recv()

    def mixed_out(at, step):
        here = pl.ds(at, step)
        in_group = pl.ds(pl.multiple_of(t * rows + at, step), step)
        mixed[here, :] = mixed[here, :] + macc[in_group, :] + inx[2, here, :].astype(f32) + vecs[5:6, :]

    by_rows(mixed_out)
    for zz in range(DEPTH):
        for yy in range(2):
            drain(O, zz, yy)
            drain(Q, zz, yy)
    x_rows_wait(grad_attn, 3)
    gctx[...] = dot_nt(grad_attn[...], w_out(0, 8)).astype(bf)
    ctx_t = ctx[...].T
    for nb in range(4):
        at = slice(nb * 256, nb * 256 + 256)
        go[:, :, at] = dot(ctx_t, grad_attn[:, at]).astype(bf).reshape(8, 64, 256)
    for zz in range(DEPTH):
        for yy in range(2):
            rc_copy(O, zz, yy).start()

    def head_back(h):
        q0, q1 = qkv[h, 0:rows, 0:128], qkv[h, rows : 2 * rows, 0:128]
        grads = []
        for block in range(2):
            at, seen = slice(block * rows, (block + 1) * rows), (block + 1) * rows
            low = probs[h, at, 0:seen]
            given = gctx[at, h * 128 : h * 128 + 128]
            prob = low.astype(f32)
            grad_probs = dot_nt(given, qkv[h, 0:seen, 256:384])
            delta = jnp.sum(prob * grad_probs, -1, keepdims=True)
            grad_scores = (prob * (grad_probs - delta)).astype(bf)
            grad_q = dot(grad_scores, qkv[h, 0:seen, 128:256]) * scale
            grad_k = dot_tn(grad_scores, q1 if block else q0) * scale
            grad_v = dot_tn(low, given)
            grads.append((grad_q, grad_k, grad_v))
        (gq0, gk0, gv0), (gq1, gk1, gv1) = grads
        top = jnp.concatenate([gq0, gk0 + gk1[0:rows], gv0 + gv1[0:rows]], 1).astype(bf)
        low_half = jnp.concatenate([gq1, gk1[rows:], gv1[rows:]], 1).astype(bf)
        qkv[h, 0:rows, :] = top
        qkv[h, rows : 2 * rows, :] = low_half
        total = jnp.sum(top.astype(f32), 0, keepdims=True) + jnp.sum(low_half.astype(f32), 0, keepdims=True)
        for side in range(2):
            vout[0, 6 + side : 7 + side, h * 256 : h * 256 + 128] = jnp.where(t == side, total[:, 0:128], 0.0)
            vout[0, 6 + side : 7 + side, h * 256 + 128 : h * 256 + 256] = jnp.where(t == side, total[:, 256:384], 0.0)
        part = dot(rows_t[...], qkv[h]).astype(bf)
        disassemble(h, part)
        for yy in (1 - y, y):
            rc_copy(Q, h, yy).start()
        product = dot_nt(qkv[h], wqkv[h])
        if h == 0:
            nacc[...] = product
        else:
            nacc[...] += product

    for h in range(DEPTH):
        head_back(h)
        if h == 0:
            for yy in (1 - y, y):
                for s in range(DEPTH):
                    rc_add(O, near(s), yy)
        else:
            for yy in (1 - y, y):
                rc_add(Q, h - 1, yy)
    far[3] = nacc[other, :].astype(bf)
    x_part(3).start()
    for yy in (1 - y, y):
        rc_add(Q, DEPTH - 1, yy)
    for s in (1, 0):
        for k in (I, W):
            ry_add(k, s)
    x_part(3).wait_recv()

    def first_back(at, step):
        here = pl.ds(at, step)
        in_group = pl.ds(pl.multiple_of(t * rows + at, step), step)
        grad = nacc[in_group, :] + inx[3, here, :].astype(f32)
        unit, inverse = norm(tokens[here, :])
        input_grad[here, :] = input_grad[here, :] + norm_grad(grad, unit, inverse, vecs[0:1, :])
        row_sum(0, grad * unit)
        row_sum(1, grad)

    by_rows(first_back)

    stages = (x_peer, c_peer, y_peer)

    def v_copy(stage):
        return remote(vout.at[stage], vin.at[stage], v_send.at[stage], v_recv.at[stage], stages[stage])

    def vz_copy(step):
        peer = (slot_of(lax.rem(z + step, DEPTH), y, c), t)
        return remote(vout.at[3], vin.at[3 + z], v_send.at[2 + step], v_recv.at[3 + z], peer)

    v_copy(0).start()
    for k in (O, Q):
        for s in range(1, DEPTH):
            ry_add(k, s)
        if k == O:
            v_copy(0).wait_recv()
            vout[1] = vout[0] + vin[0]
            v_copy(1).start()
            ry_add(k, 0)
    v_copy(1).wait_recv()
    vout[2] = vout[1] + vin[1]
    v_copy(2).start()
    ry_add(Q, 0)
    for k in (I, W, O):
        rz_add(k)
    v_copy(2).wait_recv()
    vout[3] = vout[2] + vin[2]
    for step in range(1, DEPTH):
        vz_copy(step).start()
    vin[3 + z] = vout[3]
    rz_add(Q)
    for step in range(1, DEPTH):
        zz = lax.rem(z + step, DEPTH)
        remote(vin.at[3 + zz], vin.at[3 + zz], v_send.at[0], v_recv.at[3 + zz], y_peer).wait_recv()
    count = vec_grads.shape[0]
    total = ((vin[3] + vin[4]) + vin[5]) + vin[6]
    vec_grads[...] = total[0:count]

    for stage in range(3):
        v_copy(stage).wait_send()
    for step in range(1, DEPTH):
        vz_copy(step).wait_send()
    for index, ref in enumerate((rows_one, grad_rows, rows_two, grad_attn)):
        x_rows(ref, index).wait_send()
    for index in range(4):
        x_part(index).wait_send()
    for k in range(4):
        for zz in range(DEPTH):
            for yy in range(2):
                rc_copy(k, zz, yy).wait_send()
            ry_copy(k, zz).wait_send()
        for s in range(1, DEPTH):
            rz_copy(k, near(s)).wait_send()


def run_layer(tokens, cotangent, lengths, order, weights, vec_params):
    bf, f32 = jnp.bfloat16, jnp.float32
    rows = tokens.shape[0]
    group = 2 * rows
    owners = 16
    shapes = piece_shapes()
    view = jnp.transpose(weights, (1, 2, 0))
    vmem = pl.BlockSpec(memory_space=pltpu.VMEM)
    smem = pl.BlockSpec(memory_space=pltpu.SMEM)

    def many(count):
        return [pltpu.VMEM((count,) + s, bf) for s in shapes]

    full = pltpu.VMEM((group, D), bf)
    dma = pltpu.SemaphoreType.DMA
    return pl.pallas_call(
        layer_kernel,
        out_shape=[jax.ShapeDtypeStruct((rows, D), f32)] * 2
        + [jax.ShapeDtypeStruct(s, f32) for s in shapes]
        + [jax.ShapeDtypeStruct(vec_params.shape, f32)],
        in_specs=[smem, smem, pl.BlockSpec(memory_space=pl.ANY)] + [vmem] * 3,
        out_specs=[vmem] * 7,
        scratch_shapes=[
            pltpu.VMEM((owners,) + shapes[0], bf),
            pltpu.VMEM((owners // 2, BLOCK, D), bf),
            pltpu.VMEM((owners,) + shapes[2], bf),
            pltpu.VMEM((owners,) + shapes[3], bf),
            pltpu.VMEM((DEPTH, D, 3 * HD), bf),
        ]
        + many(2 * DEPTH)
        + many(DEPTH)
        + many(DEPTH - 1)
        + [
            full,
            full,
            pltpu.VMEM((D, group), bf),
            full,
            full,
            pltpu.VMEM((DEPTH, group, group), bf),
            pltpu.VMEM((DEPTH, group, 3 * HD), bf),
            pltpu.VMEM((group, DEPTH * HD), bf),
            pltpu.VMEM((group, DEPTH * HD), bf),
            pltpu.VMEM((4, rows, D), bf),
            pltpu.VMEM((4, rows, D), bf),
            pltpu.VMEM((group, D), f32),
            pltpu.VMEM((group, D), f32),
            pltpu.VMEM((group, 2 * D), bf),
            pltpu.VMEM((group, 2 * D), bf),
            pltpu.VMEM((DEPTH, 1, 512), f32),
            pltpu.VMEM((DEPTH, 1, 3 * HD), f32),
            pltpu.VMEM((7, 16, D), f32),
            pltpu.VMEM((4, 16, D), f32),
            dma((5, owners)),
            dma((5, DEPTH)),
            dma((5, 2 * DEPTH)),
            dma((5, 2, 2 * DEPTH)),
            dma((4, 2 * DEPTH)),
            dma((4, 2 * DEPTH)),
            dma((4, DEPTH)),
            dma((4, DEPTH)),
            dma((4, DEPTH - 1)),
            dma((4, DEPTH - 1)),
            dma((8,)),
            dma((8,)),
            dma((6,)),
            dma((7,)),
            dma((1,)),
        ],
        compiler_params=pltpu.CompilerParams(
            collective_id=0, has_side_effects=True, vmem_limit_bytes=VMEM_LIMIT
        ),
        name="layer",
    )(lengths, order, view, tokens, cotangent, vec_params)


def per_device(
    grp_count,
    tp_count,
    tokens,
    cotangent,
    lengths,
    order,
    weights,
    momentum,
    stat_left,
    stat_right,
    root_left,
    root_right,
    vec_params,
    vec_momentum,
    vec_second,
):
    fits = grp_count == 4 * DEPTH and tp_count == 2 and tokens.shape[0] == 256
    if not fits or lengths.shape[1] != ARTICLES:
        return per_device_general(
            tokens,
            cotangent,
            lengths,
            order,
            weights,
            momentum,
            stat_left,
            stat_right,
            root_left,
            root_right,
            vec_params,
            vec_momentum,
            vec_second,
        )
    token_total = tokens.shape[0] * tp_count * grp_count
    mixed, input_grad, *sums, vec_grads = run_layer(tokens, cotangent, lengths, order, weights, vec_params)
    blocks, vecs, results = update_blocks(
        sums,
        (weights, momentum, stat_left, stat_right, root_left, root_right),
        vec_grads,
        (vec_params, vec_momentum, vec_second),
        (mixed, input_grad),
        token_total,
    )
    return (*results, *blocks, *vecs)


def solution(mesh):
    placed = (
        P(("grp", "tp"), None),
        P(("grp", "tp"), None),
        P("grp", None),
        P("grp", None),
        P(("tp", "grp"), None, None),
        P(("tp", "grp"), None, None),
        P(("tp", "grp"), None, None),
        P(("tp", "grp"), None, None),
        P(("tp", "grp"), None, None),
        P(("tp", "grp"), None, None),
        P(),
        P(),
        P(),
    )
    return jax.shard_map(
        functools.partial(per_device, mesh.shape["grp"], mesh.shape["tp"]),
        mesh=mesh,
        in_specs=placed,
        out_specs=(
            P(("grp", "tp"), None),
            P(("grp", "tp"), None),
            P(("tp", "grp"), None, None),
            P(("tp", "grp"), None, None),
            P(("tp", "grp"), None, None),
            P(("tp", "grp"), None, None),
            P(("tp", "grp"), None, None),
            P(),
            P(),
            P(),
            P(),
        ),
        check_vma=False,
    )
```

```python
import functools

import jax
import jax.numpy as jnp
from jax import lax
from jax.experimental import pallas as pl
from jax.experimental.pallas import tpu as pltpu
from jax.sharding import PartitionSpec as P

D = 1024
HEADS = 8
HD = 128
FF = 4096
BLOCK = 64


EPS = 1e-05
NEG = -1e30
DECAY = 0.9
BETA = 0.9
RATE = 0.05
VEC_DECAY = 0.9
VEC_RATE = 0.2
VEC_EPS = 1e-08


def norm_rows(value, gain, shift):
    average = jnp.mean(value, -1, keepdims=True)
    centred = value - average
    inverse = lax.rsqrt(jnp.mean(centred * centred, -1, keepdims=True) + EPS)
    normed = centred * inverse
    return (normed * gain + shift, normed, inverse)


def norm_back(grad_out, normed, inverse, gain):
    scaled = grad_out * gain
    return inverse * (
        scaled
        - jnp.mean(scaled, -1, keepdims=True)
        - normed * jnp.mean(scaled * normed, -1, keepdims=True)
    )


def segment_ids(lengths_row, order_row, group_rows):
    article_count = lengths_row.shape[0]
    slots = jnp.arange(article_count, dtype=jnp.int32)
    picks = (order_row[:, None] == slots[None, :]).astype(jnp.int32)
    packed = jnp.sum(picks * lengths_row[None, :], 1)
    ends = jnp.cumsum(packed)
    spots = jnp.arange(group_rows, dtype=jnp.int32)
    return jnp.sum((spots[:, None] >= ends[None, :]).astype(jnp.int32), 1)


def allowed_mask(row_ids, row_segs, segments, key_ids, article_count):
    causal = key_ids[None, :] <= row_ids[:, None]
    same = segments[None, :] == row_segs[:, None]
    alone = (row_segs[:, None] < article_count) | (key_ids[None, :] == row_ids[:, None])
    return causal & same & alone


def from_columns(tiles, row_total, col_total):
    return (
        tiles.reshape(col_total // BLOCK, row_total // BLOCK, BLOCK, BLOCK)
        .transpose(1, 2, 0, 3)
        .reshape(row_total, col_total)
    )


def from_rows(tiles, row_total, col_total):
    return (
        tiles.reshape(row_total // BLOCK, col_total // BLOCK, BLOCK, BLOCK)
        .transpose(0, 2, 1, 3)
        .reshape(row_total, col_total)
    )


def to_columns(matrix):
    row_total, col_total = matrix.shape
    return (
        matrix.reshape(row_total // BLOCK, BLOCK, col_total // BLOCK, BLOCK)
        .transpose(2, 0, 1, 3)
        .reshape(-1, BLOCK, BLOCK)
    )


def to_rows(matrix):
    row_total, col_total = matrix.shape
    return (
        matrix.reshape(row_total // BLOCK, BLOCK, col_total // BLOCK, BLOCK)
        .transpose(0, 2, 1, 3)
        .reshape(-1, BLOCK, BLOCK)
    )


def per_device_general(
    tokens,
    cotangent,
    lengths,
    order,
    weights,
    momentum,
    stat_left,
    stat_right,
    root_left,
    root_right,
    vec_params,
    vec_momentum,
    vec_second,
):
    groups = lax.axis_size("grp")
    tp_size = lax.axis_size("tp")
    tp_rank = lax.axis_index("tp")
    tok_rows = tokens.shape[0]
    group_rows = tok_rows * tp_size
    article_count = lengths.shape[1]
    owners = groups * tp_size
    block_area = BLOCK * BLOCK * owners
    qkv_count = 3 * D * D // block_area
    out_count = D * D // block_area
    in_count = D * FF // block_area
    owned_blocks = weights.shape[0]
    heads_here = HEADS // tp_size
    qkv_cols = 3 * D // tp_size
    feat_here = D // tp_size
    ff_here = FF // tp_size
    qv_width = 2 * D // tp_size
    token_total = group_rows * groups
    gathered = lax.all_gather(weights.astype(jnp.bfloat16), "grp", axis=0, tiled=True)
    per_owner = gathered.reshape(groups, owned_blocks, BLOCK, BLOCK)
    marks = [0, qkv_count, qkv_count + out_count, qkv_count + out_count + in_count, owned_blocks]
    pieces = [
        per_owner[:, marks[index] : marks[index + 1]].reshape(-1, BLOCK, BLOCK)
        for index in range(4)
    ]
    w_qkv = from_columns(pieces[0], D, qkv_cols)
    w_out = from_rows(pieces[1], feat_here, D)
    w_in = from_columns(pieces[2], D, ff_here)
    w_down = from_rows(pieces[3], ff_here, D)
    w_qkv_heads = w_qkv.reshape(D, heads_here, 3, HD)
    w_out_heads = w_out.reshape(heads_here, HD, D)
    segments = segment_ids(lengths[0], order[0], group_rows)
    gain_one = vec_params[0]
    shift_one = vec_params[1]
    gain_two = vec_params[2]
    shift_two = vec_params[3]
    bias_out = vec_params[4]
    bias_down = vec_params[5]
    qv_here = lax.dynamic_slice_in_dim(
        vec_params[6:8].reshape(2 * D), tp_rank * qv_width, qv_width
    ).reshape(heads_here, 2, HD)
    bias_heads = jnp.stack(
        [qv_here[:, 0], jnp.zeros((heads_here, HD), jnp.float32), qv_here[:, 1]], 0
    )[:, :, None, :]
    bias_in = lax.dynamic_slice_in_dim(vec_params[8:].reshape(FF), tp_rank * ff_here, ff_here)
    normed_one, unit_one, inverse_one = norm_rows(tokens, gain_one, shift_one)
    rows_one = lax.all_gather(normed_one.astype(jnp.bfloat16), "tp", axis=0, tiled=True)
    projected = (
        jnp.einsum("rx,xhcd->chrd", rows_one, w_qkv_heads, preferred_element_type=jnp.float32)
        + bias_heads
    ).astype(jnp.bfloat16)
    queries = projected[0]
    keys_all = projected[1]
    values_all = projected[2]
    span = min(512, group_rows)
    starts = jnp.arange(group_rows // span, dtype=jnp.int32) * span
    key_ids = jnp.arange(group_rows, dtype=jnp.int32)
    score_scale = HD ** (-0.5)

    def masked_scores(first_row):
        row_ids = first_row + jnp.arange(span, dtype=jnp.int32)
        row_segs = lax.dynamic_slice_in_dim(segments, first_row, span, 0)
        allowed = allowed_mask(row_ids, row_segs, segments, key_ids, article_count)
        query_rows = lax.dynamic_slice_in_dim(queries, first_row, span, 1)
        scores = (
            jnp.einsum("hqd,hkd->hqk", query_rows, keys_all, preferred_element_type=jnp.float32)
            * score_scale
        )
        return (jnp.where(allowed[None], scores, NEG), query_rows)

    def attend(context_buf, first_row):
        scores, query_rows = masked_scores(first_row)
        row_max = jnp.max(scores, -1, keepdims=True)
        expo = jnp.exp(scores - row_max)
        expsum = jnp.sum(expo, -1, keepdims=True)
        probs_low = (expo / expsum).astype(jnp.bfloat16)
        context = jnp.einsum(
            "hqk,hkd->hqd", probs_low, values_all, preferred_element_type=jnp.float32
        ).astype(jnp.bfloat16)
        context_buf = lax.dynamic_update_slice_in_dim(context_buf, context, first_row, 1)
        return (context_buf, (row_max + jnp.log(expsum))[:, :, 0])

    context_low, log_norm = lax.scan(
        attend, jnp.zeros((heads_here, group_rows, HD), jnp.bfloat16), starts
    )
    attn_sum = lax.psum_scatter(
        jnp.einsum(
            "hrd,hde->re", context_low, w_out_heads, preferred_element_type=jnp.float32
        ).astype(jnp.bfloat16),
        "tp",
        scatter_dimension=0,
        tiled=True,
    ).astype(jnp.float32)
    hidden = tokens + attn_sum + bias_out
    normed_two, unit_two, inverse_two = norm_rows(hidden, gain_two, shift_two)
    rows_two = lax.all_gather(normed_two.astype(jnp.bfloat16), "tp", axis=0, tiled=True)
    inner = jnp.dot(rows_two, w_in, preferred_element_type=jnp.float32) + bias_in
    activ, gelu_pull = jax.vjp(jax.nn.gelu, inner)
    activ_low = activ.astype(jnp.bfloat16)
    mixed = (
        hidden
        + lax.psum_scatter(
            jnp.dot(activ_low, w_down, preferred_element_type=jnp.float32).astype(jnp.bfloat16),
            "tp",
            scatter_dimension=0,
            tiled=True,
        ).astype(jnp.float32)
        + bias_down
    )
    grad_low = cotangent.astype(jnp.bfloat16)
    grad_rows = lax.all_gather(grad_low, "tp", axis=0, tiled=True)
    g_down = jnp.einsum("rf,rd->fd", activ_low, grad_rows, preferred_element_type=jnp.float32)
    grad_activ = jnp.einsum("rd,fd->rf", grad_rows, w_down, preferred_element_type=jnp.float32)
    grad_inner = gelu_pull(grad_activ)[0].astype(jnp.bfloat16)
    g_in = jnp.einsum("rd,rf->df", rows_two, grad_inner, preferred_element_type=jnp.float32)
    g_bias_in = jnp.sum(grad_inner.astype(jnp.float32), 0)
    ffn_blocks = jnp.concatenate(
        [
            to_columns(g_in).reshape(groups, in_count, BLOCK, BLOCK),
            to_rows(g_down).reshape(groups, in_count, BLOCK, BLOCK),
        ],
        1,
    )
    grad_normed_two = lax.psum_scatter(
        jnp.einsum("rf,df->rd", grad_inner, w_in, preferred_element_type=jnp.float32).astype(
            jnp.bfloat16
        ),
        "tp",
        scatter_dimension=0,
        tiled=True,
    ).astype(jnp.float32)
    grad_hidden = cotangent + norm_back(grad_normed_two, unit_two, inverse_two, gain_two)
    grad_attn_low = grad_hidden.astype(jnp.bfloat16)
    grad_attn_rows = lax.all_gather(grad_attn_low, "tp", axis=0, tiled=True)
    g_out = jnp.einsum(
        "hrd,re->hde", context_low, grad_attn_rows, preferred_element_type=jnp.float32
    ).reshape(feat_here, D)
    grad_context = jnp.einsum(
        "re,hde->hrd", grad_attn_rows, w_out_heads, preferred_element_type=jnp.float32
    ).astype(jnp.bfloat16)
    zero_heads = jnp.zeros((heads_here, group_rows, HD), jnp.float32)

    def attend_back(carry, inputs):
        grad_queries, grad_keys, grad_values = carry
        first_row, log_block = inputs
        scores, query_rows = masked_scores(first_row)
        probs = jnp.exp(scores - log_block[:, :, None])
        grad_ctx_rows = lax.dynamic_slice_in_dim(grad_context, first_row, span, 1)
        grad_probs = jnp.einsum(
            "hqd,hkd->hqk", grad_ctx_rows, values_all, preferred_element_type=jnp.float32
        )
        delta = jnp.sum(probs * grad_probs, -1, keepdims=True)
        grad_scores = (probs * (grad_probs - delta)).astype(jnp.bfloat16)
        query_part = (
            jnp.einsum("hqk,hkd->hqd", grad_scores, keys_all, preferred_element_type=jnp.float32)
            * score_scale
        )
        grad_queries = lax.dynamic_update_slice_in_dim(grad_queries, query_part, first_row, 1)
        grad_keys = (
            grad_keys
            + jnp.einsum(
                "hqk,hqd->hkd", grad_scores, query_rows, preferred_element_type=jnp.float32
            )
            * score_scale
        )
        grad_values = grad_values + jnp.einsum(
            "hqk,hqd->hkd",
            probs.astype(jnp.bfloat16),
            grad_ctx_rows,
            preferred_element_type=jnp.float32,
        )
        return ((grad_queries, grad_keys, grad_values), None)

    (grad_queries, grad_keys, grad_values), unused = lax.scan(
        attend_back, (zero_heads, zero_heads, zero_heads), (starts, log_norm)
    )
    grad_proj = jnp.stack([grad_queries, grad_keys, grad_values], 0).astype(jnp.bfloat16)
    proj_sums = jnp.sum(grad_proj.astype(jnp.float32), 2)
    g_bias_qv = jnp.stack([proj_sums[0], proj_sums[2]], 1).reshape(qv_width)
    g_qkv = jnp.einsum(
        "rx,chrd->xhcd", rows_one, grad_proj, preferred_element_type=jnp.float32
    ).reshape(D, qkv_cols)
    grad_normed_one = lax.psum_scatter(
        jnp.einsum(
            "chrd,xhcd->rx", grad_proj, w_qkv_heads, preferred_element_type=jnp.float32
        ).astype(jnp.bfloat16),
        "tp",
        scatter_dimension=0,
        tiled=True,
    ).astype(jnp.float32)
    input_grad = grad_hidden + norm_back(grad_normed_one, unit_one, inverse_one, gain_one)
    local_rows = jnp.stack(
        [
            jnp.sum(grad_normed_one * unit_one, 0),
            jnp.sum(grad_normed_one, 0),
            jnp.sum(grad_normed_two * unit_two, 0),
            jnp.sum(grad_normed_two, 0),
            jnp.sum(grad_hidden, 0),
            jnp.sum(cotangent, 0),
        ]
    )
    qv_rows = lax.dynamic_update_slice(
        jnp.zeros((2 * D,), jnp.float32), g_bias_qv, (tp_rank * qv_width,)
    ).reshape(2, D)
    in_rows = lax.dynamic_update_slice(
        jnp.zeros((FF,), jnp.float32), g_bias_in, (tp_rank * ff_here,)
    ).reshape(FF // D, D)
    vec_grads = lax.psum(jnp.concatenate([local_rows, qv_rows, in_rows], 0), ("grp", "tp"))
    attn_blocks = jnp.concatenate(
        [
            to_columns(g_qkv).reshape(groups, qkv_count, BLOCK, BLOCK),
            to_rows(g_out).reshape(groups, out_count, BLOCK, BLOCK),
        ],
        1,
    )
    every_block = jnp.concatenate([attn_blocks, ffn_blocks], 1).reshape(-1, BLOCK, BLOCK)
    weight_grads = lax.psum_scatter(
        every_block.astype(jnp.bfloat16), "grp", scatter_dimension=0, tiled=True
    ).astype(jnp.float32)
    scaled = weight_grads * token_total ** (-0.5)
    stat_left_new = DECAY * stat_left + (1.0 - DECAY) * jnp.einsum(
        "nij,nkj->nik", scaled, scaled, precision=lax.Precision.HIGHEST
    )
    stat_right_new = DECAY * stat_right + (1.0 - DECAY) * jnp.einsum(
        "nji,njk->nik", scaled, scaled, precision=lax.Precision.HIGHEST
    )
    shaped = jnp.einsum("nij,njk->nik", root_left, scaled, precision=lax.Precision.HIGHEST)
    shaped = jnp.einsum("nij,njk->nik", shaped, root_right, precision=lax.Precision.HIGHEST)
    momentum_new = BETA * momentum + shaped
    weights_new = weights - RATE * momentum_new
    vec_scaled = vec_grads * token_total ** (-0.5)
    vec_second_new = VEC_DECAY * vec_second + (1.0 - VEC_DECAY) * vec_scaled * vec_scaled
    vec_momentum_new = BETA * vec_momentum + vec_scaled * lax.rsqrt(vec_second_new + VEC_EPS)
    vec_new = vec_params - VEC_RATE * vec_momentum_new
    return (
        mixed,
        input_grad,
        weight_grads,
        stat_left_new,
        stat_right_new,
        momentum_new,
        weights_new,
        vec_grads,
        vec_second_new,
        vec_momentum_new,
        vec_new,
    )


MESH_ID = pl.DeviceIdType.MESH
LANES = 128
HALF = 64
VMEM_LIMIT = 62 * 2**20
ARTICLES = 4
GELU_A = (2.0 / 3.141592653589793) ** 0.5
GELU_B = 0.044715


def remote(src, dst, send_sem, recv_sem, device):
    return pltpu.make_async_remote_copy(
        src_ref=src,
        dst_ref=dst,
        send_sem=send_sem,
        recv_sem=recv_sem,
        device_id=device,
        device_id_type=MESH_ID,
    )


def place():
    grp = lax.axis_index("grp")
    return lax.div(grp, 4), lax.rem(lax.div(grp, 2), 2), lax.rem(grp, 2), lax.axis_index("tp")


def slot_of(z, y, c):
    return z * 4 + y * 2 + c


def lay_blocks(view_ref, stack):
    count = view_ref.shape[2]

    def row(i, carry):
        stack[pl.ds(i, count, stride=BLOCK), 0:HALF] = view_ref[i].T
        return carry

    lax.fori_loop(0, BLOCK, row, 0, unroll=8)


def piece_shapes():
    return ((768, LANES), (64, 512), (1024, LANES), (LANES, 1024))


def fold_tiles(value, mask):
    kept = jnp.where(mask, value, 0.0)
    halves = kept[:, :LANES] + kept[:, LANES:]
    return halves + pltpu.roll(halves, HALF, 1)


def update_kernel(
    scale,
    sum_q,
    sum_o,
    sum_i,
    sum_d,
    root_l,
    root_r,
    vec_g,
    vecs,
    vec_m,
    vec_s,
    mixed,
    input_grad,
    w,
    m,
    sl,
    sr,
    out_g,
    out_sl,
    out_sr,
    out_m,
    out_w,
    out_vg,
    out_vs,
    out_vm,
    out_v,
    out_mixed,
    out_input_grad,
    first,
    second,
):
    count = root_l.shape[2]
    bf = jnp.bfloat16
    out_mixed[...] = mixed[...]
    out_input_grad[...] = input_grad[...]

    @pl.when(pl.program_id(0) == 0)
    def _():
        total = vec_g[...]
        out_vg[...] = total
        scaled = total * scale
        fresh = VEC_DECAY * vec_s[...] + (1.0 - VEC_DECAY) * scaled * scaled
        out_vs[...] = fresh
        momentum = BETA * vec_m[...] + scaled * lax.rsqrt(fresh + VEC_EPS)
        out_vm[...] = momentum
        out_v[...] = vecs[...] - VEC_RATE * momentum
        rows = sum_q.shape[0]
        first[0:rows, 0:HALF] = sum_q[:, 0:HALF]
        first[rows : 2 * rows, 0:HALF] = sum_q[:, HALF:LANES]
        base = 2 * rows
        for b in range(8):
            first[base + b * 64 : base + b * 64 + 64, 0:HALF] = sum_o[:, b * HALF : (b + 1) * HALF]
        base += 512
        first[base : base + 1024, 0:HALF] = sum_i[:, 0:HALF]
        first[base + 1024 : base + 2048, 0:HALF] = sum_i[:, HALF:LANES]
        base += 2048
        for r in range(2):
            for b in range(16):
                at = base + (r * 16 + b) * 64
                first[at : at + 64, 0:HALF] = sum_d[r * 64 : r * 64 + 64, b * HALF : (b + 1) * HALF]

        def row(i, carry):
            both = jnp.concatenate([root_l[i], root_r[i]], 0)
            second[pl.ds(i, count, stride=BLOCK), :] = both.T
            return carry

        lax.fori_loop(0, BLOCK, row, 0, unroll=8)
        row_id = lax.broadcasted_iota(jnp.int32, (256, 256), 0)
        col_id = lax.broadcasted_iota(jnp.int32, (256, 256), 1)
        mask = lax.shift_right_logical(row_id, 6) == lax.shift_right_logical(col_id, 6)
        zero = jnp.zeros((256, 256), jnp.float32)

        def spread(v):
            return jnp.where(mask, jnp.concatenate([v, v, v, v], 1), zero).astype(bf)

        def four(k, carry):
            at = pl.ds(pl.multiple_of(k * 256, 256), 256)
            s32 = first[at, 0:HALF] * scale
            s = s32.astype(bf)
            left = second[at, 0:HALF]
            right = second[at, HALF:LANES].astype(bf)
            outer = lax.dot_general(s, s, (((1,), (1,)), ((), ())), preferred_element_type=jnp.float32)
            inner = lax.dot_general(spread(s32), s, (((0,), (0,)), ((), ())), preferred_element_type=jnp.float32)
            shaped = jnp.dot(spread(left), s, preferred_element_type=jnp.float32)
            shaped = jnp.dot(spread(shaped), right, preferred_element_type=jnp.float32)
            first[at, HALF:LANES] = fold_tiles(outer, mask)[:, HALF:LANES]
            second[at, 0:HALF] = inner
            second[at, HALF:LANES] = shaped
            return carry

        lax.fori_loop(0, count // 4, four, 0, unroll=4)

    i0 = pl.program_id(0) * w.shape[0]

    def rows_out(ii, carry):
        at = pl.ds(i0 + ii, count, stride=BLOCK)
        one = first[at, :].T
        two = second[at, :].T
        out_g[ii] = one[0:HALF]
        out_sl[ii] = DECAY * sl[ii] + (1.0 - DECAY) * one[HALF:LANES]
        out_sr[ii] = DECAY * sr[ii] + (1.0 - DECAY) * two[0:HALF]
        fresh = BETA * m[ii] + two[HALF:LANES]
        out_m[ii] = fresh
        out_w[ii] = w[ii] - RATE * fresh
        return carry

    lax.fori_loop(0, w.shape[0], rows_out, 0, unroll=True)


def update_blocks(sums, blocks, vec_grads, vecs, results, token_total):
    views = [jnp.transpose(a, (1, 2, 0)) for a in blocks]
    count = blocks[0].shape[0]
    rows = 8
    whole = pl.BlockSpec(memory_space=pltpu.VMEM)
    steps = BLOCK // rows
    some = pl.BlockSpec((results[0].shape[0] // steps, results[0].shape[1]), lambda i: (i, 0))
    part = pl.BlockSpec((rows, BLOCK, count), lambda i: (i, 0, 0))
    vec = jax.ShapeDtypeStruct(vec_grads.shape, jnp.float32)
    outs = pl.pallas_call(
        functools.partial(update_kernel, token_total ** (-0.5)),
        grid=(steps,),
        out_shape=[jax.ShapeDtypeStruct((BLOCK, BLOCK, count), jnp.float32)] * 5
        + [vec] * 4
        + [jax.ShapeDtypeStruct(a.shape, a.dtype) for a in results],
        in_specs=[whole] * 10 + [some] * 2 + [part] * 4,
        out_specs=[part] * 5 + [whole] * 4 + [some] * 2,
        scratch_shapes=[
            pltpu.VMEM((count * BLOCK, LANES), jnp.float32),
            pltpu.VMEM((count * BLOCK, LANES), jnp.float32),
        ],
        compiler_params=pltpu.CompilerParams(vmem_limit_bytes=VMEM_LIMIT),
        name="update_blocks",
    )(*sums, *views[4:], vec_grads, *vecs, *results, *views[:4])
    return [jnp.transpose(a, (2, 0, 1)) for a in outs[:5]], outs[5:9], outs[9:]


DEPTH = 4


def layer_kernel(
    lengths,
    order,
    view,
    tokens,
    cot,
    vecs,
    mixed,
    input_grad,
    sum_q,
    sum_o,
    sum_i,
    sum_d,
    vec_grads,
    gq,
    go,
    gi,
    gd,
    wqkv,
    cq,
    co,
    ci,
    cd,
    yq,
    yo,
    yi,
    yd,
    yv,
    zq,
    zo,
    zi,
    zd,
    zv,
    rows_one,
    rows_two,
    rows_t,
    grad_rows,
    grad_attn,
    probs,
    qkv,
    ctx,
    gctx,
    far,
    inx,
    macc,
    nacc,
    act,
    gin,
    bias_sum,
    qkv_bias,
    vin,
    vout,
    recv,
    send_y,
    send_c,
    send_z,
    rc_recv,
    rc_send,
    ry_recv,
    ry_send,
    rz_recv,
    rz_send,
    x_send,
    x_recv,
    v_send,
    v_recv,
    copy_sem,
):
    bf, f32 = jnp.bfloat16, jnp.float32
    z, y, c, t = place()
    me = slot_of(z, y, c)
    x_peer = (me, 1 - t)
    y_peer = (slot_of(z, 1 - y, c), t)
    c_peer = (slot_of(z, y, 1 - c), t)
    rows = tokens.shape[0]
    own = pl.ds(pl.multiple_of(t * rows, rows), rows)
    other = pl.ds(pl.multiple_of((1 - t) * rows, rows), rows)
    gathered, core_in = (gq, go, gi, gd), (cq, co, ci, cd)
    y_in, z_in = (yq, yo, yi, yd, yv), (zq, zo, zi, zd, zv)
    sums = (sum_q, sum_o, sum_i, sum_d)
    Q, O, I, W, V = range(5)

    def dot(a, b):
        return jnp.dot(a, b, preferred_element_type=f32)

    def dot_nt(a, b):
        return lax.dot_general(a, b, (((1,), (1,)), ((), ())), preferred_element_type=f32)

    def dot_tn(a, b):
        return lax.dot_general(a, b, (((0,), (0,)), ((), ())), preferred_element_type=f32)

    def piece(k, zz, yy, cc):
        if k == O:
            return go.at[zz * 2 + yy, :, pl.ds(pl.multiple_of(cc * 512, 512), 512)]
        return gathered[k].at[slot_of(zz, yy, cc)]

    def near(s):
        return lax.rem(z + (1 - 2 * lax.div(z, 2)) * s + DEPTH, DEPTH)

    def ag_piece(k, zz, yy, cc):
        if k == W:
            return gd.at[slot_of(zz, yy, cc), 0:HALF]
        if k == V:
            return gd.at[slot_of(zz, yy, cc), HALF:LANES]
        return piece(k, zz, yy, cc)

    def ag_copy(k, zz, yy, way):
        src = ag_piece(k, zz, yy, c)
        sem = recv.at[k, slot_of(zz, yy, c)]
        if way == "up":
            return remote(src, src, send_z.at[k, 0, yy * DEPTH + zz], sem, (slot_of(z + 1, y, c), t))
        if way == "down":
            return remote(src, src, send_z.at[k, 1, yy * DEPTH + zz], sem, (slot_of(z - 1, y, c), t))
        if way == "y":
            return remote(src, src, send_y.at[k, zz], sem, y_peer)
        return remote(src, src, send_c.at[k, yy * DEPTH + zz], sem, c_peer)

    def ag_wait(k, zz, yy, cc):
        ref = ag_piece(k, zz, yy, cc)
        remote(ref, ref, send_y.at[k, 0], recv.at[k, slot_of(zz, yy, cc)], y_peer).wait_recv()

    def own_sends_z(k):
        @pl.when(z < DEPTH - 1)
        def _():
            ag_copy(k, z, y, "up").start()

        @pl.when(z > 0)
        def _():
            ag_copy(k, z, y, "down").start()

        ag_copy(k, z, y, "core").start()

    def own_sends_y(k):
        ag_copy(k, z, y, "y").start()

    def z_arrival(kinds, dist):
        @pl.when(z >= dist)
        def _():
            for k in kinds:
                ag_wait(k, z - dist, y, c)

                @pl.when(z < DEPTH - 1)
                def _():
                    ag_copy(k, z - dist, y, "up").start()

                ag_copy(k, z - dist, y, "y").start()
                ag_copy(k, z - dist, y, "core").start()

        @pl.when(z + dist < DEPTH)
        def _():
            for k in kinds:
                ag_wait(k, z + dist, y, c)

                @pl.when(z > 0)
                def _():
                    ag_copy(k, z + dist, y, "down").start()

                ag_copy(k, z + dist, y, "y").start()
                ag_copy(k, z + dist, y, "core").start()

    def y_arrival(kinds, dist):
        def one(zz):
            for k in kinds:
                ag_wait(k, zz, 1 - y, c)
                ag_copy(k, zz, 1 - y, "core").start()

        if dist == 0:
            one(z)
            return

        @pl.when(z >= dist)
        def _():
            one(z - dist)

        @pl.when(z + dist < DEPTH)
        def _():
            one(z + dist)

    def v_forward(zz, yy):
        ag_wait(V, zz, yy, c)

        @pl.when((zz <= z) & (z < DEPTH - 1))
        def _():
            ag_copy(V, zz, yy, "up").start()

        @pl.when((zz >= z) & (z > 0))
        def _():
            ag_copy(V, zz, yy, "down").start()

        ag_copy(V, zz, yy, "core").start()

    def v_arrival(dist):
        for yy in (y, 1 - y):

            @pl.when(z >= dist)
            def _():
                v_forward(z - dist, yy)

            @pl.when(z + dist < DEPTH)
            def _():
                v_forward(z + dist, yy)

    def drain(k, zz, yy):
        ag_copy(k, zz, yy, "core").wait_send()
        if k == V:

            @pl.when((yy == y) & (zz == z))
            def _():
                ag_copy(k, zz, yy, "y").wait_send()

            @pl.when((zz <= z) & (z < DEPTH - 1))
            def _():
                ag_copy(k, zz, yy, "up").wait_send()

            @pl.when((zz >= z) & (z > 0))
            def _():
                ag_copy(k, zz, yy, "down").wait_send()

            return

        @pl.when(yy == y)
        def _():
            ag_copy(k, zz, y, "y").wait_send()

            @pl.when((zz <= z) & (z < DEPTH - 1))
            def _():
                ag_copy(k, zz, y, "up").wait_send()

            @pl.when((zz >= z) & (z > 0))
            def _():
                ag_copy(k, zz, y, "down").wait_send()

    def add(dst, *terms):
        count, width = dst.shape
        step = min(count, 256 * LANES // width)

        def body(i, carry):
            at = pl.ds(pl.multiple_of(i * step, 16), step)
            total = terms[0][at, :].astype(f32)
            for term in terms[1:]:
                total = total + term[at, :].astype(f32)
            dst[at, :] = total.astype(dst.dtype)
            return carry

        lax.fori_loop(0, count // step, body, 0)

    side = lax.div(z, 2)
    end_z, inner_z = 3 * side, 1 + side
    is_end = z == end_z

    def rc_copy(k, zz, yy):
        at = zz * 2 + yy
        return remote(piece(k, zz, yy, 1 - c), core_in[k].at[at], rc_send.at[k, at], rc_recv.at[k, at], c_peer)

    def ry_copy(k, zz):
        if k == V:
            return remote(ag_piece(V, z, 1 - y, c), y_in[V].at[0], ry_send.at[V, 0], ry_recv.at[V, 0], y_peer)
        return remote(ag_piece(k, zz, 1 - y, c), y_in[k].at[zz], ry_send.at[k, zz], ry_recv.at[k, zz], y_peer)

    def z_slot(k, slot, yy):
        return z_in[k].at[slot * 2 + yy if k == V else slot]

    def z_sem(slot, yy):
        return slot * 2 + yy

    def rz_copy(k, s, yy, from_end):
        slot = s - 1 if from_end else {3: 0, 2: 1, 1: 3}[s]
        to = inner_z if from_end else {3: end_z, 2: 3 - end_z, 1: 3 - inner_z}[s]
        sent, landed = rz_send.at[k, (s - 1) * 2 + yy], rz_recv.at[k, z_sem(slot, yy)]
        return remote(ag_piece(k, near(s), yy, c), z_slot(k, slot, yy), sent, landed, (slot_of(to, y, c), t))

    def z_landed(k, slot, yy):
        ref = z_slot(k, slot, yy)
        remote(ref, ref, rz_send.at[k, 0], rz_recv.at[k, z_sem(slot, yy)], y_peer).wait_recv()
        return ref

    def y_landed(k, zz):
        ref = y_in[k].at[0 if k == V else zz]
        remote(ref, ref, ry_send.at[k, 0], ry_recv.at[k, 0 if k == V else zz], y_peer).wait_recv()
        return ref

    def rc_add(k, zz, yy):
        at = zz * 2 + yy
        remote(core_in[k].at[at], core_in[k].at[at], rc_send.at[k, 0], rc_recv.at[k, at], c_peer).wait_recv()
        mine = piece(k, zz, yy, c)
        add(mine, mine, core_in[k].at[at])

        @pl.when(yy != y)
        def _():
            ry_copy(k, zz).start()

    def z_step(k, s, yy, *terms):
        mine = ag_piece(k, near(s), yy, c)

        @pl.when(is_end)
        def _():
            if terms:
                add(mine, mine, *terms)
            rz_copy(k, s, yy, True).start()

        @pl.when(jnp.logical_not(is_end))
        def _():
            more = terms if s == 3 else (*terms, z_landed(k, s, yy))
            if more:
                add(mine, mine, *more)
            rz_copy(k, s, yy, False).start()

    def ry_add(k, s):
        z_step(k, s, y, y_landed(k, near(s)))

    def total_of(k):
        return sum_d.at[(k - W) * HALF : (k - W + 1) * HALF] if k >= W else sums[k]

    def z_total(k, yy, dst, *terms):
        mine = ag_piece(k, z, yy, c)
        first = z_landed(k, 0, yy)

        @pl.when(is_end)
        def _():
            add(dst, mine, first, z_landed(k, 1, yy), *terms)

        @pl.when(jnp.logical_not(is_end))
        def _():
            add(dst, mine, first, z_landed(k, 3, yy), *terms)

    def own_total(k):
        z_total(k, y, total_of(k), y_landed(k, z))

    def v_cross():
        mine = ag_piece(V, z, 1 - y, c)
        z_total(V, 1 - y, mine)
        ry_copy(V, z).start()

    def x_rows(ref, index):
        return remote(ref.at[own], ref.at[own], x_send.at[index], x_recv.at[index], x_peer)

    def x_rows_wait(ref, index):
        remote(ref.at[other], ref.at[other], x_send.at[index], x_recv.at[index], x_peer).wait_recv()

    def x_part(index):
        return remote(far.at[index], inx.at[index], x_send.at[4 + index], x_recv.at[4 + index], x_peer)

    def by_rows(body, step=64):
        def run(i, carry):
            body(pl.multiple_of(i * step, step), step)
            return carry

        lax.fori_loop(0, rows // step, run, 0)

    def norm(value):
        average = jnp.mean(value, -1, keepdims=True)
        centred = value - average
        inverse = lax.rsqrt(jnp.mean(centred * centred, -1, keepdims=True) + EPS)
        return centred * inverse, inverse

    def norm_grad(grad, unit, inverse, gain):
        scaled = grad * gain
        return inverse * (
            scaled - jnp.mean(scaled, -1, keepdims=True) - unit * jnp.mean(scaled * unit, -1, keepdims=True)
        )

    barrier = pltpu.get_barrier_semaphore()
    z_peers = [(slot_of(lax.rem(z + step, DEPTH), y, c), t) for step in range(1, DEPTH)]
    everyone = [x_peer, y_peer, c_peer] + z_peers
    for device in everyone:
        pl.semaphore_signal(barrier, inc=1, device_id=device, device_id_type=MESH_ID)

    def prepare(held, stack):
        load = pltpu.make_async_copy(view, held, copy_sem.at[0])
        load.start()

        def first_norm(at, step):
            unit, inverse = norm(tokens[pl.ds(at, step), :])
            to = pl.ds(pl.multiple_of(t * rows + at, step), step)
            rows_one[to, :] = (unit * vecs[0:1, :] + vecs[1:2, :]).astype(bf)
            grad_rows[to, :] = cot[pl.ds(at, step), :].astype(bf)

        load.wait()
        lay_blocks(held, stack)
        n = gq.shape[1]
        gq[me, :, 0:HALF] = stack[0:n, 0:HALF].astype(bf)
        gq[me, :, HALF:LANES] = stack[n : 2 * n, 0:HALF].astype(bf)
        pl.semaphore_wait(barrier, len(everyone))
        own_sends_y(Q)
        own_sends_z(Q)
        by_rows(first_norm)
        x_rows(rows_one, 0).start()
        base = 2 * n
        wide = [stack[base + b * 64 : base + b * 64 + 64, 0:HALF] for b in range(8)]
        go[z * 2 + y, :, pl.ds(pl.multiple_of(c * 512, 512), 512)] = jnp.concatenate(wide, 1).astype(bf)
        own_sends_y(O)
        own_sends_z(O)
        base += 512
        gi[me, :, 0:HALF] = stack[base : base + 1024, 0:HALF].astype(bf)
        gi[me, :, HALF:LANES] = stack[base + 1024 : base + 2048, 0:HALF].astype(bf)
        base += 2048
        for r in range(2):
            for b in range(16):
                at = base + (r * 16 + b) * 64
                gd[me, r * 64 : r * 64 + 64, b * HALF : (b + 1) * HALF] = stack[at : at + 64, 0:HALF].astype(bf)

    pl.run_scoped(
        prepare,
        pltpu.VMEM(view.shape, f32),
        pltpu.VMEM((view.shape[2] * BLOCK, LANES), f32),
    )
    x_rows(grad_rows, 1).start()
    z_arrival((Q, O), 1)
    y_arrival((Q, O), 0)
    for k in (I, W, V):
        own_sends_z(k)
    z_arrival((Q, O), 2)
    own_sends_y(I)
    y_arrival((Q, O), 1)
    z_arrival((Q, O), 3)
    own_sends_y(W)
    own_sends_y(V)

    def core_waits(kinds, zz):
        for k in kinds:
            for yy in (y, 1 - y):
                ag_wait(k, zz, yy, 1 - c)

    x_rows_wait(rows_one, 0)

    ends = []
    for p in range(ARTICLES):
        length = 0
        for a in range(ARTICLES):
            length = length + jnp.where(order[0, p] == a, lengths[0, a], 0)
        ends.append(length + ends[-1] if p else length)

    def allowed(first, count):
        ids = lax.broadcasted_iota(jnp.int32, (rows, 1), 0) + first
        start = jnp.zeros((rows, 1), jnp.int32)
        for end in ends:
            start = jnp.where(ids >= end, end, start)
        start = jnp.where(ids >= ends[-1], ids, start)
        keys = lax.broadcasted_iota(jnp.int32, (rows, count), 1)
        return (keys <= ids) & (keys >= start)

    scale = HD ** (-0.5)
    strip = 1024

    def assemble(h):
        for yy in range(2):
            even, odd = gq.at[slot_of(h, yy, 0)], gq.at[slot_of(h, yy, 1)]
            at = yy * 192
            wqkv[h, 0:768, at : at + 64] = even[:, 0:64]
            wqkv[h, 768:1024, at : at + 64] = even[0:256, 64:128]
            wqkv[h, 0:512, at + 64 : at + 128] = even[256:768, 64:128]
            wqkv[h, 512:1024, at + 64 : at + 128] = odd[0:512, 0:64]
            wqkv[h, 0:256, at + 128 : at + 192] = odd[512:768, 0:64]
            wqkv[h, 256:1024, at + 128 : at + 192] = odd[:, 64:128]

    def disassemble(h, value):
        for yy in range(2):
            even, odd = gq.at[slot_of(h, yy, 0)], gq.at[slot_of(h, yy, 1)]
            at = yy * 192
            even[:, 0:64] = value[0:768, at : at + 64]
            even[0:256, 64:128] = value[768:1024, at : at + 64]
            even[256:768, 64:128] = value[0:512, at + 64 : at + 128]
            odd[0:512, 0:64] = value[512:1024, at + 64 : at + 128]
            odd[512:768, 0:64] = value[0:256, at + 128 : at + 192]
            odd[:, 64:128] = value[256:1024, at + 128 : at + 192]

    def lanes(start, size, unit):
        return pl.ds(pl.multiple_of(start, unit), size)

    qv = vecs[pl.ds(6 + t, 1), :]
    for h in range(DEPTH):
        none = jnp.zeros((1, HD), f32)
        qkv_bias[h] = jnp.concatenate([qv[:, h * 256 : h * 256 + 128], none, qv[:, h * 256 + 128 : h * 256 + 256]], 1)

    def head(h):
        core_waits((Q,), h)
        assemble(h)
        qkv[h] = (dot(rows_one[...], wqkv[h]) + qkv_bias[h]).astype(bf)
        for block in range(2):
            at, seen = slice(block * rows, (block + 1) * rows), (block + 1) * rows
            scores = dot_nt(qkv[h, at, 0:128], qkv[h, 0:seen, 128:256]) * scale
            scores = jnp.where(allowed(block * rows, seen), scores, NEG)
            expo = jnp.exp(scores - jnp.max(scores, -1, keepdims=True))
            low = (expo / jnp.sum(expo, -1, keepdims=True)).astype(bf)
            probs[h, at, 0:seen] = low
            ctx[at, lanes(h * HD, HD, HD)] = dot(low, qkv[h, 0:seen, 256:384]).astype(bf)

    head(near(0))
    y_arrival((Q, O), 2)
    head(near(1))
    y_arrival((Q, O), 3)
    head(near(2))
    z_arrival((I, W), 1)
    head(near(3))
    y_arrival((I, W), 0)
    v_forward(z, 1 - y)
    for zz in range(DEPTH):
        core_waits((O,), zz)

    def w_out(at, count):
        return go[at : at + count].reshape(count * 64, 1024)

    far[0] = dot(ctx[other, :], w_out(0, 8)).astype(bf)
    x_part(0).start()
    mixed[...] = tokens[...] + dot(ctx[own, :], w_out(0, 8)) + vecs[4:5, :]
    z_arrival((I, W), 2)
    v_arrival(1)
    y_arrival((I, W), 1)
    x_part(0).wait_recv()

    def second_norm(at, step):
        value = mixed[pl.ds(at, step), :] + inx[0, pl.ds(at, step), :].astype(f32)
        mixed[pl.ds(at, step), :] = value
        unit, inverse = norm(value)
        to = pl.ds(pl.multiple_of(t * rows + at, step), step)
        rows_two[to, :] = (unit * vecs[2:3, :] + vecs[3:4, :]).astype(bf)

    by_rows(second_norm)
    x_rows(rows_two, 2).start()
    z_arrival((I, W), 3)
    v_arrival(2)
    macc[...] = jnp.zeros_like(macc)
    nacc[...] = jnp.zeros_like(nacc)
    vout[...] = jnp.zeros_like(vout)
    x_rows_wait(grad_rows, 1)

    def ffn(half, zz):
        first = 4 * zz
        at = pl.ds(pl.multiple_of(lax.rem(t + half, 2) * rows, rows), rows)
        units = lanes(zz * 512, 512, 512)
        bias_row = vecs[pl.ds(8 + 2 * t + lax.div(zz, 2), 1), lanes(lax.rem(zz, 2) * 512, 512, 512)]

        def w_in(start, count):
            return jnp.concatenate([gi[first + j, start : start + count, :] for j in range(4)], 1)

        def w_down(start, count):
            return gd[pl.ds(first, 4), :, start : start + count].reshape(512, count)

        inner = dot(rows_two[at, :], w_in(0, D)) + bias_row
        square = inner * inner
        bent = jnp.tanh(GELU_A * inner * (1.0 + GELU_B * square))
        act[at, units] = (0.5 * inner * (1.0 + bent)).astype(bf)
        slope = 0.5 * (1.0 + bent) + 0.5 * inner * (1.0 - bent * bent) * (GELU_A * (1.0 + 3.0 * GELU_B * square))
        gin[at, units] = (dot_nt(grad_rows[at, :], w_down(0, D)) * slope).astype(bf)
        for nb in range(4):
            out = slice(nb * 256, nb * 256 + 256)
            nacc[at, out] += dot_nt(gin[at, units], w_in(nb * 256, 256))
            macc[at, out] += dot(act[at, units], w_down(nb * 256, 256))

    def own_rows(i, carry):
        @pl.when(i == 2)
        def _():
            y_arrival((I, W), 2)

        @pl.when(i == 3)
        def _():
            v_arrival(3)
            y_arrival((I, W), 3)

        core_waits((I, W, V), near(i))
        ffn(0, near(i))
        return carry

    lax.fori_loop(0, DEPTH, own_rows, 0)
    x_rows_wait(rows_two, 2)
    rows_t[...] = rows_two[...].T

    def ffn_grads(zz):
        first = 4 * zz
        units = lanes(zz * 512, 512, 512)
        for k in (I, W, V):
            for yy in range(2):
                drain(k, zz, yy)
        bias_sum[zz] = jnp.sum(gin[:, units].astype(f32), 0, keepdims=True)
        for nb in range(4):
            out = slice(nb * 256, nb * 256 + 256)
            part = dot(rows_t[out, :], gin[:, units]).astype(bf)
            for j in range(4):
                gi[first + j, out, :] = part[:, j * LANES : (j + 1) * LANES]
        for yy in (1 - y, y):
            rc_copy(I, zz, yy).start()
        act_t = act[:, units].T
        for nb in range(4):
            out = slice(nb * 256, nb * 256 + 256)
            part = dot(act_t, grad_rows[:, out]).astype(bf)
            gd[pl.ds(first, 4), :, out] = part.reshape(4, LANES, 256)
        for yy in (1 - y, y):
            rc_copy(W, zz, yy).start()

    def reduce_core(zz):
        for yy in (1 - y, y):
            for k in (I, W):
                rc_add(k, zz, yy)

    def v_step(s):
        for yy in (1 - y, y):
            z_step(V, s, yy)

    def other_rows(i, carry):
        @pl.when(i == DEPTH)
        def _():
            far[1] = nacc[other, :].astype(bf)
            x_part(1).start()
            far[2] = macc[other, :].astype(bf)
            x_part(2).start()

        @pl.when(i > 0)
        def _():
            ffn_grads(near(DEPTH - i))

        @pl.when(i > 1)
        def _():
            reduce_core(near(DEPTH + 1 - i))

        for s in (3, 2, 1):

            @pl.when(i == DEPTH + 1 - s)
            def _():
                v_step(s)

        @pl.when(i < DEPTH)
        def _():
            ffn(1, near(DEPTH - 1 - i))

        return carry

    lax.fori_loop(0, DEPTH + 1, other_rows, 0)
    reduce_core(near(0))
    for zz in range(DEPTH):
        for side in range(2):
            row, start = 8 + 2 * side + zz // 2, zz % 2 * 512
            vout[0, row : row + 1, start : start + 512] = jnp.where(t == side, bias_sum[zz], 0.0)
    rows_t[...] = rows_one[...].T
    x_part(1).wait_recv()

    def row_sum(row, value):
        vout[0, row : row + 1, :] += jnp.sum(value, 0, keepdims=True)

    def second_back(at, step):
        here = pl.ds(at, step)
        in_group = pl.ds(pl.multiple_of(t * rows + at, step), step)
        grad = nacc[in_group, :] + inx[1, here, :].astype(f32)
        unit, inverse = norm(mixed[here, :])
        back = cot[here, :] + norm_grad(grad, unit, inverse, vecs[2:3, :])
        input_grad[here, :] = back
        grad_attn[in_group, :] = back.astype(bf)
        row_sum(2, grad * unit)
        row_sum(3, grad)
        row_sum(4, back)
        row_sum(5, cot[here, :])

    by_rows(second_back)
    x_rows(grad_attn, 3).start()
    for s in (3, 2):
        for k in (I, W):
            ry_add(k, s)
    v_cross()
    x_part(2).wait_recv()

    def mixed_out(at, step):
        here = pl.ds(at, step)
        in_group = pl.ds(pl.multiple_of(t * rows + at, step), step)
        mixed[here, :] = mixed[here, :] + macc[in_group, :] + inx[2, here, :].astype(f32) + vecs[5:6, :]

    by_rows(mixed_out)
    for zz in range(DEPTH):
        for yy in range(2):
            drain(O, zz, yy)
            drain(Q, zz, yy)
    x_rows_wait(grad_attn, 3)
    gctx[...] = dot_nt(grad_attn[...], w_out(0, 8)).astype(bf)
    ctx_t = ctx[...].T
    for nb in range(4):
        at = slice(nb * 256, nb * 256 + 256)
        go[:, :, at] = dot(ctx_t, grad_attn[:, at]).astype(bf).reshape(8, 64, 256)
    for zz in range(DEPTH):
        for yy in range(2):
            rc_copy(O, zz, yy).start()

    def head_back(h):
        q0, q1 = qkv[h, 0:rows, 0:128], qkv[h, rows : 2 * rows, 0:128]
        grads = []
        for block in range(2):
            at, seen = slice(block * rows, (block + 1) * rows), (block + 1) * rows
            low = probs[h, at, 0:seen]
            given = gctx[at, h * 128 : h * 128 + 128]
            prob = low.astype(f32)
            grad_probs = dot_nt(given, qkv[h, 0:seen, 256:384])
            delta = jnp.sum(prob * grad_probs, -1, keepdims=True)
            grad_scores = (prob * (grad_probs - delta)).astype(bf)
            grad_q = dot(grad_scores, qkv[h, 0:seen, 128:256]) * scale
            grad_k = dot_tn(grad_scores, q1 if block else q0) * scale
            grad_v = dot_tn(low, given)
            grads.append((grad_q, grad_k, grad_v))
        (gq0, gk0, gv0), (gq1, gk1, gv1) = grads
        top = jnp.concatenate([gq0, gk0 + gk1[0:rows], gv0 + gv1[0:rows]], 1).astype(bf)
        low_half = jnp.concatenate([gq1, gk1[rows:], gv1[rows:]], 1).astype(bf)
        qkv[h, 0:rows, :] = top
        qkv[h, rows : 2 * rows, :] = low_half
        total = jnp.sum(top.astype(f32), 0, keepdims=True) + jnp.sum(low_half.astype(f32), 0, keepdims=True)
        for side in range(2):
            vout[0, 6 + side : 7 + side, h * 256 : h * 256 + 128] = jnp.where(t == side, total[:, 0:128], 0.0)
            vout[0, 6 + side : 7 + side, h * 256 + 128 : h * 256 + 256] = jnp.where(t == side, total[:, 256:384], 0.0)
        part = dot(rows_t[...], qkv[h]).astype(bf)
        disassemble(h, part)
        for yy in (1 - y, y):
            rc_copy(Q, h, yy).start()
        product = dot_nt(qkv[h], wqkv[h])
        if h == 0:
            nacc[...] = product
        else:
            nacc[...] += product

    for h in range(DEPTH):
        head_back(h)
        if h == 0:
            for yy in (1 - y, y):
                for s in range(DEPTH):
                    rc_add(O, near(s), yy)
        else:
            for yy in (1 - y, y):
                rc_add(Q, h - 1, yy)
        if h == 2:
            for k in (I, W):
                ry_add(k, 1)
    far[3] = nacc[other, :].astype(bf)
    x_part(3).start()
    for yy in (1 - y, y):
        rc_add(Q, DEPTH - 1, yy)
    for k in (I, W):
        own_total(k)
    z_total(V, y, total_of(V), y_landed(V, z))
    x_part(3).wait_recv()

    def first_back(at, step):
        here = pl.ds(at, step)
        in_group = pl.ds(pl.multiple_of(t * rows + at, step), step)
        grad = nacc[in_group, :] + inx[3, here, :].astype(f32)
        unit, inverse = norm(tokens[here, :])
        input_grad[here, :] = input_grad[here, :] + norm_grad(grad, unit, inverse, vecs[0:1, :])
        row_sum(0, grad * unit)
        row_sum(1, grad)

    by_rows(first_back)

    stages = (x_peer, c_peer, y_peer)

    def v_copy(stage):
        return remote(vout.at[stage], vin.at[stage], v_send.at[stage], v_recv.at[stage], stages[stage])

    def vz_copy(step):
        peer = (slot_of(lax.rem(z + step, DEPTH), y, c), t)
        return remote(vout.at[3], vin.at[3 + z], v_send.at[2 + step], v_recv.at[3 + z], peer)

    v_copy(0).start()
    for s in (3, 2, 1):
        ry_add(O, s)
    v_copy(0).wait_recv()
    vout[1] = vout[0] + vin[0]
    v_copy(1).start()
    for s in (3, 2, 1):
        ry_add(Q, s)
    v_copy(1).wait_recv()
    vout[2] = vout[1] + vin[1]
    v_copy(2).start()
    own_total(O)
    v_copy(2).wait_recv()
    vout[3] = vout[2] + vin[2]
    for step in range(1, DEPTH):
        vz_copy(step).start()
    vin[3 + z] = vout[3]
    own_total(Q)
    for step in range(1, DEPTH):
        zz = lax.rem(z + step, DEPTH)
        remote(vin.at[3 + zz], vin.at[3 + zz], v_send.at[0], v_recv.at[3 + zz], y_peer).wait_recv()
    count = vec_grads.shape[0]
    total = ((vin[3] + vin[4]) + vin[5]) + vin[6]
    vec_grads[...] = total[0:count]

    for stage in range(3):
        v_copy(stage).wait_send()
    for step in range(1, DEPTH):
        vz_copy(step).wait_send()
    for index, ref in enumerate((rows_one, grad_rows, rows_two, grad_attn)):
        x_rows(ref, index).wait_send()
    for index in range(4):
        x_part(index).wait_send()
    for k in range(4):
        for zz in range(DEPTH):
            for yy in range(2):
                rc_copy(k, zz, yy).wait_send()
            ry_copy(k, zz).wait_send()
        for s in range(1, DEPTH):
            rz_copy(k, s, y, True).wait_send()
    ry_copy(V, z).wait_send()
    for yy in range(2):
        for s in range(1, DEPTH):
            rz_copy(V, s, yy, True).wait_send()


def run_layer(tokens, cotangent, lengths, order, weights, vec_params):
    bf, f32 = jnp.bfloat16, jnp.float32
    rows = tokens.shape[0]
    group = 2 * rows
    owners = 16
    shapes = piece_shapes()
    view = jnp.transpose(weights, (1, 2, 0))
    vmem = pl.BlockSpec(memory_space=pltpu.VMEM)
    smem = pl.BlockSpec(memory_space=pltpu.SMEM)

    halved = shapes[:3] + ((HALF, D),)

    def many(count, kinds):
        return [pltpu.VMEM((count,) + s, bf) for s in kinds]

    full = pltpu.VMEM((group, D), bf)
    dma = pltpu.SemaphoreType.DMA
    return pl.pallas_call(
        layer_kernel,
        out_shape=[jax.ShapeDtypeStruct((rows, D), f32)] * 2
        + [jax.ShapeDtypeStruct(s, f32) for s in shapes]
        + [jax.ShapeDtypeStruct(vec_params.shape, f32)],
        in_specs=[smem, smem, pl.BlockSpec(memory_space=pl.ANY)] + [vmem] * 3,
        out_specs=[vmem] * 7,
        scratch_shapes=[
            pltpu.VMEM((owners,) + shapes[0], bf),
            pltpu.VMEM((owners // 2, BLOCK, D), bf),
            pltpu.VMEM((owners,) + shapes[2], bf),
            pltpu.VMEM((owners,) + shapes[3], bf),
            pltpu.VMEM((DEPTH, D, 3 * HD), bf),
        ]
        + many(2 * DEPTH, shapes)
        + many(DEPTH, halved)
        + many(1, halved[3:])
        + many(DEPTH, halved)
        + many(2 * DEPTH, halved[3:])
        + [
            full,
            full,
            pltpu.VMEM((D, group), bf),
            full,
            full,
            pltpu.VMEM((DEPTH, group, group), bf),
            pltpu.VMEM((DEPTH, group, 3 * HD), bf),
            pltpu.VMEM((group, DEPTH * HD), bf),
            pltpu.VMEM((group, DEPTH * HD), bf),
            pltpu.VMEM((4, rows, D), bf),
            pltpu.VMEM((4, rows, D), bf),
            pltpu.VMEM((group, D), f32),
            pltpu.VMEM((group, D), f32),
            pltpu.VMEM((group, 2 * D), bf),
            pltpu.VMEM((group, 2 * D), bf),
            pltpu.VMEM((DEPTH, 1, 512), f32),
            pltpu.VMEM((DEPTH, 1, 3 * HD), f32),
            pltpu.VMEM((7, 16, D), f32),
            pltpu.VMEM((4, 16, D), f32),
            dma((5, owners)),
            dma((5, DEPTH)),
            dma((5, 2 * DEPTH)),
            dma((5, 2, 2 * DEPTH)),
            dma((4, 2 * DEPTH)),
            dma((4, 2 * DEPTH)),
            dma((5, DEPTH)),
            dma((5, DEPTH)),
            dma((5, 2 * DEPTH)),
            dma((5, 2 * DEPTH)),
            dma((8,)),
            dma((8,)),
            dma((6,)),
            dma((7,)),
            dma((1,)),
        ],
        compiler_params=pltpu.CompilerParams(
            collective_id=0, has_side_effects=True, vmem_limit_bytes=VMEM_LIMIT
        ),
        name="layer",
    )(lengths, order, view, tokens, cotangent, vec_params)


def per_device(
    grp_count,
    tp_count,
    tokens,
    cotangent,
    lengths,
    order,
    weights,
    momentum,
    stat_left,
    stat_right,
    root_left,
    root_right,
    vec_params,
    vec_momentum,
    vec_second,
):
    fits = grp_count == 4 * DEPTH and tp_count == 2 and tokens.shape[0] == 256
    if not fits or lengths.shape[1] != ARTICLES:
        return per_device_general(
            tokens,
            cotangent,
            lengths,
            order,
            weights,
            momentum,
            stat_left,
            stat_right,
            root_left,
            root_right,
            vec_params,
            vec_momentum,
            vec_second,
        )
    token_total = tokens.shape[0] * tp_count * grp_count
    mixed, input_grad, *sums, vec_grads = run_layer(tokens, cotangent, lengths, order, weights, vec_params)
    blocks, vecs, results = update_blocks(
        sums,
        (weights, momentum, stat_left, stat_right, root_left, root_right),
        vec_grads,
        (vec_params, vec_momentum, vec_second),
        (mixed, input_grad),
        token_total,
    )
    return (*results, *blocks, *vecs)


def solution(mesh):
    placed = (
        P(("grp", "tp"), None),
        P(("grp", "tp"), None),
        P("grp", None),
        P("grp", None),
        P(("tp", "grp"), None, None),
        P(("tp", "grp"), None, None),
        P(("tp", "grp"), None, None),
        P(("tp", "grp"), None, None),
        P(("tp", "grp"), None, None),
        P(("tp", "grp"), None, None),
        P(),
        P(),
        P(),
    )
    return jax.shard_map(
        functools.partial(per_device, mesh.shape["grp"], mesh.shape["tp"]),
        mesh=mesh,
        in_specs=placed,
        out_specs=(
            P(("grp", "tp"), None),
            P(("grp", "tp"), None),
            P(("tp", "grp"), None, None),
            P(("tp", "grp"), None, None),
            P(("tp", "grp"), None, None),
            P(("tp", "grp"), None, None),
            P(("tp", "grp"), None, None),
            P(),
            P(),
            P(),
            P(),
        ),
        check_vma=False,
    )
```

```python
import functools

import jax
import jax.numpy as jnp
from jax import lax
from jax.experimental import pallas as pl
from jax.experimental.pallas import tpu as pltpu
from jax.sharding import PartitionSpec as P

D = 1024
HEADS = 8
HD = 128
FF = 4096
BLOCK = 64


EPS = 1e-05
NEG = -1e30
DECAY = 0.9
BETA = 0.9
RATE = 0.05
VEC_DECAY = 0.9
VEC_RATE = 0.2
VEC_EPS = 1e-08


def norm_rows(value, gain, shift):
    average = jnp.mean(value, -1, keepdims=True)
    centred = value - average
    inverse = lax.rsqrt(jnp.mean(centred * centred, -1, keepdims=True) + EPS)
    normed = centred * inverse
    return (normed * gain + shift, normed, inverse)


def norm_back(grad_out, normed, inverse, gain):
    scaled = grad_out * gain
    return inverse * (
        scaled
        - jnp.mean(scaled, -1, keepdims=True)
        - normed * jnp.mean(scaled * normed, -1, keepdims=True)
    )


def segment_ids(lengths_row, order_row, group_rows):
    article_count = lengths_row.shape[0]
    slots = jnp.arange(article_count, dtype=jnp.int32)
    picks = (order_row[:, None] == slots[None, :]).astype(jnp.int32)
    packed = jnp.sum(picks * lengths_row[None, :], 1)
    ends = jnp.cumsum(packed)
    spots = jnp.arange(group_rows, dtype=jnp.int32)
    return jnp.sum((spots[:, None] >= ends[None, :]).astype(jnp.int32), 1)


def allowed_mask(row_ids, row_segs, segments, key_ids, article_count):
    causal = key_ids[None, :] <= row_ids[:, None]
    same = segments[None, :] == row_segs[:, None]
    alone = (row_segs[:, None] < article_count) | (key_ids[None, :] == row_ids[:, None])
    return causal & same & alone


def from_columns(tiles, row_total, col_total):
    return (
        tiles.reshape(col_total // BLOCK, row_total // BLOCK, BLOCK, BLOCK)
        .transpose(1, 2, 0, 3)
        .reshape(row_total, col_total)
    )


def from_rows(tiles, row_total, col_total):
    return (
        tiles.reshape(row_total // BLOCK, col_total // BLOCK, BLOCK, BLOCK)
        .transpose(0, 2, 1, 3)
        .reshape(row_total, col_total)
    )


def to_columns(matrix):
    row_total, col_total = matrix.shape
    return (
        matrix.reshape(row_total // BLOCK, BLOCK, col_total // BLOCK, BLOCK)
        .transpose(2, 0, 1, 3)
        .reshape(-1, BLOCK, BLOCK)
    )


def to_rows(matrix):
    row_total, col_total = matrix.shape
    return (
        matrix.reshape(row_total // BLOCK, BLOCK, col_total // BLOCK, BLOCK)
        .transpose(0, 2, 1, 3)
        .reshape(-1, BLOCK, BLOCK)
    )


def per_device_general(
    tokens,
    cotangent,
    lengths,
    order,
    weights,
    momentum,
    stat_left,
    stat_right,
    root_left,
    root_right,
    vec_params,
    vec_momentum,
    vec_second,
):
    groups = lax.axis_size("grp")
    tp_size = lax.axis_size("tp")
    tp_rank = lax.axis_index("tp")
    tok_rows = tokens.shape[0]
    group_rows = tok_rows * tp_size
    article_count = lengths.shape[1]
    owners = groups * tp_size
    block_area = BLOCK * BLOCK * owners
    qkv_count = 3 * D * D // block_area
    out_count = D * D // block_area
    in_count = D * FF // block_area
    owned_blocks = weights.shape[0]
    heads_here = HEADS // tp_size
    qkv_cols = 3 * D // tp_size
    feat_here = D // tp_size
    ff_here = FF // tp_size
    qv_width = 2 * D // tp_size
    token_total = group_rows * groups
    gathered = lax.all_gather(weights.astype(jnp.bfloat16), "grp", axis=0, tiled=True)
    per_owner = gathered.reshape(groups, owned_blocks, BLOCK, BLOCK)
    marks = [0, qkv_count, qkv_count + out_count, qkv_count + out_count + in_count, owned_blocks]
    pieces = [
        per_owner[:, marks[index] : marks[index + 1]].reshape(-1, BLOCK, BLOCK)
        for index in range(4)
    ]
    w_qkv = from_columns(pieces[0], D, qkv_cols)
    w_out = from_rows(pieces[1], feat_here, D)
    w_in = from_columns(pieces[2], D, ff_here)
    w_down = from_rows(pieces[3], ff_here, D)
    w_qkv_heads = w_qkv.reshape(D, heads_here, 3, HD)
    w_out_heads = w_out.reshape(heads_here, HD, D)
    segments = segment_ids(lengths[0], order[0], group_rows)
    gain_one = vec_params[0]
    shift_one = vec_params[1]
    gain_two = vec_params[2]
    shift_two = vec_params[3]
    bias_out = vec_params[4]
    bias_down = vec_params[5]
    qv_here = lax.dynamic_slice_in_dim(
        vec_params[6:8].reshape(2 * D), tp_rank * qv_width, qv_width
    ).reshape(heads_here, 2, HD)
    bias_heads = jnp.stack(
        [qv_here[:, 0], jnp.zeros((heads_here, HD), jnp.float32), qv_here[:, 1]], 0
    )[:, :, None, :]
    bias_in = lax.dynamic_slice_in_dim(vec_params[8:].reshape(FF), tp_rank * ff_here, ff_here)
    normed_one, unit_one, inverse_one = norm_rows(tokens, gain_one, shift_one)
    rows_one = lax.all_gather(normed_one.astype(jnp.bfloat16), "tp", axis=0, tiled=True)
    projected = (
        jnp.einsum("rx,xhcd->chrd", rows_one, w_qkv_heads, preferred_element_type=jnp.float32)
        + bias_heads
    ).astype(jnp.bfloat16)
    queries = projected[0]
    keys_all = projected[1]
    values_all = projected[2]
    span = min(512, group_rows)
    starts = jnp.arange(group_rows // span, dtype=jnp.int32) * span
    key_ids = jnp.arange(group_rows, dtype=jnp.int32)
    score_scale = HD ** (-0.5)

    def masked_scores(first_row):
        row_ids = first_row + jnp.arange(span, dtype=jnp.int32)
        row_segs = lax.dynamic_slice_in_dim(segments, first_row, span, 0)
        allowed = allowed_mask(row_ids, row_segs, segments, key_ids, article_count)
        query_rows = lax.dynamic_slice_in_dim(queries, first_row, span, 1)
        scores = (
            jnp.einsum("hqd,hkd->hqk", query_rows, keys_all, preferred_element_type=jnp.float32)
            * score_scale
        )
        return (jnp.where(allowed[None], scores, NEG), query_rows)

    def attend(context_buf, first_row):
        scores, query_rows = masked_scores(first_row)
        row_max = jnp.max(scores, -1, keepdims=True)
        expo = jnp.exp(scores - row_max)
        expsum = jnp.sum(expo, -1, keepdims=True)
        probs_low = (expo / expsum).astype(jnp.bfloat16)
        context = jnp.einsum(
            "hqk,hkd->hqd", probs_low, values_all, preferred_element_type=jnp.float32
        ).astype(jnp.bfloat16)
        context_buf = lax.dynamic_update_slice_in_dim(context_buf, context, first_row, 1)
        return (context_buf, (row_max + jnp.log(expsum))[:, :, 0])

    context_low, log_norm = lax.scan(
        attend, jnp.zeros((heads_here, group_rows, HD), jnp.bfloat16), starts
    )
    attn_sum = lax.psum_scatter(
        jnp.einsum(
            "hrd,hde->re", context_low, w_out_heads, preferred_element_type=jnp.float32
        ).astype(jnp.bfloat16),
        "tp",
        scatter_dimension=0,
        tiled=True,
    ).astype(jnp.float32)
    hidden = tokens + attn_sum + bias_out
    normed_two, unit_two, inverse_two = norm_rows(hidden, gain_two, shift_two)
    rows_two = lax.all_gather(normed_two.astype(jnp.bfloat16), "tp", axis=0, tiled=True)
    inner = jnp.dot(rows_two, w_in, preferred_element_type=jnp.float32) + bias_in
    activ, gelu_pull = jax.vjp(jax.nn.gelu, inner)
    activ_low = activ.astype(jnp.bfloat16)
    mixed = (
        hidden
        + lax.psum_scatter(
            jnp.dot(activ_low, w_down, preferred_element_type=jnp.float32).astype(jnp.bfloat16),
            "tp",
            scatter_dimension=0,
            tiled=True,
        ).astype(jnp.float32)
        + bias_down
    )
    grad_low = cotangent.astype(jnp.bfloat16)
    grad_rows = lax.all_gather(grad_low, "tp", axis=0, tiled=True)
    g_down = jnp.einsum("rf,rd->fd", activ_low, grad_rows, preferred_element_type=jnp.float32)
    grad_activ = jnp.einsum("rd,fd->rf", grad_rows, w_down, preferred_element_type=jnp.float32)
    grad_inner = gelu_pull(grad_activ)[0].astype(jnp.bfloat16)
    g_in = jnp.einsum("rd,rf->df", rows_two, grad_inner, preferred_element_type=jnp.float32)
    g_bias_in = jnp.sum(grad_inner.astype(jnp.float32), 0)
    ffn_blocks = jnp.concatenate(
        [
            to_columns(g_in).reshape(groups, in_count, BLOCK, BLOCK),
            to_rows(g_down).reshape(groups, in_count, BLOCK, BLOCK),
        ],
        1,
    )
    grad_normed_two = lax.psum_scatter(
        jnp.einsum("rf,df->rd", grad_inner, w_in, preferred_element_type=jnp.float32).astype(
            jnp.bfloat16
        ),
        "tp",
        scatter_dimension=0,
        tiled=True,
    ).astype(jnp.float32)
    grad_hidden = cotangent + norm_back(grad_normed_two, unit_two, inverse_two, gain_two)
    grad_attn_low = grad_hidden.astype(jnp.bfloat16)
    grad_attn_rows = lax.all_gather(grad_attn_low, "tp", axis=0, tiled=True)
    g_out = jnp.einsum(
        "hrd,re->hde", context_low, grad_attn_rows, preferred_element_type=jnp.float32
    ).reshape(feat_here, D)
    grad_context = jnp.einsum(
        "re,hde->hrd", grad_attn_rows, w_out_heads, preferred_element_type=jnp.float32
    ).astype(jnp.bfloat16)
    zero_heads = jnp.zeros((heads_here, group_rows, HD), jnp.float32)

    def attend_back(carry, inputs):
        grad_queries, grad_keys, grad_values = carry
        first_row, log_block = inputs
        scores, query_rows = masked_scores(first_row)
        probs = jnp.exp(scores - log_block[:, :, None])
        grad_ctx_rows = lax.dynamic_slice_in_dim(grad_context, first_row, span, 1)
        grad_probs = jnp.einsum(
            "hqd,hkd->hqk", grad_ctx_rows, values_all, preferred_element_type=jnp.float32
        )
        delta = jnp.sum(probs * grad_probs, -1, keepdims=True)
        grad_scores = (probs * (grad_probs - delta)).astype(jnp.bfloat16)
        query_part = (
            jnp.einsum("hqk,hkd->hqd", grad_scores, keys_all, preferred_element_type=jnp.float32)
            * score_scale
        )
        grad_queries = lax.dynamic_update_slice_in_dim(grad_queries, query_part, first_row, 1)
        grad_keys = (
            grad_keys
            + jnp.einsum(
                "hqk,hqd->hkd", grad_scores, query_rows, preferred_element_type=jnp.float32
            )
            * score_scale
        )
        grad_values = grad_values + jnp.einsum(
            "hqk,hqd->hkd",
            probs.astype(jnp.bfloat16),
            grad_ctx_rows,
            preferred_element_type=jnp.float32,
        )
        return ((grad_queries, grad_keys, grad_values), None)

    (grad_queries, grad_keys, grad_values), unused = lax.scan(
        attend_back, (zero_heads, zero_heads, zero_heads), (starts, log_norm)
    )
    grad_proj = jnp.stack([grad_queries, grad_keys, grad_values], 0).astype(jnp.bfloat16)
    proj_sums = jnp.sum(grad_proj.astype(jnp.float32), 2)
    g_bias_qv = jnp.stack([proj_sums[0], proj_sums[2]], 1).reshape(qv_width)
    g_qkv = jnp.einsum(
        "rx,chrd->xhcd", rows_one, grad_proj, preferred_element_type=jnp.float32
    ).reshape(D, qkv_cols)
    grad_normed_one = lax.psum_scatter(
        jnp.einsum(
            "chrd,xhcd->rx", grad_proj, w_qkv_heads, preferred_element_type=jnp.float32
        ).astype(jnp.bfloat16),
        "tp",
        scatter_dimension=0,
        tiled=True,
    ).astype(jnp.float32)
    input_grad = grad_hidden + norm_back(grad_normed_one, unit_one, inverse_one, gain_one)
    local_rows = jnp.stack(
        [
            jnp.sum(grad_normed_one * unit_one, 0),
            jnp.sum(grad_normed_one, 0),
            jnp.sum(grad_normed_two * unit_two, 0),
            jnp.sum(grad_normed_two, 0),
            jnp.sum(grad_hidden, 0),
            jnp.sum(cotangent, 0),
        ]
    )
    qv_rows = lax.dynamic_update_slice(
        jnp.zeros((2 * D,), jnp.float32), g_bias_qv, (tp_rank * qv_width,)
    ).reshape(2, D)
    in_rows = lax.dynamic_update_slice(
        jnp.zeros((FF,), jnp.float32), g_bias_in, (tp_rank * ff_here,)
    ).reshape(FF // D, D)
    vec_grads = lax.psum(jnp.concatenate([local_rows, qv_rows, in_rows], 0), ("grp", "tp"))
    attn_blocks = jnp.concatenate(
        [
            to_columns(g_qkv).reshape(groups, qkv_count, BLOCK, BLOCK),
            to_rows(g_out).reshape(groups, out_count, BLOCK, BLOCK),
        ],
        1,
    )
    every_block = jnp.concatenate([attn_blocks, ffn_blocks], 1).reshape(-1, BLOCK, BLOCK)
    weight_grads = lax.psum_scatter(
        every_block.astype(jnp.bfloat16), "grp", scatter_dimension=0, tiled=True
    ).astype(jnp.float32)
    scaled = weight_grads * token_total ** (-0.5)
    stat_left_new = DECAY * stat_left + (1.0 - DECAY) * jnp.einsum(
        "nij,nkj->nik", scaled, scaled, precision=lax.Precision.HIGHEST
    )
    stat_right_new = DECAY * stat_right + (1.0 - DECAY) * jnp.einsum(
        "nji,njk->nik", scaled, scaled, precision=lax.Precision.HIGHEST
    )
    shaped = jnp.einsum("nij,njk->nik", root_left, scaled, precision=lax.Precision.HIGHEST)
    shaped = jnp.einsum("nij,njk->nik", shaped, root_right, precision=lax.Precision.HIGHEST)
    momentum_new = BETA * momentum + shaped
    weights_new = weights - RATE * momentum_new
    vec_scaled = vec_grads * token_total ** (-0.5)
    vec_second_new = VEC_DECAY * vec_second + (1.0 - VEC_DECAY) * vec_scaled * vec_scaled
    vec_momentum_new = BETA * vec_momentum + vec_scaled * lax.rsqrt(vec_second_new + VEC_EPS)
    vec_new = vec_params - VEC_RATE * vec_momentum_new
    return (
        mixed,
        input_grad,
        weight_grads,
        stat_left_new,
        stat_right_new,
        momentum_new,
        weights_new,
        vec_grads,
        vec_second_new,
        vec_momentum_new,
        vec_new,
    )


MESH_ID = pl.DeviceIdType.MESH
LANES = 128
HALF = 64
VMEM_LIMIT = 62 * 2**20
ARTICLES = 4
GELU_A = (2.0 / 3.141592653589793) ** 0.5
GELU_B = 0.044715


def remote(src, dst, send_sem, recv_sem, device):
    return pltpu.make_async_remote_copy(
        src_ref=src,
        dst_ref=dst,
        send_sem=send_sem,
        recv_sem=recv_sem,
        device_id=device,
        device_id_type=MESH_ID,
    )


def place():
    grp = lax.axis_index("grp")
    return lax.div(grp, 4), lax.rem(lax.div(grp, 2), 2), lax.rem(grp, 2), lax.axis_index("tp")


def slot_of(z, y, c):
    return z * 4 + y * 2 + c


def lay_blocks(view_ref, stack):
    half = view_ref.shape[2] // 2

    def row(i, carry):
        tile = view_ref[i].T
        stack[pl.ds(i, half, stride=BLOCK), :] = jnp.concatenate([tile[:half], tile[half:]], 1)
        return carry

    lax.fori_loop(0, BLOCK, row, 0, unroll=8)


def piece_shapes():
    return ((768, LANES), (64, 512), (1024, LANES), (LANES, 1024))


def fold_tiles(value, mask):
    kept = jnp.where(mask, value, 0.0)
    halves = kept[:, :LANES] + kept[:, LANES:]
    return halves + pltpu.roll(halves, HALF, 1)


def update_kernel(
    scale,
    sum_q,
    sum_o,
    sum_i,
    sum_d,
    root_l,
    root_r,
    vec_g,
    vecs,
    vec_m,
    vec_s,
    mixed,
    input_grad,
    w,
    m,
    sl,
    sr,
    out_g,
    out_sl,
    out_sr,
    out_m,
    out_w,
    out_vg,
    out_vs,
    out_vm,
    out_v,
    out_mixed,
    out_input_grad,
    first,
    second,
):
    count = root_l.shape[2]
    bf = jnp.bfloat16
    out_mixed[...] = mixed[...]
    out_input_grad[...] = input_grad[...]

    @pl.when(pl.program_id(0) == 0)
    def _():
        total = vec_g[...]
        out_vg[...] = total
        scaled = total * scale
        fresh = VEC_DECAY * vec_s[...] + (1.0 - VEC_DECAY) * scaled * scaled
        out_vs[...] = fresh
        momentum = BETA * vec_m[...] + scaled * lax.rsqrt(fresh + VEC_EPS)
        out_vm[...] = momentum
        out_v[...] = vecs[...] - VEC_RATE * momentum
        rows = sum_q.shape[0]
        first[0:rows, 0:HALF] = sum_q[:, 0:HALF]
        first[rows : 2 * rows, 0:HALF] = sum_q[:, HALF:LANES]
        base = 2 * rows
        for b in range(8):
            first[base + b * 64 : base + b * 64 + 64, 0:HALF] = sum_o[:, b * HALF : (b + 1) * HALF]
        base += 512
        first[base : base + 1024, 0:HALF] = sum_i[:, 0:HALF]
        first[base + 1024 : base + 2048, 0:HALF] = sum_i[:, HALF:LANES]
        base += 2048
        for r in range(2):
            for b in range(16):
                at = base + (r * 16 + b) * 64
                first[at : at + 64, 0:HALF] = sum_d[r * 64 : r * 64 + 64, b * HALF : (b + 1) * HALF]

        def row(i, carry):
            both = jnp.concatenate([root_l[i], root_r[i]], 0)
            second[pl.ds(i, count, stride=BLOCK), :] = both.T
            return carry

        lax.fori_loop(0, BLOCK, row, 0, unroll=8)
        row_id = lax.broadcasted_iota(jnp.int32, (256, 256), 0)
        col_id = lax.broadcasted_iota(jnp.int32, (256, 256), 1)
        mask = lax.shift_right_logical(row_id, 6) == lax.shift_right_logical(col_id, 6)
        zero = jnp.zeros((256, 256), jnp.float32)

        def spread(v):
            return jnp.where(mask, jnp.concatenate([v, v, v, v], 1), zero).astype(bf)

        def four(k, carry):
            at = pl.ds(pl.multiple_of(k * 256, 256), 256)
            s32 = first[at, 0:HALF] * scale
            s = s32.astype(bf)
            left = second[at, 0:HALF]
            right = second[at, HALF:LANES].astype(bf)
            outer = lax.dot_general(s, s, (((1,), (1,)), ((), ())), preferred_element_type=jnp.float32)
            inner = lax.dot_general(spread(s32), s, (((0,), (0,)), ((), ())), preferred_element_type=jnp.float32)
            shaped = jnp.dot(spread(left), s, preferred_element_type=jnp.float32)
            shaped = jnp.dot(spread(shaped), right, preferred_element_type=jnp.float32)
            first[at, HALF:LANES] = fold_tiles(outer, mask)[:, HALF:LANES]
            second[at, 0:HALF] = inner
            second[at, HALF:LANES] = shaped
            return carry

        lax.fori_loop(0, count // 4, four, 0, unroll=4)

    i0 = pl.program_id(0) * w.shape[0]

    def rows_out(ii, carry):
        at = pl.ds(i0 + ii, count, stride=BLOCK)
        one = first[at, :].T
        two = second[at, :].T
        out_g[ii] = one[0:HALF]
        out_sl[ii] = DECAY * sl[ii] + (1.0 - DECAY) * one[HALF:LANES]
        out_sr[ii] = DECAY * sr[ii] + (1.0 - DECAY) * two[0:HALF]
        fresh = BETA * m[ii] + two[HALF:LANES]
        out_m[ii] = fresh
        out_w[ii] = w[ii] - RATE * fresh
        return carry

    lax.fori_loop(0, w.shape[0], rows_out, 0, unroll=True)


def update_blocks(sums, blocks, vec_grads, vecs, results, token_total):
    views = [jnp.transpose(a, (1, 2, 0)) for a in blocks]
    count = blocks[0].shape[0]
    rows = 8
    whole = pl.BlockSpec(memory_space=pltpu.VMEM)
    steps = BLOCK // rows
    some = pl.BlockSpec((results[0].shape[0] // steps, results[0].shape[1]), lambda i: (i, 0))
    part = pl.BlockSpec((rows, BLOCK, count), lambda i: (i, 0, 0))
    vec = jax.ShapeDtypeStruct(vec_grads.shape, jnp.float32)
    outs = pl.pallas_call(
        functools.partial(update_kernel, token_total ** (-0.5)),
        grid=(steps,),
        out_shape=[jax.ShapeDtypeStruct((BLOCK, BLOCK, count), jnp.float32)] * 5
        + [vec] * 4
        + [jax.ShapeDtypeStruct(a.shape, a.dtype) for a in results],
        in_specs=[whole] * 10 + [some] * 2 + [part] * 4,
        out_specs=[part] * 5 + [whole] * 4 + [some] * 2,
        scratch_shapes=[
            pltpu.VMEM((count * BLOCK, LANES), jnp.float32),
            pltpu.VMEM((count * BLOCK, LANES), jnp.float32),
        ],
        compiler_params=pltpu.CompilerParams(vmem_limit_bytes=VMEM_LIMIT),
        name="update_blocks",
    )(*sums, *views[4:], vec_grads, *vecs, *results, *views[:4])
    return [jnp.transpose(a, (2, 0, 1)) for a in outs[:5]], outs[5:9], outs[9:]


DEPTH = 4


def layer_kernel(
    lengths,
    order,
    view,
    tokens,
    cot,
    vecs,
    mixed,
    input_grad,
    sum_q,
    sum_o,
    sum_i,
    sum_d,
    vec_grads,
    gq,
    go,
    gi,
    gd,
    wqkv,
    cq,
    co,
    ci,
    cd,
    yq,
    yo,
    yi,
    yd,
    yv,
    zq,
    zo,
    zi,
    zd,
    zv,
    rows_one,
    rows_two,
    rows_t,
    grad_rows,
    grad_attn,
    probs,
    qkv,
    ctx,
    gctx,
    far,
    inx,
    go_x,
    ctx_x,
    macc,
    nacc,
    act,
    gin,
    bias_sum,
    qkv_bias,
    vin,
    vout,
    recv,
    send_y,
    send_c,
    send_z,
    rc_recv,
    rc_send,
    ry_recv,
    ry_send,
    rz_recv,
    rz_send,
    x_send,
    x_recv,
    v_send,
    v_recv,
    copy_sem,
):
    bf, f32 = jnp.bfloat16, jnp.float32
    z, y, c, t = place()
    me = slot_of(z, y, c)
    x_peer = (me, 1 - t)
    y_peer = (slot_of(z, 1 - y, c), t)
    c_peer = (slot_of(z, y, 1 - c), t)
    rows = tokens.shape[0]
    own = pl.ds(pl.multiple_of(t * rows, rows), rows)
    other = pl.ds(pl.multiple_of((1 - t) * rows, rows), rows)

    def lanes(start, size, unit):
        return pl.ds(pl.multiple_of(start, unit), size)

    gathered, core_in = (gq, go, gi, gd), (cq, co, ci, cd)
    y_in, z_in = (yq, yo, yi, yd, yv), (zq, zo, zi, zd, zv)
    sums = (sum_q, sum_o, sum_i, sum_d)
    Q, O, I, W, V = range(5)

    def dot(a, b):
        return jnp.dot(a, b, preferred_element_type=f32)

    def dot_nt(a, b):
        return lax.dot_general(a, b, (((1,), (1,)), ((), ())), preferred_element_type=f32)

    def dot_tn(a, b):
        return lax.dot_general(a, b, (((0,), (0,)), ((), ())), preferred_element_type=f32)

    def piece(k, zz, yy, cc):
        if k == O:
            return go.at[zz * 2 + yy, :, pl.ds(pl.multiple_of(cc * 512, 512), 512)]
        return gathered[k].at[slot_of(zz, yy, cc)]

    def near(s):
        return lax.rem(z + (1 - 2 * lax.div(z, 2)) * s + DEPTH, DEPTH)

    def ag_piece(k, zz, yy, cc):
        if k == W:
            return gd.at[slot_of(zz, yy, cc), 0:HALF]
        if k == V:
            return gd.at[slot_of(zz, yy, cc), HALF:LANES]
        return piece(k, zz, yy, cc)

    def ag_copy(k, zz, yy, way):
        src = ag_piece(k, zz, yy, c)
        sem = recv.at[k, slot_of(zz, yy, c)]
        if way == "up":
            return remote(src, src, send_z.at[k, 0, yy * DEPTH + zz], sem, (slot_of(z + 1, y, c), t))
        if way == "down":
            return remote(src, src, send_z.at[k, 1, yy * DEPTH + zz], sem, (slot_of(z - 1, y, c), t))
        if way == "y":
            return remote(src, src, send_y.at[k, zz], sem, y_peer)
        return remote(src, src, send_c.at[k, yy * DEPTH + zz], sem, c_peer)

    def ag_wait(k, zz, yy, cc):
        ref = ag_piece(k, zz, yy, cc)
        remote(ref, ref, send_y.at[k, 0], recv.at[k, slot_of(zz, yy, cc)], y_peer).wait_recv()

    def own_sends_z(k):
        @pl.when(z < DEPTH - 1)
        def _():
            ag_copy(k, z, y, "up").start()

        @pl.when(z > 0)
        def _():
            ag_copy(k, z, y, "down").start()

        ag_copy(k, z, y, "core").start()

    def own_sends_y(k):
        ag_copy(k, z, y, "y").start()

    def z_arrival(kinds, dist):
        @pl.when(z >= dist)
        def _():
            for k in kinds:
                ag_wait(k, z - dist, y, c)

                @pl.when(z < DEPTH - 1)
                def _():
                    ag_copy(k, z - dist, y, "up").start()

                ag_copy(k, z - dist, y, "y").start()
                ag_copy(k, z - dist, y, "core").start()

        @pl.when(z + dist < DEPTH)
        def _():
            for k in kinds:
                ag_wait(k, z + dist, y, c)

                @pl.when(z > 0)
                def _():
                    ag_copy(k, z + dist, y, "down").start()

                ag_copy(k, z + dist, y, "y").start()
                ag_copy(k, z + dist, y, "core").start()

    def y_arrival(kinds, dist):
        def one(zz):
            for k in kinds:
                ag_wait(k, zz, 1 - y, c)
                ag_copy(k, zz, 1 - y, "core").start()

        if dist == 0:
            one(z)
            return

        @pl.when(z >= dist)
        def _():
            one(z - dist)

        @pl.when(z + dist < DEPTH)
        def _():
            one(z + dist)

    def v_forward(zz, yy):
        ag_wait(V, zz, yy, c)

        @pl.when((zz <= z) & (z < DEPTH - 1))
        def _():
            ag_copy(V, zz, yy, "up").start()

        @pl.when((zz >= z) & (z > 0))
        def _():
            ag_copy(V, zz, yy, "down").start()

        ag_copy(V, zz, yy, "core").start()

    def v_arrival(dist):
        for yy in (y, 1 - y):

            @pl.when(z >= dist)
            def _():
                v_forward(z - dist, yy)

            @pl.when(z + dist < DEPTH)
            def _():
                v_forward(z + dist, yy)

    def drain(k, zz, yy):
        ag_copy(k, zz, yy, "core").wait_send()
        if k == V:

            @pl.when((yy == y) & (zz == z))
            def _():
                ag_copy(k, zz, yy, "y").wait_send()

            @pl.when((zz <= z) & (z < DEPTH - 1))
            def _():
                ag_copy(k, zz, yy, "up").wait_send()

            @pl.when((zz >= z) & (z > 0))
            def _():
                ag_copy(k, zz, yy, "down").wait_send()

            return

        @pl.when(yy == y)
        def _():
            ag_copy(k, zz, y, "y").wait_send()

            @pl.when((zz <= z) & (z < DEPTH - 1))
            def _():
                ag_copy(k, zz, y, "up").wait_send()

            @pl.when((zz >= z) & (z > 0))
            def _():
                ag_copy(k, zz, y, "down").wait_send()

    def add(dst, *terms):
        count, width = dst.shape
        step = min(count, 256 * LANES // width)

        def body(i, carry):
            at = pl.ds(pl.multiple_of(i * step, 16), step)
            total = terms[0][at, :].astype(f32)
            for term in terms[1:]:
                total = total + term[at, :].astype(f32)
            dst[at, :] = total.astype(dst.dtype)
            return carry

        lax.fori_loop(0, count // step, body, 0)

    side = lax.div(z, 2)
    end_z, inner_z = 3 * side, 1 + side
    is_end = z == end_z

    def rc_copy(k, zz, yy):
        at = zz * 2 + yy
        return remote(piece(k, zz, yy, 1 - c), core_in[k].at[at], rc_send.at[k, at], rc_recv.at[k, at], c_peer)

    def ry_copy(k, zz):
        if k == V:
            return remote(ag_piece(V, z, 1 - y, c), y_in[V].at[0], ry_send.at[V, 0], ry_recv.at[V, 0], y_peer)
        return remote(ag_piece(k, zz, 1 - y, c), y_in[k].at[zz], ry_send.at[k, zz], ry_recv.at[k, zz], y_peer)

    def z_slot(k, slot, yy):
        return z_in[k].at[slot * 2 + yy if k == V else slot]

    def z_sem(slot, yy):
        return slot * 2 + yy

    def rz_copy(k, s, yy, from_end):
        slot = s - 1 if from_end else {3: 0, 2: 1, 1: 3}[s]
        to = inner_z if from_end else {3: end_z, 2: 3 - end_z, 1: 3 - inner_z}[s]
        sent, landed = rz_send.at[k, (s - 1) * 2 + yy], rz_recv.at[k, z_sem(slot, yy)]
        return remote(ag_piece(k, near(s), yy, c), z_slot(k, slot, yy), sent, landed, (slot_of(to, y, c), t))

    def z_landed(k, slot, yy):
        ref = z_slot(k, slot, yy)
        remote(ref, ref, rz_send.at[k, 0], rz_recv.at[k, z_sem(slot, yy)], y_peer).wait_recv()
        return ref

    def y_landed(k, zz):
        ref = y_in[k].at[0 if k == V else zz]
        remote(ref, ref, ry_send.at[k, 0], ry_recv.at[k, 0 if k == V else zz], y_peer).wait_recv()
        return ref

    def rc_add(k, zz, yy):
        at = zz * 2 + yy
        remote(core_in[k].at[at], core_in[k].at[at], rc_send.at[k, 0], rc_recv.at[k, at], c_peer).wait_recv()
        mine = piece(k, zz, yy, c)
        add(mine, mine, core_in[k].at[at])

        @pl.when(yy != y)
        def _():
            ry_copy(k, zz).start()

    def z_step(k, s, yy, *terms):
        mine = ag_piece(k, near(s), yy, c)
        if terms:
            add(mine, mine, *terms)

        @pl.when(is_end)
        def _():
            rz_copy(k, s, yy, True).start()

        if s == 3:

            @pl.when(jnp.logical_not(is_end))
            def _():
                rz_copy(k, s, yy, False).start()

    def z_merge(k, s, yy):
        @pl.when(jnp.logical_not(is_end))
        def _():
            mine = ag_piece(k, near(s), yy, c)
            add(mine, mine, z_landed(k, s, yy))
            rz_copy(k, s, yy, False).start()

    def ry_add(k, s):
        z_step(k, s, y, y_landed(k, near(s)))

    def ry_merge(k, s):
        z_merge(k, s, y)

    def total_of(k):
        return sum_d.at[(k - W) * HALF : (k - W + 1) * HALF] if k >= W else sums[k]

    def z_total(k, yy, dst, *terms):
        mine = ag_piece(k, z, yy, c)
        first = z_landed(k, 0, yy)

        @pl.when(is_end)
        def _():
            add(dst, mine, first, z_landed(k, 1, yy), *terms)

        @pl.when(jnp.logical_not(is_end))
        def _():
            add(dst, mine, first, z_landed(k, 3, yy), *terms)

    def own_total(k):
        z_total(k, y, total_of(k), y_landed(k, z))

    def v_cross():
        mine = ag_piece(V, z, 1 - y, c)
        z_total(V, 1 - y, mine)
        ry_copy(V, z).start()

    def x_rows(ref, index):
        return remote(ref.at[own], ref.at[own], x_send.at[index], x_recv.at[index], x_peer)

    def x_rows_wait(ref, index):
        remote(ref.at[other], ref.at[other], x_send.at[index], x_recv.at[index], x_peer).wait_recv()

    def x_part(index):
        return remote(far.at[index - 1 & 1], inx.at[index - 1 & 1], x_send.at[4 + index], x_recv.at[4 + index], x_peer)

    def by_rows(body, step=64):
        def run(i, carry):
            body(pl.multiple_of(i * step, step), step)
            return carry

        lax.fori_loop(0, rows // step, run, 0)

    def norm(value):
        average = jnp.mean(value, -1, keepdims=True)
        centred = value - average
        inverse = lax.rsqrt(jnp.mean(centred * centred, -1, keepdims=True) + EPS)
        return centred * inverse, inverse

    def norm_grad(grad, unit, inverse, gain):
        scaled = grad * gain
        return inverse * (
            scaled - jnp.mean(scaled, -1, keepdims=True) - unit * jnp.mean(scaled * unit, -1, keepdims=True)
        )

    def x_out():
        half = (slice(None), slice(None), lanes(c * 512, 512, 512))
        return remote(go.at[half], go_x.at[half], x_send.at[4], x_recv.at[4], x_peer)

    def x_out_core(cc):
        half = (slice(None), slice(None), lanes(cc * 512, 512, 512))
        return remote(go_x.at[half], go_x.at[half], x_send.at[8], x_recv.at[8], c_peer)

    def x_context(h):
        src = ctx.at[other, lanes(h * HD, HD, HD)]
        return remote(src, ctx_x.at[:, lanes(h * HD, HD, HD)], x_send.at[9 + h], x_recv.at[9 + h], x_peer)

    def x_grad_context():
        return remote(ctx_x, gctx.at[own], x_send.at[13], x_recv.at[13], x_peer)

    def x_grad_context_wait():
        remote(gctx.at[other], gctx.at[other], x_send.at[13], x_recv.at[13], x_peer).wait_recv()

    barrier = pltpu.get_barrier_semaphore()
    z_peers = [(slot_of(lax.rem(z + step, DEPTH), y, c), t) for step in range(1, DEPTH)]
    everyone = [x_peer, y_peer, c_peer] + z_peers
    for device in everyone:
        pl.semaphore_signal(barrier, inc=1, device_id=device, device_id_type=MESH_ID)

    def prepare(held, stack):
        load = pltpu.make_async_copy(view, held, copy_sem.at[0])
        load.start()

        def first_norm(at, step):
            unit, inverse = norm(tokens[pl.ds(at, step), :])
            to = pl.ds(pl.multiple_of(t * rows + at, step), step)
            rows_one[to, :] = (unit * vecs[0:1, :] + vecs[1:2, :]).astype(bf)
            grad_rows[to, :] = cot[pl.ds(at, step), :].astype(bf)

        load.wait()
        lay_blocks(held, stack)

        def pair(left, right, count, left_high=False, right_high=False):
            first, second = stack[left : left + count, :], stack[right : right + count, :]
            first = pltpu.roll(first, HALF, 1) if left_high else first
            second = second if right_high else pltpu.roll(second, HALF, 1)
            lane = lax.broadcasted_iota(jnp.int32, (count, LANES), 1)
            return jnp.where(lane < HALF, first, second).astype(bf)

        n = gq.shape[1]
        gq[me] = pair(0, n, n)
        base = 2 * n
        wide = [pair(base + b * 64, base + b * 64 + 64, 64) for b in range(0, 8, 2)]
        go[z * 2 + y, :, lanes(c * 512, 512, 512)] = jnp.concatenate(wide, 1)
        pl.semaphore_wait(barrier, len(everyone))
        for k in (O, Q):
            own_sends_y(k)
            own_sends_z(k)
        by_rows(first_norm)
        x_rows(rows_one, 0).start()
        base += 512
        gi[me] = pair(base, 0, D, right_high=True)
        for r in range(2):
            for b in range(0, 16, 2):
                at = D + (r * 16 + b) * 64
                gd[me, r * 64 : r * 64 + 64, b * HALF : b * HALF + LANES] = pair(at, at + 64, 64, True, True)

    pl.run_scoped(
        prepare,
        pltpu.VMEM(view.shape, f32),
        pltpu.VMEM((view.shape[2] // 2 * BLOCK, LANES), f32),
    )
    z_arrival((O, Q), 1)
    y_arrival((O, Q), 0)
    for k in (I, W, V):
        own_sends_z(k)
    z_arrival((O, Q), 2)
    own_sends_y(I)
    y_arrival((O, Q), 1)
    z_arrival((O, Q), 3)
    y_arrival((O,), 2)
    y_arrival((O,), 3)
    x_out().start()
    x_rows(grad_rows, 1).start()
    own_sends_y(W)
    own_sends_y(V)

    def core_waits(kinds, zz):
        for k in kinds:
            for yy in (y, 1 - y):
                ag_wait(k, zz, yy, 1 - c)

    x_rows_wait(rows_one, 0)

    ends = []
    for p in range(ARTICLES):
        length = 0
        for a in range(ARTICLES):
            length = length + jnp.where(order[0, p] == a, lengths[0, a], 0)
        ends.append(length + ends[-1] if p else length)

    def allowed(first, count):
        ids = lax.broadcasted_iota(jnp.int32, (rows, 1), 0) + first
        start = jnp.zeros((rows, 1), jnp.int32)
        for end in ends:
            start = jnp.where(ids >= end, end, start)
        start = jnp.where(ids >= ends[-1], ids, start)
        keys = lax.broadcasted_iota(jnp.int32, (rows, count), 1)
        return (keys <= ids) & (keys >= start)

    scale = HD ** (-0.5)
    strip = 1024

    def assemble(h):
        for yy in range(2):
            even, odd = gq.at[slot_of(h, yy, 0)], gq.at[slot_of(h, yy, 1)]
            at = yy * 192
            wqkv[h, 0:768, at : at + 64] = even[:, 0:64]
            wqkv[h, 768:1024, at : at + 64] = even[0:256, 64:128]
            wqkv[h, 0:512, at + 64 : at + 128] = even[256:768, 64:128]
            wqkv[h, 512:1024, at + 64 : at + 128] = odd[0:512, 0:64]
            wqkv[h, 0:256, at + 128 : at + 192] = odd[512:768, 0:64]
            wqkv[h, 256:1024, at + 128 : at + 192] = odd[:, 64:128]

    def disassemble(h, value):
        for yy in range(2):
            even, odd = gq.at[slot_of(h, yy, 0)], gq.at[slot_of(h, yy, 1)]
            at = yy * 192
            even[:, 0:64] = value[0:768, at : at + 64]
            even[0:256, 64:128] = value[768:1024, at : at + 64]
            even[256:768, 64:128] = value[0:512, at + 64 : at + 128]
            odd[0:512, 0:64] = value[512:1024, at + 64 : at + 128]
            odd[512:768, 0:64] = value[0:256, at + 128 : at + 192]
            odd[:, 64:128] = value[256:1024, at + 128 : at + 192]

    qv = vecs[pl.ds(6 + t, 1), :]
    for h in range(DEPTH):
        none = jnp.zeros((1, HD), f32)
        qkv_bias[h] = jnp.concatenate([qv[:, h * 256 : h * 256 + 128], none, qv[:, h * 256 + 128 : h * 256 + 256]], 1)

    def head(h):
        core_waits((Q,), h)
        assemble(h)
        qkv[h] = (dot(rows_one[...], wqkv[h]) + qkv_bias[h]).astype(bf)
        for block in range(2):
            at, seen = slice(block * rows, (block + 1) * rows), (block + 1) * rows
            scores = dot_nt(qkv[h, at, 0:128], qkv[h, 0:seen, 128:256]) * scale
            scores = jnp.where(allowed(block * rows, seen), scores, NEG)
            expo = jnp.exp(scores - jnp.max(scores, -1, keepdims=True))
            low = (expo / jnp.sum(expo, -1, keepdims=True)).astype(bf)
            probs[h, at, 0:seen] = low
            ctx[at, lanes(h * HD, HD, HD)] = dot(low, qkv[h, 0:seen, 256:384]).astype(bf)

    head(near(0))
    x_context(near(0)).start()
    y_arrival((Q,), 2)
    head(near(1))
    x_context(near(1)).start()
    y_arrival((Q,), 3)
    head(near(2))
    x_context(near(2)).start()
    z_arrival((I, W), 1)
    head(near(3))
    x_context(near(3)).start()
    y_arrival((I, W), 0)
    v_forward(z, 1 - y)
    for zz in range(DEPTH):
        core_waits((O,), zz)
    x_out().wait_recv()
    x_out_core(c).start()

    def w_out(ref):
        return ref[...].reshape(DEPTH * HD, D)

    mixed[...] = tokens[...] + dot(ctx[own, :], w_out(go)) + vecs[4:5, :]
    z_arrival((I, W), 2)
    v_arrival(1)
    y_arrival((I, W), 1)
    x_out_core(1 - c).wait_recv()
    for h in range(DEPTH):
        x_context(h).wait_recv()
    mixed[...] += dot(ctx_x[...], w_out(go_x))

    def second_norm(at, step):
        unit, inverse = norm(mixed[pl.ds(at, step), :])
        to = pl.ds(pl.multiple_of(t * rows + at, step), step)
        rows_two[to, :] = (unit * vecs[2:3, :] + vecs[3:4, :]).astype(bf)

    by_rows(second_norm)
    x_rows(rows_two, 2).start()
    z_arrival((I, W), 3)
    v_arrival(2)
    macc[...] = jnp.zeros_like(macc)
    nacc[...] = jnp.zeros_like(nacc)
    vout[...] = jnp.zeros_like(vout)
    x_rows_wait(grad_rows, 1)

    def ffn(half, zz):
        first = 4 * zz
        at = pl.ds(pl.multiple_of(lax.rem(t + half, 2) * rows, rows), rows)
        units = lanes(zz * 512, 512, 512)
        bias_row = vecs[pl.ds(8 + 2 * t + lax.div(zz, 2), 1), lanes(lax.rem(zz, 2) * 512, 512, 512)]

        def w_in(start, count):
            return jnp.concatenate([gi[first + j, start : start + count, :] for j in range(4)], 1)

        def w_down(start, count):
            return gd[pl.ds(first, 4), :, start : start + count].reshape(512, count)

        inner = dot(rows_two[at, :], w_in(0, D)) + bias_row
        square = inner * inner
        bent = jnp.tanh(GELU_A * inner * (1.0 + GELU_B * square))
        act[at, units] = (0.5 * inner * (1.0 + bent)).astype(bf)
        slope = 0.5 * (1.0 + bent) + 0.5 * inner * (1.0 - bent * bent) * (GELU_A * (1.0 + 3.0 * GELU_B * square))
        gin[at, units] = (dot_nt(grad_rows[at, :], w_down(0, D)) * slope).astype(bf)
        for nb in range(4):
            out = slice(nb * 256, nb * 256 + 256)
            nacc[at, out] += dot_nt(gin[at, units], w_in(nb * 256, 256))
            macc[at, out] += dot(act[at, units], w_down(nb * 256, 256))

    def ffn_grads(zz):
        first = 4 * zz
        units = lanes(zz * 512, 512, 512)
        for k in (I, W, V):
            for yy in range(2):
                drain(k, zz, yy)
        bias_sum[zz] = jnp.sum(gin[:, units].astype(f32), 0, keepdims=True)
        for nb in range(4):
            out = slice(nb * 256, nb * 256 + 256)
            part = dot(rows_t[out, :], gin[:, units]).astype(bf)
            for j in range(4):
                gi[first + j, out, :] = part[:, j * LANES : (j + 1) * LANES]
        for yy in (1 - y, y):
            rc_copy(I, zz, yy).start()
        act_t = act[:, units].T
        for nb in range(4):
            out = slice(nb * 256, nb * 256 + 256)
            part = dot(act_t, grad_rows[:, out]).astype(bf)
            gd[pl.ds(first, 4), :, out] = part.reshape(4, LANES, 256)
        for yy in (1 - y, y):
            rc_copy(W, zz, yy).start()

    def reduce_core(zz):
        for yy in (1 - y, y):
            for k in (I, W):
                rc_add(k, zz, yy)

    def v_step(s):
        for yy in (1 - y, y):
            z_step(V, s, yy)

    def v_merge(s):
        for yy in (1 - y, y):
            z_merge(V, s, yy)

    core_waits((I, W, V), z)
    ffn(0, z)
    y_arrival((I, W), 2)
    core_waits((I, W, V), near(1))
    ffn(0, near(1))
    x_rows_wait(rows_two, 2)
    rows_t[...] = rows_two[...].T

    def by_z(s, carry):
        @pl.when(s == 2)
        def _():
            v_arrival(3)
            y_arrival((I, W), 3)

        @pl.when(s >= 2)
        def _():
            core_waits((I, W, V), near(s))
            ffn(0, near(s))

        ffn(1, near(s))

        @pl.when(s == DEPTH - 1)
        def _():
            far[0] = nacc[other, :].astype(bf)
            x_part(1).start()
            far[1] = macc[other, :].astype(bf)
            x_part(2).start()

        @pl.when(s > 0)
        def _():
            reduce_core(near(s - 1))

        for before in (1, 2):

            @pl.when(s == before + 1)
            def _():
                v_step(before)

        ffn_grads(near(s))
        return carry

    lax.fori_loop(0, DEPTH, by_z, 0)
    reduce_core(near(3))
    v_step(3)
    v_merge(1)
    for zz in range(DEPTH):
        for side in range(2):
            row, start = 8 + 2 * side + zz // 2, zz % 2 * 512
            vout[0, row : row + 1, start : start + 512] = jnp.where(t == side, bias_sum[zz], 0.0)
    rows_t[...] = rows_one[...].T
    x_part(1).wait_recv()

    def row_sum(row, value):
        vout[0, row : row + 1, :] += jnp.sum(value, 0, keepdims=True)

    def second_back(at, step):
        here = pl.ds(at, step)
        in_group = pl.ds(pl.multiple_of(t * rows + at, step), step)
        grad = nacc[in_group, :] + inx[0, here, :].astype(f32)
        unit, inverse = norm(mixed[here, :])
        back = cot[here, :] + norm_grad(grad, unit, inverse, vecs[2:3, :])
        input_grad[here, :] = back
        grad_attn[in_group, :] = back.astype(bf)
        row_sum(2, grad * unit)
        row_sum(3, grad)
        row_sum(4, back)
        row_sum(5, cot[here, :])

    by_rows(second_back)
    ctx_x[...] = dot_nt(grad_attn[own, :], w_out(go_x)).astype(bf)
    x_grad_context().start()
    x_rows(grad_attn, 3).start()
    gctx[own, :] = dot_nt(grad_attn[own, :], w_out(go)).astype(bf)
    for k in (I, W):
        ry_add(k, 1)
    v_merge(2)
    v_cross()
    x_part(2).wait_recv()

    def mixed_out(at, step):
        here = pl.ds(at, step)
        in_group = pl.ds(pl.multiple_of(t * rows + at, step), step)
        mixed[here, :] = mixed[here, :] + macc[in_group, :] + inx[1, here, :].astype(f32) + vecs[5:6, :]

    by_rows(mixed_out)
    for zz in range(DEPTH):
        for yy in range(2):
            drain(O, zz, yy)
            drain(Q, zz, yy)
    x_out().wait_send()
    x_grad_context_wait()

    def out_grads():
        x_rows_wait(grad_attn, 3)
        ctx_t = ctx[...].T
        for nb in range(4):
            at = slice(nb * 256, nb * 256 + 256)
            go[:, :, at] = dot(ctx_t, grad_attn[:, at]).astype(bf).reshape(8, 64, 256)
        for zz in range(DEPTH):
            for yy in range(2):
                rc_copy(O, zz, yy).start()

    def head_back(h):
        q0, q1 = qkv[h, 0:rows, 0:128], qkv[h, rows : 2 * rows, 0:128]
        grads = []
        for block in range(2):
            at, seen = slice(block * rows, (block + 1) * rows), (block + 1) * rows
            low = probs[h, at, 0:seen]
            given = gctx[at, h * 128 : h * 128 + 128]
            prob = low.astype(f32)
            grad_probs = dot_nt(given, qkv[h, 0:seen, 256:384])
            delta = jnp.sum(prob * grad_probs, -1, keepdims=True)
            grad_scores = (prob * (grad_probs - delta)).astype(bf)
            grad_q = dot(grad_scores, qkv[h, 0:seen, 128:256]) * scale
            grad_k = dot_tn(grad_scores, q1 if block else q0) * scale
            grad_v = dot_tn(low, given)
            grads.append((grad_q, grad_k, grad_v))
        (gq0, gk0, gv0), (gq1, gk1, gv1) = grads
        top = jnp.concatenate([gq0, gk0 + gk1[0:rows], gv0 + gv1[0:rows]], 1).astype(bf)
        low_half = jnp.concatenate([gq1, gk1[rows:], gv1[rows:]], 1).astype(bf)
        qkv[h, 0:rows, :] = top
        qkv[h, rows : 2 * rows, :] = low_half
        total = jnp.sum(top.astype(f32), 0, keepdims=True) + jnp.sum(low_half.astype(f32), 0, keepdims=True)
        for side in range(2):
            vout[0, 6 + side : 7 + side, h * 256 : h * 256 + 128] = jnp.where(t == side, total[:, 0:128], 0.0)
            vout[0, 6 + side : 7 + side, h * 256 + 128 : h * 256 + 256] = jnp.where(t == side, total[:, 256:384], 0.0)
        product = dot_nt(qkv[h], wqkv[h])
        if h == 0:
            nacc[...] = product
        else:
            nacc[...] += product
        if h == DEPTH - 1:
            x_part(1).wait_send()
            far[0] = nacc[other, :].astype(bf)
            x_part(3).start()
        part = dot(rows_t[...], qkv[h]).astype(bf)
        disassemble(h, part)
        for yy in (1 - y, y):
            rc_copy(Q, h, yy).start()

    for h in range(DEPTH):
        head_back(h)
        if h > 0:
            for yy in (1 - y, y):
                rc_add(Q, h - 1, yy)
        if h == 0:
            out_grads()
        if h == 1:
            for yy in (1 - y, y):
                for s in range(DEPTH):
                    rc_add(O, near(s), yy)
            for k in (I, W):
                ry_add(k, 2)
                ry_merge(k, 1)
        if h == 2:
            for k in (I, W):
                ry_add(k, 3)
                ry_merge(k, 2)
    for yy in (1 - y, y):
        rc_add(Q, DEPTH - 1, yy)
    for k in (I, W):
        own_total(k)
    z_total(V, y, total_of(V), y_landed(V, z))
    x_part(3).wait_recv()

    def first_back(at, step):
        here = pl.ds(at, step)
        in_group = pl.ds(pl.multiple_of(t * rows + at, step), step)
        grad = nacc[in_group, :] + inx[0, here, :].astype(f32)
        unit, inverse = norm(tokens[here, :])
        input_grad[here, :] = input_grad[here, :] + norm_grad(grad, unit, inverse, vecs[0:1, :])
        row_sum(0, grad * unit)
        row_sum(1, grad)

    by_rows(first_back)

    stages = (x_peer, c_peer, y_peer)

    def v_copy(stage):
        return remote(vout.at[stage], vin.at[stage], v_send.at[stage], v_recv.at[stage], stages[stage])

    def vz_copy(step):
        peer = (slot_of(lax.rem(z + step, DEPTH), y, c), t)
        return remote(vout.at[3], vin.at[3 + z], v_send.at[2 + step], v_recv.at[3 + z], peer)

    v_copy(0).start()
    for s in (3, 2, 1):
        ry_add(O, s)
    ry_merge(O, 2)
    ry_merge(O, 1)
    v_copy(0).wait_recv()
    vout[1] = vout[0] + vin[0]
    v_copy(1).start()
    for s in (3, 2, 1):
        ry_add(Q, s)
    ry_merge(Q, 2)
    ry_merge(Q, 1)
    v_copy(1).wait_recv()
    vout[2] = vout[1] + vin[1]
    v_copy(2).start()
    own_total(O)
    v_copy(2).wait_recv()
    vout[3] = vout[2] + vin[2]
    for step in range(1, DEPTH):
        vz_copy(step).start()
    vin[3 + z] = vout[3]
    own_total(Q)
    for step in range(1, DEPTH):
        zz = lax.rem(z + step, DEPTH)
        remote(vin.at[3 + zz], vin.at[3 + zz], v_send.at[0], v_recv.at[3 + zz], y_peer).wait_recv()
    count = vec_grads.shape[0]
    total = ((vin[3] + vin[4]) + vin[5]) + vin[6]
    vec_grads[...] = total[0:count]

    for stage in range(3):
        v_copy(stage).wait_send()
    for step in range(1, DEPTH):
        vz_copy(step).wait_send()
    for index, ref in enumerate((rows_one, grad_rows, rows_two, grad_attn)):
        x_rows(ref, index).wait_send()
    for index in (2, 3):
        x_part(index).wait_send()
    x_out_core(c).wait_send()
    x_grad_context().wait_send()
    for h in range(DEPTH):
        x_context(h).wait_send()
    for k in range(4):
        for zz in range(DEPTH):
            for yy in range(2):
                rc_copy(k, zz, yy).wait_send()
            ry_copy(k, zz).wait_send()
        for s in range(1, DEPTH):
            rz_copy(k, s, y, True).wait_send()
    ry_copy(V, z).wait_send()
    for yy in range(2):
        for s in range(1, DEPTH):
            rz_copy(V, s, yy, True).wait_send()


def run_layer(tokens, cotangent, lengths, order, weights, vec_params):
    bf, f32 = jnp.bfloat16, jnp.float32
    rows = tokens.shape[0]
    group = 2 * rows
    owners = 16
    shapes = piece_shapes()
    view = jnp.transpose(weights, (1, 2, 0))
    vmem = pl.BlockSpec(memory_space=pltpu.VMEM)
    smem = pl.BlockSpec(memory_space=pltpu.SMEM)

    halved = shapes[:3] + ((HALF, D),)

    def many(count, kinds):
        return [pltpu.VMEM((count,) + s, bf) for s in kinds]

    full = pltpu.VMEM((group, D), bf)
    dma = pltpu.SemaphoreType.DMA
    return pl.pallas_call(
        layer_kernel,
        out_shape=[jax.ShapeDtypeStruct((rows, D), f32)] * 2
        + [jax.ShapeDtypeStruct(s, f32) for s in shapes]
        + [jax.ShapeDtypeStruct(vec_params.shape, f32)],
        in_specs=[smem, smem, pl.BlockSpec(memory_space=pl.ANY)] + [vmem] * 3,
        out_specs=[vmem] * 7,
        scratch_shapes=[
            pltpu.VMEM((owners,) + shapes[0], bf),
            pltpu.VMEM((owners // 2, BLOCK, D), bf),
            pltpu.VMEM((owners,) + shapes[2], bf),
            pltpu.VMEM((owners,) + shapes[3], bf),
            pltpu.VMEM((DEPTH, D, 3 * HD), bf),
        ]
        + many(2 * DEPTH, shapes)
        + many(DEPTH, halved)
        + many(1, halved[3:])
        + many(DEPTH, halved)
        + many(2 * DEPTH, halved[3:])
        + [
            full,
            full,
            pltpu.VMEM((D, group), bf),
            full,
            full,
            pltpu.VMEM((DEPTH, group, group), bf),
            pltpu.VMEM((DEPTH, group, 3 * HD), bf),
            pltpu.VMEM((group, DEPTH * HD), bf),
            pltpu.VMEM((group, DEPTH * HD), bf),
            pltpu.VMEM((2, rows, D), bf),
            pltpu.VMEM((2, rows, D), bf),
            pltpu.VMEM((owners // 2, BLOCK, D), bf),
            pltpu.VMEM((rows, DEPTH * HD), bf),
            pltpu.VMEM((group, D), f32),
            pltpu.VMEM((group, D), f32),
            pltpu.VMEM((group, 2 * D), bf),
            pltpu.VMEM((group, 2 * D), bf),
            pltpu.VMEM((DEPTH, 1, 512), f32),
            pltpu.VMEM((DEPTH, 1, 3 * HD), f32),
            pltpu.VMEM((7, 16, D), f32),
            pltpu.VMEM((4, 16, D), f32),
            dma((5, owners)),
            dma((5, DEPTH)),
            dma((5, 2 * DEPTH)),
            dma((5, 2, 2 * DEPTH)),
            dma((4, 2 * DEPTH)),
            dma((4, 2 * DEPTH)),
            dma((5, DEPTH)),
            dma((5, DEPTH)),
            dma((5, 2 * DEPTH)),
            dma((5, 2 * DEPTH)),
            dma((14,)),
            dma((14,)),
            dma((6,)),
            dma((7,)),
            dma((1,)),
        ],
        compiler_params=pltpu.CompilerParams(
            collective_id=0, has_side_effects=True, vmem_limit_bytes=VMEM_LIMIT
        ),
        name="layer",
    )(lengths, order, view, tokens, cotangent, vec_params)


def per_device(
    grp_count,
    tp_count,
    tokens,
    cotangent,
    lengths,
    order,
    weights,
    momentum,
    stat_left,
    stat_right,
    root_left,
    root_right,
    vec_params,
    vec_momentum,
    vec_second,
):
    fits = grp_count == 4 * DEPTH and tp_count == 2 and tokens.shape[0] == 256
    if not fits or lengths.shape[1] != ARTICLES:
        return per_device_general(
            tokens,
            cotangent,
            lengths,
            order,
            weights,
            momentum,
            stat_left,
            stat_right,
            root_left,
            root_right,
            vec_params,
            vec_momentum,
            vec_second,
        )
    token_total = tokens.shape[0] * tp_count * grp_count
    mixed, input_grad, *sums, vec_grads = run_layer(tokens, cotangent, lengths, order, weights, vec_params)
    blocks, vecs, results = update_blocks(
        sums,
        (weights, momentum, stat_left, stat_right, root_left, root_right),
        vec_grads,
        (vec_params, vec_momentum, vec_second),
        (mixed, input_grad),
        token_total,
    )
    return (*results, *blocks, *vecs)


def solution(mesh):
    placed = (
        P(("grp", "tp"), None),
        P(("grp", "tp"), None),
        P("grp", None),
        P("grp", None),
        P(("tp", "grp"), None, None),
        P(("tp", "grp"), None, None),
        P(("tp", "grp"), None, None),
        P(("tp", "grp"), None, None),
        P(("tp", "grp"), None, None),
        P(("tp", "grp"), None, None),
        P(),
        P(),
        P(),
    )
    return jax.shard_map(
        functools.partial(per_device, mesh.shape["grp"], mesh.shape["tp"]),
        mesh=mesh,
        in_specs=placed,
        out_specs=(
            P(("grp", "tp"), None),
            P(("grp", "tp"), None),
            P(("tp", "grp"), None, None),
            P(("tp", "grp"), None, None),
            P(("tp", "grp"), None, None),
            P(("tp", "grp"), None, None),
            P(("tp", "grp"), None, None),
            P(),
            P(),
            P(),
            P(),
        ),
        check_vma=False,
    )
```

```python
import functools

import jax
import jax.numpy as jnp
from jax import lax
from jax.experimental import pallas as pl
from jax.experimental.pallas import tpu as pltpu
from jax.sharding import PartitionSpec as P

D = 1024
HEADS = 8
HD = 128
FF = 4096
BLOCK = 64


EPS = 1e-05
NEG = -1e30
DECAY = 0.9
BETA = 0.9
RATE = 0.05
VEC_DECAY = 0.9
VEC_RATE = 0.2
VEC_EPS = 1e-08


def norm_rows(value, gain, shift):
    average = jnp.mean(value, -1, keepdims=True)
    centred = value - average
    inverse = lax.rsqrt(jnp.mean(centred * centred, -1, keepdims=True) + EPS)
    normed = centred * inverse
    return (normed * gain + shift, normed, inverse)


def norm_back(grad_out, normed, inverse, gain):
    scaled = grad_out * gain
    return inverse * (
        scaled
        - jnp.mean(scaled, -1, keepdims=True)
        - normed * jnp.mean(scaled * normed, -1, keepdims=True)
    )


def segment_ids(lengths_row, order_row, group_rows):
    article_count = lengths_row.shape[0]
    slots = jnp.arange(article_count, dtype=jnp.int32)
    picks = (order_row[:, None] == slots[None, :]).astype(jnp.int32)
    packed = jnp.sum(picks * lengths_row[None, :], 1)
    ends = jnp.cumsum(packed)
    spots = jnp.arange(group_rows, dtype=jnp.int32)
    return jnp.sum((spots[:, None] >= ends[None, :]).astype(jnp.int32), 1)


def allowed_mask(row_ids, row_segs, segments, key_ids, article_count):
    causal = key_ids[None, :] <= row_ids[:, None]
    same = segments[None, :] == row_segs[:, None]
    alone = (row_segs[:, None] < article_count) | (key_ids[None, :] == row_ids[:, None])
    return causal & same & alone


def from_columns(tiles, row_total, col_total):
    return (
        tiles.reshape(col_total // BLOCK, row_total // BLOCK, BLOCK, BLOCK)
        .transpose(1, 2, 0, 3)
        .reshape(row_total, col_total)
    )


def from_rows(tiles, row_total, col_total):
    return (
        tiles.reshape(row_total // BLOCK, col_total // BLOCK, BLOCK, BLOCK)
        .transpose(0, 2, 1, 3)
        .reshape(row_total, col_total)
    )


def to_columns(matrix):
    row_total, col_total = matrix.shape
    return (
        matrix.reshape(row_total // BLOCK, BLOCK, col_total // BLOCK, BLOCK)
        .transpose(2, 0, 1, 3)
        .reshape(-1, BLOCK, BLOCK)
    )


def to_rows(matrix):
    row_total, col_total = matrix.shape
    return (
        matrix.reshape(row_total // BLOCK, BLOCK, col_total // BLOCK, BLOCK)
        .transpose(0, 2, 1, 3)
        .reshape(-1, BLOCK, BLOCK)
    )


def per_device_general(
    tokens,
    cotangent,
    lengths,
    order,
    weights,
    momentum,
    stat_left,
    stat_right,
    root_left,
    root_right,
    vec_params,
    vec_momentum,
    vec_second,
):
    groups = lax.axis_size("grp")
    tp_size = lax.axis_size("tp")
    tp_rank = lax.axis_index("tp")
    tok_rows = tokens.shape[0]
    group_rows = tok_rows * tp_size
    article_count = lengths.shape[1]
    owners = groups * tp_size
    block_area = BLOCK * BLOCK * owners
    qkv_count = 3 * D * D // block_area
    out_count = D * D // block_area
    in_count = D * FF // block_area
    owned_blocks = weights.shape[0]
    heads_here = HEADS // tp_size
    qkv_cols = 3 * D // tp_size
    feat_here = D // tp_size
    ff_here = FF // tp_size
    qv_width = 2 * D // tp_size
    token_total = group_rows * groups
    gathered = lax.all_gather(weights.astype(jnp.bfloat16), "grp", axis=0, tiled=True)
    per_owner = gathered.reshape(groups, owned_blocks, BLOCK, BLOCK)
    marks = [0, qkv_count, qkv_count + out_count, qkv_count + out_count + in_count, owned_blocks]
    pieces = [
        per_owner[:, marks[index] : marks[index + 1]].reshape(-1, BLOCK, BLOCK)
        for index in range(4)
    ]
    w_qkv = from_columns(pieces[0], D, qkv_cols)
    w_out = from_rows(pieces[1], feat_here, D)
    w_in = from_columns(pieces[2], D, ff_here)
    w_down = from_rows(pieces[3], ff_here, D)
    w_qkv_heads = w_qkv.reshape(D, heads_here, 3, HD)
    w_out_heads = w_out.reshape(heads_here, HD, D)
    segments = segment_ids(lengths[0], order[0], group_rows)
    gain_one = vec_params[0]
    shift_one = vec_params[1]
    gain_two = vec_params[2]
    shift_two = vec_params[3]
    bias_out = vec_params[4]
    bias_down = vec_params[5]
    qv_here = lax.dynamic_slice_in_dim(
        vec_params[6:8].reshape(2 * D), tp_rank * qv_width, qv_width
    ).reshape(heads_here, 2, HD)
    bias_heads = jnp.stack(
        [qv_here[:, 0], jnp.zeros((heads_here, HD), jnp.float32), qv_here[:, 1]], 0
    )[:, :, None, :]
    bias_in = lax.dynamic_slice_in_dim(vec_params[8:].reshape(FF), tp_rank * ff_here, ff_here)
    normed_one, unit_one, inverse_one = norm_rows(tokens, gain_one, shift_one)
    rows_one = lax.all_gather(normed_one.astype(jnp.bfloat16), "tp", axis=0, tiled=True)
    projected = (
        jnp.einsum("rx,xhcd->chrd", rows_one, w_qkv_heads, preferred_element_type=jnp.float32)
        + bias_heads
    ).astype(jnp.bfloat16)
    queries = projected[0]
    keys_all = projected[1]
    values_all = projected[2]
    span = min(512, group_rows)
    starts = jnp.arange(group_rows // span, dtype=jnp.int32) * span
    key_ids = jnp.arange(group_rows, dtype=jnp.int32)
    score_scale = HD ** (-0.5)

    def masked_scores(first_row):
        row_ids = first_row + jnp.arange(span, dtype=jnp.int32)
        row_segs = lax.dynamic_slice_in_dim(segments, first_row, span, 0)
        allowed = allowed_mask(row_ids, row_segs, segments, key_ids, article_count)
        query_rows = lax.dynamic_slice_in_dim(queries, first_row, span, 1)
        scores = (
            jnp.einsum("hqd,hkd->hqk", query_rows, keys_all, preferred_element_type=jnp.float32)
            * score_scale
        )
        return (jnp.where(allowed[None], scores, NEG), query_rows)

    def attend(context_buf, first_row):
        scores, query_rows = masked_scores(first_row)
        row_max = jnp.max(scores, -1, keepdims=True)
        expo = jnp.exp(scores - row_max)
        expsum = jnp.sum(expo, -1, keepdims=True)
        probs_low = (expo / expsum).astype(jnp.bfloat16)
        context = jnp.einsum(
            "hqk,hkd->hqd", probs_low, values_all, preferred_element_type=jnp.float32
        ).astype(jnp.bfloat16)
        context_buf = lax.dynamic_update_slice_in_dim(context_buf, context, first_row, 1)
        return (context_buf, (row_max + jnp.log(expsum))[:, :, 0])

    context_low, log_norm = lax.scan(
        attend, jnp.zeros((heads_here, group_rows, HD), jnp.bfloat16), starts
    )
    attn_sum = lax.psum_scatter(
        jnp.einsum(
            "hrd,hde->re", context_low, w_out_heads, preferred_element_type=jnp.float32
        ).astype(jnp.bfloat16),
        "tp",
        scatter_dimension=0,
        tiled=True,
    ).astype(jnp.float32)
    hidden = tokens + attn_sum + bias_out
    normed_two, unit_two, inverse_two = norm_rows(hidden, gain_two, shift_two)
    rows_two = lax.all_gather(normed_two.astype(jnp.bfloat16), "tp", axis=0, tiled=True)
    inner = jnp.dot(rows_two, w_in, preferred_element_type=jnp.float32) + bias_in
    activ, gelu_pull = jax.vjp(jax.nn.gelu, inner)
    activ_low = activ.astype(jnp.bfloat16)
    mixed = (
        hidden
        + lax.psum_scatter(
            jnp.dot(activ_low, w_down, preferred_element_type=jnp.float32).astype(jnp.bfloat16),
            "tp",
            scatter_dimension=0,
            tiled=True,
        ).astype(jnp.float32)
        + bias_down
    )
    grad_low = cotangent.astype(jnp.bfloat16)
    grad_rows = lax.all_gather(grad_low, "tp", axis=0, tiled=True)
    g_down = jnp.einsum("rf,rd->fd", activ_low, grad_rows, preferred_element_type=jnp.float32)
    grad_activ = jnp.einsum("rd,fd->rf", grad_rows, w_down, preferred_element_type=jnp.float32)
    grad_inner = gelu_pull(grad_activ)[0].astype(jnp.bfloat16)
    g_in = jnp.einsum("rd,rf->df", rows_two, grad_inner, preferred_element_type=jnp.float32)
    g_bias_in = jnp.sum(grad_inner.astype(jnp.float32), 0)
    ffn_blocks = jnp.concatenate(
        [
            to_columns(g_in).reshape(groups, in_count, BLOCK, BLOCK),
            to_rows(g_down).reshape(groups, in_count, BLOCK, BLOCK),
        ],
        1,
    )
    grad_normed_two = lax.psum_scatter(
        jnp.einsum("rf,df->rd", grad_inner, w_in, preferred_element_type=jnp.float32).astype(
            jnp.bfloat16
        ),
        "tp",
        scatter_dimension=0,
        tiled=True,
    ).astype(jnp.float32)
    grad_hidden = cotangent + norm_back(grad_normed_two, unit_two, inverse_two, gain_two)
    grad_attn_low = grad_hidden.astype(jnp.bfloat16)
    grad_attn_rows = lax.all_gather(grad_attn_low, "tp", axis=0, tiled=True)
    g_out = jnp.einsum(
        "hrd,re->hde", context_low, grad_attn_rows, preferred_element_type=jnp.float32
    ).reshape(feat_here, D)
    grad_context = jnp.einsum(
        "re,hde->hrd", grad_attn_rows, w_out_heads, preferred_element_type=jnp.float32
    ).astype(jnp.bfloat16)
    zero_heads = jnp.zeros((heads_here, group_rows, HD), jnp.float32)

    def attend_back(carry, inputs):
        grad_queries, grad_keys, grad_values = carry
        first_row, log_block = inputs
        scores, query_rows = masked_scores(first_row)
        probs = jnp.exp(scores - log_block[:, :, None])
        grad_ctx_rows = lax.dynamic_slice_in_dim(grad_context, first_row, span, 1)
        grad_probs = jnp.einsum(
            "hqd,hkd->hqk", grad_ctx_rows, values_all, preferred_element_type=jnp.float32
        )
        delta = jnp.sum(probs * grad_probs, -1, keepdims=True)
        grad_scores = (probs * (grad_probs - delta)).astype(jnp.bfloat16)
        query_part = (
            jnp.einsum("hqk,hkd->hqd", grad_scores, keys_all, preferred_element_type=jnp.float32)
            * score_scale
        )
        grad_queries = lax.dynamic_update_slice_in_dim(grad_queries, query_part, first_row, 1)
        grad_keys = (
            grad_keys
            + jnp.einsum(
                "hqk,hqd->hkd", grad_scores, query_rows, preferred_element_type=jnp.float32
            )
            * score_scale
        )
        grad_values = grad_values + jnp.einsum(
            "hqk,hqd->hkd",
            probs.astype(jnp.bfloat16),
            grad_ctx_rows,
            preferred_element_type=jnp.float32,
        )
        return ((grad_queries, grad_keys, grad_values), None)

    (grad_queries, grad_keys, grad_values), unused = lax.scan(
        attend_back, (zero_heads, zero_heads, zero_heads), (starts, log_norm)
    )
    grad_proj = jnp.stack([grad_queries, grad_keys, grad_values], 0).astype(jnp.bfloat16)
    proj_sums = jnp.sum(grad_proj.astype(jnp.float32), 2)
    g_bias_qv = jnp.stack([proj_sums[0], proj_sums[2]], 1).reshape(qv_width)
    g_qkv = jnp.einsum(
        "rx,chrd->xhcd", rows_one, grad_proj, preferred_element_type=jnp.float32
    ).reshape(D, qkv_cols)
    grad_normed_one = lax.psum_scatter(
        jnp.einsum(
            "chrd,xhcd->rx", grad_proj, w_qkv_heads, preferred_element_type=jnp.float32
        ).astype(jnp.bfloat16),
        "tp",
        scatter_dimension=0,
        tiled=True,
    ).astype(jnp.float32)
    input_grad = grad_hidden + norm_back(grad_normed_one, unit_one, inverse_one, gain_one)
    local_rows = jnp.stack(
        [
            jnp.sum(grad_normed_one * unit_one, 0),
            jnp.sum(grad_normed_one, 0),
            jnp.sum(grad_normed_two * unit_two, 0),
            jnp.sum(grad_normed_two, 0),
            jnp.sum(grad_hidden, 0),
            jnp.sum(cotangent, 0),
        ]
    )
    qv_rows = lax.dynamic_update_slice(
        jnp.zeros((2 * D,), jnp.float32), g_bias_qv, (tp_rank * qv_width,)
    ).reshape(2, D)
    in_rows = lax.dynamic_update_slice(
        jnp.zeros((FF,), jnp.float32), g_bias_in, (tp_rank * ff_here,)
    ).reshape(FF // D, D)
    vec_grads = lax.psum(jnp.concatenate([local_rows, qv_rows, in_rows], 0), ("grp", "tp"))
    attn_blocks = jnp.concatenate(
        [
            to_columns(g_qkv).reshape(groups, qkv_count, BLOCK, BLOCK),
            to_rows(g_out).reshape(groups, out_count, BLOCK, BLOCK),
        ],
        1,
    )
    every_block = jnp.concatenate([attn_blocks, ffn_blocks], 1).reshape(-1, BLOCK, BLOCK)
    weight_grads = lax.psum_scatter(
        every_block.astype(jnp.bfloat16), "grp", scatter_dimension=0, tiled=True
    ).astype(jnp.float32)
    scaled = weight_grads * token_total ** (-0.5)
    stat_left_new = DECAY * stat_left + (1.0 - DECAY) * jnp.einsum(
        "nij,nkj->nik", scaled, scaled, precision=lax.Precision.HIGHEST
    )
    stat_right_new = DECAY * stat_right + (1.0 - DECAY) * jnp.einsum(
        "nji,njk->nik", scaled, scaled, precision=lax.Precision.HIGHEST
    )
    shaped = jnp.einsum("nij,njk->nik", root_left, scaled, precision=lax.Precision.HIGHEST)
    shaped = jnp.einsum("nij,njk->nik", shaped, root_right, precision=lax.Precision.HIGHEST)
    momentum_new = BETA * momentum + shaped
    weights_new = weights - RATE * momentum_new
    vec_scaled = vec_grads * token_total ** (-0.5)
    vec_second_new = VEC_DECAY * vec_second + (1.0 - VEC_DECAY) * vec_scaled * vec_scaled
    vec_momentum_new = BETA * vec_momentum + vec_scaled * lax.rsqrt(vec_second_new + VEC_EPS)
    vec_new = vec_params - VEC_RATE * vec_momentum_new
    return (
        mixed,
        input_grad,
        weight_grads,
        stat_left_new,
        stat_right_new,
        momentum_new,
        weights_new,
        vec_grads,
        vec_second_new,
        vec_momentum_new,
        vec_new,
    )


MESH_ID = pl.DeviceIdType.MESH
LANES = 128
HALF = 64
VMEM_LIMIT = 62 * 2**20
ARTICLES = 4
GELU_A = (2.0 / 3.141592653589793) ** 0.5
GELU_B = 0.044715


def remote(src, dst, send_sem, recv_sem, device):
    return pltpu.make_async_remote_copy(
        src_ref=src,
        dst_ref=dst,
        send_sem=send_sem,
        recv_sem=recv_sem,
        device_id=device,
        device_id_type=MESH_ID,
    )


def place():
    grp = lax.axis_index("grp")
    return lax.div(grp, 4), lax.rem(lax.div(grp, 2), 2), lax.rem(grp, 2), lax.axis_index("tp")


def slot_of(z, y, c):
    return z * 4 + y * 2 + c


def lay_blocks(view_ref, stack):
    half = view_ref.shape[2] // 2

    def row(i, carry):
        tile = view_ref[i].T
        stack[pl.ds(i, half, stride=BLOCK), :] = jnp.concatenate([tile[:half], tile[half:]], 1)
        return carry

    lax.fori_loop(0, BLOCK, row, 0, unroll=8)


def piece_shapes():
    return ((768, LANES), (64, 512), (1024, LANES), (LANES, 1024))


def fold_tiles(value, mask):
    kept = jnp.where(mask, value, 0.0)
    halves = kept[:, :LANES] + kept[:, LANES:]
    return halves + pltpu.roll(halves, HALF, 1)


def update_kernel(
    scale,
    sum_q,
    sum_o,
    sum_i,
    sum_d,
    root_l,
    root_r,
    vec_g,
    vecs,
    vec_m,
    vec_s,
    mixed,
    input_grad,
    w,
    m,
    sl,
    sr,
    out_g,
    out_sl,
    out_sr,
    out_m,
    out_w,
    out_vg,
    out_vs,
    out_vm,
    out_v,
    out_mixed,
    out_input_grad,
    first,
    second,
):
    count = root_l.shape[2]
    bf = jnp.bfloat16
    out_mixed[...] = mixed[...]
    out_input_grad[...] = input_grad[...]

    @pl.when(pl.program_id(0) == 0)
    def _():
        total = vec_g[...]
        out_vg[...] = total
        scaled = total * scale
        fresh = VEC_DECAY * vec_s[...] + (1.0 - VEC_DECAY) * scaled * scaled
        out_vs[...] = fresh
        momentum = BETA * vec_m[...] + scaled * lax.rsqrt(fresh + VEC_EPS)
        out_vm[...] = momentum
        out_v[...] = vecs[...] - VEC_RATE * momentum
        rows = sum_q.shape[0]
        first[0:rows, 0:HALF] = sum_q[:, 0:HALF]
        first[rows : 2 * rows, 0:HALF] = sum_q[:, HALF:LANES]
        base = 2 * rows
        for b in range(8):
            first[base + b * 64 : base + b * 64 + 64, 0:HALF] = sum_o[:, b * HALF : (b + 1) * HALF]
        base += 512
        first[base : base + 1024, 0:HALF] = sum_i[:, 0:HALF]
        first[base + 1024 : base + 2048, 0:HALF] = sum_i[:, HALF:LANES]
        base += 2048
        for r in range(2):
            for b in range(16):
                at = base + (r * 16 + b) * 64
                first[at : at + 64, 0:HALF] = sum_d[r * 64 : r * 64 + 64, b * HALF : (b + 1) * HALF]

        def row(i, carry):
            both = jnp.concatenate([root_l[i], root_r[i]], 0)
            second[pl.ds(i, count, stride=BLOCK), :] = both.T
            return carry

        lax.fori_loop(0, BLOCK, row, 0, unroll=8)
        row_id = lax.broadcasted_iota(jnp.int32, (256, 256), 0)
        col_id = lax.broadcasted_iota(jnp.int32, (256, 256), 1)
        mask = lax.shift_right_logical(row_id, 6) == lax.shift_right_logical(col_id, 6)
        zero = jnp.zeros((256, 256), jnp.float32)

        def spread(v):
            return jnp.where(mask, jnp.concatenate([v, v, v, v], 1), zero).astype(bf)

        def four(k, carry):
            at = pl.ds(pl.multiple_of(k * 256, 256), 256)
            s32 = first[at, 0:HALF] * scale
            s = s32.astype(bf)
            left = second[at, 0:HALF]
            right = second[at, HALF:LANES].astype(bf)
            outer = lax.dot_general(s, s, (((1,), (1,)), ((), ())), preferred_element_type=jnp.float32)
            inner = lax.dot_general(spread(s32), s, (((0,), (0,)), ((), ())), preferred_element_type=jnp.float32)
            shaped = jnp.dot(spread(left), s, preferred_element_type=jnp.float32)
            shaped = jnp.dot(spread(shaped), right, preferred_element_type=jnp.float32)
            first[at, HALF:LANES] = fold_tiles(outer, mask)[:, HALF:LANES]
            second[at, 0:HALF] = inner
            second[at, HALF:LANES] = shaped
            return carry

        lax.fori_loop(0, count // 4, four, 0, unroll=4)

    i0 = pl.program_id(0) * w.shape[0]

    def rows_out(ii, carry):
        at = pl.ds(i0 + ii, count, stride=BLOCK)
        one = first[at, :].T
        two = second[at, :].T
        out_g[ii] = one[0:HALF]
        out_sl[ii] = DECAY * sl[ii] + (1.0 - DECAY) * one[HALF:LANES]
        out_sr[ii] = DECAY * sr[ii] + (1.0 - DECAY) * two[0:HALF]
        fresh = BETA * m[ii] + two[HALF:LANES]
        out_m[ii] = fresh
        out_w[ii] = w[ii] - RATE * fresh
        return carry

    lax.fori_loop(0, w.shape[0], rows_out, 0, unroll=True)


def update_blocks(sums, blocks, vec_grads, vecs, results, token_total):
    views = [jnp.transpose(a, (1, 2, 0)) for a in blocks]
    count = blocks[0].shape[0]
    rows = 8
    whole = pl.BlockSpec(memory_space=pltpu.VMEM)
    steps = BLOCK // rows
    some = pl.BlockSpec((results[0].shape[0] // steps, results[0].shape[1]), lambda i: (i, 0))
    part = pl.BlockSpec((rows, BLOCK, count), lambda i: (i, 0, 0))
    vec = jax.ShapeDtypeStruct(vec_grads.shape, jnp.float32)
    outs = pl.pallas_call(
        functools.partial(update_kernel, token_total ** (-0.5)),
        grid=(steps,),
        out_shape=[jax.ShapeDtypeStruct((BLOCK, BLOCK, count), jnp.float32)] * 5
        + [vec] * 4
        + [jax.ShapeDtypeStruct(a.shape, a.dtype) for a in results],
        in_specs=[whole] * 10 + [some] * 2 + [part] * 4,
        out_specs=[part] * 5 + [whole] * 4 + [some] * 2,
        scratch_shapes=[
            pltpu.VMEM((count * BLOCK, LANES), jnp.float32),
            pltpu.VMEM((count * BLOCK, LANES), jnp.float32),
        ],
        compiler_params=pltpu.CompilerParams(vmem_limit_bytes=VMEM_LIMIT),
        name="update_blocks",
    )(*sums, *views[4:], vec_grads, *vecs, *results, *views[:4])
    return [jnp.transpose(a, (2, 0, 1)) for a in outs[:5]], outs[5:9], outs[9:]


DEPTH = 4


def layer_kernel(
    lengths,
    order,
    view,
    tokens,
    cot,
    vecs,
    mixed,
    input_grad,
    sum_q,
    sum_o,
    sum_i,
    sum_d,
    vec_grads,
    gq,
    go,
    gi,
    gd,
    wqkv,
    cq,
    co,
    ci,
    cd,
    yq,
    yo,
    yi,
    yd,
    yv,
    zq,
    zo,
    zi,
    zd,
    zv,
    rows_one,
    rows_two,
    rows_t,
    grad_rows,
    grad_attn,
    probs,
    qkv,
    ctx,
    gctx,
    far,
    inx,
    go_x,
    ctx_x,
    macc,
    nacc,
    act,
    gin,
    bias_sum,
    qkv_bias,
    vin,
    vout,
    late,
    late_sum,
    late_in,
    recv,
    send_y,
    send_c,
    send_z,
    rc_recv,
    rc_send,
    ry_recv,
    ry_send,
    rz_recv,
    rz_send,
    x_send,
    x_recv,
    v_send,
    v_recv,
    l_send,
    l_recv,
    copy_sem,
):
    bf, f32 = jnp.bfloat16, jnp.float32
    z, y, c, t = place()
    me = slot_of(z, y, c)
    x_peer = (me, 1 - t)
    y_peer = (slot_of(z, 1 - y, c), t)
    c_peer = (slot_of(z, y, 1 - c), t)
    rows = tokens.shape[0]
    own = pl.ds(pl.multiple_of(t * rows, rows), rows)
    other = pl.ds(pl.multiple_of((1 - t) * rows, rows), rows)

    def lanes(start, size, unit):
        return pl.ds(pl.multiple_of(start, unit), size)

    gathered, core_in = (gq, go, gi, gd), (cq, co, ci, cd)
    y_in, z_in = (yq, yo, yi, yd, yv), (zq, zo, zi, zd, zv)
    sums = (sum_q, sum_o, sum_i, sum_d)
    Q, O, I, W, V = range(5)

    def dot(a, b):
        return jnp.dot(a, b, preferred_element_type=f32)

    def dot_nt(a, b):
        return lax.dot_general(a, b, (((1,), (1,)), ((), ())), preferred_element_type=f32)

    def dot_tn(a, b):
        return lax.dot_general(a, b, (((0,), (0,)), ((), ())), preferred_element_type=f32)

    def piece(k, zz, yy, cc):
        if k == O:
            return go.at[zz * 2 + yy, :, pl.ds(pl.multiple_of(cc * 512, 512), 512)]
        return gathered[k].at[slot_of(zz, yy, cc)]

    def near(s):
        return lax.rem(z + (1 - 2 * lax.div(z, 2)) * s + DEPTH, DEPTH)

    def ag_piece(k, zz, yy, cc):
        if k == W:
            return gd.at[slot_of(zz, yy, cc), 0:HALF]
        if k == V:
            return gd.at[slot_of(zz, yy, cc), HALF:LANES]
        return piece(k, zz, yy, cc)

    def ag_copy(k, zz, yy, way):
        src = ag_piece(k, zz, yy, c)
        sem = recv.at[k, slot_of(zz, yy, c)]
        if way == "up":
            return remote(src, src, send_z.at[k, 0, yy * DEPTH + zz], sem, (slot_of(z + 1, y, c), t))
        if way == "down":
            return remote(src, src, send_z.at[k, 1, yy * DEPTH + zz], sem, (slot_of(z - 1, y, c), t))
        if way == "y":
            return remote(src, src, send_y.at[k, zz], sem, y_peer)
        return remote(src, src, send_c.at[k, yy * DEPTH + zz], sem, c_peer)

    def ag_wait(k, zz, yy, cc):
        ref = ag_piece(k, zz, yy, cc)
        remote(ref, ref, send_y.at[k, 0], recv.at[k, slot_of(zz, yy, cc)], y_peer).wait_recv()

    def own_sends_z(k):
        @pl.when(z < DEPTH - 1)
        def _():
            ag_copy(k, z, y, "up").start()

        @pl.when(z > 0)
        def _():
            ag_copy(k, z, y, "down").start()

        ag_copy(k, z, y, "core").start()

    def own_sends_y(k):
        ag_copy(k, z, y, "y").start()

    def z_arrival(kinds, dist):
        @pl.when(z >= dist)
        def _():
            for k in kinds:
                ag_wait(k, z - dist, y, c)

                @pl.when(z < DEPTH - 1)
                def _():
                    ag_copy(k, z - dist, y, "up").start()

                ag_copy(k, z - dist, y, "y").start()
                ag_copy(k, z - dist, y, "core").start()

        @pl.when(z + dist < DEPTH)
        def _():
            for k in kinds:
                ag_wait(k, z + dist, y, c)

                @pl.when(z > 0)
                def _():
                    ag_copy(k, z + dist, y, "down").start()

                ag_copy(k, z + dist, y, "y").start()
                ag_copy(k, z + dist, y, "core").start()

    def y_arrival(kinds, dist):
        def one(zz):
            for k in kinds:
                ag_wait(k, zz, 1 - y, c)
                ag_copy(k, zz, 1 - y, "core").start()

        if dist == 0:
            one(z)
            return

        @pl.when(z >= dist)
        def _():
            one(z - dist)

        @pl.when(z + dist < DEPTH)
        def _():
            one(z + dist)

    def v_forward(zz, yy):
        ag_wait(V, zz, yy, c)

        @pl.when((zz <= z) & (z < DEPTH - 1))
        def _():
            ag_copy(V, zz, yy, "up").start()

        @pl.when((zz >= z) & (z > 0))
        def _():
            ag_copy(V, zz, yy, "down").start()

        ag_copy(V, zz, yy, "core").start()

    def v_arrival(dist):
        for yy in (y, 1 - y):

            @pl.when(z >= dist)
            def _():
                v_forward(z - dist, yy)

            @pl.when(z + dist < DEPTH)
            def _():
                v_forward(z + dist, yy)

    def drain(k, zz, yy):
        ag_copy(k, zz, yy, "core").wait_send()
        if k == V:

            @pl.when((yy == y) & (zz == z))
            def _():
                ag_copy(k, zz, yy, "y").wait_send()

            @pl.when((zz <= z) & (z < DEPTH - 1))
            def _():
                ag_copy(k, zz, yy, "up").wait_send()

            @pl.when((zz >= z) & (z > 0))
            def _():
                ag_copy(k, zz, yy, "down").wait_send()

            return

        @pl.when(yy == y)
        def _():
            ag_copy(k, zz, y, "y").wait_send()

            @pl.when((zz <= z) & (z < DEPTH - 1))
            def _():
                ag_copy(k, zz, y, "up").wait_send()

            @pl.when((zz >= z) & (z > 0))
            def _():
                ag_copy(k, zz, y, "down").wait_send()

    def add(dst, *terms):
        count, width = dst.shape
        step = min(count, 256 * LANES // width)

        def body(i, carry):
            at = pl.ds(pl.multiple_of(i * step, 16), step)
            total = terms[0][at, :].astype(f32)
            for term in terms[1:]:
                total = total + term[at, :].astype(f32)
            dst[at, :] = total.astype(dst.dtype)
            return carry

        lax.fori_loop(0, count // step, body, 0)

    side = lax.div(z, 2)
    end_z, inner_z = 3 * side, 1 + side
    is_end = z == end_z

    def rc_copy(k, zz, yy):
        at = zz * 2 + yy
        return remote(piece(k, zz, yy, 1 - c), core_in[k].at[at], rc_send.at[k, at], rc_recv.at[k, at], c_peer)

    def ry_copy(k, zz):
        if k == V:
            return remote(ag_piece(V, z, 1 - y, c), y_in[V].at[0], ry_send.at[V, 0], ry_recv.at[V, 0], y_peer)
        return remote(ag_piece(k, zz, 1 - y, c), y_in[k].at[zz], ry_send.at[k, zz], ry_recv.at[k, zz], y_peer)

    def z_slot(k, slot, yy):
        return z_in[k].at[slot * 2 + yy if k == V else slot]

    def z_sem(slot, yy):
        return slot * 2 + yy

    def rz_copy(k, s, yy, from_end):
        slot = s - 1 if from_end else {3: 0, 2: 1, 1: 3}[s]
        to = inner_z if from_end else {3: end_z, 2: 3 - end_z, 1: 3 - inner_z}[s]
        sent, landed = rz_send.at[k, (s - 1) * 2 + yy], rz_recv.at[k, z_sem(slot, yy)]
        return remote(ag_piece(k, near(s), yy, c), z_slot(k, slot, yy), sent, landed, (slot_of(to, y, c), t))

    def z_landed(k, slot, yy):
        ref = z_slot(k, slot, yy)
        remote(ref, ref, rz_send.at[k, 0], rz_recv.at[k, z_sem(slot, yy)], y_peer).wait_recv()
        return ref

    def y_landed(k, zz):
        ref = y_in[k].at[0 if k == V else zz]
        remote(ref, ref, ry_send.at[k, 0], ry_recv.at[k, 0 if k == V else zz], y_peer).wait_recv()
        return ref

    def rc_add(k, zz, yy):
        at = zz * 2 + yy
        remote(core_in[k].at[at], core_in[k].at[at], rc_send.at[k, 0], rc_recv.at[k, at], c_peer).wait_recv()
        mine = piece(k, zz, yy, c)
        add(mine, mine, core_in[k].at[at])

        @pl.when(yy != y)
        def _():
            ry_copy(k, zz).start()

    def z_step(k, s, yy, *terms):
        mine = ag_piece(k, near(s), yy, c)
        if terms:
            add(mine, mine, *terms)

        @pl.when(is_end)
        def _():
            rz_copy(k, s, yy, True).start()

        if s == 3:

            @pl.when(jnp.logical_not(is_end))
            def _():
                rz_copy(k, s, yy, False).start()

    def z_merge(k, s, yy):
        @pl.when(jnp.logical_not(is_end))
        def _():
            mine = ag_piece(k, near(s), yy, c)
            add(mine, mine, z_landed(k, s, yy))
            rz_copy(k, s, yy, False).start()

    def ry_add(k, s):
        z_step(k, s, y, y_landed(k, near(s)))

    def ry_merge(k, s):
        z_merge(k, s, y)

    def total_of(k):
        return sum_d.at[(k - W) * HALF : (k - W + 1) * HALF] if k >= W else sums[k]

    def z_total(k, yy, dst, *terms):
        mine = ag_piece(k, z, yy, c)
        first = z_landed(k, 0, yy)

        @pl.when(is_end)
        def _():
            add(dst, mine, first, z_landed(k, 1, yy), *terms)

        @pl.when(jnp.logical_not(is_end))
        def _():
            add(dst, mine, first, z_landed(k, 3, yy), *terms)

    def own_total(k):
        z_total(k, y, total_of(k), y_landed(k, z))

    def v_cross():
        mine = ag_piece(V, z, 1 - y, c)
        z_total(V, 1 - y, mine)
        ry_copy(V, z).start()

    def x_rows(ref, index):
        return remote(ref.at[own], ref.at[own], x_send.at[index], x_recv.at[index], x_peer)

    def x_rows_wait(ref, index):
        remote(ref.at[other], ref.at[other], x_send.at[index], x_recv.at[index], x_peer).wait_recv()

    def x_part(index):
        slot = 1 if index == 2 else 0
        return remote(far.at[slot], inx.at[slot], x_send.at[5 + index], x_recv.at[5 + index], x_peer)

    def by_rows(body, step=64):
        def run(i, carry):
            body(pl.multiple_of(i * step, step), step)
            return carry

        lax.fori_loop(0, rows // step, run, 0)

    def norm(value):
        average = jnp.mean(value, -1, keepdims=True)
        centred = value - average
        inverse = lax.rsqrt(jnp.mean(centred * centred, -1, keepdims=True) + EPS)
        return centred * inverse, inverse

    def norm_grad(grad, unit, inverse, gain):
        scaled = grad * gain
        return inverse * (
            scaled - jnp.mean(scaled, -1, keepdims=True) - unit * jnp.mean(scaled * unit, -1, keepdims=True)
        )

    def x_out():
        half = (slice(None), slice(None), lanes(c * 512, 512, 512))
        return remote(go.at[half], go_x.at[half], x_send.at[4], x_recv.at[4], x_peer)

    def x_out_core(cc):
        half = (slice(None), slice(None), lanes(cc * 512, 512, 512))
        return remote(go_x.at[half], go_x.at[half], x_send.at[9], x_recv.at[9], c_peer)

    def x_grad_context():
        return remote(ctx_x, gctx.at[own], x_send.at[10], x_recv.at[10], x_peer)

    def x_grad_context_wait():
        remote(gctx.at[other], gctx.at[other], x_send.at[10], x_recv.at[10], x_peer).wait_recv()

    stages = (x_peer, c_peer, y_peer)

    def v_copy(stage):
        return remote(vout.at[1 + stage], vin.at[stage], v_send.at[stage], v_recv.at[stage], stages[stage])

    def vz_copy(step):
        peer = (slot_of(lax.rem(z + step, DEPTH), y, c), t)
        return remote(vout.at[4], vin.at[3 + z], v_send.at[2 + step], v_recv.at[3 + z], peer)

    def early_rows(hop):
        if hop == 0:
            vout[1] = vout[0]
        else:
            v_copy(hop - 1).wait_recv()
            vout[1 + hop] = vout[hop] + vin[hop - 1]
        if hop < 3:
            v_copy(hop).start()
        else:
            for step in range(1, DEPTH):
                vz_copy(step).start()
            vin[3 + z] = vout[4]

    def late_turn(turn):
        dx, dy, dc = turn // 4, turn // 2 % 2, turn % 2
        xx, yy, cc = (1 - t if dx else t), (1 - y if dy else y), (1 - c if dc else c)
        return (slot_of(z, yy, cc), xx), xx * 4 + yy * 2 + cc

    def late_copy(turn):
        here = t * 4 + y * 2 + c
        return remote(late, late_in.at[here], l_send.at[turn], l_recv.at[here], late_turn(turn)[0])

    def late_wait(index):
        remote(late_in.at[index], late_in.at[index], l_send.at[0], l_recv.at[index], y_peer).wait_recv()

    def late_z(step):
        peer = (slot_of(lax.rem(z + step, DEPTH), y, c), t)
        return remote(late_sum, late_in.at[8 + z], l_send.at[7 + step], l_recv.at[8 + z], peer)

    barrier = pltpu.get_barrier_semaphore()
    z_peers = [(slot_of(lax.rem(z + step, DEPTH), y, c), t) for step in range(1, DEPTH)]
    everyone = [late_turn(turn)[0] for turn in range(1, 8)] + z_peers
    for device in everyone:
        pl.semaphore_signal(barrier, inc=1, device_id=device, device_id_type=MESH_ID)

    def prepare(held, stack):
        load = pltpu.make_async_copy(view, held, copy_sem.at[0])
        load.start()

        def first_norm(at, step):
            unit, inverse = norm(tokens[pl.ds(at, step), :])
            to = pl.ds(pl.multiple_of(t * rows + at, step), step)
            rows_one[to, :] = (unit * vecs[0:1, :] + vecs[1:2, :]).astype(bf)
            grad_rows[to, :] = cot[pl.ds(at, step), :].astype(bf)

        load.wait()
        lay_blocks(held, stack)

        def pair(left, right, count, left_high=False, right_high=False):
            first, second = stack[left : left + count, :], stack[right : right + count, :]
            first = pltpu.roll(first, HALF, 1) if left_high else first
            second = second if right_high else pltpu.roll(second, HALF, 1)
            lane = lax.broadcasted_iota(jnp.int32, (count, LANES), 1)
            return jnp.where(lane < HALF, first, second).astype(bf)

        n = gq.shape[1]
        gq[me] = pair(0, n, n)
        base = 2 * n
        wide = [pair(base + b * 64, base + b * 64 + 64, 64) for b in range(0, 8, 2)]
        go[z * 2 + y, :, lanes(c * 512, 512, 512)] = jnp.concatenate(wide, 1)
        pl.semaphore_wait(barrier, len(everyone))
        for k in (Q, O):
            own_sends_y(k)
            own_sends_z(k)
        by_rows(first_norm)
        x_rows(rows_one, 0).start()
        base += 512
        gi[me] = pair(base, 0, D, right_high=True)
        for r in range(2):
            for b in range(0, 16, 2):
                at = D + (r * 16 + b) * 64
                gd[me, r * 64 : r * 64 + 64, b * HALF : b * HALF + LANES] = pair(at, at + 64, 64, True, True)

    pl.run_scoped(
        prepare,
        pltpu.VMEM(view.shape, f32),
        pltpu.VMEM((view.shape[2] // 2 * BLOCK, LANES), f32),
    )
    x_rows(grad_rows, 1).start()
    z_arrival((Q, O), 1)
    y_arrival((Q, O), 0)
    for k in (I, W, V):
        own_sends_z(k)
    z_arrival((Q, O), 2)
    y_arrival((Q, O), 1)
    z_arrival((Q, O), 3)
    for k in (I, W, V):
        own_sends_y(k)

    def core_waits(kinds, zz):
        for k in kinds:
            for yy in (y, 1 - y):
                ag_wait(k, zz, yy, 1 - c)

    x_rows_wait(rows_one, 0)

    ends = []
    for p in range(ARTICLES):
        length = 0
        for a in range(ARTICLES):
            length = length + jnp.where(order[0, p] == a, lengths[0, a], 0)
        ends.append(length + ends[-1] if p else length)

    def allowed(first, count):
        ids = lax.broadcasted_iota(jnp.int32, (rows, 1), 0) + first
        start = jnp.zeros((rows, 1), jnp.int32)
        for end in ends:
            start = jnp.where(ids >= end, end, start)
        start = jnp.where(ids >= ends[-1], ids, start)
        keys = lax.broadcasted_iota(jnp.int32, (rows, count), 1)
        return (keys <= ids) & (keys >= start)

    scale = HD ** (-0.5)
    strip = 1024

    def assemble(h):
        for yy in range(2):
            even, odd = gq.at[slot_of(h, yy, 0)], gq.at[slot_of(h, yy, 1)]
            at = yy * 192
            wqkv[h, 0:768, at : at + 64] = even[:, 0:64]
            wqkv[h, 768:1024, at : at + 64] = even[0:256, 64:128]
            wqkv[h, 0:512, at + 64 : at + 128] = even[256:768, 64:128]
            wqkv[h, 512:1024, at + 64 : at + 128] = odd[0:512, 0:64]
            wqkv[h, 0:256, at + 128 : at + 192] = odd[512:768, 0:64]
            wqkv[h, 256:1024, at + 128 : at + 192] = odd[:, 64:128]

    def disassemble(h, value):
        for yy in range(2):
            even, odd = gq.at[slot_of(h, yy, 0)], gq.at[slot_of(h, yy, 1)]
            at = yy * 192
            even[:, 0:64] = value[0:768, at : at + 64]
            even[0:256, 64:128] = value[768:1024, at : at + 64]
            even[256:768, 64:128] = value[0:512, at + 64 : at + 128]
            odd[0:512, 0:64] = value[512:1024, at + 64 : at + 128]
            odd[512:768, 0:64] = value[0:256, at + 128 : at + 192]
            odd[:, 64:128] = value[256:1024, at + 128 : at + 192]

    qv = vecs[pl.ds(6 + t, 1), :]
    for h in range(DEPTH):
        none = jnp.zeros((1, HD), f32)
        qkv_bias[h] = jnp.concatenate([qv[:, h * 256 : h * 256 + 128], none, qv[:, h * 256 + 128 : h * 256 + 256]], 1)

    def head(h):
        core_waits((Q,), h)
        assemble(h)
        qkv[h] = (dot(rows_one[...], wqkv[h]) + qkv_bias[h]).astype(bf)
        for block in range(2):
            at, seen = slice(block * rows, (block + 1) * rows), (block + 1) * rows
            scores = dot_nt(qkv[h, at, 0:128], qkv[h, 0:seen, 128:256]) * scale
            scores = jnp.where(allowed(block * rows, seen), scores, NEG)
            expo = jnp.exp(scores - jnp.max(scores, -1, keepdims=True))
            low = (expo / jnp.sum(expo, -1, keepdims=True)).astype(bf)
            probs[h, at, 0:seen] = low
            ctx[at, lanes(h * HD, HD, HD)] = dot(low, qkv[h, 0:seen, 256:384]).astype(bf)

    head(near(0))
    y_arrival((Q, O), 2)
    head(near(1))
    y_arrival((Q, O), 3)
    head(near(2))
    z_arrival((I, W), 1)
    head(near(3))
    y_arrival((I, W), 0)
    v_forward(z, 1 - y)
    for zz in range(DEPTH):
        core_waits((O,), zz)

    def w_out(ref):
        return ref[...].reshape(DEPTH * HD, D)

    far[0] = dot(ctx[other, :], w_out(go)).astype(bf)
    x_part(0).start()
    mixed[...] = tokens[...] + dot(ctx[own, :], w_out(go)) + vecs[4:5, :]
    z_arrival((I, W), 2)
    v_arrival(1)
    y_arrival((I, W), 1)
    x_part(0).wait_recv()

    def second_norm(at, step):
        value = mixed[pl.ds(at, step), :] + inx[0, pl.ds(at, step), :].astype(f32)
        mixed[pl.ds(at, step), :] = value
        unit, inverse = norm(value)
        to = pl.ds(pl.multiple_of(t * rows + at, step), step)
        rows_two[to, :] = (unit * vecs[2:3, :] + vecs[3:4, :]).astype(bf)

    by_rows(second_norm)
    x_rows(rows_two, 2).start()
    x_out().start()
    z_arrival((I, W), 3)
    v_arrival(2)
    macc[...] = jnp.zeros_like(macc)
    nacc[...] = jnp.zeros_like(nacc)
    vout[...] = jnp.zeros_like(vout)
    x_rows_wait(grad_rows, 1)

    def ffn(half, zz):
        first = 4 * zz
        at = pl.ds(pl.multiple_of(lax.rem(t + half, 2) * rows, rows), rows)
        units = lanes(zz * 512, 512, 512)
        bias_row = vecs[pl.ds(8 + 2 * t + lax.div(zz, 2), 1), lanes(lax.rem(zz, 2) * 512, 512, 512)]

        def w_in(start, count):
            return jnp.concatenate([gi[first + j, start : start + count, :] for j in range(4)], 1)

        def w_down(start, count):
            return gd[pl.ds(first, 4), :, start : start + count].reshape(512, count)

        inner = dot(rows_two[at, :], w_in(0, D)) + bias_row
        square = inner * inner
        bent = jnp.tanh(GELU_A * inner * (1.0 + GELU_B * square))
        act[at, units] = (0.5 * inner * (1.0 + bent)).astype(bf)
        slope = 0.5 * (1.0 + bent) + 0.5 * inner * (1.0 - bent * bent) * (GELU_A * (1.0 + 3.0 * GELU_B * square))
        gin[at, units] = (dot_nt(grad_rows[at, :], w_down(0, D)) * slope).astype(bf)
        for nb in range(4):
            out = slice(nb * 256, nb * 256 + 256)
            nacc[at, out] += dot_nt(gin[at, units], w_in(nb * 256, 256))
            macc[at, out] += dot(act[at, units], w_down(nb * 256, 256))

    def ffn_grads(zz):
        first = 4 * zz
        units = lanes(zz * 512, 512, 512)
        for k in (I, W, V):
            for yy in range(2):
                drain(k, zz, yy)
        bias_sum[zz] = jnp.sum(gin[:, units].astype(f32), 0, keepdims=True)
        for nb in range(4):
            out = slice(nb * 256, nb * 256 + 256)
            part = dot(rows_t[out, :], gin[:, units]).astype(bf)
            for j in range(4):
                gi[first + j, out, :] = part[:, j * LANES : (j + 1) * LANES]
        for yy in (1 - y, y):
            rc_copy(I, zz, yy).start()
        act_t = act[:, units].T
        for nb in range(4):
            out = slice(nb * 256, nb * 256 + 256)
            part = dot(act_t, grad_rows[:, out]).astype(bf)
            gd[pl.ds(first, 4), :, out] = part.reshape(4, LANES, 256)
        for yy in (1 - y, y):
            rc_copy(W, zz, yy).start()

    def reduce_core(zz):
        for yy in (1 - y, y):
            for k in (I, W):
                rc_add(k, zz, yy)

    def v_step(s):
        for yy in (1 - y, y):
            z_step(V, s, yy)

    def v_merge(s):
        for yy in (1 - y, y):
            z_merge(V, s, yy)

    core_waits((I, W, V), z)
    ffn(0, z)
    y_arrival((I, W), 2)
    core_waits((I, W, V), near(1))
    ffn(0, near(1))
    x_rows_wait(rows_two, 2)
    rows_t[...] = rows_two[...].T

    def by_z(s, carry):
        @pl.when(s == 2)
        def _():
            v_arrival(3)
            y_arrival((I, W), 3)

        @pl.when(s >= 2)
        def _():
            core_waits((I, W, V), near(s))
            ffn(0, near(s))

        ffn(1, near(s))

        @pl.when(s == DEPTH - 1)
        def _():
            x_part(0).wait_send()
            far[0] = nacc[other, :].astype(bf)
            x_part(1).start()

        @pl.when(s > 0)
        def _():
            reduce_core(near(s - 1))

        for before in (1, 2):

            @pl.when(s == before + 1)
            def _():
                v_step(before)

        ffn_grads(near(s))
        return carry

    lax.fori_loop(0, DEPTH, by_z, 0)
    x_out().wait_recv()
    x_out_core(c).start()
    reduce_core(near(3))
    v_step(3)
    v_merge(1)
    for zz in range(DEPTH):
        for side in range(2):
            row, start = 8 + 2 * side + zz // 2, zz % 2 * 512
            vout[0, row : row + 1, start : start + 512] = jnp.where(t == side, bias_sum[zz], 0.0)
    rows_t[...] = rows_one[...].T
    x_part(1).wait_recv()

    def row_sum(row, value):
        vout[0, row : row + 1, :] += jnp.sum(value, 0, keepdims=True)

    def second_back(at, step):
        here = pl.ds(at, step)
        in_group = pl.ds(pl.multiple_of(t * rows + at, step), step)
        grad = nacc[in_group, :] + inx[0, here, :].astype(f32)
        unit, inverse = norm(mixed[here, :])
        back = cot[here, :] + norm_grad(grad, unit, inverse, vecs[2:3, :])
        input_grad[here, :] = back
        grad_attn[in_group, :] = back.astype(bf)
        row_sum(2, grad * unit)
        row_sum(3, grad)
        row_sum(4, back)
        row_sum(5, cot[here, :])

    by_rows(second_back)
    early_rows(0)
    x_out_core(1 - c).wait_recv()
    ctx_x[...] = dot_nt(grad_attn[own, :], w_out(go_x)).astype(bf)
    x_grad_context().start()
    x_rows(grad_attn, 3).start()
    far[1] = macc[other, :].astype(bf)
    x_part(2).start()
    gctx[own, :] = dot_nt(grad_attn[own, :], w_out(go)).astype(bf)
    for k in (I, W):
        ry_add(k, 1)
    v_merge(2)
    v_cross()
    for zz in range(DEPTH):
        for yy in range(2):
            drain(O, zz, yy)
            drain(Q, zz, yy)
    def mixed_out(at, step):
        here = pl.ds(at, step)
        in_group = pl.ds(pl.multiple_of(t * rows + at, step), step)
        mixed[here, :] = mixed[here, :] + macc[in_group, :] + inx[1, here, :].astype(f32) + vecs[5:6, :]

    x_out().wait_send()
    x_grad_context_wait()

    def out_grads():
        x_rows_wait(grad_attn, 3)
        ctx_t = ctx[...].T
        for nb in range(4):
            at = slice(nb * 256, nb * 256 + 256)
            go[:, :, at] = dot(ctx_t, grad_attn[:, at]).astype(bf).reshape(8, 64, 256)
        for zz in range(DEPTH):
            for yy in range(2):
                rc_copy(O, zz, yy).start()

    def head_back(h):
        q0, q1 = qkv[h, 0:rows, 0:128], qkv[h, rows : 2 * rows, 0:128]
        grads = []
        for block in range(2):
            at, seen = slice(block * rows, (block + 1) * rows), (block + 1) * rows
            low = probs[h, at, 0:seen]
            given = gctx[at, h * 128 : h * 128 + 128]
            prob = low.astype(f32)
            grad_probs = dot_nt(given, qkv[h, 0:seen, 256:384])
            delta = jnp.sum(prob * grad_probs, -1, keepdims=True)
            grad_scores = (prob * (grad_probs - delta)).astype(bf)
            grad_q = dot(grad_scores, qkv[h, 0:seen, 128:256]) * scale
            grad_k = dot_tn(grad_scores, q1 if block else q0) * scale
            grad_v = dot_tn(low, given)
            grads.append((grad_q, grad_k, grad_v))
        (gq0, gk0, gv0), (gq1, gk1, gv1) = grads
        top = jnp.concatenate([gq0, gk0 + gk1[0:rows], gv0 + gv1[0:rows]], 1).astype(bf)
        low_half = jnp.concatenate([gq1, gk1[rows:], gv1[rows:]], 1).astype(bf)
        qkv[h, 0:rows, :] = top
        qkv[h, rows : 2 * rows, :] = low_half
        total = jnp.sum(top.astype(f32), 0, keepdims=True) + jnp.sum(low_half.astype(f32), 0, keepdims=True)
        for side in range(2):
            vout[0, 6 + side : 7 + side, h * 256 : h * 256 + 128] = jnp.where(t == side, total[:, 0:128], 0.0)
            vout[0, 6 + side : 7 + side, h * 256 + 128 : h * 256 + 256] = jnp.where(t == side, total[:, 256:384], 0.0)
        for half in (other, own):
            product = dot_nt(qkv[h, half, :], wqkv[h])
            if h == 0:
                nacc[half, :] = product
            else:
                nacc[half, :] += product
            if h == DEPTH - 1 and half is other:
                x_part(1).wait_send()
                far[0] = nacc[other, :].astype(bf)
                x_part(3).start()
        part = dot(rows_t[...], qkv[h]).astype(bf)
        disassemble(h, part)
        for yy in (1 - y, y):
            rc_copy(Q, h, yy).start()

    for h in range(DEPTH):
        head_back(h)
        if h < 3:
            early_rows(h + 1)
        if h > 0:
            for yy in (1 - y, y):
                rc_add(Q, h - 1, yy)
        if h == 0:
            out_grads()
        if h == 1:
            for yy in (1 - y, y):
                for s in range(DEPTH):
                    rc_add(O, near(s), yy)
            for k in (I, W):
                ry_add(k, 2)
                ry_merge(k, 1)
        if h == 2:
            for k in (I, W):
                ry_add(k, 3)
                ry_merge(k, 2)
    for yy in (1 - y, y):
        rc_add(Q, DEPTH - 1, yy)
    x_part(2).wait_recv()
    by_rows(mixed_out)
    for k in (I, W):
        own_total(k)
    z_total(V, y, total_of(V), y_landed(V, z))
    x_part(3).wait_recv()

    def first_back(at, step):
        here = pl.ds(at, step)
        in_group = pl.ds(pl.multiple_of(t * rows + at, step), step)
        grad = nacc[in_group, :] + inx[0, here, :].astype(f32)
        unit, inverse = norm(tokens[here, :])
        input_grad[here, :] = input_grad[here, :] + norm_grad(grad, unit, inverse, vecs[0:1, :])
        row_sum(0, grad * unit)
        row_sum(1, grad)

    by_rows(first_back)

    for row in range(4):
        for j in range(8):
            late[row * 8 + j : row * 8 + j + 1, :] = vout[0, (0, 1, 6, 7)[row] : (0, 1, 6, 7)[row] + 1, j * LANES : (j + 1) * LANES]
    here = t * 4 + y * 2 + c
    late_in[here] = late[...]
    for turn in range(1, 8):
        late_copy(turn).start()
    for s in (3, 2, 1):
        ry_add(O, s)
    ry_merge(O, 2)
    ry_merge(O, 1)
    for turn in range(1, 8):
        late_wait(late_turn(turn)[1])
    total = late_in[0]
    for index in range(1, 8):
        total = total + late_in[index]
    late_sum[...] = total
    late_in[8 + z] = total
    for step in range(1, DEPTH):
        late_z(step).start()
    for s in (3, 2, 1):
        ry_add(Q, s)
    ry_merge(Q, 2)
    ry_merge(Q, 1)
    own_total(O)
    own_total(Q)
    for step in range(1, DEPTH):
        late_wait(8 + lax.rem(z + step, DEPTH))
    total = ((late_in[8] + late_in[9]) + late_in[10]) + late_in[11]
    for step in range(1, DEPTH):
        zz = lax.rem(z + step, DEPTH)
        remote(vin.at[3 + zz], vin.at[3 + zz], v_send.at[0], v_recv.at[3 + zz], y_peer).wait_recv()
    early = ((vin[3] + vin[4]) + vin[5]) + vin[6]
    vec_grads[...] = early[0 : vec_grads.shape[0]]
    for row in range(4):
        for j in range(8):
            vec_grads[(0, 1, 6, 7)[row] : (0, 1, 6, 7)[row] + 1, j * LANES : (j + 1) * LANES] = total[row * 8 + j : row * 8 + j + 1, :]

    for stage in range(3):
        v_copy(stage).wait_send()
    for turn in range(1, 8):
        late_copy(turn).wait_send()
    for step in range(1, DEPTH):
        vz_copy(step).wait_send()
        late_z(step).wait_send()
    for index, ref in enumerate((rows_one, grad_rows, rows_two, grad_attn)):
        x_rows(ref, index).wait_send()
    for index in (2, 3):
        x_part(index).wait_send()
    x_out_core(c).wait_send()
    x_grad_context().wait_send()
    for k in range(4):
        for zz in range(DEPTH):
            for yy in range(2):
                rc_copy(k, zz, yy).wait_send()
            ry_copy(k, zz).wait_send()
        for s in range(1, DEPTH):
            rz_copy(k, s, y, True).wait_send()
    ry_copy(V, z).wait_send()
    for yy in range(2):
        for s in range(1, DEPTH):
            rz_copy(V, s, yy, True).wait_send()


def run_layer(tokens, cotangent, lengths, order, weights, vec_params):
    bf, f32 = jnp.bfloat16, jnp.float32
    rows = tokens.shape[0]
    group = 2 * rows
    owners = 16
    shapes = piece_shapes()
    view = jnp.transpose(weights, (1, 2, 0))
    vmem = pl.BlockSpec(memory_space=pltpu.VMEM)
    smem = pl.BlockSpec(memory_space=pltpu.SMEM)

    halved = shapes[:3] + ((HALF, D),)

    def many(count, kinds):
        return [pltpu.VMEM((count,) + s, bf) for s in kinds]

    full = pltpu.VMEM((group, D), bf)
    dma = pltpu.SemaphoreType.DMA
    return pl.pallas_call(
        layer_kernel,
        out_shape=[jax.ShapeDtypeStruct((rows, D), f32)] * 2
        + [jax.ShapeDtypeStruct(s, f32) for s in shapes]
        + [jax.ShapeDtypeStruct(vec_params.shape, f32)],
        in_specs=[smem, smem, pl.BlockSpec(memory_space=pl.ANY)] + [vmem] * 3,
        out_specs=[vmem] * 7,
        scratch_shapes=[
            pltpu.VMEM((owners,) + shapes[0], bf),
            pltpu.VMEM((owners // 2, BLOCK, D), bf),
            pltpu.VMEM((owners,) + shapes[2], bf),
            pltpu.VMEM((owners,) + shapes[3], bf),
            pltpu.VMEM((DEPTH, D, 3 * HD), bf),
        ]
        + many(2 * DEPTH, shapes)
        + many(DEPTH, halved)
        + many(1, halved[3:])
        + many(DEPTH, halved)
        + many(2 * DEPTH, halved[3:])
        + [
            full,
            full,
            pltpu.VMEM((D, group), bf),
            full,
            full,
            pltpu.VMEM((DEPTH, group, group), bf),
            pltpu.VMEM((DEPTH, group, 3 * HD), bf),
            pltpu.VMEM((group, DEPTH * HD), bf),
            pltpu.VMEM((group, DEPTH * HD), bf),
            pltpu.VMEM((2, rows, D), bf),
            pltpu.VMEM((2, rows, D), bf),
            pltpu.VMEM((owners // 2, BLOCK, D), bf),
            pltpu.VMEM((rows, DEPTH * HD), bf),
            pltpu.VMEM((group, D), f32),
            pltpu.VMEM((group, D), f32),
            pltpu.VMEM((group, 2 * D), bf),
            pltpu.VMEM((group, 2 * D), bf),
            pltpu.VMEM((DEPTH, 1, 512), f32),
            pltpu.VMEM((DEPTH, 1, 3 * HD), f32),
            pltpu.VMEM((7, 16, D), f32),
            pltpu.VMEM((5, 16, D), f32),
            pltpu.VMEM((32, LANES), f32),
            pltpu.VMEM((32, LANES), f32),
            pltpu.VMEM((12, 32, LANES), f32),
            dma((5, owners)),
            dma((5, DEPTH)),
            dma((5, 2 * DEPTH)),
            dma((5, 2, 2 * DEPTH)),
            dma((4, 2 * DEPTH)),
            dma((4, 2 * DEPTH)),
            dma((5, DEPTH)),
            dma((5, DEPTH)),
            dma((5, 2 * DEPTH)),
            dma((5, 2 * DEPTH)),
            dma((11,)),
            dma((11,)),
            dma((6,)),
            dma((7,)),
            dma((11,)),
            dma((12,)),
            dma((1,)),
        ],
        compiler_params=pltpu.CompilerParams(
            collective_id=0, has_side_effects=True, vmem_limit_bytes=VMEM_LIMIT
        ),
        name="layer",
    )(lengths, order, view, tokens, cotangent, vec_params)


def per_device(
    grp_count,
    tp_count,
    tokens,
    cotangent,
    lengths,
    order,
    weights,
    momentum,
    stat_left,
    stat_right,
    root_left,
    root_right,
    vec_params,
    vec_momentum,
    vec_second,
):
    fits = grp_count == 4 * DEPTH and tp_count == 2 and tokens.shape[0] == 256
    if not fits or lengths.shape[1] != ARTICLES:
        return per_device_general(
            tokens,
            cotangent,
            lengths,
            order,
            weights,
            momentum,
            stat_left,
            stat_right,
            root_left,
            root_right,
            vec_params,
            vec_momentum,
            vec_second,
        )
    token_total = tokens.shape[0] * tp_count * grp_count
    mixed, input_grad, *sums, vec_grads = run_layer(tokens, cotangent, lengths, order, weights, vec_params)
    blocks, vecs, results = update_blocks(
        sums,
        (weights, momentum, stat_left, stat_right, root_left, root_right),
        vec_grads,
        (vec_params, vec_momentum, vec_second),
        (mixed, input_grad),
        token_total,
    )
    return (*results, *blocks, *vecs)


def solution(mesh):
    placed = (
        P(("grp", "tp"), None),
        P(("grp", "tp"), None),
        P("grp", None),
        P("grp", None),
        P(("tp", "grp"), None, None),
        P(("tp", "grp"), None, None),
        P(("tp", "grp"), None, None),
        P(("tp", "grp"), None, None),
        P(("tp", "grp"), None, None),
        P(("tp", "grp"), None, None),
        P(),
        P(),
        P(),
    )
    return jax.shard_map(
        functools.partial(per_device, mesh.shape["grp"], mesh.shape["tp"]),
        mesh=mesh,
        in_specs=placed,
        out_specs=(
            P(("grp", "tp"), None),
            P(("grp", "tp"), None),
            P(("tp", "grp"), None, None),
            P(("tp", "grp"), None, None),
            P(("tp", "grp"), None, None),
            P(("tp", "grp"), None, None),
            P(("tp", "grp"), None, None),
            P(),
            P(),
            P(),
            P(),
        ),
        check_vma=False,
    )
```

```python
import functools

import jax
import jax.numpy as jnp
from jax import lax
from jax.experimental import pallas as pl
from jax.experimental.pallas import tpu as pltpu
from jax.sharding import PartitionSpec as P

D = 1024
HEADS = 8
HD = 128
FF = 4096
BLOCK = 64


EPS = 1e-05
NEG = -1e30
DECAY = 0.9
BETA = 0.9
RATE = 0.05
VEC_DECAY = 0.9
VEC_RATE = 0.2
VEC_EPS = 1e-08


def norm_rows(value, gain, shift):
    average = jnp.mean(value, -1, keepdims=True)
    centred = value - average
    inverse = lax.rsqrt(jnp.mean(centred * centred, -1, keepdims=True) + EPS)
    normed = centred * inverse
    return (normed * gain + shift, normed, inverse)


def norm_back(grad_out, normed, inverse, gain):
    scaled = grad_out * gain
    return inverse * (
        scaled
        - jnp.mean(scaled, -1, keepdims=True)
        - normed * jnp.mean(scaled * normed, -1, keepdims=True)
    )


def segment_ids(lengths_row, order_row, group_rows):
    article_count = lengths_row.shape[0]
    slots = jnp.arange(article_count, dtype=jnp.int32)
    picks = (order_row[:, None] == slots[None, :]).astype(jnp.int32)
    packed = jnp.sum(picks * lengths_row[None, :], 1)
    ends = jnp.cumsum(packed)
    spots = jnp.arange(group_rows, dtype=jnp.int32)
    return jnp.sum((spots[:, None] >= ends[None, :]).astype(jnp.int32), 1)


def allowed_mask(row_ids, row_segs, segments, key_ids, article_count):
    causal = key_ids[None, :] <= row_ids[:, None]
    same = segments[None, :] == row_segs[:, None]
    alone = (row_segs[:, None] < article_count) | (key_ids[None, :] == row_ids[:, None])
    return causal & same & alone


def from_columns(tiles, row_total, col_total):
    return (
        tiles.reshape(col_total // BLOCK, row_total // BLOCK, BLOCK, BLOCK)
        .transpose(1, 2, 0, 3)
        .reshape(row_total, col_total)
    )


def from_rows(tiles, row_total, col_total):
    return (
        tiles.reshape(row_total // BLOCK, col_total // BLOCK, BLOCK, BLOCK)
        .transpose(0, 2, 1, 3)
        .reshape(row_total, col_total)
    )


def to_columns(matrix):
    row_total, col_total = matrix.shape
    return (
        matrix.reshape(row_total // BLOCK, BLOCK, col_total // BLOCK, BLOCK)
        .transpose(2, 0, 1, 3)
        .reshape(-1, BLOCK, BLOCK)
    )


def to_rows(matrix):
    row_total, col_total = matrix.shape
    return (
        matrix.reshape(row_total // BLOCK, BLOCK, col_total // BLOCK, BLOCK)
        .transpose(0, 2, 1, 3)
        .reshape(-1, BLOCK, BLOCK)
    )


def per_device_general(
    tokens,
    cotangent,
    lengths,
    order,
    weights,
    momentum,
    stat_left,
    stat_right,
    root_left,
    root_right,
    vec_params,
    vec_momentum,
    vec_second,
):
    groups = lax.axis_size("grp")
    tp_size = lax.axis_size("tp")
    tp_rank = lax.axis_index("tp")
    tok_rows = tokens.shape[0]
    group_rows = tok_rows * tp_size
    article_count = lengths.shape[1]
    owners = groups * tp_size
    block_area = BLOCK * BLOCK * owners
    qkv_count = 3 * D * D // block_area
    out_count = D * D // block_area
    in_count = D * FF // block_area
    owned_blocks = weights.shape[0]
    heads_here = HEADS // tp_size
    qkv_cols = 3 * D // tp_size
    feat_here = D // tp_size
    ff_here = FF // tp_size
    qv_width = 2 * D // tp_size
    token_total = group_rows * groups
    gathered = lax.all_gather(weights.astype(jnp.bfloat16), "grp", axis=0, tiled=True)
    per_owner = gathered.reshape(groups, owned_blocks, BLOCK, BLOCK)
    marks = [0, qkv_count, qkv_count + out_count, qkv_count + out_count + in_count, owned_blocks]
    pieces = [
        per_owner[:, marks[index] : marks[index + 1]].reshape(-1, BLOCK, BLOCK)
        for index in range(4)
    ]
    w_qkv = from_columns(pieces[0], D, qkv_cols)
    w_out = from_rows(pieces[1], feat_here, D)
    w_in = from_columns(pieces[2], D, ff_here)
    w_down = from_rows(pieces[3], ff_here, D)
    w_qkv_heads = w_qkv.reshape(D, heads_here, 3, HD)
    w_out_heads = w_out.reshape(heads_here, HD, D)
    segments = segment_ids(lengths[0], order[0], group_rows)
    gain_one = vec_params[0]
    shift_one = vec_params[1]
    gain_two = vec_params[2]
    shift_two = vec_params[3]
    bias_out = vec_params[4]
    bias_down = vec_params[5]
    qv_here = lax.dynamic_slice_in_dim(
        vec_params[6:8].reshape(2 * D), tp_rank * qv_width, qv_width
    ).reshape(heads_here, 2, HD)
    bias_heads = jnp.stack(
        [qv_here[:, 0], jnp.zeros((heads_here, HD), jnp.float32), qv_here[:, 1]], 0
    )[:, :, None, :]
    bias_in = lax.dynamic_slice_in_dim(vec_params[8:].reshape(FF), tp_rank * ff_here, ff_here)
    normed_one, unit_one, inverse_one = norm_rows(tokens, gain_one, shift_one)
    rows_one = lax.all_gather(normed_one.astype(jnp.bfloat16), "tp", axis=0, tiled=True)
    projected = (
        jnp.einsum("rx,xhcd->chrd", rows_one, w_qkv_heads, preferred_element_type=jnp.float32)
        + bias_heads
    ).astype(jnp.bfloat16)
    queries = projected[0]
    keys_all = projected[1]
    values_all = projected[2]
    span = min(512, group_rows)
    starts = jnp.arange(group_rows // span, dtype=jnp.int32) * span
    key_ids = jnp.arange(group_rows, dtype=jnp.int32)
    score_scale = HD ** (-0.5)

    def masked_scores(first_row):
        row_ids = first_row + jnp.arange(span, dtype=jnp.int32)
        row_segs = lax.dynamic_slice_in_dim(segments, first_row, span, 0)
        allowed = allowed_mask(row_ids, row_segs, segments, key_ids, article_count)
        query_rows = lax.dynamic_slice_in_dim(queries, first_row, span, 1)
        scores = (
            jnp.einsum("hqd,hkd->hqk", query_rows, keys_all, preferred_element_type=jnp.float32)
            * score_scale
        )
        return (jnp.where(allowed[None], scores, NEG), query_rows)

    def attend(context_buf, first_row):
        scores, query_rows = masked_scores(first_row)
        row_max = jnp.max(scores, -1, keepdims=True)
        expo = jnp.exp(scores - row_max)
        expsum = jnp.sum(expo, -1, keepdims=True)
        probs_low = (expo / expsum).astype(jnp.bfloat16)
        context = jnp.einsum(
            "hqk,hkd->hqd", probs_low, values_all, preferred_element_type=jnp.float32
        ).astype(jnp.bfloat16)
        context_buf = lax.dynamic_update_slice_in_dim(context_buf, context, first_row, 1)
        return (context_buf, (row_max + jnp.log(expsum))[:, :, 0])

    context_low, log_norm = lax.scan(
        attend, jnp.zeros((heads_here, group_rows, HD), jnp.bfloat16), starts
    )
    attn_sum = lax.psum_scatter(
        jnp.einsum(
            "hrd,hde->re", context_low, w_out_heads, preferred_element_type=jnp.float32
        ).astype(jnp.bfloat16),
        "tp",
        scatter_dimension=0,
        tiled=True,
    ).astype(jnp.float32)
    hidden = tokens + attn_sum + bias_out
    normed_two, unit_two, inverse_two = norm_rows(hidden, gain_two, shift_two)
    rows_two = lax.all_gather(normed_two.astype(jnp.bfloat16), "tp", axis=0, tiled=True)
    inner = jnp.dot(rows_two, w_in, preferred_element_type=jnp.float32) + bias_in
    activ, gelu_pull = jax.vjp(jax.nn.gelu, inner)
    activ_low = activ.astype(jnp.bfloat16)
    mixed = (
        hidden
        + lax.psum_scatter(
            jnp.dot(activ_low, w_down, preferred_element_type=jnp.float32).astype(jnp.bfloat16),
            "tp",
            scatter_dimension=0,
            tiled=True,
        ).astype(jnp.float32)
        + bias_down
    )
    grad_low = cotangent.astype(jnp.bfloat16)
    grad_rows = lax.all_gather(grad_low, "tp", axis=0, tiled=True)
    g_down = jnp.einsum("rf,rd->fd", activ_low, grad_rows, preferred_element_type=jnp.float32)
    grad_activ = jnp.einsum("rd,fd->rf", grad_rows, w_down, preferred_element_type=jnp.float32)
    grad_inner = gelu_pull(grad_activ)[0].astype(jnp.bfloat16)
    g_in = jnp.einsum("rd,rf->df", rows_two, grad_inner, preferred_element_type=jnp.float32)
    g_bias_in = jnp.sum(grad_inner.astype(jnp.float32), 0)
    ffn_blocks = jnp.concatenate(
        [
            to_columns(g_in).reshape(groups, in_count, BLOCK, BLOCK),
            to_rows(g_down).reshape(groups, in_count, BLOCK, BLOCK),
        ],
        1,
    )
    grad_normed_two = lax.psum_scatter(
        jnp.einsum("rf,df->rd", grad_inner, w_in, preferred_element_type=jnp.float32).astype(
            jnp.bfloat16
        ),
        "tp",
        scatter_dimension=0,
        tiled=True,
    ).astype(jnp.float32)
    grad_hidden = cotangent + norm_back(grad_normed_two, unit_two, inverse_two, gain_two)
    grad_attn_low = grad_hidden.astype(jnp.bfloat16)
    grad_attn_rows = lax.all_gather(grad_attn_low, "tp", axis=0, tiled=True)
    g_out = jnp.einsum(
        "hrd,re->hde", context_low, grad_attn_rows, preferred_element_type=jnp.float32
    ).reshape(feat_here, D)
    grad_context = jnp.einsum(
        "re,hde->hrd", grad_attn_rows, w_out_heads, preferred_element_type=jnp.float32
    ).astype(jnp.bfloat16)
    zero_heads = jnp.zeros((heads_here, group_rows, HD), jnp.float32)

    def attend_back(carry, inputs):
        grad_queries, grad_keys, grad_values = carry
        first_row, log_block = inputs
        scores, query_rows = masked_scores(first_row)
        probs = jnp.exp(scores - log_block[:, :, None])
        grad_ctx_rows = lax.dynamic_slice_in_dim(grad_context, first_row, span, 1)
        grad_probs = jnp.einsum(
            "hqd,hkd->hqk", grad_ctx_rows, values_all, preferred_element_type=jnp.float32
        )
        delta = jnp.sum(probs * grad_probs, -1, keepdims=True)
        grad_scores = (probs * (grad_probs - delta)).astype(jnp.bfloat16)
        query_part = (
            jnp.einsum("hqk,hkd->hqd", grad_scores, keys_all, preferred_element_type=jnp.float32)
            * score_scale
        )
        grad_queries = lax.dynamic_update_slice_in_dim(grad_queries, query_part, first_row, 1)
        grad_keys = (
            grad_keys
            + jnp.einsum(
                "hqk,hqd->hkd", grad_scores, query_rows, preferred_element_type=jnp.float32
            )
            * score_scale
        )
        grad_values = grad_values + jnp.einsum(
            "hqk,hqd->hkd",
            probs.astype(jnp.bfloat16),
            grad_ctx_rows,
            preferred_element_type=jnp.float32,
        )
        return ((grad_queries, grad_keys, grad_values), None)

    (grad_queries, grad_keys, grad_values), unused = lax.scan(
        attend_back, (zero_heads, zero_heads, zero_heads), (starts, log_norm)
    )
    grad_proj = jnp.stack([grad_queries, grad_keys, grad_values], 0).astype(jnp.bfloat16)
    proj_sums = jnp.sum(grad_proj.astype(jnp.float32), 2)
    g_bias_qv = jnp.stack([proj_sums[0], proj_sums[2]], 1).reshape(qv_width)
    g_qkv = jnp.einsum(
        "rx,chrd->xhcd", rows_one, grad_proj, preferred_element_type=jnp.float32
    ).reshape(D, qkv_cols)
    grad_normed_one = lax.psum_scatter(
        jnp.einsum(
            "chrd,xhcd->rx", grad_proj, w_qkv_heads, preferred_element_type=jnp.float32
        ).astype(jnp.bfloat16),
        "tp",
        scatter_dimension=0,
        tiled=True,
    ).astype(jnp.float32)
    input_grad = grad_hidden + norm_back(grad_normed_one, unit_one, inverse_one, gain_one)
    local_rows = jnp.stack(
        [
            jnp.sum(grad_normed_one * unit_one, 0),
            jnp.sum(grad_normed_one, 0),
            jnp.sum(grad_normed_two * unit_two, 0),
            jnp.sum(grad_normed_two, 0),
            jnp.sum(grad_hidden, 0),
            jnp.sum(cotangent, 0),
        ]
    )
    qv_rows = lax.dynamic_update_slice(
        jnp.zeros((2 * D,), jnp.float32), g_bias_qv, (tp_rank * qv_width,)
    ).reshape(2, D)
    in_rows = lax.dynamic_update_slice(
        jnp.zeros((FF,), jnp.float32), g_bias_in, (tp_rank * ff_here,)
    ).reshape(FF // D, D)
    vec_grads = lax.psum(jnp.concatenate([local_rows, qv_rows, in_rows], 0), ("grp", "tp"))
    attn_blocks = jnp.concatenate(
        [
            to_columns(g_qkv).reshape(groups, qkv_count, BLOCK, BLOCK),
            to_rows(g_out).reshape(groups, out_count, BLOCK, BLOCK),
        ],
        1,
    )
    every_block = jnp.concatenate([attn_blocks, ffn_blocks], 1).reshape(-1, BLOCK, BLOCK)
    weight_grads = lax.psum_scatter(
        every_block.astype(jnp.bfloat16), "grp", scatter_dimension=0, tiled=True
    ).astype(jnp.float32)
    scaled = weight_grads * token_total ** (-0.5)
    stat_left_new = DECAY * stat_left + (1.0 - DECAY) * jnp.einsum(
        "nij,nkj->nik", scaled, scaled, precision=lax.Precision.HIGHEST
    )
    stat_right_new = DECAY * stat_right + (1.0 - DECAY) * jnp.einsum(
        "nji,njk->nik", scaled, scaled, precision=lax.Precision.HIGHEST
    )
    shaped = jnp.einsum("nij,njk->nik", root_left, scaled, precision=lax.Precision.HIGHEST)
    shaped = jnp.einsum("nij,njk->nik", shaped, root_right, precision=lax.Precision.HIGHEST)
    momentum_new = BETA * momentum + shaped
    weights_new = weights - RATE * momentum_new
    vec_scaled = vec_grads * token_total ** (-0.5)
    vec_second_new = VEC_DECAY * vec_second + (1.0 - VEC_DECAY) * vec_scaled * vec_scaled
    vec_momentum_new = BETA * vec_momentum + vec_scaled * lax.rsqrt(vec_second_new + VEC_EPS)
    vec_new = vec_params - VEC_RATE * vec_momentum_new
    return (
        mixed,
        input_grad,
        weight_grads,
        stat_left_new,
        stat_right_new,
        momentum_new,
        weights_new,
        vec_grads,
        vec_second_new,
        vec_momentum_new,
        vec_new,
    )


MESH_ID = pl.DeviceIdType.MESH
LANES = 128
HALF = 64
VMEM_LIMIT = 62 * 2**20
ARTICLES = 4
GELU_A = (2.0 / 3.141592653589793) ** 0.5
GELU_B = 0.044715


def remote(src, dst, send_sem, recv_sem, device):
    return pltpu.make_async_remote_copy(
        src_ref=src,
        dst_ref=dst,
        send_sem=send_sem,
        recv_sem=recv_sem,
        device_id=device,
        device_id_type=MESH_ID,
    )


def place():
    grp = lax.axis_index("grp")
    return lax.div(grp, 4), lax.rem(lax.div(grp, 2), 2), lax.rem(grp, 2), lax.axis_index("tp")


def slot_of(z, y, c):
    return z * 4 + y * 2 + c


def lay_blocks(view_ref, stack):
    half = view_ref.shape[2] // 2

    def row(i, carry):
        tile = view_ref[i].T
        stack[pl.ds(i, half, stride=BLOCK), :] = jnp.concatenate([tile[:half], tile[half:]], 1)
        return carry

    lax.fori_loop(0, BLOCK, row, 0, unroll=8)


def piece_shapes():
    return ((768, LANES), (64, 512), (1024, LANES), (LANES, 1024))


def fold_tiles(value, mask):
    kept = jnp.where(mask, value, 0.0)
    halves = kept[:, :LANES] + kept[:, LANES:]
    return halves + pltpu.roll(halves, HALF, 1)


def update_kernel(
    scale,
    sum_q,
    sum_o,
    sum_i,
    sum_d,
    root_l,
    root_r,
    vec_g,
    vecs,
    vec_m,
    vec_s,
    mixed,
    input_grad,
    w,
    m,
    sl,
    sr,
    out_g,
    out_sl,
    out_sr,
    out_m,
    out_w,
    out_vg,
    out_vs,
    out_vm,
    out_v,
    out_mixed,
    out_input_grad,
    first,
    second,
):
    count = root_l.shape[2]
    bf = jnp.bfloat16
    out_mixed[...] = mixed[...]
    out_input_grad[...] = input_grad[...]

    @pl.when(pl.program_id(0) == 0)
    def _():
        total = vec_g[...]
        out_vg[...] = total
        scaled = total * scale
        fresh = VEC_DECAY * vec_s[...] + (1.0 - VEC_DECAY) * scaled * scaled
        out_vs[...] = fresh
        momentum = BETA * vec_m[...] + scaled * lax.rsqrt(fresh + VEC_EPS)
        out_vm[...] = momentum
        out_v[...] = vecs[...] - VEC_RATE * momentum
        rows = sum_q.shape[0]
        first[0:rows, 0:HALF] = sum_q[:, 0:HALF]
        first[rows : 2 * rows, 0:HALF] = sum_q[:, HALF:LANES]
        base = 2 * rows
        for b in range(8):
            first[base + b * 64 : base + b * 64 + 64, 0:HALF] = sum_o[:, b * HALF : (b + 1) * HALF]
        base += 512
        first[base : base + 1024, 0:HALF] = sum_i[:, 0:HALF]
        first[base + 1024 : base + 2048, 0:HALF] = sum_i[:, HALF:LANES]
        base += 2048
        for r in range(2):
            for b in range(16):
                at = base + (r * 16 + b) * 64
                first[at : at + 64, 0:HALF] = sum_d[r * 64 : r * 64 + 64, b * HALF : (b + 1) * HALF]

        def row(i, carry):
            both = jnp.concatenate([root_l[i], root_r[i]], 0)
            second[pl.ds(i, count, stride=BLOCK), :] = both.T
            return carry

        lax.fori_loop(0, BLOCK, row, 0, unroll=8)
        row_id = lax.broadcasted_iota(jnp.int32, (256, 256), 0)
        col_id = lax.broadcasted_iota(jnp.int32, (256, 256), 1)
        mask = lax.shift_right_logical(row_id, 6) == lax.shift_right_logical(col_id, 6)
        zero = jnp.zeros((256, 256), jnp.float32)

        def spread(v):
            return jnp.where(mask, jnp.concatenate([v, v, v, v], 1), zero).astype(bf)

        def four(k, carry):
            at = pl.ds(pl.multiple_of(k * 256, 256), 256)
            s32 = first[at, 0:HALF] * scale
            s = s32.astype(bf)
            left = second[at, 0:HALF]
            right = second[at, HALF:LANES].astype(bf)
            outer = lax.dot_general(s, s, (((1,), (1,)), ((), ())), preferred_element_type=jnp.float32)
            inner = lax.dot_general(spread(s32), s, (((0,), (0,)), ((), ())), preferred_element_type=jnp.float32)
            shaped = jnp.dot(spread(left), s, preferred_element_type=jnp.float32)
            shaped = jnp.dot(spread(shaped), right, preferred_element_type=jnp.float32)
            first[at, HALF:LANES] = fold_tiles(outer, mask)[:, HALF:LANES]
            second[at, 0:HALF] = inner
            second[at, HALF:LANES] = shaped
            return carry

        lax.fori_loop(0, count // 4, four, 0, unroll=4)

    i0 = pl.program_id(0) * w.shape[0]

    def rows_out(ii, carry):
        at = pl.ds(i0 + ii, count, stride=BLOCK)
        one = first[at, :].T
        two = second[at, :].T
        out_g[ii] = one[0:HALF]
        out_sl[ii] = DECAY * sl[ii] + (1.0 - DECAY) * one[HALF:LANES]
        out_sr[ii] = DECAY * sr[ii] + (1.0 - DECAY) * two[0:HALF]
        fresh = BETA * m[ii] + two[HALF:LANES]
        out_m[ii] = fresh
        out_w[ii] = w[ii] - RATE * fresh
        return carry

    lax.fori_loop(0, w.shape[0], rows_out, 0, unroll=True)


def update_blocks(sums, blocks, vec_grads, vecs, results, token_total):
    views = [jnp.transpose(a, (1, 2, 0)) for a in blocks]
    count = blocks[0].shape[0]
    rows = 8
    whole = pl.BlockSpec(memory_space=pltpu.VMEM)
    steps = BLOCK // rows
    some = pl.BlockSpec((results[0].shape[0] // steps, results[0].shape[1]), lambda i: (i, 0))
    part = pl.BlockSpec((rows, BLOCK, count), lambda i: (i, 0, 0))
    vec = jax.ShapeDtypeStruct(vec_grads.shape, jnp.float32)
    outs = pl.pallas_call(
        functools.partial(update_kernel, token_total ** (-0.5)),
        grid=(steps,),
        out_shape=[jax.ShapeDtypeStruct((BLOCK, BLOCK, count), jnp.float32)] * 5
        + [vec] * 4
        + [jax.ShapeDtypeStruct(a.shape, a.dtype) for a in results],
        in_specs=[whole] * 10 + [some] * 2 + [part] * 4,
        out_specs=[part] * 5 + [whole] * 4 + [some] * 2,
        scratch_shapes=[
            pltpu.VMEM((count * BLOCK, LANES), jnp.float32),
            pltpu.VMEM((count * BLOCK, LANES), jnp.float32),
        ],
        compiler_params=pltpu.CompilerParams(vmem_limit_bytes=VMEM_LIMIT),
        name="update_blocks",
    )(*sums, *views[4:], vec_grads, *vecs, *results, *views[:4])
    return [jnp.transpose(a, (2, 0, 1)) for a in outs[:5]], outs[5:9], outs[9:]


DEPTH = 4


def layer_kernel(
    lengths,
    order,
    view,
    tokens,
    cot,
    vecs,
    mixed,
    input_grad,
    sum_q,
    sum_o,
    sum_i,
    sum_d,
    vec_grads,
    gq,
    go,
    gi,
    gd,
    wqkv,
    cq,
    co,
    ci,
    cd,
    yq,
    yo,
    yi,
    yd,
    yv,
    zq,
    zo,
    zi,
    zd,
    zv,
    rows_one,
    rows_two,
    rows_t,
    grad_rows,
    grad_attn,
    probs,
    qkv,
    ctx,
    gctx,
    far,
    inx,
    go_x,
    ctx_x,
    macc,
    nacc,
    act,
    gin,
    bias_sum,
    qkv_bias,
    vin,
    vout,
    late,
    late_sum,
    late_in,
    recv,
    send_y,
    send_c,
    send_z,
    rc_recv,
    rc_send,
    ry_recv,
    ry_send,
    rz_recv,
    rz_send,
    x_send,
    x_recv,
    v_send,
    v_recv,
    l_send,
    l_recv,
    copy_sem,
):
    bf, f32 = jnp.bfloat16, jnp.float32
    z, y, c, t = place()
    me = slot_of(z, y, c)
    x_peer = (me, 1 - t)
    y_peer = (slot_of(z, 1 - y, c), t)
    c_peer = (slot_of(z, y, 1 - c), t)
    rows = tokens.shape[0]
    own = pl.ds(pl.multiple_of(t * rows, rows), rows)
    other = pl.ds(pl.multiple_of((1 - t) * rows, rows), rows)

    def lanes(start, size, unit):
        return pl.ds(pl.multiple_of(start, unit), size)

    gathered, core_in = (gq, go, gi, gd), (cq, co, ci, cd)
    y_in, z_in = (yq, yo, yi, yd, yv), (zq, zo, zi, zd, zv)
    sums = (sum_q, sum_o, sum_i, sum_d)
    Q, O, I, W, V = range(5)

    def dot(a, b):
        return jnp.dot(a, b, preferred_element_type=f32)

    def dot_nt(a, b):
        return lax.dot_general(a, b, (((1,), (1,)), ((), ())), preferred_element_type=f32)

    def dot_tn(a, b):
        return lax.dot_general(a, b, (((0,), (0,)), ((), ())), preferred_element_type=f32)

    def piece(k, zz, yy, cc):
        if k == O:
            return go.at[zz * 2 + yy, :, pl.ds(pl.multiple_of(cc * 512, 512), 512)]
        return gathered[k].at[slot_of(zz, yy, cc)]

    def near(s):
        return lax.rem(z + (1 - 2 * lax.div(z, 2)) * s + DEPTH, DEPTH)

    def ag_piece(k, zz, yy, cc):
        if k == W:
            return gd.at[slot_of(zz, yy, cc), 0:HALF]
        if k == V:
            return gd.at[slot_of(zz, yy, cc), HALF:LANES]
        return piece(k, zz, yy, cc)

    def ag_copy(k, zz, yy, way):
        src = ag_piece(k, zz, yy, c)
        sem = recv.at[k, slot_of(zz, yy, c)]
        if way == "up":
            return remote(src, src, send_z.at[k, 0, yy * DEPTH + zz], sem, (slot_of(z + 1, y, c), t))
        if way == "down":
            return remote(src, src, send_z.at[k, 1, yy * DEPTH + zz], sem, (slot_of(z - 1, y, c), t))
        if way == "y":
            return remote(src, src, send_y.at[k, zz], sem, y_peer)
        return remote(src, src, send_c.at[k, yy * DEPTH + zz], sem, c_peer)

    def ag_wait(k, zz, yy, cc):
        ref = ag_piece(k, zz, yy, cc)
        remote(ref, ref, send_y.at[k, 0], recv.at[k, slot_of(zz, yy, cc)], y_peer).wait_recv()

    def own_sends_z(k):
        @pl.when(z < DEPTH - 1)
        def _():
            ag_copy(k, z, y, "up").start()

        @pl.when(z > 0)
        def _():
            ag_copy(k, z, y, "down").start()

        ag_copy(k, z, y, "core").start()

    def own_sends_y(k):
        ag_copy(k, z, y, "y").start()

    def z_arrival(kinds, dist):
        @pl.when(z >= dist)
        def _():
            for k in kinds:
                ag_wait(k, z - dist, y, c)

                @pl.when(z < DEPTH - 1)
                def _():
                    ag_copy(k, z - dist, y, "up").start()

                ag_copy(k, z - dist, y, "y").start()
                ag_copy(k, z - dist, y, "core").start()

        @pl.when(z + dist < DEPTH)
        def _():
            for k in kinds:
                ag_wait(k, z + dist, y, c)

                @pl.when(z > 0)
                def _():
                    ag_copy(k, z + dist, y, "down").start()

                ag_copy(k, z + dist, y, "y").start()
                ag_copy(k, z + dist, y, "core").start()

    def y_arrival(kinds, dist):
        def one(zz):
            for k in kinds:
                ag_wait(k, zz, 1 - y, c)
                ag_copy(k, zz, 1 - y, "core").start()

        if dist == 0:
            one(z)
            return

        @pl.when(z >= dist)
        def _():
            one(z - dist)

        @pl.when(z + dist < DEPTH)
        def _():
            one(z + dist)

    def v_forward(zz, yy):
        ag_wait(V, zz, yy, c)

        @pl.when((zz <= z) & (z < DEPTH - 1))
        def _():
            ag_copy(V, zz, yy, "up").start()

        @pl.when((zz >= z) & (z > 0))
        def _():
            ag_copy(V, zz, yy, "down").start()

        ag_copy(V, zz, yy, "core").start()

    def v_arrival(dist):
        for yy in (y, 1 - y):

            @pl.when(z >= dist)
            def _():
                v_forward(z - dist, yy)

            @pl.when(z + dist < DEPTH)
            def _():
                v_forward(z + dist, yy)

    def drain(k, zz, yy):
        ag_copy(k, zz, yy, "core").wait_send()
        if k == V:

            @pl.when((yy == y) & (zz == z))
            def _():
                ag_copy(k, zz, yy, "y").wait_send()

            @pl.when((zz <= z) & (z < DEPTH - 1))
            def _():
                ag_copy(k, zz, yy, "up").wait_send()

            @pl.when((zz >= z) & (z > 0))
            def _():
                ag_copy(k, zz, yy, "down").wait_send()

            return

        @pl.when(yy == y)
        def _():
            ag_copy(k, zz, y, "y").wait_send()

            @pl.when((zz <= z) & (z < DEPTH - 1))
            def _():
                ag_copy(k, zz, y, "up").wait_send()

            @pl.when((zz >= z) & (z > 0))
            def _():
                ag_copy(k, zz, y, "down").wait_send()

    def add(dst, *terms):
        count, width = dst.shape
        step = min(count, 256 * LANES // width)

        def body(i, carry):
            at = pl.ds(pl.multiple_of(i * step, 16), step)
            total = terms[0][at, :].astype(f32)
            for term in terms[1:]:
                total = total + term[at, :].astype(f32)
            dst[at, :] = total.astype(dst.dtype)
            return carry

        lax.fori_loop(0, count // step, body, 0)

    side = lax.div(z, 2)
    end_z, inner_z = 3 * side, 1 + side
    is_end = z == end_z

    def rc_copy(k, zz, yy):
        at = zz * 2 + yy
        return remote(piece(k, zz, yy, 1 - c), core_in[k].at[at], rc_send.at[k, at], rc_recv.at[k, at], c_peer)

    def ry_copy(k, zz):
        if k == V:
            return remote(ag_piece(V, z, 1 - y, c), y_in[V].at[0], ry_send.at[V, 0], ry_recv.at[V, 0], y_peer)
        return remote(ag_piece(k, zz, 1 - y, c), y_in[k].at[zz], ry_send.at[k, zz], ry_recv.at[k, zz], y_peer)

    def z_slot(k, slot, yy):
        return z_in[k].at[slot * 2 + yy if k == V else slot]

    def z_sem(slot, yy):
        return slot * 2 + yy

    def rz_copy(k, s, yy, from_end):
        slot = s - 1 if from_end else {3: 0, 2: 1, 1: 3}[s]
        to = inner_z if from_end else {3: end_z, 2: 3 - end_z, 1: 3 - inner_z}[s]
        sent, landed = rz_send.at[k, (s - 1) * 2 + yy], rz_recv.at[k, z_sem(slot, yy)]
        return remote(ag_piece(k, near(s), yy, c), z_slot(k, slot, yy), sent, landed, (slot_of(to, y, c), t))

    def z_landed(k, slot, yy):
        ref = z_slot(k, slot, yy)
        remote(ref, ref, rz_send.at[k, 0], rz_recv.at[k, z_sem(slot, yy)], y_peer).wait_recv()
        return ref

    def y_landed(k, zz):
        ref = y_in[k].at[0 if k == V else zz]
        remote(ref, ref, ry_send.at[k, 0], ry_recv.at[k, 0 if k == V else zz], y_peer).wait_recv()
        return ref

    def rc_add(k, zz, yy):
        at = zz * 2 + yy
        remote(core_in[k].at[at], core_in[k].at[at], rc_send.at[k, 0], rc_recv.at[k, at], c_peer).wait_recv()
        mine = piece(k, zz, yy, c)
        add(mine, mine, core_in[k].at[at])

        @pl.when(yy != y)
        def _():
            ry_copy(k, zz).start()

    def z_step(k, s, yy, *terms):
        mine = ag_piece(k, near(s), yy, c)
        if terms:
            add(mine, mine, *terms)

        @pl.when(is_end)
        def _():
            rz_copy(k, s, yy, True).start()

        if s == 3:

            @pl.when(jnp.logical_not(is_end))
            def _():
                rz_copy(k, s, yy, False).start()

    def z_merge(k, s, yy):
        @pl.when(jnp.logical_not(is_end))
        def _():
            mine = ag_piece(k, near(s), yy, c)
            add(mine, mine, z_landed(k, s, yy))
            rz_copy(k, s, yy, False).start()

    def ry_add(k, s):
        z_step(k, s, y, y_landed(k, near(s)))

    def ry_merge(k, s):
        z_merge(k, s, y)

    def total_of(k):
        return sum_d.at[(k - W) * HALF : (k - W + 1) * HALF] if k >= W else sums[k]

    def z_total(k, yy, dst, *terms):
        mine = ag_piece(k, z, yy, c)
        first = z_landed(k, 0, yy)

        @pl.when(is_end)
        def _():
            add(dst, mine, first, z_landed(k, 1, yy), *terms)

        @pl.when(jnp.logical_not(is_end))
        def _():
            add(dst, mine, first, z_landed(k, 3, yy), *terms)

    def own_total(k):
        z_total(k, y, total_of(k), y_landed(k, z))

    def v_cross():
        mine = ag_piece(V, z, 1 - y, c)
        z_total(V, 1 - y, mine)
        ry_copy(V, z).start()

    def x_rows(ref, index):
        return remote(ref.at[own], ref.at[own], x_send.at[index], x_recv.at[index], x_peer)

    def x_rows_wait(ref, index):
        remote(ref.at[other], ref.at[other], x_send.at[index], x_recv.at[index], x_peer).wait_recv()

    def x_part(index):
        slot = 1 if index == 2 else 0
        return remote(far.at[slot], inx.at[slot], x_send.at[5 + index], x_recv.at[5 + index], x_peer)

    def by_rows(body, step=64):
        def run(i, carry):
            body(pl.multiple_of(i * step, step), step)
            return carry

        lax.fori_loop(0, rows // step, run, 0)

    def norm(value):
        average = jnp.mean(value, -1, keepdims=True)
        centred = value - average
        inverse = lax.rsqrt(jnp.mean(centred * centred, -1, keepdims=True) + EPS)
        return centred * inverse, inverse

    def norm_grad(grad, unit, inverse, gain):
        scaled = grad * gain
        return inverse * (
            scaled - jnp.mean(scaled, -1, keepdims=True) - unit * jnp.mean(scaled * unit, -1, keepdims=True)
        )

    def x_out():
        half = (slice(None), slice(None), lanes(c * 512, 512, 512))
        return remote(go.at[half], go_x.at[half], x_send.at[4], x_recv.at[4], x_peer)

    def x_out_core(cc):
        half = (slice(None), slice(None), lanes(cc * 512, 512, 512))
        return remote(go_x.at[half], go_x.at[half], x_send.at[9], x_recv.at[9], c_peer)

    def x_grad_context():
        return remote(ctx_x, gctx.at[own], x_send.at[10], x_recv.at[10], x_peer)

    def x_grad_context_wait():
        remote(gctx.at[other], gctx.at[other], x_send.at[10], x_recv.at[10], x_peer).wait_recv()

    stages = (x_peer, c_peer, y_peer)

    def v_copy(stage):
        return remote(vout.at[1 + stage], vin.at[stage], v_send.at[stage], v_recv.at[stage], stages[stage])

    def vz_copy(step):
        peer = (slot_of(lax.rem(z + step, DEPTH), y, c), t)
        return remote(vout.at[4], vin.at[3 + z], v_send.at[2 + step], v_recv.at[3 + z], peer)

    def early_rows(hop):
        if hop == 0:
            vout[1] = vout[0]
        else:
            v_copy(hop - 1).wait_recv()
            vout[1 + hop] = vout[hop] + vin[hop - 1]
        if hop < 3:
            v_copy(hop).start()
        else:
            for step in range(1, DEPTH):
                vz_copy(step).start()
            vin[3 + z] = vout[4]

    def late_turn(turn):
        dx, dy, dc = turn // 4, turn // 2 % 2, turn % 2
        xx, yy, cc = (1 - t if dx else t), (1 - y if dy else y), (1 - c if dc else c)
        return (slot_of(z, yy, cc), xx), xx * 4 + yy * 2 + cc

    def late_copy(turn):
        here = t * 4 + y * 2 + c
        return remote(late, late_in.at[here], l_send.at[turn], l_recv.at[here], late_turn(turn)[0])

    def late_wait(index):
        remote(late_in.at[index], late_in.at[index], l_send.at[0], l_recv.at[index], y_peer).wait_recv()

    def late_z(step):
        peer = (slot_of(lax.rem(z + step, DEPTH), y, c), t)
        return remote(late_sum, late_in.at[8 + z], l_send.at[7 + step], l_recv.at[8 + z], peer)

    barrier = pltpu.get_barrier_semaphore()
    z_peers = [(slot_of(lax.rem(z + step, DEPTH), y, c), t) for step in range(1, DEPTH)]
    everyone = [late_turn(turn)[0] for turn in range(1, 8)] + z_peers
    for device in everyone:
        pl.semaphore_signal(barrier, inc=1, device_id=device, device_id_type=MESH_ID)

    def prepare(held, stack):
        load = pltpu.make_async_copy(view, held, copy_sem.at[0])
        load.start()

        def first_norm(at, step):
            unit, inverse = norm(tokens[pl.ds(at, step), :])
            to = pl.ds(pl.multiple_of(t * rows + at, step), step)
            rows_one[to, :] = (unit * vecs[0:1, :] + vecs[1:2, :]).astype(bf)
            grad_rows[to, :] = cot[pl.ds(at, step), :].astype(bf)

        load.wait()
        lay_blocks(held, stack)

        def pair(left, right, count, left_high=False, right_high=False):
            first, second = stack[left : left + count, :], stack[right : right + count, :]
            first = pltpu.roll(first, HALF, 1) if left_high else first
            second = second if right_high else pltpu.roll(second, HALF, 1)
            lane = lax.broadcasted_iota(jnp.int32, (count, LANES), 1)
            return jnp.where(lane < HALF, first, second).astype(bf)

        n = gq.shape[1]
        gq[me] = pair(0, n, n)
        base = 2 * n
        wide = [pair(base + b * 64, base + b * 64 + 64, 64) for b in range(0, 8, 2)]
        go[z * 2 + y, :, lanes(c * 512, 512, 512)] = jnp.concatenate(wide, 1)
        pl.semaphore_wait(barrier, len(everyone))
        for k in (Q, O):
            own_sends_y(k)
            own_sends_z(k)
        by_rows(first_norm)
        x_rows(rows_one, 0).start()
        base += 512
        gi[me] = pair(base, 0, D, right_high=True)
        for r in range(2):
            for b in range(0, 16, 2):
                at = D + (r * 16 + b) * 64
                gd[me, r * 64 : r * 64 + 64, b * HALF : b * HALF + LANES] = pair(at, at + 64, 64, True, True)

    pl.run_scoped(
        prepare,
        pltpu.VMEM(view.shape, f32),
        pltpu.VMEM((view.shape[2] // 2 * BLOCK, LANES), f32),
    )
    x_rows(grad_rows, 1).start()
    z_arrival((Q, O), 1)
    y_arrival((Q, O), 0)
    for k in (I, W, V):
        own_sends_z(k)
    z_arrival((Q, O), 2)
    y_arrival((Q, O), 1)
    z_arrival((Q, O), 3)
    for k in (I, W, V):
        own_sends_y(k)

    def core_waits(kinds, zz):
        for k in kinds:
            for yy in (y, 1 - y):
                ag_wait(k, zz, yy, 1 - c)

    x_rows_wait(rows_one, 0)

    ends = []
    for p in range(ARTICLES):
        length = 0
        for a in range(ARTICLES):
            length = length + jnp.where(order[0, p] == a, lengths[0, a], 0)
        ends.append(length + ends[-1] if p else length)

    def allowed(first, count):
        ids = lax.broadcasted_iota(jnp.int32, (rows, 1), 0) + first
        start = jnp.zeros((rows, 1), jnp.int32)
        for end in ends:
            start = jnp.where(ids >= end, end, start)
        start = jnp.where(ids >= ends[-1], ids, start)
        keys = lax.broadcasted_iota(jnp.int32, (rows, count), 1)
        return (keys <= ids) & (keys >= start)

    scale = HD ** (-0.5)
    strip = 1024

    def assemble(h):
        for yy in range(2):
            even, odd = gq.at[slot_of(h, yy, 0)], gq.at[slot_of(h, yy, 1)]
            at = yy * 192
            wqkv[h, 0:768, at : at + 64] = even[:, 0:64]
            wqkv[h, 768:1024, at : at + 64] = even[0:256, 64:128]
            wqkv[h, 0:512, at + 64 : at + 128] = even[256:768, 64:128]
            wqkv[h, 512:1024, at + 64 : at + 128] = odd[0:512, 0:64]
            wqkv[h, 0:256, at + 128 : at + 192] = odd[512:768, 0:64]
            wqkv[h, 256:1024, at + 128 : at + 192] = odd[:, 64:128]

    def disassemble(h, value):
        for yy in range(2):
            even, odd = gq.at[slot_of(h, yy, 0)], gq.at[slot_of(h, yy, 1)]
            at = yy * 192
            even[:, 0:64] = value[0:768, at : at + 64]
            even[0:256, 64:128] = value[768:1024, at : at + 64]
            even[256:768, 64:128] = value[0:512, at + 64 : at + 128]
            odd[0:512, 0:64] = value[512:1024, at + 64 : at + 128]
            odd[512:768, 0:64] = value[0:256, at + 128 : at + 192]
            odd[:, 64:128] = value[256:1024, at + 128 : at + 192]

    qv = vecs[pl.ds(6 + t, 1), :]
    for h in range(DEPTH):
        none = jnp.zeros((1, HD), f32)
        qkv_bias[h] = jnp.concatenate([qv[:, h * 256 : h * 256 + 128], none, qv[:, h * 256 + 128 : h * 256 + 256]], 1)

    def head(h):
        core_waits((Q,), h)
        assemble(h)
        qkv[h] = (dot(rows_one[...], wqkv[h]) + qkv_bias[h]).astype(bf)
        for block in range(2):
            at, seen = slice(block * rows, (block + 1) * rows), (block + 1) * rows
            scores = dot_nt(qkv[h, at, 0:128], qkv[h, 0:seen, 128:256]) * scale
            scores = jnp.where(allowed(block * rows, seen), scores, NEG)
            expo = jnp.exp(scores - jnp.max(scores, -1, keepdims=True))
            low = (expo / jnp.sum(expo, -1, keepdims=True)).astype(bf)
            probs[h, at, 0:seen] = low
            ctx[at, lanes(h * HD, HD, HD)] = dot(low, qkv[h, 0:seen, 256:384]).astype(bf)

    head(near(0))
    y_arrival((Q, O), 2)
    head(near(1))
    y_arrival((Q, O), 3)
    head(near(2))
    z_arrival((I, W), 1)
    head(near(3))
    y_arrival((I, W), 0)
    v_forward(z, 1 - y)
    for zz in range(DEPTH):
        core_waits((O,), zz)

    def w_out(ref):
        return ref[...].reshape(DEPTH * HD, D)

    far[0] = dot(ctx[other, :], w_out(go)).astype(bf)
    x_part(0).start()
    mixed[...] = tokens[...] + dot(ctx[own, :], w_out(go)) + vecs[4:5, :]
    z_arrival((I, W), 2)
    v_arrival(1)
    y_arrival((I, W), 1)
    x_part(0).wait_recv()

    def second_norm(at, step):
        value = mixed[pl.ds(at, step), :] + inx[0, pl.ds(at, step), :].astype(f32)
        mixed[pl.ds(at, step), :] = value
        unit, inverse = norm(value)
        to = pl.ds(pl.multiple_of(t * rows + at, step), step)
        rows_two[to, :] = (unit * vecs[2:3, :] + vecs[3:4, :]).astype(bf)

    by_rows(second_norm)
    x_rows(rows_two, 2).start()
    x_out().start()
    z_arrival((I, W), 3)
    v_arrival(2)
    macc[...] = jnp.zeros_like(macc)
    nacc[...] = jnp.zeros_like(nacc)
    vout[...] = jnp.zeros_like(vout)
    x_rows_wait(grad_rows, 1)

    def ffn(half, zz):
        first = 4 * zz
        at = pl.ds(pl.multiple_of(lax.rem(t + half, 2) * rows, rows), rows)
        units = lanes(zz * 512, 512, 512)
        bias_row = vecs[pl.ds(8 + 2 * t + lax.div(zz, 2), 1), lanes(lax.rem(zz, 2) * 512, 512, 512)]

        def w_in(start, count):
            return jnp.concatenate([gi[first + j, start : start + count, :] for j in range(4)], 1)

        def w_down(start, count):
            return gd[pl.ds(first, 4), :, start : start + count].reshape(512, count)

        inner = dot(rows_two[at, :], w_in(0, D)) + bias_row
        square = inner * inner
        bent = jnp.tanh(GELU_A * inner * (1.0 + GELU_B * square))
        act[at, units] = (0.5 * inner * (1.0 + bent)).astype(bf)
        slope = 0.5 * (1.0 + bent) + 0.5 * inner * (1.0 - bent * bent) * (GELU_A * (1.0 + 3.0 * GELU_B * square))
        gin[at, units] = (dot_nt(grad_rows[at, :], w_down(0, D)) * slope).astype(bf)
        for nb in range(4):
            out = slice(nb * 256, nb * 256 + 256)
            nacc[at, out] += dot_nt(gin[at, units], w_in(nb * 256, 256))
            macc[at, out] += dot(act[at, units], w_down(nb * 256, 256))

    def ffn_grads(zz):
        first = 4 * zz
        units = lanes(zz * 512, 512, 512)
        for k in (I, W, V):
            for yy in range(2):
                drain(k, zz, yy)
        bias_sum[zz] = jnp.sum(gin[:, units].astype(f32), 0, keepdims=True)
        for nb in range(4):
            out = slice(nb * 256, nb * 256 + 256)
            part = dot(rows_t[out, :], gin[:, units]).astype(bf)
            for j in range(4):
                gi[first + j, out, :] = part[:, j * LANES : (j + 1) * LANES]
        for yy in (1 - y, y):
            rc_copy(I, zz, yy).start()
        act_t = act[:, units].T
        for nb in range(4):
            out = slice(nb * 256, nb * 256 + 256)
            part = dot(act_t, grad_rows[:, out]).astype(bf)
            gd[pl.ds(first, 4), :, out] = part.reshape(4, LANES, 256)
        for yy in (1 - y, y):
            rc_copy(W, zz, yy).start()

    def reduce_core(zz):
        for yy in (1 - y, y):
            for k in (I, W):
                rc_add(k, zz, yy)

    def v_step(s):
        for yy in (1 - y, y):
            z_step(V, s, yy)

    def v_merge(s):
        for yy in (1 - y, y):
            z_merge(V, s, yy)

    core_waits((I, W, V), z)
    ffn(0, z)
    y_arrival((I, W), 2)
    core_waits((I, W, V), near(1))
    ffn(0, near(1))
    x_rows_wait(rows_two, 2)
    rows_t[...] = rows_two[...].T

    def by_z(s, carry):
        @pl.when(s == 2)
        def _():
            v_arrival(3)
            y_arrival((I, W), 3)

        @pl.when(s >= 2)
        def _():
            core_waits((I, W, V), near(s))
            ffn(0, near(s))

        ffn(1, near(s))

        @pl.when(s == DEPTH - 1)
        def _():
            x_part(0).wait_send()
            far[0] = nacc[other, :].astype(bf)
            x_part(1).start()

        @pl.when(s > 0)
        def _():
            reduce_core(near(s - 1))

        for before in (1, 2):

            @pl.when(s == before + 1)
            def _():
                v_step(before)

        ffn_grads(near(s))
        return carry

    lax.fori_loop(0, DEPTH, by_z, 0)
    x_out().wait_recv()
    x_out_core(c).start()
    reduce_core(near(3))
    v_step(3)
    v_merge(1)
    for zz in range(DEPTH):
        for side in range(2):
            row, start = 8 + 2 * side + zz // 2, zz % 2 * 512
            vout[0, row : row + 1, start : start + 512] = jnp.where(t == side, bias_sum[zz], 0.0)
    rows_t[...] = rows_one[...].T
    x_part(1).wait_recv()

    def row_sum(row, value):
        vout[0, row : row + 1, :] += jnp.sum(value, 0, keepdims=True)

    def second_back(at, step):
        here = pl.ds(at, step)
        in_group = pl.ds(pl.multiple_of(t * rows + at, step), step)
        grad = nacc[in_group, :] + inx[0, here, :].astype(f32)
        unit, inverse = norm(mixed[here, :])
        back = cot[here, :] + norm_grad(grad, unit, inverse, vecs[2:3, :])
        input_grad[here, :] = back
        grad_attn[in_group, :] = back.astype(bf)
        row_sum(2, grad * unit)
        row_sum(3, grad)
        row_sum(4, back)
        row_sum(5, cot[here, :])

    by_rows(second_back)
    early_rows(0)
    x_out_core(1 - c).wait_recv()
    ctx_x[...] = dot_nt(grad_attn[own, :], w_out(go_x)).astype(bf)
    x_grad_context().start()
    x_rows(grad_attn, 3).start()
    far[1] = macc[other, :].astype(bf)
    x_part(2).start()
    gctx[own, :] = dot_nt(grad_attn[own, :], w_out(go)).astype(bf)
    for k in (I, W):
        ry_add(k, 1)
    v_merge(2)
    for zz in range(DEPTH):
        for yy in range(2):
            drain(O, zz, yy)
            drain(Q, zz, yy)
    def mixed_out(at, step):
        here = pl.ds(at, step)
        in_group = pl.ds(pl.multiple_of(t * rows + at, step), step)
        mixed[here, :] = mixed[here, :] + macc[in_group, :] + inx[1, here, :].astype(f32) + vecs[5:6, :]

    x_out().wait_send()
    x_grad_context_wait()

    def out_grads():
        x_rows_wait(grad_attn, 3)
        ctx_t = ctx[...].T
        for nb in range(4):
            at = slice(nb * 256, nb * 256 + 256)
            go[:, :, at] = dot(ctx_t, grad_attn[:, at]).astype(bf).reshape(8, 64, 256)
        for zz in range(DEPTH):
            for yy in range(2):
                rc_copy(O, zz, yy).start()

    def head_back(h):
        q0, q1 = qkv[h, 0:rows, 0:128], qkv[h, rows : 2 * rows, 0:128]
        grads = []
        for block in range(2):
            at, seen = slice(block * rows, (block + 1) * rows), (block + 1) * rows
            low = probs[h, at, 0:seen]
            given = gctx[at, h * 128 : h * 128 + 128]
            prob = low.astype(f32)
            grad_probs = dot_nt(given, qkv[h, 0:seen, 256:384])
            delta = jnp.sum(prob * grad_probs, -1, keepdims=True)
            grad_scores = (prob * (grad_probs - delta)).astype(bf)
            grad_q = dot(grad_scores, qkv[h, 0:seen, 128:256]) * scale
            grad_k = dot_tn(grad_scores, q1 if block else q0) * scale
            grad_v = dot_tn(low, given)
            grads.append((grad_q, grad_k, grad_v))
        (gq0, gk0, gv0), (gq1, gk1, gv1) = grads
        top = jnp.concatenate([gq0, gk0 + gk1[0:rows], gv0 + gv1[0:rows]], 1).astype(bf)
        low_half = jnp.concatenate([gq1, gk1[rows:], gv1[rows:]], 1).astype(bf)
        qkv[h, 0:rows, :] = top
        qkv[h, rows : 2 * rows, :] = low_half
        total = jnp.sum(top.astype(f32), 0, keepdims=True) + jnp.sum(low_half.astype(f32), 0, keepdims=True)
        for side in range(2):
            vout[0, 6 + side : 7 + side, h * 256 : h * 256 + 128] = jnp.where(t == side, total[:, 0:128], 0.0)
            vout[0, 6 + side : 7 + side, h * 256 + 128 : h * 256 + 256] = jnp.where(t == side, total[:, 256:384], 0.0)
        for half in (other, own):
            product = dot_nt(qkv[h, half, :], wqkv[h])
            if h == 0:
                nacc[half, :] = product
            else:
                nacc[half, :] += product
            if h == DEPTH - 1 and half is other:
                x_part(1).wait_send()
                far[0] = nacc[other, :].astype(bf)
                x_part(3).start()
        part = dot(rows_t[...], qkv[h]).astype(bf)
        disassemble(h, part)
        for yy in (1 - y, y):
            rc_copy(Q, h, yy).start()

    for h in range(DEPTH):
        head_back(h)
        if h < 3:
            early_rows(h + 1)
        if h > 0:
            for yy in (1 - y, y):
                rc_add(Q, h - 1, yy)
        if h == 0:
            v_cross()
        if h == 1:
            for k in (I, W):
                ry_add(k, 2)
            out_grads()
        if h == 2:
            for k in (I, W):
                ry_add(k, 3)
                ry_merge(k, 1)
            for yy in (1 - y, y):
                for s in range(DEPTH):
                    rc_add(O, near(s), yy)
    for yy in (1 - y, y):
        rc_add(Q, DEPTH - 1, yy)
    for k in (I, W):
        ry_merge(k, 2)
    x_part(2).wait_recv()
    by_rows(mixed_out)
    for k in (I, W):
        own_total(k)
    z_total(V, y, total_of(V), y_landed(V, z))
    x_part(3).wait_recv()

    def first_back(at, step):
        here = pl.ds(at, step)
        in_group = pl.ds(pl.multiple_of(t * rows + at, step), step)
        grad = nacc[in_group, :] + inx[0, here, :].astype(f32)
        unit, inverse = norm(tokens[here, :])
        input_grad[here, :] = input_grad[here, :] + norm_grad(grad, unit, inverse, vecs[0:1, :])
        row_sum(0, grad * unit)
        row_sum(1, grad)

    by_rows(first_back)

    for row in range(4):
        for j in range(8):
            late[row * 8 + j : row * 8 + j + 1, :] = vout[0, (0, 1, 6, 7)[row] : (0, 1, 6, 7)[row] + 1, j * LANES : (j + 1) * LANES]
    here = t * 4 + y * 2 + c
    late_in[here] = late[...]
    for turn in range(1, 8):
        late_copy(turn).start()
    for s in (3, 2, 1):
        ry_add(O, s)
    ry_merge(O, 2)
    ry_merge(O, 1)
    for turn in range(1, 8):
        late_wait(late_turn(turn)[1])
    total = late_in[0]
    for index in range(1, 8):
        total = total + late_in[index]
    late_sum[...] = total
    late_in[8 + z] = total
    for step in range(1, DEPTH):
        late_z(step).start()
    for s in (3, 2, 1):
        ry_add(Q, s)
    ry_merge(Q, 2)
    ry_merge(Q, 1)
    own_total(O)
    own_total(Q)
    for step in range(1, DEPTH):
        late_wait(8 + lax.rem(z + step, DEPTH))
    total = ((late_in[8] + late_in[9]) + late_in[10]) + late_in[11]
    for step in range(1, DEPTH):
        zz = lax.rem(z + step, DEPTH)
        remote(vin.at[3 + zz], vin.at[3 + zz], v_send.at[0], v_recv.at[3 + zz], y_peer).wait_recv()
    early = ((vin[3] + vin[4]) + vin[5]) + vin[6]
    vec_grads[...] = early[0 : vec_grads.shape[0]]
    for row in range(4):
        for j in range(8):
            vec_grads[(0, 1, 6, 7)[row] : (0, 1, 6, 7)[row] + 1, j * LANES : (j + 1) * LANES] = total[row * 8 + j : row * 8 + j + 1, :]

    for stage in range(3):
        v_copy(stage).wait_send()
    for turn in range(1, 8):
        late_copy(turn).wait_send()
    for step in range(1, DEPTH):
        vz_copy(step).wait_send()
        late_z(step).wait_send()
    for index, ref in enumerate((rows_one, grad_rows, rows_two, grad_attn)):
        x_rows(ref, index).wait_send()
    for index in (2, 3):
        x_part(index).wait_send()
    x_out_core(c).wait_send()
    x_grad_context().wait_send()
    for k in range(4):
        for zz in range(DEPTH):
            for yy in range(2):
                rc_copy(k, zz, yy).wait_send()
            ry_copy(k, zz).wait_send()
        for s in range(1, DEPTH):
            rz_copy(k, s, y, True).wait_send()
    ry_copy(V, z).wait_send()
    for yy in range(2):
        for s in range(1, DEPTH):
            rz_copy(V, s, yy, True).wait_send()


def run_layer(tokens, cotangent, lengths, order, weights, vec_params):
    bf, f32 = jnp.bfloat16, jnp.float32
    rows = tokens.shape[0]
    group = 2 * rows
    owners = 16
    shapes = piece_shapes()
    view = jnp.transpose(weights, (1, 2, 0))
    vmem = pl.BlockSpec(memory_space=pltpu.VMEM)
    smem = pl.BlockSpec(memory_space=pltpu.SMEM)

    halved = shapes[:3] + ((HALF, D),)

    def many(count, kinds):
        return [pltpu.VMEM((count,) + s, bf) for s in kinds]

    full = pltpu.VMEM((group, D), bf)
    dma = pltpu.SemaphoreType.DMA
    return pl.pallas_call(
        layer_kernel,
        out_shape=[jax.ShapeDtypeStruct((rows, D), f32)] * 2
        + [jax.ShapeDtypeStruct(s, f32) for s in shapes]
        + [jax.ShapeDtypeStruct(vec_params.shape, f32)],
        in_specs=[smem, smem, pl.BlockSpec(memory_space=pl.ANY)] + [vmem] * 3,
        out_specs=[vmem] * 7,
        scratch_shapes=[
            pltpu.VMEM((owners,) + shapes[0], bf),
            pltpu.VMEM((owners // 2, BLOCK, D), bf),
            pltpu.VMEM((owners,) + shapes[2], bf),
            pltpu.VMEM((owners,) + shapes[3], bf),
            pltpu.VMEM((DEPTH, D, 3 * HD), bf),
        ]
        + many(2 * DEPTH, shapes)
        + many(DEPTH, halved)
        + many(1, halved[3:])
        + many(DEPTH, halved)
        + many(2 * DEPTH, halved[3:])
        + [
            full,
            full,
            pltpu.VMEM((D, group), bf),
            full,
            full,
            pltpu.VMEM((DEPTH, group, group), bf),
            pltpu.VMEM((DEPTH, group, 3 * HD), bf),
            pltpu.VMEM((group, DEPTH * HD), bf),
            pltpu.VMEM((group, DEPTH * HD), bf),
            pltpu.VMEM((2, rows, D), bf),
            pltpu.VMEM((2, rows, D), bf),
            pltpu.VMEM((owners // 2, BLOCK, D), bf),
            pltpu.VMEM((rows, DEPTH * HD), bf),
            pltpu.VMEM((group, D), f32),
            pltpu.VMEM((group, D), f32),
            pltpu.VMEM((group, 2 * D), bf),
            pltpu.VMEM((group, 2 * D), bf),
            pltpu.VMEM((DEPTH, 1, 512), f32),
            pltpu.VMEM((DEPTH, 1, 3 * HD), f32),
            pltpu.VMEM((7, 16, D), f32),
            pltpu.VMEM((5, 16, D), f32),
            pltpu.VMEM((32, LANES), f32),
            pltpu.VMEM((32, LANES), f32),
            pltpu.VMEM((12, 32, LANES), f32),
            dma((5, owners)),
            dma((5, DEPTH)),
            dma((5, 2 * DEPTH)),
            dma((5, 2, 2 * DEPTH)),
            dma((4, 2 * DEPTH)),
            dma((4, 2 * DEPTH)),
            dma((5, DEPTH)),
            dma((5, DEPTH)),
            dma((5, 2 * DEPTH)),
            dma((5, 2 * DEPTH)),
            dma((11,)),
            dma((11,)),
            dma((6,)),
            dma((7,)),
            dma((11,)),
            dma((12,)),
            dma((1,)),
        ],
        compiler_params=pltpu.CompilerParams(
            collective_id=0, has_side_effects=True, vmem_limit_bytes=VMEM_LIMIT
        ),
        name="layer",
    )(lengths, order, view, tokens, cotangent, vec_params)


def per_device(
    grp_count,
    tp_count,
    tokens,
    cotangent,
    lengths,
    order,
    weights,
    momentum,
    stat_left,
    stat_right,
    root_left,
    root_right,
    vec_params,
    vec_momentum,
    vec_second,
):
    fits = grp_count == 4 * DEPTH and tp_count == 2 and tokens.shape[0] == 256
    if not fits or lengths.shape[1] != ARTICLES:
        return per_device_general(
            tokens,
            cotangent,
            lengths,
            order,
            weights,
            momentum,
            stat_left,
            stat_right,
            root_left,
            root_right,
            vec_params,
            vec_momentum,
            vec_second,
        )
    token_total = tokens.shape[0] * tp_count * grp_count
    mixed, input_grad, *sums, vec_grads = run_layer(tokens, cotangent, lengths, order, weights, vec_params)
    blocks, vecs, results = update_blocks(
        sums,
        (weights, momentum, stat_left, stat_right, root_left, root_right),
        vec_grads,
        (vec_params, vec_momentum, vec_second),
        (mixed, input_grad),
        token_total,
    )
    return (*results, *blocks, *vecs)


def solution(mesh):
    placed = (
        P(("grp", "tp"), None),
        P(("grp", "tp"), None),
        P("grp", None),
        P("grp", None),
        P(("tp", "grp"), None, None),
        P(("tp", "grp"), None, None),
        P(("tp", "grp"), None, None),
        P(("tp", "grp"), None, None),
        P(("tp", "grp"), None, None),
        P(("tp", "grp"), None, None),
        P(),
        P(),
        P(),
    )
    return jax.shard_map(
        functools.partial(per_device, mesh.shape["grp"], mesh.shape["tp"]),
        mesh=mesh,
        in_specs=placed,
        out_specs=(
            P(("grp", "tp"), None),
            P(("grp", "tp"), None),
            P(("tp", "grp"), None, None),
            P(("tp", "grp"), None, None),
            P(("tp", "grp"), None, None),
            P(("tp", "grp"), None, None),
            P(("tp", "grp"), None, None),
            P(),
            P(),
            P(),
            P(),
        ),
        check_vma=False,
    )
```

```python
import functools

import jax
import jax.numpy as jnp
from jax import lax
from jax.experimental import pallas as pl
from jax.experimental.pallas import tpu as pltpu
from jax.sharding import PartitionSpec as P

D = 1024
HEADS = 8
HD = 128
FF = 4096
BLOCK = 64


EPS = 1e-05
NEG = -1e30
DECAY = 0.9
BETA = 0.9
RATE = 0.05
VEC_DECAY = 0.9
VEC_RATE = 0.2
VEC_EPS = 1e-08


def norm_rows(value, gain, shift):
    average = jnp.mean(value, -1, keepdims=True)
    centred = value - average
    inverse = lax.rsqrt(jnp.mean(centred * centred, -1, keepdims=True) + EPS)
    normed = centred * inverse
    return (normed * gain + shift, normed, inverse)


def norm_back(grad_out, normed, inverse, gain):
    scaled = grad_out * gain
    return inverse * (
        scaled
        - jnp.mean(scaled, -1, keepdims=True)
        - normed * jnp.mean(scaled * normed, -1, keepdims=True)
    )


def segment_ids(lengths_row, order_row, group_rows):
    article_count = lengths_row.shape[0]
    slots = jnp.arange(article_count, dtype=jnp.int32)
    picks = (order_row[:, None] == slots[None, :]).astype(jnp.int32)
    packed = jnp.sum(picks * lengths_row[None, :], 1)
    ends = jnp.cumsum(packed)
    spots = jnp.arange(group_rows, dtype=jnp.int32)
    return jnp.sum((spots[:, None] >= ends[None, :]).astype(jnp.int32), 1)


def allowed_mask(row_ids, row_segs, segments, key_ids, article_count):
    causal = key_ids[None, :] <= row_ids[:, None]
    same = segments[None, :] == row_segs[:, None]
    alone = (row_segs[:, None] < article_count) | (key_ids[None, :] == row_ids[:, None])
    return causal & same & alone


def from_columns(tiles, row_total, col_total):
    return (
        tiles.reshape(col_total // BLOCK, row_total // BLOCK, BLOCK, BLOCK)
        .transpose(1, 2, 0, 3)
        .reshape(row_total, col_total)
    )


def from_rows(tiles, row_total, col_total):
    return (
        tiles.reshape(row_total // BLOCK, col_total // BLOCK, BLOCK, BLOCK)
        .transpose(0, 2, 1, 3)
        .reshape(row_total, col_total)
    )


def to_columns(matrix):
    row_total, col_total = matrix.shape
    return (
        matrix.reshape(row_total // BLOCK, BLOCK, col_total // BLOCK, BLOCK)
        .transpose(2, 0, 1, 3)
        .reshape(-1, BLOCK, BLOCK)
    )


def to_rows(matrix):
    row_total, col_total = matrix.shape
    return (
        matrix.reshape(row_total // BLOCK, BLOCK, col_total // BLOCK, BLOCK)
        .transpose(0, 2, 1, 3)
        .reshape(-1, BLOCK, BLOCK)
    )


def per_device_general(
    tokens,
    cotangent,
    lengths,
    order,
    weights,
    momentum,
    stat_left,
    stat_right,
    root_left,
    root_right,
    vec_params,
    vec_momentum,
    vec_second,
):
    groups = lax.axis_size("grp")
    tp_size = lax.axis_size("tp")
    tp_rank = lax.axis_index("tp")
    tok_rows = tokens.shape[0]
    group_rows = tok_rows * tp_size
    article_count = lengths.shape[1]
    owners = groups * tp_size
    block_area = BLOCK * BLOCK * owners
    qkv_count = 3 * D * D // block_area
    out_count = D * D // block_area
    in_count = D * FF // block_area
    owned_blocks = weights.shape[0]
    heads_here = HEADS // tp_size
    qkv_cols = 3 * D // tp_size
    feat_here = D // tp_size
    ff_here = FF // tp_size
    qv_width = 2 * D // tp_size
    token_total = group_rows * groups
    gathered = lax.all_gather(weights.astype(jnp.bfloat16), "grp", axis=0, tiled=True)
    per_owner = gathered.reshape(groups, owned_blocks, BLOCK, BLOCK)
    marks = [0, qkv_count, qkv_count + out_count, qkv_count + out_count + in_count, owned_blocks]
    pieces = [
        per_owner[:, marks[index] : marks[index + 1]].reshape(-1, BLOCK, BLOCK)
        for index in range(4)
    ]
    w_qkv = from_columns(pieces[0], D, qkv_cols)
    w_out = from_rows(pieces[1], feat_here, D)
    w_in = from_columns(pieces[2], D, ff_here)
    w_down = from_rows(pieces[3], ff_here, D)
    w_qkv_heads = w_qkv.reshape(D, heads_here, 3, HD)
    w_out_heads = w_out.reshape(heads_here, HD, D)
    segments = segment_ids(lengths[0], order[0], group_rows)
    gain_one = vec_params[0]
    shift_one = vec_params[1]
    gain_two = vec_params[2]
    shift_two = vec_params[3]
    bias_out = vec_params[4]
    bias_down = vec_params[5]
    qv_here = lax.dynamic_slice_in_dim(
        vec_params[6:8].reshape(2 * D), tp_rank * qv_width, qv_width
    ).reshape(heads_here, 2, HD)
    bias_heads = jnp.stack(
        [qv_here[:, 0], jnp.zeros((heads_here, HD), jnp.float32), qv_here[:, 1]], 0
    )[:, :, None, :]
    bias_in = lax.dynamic_slice_in_dim(vec_params[8:].reshape(FF), tp_rank * ff_here, ff_here)
    normed_one, unit_one, inverse_one = norm_rows(tokens, gain_one, shift_one)
    rows_one = lax.all_gather(normed_one.astype(jnp.bfloat16), "tp", axis=0, tiled=True)
    projected = (
        jnp.einsum("rx,xhcd->chrd", rows_one, w_qkv_heads, preferred_element_type=jnp.float32)
        + bias_heads
    ).astype(jnp.bfloat16)
    queries = projected[0]
    keys_all = projected[1]
    values_all = projected[2]
    span = min(512, group_rows)
    starts = jnp.arange(group_rows // span, dtype=jnp.int32) * span
    key_ids = jnp.arange(group_rows, dtype=jnp.int32)
    score_scale = HD ** (-0.5)

    def masked_scores(first_row):
        row_ids = first_row + jnp.arange(span, dtype=jnp.int32)
        row_segs = lax.dynamic_slice_in_dim(segments, first_row, span, 0)
        allowed = allowed_mask(row_ids, row_segs, segments, key_ids, article_count)
        query_rows = lax.dynamic_slice_in_dim(queries, first_row, span, 1)
        scores = (
            jnp.einsum("hqd,hkd->hqk", query_rows, keys_all, preferred_element_type=jnp.float32)
            * score_scale
        )
        return (jnp.where(allowed[None], scores, NEG), query_rows)

    def attend(context_buf, first_row):
        scores, query_rows = masked_scores(first_row)
        row_max = jnp.max(scores, -1, keepdims=True)
        expo = jnp.exp(scores - row_max)
        expsum = jnp.sum(expo, -1, keepdims=True)
        probs_low = (expo / expsum).astype(jnp.bfloat16)
        context = jnp.einsum(
            "hqk,hkd->hqd", probs_low, values_all, preferred_element_type=jnp.float32
        ).astype(jnp.bfloat16)
        context_buf = lax.dynamic_update_slice_in_dim(context_buf, context, first_row, 1)
        return (context_buf, (row_max + jnp.log(expsum))[:, :, 0])

    context_low, log_norm = lax.scan(
        attend, jnp.zeros((heads_here, group_rows, HD), jnp.bfloat16), starts
    )
    attn_sum = lax.psum_scatter(
        jnp.einsum(
            "hrd,hde->re", context_low, w_out_heads, preferred_element_type=jnp.float32
        ).astype(jnp.bfloat16),
        "tp",
        scatter_dimension=0,
        tiled=True,
    ).astype(jnp.float32)
    hidden = tokens + attn_sum + bias_out
    normed_two, unit_two, inverse_two = norm_rows(hidden, gain_two, shift_two)
    rows_two = lax.all_gather(normed_two.astype(jnp.bfloat16), "tp", axis=0, tiled=True)
    inner = jnp.dot(rows_two, w_in, preferred_element_type=jnp.float32) + bias_in
    activ, gelu_pull = jax.vjp(jax.nn.gelu, inner)
    activ_low = activ.astype(jnp.bfloat16)
    mixed = (
        hidden
        + lax.psum_scatter(
            jnp.dot(activ_low, w_down, preferred_element_type=jnp.float32).astype(jnp.bfloat16),
            "tp",
            scatter_dimension=0,
            tiled=True,
        ).astype(jnp.float32)
        + bias_down
    )
    grad_low = cotangent.astype(jnp.bfloat16)
    grad_rows = lax.all_gather(grad_low, "tp", axis=0, tiled=True)
    g_down = jnp.einsum("rf,rd->fd", activ_low, grad_rows, preferred_element_type=jnp.float32)
    grad_activ = jnp.einsum("rd,fd->rf", grad_rows, w_down, preferred_element_type=jnp.float32)
    grad_inner = gelu_pull(grad_activ)[0].astype(jnp.bfloat16)
    g_in = jnp.einsum("rd,rf->df", rows_two, grad_inner, preferred_element_type=jnp.float32)
    g_bias_in = jnp.sum(grad_inner.astype(jnp.float32), 0)
    ffn_blocks = jnp.concatenate(
        [
            to_columns(g_in).reshape(groups, in_count, BLOCK, BLOCK),
            to_rows(g_down).reshape(groups, in_count, BLOCK, BLOCK),
        ],
        1,
    )
    grad_normed_two = lax.psum_scatter(
        jnp.einsum("rf,df->rd", grad_inner, w_in, preferred_element_type=jnp.float32).astype(
            jnp.bfloat16
        ),
        "tp",
        scatter_dimension=0,
        tiled=True,
    ).astype(jnp.float32)
    grad_hidden = cotangent + norm_back(grad_normed_two, unit_two, inverse_two, gain_two)
    grad_attn_low = grad_hidden.astype(jnp.bfloat16)
    grad_attn_rows = lax.all_gather(grad_attn_low, "tp", axis=0, tiled=True)
    g_out = jnp.einsum(
        "hrd,re->hde", context_low, grad_attn_rows, preferred_element_type=jnp.float32
    ).reshape(feat_here, D)
    grad_context = jnp.einsum(
        "re,hde->hrd", grad_attn_rows, w_out_heads, preferred_element_type=jnp.float32
    ).astype(jnp.bfloat16)
    zero_heads = jnp.zeros((heads_here, group_rows, HD), jnp.float32)

    def attend_back(carry, inputs):
        grad_queries, grad_keys, grad_values = carry
        first_row, log_block = inputs
        scores, query_rows = masked_scores(first_row)
        probs = jnp.exp(scores - log_block[:, :, None])
        grad_ctx_rows = lax.dynamic_slice_in_dim(grad_context, first_row, span, 1)
        grad_probs = jnp.einsum(
            "hqd,hkd->hqk", grad_ctx_rows, values_all, preferred_element_type=jnp.float32
        )
        delta = jnp.sum(probs * grad_probs, -1, keepdims=True)
        grad_scores = (probs * (grad_probs - delta)).astype(jnp.bfloat16)
        query_part = (
            jnp.einsum("hqk,hkd->hqd", grad_scores, keys_all, preferred_element_type=jnp.float32)
            * score_scale
        )
        grad_queries = lax.dynamic_update_slice_in_dim(grad_queries, query_part, first_row, 1)
        grad_keys = (
            grad_keys
            + jnp.einsum(
                "hqk,hqd->hkd", grad_scores, query_rows, preferred_element_type=jnp.float32
            )
            * score_scale
        )
        grad_values = grad_values + jnp.einsum(
            "hqk,hqd->hkd",
            probs.astype(jnp.bfloat16),
            grad_ctx_rows,
            preferred_element_type=jnp.float32,
        )
        return ((grad_queries, grad_keys, grad_values), None)

    (grad_queries, grad_keys, grad_values), unused = lax.scan(
        attend_back, (zero_heads, zero_heads, zero_heads), (starts, log_norm)
    )
    grad_proj = jnp.stack([grad_queries, grad_keys, grad_values], 0).astype(jnp.bfloat16)
    proj_sums = jnp.sum(grad_proj.astype(jnp.float32), 2)
    g_bias_qv = jnp.stack([proj_sums[0], proj_sums[2]], 1).reshape(qv_width)
    g_qkv = jnp.einsum(
        "rx,chrd->xhcd", rows_one, grad_proj, preferred_element_type=jnp.float32
    ).reshape(D, qkv_cols)
    grad_normed_one = lax.psum_scatter(
        jnp.einsum(
            "chrd,xhcd->rx", grad_proj, w_qkv_heads, preferred_element_type=jnp.float32
        ).astype(jnp.bfloat16),
        "tp",
        scatter_dimension=0,
        tiled=True,
    ).astype(jnp.float32)
    input_grad = grad_hidden + norm_back(grad_normed_one, unit_one, inverse_one, gain_one)
    local_rows = jnp.stack(
        [
            jnp.sum(grad_normed_one * unit_one, 0),
            jnp.sum(grad_normed_one, 0),
            jnp.sum(grad_normed_two * unit_two, 0),
            jnp.sum(grad_normed_two, 0),
            jnp.sum(grad_hidden, 0),
            jnp.sum(cotangent, 0),
        ]
    )
    qv_rows = lax.dynamic_update_slice(
        jnp.zeros((2 * D,), jnp.float32), g_bias_qv, (tp_rank * qv_width,)
    ).reshape(2, D)
    in_rows = lax.dynamic_update_slice(
        jnp.zeros((FF,), jnp.float32), g_bias_in, (tp_rank * ff_here,)
    ).reshape(FF // D, D)
    vec_grads = lax.psum(jnp.concatenate([local_rows, qv_rows, in_rows], 0), ("grp", "tp"))
    attn_blocks = jnp.concatenate(
        [
            to_columns(g_qkv).reshape(groups, qkv_count, BLOCK, BLOCK),
            to_rows(g_out).reshape(groups, out_count, BLOCK, BLOCK),
        ],
        1,
    )
    every_block = jnp.concatenate([attn_blocks, ffn_blocks], 1).reshape(-1, BLOCK, BLOCK)
    weight_grads = lax.psum_scatter(
        every_block.astype(jnp.bfloat16), "grp", scatter_dimension=0, tiled=True
    ).astype(jnp.float32)
    scaled = weight_grads * token_total ** (-0.5)
    stat_left_new = DECAY * stat_left + (1.0 - DECAY) * jnp.einsum(
        "nij,nkj->nik", scaled, scaled, precision=lax.Precision.HIGHEST
    )
    stat_right_new = DECAY * stat_right + (1.0 - DECAY) * jnp.einsum(
        "nji,njk->nik", scaled, scaled, precision=lax.Precision.HIGHEST
    )
    shaped = jnp.einsum("nij,njk->nik", root_left, scaled, precision=lax.Precision.HIGHEST)
    shaped = jnp.einsum("nij,njk->nik", shaped, root_right, precision=lax.Precision.HIGHEST)
    momentum_new = BETA * momentum + shaped
    weights_new = weights - RATE * momentum_new
    vec_scaled = vec_grads * token_total ** (-0.5)
    vec_second_new = VEC_DECAY * vec_second + (1.0 - VEC_DECAY) * vec_scaled * vec_scaled
    vec_momentum_new = BETA * vec_momentum + vec_scaled * lax.rsqrt(vec_second_new + VEC_EPS)
    vec_new = vec_params - VEC_RATE * vec_momentum_new
    return (
        mixed,
        input_grad,
        weight_grads,
        stat_left_new,
        stat_right_new,
        momentum_new,
        weights_new,
        vec_grads,
        vec_second_new,
        vec_momentum_new,
        vec_new,
    )


MESH_ID = pl.DeviceIdType.MESH
LANES = 128
HALF = 64
VMEM_LIMIT = 62 * 2**20
ARTICLES = 4
GELU_A = (2.0 / 3.141592653589793) ** 0.5
GELU_B = 0.044715


def remote(src, dst, send_sem, recv_sem, device):
    return pltpu.make_async_remote_copy(
        src_ref=src,
        dst_ref=dst,
        send_sem=send_sem,
        recv_sem=recv_sem,
        device_id=device,
        device_id_type=MESH_ID,
    )


def place():
    grp = lax.axis_index("grp")
    return lax.div(grp, 4), lax.rem(lax.div(grp, 2), 2), lax.rem(grp, 2), lax.axis_index("tp")


def slot_of(z, y, c):
    return z * 4 + y * 2 + c


def lay_blocks(view_ref, stack):
    half = view_ref.shape[2] // 2

    def row(i, carry):
        tile = view_ref[i].T
        stack[pl.ds(i, half, stride=BLOCK), :] = jnp.concatenate([tile[:half], tile[half:]], 1)
        return carry

    lax.fori_loop(0, BLOCK, row, 0, unroll=8)


def piece_shapes():
    return ((768, LANES), (64, 512), (1024, LANES), (LANES, 1024))


def fold_tiles(value, mask):
    kept = jnp.where(mask, value, 0.0)
    halves = kept[:, :LANES] + kept[:, LANES:]
    return halves + pltpu.roll(halves, HALF, 1)


def update_kernel(
    scale,
    sum_q,
    sum_o,
    sum_i,
    sum_d,
    root_l,
    root_r,
    vec_g,
    vecs,
    vec_m,
    vec_s,
    mixed,
    input_grad,
    w,
    m,
    sl,
    sr,
    out_g,
    out_sl,
    out_sr,
    out_m,
    out_w,
    out_vg,
    out_vs,
    out_vm,
    out_v,
    out_mixed,
    out_input_grad,
    first,
    second,
):
    count = root_l.shape[2]
    bf = jnp.bfloat16
    out_mixed[...] = mixed[...]
    out_input_grad[...] = input_grad[...]

    @pl.when(pl.program_id(0) == 0)
    def _():
        total = vec_g[...]
        out_vg[...] = total
        scaled = total * scale
        fresh = VEC_DECAY * vec_s[...] + (1.0 - VEC_DECAY) * scaled * scaled
        out_vs[...] = fresh
        momentum = BETA * vec_m[...] + scaled * lax.rsqrt(fresh + VEC_EPS)
        out_vm[...] = momentum
        out_v[...] = vecs[...] - VEC_RATE * momentum
        rows = sum_q.shape[0]
        first[0:rows, 0:HALF] = sum_q[:, 0:HALF]
        first[rows : 2 * rows, 0:HALF] = sum_q[:, HALF:LANES]
        base = 2 * rows
        for b in range(8):
            first[base + b * 64 : base + b * 64 + 64, 0:HALF] = sum_o[:, b * HALF : (b + 1) * HALF]
        base += 512
        first[base : base + 1024, 0:HALF] = sum_i[:, 0:HALF]
        first[base + 1024 : base + 2048, 0:HALF] = sum_i[:, HALF:LANES]
        base += 2048
        for r in range(2):
            for b in range(16):
                at = base + (r * 16 + b) * 64
                first[at : at + 64, 0:HALF] = sum_d[r * 64 : r * 64 + 64, b * HALF : (b + 1) * HALF]

        def row(i, carry):
            both = jnp.concatenate([root_l[i], root_r[i]], 0)
            second[pl.ds(i, count, stride=BLOCK), :] = both.T
            return carry

        lax.fori_loop(0, BLOCK, row, 0, unroll=8)
        row_id = lax.broadcasted_iota(jnp.int32, (256, 256), 0)
        col_id = lax.broadcasted_iota(jnp.int32, (256, 256), 1)
        mask = lax.shift_right_logical(row_id, 6) == lax.shift_right_logical(col_id, 6)
        zero = jnp.zeros((256, 256), jnp.float32)

        def spread(v):
            return jnp.where(mask, jnp.concatenate([v, v, v, v], 1), zero).astype(bf)

        def four(k, carry):
            at = pl.ds(pl.multiple_of(k * 256, 256), 256)
            s32 = first[at, 0:HALF] * scale
            s = s32.astype(bf)
            left = second[at, 0:HALF]
            right = second[at, HALF:LANES].astype(bf)
            outer = lax.dot_general(s, s, (((1,), (1,)), ((), ())), preferred_element_type=jnp.float32)
            inner = lax.dot_general(spread(s32), s, (((0,), (0,)), ((), ())), preferred_element_type=jnp.float32)
            shaped = jnp.dot(spread(left), s, preferred_element_type=jnp.float32)
            shaped = jnp.dot(spread(shaped), right, preferred_element_type=jnp.float32)
            first[at, HALF:LANES] = fold_tiles(outer, mask)[:, HALF:LANES]
            second[at, 0:HALF] = inner
            second[at, HALF:LANES] = shaped
            return carry

        lax.fori_loop(0, count // 4, four, 0, unroll=4)

    i0 = pl.program_id(0) * w.shape[0]

    def rows_out(ii, carry):
        at = pl.ds(i0 + ii, count, stride=BLOCK)
        one = first[at, :].T
        two = second[at, :].T
        out_g[ii] = one[0:HALF]
        out_sl[ii] = DECAY * sl[ii] + (1.0 - DECAY) * one[HALF:LANES]
        out_sr[ii] = DECAY * sr[ii] + (1.0 - DECAY) * two[0:HALF]
        fresh = BETA * m[ii] + two[HALF:LANES]
        out_m[ii] = fresh
        out_w[ii] = w[ii] - RATE * fresh
        return carry

    lax.fori_loop(0, w.shape[0], rows_out, 0, unroll=True)


def update_blocks(sums, blocks, vec_grads, vecs, results, token_total):
    views = [jnp.transpose(a, (1, 2, 0)) for a in blocks]
    count = blocks[0].shape[0]
    rows = 8
    whole = pl.BlockSpec(memory_space=pltpu.VMEM)
    steps = BLOCK // rows
    some = pl.BlockSpec((results[0].shape[0] // steps, results[0].shape[1]), lambda i: (i, 0))
    part = pl.BlockSpec((rows, BLOCK, count), lambda i: (i, 0, 0))
    vec = jax.ShapeDtypeStruct(vec_grads.shape, jnp.float32)
    outs = pl.pallas_call(
        functools.partial(update_kernel, token_total ** (-0.5)),
        grid=(steps,),
        out_shape=[jax.ShapeDtypeStruct((BLOCK, BLOCK, count), jnp.float32)] * 5
        + [vec] * 4
        + [jax.ShapeDtypeStruct(a.shape, a.dtype) for a in results],
        in_specs=[whole] * 10 + [some] * 2 + [part] * 4,
        out_specs=[part] * 5 + [whole] * 4 + [some] * 2,
        scratch_shapes=[
            pltpu.VMEM((count * BLOCK, LANES), jnp.float32),
            pltpu.VMEM((count * BLOCK, LANES), jnp.float32),
        ],
        compiler_params=pltpu.CompilerParams(vmem_limit_bytes=VMEM_LIMIT),
        name="update_blocks",
    )(*sums, *views[4:], vec_grads, *vecs, *results, *views[:4])
    return [jnp.transpose(a, (2, 0, 1)) for a in outs[:5]], outs[5:9], outs[9:]


DEPTH = 4


def layer_kernel(
    lengths,
    order,
    view,
    tokens,
    cot,
    vecs,
    mixed,
    input_grad,
    sum_q,
    sum_o,
    sum_i,
    sum_d,
    vec_grads,
    gq,
    go,
    gi,
    gd,
    wqkv,
    cq,
    co,
    ci,
    cd,
    yq,
    yo,
    yi,
    yd,
    yv,
    zq,
    zo,
    zi,
    zd,
    zv,
    rows_one,
    rows_two,
    rows_t,
    grad_rows,
    grad_attn,
    probs,
    qkv,
    ctx,
    gctx,
    far,
    inx,
    go_x,
    ctx_x,
    macc,
    nacc,
    act,
    gin,
    bias_sum,
    qkv_bias,
    qv_sum,
    vin,
    vout,
    late,
    late_sum,
    late_in,
    recv,
    send_y,
    send_c,
    send_z,
    rc_recv,
    rc_send,
    ry_recv,
    ry_send,
    rz_recv,
    rz_send,
    x_send,
    x_recv,
    v_send,
    v_recv,
    l_send,
    l_recv,
    copy_sem,
):
    bf, f32 = jnp.bfloat16, jnp.float32
    z, y, c, t = place()
    me = slot_of(z, y, c)
    x_peer = (me, 1 - t)
    y_peer = (slot_of(z, 1 - y, c), t)
    c_peer = (slot_of(z, y, 1 - c), t)
    rows = tokens.shape[0]
    own = pl.ds(pl.multiple_of(t * rows, rows), rows)
    other = pl.ds(pl.multiple_of((1 - t) * rows, rows), rows)

    def lanes(start, size, unit):
        return pl.ds(pl.multiple_of(start, unit), size)

    gathered, core_in = (gq, go, gi, gd), (cq, co, ci, cd)
    y_in, z_in = (yq, yo, yi, yd, yv), (zq, zo, zi, zd, zv)
    sums = (sum_q, sum_o, sum_i, sum_d)
    Q, O, I, W, V = range(5)

    def dot(a, b):
        return jnp.dot(a, b, preferred_element_type=f32)

    def dot_nt(a, b):
        return lax.dot_general(a, b, (((1,), (1,)), ((), ())), preferred_element_type=f32)

    def dot_tn(a, b):
        return lax.dot_general(a, b, (((0,), (0,)), ((), ())), preferred_element_type=f32)

    def piece(k, zz, yy, cc):
        if k == O:
            return go.at[zz * 2 + yy, :, pl.ds(pl.multiple_of(cc * 512, 512), 512)]
        return gathered[k].at[slot_of(zz, yy, cc)]

    def near(s):
        return lax.rem(z + (1 - 2 * lax.div(z, 2)) * s + DEPTH, DEPTH)

    def ag_piece(k, zz, yy, cc):
        if k == W:
            return gd.at[slot_of(zz, yy, cc), 0:HALF]
        if k == V:
            return gd.at[slot_of(zz, yy, cc), HALF:LANES]
        return piece(k, zz, yy, cc)

    def ag_copy(k, zz, yy, way):
        src = ag_piece(k, zz, yy, c)
        sem = recv.at[k, slot_of(zz, yy, c)]
        if way == "up":
            return remote(src, src, send_z.at[k, 0, yy * DEPTH + zz], sem, (slot_of(z + 1, y, c), t))
        if way == "down":
            return remote(src, src, send_z.at[k, 1, yy * DEPTH + zz], sem, (slot_of(z - 1, y, c), t))
        if way == "y":
            return remote(src, src, send_y.at[k, zz], sem, y_peer)
        return remote(src, src, send_c.at[k, yy * DEPTH + zz], sem, c_peer)

    def ag_wait(k, zz, yy, cc):
        ref = ag_piece(k, zz, yy, cc)
        remote(ref, ref, send_y.at[k, 0], recv.at[k, slot_of(zz, yy, cc)], y_peer).wait_recv()

    def own_sends_z(k):
        @pl.when(z < DEPTH - 1)
        def _():
            ag_copy(k, z, y, "up").start()

        @pl.when(z > 0)
        def _():
            ag_copy(k, z, y, "down").start()

        ag_copy(k, z, y, "core").start()

    def own_sends_y(k):
        ag_copy(k, z, y, "y").start()

    def z_arrival(kinds, dist):
        @pl.when(z >= dist)
        def _():
            for k in kinds:
                ag_wait(k, z - dist, y, c)

                @pl.when(z < DEPTH - 1)
                def _():
                    ag_copy(k, z - dist, y, "up").start()

                ag_copy(k, z - dist, y, "y").start()
                ag_copy(k, z - dist, y, "core").start()

        @pl.when(z + dist < DEPTH)
        def _():
            for k in kinds:
                ag_wait(k, z + dist, y, c)

                @pl.when(z > 0)
                def _():
                    ag_copy(k, z + dist, y, "down").start()

                ag_copy(k, z + dist, y, "y").start()
                ag_copy(k, z + dist, y, "core").start()

    def y_arrival(kinds, dist):
        def one(zz):
            for k in kinds:
                ag_wait(k, zz, 1 - y, c)
                ag_copy(k, zz, 1 - y, "core").start()

        if dist == 0:
            one(z)
            return

        @pl.when(z >= dist)
        def _():
            one(z - dist)

        @pl.when(z + dist < DEPTH)
        def _():
            one(z + dist)

    def v_forward(zz, yy):
        ag_wait(V, zz, yy, c)

        @pl.when((zz <= z) & (z < DEPTH - 1))
        def _():
            ag_copy(V, zz, yy, "up").start()

        @pl.when((zz >= z) & (z > 0))
        def _():
            ag_copy(V, zz, yy, "down").start()

        ag_copy(V, zz, yy, "core").start()

    def v_arrival(dist):
        for yy in (y, 1 - y):

            @pl.when(z >= dist)
            def _():
                v_forward(z - dist, yy)

            @pl.when(z + dist < DEPTH)
            def _():
                v_forward(z + dist, yy)

    def drain(k, zz, yy):
        ag_copy(k, zz, yy, "core").wait_send()
        if k == V:

            @pl.when((yy == y) & (zz == z))
            def _():
                ag_copy(k, zz, yy, "y").wait_send()

            @pl.when((zz <= z) & (z < DEPTH - 1))
            def _():
                ag_copy(k, zz, yy, "up").wait_send()

            @pl.when((zz >= z) & (z > 0))
            def _():
                ag_copy(k, zz, yy, "down").wait_send()

            return

        @pl.when(yy == y)
        def _():
            ag_copy(k, zz, y, "y").wait_send()

            @pl.when((zz <= z) & (z < DEPTH - 1))
            def _():
                ag_copy(k, zz, y, "up").wait_send()

            @pl.when((zz >= z) & (z > 0))
            def _():
                ag_copy(k, zz, y, "down").wait_send()

    def add(dst, *terms):
        count, width = dst.shape
        step = min(count, 256 * LANES // width)

        def body(i, carry):
            at = pl.ds(pl.multiple_of(i * step, 16), step)
            total = terms[0][at, :].astype(f32)
            for term in terms[1:]:
                total = total + term[at, :].astype(f32)
            dst[at, :] = total.astype(dst.dtype)
            return carry

        lax.fori_loop(0, count // step, body, 0)

    side = lax.div(z, 2)
    end_z, inner_z = 3 * side, 1 + side
    is_end = z == end_z

    def rc_copy(k, zz, yy):
        at = zz * 2 + yy
        return remote(piece(k, zz, yy, 1 - c), core_in[k].at[at], rc_send.at[k, at], rc_recv.at[k, at], c_peer)

    def ry_copy(k, zz):
        if k == V:
            return remote(ag_piece(V, z, 1 - y, c), y_in[V].at[0], ry_send.at[V, 0], ry_recv.at[V, 0], y_peer)
        return remote(ag_piece(k, zz, 1 - y, c), y_in[k].at[zz], ry_send.at[k, zz], ry_recv.at[k, zz], y_peer)

    def z_slot(k, slot, yy):
        return z_in[k].at[slot * 2 + yy if k == V else slot]

    def z_sem(slot, yy):
        return slot * 2 + yy

    def rz_copy(k, s, yy, from_end):
        slot = s - 1 if from_end else {3: 0, 2: 1, 1: 3}[s]
        to = inner_z if from_end else {3: end_z, 2: 3 - end_z, 1: 3 - inner_z}[s]
        sent, landed = rz_send.at[k, (s - 1) * 2 + yy], rz_recv.at[k, z_sem(slot, yy)]
        return remote(ag_piece(k, near(s), yy, c), z_slot(k, slot, yy), sent, landed, (slot_of(to, y, c), t))

    def z_landed(k, slot, yy):
        ref = z_slot(k, slot, yy)
        remote(ref, ref, rz_send.at[k, 0], rz_recv.at[k, z_sem(slot, yy)], y_peer).wait_recv()
        return ref

    def y_landed(k, zz):
        ref = y_in[k].at[0 if k == V else zz]
        remote(ref, ref, ry_send.at[k, 0], ry_recv.at[k, 0 if k == V else zz], y_peer).wait_recv()
        return ref

    def rc_add(k, zz, yy):
        at = zz * 2 + yy
        remote(core_in[k].at[at], core_in[k].at[at], rc_send.at[k, 0], rc_recv.at[k, at], c_peer).wait_recv()
        mine = piece(k, zz, yy, c)
        add(mine, mine, core_in[k].at[at])

        @pl.when(yy != y)
        def _():
            ry_copy(k, zz).start()

    def z_step(k, s, yy, *terms):
        mine = ag_piece(k, near(s), yy, c)
        if terms:
            add(mine, mine, *terms)

        @pl.when(is_end)
        def _():
            rz_copy(k, s, yy, True).start()

        if s == 3:

            @pl.when(jnp.logical_not(is_end))
            def _():
                rz_copy(k, s, yy, False).start()

    def z_merge(k, s, yy):
        @pl.when(jnp.logical_not(is_end))
        def _():
            mine = ag_piece(k, near(s), yy, c)
            add(mine, mine, z_landed(k, s, yy))
            rz_copy(k, s, yy, False).start()

    def ry_add(k, s):
        z_step(k, s, y, y_landed(k, near(s)))

    def ry_merge(k, s):
        z_merge(k, s, y)

    def total_of(k):
        return sum_d.at[(k - W) * HALF : (k - W + 1) * HALF] if k >= W else sums[k]

    def z_total(k, yy, dst, *terms):
        mine = ag_piece(k, z, yy, c)
        first = z_landed(k, 0, yy)

        @pl.when(is_end)
        def _():
            add(dst, mine, first, z_landed(k, 1, yy), *terms)

        @pl.when(jnp.logical_not(is_end))
        def _():
            add(dst, mine, first, z_landed(k, 3, yy), *terms)

    def own_total(k):
        z_total(k, y, total_of(k), y_landed(k, z))

    def v_cross():
        mine = ag_piece(V, z, 1 - y, c)
        z_total(V, 1 - y, mine)
        ry_copy(V, z).start()

    def x_rows(ref, index):
        return remote(ref.at[own], ref.at[own], x_send.at[index], x_recv.at[index], x_peer)

    def x_rows_wait(ref, index):
        remote(ref.at[other], ref.at[other], x_send.at[index], x_recv.at[index], x_peer).wait_recv()

    def x_part(index):
        slot = 1 if index == 2 else 0
        return remote(far.at[slot], inx.at[slot], x_send.at[5 + index], x_recv.at[5 + index], x_peer)

    def by_rows(body, step=64):
        def run(i, carry):
            body(pl.multiple_of(i * step, step), step)
            return carry

        lax.fori_loop(0, rows // step, run, 0)

    def norm(value):
        average = jnp.mean(value, -1, keepdims=True)
        centred = value - average
        inverse = lax.rsqrt(jnp.mean(centred * centred, -1, keepdims=True) + EPS)
        return centred * inverse, inverse

    def norm_grad(grad, unit, inverse, gain):
        scaled = grad * gain
        return inverse * (
            scaled - jnp.mean(scaled, -1, keepdims=True) - unit * jnp.mean(scaled * unit, -1, keepdims=True)
        )

    def x_out():
        half = (slice(None), slice(None), lanes(c * 512, 512, 512))
        return remote(go.at[half], go_x.at[half], x_send.at[4], x_recv.at[4], x_peer)

    def x_out_core(cc):
        half = (slice(None), slice(None), lanes(cc * 512, 512, 512))
        return remote(go_x.at[half], go_x.at[half], x_send.at[9], x_recv.at[9], c_peer)

    def x_grad_context():
        return remote(ctx_x, gctx.at[own], x_send.at[10], x_recv.at[10], x_peer)

    def x_grad_context_wait():
        remote(gctx.at[other], gctx.at[other], x_send.at[10], x_recv.at[10], x_peer).wait_recv()

    stages = (x_peer, c_peer, y_peer)

    def v_copy(stage):
        return remote(vout.at[1 + stage], vin.at[stage], v_send.at[stage], v_recv.at[stage], stages[stage])

    def vz_copy(step):
        peer = (slot_of(lax.rem(z + step, DEPTH), y, c), t)
        return remote(vout.at[4], vin.at[3 + z], v_send.at[2 + step], v_recv.at[3 + z], peer)

    def early_rows(hop):
        if hop == 0:
            vout[1] = vout[0]
        else:
            v_copy(hop - 1).wait_recv()
            vout[1 + hop] = vout[hop] + vin[hop - 1]
        if hop < 3:
            v_copy(hop).start()
        else:
            for step in range(1, DEPTH):
                vz_copy(step).start()
            vin[3 + z] = vout[4]

    def late_turn(turn):
        dx, dy, dc = turn // 4, turn // 2 % 2, turn % 2
        xx, yy, cc = (1 - t if dx else t), (1 - y if dy else y), (1 - c if dc else c)
        return (slot_of(z, yy, cc), xx), xx * 4 + yy * 2 + cc

    def late_copy(turn):
        here = t * 4 + y * 2 + c
        return remote(late, late_in.at[here], l_send.at[turn], l_recv.at[here], late_turn(turn)[0])

    def late_wait(index):
        remote(late_in.at[index], late_in.at[index], l_send.at[0], l_recv.at[index], y_peer).wait_recv()

    def late_z(step):
        peer = (slot_of(lax.rem(z + step, DEPTH), y, c), t)
        return remote(late_sum, late_in.at[8 + z], l_send.at[7 + step], l_recv.at[8 + z], peer)

    barrier = pltpu.get_barrier_semaphore()
    z_peers = [(slot_of(lax.rem(z + step, DEPTH), y, c), t) for step in range(1, DEPTH)]
    everyone = [late_turn(turn)[0] for turn in range(1, 8)] + z_peers
    for device in everyone:
        pl.semaphore_signal(barrier, inc=1, device_id=device, device_id_type=MESH_ID)

    def prepare(held, stack):
        load = pltpu.make_async_copy(view, held, copy_sem.at[0])
        load.start()

        def first_norm(at, step):
            unit, inverse = norm(tokens[pl.ds(at, step), :])
            to = pl.ds(pl.multiple_of(t * rows + at, step), step)
            rows_one[to, :] = (unit * vecs[0:1, :] + vecs[1:2, :]).astype(bf)
            grad_rows[to, :] = cot[pl.ds(at, step), :].astype(bf)

        load.wait()
        lay_blocks(held, stack)

        def pair(left, right, count, left_high=False, right_high=False):
            first, second = stack[left : left + count, :], stack[right : right + count, :]
            first = pltpu.roll(first, HALF, 1) if left_high else first
            second = second if right_high else pltpu.roll(second, HALF, 1)
            lane = lax.broadcasted_iota(jnp.int32, (count, LANES), 1)
            return jnp.where(lane < HALF, first, second).astype(bf)

        n = gq.shape[1]
        gq[me] = pair(0, n, n)
        base = 2 * n
        wide = [pair(base + b * 64, base + b * 64 + 64, 64) for b in range(0, 8, 2)]
        go[z * 2 + y, :, lanes(c * 512, 512, 512)] = jnp.concatenate(wide, 1)
        pl.semaphore_wait(barrier, len(everyone))
        for k in (Q, O):
            own_sends_y(k)
            own_sends_z(k)
        by_rows(first_norm)
        x_rows(rows_one, 0).start()
        base += 512
        gi[me] = pair(base, 0, D, right_high=True)
        for r in range(2):
            for b in range(0, 16, 2):
                at = D + (r * 16 + b) * 64
                gd[me, r * 64 : r * 64 + 64, b * HALF : b * HALF + LANES] = pair(at, at + 64, 64, True, True)

    pl.run_scoped(
        prepare,
        pltpu.VMEM(view.shape, f32),
        pltpu.VMEM((view.shape[2] // 2 * BLOCK, LANES), f32),
    )
    x_rows(grad_rows, 1).start()
    z_arrival((Q, O), 1)
    y_arrival((Q, O), 0)
    for k in (I, W, V):
        own_sends_z(k)
    z_arrival((Q, O), 2)
    y_arrival((Q, O), 1)
    z_arrival((Q, O), 3)
    for k in (I, W, V):
        own_sends_y(k)

    def core_waits(kinds, zz):
        for k in kinds:
            for yy in (y, 1 - y):
                ag_wait(k, zz, yy, 1 - c)

    x_rows_wait(rows_one, 0)

    ends = []
    for p in range(ARTICLES):
        length = 0
        for a in range(ARTICLES):
            length = length + jnp.where(order[0, p] == a, lengths[0, a], 0)
        ends.append(length + ends[-1] if p else length)

    def allowed(first, count):
        ids = lax.broadcasted_iota(jnp.int32, (rows, 1), 0) + first
        start = jnp.zeros((rows, 1), jnp.int32)
        for end in ends:
            start = jnp.where(ids >= end, end, start)
        start = jnp.where(ids >= ends[-1], ids, start)
        keys = lax.broadcasted_iota(jnp.int32, (rows, count), 1)
        return (keys <= ids) & (keys >= start)

    scale = HD ** (-0.5)
    strip = 1024

    def assemble(h):
        for yy in range(2):
            even, odd = gq.at[slot_of(h, yy, 0)], gq.at[slot_of(h, yy, 1)]
            at = yy * 192
            wqkv[h, 0:768, at : at + 64] = even[:, 0:64]
            wqkv[h, 768:1024, at : at + 64] = even[0:256, 64:128]
            wqkv[h, 0:512, at + 64 : at + 128] = even[256:768, 64:128]
            wqkv[h, 512:1024, at + 64 : at + 128] = odd[0:512, 0:64]
            wqkv[h, 0:256, at + 128 : at + 192] = odd[512:768, 0:64]
            wqkv[h, 256:1024, at + 128 : at + 192] = odd[:, 64:128]

    def disassemble(h, value):
        for yy in range(2):
            even, odd = gq.at[slot_of(h, yy, 0)], gq.at[slot_of(h, yy, 1)]
            at = yy * 192
            even[:, 0:64] = value[0:768, at : at + 64]
            even[0:256, 64:128] = value[768:1024, at : at + 64]
            even[256:768, 64:128] = value[0:512, at + 64 : at + 128]
            odd[0:512, 0:64] = value[512:1024, at + 64 : at + 128]
            odd[512:768, 0:64] = value[0:256, at + 128 : at + 192]
            odd[:, 64:128] = value[256:1024, at + 128 : at + 192]

    qv = vecs[pl.ds(6 + t, 1), :]
    for h in range(DEPTH):
        none = jnp.zeros((1, HD), f32)
        qkv_bias[h] = jnp.concatenate([qv[:, h * 256 : h * 256 + 128], none, qv[:, h * 256 + 128 : h * 256 + 256]], 1)

    def head(h):
        core_waits((Q,), h)
        assemble(h)
        qkv[h] = (dot(rows_one[...], wqkv[h]) + qkv_bias[h]).astype(bf)
        for block in range(2):
            at, seen = slice(block * rows, (block + 1) * rows), (block + 1) * rows
            scores = dot_nt(qkv[h, at, 0:128], qkv[h, 0:seen, 128:256]) * scale
            scores = jnp.where(allowed(block * rows, seen), scores, NEG)
            expo = jnp.exp(scores - jnp.max(scores, -1, keepdims=True))
            low = (expo / jnp.sum(expo, -1, keepdims=True)).astype(bf)
            probs[h, at, 0:seen] = low
            ctx[at, lanes(h * HD, HD, HD)] = dot(low, qkv[h, 0:seen, 256:384]).astype(bf)

    head(near(0))
    y_arrival((Q, O), 2)
    head(near(1))
    y_arrival((Q, O), 3)
    head(near(2))
    z_arrival((I, W), 1)
    head(near(3))
    y_arrival((I, W), 0)
    v_forward(z, 1 - y)
    for zz in range(DEPTH):
        core_waits((O,), zz)

    def w_out(ref):
        return ref[...].reshape(DEPTH * HD, D)

    far[0] = dot(ctx[other, :], w_out(go)).astype(bf)
    x_part(0).start()
    mixed[...] = tokens[...] + dot(ctx[own, :], w_out(go)) + vecs[4:5, :]
    z_arrival((I, W), 2)
    y_arrival((I, W), 1)
    x_part(0).wait_recv()

    def second_norm(at, step):
        value = mixed[pl.ds(at, step), :] + inx[0, pl.ds(at, step), :].astype(f32)
        mixed[pl.ds(at, step), :] = value
        unit, inverse = norm(value)
        to = pl.ds(pl.multiple_of(t * rows + at, step), step)
        rows_two[to, :] = (unit * vecs[2:3, :] + vecs[3:4, :]).astype(bf)

    by_rows(second_norm)
    x_rows(rows_two, 2).start()
    x_out().start()
    v_arrival(1)
    z_arrival((I, W), 3)
    v_arrival(2)
    macc[...] = jnp.zeros_like(macc)
    nacc[...] = jnp.zeros_like(nacc)
    vout[...] = jnp.zeros_like(vout)
    x_rows_wait(grad_rows, 1)

    def ffn(half, zz):
        first = 4 * zz
        at = pl.ds(pl.multiple_of(lax.rem(t + half, 2) * rows, rows), rows)
        units = lanes(zz * 512, 512, 512)
        bias_row = vecs[pl.ds(8 + 2 * t + lax.div(zz, 2), 1), lanes(lax.rem(zz, 2) * 512, 512, 512)]

        def w_in(start, count):
            return jnp.concatenate([gi[first + j, start : start + count, :] for j in range(4)], 1)

        def w_down(start, count):
            return gd[pl.ds(first, 4), :, start : start + count].reshape(512, count)

        inner = dot(rows_two[at, :], w_in(0, D)) + bias_row
        square = inner * inner
        bent = jnp.tanh(GELU_A * inner * (1.0 + GELU_B * square))
        act[at, units] = (0.5 * inner * (1.0 + bent)).astype(bf)
        slope = 0.5 * (1.0 + bent) + 0.5 * inner * (1.0 - bent * bent) * (GELU_A * (1.0 + 3.0 * GELU_B * square))
        gin[at, units] = (dot_nt(grad_rows[at, :], w_down(0, D)) * slope).astype(bf)
        for nb in range(4):
            out = slice(nb * 256, nb * 256 + 256)
            nacc[at, out] += dot_nt(gin[at, units], w_in(nb * 256, 256))
            macc[at, out] += dot(act[at, units], w_down(nb * 256, 256))

    def ffn_grads(zz):
        first = 4 * zz
        units = lanes(zz * 512, 512, 512)
        for k in (I, W, V):
            for yy in range(2):
                drain(k, zz, yy)
        bias_sum[zz] = jnp.sum(gin[:, units].astype(f32), 0, keepdims=True)
        for nb in range(4):
            out = slice(nb * 256, nb * 256 + 256)
            part = dot(rows_t[out, :], gin[:, units]).astype(bf)
            for j in range(4):
                gi[first + j, out, :] = part[:, j * LANES : (j + 1) * LANES]
        for yy in (1 - y, y):
            rc_copy(I, zz, yy).start()
        act_t = act[:, units].T
        for nb in range(4):
            out = slice(nb * 256, nb * 256 + 256)
            part = dot(act_t, grad_rows[:, out]).astype(bf)
            gd[pl.ds(first, 4), :, out] = part.reshape(4, LANES, 256)
        for yy in (1 - y, y):
            rc_copy(W, zz, yy).start()

    def reduce_core(zz):
        for yy in (1 - y, y):
            for k in (I, W):
                rc_add(k, zz, yy)

    def v_step(s):
        for yy in (1 - y, y):
            z_step(V, s, yy)

    def v_merge(s):
        for yy in (1 - y, y):
            z_merge(V, s, yy)

    core_waits((I, W, V), z)
    ffn(0, z)
    y_arrival((I, W), 2)
    core_waits((I, W, V), near(1))
    ffn(0, near(1))
    x_rows_wait(rows_two, 2)
    rows_t[...] = rows_two[...].T

    def by_z(s, carry):
        @pl.when(s == 2)
        def _():
            v_arrival(3)
            y_arrival((I, W), 3)

        @pl.when(s >= 2)
        def _():
            core_waits((I, W, V), near(s))
            ffn(0, near(s))

        ffn(1, near(s))

        @pl.when(s == DEPTH - 1)
        def _():
            x_part(0).wait_send()
            far[0] = nacc[other, :].astype(bf)
            x_part(1).start()

        @pl.when(s > 0)
        def _():
            reduce_core(near(s - 1))

        for before in (1, 2):

            @pl.when(s == before + 1)
            def _():
                v_step(before)

        ffn_grads(near(s))
        return carry

    lax.fori_loop(0, DEPTH, by_z, 0)
    x_out().wait_recv()
    x_out_core(c).start()
    reduce_core(near(3))
    v_step(3)
    v_merge(1)
    for zz in range(DEPTH):
        for side in range(2):
            row, start = 8 + 2 * side + zz // 2, zz % 2 * 512
            vout[0, row : row + 1, start : start + 512] = jnp.where(t == side, bias_sum[zz], 0.0)
    rows_t[...] = rows_one[...].T
    x_part(1).wait_recv()

    def row_sum(row, value):
        vout[0, row : row + 1, :] += jnp.sum(value, 0, keepdims=True)

    def second_back(at, step):
        here = pl.ds(at, step)
        in_group = pl.ds(pl.multiple_of(t * rows + at, step), step)
        grad = nacc[in_group, :] + inx[0, here, :].astype(f32)
        unit, inverse = norm(mixed[here, :])
        back = cot[here, :] + norm_grad(grad, unit, inverse, vecs[2:3, :])
        input_grad[here, :] = back
        grad_attn[in_group, :] = back.astype(bf)
        row_sum(2, grad * unit)
        row_sum(3, grad)
        row_sum(4, back)
        row_sum(5, cot[here, :])

    by_rows(second_back)
    early_rows(0)
    x_out_core(1 - c).wait_recv()
    ctx_x[...] = dot_nt(grad_attn[own, :], w_out(go_x)).astype(bf)
    x_grad_context().start()
    gctx[own, :] = dot_nt(grad_attn[own, :], w_out(go)).astype(bf)
    for k in (I, W):
        ry_add(k, 1)
    v_merge(2)
    for zz in range(DEPTH):
        for yy in range(2):
            drain(O, zz, yy)
            drain(Q, zz, yy)
    def mixed_out(at, step):
        here = pl.ds(at, step)
        in_group = pl.ds(pl.multiple_of(t * rows + at, step), step)
        mixed[here, :] = mixed[here, :] + macc[in_group, :] + inx[1, here, :].astype(f32) + vecs[5:6, :]

    x_out().wait_send()
    x_grad_context_wait()
    x_rows(grad_attn, 3).start()
    far[1] = macc[other, :].astype(bf)

    def out_grads():
        x_rows_wait(grad_attn, 3)
        ctx_t = ctx[...].T
        for nb in range(4):
            at = slice(nb * 256, nb * 256 + 256)
            go[:, :, at] = dot(ctx_t, grad_attn[:, at]).astype(bf).reshape(8, 64, 256)
        for zz in range(DEPTH):
            for yy in range(2):
                rc_copy(O, zz, yy).start()

    def head_back(h, turn):
        q0, q1 = qkv[h, 0:rows, 0:128], qkv[h, rows : 2 * rows, 0:128]
        grads = []
        for block in range(2):
            at, seen = slice(block * rows, (block + 1) * rows), (block + 1) * rows
            low = probs[h, at, 0:seen]
            given = gctx[at, lanes(h * HD, HD, HD)]
            prob = low.astype(f32)
            grad_probs = dot_nt(given, qkv[h, 0:seen, 256:384])
            delta = jnp.sum(prob * grad_probs, -1, keepdims=True)
            grad_scores = (prob * (grad_probs - delta)).astype(bf)
            grad_q = dot(grad_scores, qkv[h, 0:seen, 128:256]) * scale
            grad_k = dot_tn(grad_scores, q1 if block else q0) * scale
            grad_v = dot_tn(low, given)
            grads.append((grad_q, grad_k, grad_v))
        (gq0, gk0, gv0), (gq1, gk1, gv1) = grads
        top = jnp.concatenate([gq0, gk0 + gk1[0:rows], gv0 + gv1[0:rows]], 1).astype(bf)
        low_half = jnp.concatenate([gq1, gk1[rows:], gv1[rows:]], 1).astype(bf)
        qkv[h, 0:rows, :] = top
        qkv[h, rows : 2 * rows, :] = low_half
        total = jnp.sum(top.astype(f32), 0, keepdims=True) + jnp.sum(low_half.astype(f32), 0, keepdims=True)
        qv_sum[h] = total
        for half in (other, own):
            product = dot_nt(qkv[h, half, :], wqkv[h])
            if turn == 0:
                nacc[half, :] = product
            else:
                nacc[half, :] += product
            if turn == DEPTH - 1 and half is other:
                x_part(1).wait_send()
                far[0] = nacc[other, :].astype(bf)
                x_part(3).start()
        part = dot(rows_t[...], qkv[h]).astype(bf)
        disassemble(h, part)
        for yy in (1 - y, y):
            rc_copy(Q, h, yy).start()

    for turn in range(DEPTH):
        head_back(near(DEPTH - 1 - turn), turn)
        if turn < 3:
            early_rows(turn + 1)
        if turn > 0:
            for yy in (1 - y, y):
                rc_add(Q, near(DEPTH - turn), yy)
        if turn == 0:
            v_cross()
        if turn == 1:
            for k in (I, W):
                ry_add(k, 2)
            out_grads()
            x_part(2).start()
        if turn == 2:
            for k in (I, W):
                ry_add(k, 3)
                ry_merge(k, 1)
            for yy in (1 - y, y):
                for s in (3, 2, 1, 0):
                    rc_add(O, near(s), yy)
            ry_add(Q, 3)
    for yy in (1 - y, y):
        rc_add(Q, z, yy)
    for k in (I, W):
        ry_merge(k, 2)
    ry_add(Q, 2)
    ry_merge(Q, 2)
    for s in (3, 2, 1):
        ry_add(O, s)
    x_part(2).wait_recv()
    by_rows(mixed_out)
    for k in (I, W):
        own_total(k)
    z_total(V, y, total_of(V), y_landed(V, z))
    ry_add(Q, 1)
    ry_merge(Q, 1)
    ry_merge(O, 2)
    ry_merge(O, 1)
    x_part(3).wait_recv()

    def first_back(at, step):
        here = pl.ds(at, step)
        in_group = pl.ds(pl.multiple_of(t * rows + at, step), step)
        grad = nacc[in_group, :] + inx[0, here, :].astype(f32)
        unit, inverse = norm(tokens[here, :])
        input_grad[here, :] = input_grad[here, :] + norm_grad(grad, unit, inverse, vecs[0:1, :])
        row_sum(0, grad * unit)
        row_sum(1, grad)

    by_rows(first_back)

    for h in range(DEPTH):
        for row in range(2):
            total = jnp.where(t == row, qv_sum[h], 0.0)
            vout[0, 6 + row : 7 + row, h * 256 : h * 256 + 128] = total[:, 0:128]
            vout[0, 6 + row : 7 + row, h * 256 + 128 : h * 256 + 256] = total[:, 256:384]
    for row in range(4):
        for j in range(8):
            late[row * 8 + j : row * 8 + j + 1, :] = vout[0, (0, 1, 6, 7)[row] : (0, 1, 6, 7)[row] + 1, j * LANES : (j + 1) * LANES]
    here = t * 4 + y * 2 + c
    late_in[here] = late[...]
    for turn in range(1, 8):
        late_copy(turn).start()
    own_total(O)
    for turn in range(1, 8):
        late_wait(late_turn(turn)[1])
    total = late_in[0]
    for index in range(1, 8):
        total = total + late_in[index]
    late_sum[...] = total
    late_in[8 + z] = total
    for step in range(1, DEPTH):
        late_z(step).start()
    own_total(Q)
    for step in range(1, DEPTH):
        late_wait(8 + lax.rem(z + step, DEPTH))
    total = ((late_in[8] + late_in[9]) + late_in[10]) + late_in[11]
    for step in range(1, DEPTH):
        zz = lax.rem(z + step, DEPTH)
        remote(vin.at[3 + zz], vin.at[3 + zz], v_send.at[0], v_recv.at[3 + zz], y_peer).wait_recv()
    early = ((vin[3] + vin[4]) + vin[5]) + vin[6]
    vec_grads[...] = early[0 : vec_grads.shape[0]]
    for row in range(4):
        for j in range(8):
            vec_grads[(0, 1, 6, 7)[row] : (0, 1, 6, 7)[row] + 1, j * LANES : (j + 1) * LANES] = total[row * 8 + j : row * 8 + j + 1, :]

    for stage in range(3):
        v_copy(stage).wait_send()
    for turn in range(1, 8):
        late_copy(turn).wait_send()
    for step in range(1, DEPTH):
        vz_copy(step).wait_send()
        late_z(step).wait_send()
    for index, ref in enumerate((rows_one, grad_rows, rows_two, grad_attn)):
        x_rows(ref, index).wait_send()
    for index in (2, 3):
        x_part(index).wait_send()
    x_out_core(c).wait_send()
    x_grad_context().wait_send()
    for k in range(4):
        for zz in range(DEPTH):
            for yy in range(2):
                rc_copy(k, zz, yy).wait_send()
            ry_copy(k, zz).wait_send()
        for s in range(1, DEPTH):
            rz_copy(k, s, y, True).wait_send()
    ry_copy(V, z).wait_send()
    for yy in range(2):
        for s in range(1, DEPTH):
            rz_copy(V, s, yy, True).wait_send()


def run_layer(tokens, cotangent, lengths, order, weights, vec_params):
    bf, f32 = jnp.bfloat16, jnp.float32
    rows = tokens.shape[0]
    group = 2 * rows
    owners = 16
    shapes = piece_shapes()
    view = jnp.transpose(weights, (1, 2, 0))
    vmem = pl.BlockSpec(memory_space=pltpu.VMEM)
    smem = pl.BlockSpec(memory_space=pltpu.SMEM)

    halved = shapes[:3] + ((HALF, D),)

    def many(count, kinds):
        return [pltpu.VMEM((count,) + s, bf) for s in kinds]

    full = pltpu.VMEM((group, D), bf)
    dma = pltpu.SemaphoreType.DMA
    return pl.pallas_call(
        layer_kernel,
        out_shape=[jax.ShapeDtypeStruct((rows, D), f32)] * 2
        + [jax.ShapeDtypeStruct(s, f32) for s in shapes]
        + [jax.ShapeDtypeStruct(vec_params.shape, f32)],
        in_specs=[smem, smem, pl.BlockSpec(memory_space=pl.ANY)] + [vmem] * 3,
        out_specs=[vmem] * 7,
        scratch_shapes=[
            pltpu.VMEM((owners,) + shapes[0], bf),
            pltpu.VMEM((owners // 2, BLOCK, D), bf),
            pltpu.VMEM((owners,) + shapes[2], bf),
            pltpu.VMEM((owners,) + shapes[3], bf),
            pltpu.VMEM((DEPTH, D, 3 * HD), bf),
        ]
        + many(2 * DEPTH, shapes)
        + many(DEPTH, halved)
        + many(1, halved[3:])
        + many(DEPTH, halved)
        + many(2 * DEPTH, halved[3:])
        + [
            full,
            full,
            pltpu.VMEM((D, group), bf),
            full,
            full,
            pltpu.VMEM((DEPTH, group, group), bf),
            pltpu.VMEM((DEPTH, group, 3 * HD), bf),
            pltpu.VMEM((group, DEPTH * HD), bf),
            pltpu.VMEM((group, DEPTH * HD), bf),
            pltpu.VMEM((2, rows, D), bf),
            pltpu.VMEM((2, rows, D), bf),
            pltpu.VMEM((owners // 2, BLOCK, D), bf),
            pltpu.VMEM((rows, DEPTH * HD), bf),
            pltpu.VMEM((group, D), f32),
            pltpu.VMEM((group, D), f32),
            pltpu.VMEM((group, 2 * D), bf),
            pltpu.VMEM((group, 2 * D), bf),
            pltpu.VMEM((DEPTH, 1, 512), f32),
            pltpu.VMEM((DEPTH, 1, 3 * HD), f32),
            pltpu.VMEM((DEPTH, 1, 3 * HD), f32),
            pltpu.VMEM((7, 16, D), f32),
            pltpu.VMEM((5, 16, D), f32),
            pltpu.VMEM((32, LANES), f32),
            pltpu.VMEM((32, LANES), f32),
            pltpu.VMEM((12, 32, LANES), f32),
            dma((5, owners)),
            dma((5, DEPTH)),
            dma((5, 2 * DEPTH)),
            dma((5, 2, 2 * DEPTH)),
            dma((4, 2 * DEPTH)),
            dma((4, 2 * DEPTH)),
            dma((5, DEPTH)),
            dma((5, DEPTH)),
            dma((5, 2 * DEPTH)),
            dma((5, 2 * DEPTH)),
            dma((11,)),
            dma((11,)),
            dma((6,)),
            dma((7,)),
            dma((11,)),
            dma((12,)),
            dma((1,)),
        ],
        compiler_params=pltpu.CompilerParams(
            collective_id=0, has_side_effects=True, vmem_limit_bytes=VMEM_LIMIT
        ),
        name="layer",
    )(lengths, order, view, tokens, cotangent, vec_params)


def per_device(
    grp_count,
    tp_count,
    tokens,
    cotangent,
    lengths,
    order,
    weights,
    momentum,
    stat_left,
    stat_right,
    root_left,
    root_right,
    vec_params,
    vec_momentum,
    vec_second,
):
    fits = grp_count == 4 * DEPTH and tp_count == 2 and tokens.shape[0] == 256
    if not fits or lengths.shape[1] != ARTICLES:
        return per_device_general(
            tokens,
            cotangent,
            lengths,
            order,
            weights,
            momentum,
            stat_left,
            stat_right,
            root_left,
            root_right,
            vec_params,
            vec_momentum,
            vec_second,
        )
    token_total = tokens.shape[0] * tp_count * grp_count
    mixed, input_grad, *sums, vec_grads = run_layer(tokens, cotangent, lengths, order, weights, vec_params)
    blocks, vecs, results = update_blocks(
        sums,
        (weights, momentum, stat_left, stat_right, root_left, root_right),
        vec_grads,
        (vec_params, vec_momentum, vec_second),
        (mixed, input_grad),
        token_total,
    )
    return (*results, *blocks, *vecs)


def solution(mesh):
    placed = (
        P(("grp", "tp"), None),
        P(("grp", "tp"), None),
        P("grp", None),
        P("grp", None),
        P(("tp", "grp"), None, None),
        P(("tp", "grp"), None, None),
        P(("tp", "grp"), None, None),
        P(("tp", "grp"), None, None),
        P(("tp", "grp"), None, None),
        P(("tp", "grp"), None, None),
        P(),
        P(),
        P(),
    )
    return jax.shard_map(
        functools.partial(per_device, mesh.shape["grp"], mesh.shape["tp"]),
        mesh=mesh,
        in_specs=placed,
        out_specs=(
            P(("grp", "tp"), None),
            P(("grp", "tp"), None),
            P(("tp", "grp"), None, None),
            P(("tp", "grp"), None, None),
            P(("tp", "grp"), None, None),
            P(("tp", "grp"), None, None),
            P(("tp", "grp"), None, None),
            P(),
            P(),
            P(),
            P(),
        ),
        check_vma=False,
    )
```

```python
import functools

import jax
import jax.numpy as jnp
from jax import lax
from jax.experimental import pallas as pl
from jax.experimental.pallas import tpu as pltpu
from jax.sharding import PartitionSpec as P

D = 1024
HEADS = 8
HD = 128
FF = 4096
BLOCK = 64


EPS = 1e-05
NEG = -1e30
DECAY = 0.9
BETA = 0.9
RATE = 0.05
VEC_DECAY = 0.9
VEC_RATE = 0.2
VEC_EPS = 1e-08


def norm_rows(value, gain, shift):
    average = jnp.mean(value, -1, keepdims=True)
    centred = value - average
    inverse = lax.rsqrt(jnp.mean(centred * centred, -1, keepdims=True) + EPS)
    normed = centred * inverse
    return (normed * gain + shift, normed, inverse)


def norm_back(grad_out, normed, inverse, gain):
    scaled = grad_out * gain
    return inverse * (
        scaled
        - jnp.mean(scaled, -1, keepdims=True)
        - normed * jnp.mean(scaled * normed, -1, keepdims=True)
    )


def segment_ids(lengths_row, order_row, group_rows):
    article_count = lengths_row.shape[0]
    slots = jnp.arange(article_count, dtype=jnp.int32)
    picks = (order_row[:, None] == slots[None, :]).astype(jnp.int32)
    packed = jnp.sum(picks * lengths_row[None, :], 1)
    ends = jnp.cumsum(packed)
    spots = jnp.arange(group_rows, dtype=jnp.int32)
    return jnp.sum((spots[:, None] >= ends[None, :]).astype(jnp.int32), 1)


def allowed_mask(row_ids, row_segs, segments, key_ids, article_count):
    causal = key_ids[None, :] <= row_ids[:, None]
    same = segments[None, :] == row_segs[:, None]
    alone = (row_segs[:, None] < article_count) | (key_ids[None, :] == row_ids[:, None])
    return causal & same & alone


def from_columns(tiles, row_total, col_total):
    return (
        tiles.reshape(col_total // BLOCK, row_total // BLOCK, BLOCK, BLOCK)
        .transpose(1, 2, 0, 3)
        .reshape(row_total, col_total)
    )


def from_rows(tiles, row_total, col_total):
    return (
        tiles.reshape(row_total // BLOCK, col_total // BLOCK, BLOCK, BLOCK)
        .transpose(0, 2, 1, 3)
        .reshape(row_total, col_total)
    )


def to_columns(matrix):
    row_total, col_total = matrix.shape
    return (
        matrix.reshape(row_total // BLOCK, BLOCK, col_total // BLOCK, BLOCK)
        .transpose(2, 0, 1, 3)
        .reshape(-1, BLOCK, BLOCK)
    )


def to_rows(matrix):
    row_total, col_total = matrix.shape
    return (
        matrix.reshape(row_total // BLOCK, BLOCK, col_total // BLOCK, BLOCK)
        .transpose(0, 2, 1, 3)
        .reshape(-1, BLOCK, BLOCK)
    )


def per_device_general(
    tokens,
    cotangent,
    lengths,
    order,
    weights,
    momentum,
    stat_left,
    stat_right,
    root_left,
    root_right,
    vec_params,
    vec_momentum,
    vec_second,
):
    groups = lax.axis_size("grp")
    tp_size = lax.axis_size("tp")
    tp_rank = lax.axis_index("tp")
    tok_rows = tokens.shape[0]
    group_rows = tok_rows * tp_size
    article_count = lengths.shape[1]
    owners = groups * tp_size
    block_area = BLOCK * BLOCK * owners
    qkv_count = 3 * D * D // block_area
    out_count = D * D // block_area
    in_count = D * FF // block_area
    owned_blocks = weights.shape[0]
    heads_here = HEADS // tp_size
    qkv_cols = 3 * D // tp_size
    feat_here = D // tp_size
    ff_here = FF // tp_size
    qv_width = 2 * D // tp_size
    token_total = group_rows * groups
    gathered = lax.all_gather(weights.astype(jnp.bfloat16), "grp", axis=0, tiled=True)
    per_owner = gathered.reshape(groups, owned_blocks, BLOCK, BLOCK)
    marks = [0, qkv_count, qkv_count + out_count, qkv_count + out_count + in_count, owned_blocks]
    pieces = [
        per_owner[:, marks[index] : marks[index + 1]].reshape(-1, BLOCK, BLOCK)
        for index in range(4)
    ]
    w_qkv = from_columns(pieces[0], D, qkv_cols)
    w_out = from_rows(pieces[1], feat_here, D)
    w_in = from_columns(pieces[2], D, ff_here)
    w_down = from_rows(pieces[3], ff_here, D)
    w_qkv_heads = w_qkv.reshape(D, heads_here, 3, HD)
    w_out_heads = w_out.reshape(heads_here, HD, D)
    segments = segment_ids(lengths[0], order[0], group_rows)
    gain_one = vec_params[0]
    shift_one = vec_params[1]
    gain_two = vec_params[2]
    shift_two = vec_params[3]
    bias_out = vec_params[4]
    bias_down = vec_params[5]
    qv_here = lax.dynamic_slice_in_dim(
        vec_params[6:8].reshape(2 * D), tp_rank * qv_width, qv_width
    ).reshape(heads_here, 2, HD)
    bias_heads = jnp.stack(
        [qv_here[:, 0], jnp.zeros((heads_here, HD), jnp.float32), qv_here[:, 1]], 0
    )[:, :, None, :]
    bias_in = lax.dynamic_slice_in_dim(vec_params[8:].reshape(FF), tp_rank * ff_here, ff_here)
    normed_one, unit_one, inverse_one = norm_rows(tokens, gain_one, shift_one)
    rows_one = lax.all_gather(normed_one.astype(jnp.bfloat16), "tp", axis=0, tiled=True)
    projected = (
        jnp.einsum("rx,xhcd->chrd", rows_one, w_qkv_heads, preferred_element_type=jnp.float32)
        + bias_heads
    ).astype(jnp.bfloat16)
    queries = projected[0]
    keys_all = projected[1]
    values_all = projected[2]
    span = min(512, group_rows)
    starts = jnp.arange(group_rows // span, dtype=jnp.int32) * span
    key_ids = jnp.arange(group_rows, dtype=jnp.int32)
    score_scale = HD ** (-0.5)

    def masked_scores(first_row):
        row_ids = first_row + jnp.arange(span, dtype=jnp.int32)
        row_segs = lax.dynamic_slice_in_dim(segments, first_row, span, 0)
        allowed = allowed_mask(row_ids, row_segs, segments, key_ids, article_count)
        query_rows = lax.dynamic_slice_in_dim(queries, first_row, span, 1)
        scores = (
            jnp.einsum("hqd,hkd->hqk", query_rows, keys_all, preferred_element_type=jnp.float32)
            * score_scale
        )
        return (jnp.where(allowed[None], scores, NEG), query_rows)

    def attend(context_buf, first_row):
        scores, query_rows = masked_scores(first_row)
        row_max = jnp.max(scores, -1, keepdims=True)
        expo = jnp.exp(scores - row_max)
        expsum = jnp.sum(expo, -1, keepdims=True)
        probs_low = (expo / expsum).astype(jnp.bfloat16)
        context = jnp.einsum(
            "hqk,hkd->hqd", probs_low, values_all, preferred_element_type=jnp.float32
        ).astype(jnp.bfloat16)
        context_buf = lax.dynamic_update_slice_in_dim(context_buf, context, first_row, 1)
        return (context_buf, (row_max + jnp.log(expsum))[:, :, 0])

    context_low, log_norm = lax.scan(
        attend, jnp.zeros((heads_here, group_rows, HD), jnp.bfloat16), starts
    )
    attn_sum = lax.psum_scatter(
        jnp.einsum(
            "hrd,hde->re", context_low, w_out_heads, preferred_element_type=jnp.float32
        ).astype(jnp.bfloat16),
        "tp",
        scatter_dimension=0,
        tiled=True,
    ).astype(jnp.float32)
    hidden = tokens + attn_sum + bias_out
    normed_two, unit_two, inverse_two = norm_rows(hidden, gain_two, shift_two)
    rows_two = lax.all_gather(normed_two.astype(jnp.bfloat16), "tp", axis=0, tiled=True)
    inner = jnp.dot(rows_two, w_in, preferred_element_type=jnp.float32) + bias_in
    activ, gelu_pull = jax.vjp(jax.nn.gelu, inner)
    activ_low = activ.astype(jnp.bfloat16)
    mixed = (
        hidden
        + lax.psum_scatter(
            jnp.dot(activ_low, w_down, preferred_element_type=jnp.float32).astype(jnp.bfloat16),
            "tp",
            scatter_dimension=0,
            tiled=True,
        ).astype(jnp.float32)
        + bias_down
    )
    grad_low = cotangent.astype(jnp.bfloat16)
    grad_rows = lax.all_gather(grad_low, "tp", axis=0, tiled=True)
    g_down = jnp.einsum("rf,rd->fd", activ_low, grad_rows, preferred_element_type=jnp.float32)
    grad_activ = jnp.einsum("rd,fd->rf", grad_rows, w_down, preferred_element_type=jnp.float32)
    grad_inner = gelu_pull(grad_activ)[0].astype(jnp.bfloat16)
    g_in = jnp.einsum("rd,rf->df", rows_two, grad_inner, preferred_element_type=jnp.float32)
    g_bias_in = jnp.sum(grad_inner.astype(jnp.float32), 0)
    ffn_blocks = jnp.concatenate(
        [
            to_columns(g_in).reshape(groups, in_count, BLOCK, BLOCK),
            to_rows(g_down).reshape(groups, in_count, BLOCK, BLOCK),
        ],
        1,
    )
    grad_normed_two = lax.psum_scatter(
        jnp.einsum("rf,df->rd", grad_inner, w_in, preferred_element_type=jnp.float32).astype(
            jnp.bfloat16
        ),
        "tp",
        scatter_dimension=0,
        tiled=True,
    ).astype(jnp.float32)
    grad_hidden = cotangent + norm_back(grad_normed_two, unit_two, inverse_two, gain_two)
    grad_attn_low = grad_hidden.astype(jnp.bfloat16)
    grad_attn_rows = lax.all_gather(grad_attn_low, "tp", axis=0, tiled=True)
    g_out = jnp.einsum(
        "hrd,re->hde", context_low, grad_attn_rows, preferred_element_type=jnp.float32
    ).reshape(feat_here, D)
    grad_context = jnp.einsum(
        "re,hde->hrd", grad_attn_rows, w_out_heads, preferred_element_type=jnp.float32
    ).astype(jnp.bfloat16)
    zero_heads = jnp.zeros((heads_here, group_rows, HD), jnp.float32)

    def attend_back(carry, inputs):
        grad_queries, grad_keys, grad_values = carry
        first_row, log_block = inputs
        scores, query_rows = masked_scores(first_row)
        probs = jnp.exp(scores - log_block[:, :, None])
        grad_ctx_rows = lax.dynamic_slice_in_dim(grad_context, first_row, span, 1)
        grad_probs = jnp.einsum(
            "hqd,hkd->hqk", grad_ctx_rows, values_all, preferred_element_type=jnp.float32
        )
        delta = jnp.sum(probs * grad_probs, -1, keepdims=True)
        grad_scores = (probs * (grad_probs - delta)).astype(jnp.bfloat16)
        query_part = (
            jnp.einsum("hqk,hkd->hqd", grad_scores, keys_all, preferred_element_type=jnp.float32)
            * score_scale
        )
        grad_queries = lax.dynamic_update_slice_in_dim(grad_queries, query_part, first_row, 1)
        grad_keys = (
            grad_keys
            + jnp.einsum(
                "hqk,hqd->hkd", grad_scores, query_rows, preferred_element_type=jnp.float32
            )
            * score_scale
        )
        grad_values = grad_values + jnp.einsum(
            "hqk,hqd->hkd",
            probs.astype(jnp.bfloat16),
            grad_ctx_rows,
            preferred_element_type=jnp.float32,
        )
        return ((grad_queries, grad_keys, grad_values), None)

    (grad_queries, grad_keys, grad_values), unused = lax.scan(
        attend_back, (zero_heads, zero_heads, zero_heads), (starts, log_norm)
    )
    grad_proj = jnp.stack([grad_queries, grad_keys, grad_values], 0).astype(jnp.bfloat16)
    proj_sums = jnp.sum(grad_proj.astype(jnp.float32), 2)
    g_bias_qv = jnp.stack([proj_sums[0], proj_sums[2]], 1).reshape(qv_width)
    g_qkv = jnp.einsum(
        "rx,chrd->xhcd", rows_one, grad_proj, preferred_element_type=jnp.float32
    ).reshape(D, qkv_cols)
    grad_normed_one = lax.psum_scatter(
        jnp.einsum(
            "chrd,xhcd->rx", grad_proj, w_qkv_heads, preferred_element_type=jnp.float32
        ).astype(jnp.bfloat16),
        "tp",
        scatter_dimension=0,
        tiled=True,
    ).astype(jnp.float32)
    input_grad = grad_hidden + norm_back(grad_normed_one, unit_one, inverse_one, gain_one)
    local_rows = jnp.stack(
        [
            jnp.sum(grad_normed_one * unit_one, 0),
            jnp.sum(grad_normed_one, 0),
            jnp.sum(grad_normed_two * unit_two, 0),
            jnp.sum(grad_normed_two, 0),
            jnp.sum(grad_hidden, 0),
            jnp.sum(cotangent, 0),
        ]
    )
    qv_rows = lax.dynamic_update_slice(
        jnp.zeros((2 * D,), jnp.float32), g_bias_qv, (tp_rank * qv_width,)
    ).reshape(2, D)
    in_rows = lax.dynamic_update_slice(
        jnp.zeros((FF,), jnp.float32), g_bias_in, (tp_rank * ff_here,)
    ).reshape(FF // D, D)
    vec_grads = lax.psum(jnp.concatenate([local_rows, qv_rows, in_rows], 0), ("grp", "tp"))
    attn_blocks = jnp.concatenate(
        [
            to_columns(g_qkv).reshape(groups, qkv_count, BLOCK, BLOCK),
            to_rows(g_out).reshape(groups, out_count, BLOCK, BLOCK),
        ],
        1,
    )
    every_block = jnp.concatenate([attn_blocks, ffn_blocks], 1).reshape(-1, BLOCK, BLOCK)
    weight_grads = lax.psum_scatter(
        every_block.astype(jnp.bfloat16), "grp", scatter_dimension=0, tiled=True
    ).astype(jnp.float32)
    scaled = weight_grads * token_total ** (-0.5)
    stat_left_new = DECAY * stat_left + (1.0 - DECAY) * jnp.einsum(
        "nij,nkj->nik", scaled, scaled, precision=lax.Precision.HIGHEST
    )
    stat_right_new = DECAY * stat_right + (1.0 - DECAY) * jnp.einsum(
        "nji,njk->nik", scaled, scaled, precision=lax.Precision.HIGHEST
    )
    shaped = jnp.einsum("nij,njk->nik", root_left, scaled, precision=lax.Precision.HIGHEST)
    shaped = jnp.einsum("nij,njk->nik", shaped, root_right, precision=lax.Precision.HIGHEST)
    momentum_new = BETA * momentum + shaped
    weights_new = weights - RATE * momentum_new
    vec_scaled = vec_grads * token_total ** (-0.5)
    vec_second_new = VEC_DECAY * vec_second + (1.0 - VEC_DECAY) * vec_scaled * vec_scaled
    vec_momentum_new = BETA * vec_momentum + vec_scaled * lax.rsqrt(vec_second_new + VEC_EPS)
    vec_new = vec_params - VEC_RATE * vec_momentum_new
    return (
        mixed,
        input_grad,
        weight_grads,
        stat_left_new,
        stat_right_new,
        momentum_new,
        weights_new,
        vec_grads,
        vec_second_new,
        vec_momentum_new,
        vec_new,
    )


MESH_ID = pl.DeviceIdType.MESH
LANES = 128
HALF = 64
VMEM_LIMIT = 62 * 2**20
ARTICLES = 4
GELU_A = (2.0 / 3.141592653589793) ** 0.5
GELU_B = 0.044715


def remote(src, dst, send_sem, recv_sem, device):
    return pltpu.make_async_remote_copy(
        src_ref=src,
        dst_ref=dst,
        send_sem=send_sem,
        recv_sem=recv_sem,
        device_id=device,
        device_id_type=MESH_ID,
    )


def place():
    grp = lax.axis_index("grp")
    return lax.div(grp, 4), lax.rem(lax.div(grp, 2), 2), lax.rem(grp, 2), lax.axis_index("tp")


def slot_of(z, y, c):
    return z * 4 + y * 2 + c


def lay_blocks(view_ref, stack):
    half = view_ref.shape[2] // 2

    def row(i, carry):
        tile = view_ref[i].T
        stack[pl.ds(i, half, stride=BLOCK), :] = jnp.concatenate([tile[:half], tile[half:]], 1)
        return carry

    lax.fori_loop(0, BLOCK, row, 0, unroll=8)


def piece_shapes():
    return ((768, LANES), (64, 512), (1024, LANES), (LANES, 1024))


def fold_tiles(value, mask):
    kept = jnp.where(mask, value, 0.0)
    halves = kept[:, :LANES] + kept[:, LANES:]
    return halves + pltpu.roll(halves, HALF, 1)


def update_kernel(
    scale,
    sum_q,
    sum_o,
    sum_i,
    sum_d,
    root_l,
    root_r,
    vec_g,
    vecs,
    vec_m,
    vec_s,
    mixed,
    input_grad,
    w,
    m,
    sl,
    sr,
    out_g,
    out_sl,
    out_sr,
    out_m,
    out_w,
    out_vg,
    out_vs,
    out_vm,
    out_v,
    out_mixed,
    out_input_grad,
    first,
    second,
):
    count = root_l.shape[2]
    bf = jnp.bfloat16
    out_mixed[...] = mixed[...]
    out_input_grad[...] = input_grad[...]

    @pl.when(pl.program_id(0) == 0)
    def _():
        total = vec_g[...]
        out_vg[...] = total
        scaled = total * scale
        fresh = VEC_DECAY * vec_s[...] + (1.0 - VEC_DECAY) * scaled * scaled
        out_vs[...] = fresh
        momentum = BETA * vec_m[...] + scaled * lax.rsqrt(fresh + VEC_EPS)
        out_vm[...] = momentum
        out_v[...] = vecs[...] - VEC_RATE * momentum
        rows = sum_q.shape[0]
        first[0:rows, 0:HALF] = sum_q[:, 0:HALF]
        first[rows : 2 * rows, 0:HALF] = sum_q[:, HALF:LANES]
        base = 2 * rows
        for b in range(8):
            first[base + b * 64 : base + b * 64 + 64, 0:HALF] = sum_o[:, b * HALF : (b + 1) * HALF]
        base += 512
        first[base : base + 1024, 0:HALF] = sum_i[:, 0:HALF]
        first[base + 1024 : base + 2048, 0:HALF] = sum_i[:, HALF:LANES]
        base += 2048
        for r in range(2):
            for b in range(16):
                at = base + (r * 16 + b) * 64
                first[at : at + 64, 0:HALF] = sum_d[r * 64 : r * 64 + 64, b * HALF : (b + 1) * HALF]

        def row(i, carry):
            both = jnp.concatenate([root_l[i], root_r[i]], 0)
            second[pl.ds(i, count, stride=BLOCK), :] = both.T
            return carry

        lax.fori_loop(0, BLOCK, row, 0, unroll=8)
        row_id = lax.broadcasted_iota(jnp.int32, (256, 256), 0)
        col_id = lax.broadcasted_iota(jnp.int32, (256, 256), 1)
        mask = lax.shift_right_logical(row_id, 6) == lax.shift_right_logical(col_id, 6)
        zero = jnp.zeros((256, 256), jnp.float32)

        def spread(v):
            return jnp.where(mask, jnp.concatenate([v, v, v, v], 1), zero).astype(bf)

        def four(k, carry):
            at = pl.ds(pl.multiple_of(k * 256, 256), 256)
            s32 = first[at, 0:HALF] * scale
            s = s32.astype(bf)
            left = second[at, 0:HALF]
            right = second[at, HALF:LANES].astype(bf)
            outer = lax.dot_general(s, s, (((1,), (1,)), ((), ())), preferred_element_type=jnp.float32)
            inner = lax.dot_general(spread(s32), s, (((0,), (0,)), ((), ())), preferred_element_type=jnp.float32)
            shaped = jnp.dot(spread(left), s, preferred_element_type=jnp.float32)
            shaped = jnp.dot(spread(shaped), right, preferred_element_type=jnp.float32)
            first[at, HALF:LANES] = fold_tiles(outer, mask)[:, HALF:LANES]
            second[at, 0:HALF] = inner
            second[at, HALF:LANES] = shaped
            return carry

        lax.fori_loop(0, count // 4, four, 0, unroll=4)

    i0 = pl.program_id(0) * w.shape[0]

    def rows_out(ii, carry):
        at = pl.ds(i0 + ii, count, stride=BLOCK)
        one = first[at, :].T
        two = second[at, :].T
        out_g[ii] = one[0:HALF]
        out_sl[ii] = DECAY * sl[ii] + (1.0 - DECAY) * one[HALF:LANES]
        out_sr[ii] = DECAY * sr[ii] + (1.0 - DECAY) * two[0:HALF]
        fresh = BETA * m[ii] + two[HALF:LANES]
        out_m[ii] = fresh
        out_w[ii] = w[ii] - RATE * fresh
        return carry

    lax.fori_loop(0, w.shape[0], rows_out, 0, unroll=True)


def update_blocks(sums, blocks, vec_grads, vecs, results, token_total):
    views = [jnp.transpose(a, (1, 2, 0)) for a in blocks]
    count = blocks[0].shape[0]
    rows = 8
    whole = pl.BlockSpec(memory_space=pltpu.VMEM)
    steps = BLOCK // rows
    some = pl.BlockSpec((results[0].shape[0] // steps, results[0].shape[1]), lambda i: (i, 0))
    part = pl.BlockSpec((rows, BLOCK, count), lambda i: (i, 0, 0))
    vec = jax.ShapeDtypeStruct(vec_grads.shape, jnp.float32)
    outs = pl.pallas_call(
        functools.partial(update_kernel, token_total ** (-0.5)),
        grid=(steps,),
        out_shape=[jax.ShapeDtypeStruct((BLOCK, BLOCK, count), jnp.float32)] * 5
        + [vec] * 4
        + [jax.ShapeDtypeStruct(a.shape, a.dtype) for a in results],
        in_specs=[whole] * 10 + [some] * 2 + [part] * 4,
        out_specs=[part] * 5 + [whole] * 4 + [some] * 2,
        scratch_shapes=[
            pltpu.VMEM((count * BLOCK, LANES), jnp.float32),
            pltpu.VMEM((count * BLOCK, LANES), jnp.float32),
        ],
        compiler_params=pltpu.CompilerParams(vmem_limit_bytes=VMEM_LIMIT),
        name="update_blocks",
    )(*sums, *views[4:], vec_grads, *vecs, *results, *views[:4])
    return [jnp.transpose(a, (2, 0, 1)) for a in outs[:5]], outs[5:9], outs[9:]


DEPTH = 4


def layer_kernel(
    lengths,
    order,
    view,
    tokens,
    cot,
    vecs,
    mixed,
    input_grad,
    sum_q,
    sum_o,
    sum_i,
    sum_d,
    vec_grads,
    gq,
    go,
    gi,
    gd,
    wqkv,
    cq,
    co,
    ci,
    cd,
    yq,
    yo,
    yi,
    yd,
    yv,
    zq,
    zo,
    zi,
    zd,
    zv,
    rows_one,
    rows_two,
    rows_t,
    grad_rows,
    grad_attn,
    probs,
    qkv,
    ctx,
    gctx,
    far,
    inx,
    go_x,
    ctx_x,
    macc,
    nacc,
    act,
    gin,
    bias_sum,
    qkv_bias,
    qv_sum,
    vin,
    vout,
    late,
    late_sum,
    late_in,
    recv,
    send_y,
    send_c,
    send_z,
    rc_recv,
    rc_send,
    ry_recv,
    ry_send,
    rz_recv,
    rz_send,
    x_send,
    x_recv,
    v_send,
    v_recv,
    l_send,
    l_recv,
    copy_sem,
):
    bf, f32 = jnp.bfloat16, jnp.float32
    z, y, c, t = place()
    me = slot_of(z, y, c)
    x_peer = (me, 1 - t)
    y_peer = (slot_of(z, 1 - y, c), t)
    c_peer = (slot_of(z, y, 1 - c), t)
    rows = tokens.shape[0]
    own = pl.ds(pl.multiple_of(t * rows, rows), rows)
    other = pl.ds(pl.multiple_of((1 - t) * rows, rows), rows)

    def lanes(start, size, unit):
        return pl.ds(pl.multiple_of(start, unit), size)

    gathered, core_in = (gq, go, gi, gd), (cq, co, ci, cd)
    y_in, z_in = (yq, yo, yi, yd, yv), (zq, zo, zi, zd, zv)
    sums = (sum_q, sum_o, sum_i, sum_d)
    Q, O, I, W, V = range(5)

    def dot(a, b):
        return jnp.dot(a, b, preferred_element_type=f32)

    def dot_nt(a, b):
        return lax.dot_general(a, b, (((1,), (1,)), ((), ())), preferred_element_type=f32)

    def dot_tn(a, b):
        return lax.dot_general(a, b, (((0,), (0,)), ((), ())), preferred_element_type=f32)

    def piece(k, zz, yy, cc):
        if k == O:
            return go.at[zz * 2 + yy, :, pl.ds(pl.multiple_of(cc * 512, 512), 512)]
        return gathered[k].at[slot_of(zz, yy, cc)]

    def near(s):
        return lax.rem(z + (1 - 2 * lax.div(z, 2)) * s + DEPTH, DEPTH)

    def ag_piece(k, zz, yy, cc):
        if k == W:
            return gd.at[slot_of(zz, yy, cc), 0:HALF]
        if k == V:
            return gd.at[slot_of(zz, yy, cc), HALF:LANES]
        return piece(k, zz, yy, cc)

    def ag_copy(k, zz, yy, way):
        src = ag_piece(k, zz, yy, c)
        sem = recv.at[k, slot_of(zz, yy, c)]
        if way == "up":
            return remote(src, src, send_z.at[k, 0, yy * DEPTH + zz], sem, (slot_of(z + 1, y, c), t))
        if way == "down":
            return remote(src, src, send_z.at[k, 1, yy * DEPTH + zz], sem, (slot_of(z - 1, y, c), t))
        if way == "y":
            return remote(src, src, send_y.at[k, zz], sem, y_peer)
        return remote(src, src, send_c.at[k, yy * DEPTH + zz], sem, c_peer)

    def ag_wait(k, zz, yy, cc):
        ref = ag_piece(k, zz, yy, cc)
        remote(ref, ref, send_y.at[k, 0], recv.at[k, slot_of(zz, yy, cc)], y_peer).wait_recv()

    def own_sends_z(k):
        @pl.when(z < DEPTH - 1)
        def _():
            ag_copy(k, z, y, "up").start()

        @pl.when(z > 0)
        def _():
            ag_copy(k, z, y, "down").start()

        ag_copy(k, z, y, "core").start()

    def own_sends_y(k):
        ag_copy(k, z, y, "y").start()

    def z_arrival(kinds, dist):
        @pl.when(z >= dist)
        def _():
            for k in kinds:
                ag_wait(k, z - dist, y, c)

                @pl.when(z < DEPTH - 1)
                def _():
                    ag_copy(k, z - dist, y, "up").start()

                ag_copy(k, z - dist, y, "y").start()
                ag_copy(k, z - dist, y, "core").start()

        @pl.when(z + dist < DEPTH)
        def _():
            for k in kinds:
                ag_wait(k, z + dist, y, c)

                @pl.when(z > 0)
                def _():
                    ag_copy(k, z + dist, y, "down").start()

                ag_copy(k, z + dist, y, "y").start()
                ag_copy(k, z + dist, y, "core").start()

    def y_arrival(kinds, dist):
        def one(zz):
            for k in kinds:
                ag_wait(k, zz, 1 - y, c)
                ag_copy(k, zz, 1 - y, "core").start()

        if dist == 0:
            one(z)
            return

        @pl.when(z >= dist)
        def _():
            one(z - dist)

        @pl.when(z + dist < DEPTH)
        def _():
            one(z + dist)

    def v_forward(zz, yy):
        ag_wait(V, zz, yy, c)

        @pl.when((zz <= z) & (z < DEPTH - 1))
        def _():
            ag_copy(V, zz, yy, "up").start()

        @pl.when((zz >= z) & (z > 0))
        def _():
            ag_copy(V, zz, yy, "down").start()

        ag_copy(V, zz, yy, "core").start()

    def v_arrival(dist):
        for yy in (y, 1 - y):

            @pl.when(z >= dist)
            def _():
                v_forward(z - dist, yy)

            @pl.when(z + dist < DEPTH)
            def _():
                v_forward(z + dist, yy)

    def drain(k, zz, yy):
        ag_copy(k, zz, yy, "core").wait_send()
        if k == V:

            @pl.when((yy == y) & (zz == z))
            def _():
                ag_copy(k, zz, yy, "y").wait_send()

            @pl.when((zz <= z) & (z < DEPTH - 1))
            def _():
                ag_copy(k, zz, yy, "up").wait_send()

            @pl.when((zz >= z) & (z > 0))
            def _():
                ag_copy(k, zz, yy, "down").wait_send()

            return

        @pl.when(yy == y)
        def _():
            ag_copy(k, zz, y, "y").wait_send()

            @pl.when((zz <= z) & (z < DEPTH - 1))
            def _():
                ag_copy(k, zz, y, "up").wait_send()

            @pl.when((zz >= z) & (z > 0))
            def _():
                ag_copy(k, zz, y, "down").wait_send()

    def add(dst, *terms):
        count, width = dst.shape
        step = min(count, 256 * LANES // width)

        def body(i, carry):
            at = pl.ds(pl.multiple_of(i * step, 16), step)
            total = terms[0][at, :].astype(f32)
            for term in terms[1:]:
                total = total + term[at, :].astype(f32)
            dst[at, :] = total.astype(dst.dtype)
            return carry

        lax.fori_loop(0, count // step, body, 0)

    side = lax.div(z, 2)
    end_z, inner_z = 3 * side, 1 + side
    is_end = z == end_z

    def rc_copy(k, zz, yy):
        at = zz * 2 + yy
        return remote(piece(k, zz, yy, 1 - c), core_in[k].at[at], rc_send.at[k, at], rc_recv.at[k, at], c_peer)

    def ry_copy(k, zz):
        if k == V:
            return remote(ag_piece(V, z, 1 - y, c), y_in[V].at[0], ry_send.at[V, 0], ry_recv.at[V, 0], y_peer)
        return remote(ag_piece(k, zz, 1 - y, c), y_in[k].at[zz], ry_send.at[k, zz], ry_recv.at[k, zz], y_peer)

    def z_slot(k, slot, yy):
        return z_in[k].at[slot * 2 + yy if k == V else slot]

    def z_sem(slot, yy):
        return slot * 2 + yy

    def rz_copy(k, s, yy, from_end):
        slot = s - 1 if from_end else {3: 0, 2: 1, 1: 3}[s]
        to = inner_z if from_end else {3: end_z, 2: 3 - end_z, 1: 3 - inner_z}[s]
        sent, landed = rz_send.at[k, (s - 1) * 2 + yy], rz_recv.at[k, z_sem(slot, yy)]
        return remote(ag_piece(k, near(s), yy, c), z_slot(k, slot, yy), sent, landed, (slot_of(to, y, c), t))

    def z_landed(k, slot, yy):
        ref = z_slot(k, slot, yy)
        remote(ref, ref, rz_send.at[k, 0], rz_recv.at[k, z_sem(slot, yy)], y_peer).wait_recv()
        return ref

    def y_landed(k, zz):
        ref = y_in[k].at[0 if k == V else zz]
        remote(ref, ref, ry_send.at[k, 0], ry_recv.at[k, 0 if k == V else zz], y_peer).wait_recv()
        return ref

    def rc_add(k, zz, yy):
        at = zz * 2 + yy
        remote(core_in[k].at[at], core_in[k].at[at], rc_send.at[k, 0], rc_recv.at[k, at], c_peer).wait_recv()
        mine = piece(k, zz, yy, c)
        add(mine, mine, core_in[k].at[at])

        @pl.when(yy != y)
        def _():
            ry_copy(k, zz).start()

    def z_step(k, s, yy, *terms):
        mine = ag_piece(k, near(s), yy, c)
        if terms:
            add(mine, mine, *terms)

        @pl.when(is_end)
        def _():
            rz_copy(k, s, yy, True).start()

        if s == 3:

            @pl.when(jnp.logical_not(is_end))
            def _():
                rz_copy(k, s, yy, False).start()

    def z_merge(k, s, yy):
        @pl.when(jnp.logical_not(is_end))
        def _():
            mine = ag_piece(k, near(s), yy, c)
            add(mine, mine, z_landed(k, s, yy))
            rz_copy(k, s, yy, False).start()

    def ry_add(k, s):
        z_step(k, s, y, y_landed(k, near(s)))

    def ry_merge(k, s):
        z_merge(k, s, y)

    def total_of(k):
        return sum_d.at[(k - W) * HALF : (k - W + 1) * HALF] if k >= W else sums[k]

    def z_total(k, yy, dst, *terms):
        mine = ag_piece(k, z, yy, c)
        first = z_landed(k, 0, yy)

        @pl.when(is_end)
        def _():
            add(dst, mine, first, z_landed(k, 1, yy), *terms)

        @pl.when(jnp.logical_not(is_end))
        def _():
            add(dst, mine, first, z_landed(k, 3, yy), *terms)

    def own_total(k):
        z_total(k, y, total_of(k), y_landed(k, z))

    def v_cross():
        mine = ag_piece(V, z, 1 - y, c)
        z_total(V, 1 - y, mine)
        ry_copy(V, z).start()

    def x_rows(ref, index):
        return remote(ref.at[own], ref.at[own], x_send.at[index], x_recv.at[index], x_peer)

    def x_rows_wait(ref, index):
        remote(ref.at[other], ref.at[other], x_send.at[index], x_recv.at[index], x_peer).wait_recv()

    def x_part(index):
        slot = 1 if index == 2 else 0
        return remote(far.at[slot], inx.at[slot], x_send.at[5 + index], x_recv.at[5 + index], x_peer)

    def by_rows(body, step=64):
        def run(i, carry):
            body(pl.multiple_of(i * step, step), step)
            return carry

        lax.fori_loop(0, rows // step, run, 0)

    def norm(value):
        average = jnp.mean(value, -1, keepdims=True)
        centred = value - average
        inverse = lax.rsqrt(jnp.mean(centred * centred, -1, keepdims=True) + EPS)
        return centred * inverse, inverse

    def norm_grad(grad, unit, inverse, gain):
        scaled = grad * gain
        return inverse * (
            scaled - jnp.mean(scaled, -1, keepdims=True) - unit * jnp.mean(scaled * unit, -1, keepdims=True)
        )

    def x_out():
        half = (slice(None), slice(None), lanes(c * 512, 512, 512))
        return remote(go.at[half], go_x.at[half], x_send.at[4], x_recv.at[4], x_peer)

    def x_out_core(cc):
        half = (slice(None), slice(None), lanes(cc * 512, 512, 512))
        return remote(go_x.at[half], go_x.at[half], x_send.at[9], x_recv.at[9], c_peer)

    def x_grad_context():
        return remote(ctx_x, gctx.at[own], x_send.at[10], x_recv.at[10], x_peer)

    def x_grad_context_wait():
        remote(gctx.at[other], gctx.at[other], x_send.at[10], x_recv.at[10], x_peer).wait_recv()

    stages = (x_peer, c_peer, y_peer)

    def v_copy(stage):
        return remote(vout.at[1 + stage], vin.at[stage], v_send.at[stage], v_recv.at[stage], stages[stage])

    def vz_copy(step):
        peer = (slot_of(lax.rem(z + step, DEPTH), y, c), t)
        return remote(vout.at[4], vin.at[3 + z], v_send.at[2 + step], v_recv.at[3 + z], peer)

    def early_rows(hop):
        if hop == 0:
            vout[1] = vout[0]
        else:
            v_copy(hop - 1).wait_recv()
            vout[1 + hop] = vout[hop] + vin[hop - 1]
        if hop < 3:
            v_copy(hop).start()
        else:
            for step in range(1, DEPTH):
                vz_copy(step).start()
            vin[3 + z] = vout[4]

    def late_turn(turn):
        dx, dy, dc = turn // 4, turn // 2 % 2, turn % 2
        xx, yy, cc = (1 - t if dx else t), (1 - y if dy else y), (1 - c if dc else c)
        return (slot_of(z, yy, cc), xx), xx * 4 + yy * 2 + cc

    def late_copy(turn):
        here = t * 4 + y * 2 + c
        return remote(late, late_in.at[here], l_send.at[turn], l_recv.at[here], late_turn(turn)[0])

    def late_wait(index):
        remote(late_in.at[index], late_in.at[index], l_send.at[0], l_recv.at[index], y_peer).wait_recv()

    def late_z(step):
        peer = (slot_of(lax.rem(z + step, DEPTH), y, c), t)
        return remote(late_sum, late_in.at[8 + z], l_send.at[7 + step], l_recv.at[8 + z], peer)

    barrier = pltpu.get_barrier_semaphore()
    z_peers = [(slot_of(lax.rem(z + step, DEPTH), y, c), t) for step in range(1, DEPTH)]
    everyone = [late_turn(turn)[0] for turn in range(1, 8)] + z_peers
    for device in everyone:
        pl.semaphore_signal(barrier, inc=1, device_id=device, device_id_type=MESH_ID)

    def prepare(held, stack):
        load = pltpu.make_async_copy(view, held, copy_sem.at[0])
        load.start()

        def first_norm(at, step):
            unit, inverse = norm(tokens[pl.ds(at, step), :])
            to = pl.ds(pl.multiple_of(t * rows + at, step), step)
            rows_one[to, :] = (unit * vecs[0:1, :] + vecs[1:2, :]).astype(bf)
            grad_rows[to, :] = cot[pl.ds(at, step), :].astype(bf)

        load.wait()
        lay_blocks(held, stack)

        def pair(left, right, count, left_high=False, right_high=False):
            first, second = stack[left : left + count, :], stack[right : right + count, :]
            first = pltpu.roll(first, HALF, 1) if left_high else first
            second = second if right_high else pltpu.roll(second, HALF, 1)
            lane = lax.broadcasted_iota(jnp.int32, (count, LANES), 1)
            return jnp.where(lane < HALF, first, second).astype(bf)

        n = gq.shape[1]
        gq[me] = pair(0, n, n)
        base = 2 * n
        wide = [pair(base + b * 64, base + b * 64 + 64, 64) for b in range(0, 8, 2)]
        go[z * 2 + y, :, lanes(c * 512, 512, 512)] = jnp.concatenate(wide, 1)
        pl.semaphore_wait(barrier, len(everyone))
        for k in (Q, O):
            own_sends_y(k)
            own_sends_z(k)
        by_rows(first_norm)
        x_rows(rows_one, 0).start()
        base += 512
        gi[me] = pair(base, 0, D, right_high=True)
        for r in range(2):
            for b in range(0, 16, 2):
                at = D + (r * 16 + b) * 64
                gd[me, r * 64 : r * 64 + 64, b * HALF : b * HALF + LANES] = pair(at, at + 64, 64, True, True)

    pl.run_scoped(
        prepare,
        pltpu.VMEM(view.shape, f32),
        pltpu.VMEM((view.shape[2] // 2 * BLOCK, LANES), f32),
    )
    x_rows(grad_rows, 1).start()
    z_arrival((Q, O), 1)
    y_arrival((Q, O), 0)
    z_arrival((Q, O), 2)
    for k in (I, W, V):
        own_sends_z(k)
    own_sends_y(I)
    y_arrival((Q, O), 1)

    def core_waits(kinds, zz):
        for k in kinds:
            for yy in (y, 1 - y):
                ag_wait(k, zz, yy, 1 - c)

    x_rows_wait(rows_one, 0)

    ends = []
    for p in range(ARTICLES):
        length = 0
        for a in range(ARTICLES):
            length = length + jnp.where(order[0, p] == a, lengths[0, a], 0)
        ends.append(length + ends[-1] if p else length)

    def allowed(first, count):
        ids = lax.broadcasted_iota(jnp.int32, (rows, 1), 0) + first
        start = jnp.zeros((rows, 1), jnp.int32)
        for end in ends:
            start = jnp.where(ids >= end, end, start)
        start = jnp.where(ids >= ends[-1], ids, start)
        keys = lax.broadcasted_iota(jnp.int32, (rows, count), 1)
        return (keys <= ids) & (keys >= start)

    scale = HD ** (-0.5)
    strip = 1024

    def assemble(h):
        for yy in range(2):
            even, odd = gq.at[slot_of(h, yy, 0)], gq.at[slot_of(h, yy, 1)]
            at = yy * 192
            wqkv[h, 0:768, at : at + 64] = even[:, 0:64]
            wqkv[h, 768:1024, at : at + 64] = even[0:256, 64:128]
            wqkv[h, 0:512, at + 64 : at + 128] = even[256:768, 64:128]
            wqkv[h, 512:1024, at + 64 : at + 128] = odd[0:512, 0:64]
            wqkv[h, 0:256, at + 128 : at + 192] = odd[512:768, 0:64]
            wqkv[h, 256:1024, at + 128 : at + 192] = odd[:, 64:128]

    def disassemble(h, value):
        for yy in range(2):
            even, odd = gq.at[slot_of(h, yy, 0)], gq.at[slot_of(h, yy, 1)]
            at = yy * 192
            even[:, 0:64] = value[0:768, at : at + 64]
            even[0:256, 64:128] = value[768:1024, at : at + 64]
            even[256:768, 64:128] = value[0:512, at + 64 : at + 128]
            odd[0:512, 0:64] = value[512:1024, at + 64 : at + 128]
            odd[512:768, 0:64] = value[0:256, at + 128 : at + 192]
            odd[:, 64:128] = value[256:1024, at + 128 : at + 192]

    qv = vecs[pl.ds(6 + t, 1), :]
    for h in range(DEPTH):
        none = jnp.zeros((1, HD), f32)
        qkv_bias[h] = jnp.concatenate([qv[:, h * 256 : h * 256 + 128], none, qv[:, h * 256 + 128 : h * 256 + 256]], 1)

    def head(h):
        core_waits((Q,), h)
        assemble(h)
        qkv[h] = (dot(rows_one[...], wqkv[h]) + qkv_bias[h]).astype(bf)
        for block in range(2):
            at, seen = slice(block * rows, (block + 1) * rows), (block + 1) * rows
            scores = dot_nt(qkv[h, at, 0:128], qkv[h, 0:seen, 128:256]) * scale
            scores = jnp.where(allowed(block * rows, seen), scores, NEG)
            expo = jnp.exp(scores - jnp.max(scores, -1, keepdims=True))
            low = (expo / jnp.sum(expo, -1, keepdims=True)).astype(bf)
            probs[h, at, 0:seen] = low
            ctx[at, lanes(h * HD, HD, HD)] = dot(low, qkv[h, 0:seen, 256:384]).astype(bf)

    head(near(0))
    z_arrival((Q, O), 3)
    own_sends_y(W)
    own_sends_y(V)
    head(near(1))
    y_arrival((Q, O), 2)
    head(near(2))
    y_arrival((Q, O), 3)
    z_arrival((I, W), 1)
    head(near(3))
    y_arrival((I, W), 0)
    v_forward(z, 1 - y)
    for zz in range(DEPTH):
        core_waits((O,), zz)

    def w_out(ref):
        return ref[...].reshape(DEPTH * HD, D)

    far[0] = dot(ctx[other, :], w_out(go)).astype(bf)
    x_part(0).start()
    mixed[...] = tokens[...] + dot(ctx[own, :], w_out(go)) + vecs[4:5, :]
    z_arrival((I, W), 2)
    y_arrival((I, W), 1)
    x_part(0).wait_recv()

    def second_norm(at, step):
        value = mixed[pl.ds(at, step), :] + inx[0, pl.ds(at, step), :].astype(f32)
        mixed[pl.ds(at, step), :] = value
        unit, inverse = norm(value)
        to = pl.ds(pl.multiple_of(t * rows + at, step), step)
        rows_two[to, :] = (unit * vecs[2:3, :] + vecs[3:4, :]).astype(bf)

    by_rows(second_norm)
    x_rows(rows_two, 2).start()
    z_arrival((I, W), 3)
    macc[...] = jnp.zeros_like(macc)
    nacc[...] = jnp.zeros_like(nacc)
    vout[...] = jnp.zeros_like(vout)
    x_rows_wait(grad_rows, 1)

    def ffn(half, zz):
        first = 4 * zz
        at = pl.ds(pl.multiple_of(lax.rem(t + half, 2) * rows, rows), rows)
        units = lanes(zz * 512, 512, 512)
        bias_row = vecs[pl.ds(8 + 2 * t + lax.div(zz, 2), 1), lanes(lax.rem(zz, 2) * 512, 512, 512)]

        def w_in(start, count):
            return jnp.concatenate([gi[first + j, start : start + count, :] for j in range(4)], 1)

        def w_down(start, count):
            return gd[pl.ds(first, 4), :, start : start + count].reshape(512, count)

        inner = dot(rows_two[at, :], w_in(0, D)) + bias_row
        square = inner * inner
        bent = jnp.tanh(GELU_A * inner * (1.0 + GELU_B * square))
        act[at, units] = (0.5 * inner * (1.0 + bent)).astype(bf)
        slope = 0.5 * (1.0 + bent) + 0.5 * inner * (1.0 - bent * bent) * (GELU_A * (1.0 + 3.0 * GELU_B * square))
        gin[at, units] = (dot_nt(grad_rows[at, :], w_down(0, D)) * slope).astype(bf)
        for nb in range(4):
            out = slice(nb * 256, nb * 256 + 256)
            nacc[at, out] += dot_nt(gin[at, units], w_in(nb * 256, 256))
            macc[at, out] += dot(act[at, units], w_down(nb * 256, 256))

    def ffn_grads(zz):
        first = 4 * zz
        units = lanes(zz * 512, 512, 512)
        for k in (I, W, V):
            for yy in range(2):
                drain(k, zz, yy)
        bias_sum[zz] = jnp.sum(gin[:, units].astype(f32), 0, keepdims=True)
        for nb in range(4):
            out = slice(nb * 256, nb * 256 + 256)
            part = dot(rows_t[out, :], gin[:, units]).astype(bf)
            for j in range(4):
                gi[first + j, out, :] = part[:, j * LANES : (j + 1) * LANES]
        for yy in (1 - y, y):
            rc_copy(I, zz, yy).start()
        act_t = act[:, units].T
        for nb in range(4):
            out = slice(nb * 256, nb * 256 + 256)
            part = dot(act_t, grad_rows[:, out]).astype(bf)
            gd[pl.ds(first, 4), :, out] = part.reshape(4, LANES, 256)
        for yy in (1 - y, y):
            rc_copy(W, zz, yy).start()

    def reduce_core(zz):
        for yy in (1 - y, y):
            for k in (I, W):
                rc_add(k, zz, yy)

    def v_step(s):
        for yy in (1 - y, y):
            z_step(V, s, yy)

    def v_merge(s):
        for yy in (1 - y, y):
            z_merge(V, s, yy)

    core_waits((I, W, V), z)
    ffn(0, z)
    v_arrival(1)
    y_arrival((I, W), 2)
    core_waits((I, W, V), near(1))
    ffn(0, near(1))
    v_arrival(2)
    x_rows_wait(rows_two, 2)
    x_out().start()
    rows_t[...] = rows_two[...].T

    def by_z(s, carry):
        @pl.when(s == 2)
        def _():
            v_arrival(3)
            y_arrival((I, W), 3)

        @pl.when(s >= 2)
        def _():
            core_waits((I, W, V), near(s))
            ffn(0, near(s))

        ffn(1, near(s))

        @pl.when(s == DEPTH - 1)
        def _():
            x_part(0).wait_send()
            far[0] = nacc[other, :].astype(bf)
            x_part(1).start()

        ffn_grads(near(s))

        @pl.when(s > 0)
        def _():
            reduce_core(near(s - 1))

        for before in (1, 2):

            @pl.when(s == before + 1)
            def _():
                v_step(before)

        return carry

    lax.fori_loop(0, DEPTH, by_z, 0)
    x_out().wait_recv()
    x_out_core(c).start()
    reduce_core(near(3))
    v_step(3)
    v_merge(1)
    for zz in range(DEPTH):
        for side in range(2):
            row, start = 8 + 2 * side + zz // 2, zz % 2 * 512
            vout[0, row : row + 1, start : start + 512] = jnp.where(t == side, bias_sum[zz], 0.0)
    rows_t[...] = rows_one[...].T
    x_part(1).wait_recv()

    def row_sum(row, value):
        vout[0, row : row + 1, :] += jnp.sum(value, 0, keepdims=True)

    def second_back(at, step):
        here = pl.ds(at, step)
        in_group = pl.ds(pl.multiple_of(t * rows + at, step), step)
        grad = nacc[in_group, :] + inx[0, here, :].astype(f32)
        unit, inverse = norm(mixed[here, :])
        back = cot[here, :] + norm_grad(grad, unit, inverse, vecs[2:3, :])
        input_grad[here, :] = back
        grad_attn[in_group, :] = back.astype(bf)
        row_sum(2, grad * unit)
        row_sum(3, grad)
        row_sum(4, back)
        row_sum(5, cot[here, :])

    by_rows(second_back)
    early_rows(0)
    x_out_core(1 - c).wait_recv()
    ctx_x[...] = dot_nt(grad_attn[own, :], w_out(go_x)).astype(bf)
    x_grad_context().start()
    gctx[own, :] = dot_nt(grad_attn[own, :], w_out(go)).astype(bf)
    for s in (1, 2):
        for k in (I, W):
            ry_add(k, s)
    v_merge(2)
    for zz in range(DEPTH):
        for yy in range(2):
            drain(O, zz, yy)
            drain(Q, zz, yy)
    def mixed_out(at, step):
        here = pl.ds(at, step)
        in_group = pl.ds(pl.multiple_of(t * rows + at, step), step)
        mixed[here, :] = mixed[here, :] + macc[in_group, :] + inx[1, here, :].astype(f32) + vecs[5:6, :]

    x_out().wait_send()
    x_grad_context_wait()
    x_rows(grad_attn, 3).start()
    far[1] = macc[other, :].astype(bf)

    def out_grads():
        x_rows_wait(grad_attn, 3)
        ctx_t = ctx[...].T
        for nb in range(4):
            at = slice(nb * 256, nb * 256 + 256)
            go[:, :, at] = dot(ctx_t, grad_attn[:, at]).astype(bf).reshape(8, 64, 256)
        for zz in range(DEPTH):
            for yy in range(2):
                rc_copy(O, zz, yy).start()

    def head_back(h, turn):
        q0, q1 = qkv[h, 0:rows, 0:128], qkv[h, rows : 2 * rows, 0:128]
        grads = []
        for block in range(2):
            at, seen = slice(block * rows, (block + 1) * rows), (block + 1) * rows
            low = probs[h, at, 0:seen]
            given = gctx[at, lanes(h * HD, HD, HD)]
            prob = low.astype(f32)
            grad_probs = dot_nt(given, qkv[h, 0:seen, 256:384])
            delta = jnp.sum(prob * grad_probs, -1, keepdims=True)
            grad_scores = (prob * (grad_probs - delta)).astype(bf)
            grad_q = dot(grad_scores, qkv[h, 0:seen, 128:256]) * scale
            grad_k = dot_tn(grad_scores, q1 if block else q0) * scale
            grad_v = dot_tn(low, given)
            grads.append((grad_q, grad_k, grad_v))
        (gq0, gk0, gv0), (gq1, gk1, gv1) = grads
        top = jnp.concatenate([gq0, gk0 + gk1[0:rows], gv0 + gv1[0:rows]], 1).astype(bf)
        low_half = jnp.concatenate([gq1, gk1[rows:], gv1[rows:]], 1).astype(bf)
        qkv[h, 0:rows, :] = top
        qkv[h, rows : 2 * rows, :] = low_half
        total = jnp.sum(top.astype(f32), 0, keepdims=True) + jnp.sum(low_half.astype(f32), 0, keepdims=True)
        qv_sum[h] = total
        for half in (other, own):
            product = dot_nt(qkv[h, half, :], wqkv[h])
            if turn == 0:
                nacc[half, :] = product
            else:
                nacc[half, :] += product
            if turn == DEPTH - 1 and half is other:
                x_part(1).wait_send()
                far[0] = nacc[other, :].astype(bf)
                x_part(3).start()
        part = dot(rows_t[...], qkv[h]).astype(bf)
        disassemble(h, part)
        for yy in (1 - y, y):
            rc_copy(Q, h, yy).start()

    for turn in range(DEPTH):
        head_back(near(DEPTH - 1 - turn), turn)
        if turn < 3:
            early_rows(turn + 1)
        if turn > 0:
            for yy in (1 - y, y):
                rc_add(Q, near(DEPTH - turn), yy)
        if turn == 0:
            for k in (I, W):
                ry_add(k, 3)
            v_cross()
        if turn == 1:
            for k in (I, W):
                ry_merge(k, 1)
            out_grads()
            x_part(2).start()
        if turn == 2:
            for k in (I, W):
                ry_merge(k, 2)
            for yy in (1 - y, y):
                for s in (3, 2, 1, 0):
                    rc_add(O, near(s), yy)
            ry_add(Q, 3)
    for yy in (1 - y, y):
        rc_add(Q, z, yy)
    ry_add(Q, 2)
    ry_merge(Q, 2)
    for k in (I, W):
        own_total(k)
    for s in (3, 2, 1):
        ry_add(O, s)
    x_part(2).wait_recv()
    by_rows(mixed_out)
    x_part(3).wait_recv()

    def first_back(at, step):
        here = pl.ds(at, step)
        in_group = pl.ds(pl.multiple_of(t * rows + at, step), step)
        grad = nacc[in_group, :] + inx[0, here, :].astype(f32)
        unit, inverse = norm(tokens[here, :])
        input_grad[here, :] = input_grad[here, :] + norm_grad(grad, unit, inverse, vecs[0:1, :])
        row_sum(0, grad * unit)
        row_sum(1, grad)

    by_rows(first_back)

    for h in range(DEPTH):
        for row in range(2):
            total = jnp.where(t == row, qv_sum[h], 0.0)
            vout[0, 6 + row : 7 + row, h * 256 : h * 256 + 128] = total[:, 0:128]
            vout[0, 6 + row : 7 + row, h * 256 + 128 : h * 256 + 256] = total[:, 256:384]
    for row in range(4):
        for j in range(8):
            late[row * 8 + j : row * 8 + j + 1, :] = vout[0, (0, 1, 6, 7)[row] : (0, 1, 6, 7)[row] + 1, j * LANES : (j + 1) * LANES]
    here = t * 4 + y * 2 + c
    late_in[here] = late[...]
    for turn in range(1, 8):
        late_copy(turn).start()
    ry_add(Q, 1)
    ry_merge(O, 2)
    ry_merge(Q, 1)
    ry_merge(O, 1)
    z_total(V, y, total_of(V), y_landed(V, z))
    for turn in range(1, 8):
        late_wait(late_turn(turn)[1])
    total = late_in[0]
    for index in range(1, 8):
        total = total + late_in[index]
    late_sum[...] = total
    late_in[8 + z] = total
    for step in range(1, DEPTH):
        late_z(step).start()
    own_total(O)
    own_total(Q)
    for step in range(1, DEPTH):
        late_wait(8 + lax.rem(z + step, DEPTH))
    total = ((late_in[8] + late_in[9]) + late_in[10]) + late_in[11]
    for step in range(1, DEPTH):
        zz = lax.rem(z + step, DEPTH)
        remote(vin.at[3 + zz], vin.at[3 + zz], v_send.at[0], v_recv.at[3 + zz], y_peer).wait_recv()
    early = ((vin[3] + vin[4]) + vin[5]) + vin[6]
    vec_grads[...] = early[0 : vec_grads.shape[0]]
    for row in range(4):
        for j in range(8):
            vec_grads[(0, 1, 6, 7)[row] : (0, 1, 6, 7)[row] + 1, j * LANES : (j + 1) * LANES] = total[row * 8 + j : row * 8 + j + 1, :]

    for stage in range(3):
        v_copy(stage).wait_send()
    for turn in range(1, 8):
        late_copy(turn).wait_send()
    for step in range(1, DEPTH):
        vz_copy(step).wait_send()
        late_z(step).wait_send()
    for index, ref in enumerate((rows_one, grad_rows, rows_two, grad_attn)):
        x_rows(ref, index).wait_send()
    for index in (2, 3):
        x_part(index).wait_send()
    x_out_core(c).wait_send()
    x_grad_context().wait_send()
    for k in range(4):
        for zz in range(DEPTH):
            for yy in range(2):
                rc_copy(k, zz, yy).wait_send()
            ry_copy(k, zz).wait_send()
        for s in range(1, DEPTH):
            rz_copy(k, s, y, True).wait_send()
    ry_copy(V, z).wait_send()
    for yy in range(2):
        for s in range(1, DEPTH):
            rz_copy(V, s, yy, True).wait_send()


def run_layer(tokens, cotangent, lengths, order, weights, vec_params):
    bf, f32 = jnp.bfloat16, jnp.float32
    rows = tokens.shape[0]
    group = 2 * rows
    owners = 16
    shapes = piece_shapes()
    view = jnp.transpose(weights, (1, 2, 0))
    vmem = pl.BlockSpec(memory_space=pltpu.VMEM)
    smem = pl.BlockSpec(memory_space=pltpu.SMEM)

    halved = shapes[:3] + ((HALF, D),)

    def many(count, kinds):
        return [pltpu.VMEM((count,) + s, bf) for s in kinds]

    full = pltpu.VMEM((group, D), bf)
    dma = pltpu.SemaphoreType.DMA
    return pl.pallas_call(
        layer_kernel,
        out_shape=[jax.ShapeDtypeStruct((rows, D), f32)] * 2
        + [jax.ShapeDtypeStruct(s, f32) for s in shapes]
        + [jax.ShapeDtypeStruct(vec_params.shape, f32)],
        in_specs=[smem, smem, pl.BlockSpec(memory_space=pl.ANY)] + [vmem] * 3,
        out_specs=[vmem] * 7,
        scratch_shapes=[
            pltpu.VMEM((owners,) + shapes[0], bf),
            pltpu.VMEM((owners // 2, BLOCK, D), bf),
            pltpu.VMEM((owners,) + shapes[2], bf),
            pltpu.VMEM((owners,) + shapes[3], bf),
            pltpu.VMEM((DEPTH, D, 3 * HD), bf),
        ]
        + many(2 * DEPTH, shapes)
        + many(DEPTH, halved)
        + many(1, halved[3:])
        + many(DEPTH, halved)
        + many(2 * DEPTH, halved[3:])
        + [
            full,
            full,
            pltpu.VMEM((D, group), bf),
            full,
            full,
            pltpu.VMEM((DEPTH, group, group), bf),
            pltpu.VMEM((DEPTH, group, 3 * HD), bf),
            pltpu.VMEM((group, DEPTH * HD), bf),
            pltpu.VMEM((group, DEPTH * HD), bf),
            pltpu.VMEM((2, rows, D), bf),
            pltpu.VMEM((2, rows, D), bf),
            pltpu.VMEM((owners // 2, BLOCK, D), bf),
            pltpu.VMEM((rows, DEPTH * HD), bf),
            pltpu.VMEM((group, D), f32),
            pltpu.VMEM((group, D), f32),
            pltpu.VMEM((group, 2 * D), bf),
            pltpu.VMEM((group, 2 * D), bf),
            pltpu.VMEM((DEPTH, 1, 512), f32),
            pltpu.VMEM((DEPTH, 1, 3 * HD), f32),
            pltpu.VMEM((DEPTH, 1, 3 * HD), f32),
            pltpu.VMEM((7, 16, D), f32),
            pltpu.VMEM((5, 16, D), f32),
            pltpu.VMEM((32, LANES), f32),
            pltpu.VMEM((32, LANES), f32),
            pltpu.VMEM((12, 32, LANES), f32),
            dma((5, owners)),
            dma((5, DEPTH)),
            dma((5, 2 * DEPTH)),
            dma((5, 2, 2 * DEPTH)),
            dma((4, 2 * DEPTH)),
            dma((4, 2 * DEPTH)),
            dma((5, DEPTH)),
            dma((5, DEPTH)),
            dma((5, 2 * DEPTH)),
            dma((5, 2 * DEPTH)),
            dma((11,)),
            dma((11,)),
            dma((6,)),
            dma((7,)),
            dma((11,)),
            dma((12,)),
            dma((1,)),
        ],
        compiler_params=pltpu.CompilerParams(
            collective_id=0, has_side_effects=True, vmem_limit_bytes=VMEM_LIMIT
        ),
        name="layer",
    )(lengths, order, view, tokens, cotangent, vec_params)


def per_device(
    grp_count,
    tp_count,
    tokens,
    cotangent,
    lengths,
    order,
    weights,
    momentum,
    stat_left,
    stat_right,
    root_left,
    root_right,
    vec_params,
    vec_momentum,
    vec_second,
):
    fits = grp_count == 4 * DEPTH and tp_count == 2 and tokens.shape[0] == 256
    if not fits or lengths.shape[1] != ARTICLES:
        return per_device_general(
            tokens,
            cotangent,
            lengths,
            order,
            weights,
            momentum,
            stat_left,
            stat_right,
            root_left,
            root_right,
            vec_params,
            vec_momentum,
            vec_second,
        )
    token_total = tokens.shape[0] * tp_count * grp_count
    mixed, input_grad, *sums, vec_grads = run_layer(tokens, cotangent, lengths, order, weights, vec_params)
    blocks, vecs, results = update_blocks(
        sums,
        (weights, momentum, stat_left, stat_right, root_left, root_right),
        vec_grads,
        (vec_params, vec_momentum, vec_second),
        (mixed, input_grad),
        token_total,
    )
    return (*results, *blocks, *vecs)


def solution(mesh):
    placed = (
        P(("grp", "tp"), None),
        P(("grp", "tp"), None),
        P("grp", None),
        P("grp", None),
        P(("tp", "grp"), None, None),
        P(("tp", "grp"), None, None),
        P(("tp", "grp"), None, None),
        P(("tp", "grp"), None, None),
        P(("tp", "grp"), None, None),
        P(("tp", "grp"), None, None),
        P(),
        P(),
        P(),
    )
    return jax.shard_map(
        functools.partial(per_device, mesh.shape["grp"], mesh.shape["tp"]),
        mesh=mesh,
        in_specs=placed,
        out_specs=(
            P(("grp", "tp"), None),
            P(("grp", "tp"), None),
            P(("tp", "grp"), None, None),
            P(("tp", "grp"), None, None),
            P(("tp", "grp"), None, None),
            P(("tp", "grp"), None, None),
            P(("tp", "grp"), None, None),
            P(),
            P(),
            P(),
            P(),
        ),
        check_vma=False,
    )
```

```python
import functools

import jax
import jax.numpy as jnp
from jax import lax
from jax.experimental import pallas as pl
from jax.experimental.pallas import tpu as pltpu
from jax.sharding import PartitionSpec as P

D = 1024
HEADS = 8
HD = 128
FF = 4096
BLOCK = 64


EPS = 1e-05
NEG = -1e30
DECAY = 0.9
BETA = 0.9
RATE = 0.05
VEC_DECAY = 0.9
VEC_RATE = 0.2
VEC_EPS = 1e-08


def norm_rows(value, gain, shift):
    average = jnp.mean(value, -1, keepdims=True)
    centred = value - average
    inverse = lax.rsqrt(jnp.mean(centred * centred, -1, keepdims=True) + EPS)
    normed = centred * inverse
    return (normed * gain + shift, normed, inverse)


def norm_back(grad_out, normed, inverse, gain):
    scaled = grad_out * gain
    return inverse * (
        scaled
        - jnp.mean(scaled, -1, keepdims=True)
        - normed * jnp.mean(scaled * normed, -1, keepdims=True)
    )


def segment_ids(lengths_row, order_row, group_rows):
    article_count = lengths_row.shape[0]
    slots = jnp.arange(article_count, dtype=jnp.int32)
    picks = (order_row[:, None] == slots[None, :]).astype(jnp.int32)
    packed = jnp.sum(picks * lengths_row[None, :], 1)
    ends = jnp.cumsum(packed)
    spots = jnp.arange(group_rows, dtype=jnp.int32)
    return jnp.sum((spots[:, None] >= ends[None, :]).astype(jnp.int32), 1)


def allowed_mask(row_ids, row_segs, segments, key_ids, article_count):
    causal = key_ids[None, :] <= row_ids[:, None]
    same = segments[None, :] == row_segs[:, None]
    alone = (row_segs[:, None] < article_count) | (key_ids[None, :] == row_ids[:, None])
    return causal & same & alone


def from_columns(tiles, row_total, col_total):
    return (
        tiles.reshape(col_total // BLOCK, row_total // BLOCK, BLOCK, BLOCK)
        .transpose(1, 2, 0, 3)
        .reshape(row_total, col_total)
    )


def from_rows(tiles, row_total, col_total):
    return (
        tiles.reshape(row_total // BLOCK, col_total // BLOCK, BLOCK, BLOCK)
        .transpose(0, 2, 1, 3)
        .reshape(row_total, col_total)
    )


def to_columns(matrix):
    row_total, col_total = matrix.shape
    return (
        matrix.reshape(row_total // BLOCK, BLOCK, col_total // BLOCK, BLOCK)
        .transpose(2, 0, 1, 3)
        .reshape(-1, BLOCK, BLOCK)
    )


def to_rows(matrix):
    row_total, col_total = matrix.shape
    return (
        matrix.reshape(row_total // BLOCK, BLOCK, col_total // BLOCK, BLOCK)
        .transpose(0, 2, 1, 3)
        .reshape(-1, BLOCK, BLOCK)
    )


def per_device_general(
    tokens,
    cotangent,
    lengths,
    order,
    weights,
    momentum,
    stat_left,
    stat_right,
    root_left,
    root_right,
    vec_params,
    vec_momentum,
    vec_second,
):
    groups = lax.axis_size("grp")
    tp_size = lax.axis_size("tp")
    tp_rank = lax.axis_index("tp")
    tok_rows = tokens.shape[0]
    group_rows = tok_rows * tp_size
    article_count = lengths.shape[1]
    owners = groups * tp_size
    block_area = BLOCK * BLOCK * owners
    qkv_count = 3 * D * D // block_area
    out_count = D * D // block_area
    in_count = D * FF // block_area
    owned_blocks = weights.shape[0]
    heads_here = HEADS // tp_size
    qkv_cols = 3 * D // tp_size
    feat_here = D // tp_size
    ff_here = FF // tp_size
    qv_width = 2 * D // tp_size
    token_total = group_rows * groups
    gathered = lax.all_gather(weights.astype(jnp.bfloat16), "grp", axis=0, tiled=True)
    per_owner = gathered.reshape(groups, owned_blocks, BLOCK, BLOCK)
    marks = [0, qkv_count, qkv_count + out_count, qkv_count + out_count + in_count, owned_blocks]
    pieces = [
        per_owner[:, marks[index] : marks[index + 1]].reshape(-1, BLOCK, BLOCK)
        for index in range(4)
    ]
    w_qkv = from_columns(pieces[0], D, qkv_cols)
    w_out = from_rows(pieces[1], feat_here, D)
    w_in = from_columns(pieces[2], D, ff_here)
    w_down = from_rows(pieces[3], ff_here, D)
    w_qkv_heads = w_qkv.reshape(D, heads_here, 3, HD)
    w_out_heads = w_out.reshape(heads_here, HD, D)
    segments = segment_ids(lengths[0], order[0], group_rows)
    gain_one = vec_params[0]
    shift_one = vec_params[1]
    gain_two = vec_params[2]
    shift_two = vec_params[3]
    bias_out = vec_params[4]
    bias_down = vec_params[5]
    qv_here = lax.dynamic_slice_in_dim(
        vec_params[6:8].reshape(2 * D), tp_rank * qv_width, qv_width
    ).reshape(heads_here, 2, HD)
    bias_heads = jnp.stack(
        [qv_here[:, 0], jnp.zeros((heads_here, HD), jnp.float32), qv_here[:, 1]], 0
    )[:, :, None, :]
    bias_in = lax.dynamic_slice_in_dim(vec_params[8:].reshape(FF), tp_rank * ff_here, ff_here)
    normed_one, unit_one, inverse_one = norm_rows(tokens, gain_one, shift_one)
    rows_one = lax.all_gather(normed_one.astype(jnp.bfloat16), "tp", axis=0, tiled=True)
    projected = (
        jnp.einsum("rx,xhcd->chrd", rows_one, w_qkv_heads, preferred_element_type=jnp.float32)
        + bias_heads
    ).astype(jnp.bfloat16)
    queries = projected[0]
    keys_all = projected[1]
    values_all = projected[2]
    span = min(512, group_rows)
    starts = jnp.arange(group_rows // span, dtype=jnp.int32) * span
    key_ids = jnp.arange(group_rows, dtype=jnp.int32)
    score_scale = HD ** (-0.5)

    def masked_scores(first_row):
        row_ids = first_row + jnp.arange(span, dtype=jnp.int32)
        row_segs = lax.dynamic_slice_in_dim(segments, first_row, span, 0)
        allowed = allowed_mask(row_ids, row_segs, segments, key_ids, article_count)
        query_rows = lax.dynamic_slice_in_dim(queries, first_row, span, 1)
        scores = (
            jnp.einsum("hqd,hkd->hqk", query_rows, keys_all, preferred_element_type=jnp.float32)
            * score_scale
        )
        return (jnp.where(allowed[None], scores, NEG), query_rows)

    def attend(context_buf, first_row):
        scores, query_rows = masked_scores(first_row)
        row_max = jnp.max(scores, -1, keepdims=True)
        expo = jnp.exp(scores - row_max)
        expsum = jnp.sum(expo, -1, keepdims=True)
        probs_low = (expo / expsum).astype(jnp.bfloat16)
        context = jnp.einsum(
            "hqk,hkd->hqd", probs_low, values_all, preferred_element_type=jnp.float32
        ).astype(jnp.bfloat16)
        context_buf = lax.dynamic_update_slice_in_dim(context_buf, context, first_row, 1)
        return (context_buf, (row_max + jnp.log(expsum))[:, :, 0])

    context_low, log_norm = lax.scan(
        attend, jnp.zeros((heads_here, group_rows, HD), jnp.bfloat16), starts
    )
    attn_sum = lax.psum_scatter(
        jnp.einsum(
            "hrd,hde->re", context_low, w_out_heads, preferred_element_type=jnp.float32
        ).astype(jnp.bfloat16),
        "tp",
        scatter_dimension=0,
        tiled=True,
    ).astype(jnp.float32)
    hidden = tokens + attn_sum + bias_out
    normed_two, unit_two, inverse_two = norm_rows(hidden, gain_two, shift_two)
    rows_two = lax.all_gather(normed_two.astype(jnp.bfloat16), "tp", axis=0, tiled=True)
    inner = jnp.dot(rows_two, w_in, preferred_element_type=jnp.float32) + bias_in
    activ, gelu_pull = jax.vjp(jax.nn.gelu, inner)
    activ_low = activ.astype(jnp.bfloat16)
    mixed = (
        hidden
        + lax.psum_scatter(
            jnp.dot(activ_low, w_down, preferred_element_type=jnp.float32).astype(jnp.bfloat16),
            "tp",
            scatter_dimension=0,
            tiled=True,
        ).astype(jnp.float32)
        + bias_down
    )
    grad_low = cotangent.astype(jnp.bfloat16)
    grad_rows = lax.all_gather(grad_low, "tp", axis=0, tiled=True)
    g_down = jnp.einsum("rf,rd->fd", activ_low, grad_rows, preferred_element_type=jnp.float32)
    grad_activ = jnp.einsum("rd,fd->rf", grad_rows, w_down, preferred_element_type=jnp.float32)
    grad_inner = gelu_pull(grad_activ)[0].astype(jnp.bfloat16)
    g_in = jnp.einsum("rd,rf->df", rows_two, grad_inner, preferred_element_type=jnp.float32)
    g_bias_in = jnp.sum(grad_inner.astype(jnp.float32), 0)
    ffn_blocks = jnp.concatenate(
        [
            to_columns(g_in).reshape(groups, in_count, BLOCK, BLOCK),
            to_rows(g_down).reshape(groups, in_count, BLOCK, BLOCK),
        ],
        1,
    )
    grad_normed_two = lax.psum_scatter(
        jnp.einsum("rf,df->rd", grad_inner, w_in, preferred_element_type=jnp.float32).astype(
            jnp.bfloat16
        ),
        "tp",
        scatter_dimension=0,
        tiled=True,
    ).astype(jnp.float32)
    grad_hidden = cotangent + norm_back(grad_normed_two, unit_two, inverse_two, gain_two)
    grad_attn_low = grad_hidden.astype(jnp.bfloat16)
    grad_attn_rows = lax.all_gather(grad_attn_low, "tp", axis=0, tiled=True)
    g_out = jnp.einsum(
        "hrd,re->hde", context_low, grad_attn_rows, preferred_element_type=jnp.float32
    ).reshape(feat_here, D)
    grad_context = jnp.einsum(
        "re,hde->hrd", grad_attn_rows, w_out_heads, preferred_element_type=jnp.float32
    ).astype(jnp.bfloat16)
    zero_heads = jnp.zeros((heads_here, group_rows, HD), jnp.float32)

    def attend_back(carry, inputs):
        grad_queries, grad_keys, grad_values = carry
        first_row, log_block = inputs
        scores, query_rows = masked_scores(first_row)
        probs = jnp.exp(scores - log_block[:, :, None])
        grad_ctx_rows = lax.dynamic_slice_in_dim(grad_context, first_row, span, 1)
        grad_probs = jnp.einsum(
            "hqd,hkd->hqk", grad_ctx_rows, values_all, preferred_element_type=jnp.float32
        )
        delta = jnp.sum(probs * grad_probs, -1, keepdims=True)
        grad_scores = (probs * (grad_probs - delta)).astype(jnp.bfloat16)
        query_part = (
            jnp.einsum("hqk,hkd->hqd", grad_scores, keys_all, preferred_element_type=jnp.float32)
            * score_scale
        )
        grad_queries = lax.dynamic_update_slice_in_dim(grad_queries, query_part, first_row, 1)
        grad_keys = (
            grad_keys
            + jnp.einsum(
                "hqk,hqd->hkd", grad_scores, query_rows, preferred_element_type=jnp.float32
            )
            * score_scale
        )
        grad_values = grad_values + jnp.einsum(
            "hqk,hqd->hkd",
            probs.astype(jnp.bfloat16),
            grad_ctx_rows,
            preferred_element_type=jnp.float32,
        )
        return ((grad_queries, grad_keys, grad_values), None)

    (grad_queries, grad_keys, grad_values), unused = lax.scan(
        attend_back, (zero_heads, zero_heads, zero_heads), (starts, log_norm)
    )
    grad_proj = jnp.stack([grad_queries, grad_keys, grad_values], 0).astype(jnp.bfloat16)
    proj_sums = jnp.sum(grad_proj.astype(jnp.float32), 2)
    g_bias_qv = jnp.stack([proj_sums[0], proj_sums[2]], 1).reshape(qv_width)
    g_qkv = jnp.einsum(
        "rx,chrd->xhcd", rows_one, grad_proj, preferred_element_type=jnp.float32
    ).reshape(D, qkv_cols)
    grad_normed_one = lax.psum_scatter(
        jnp.einsum(
            "chrd,xhcd->rx", grad_proj, w_qkv_heads, preferred_element_type=jnp.float32
        ).astype(jnp.bfloat16),
        "tp",
        scatter_dimension=0,
        tiled=True,
    ).astype(jnp.float32)
    input_grad = grad_hidden + norm_back(grad_normed_one, unit_one, inverse_one, gain_one)
    local_rows = jnp.stack(
        [
            jnp.sum(grad_normed_one * unit_one, 0),
            jnp.sum(grad_normed_one, 0),
            jnp.sum(grad_normed_two * unit_two, 0),
            jnp.sum(grad_normed_two, 0),
            jnp.sum(grad_hidden, 0),
            jnp.sum(cotangent, 0),
        ]
    )
    qv_rows = lax.dynamic_update_slice(
        jnp.zeros((2 * D,), jnp.float32), g_bias_qv, (tp_rank * qv_width,)
    ).reshape(2, D)
    in_rows = lax.dynamic_update_slice(
        jnp.zeros((FF,), jnp.float32), g_bias_in, (tp_rank * ff_here,)
    ).reshape(FF // D, D)
    vec_grads = lax.psum(jnp.concatenate([local_rows, qv_rows, in_rows], 0), ("grp", "tp"))
    attn_blocks = jnp.concatenate(
        [
            to_columns(g_qkv).reshape(groups, qkv_count, BLOCK, BLOCK),
            to_rows(g_out).reshape(groups, out_count, BLOCK, BLOCK),
        ],
        1,
    )
    every_block = jnp.concatenate([attn_blocks, ffn_blocks], 1).reshape(-1, BLOCK, BLOCK)
    weight_grads = lax.psum_scatter(
        every_block.astype(jnp.bfloat16), "grp", scatter_dimension=0, tiled=True
    ).astype(jnp.float32)
    scaled = weight_grads * token_total ** (-0.5)
    stat_left_new = DECAY * stat_left + (1.0 - DECAY) * jnp.einsum(
        "nij,nkj->nik", scaled, scaled, precision=lax.Precision.HIGHEST
    )
    stat_right_new = DECAY * stat_right + (1.0 - DECAY) * jnp.einsum(
        "nji,njk->nik", scaled, scaled, precision=lax.Precision.HIGHEST
    )
    shaped = jnp.einsum("nij,njk->nik", root_left, scaled, precision=lax.Precision.HIGHEST)
    shaped = jnp.einsum("nij,njk->nik", shaped, root_right, precision=lax.Precision.HIGHEST)
    momentum_new = BETA * momentum + shaped
    weights_new = weights - RATE * momentum_new
    vec_scaled = vec_grads * token_total ** (-0.5)
    vec_second_new = VEC_DECAY * vec_second + (1.0 - VEC_DECAY) * vec_scaled * vec_scaled
    vec_momentum_new = BETA * vec_momentum + vec_scaled * lax.rsqrt(vec_second_new + VEC_EPS)
    vec_new = vec_params - VEC_RATE * vec_momentum_new
    return (
        mixed,
        input_grad,
        weight_grads,
        stat_left_new,
        stat_right_new,
        momentum_new,
        weights_new,
        vec_grads,
        vec_second_new,
        vec_momentum_new,
        vec_new,
    )


MESH_ID = pl.DeviceIdType.MESH
LANES = 128
HALF = 64
VMEM_LIMIT = 62 * 2**20
ARTICLES = 4
GELU_A = (2.0 / 3.141592653589793) ** 0.5
GELU_B = 0.044715


def remote(src, dst, send_sem, recv_sem, device):
    return pltpu.make_async_remote_copy(
        src_ref=src,
        dst_ref=dst,
        send_sem=send_sem,
        recv_sem=recv_sem,
        device_id=device,
        device_id_type=MESH_ID,
    )


def place():
    grp = lax.axis_index("grp")
    return lax.div(grp, 4), lax.rem(lax.div(grp, 2), 2), lax.rem(grp, 2), lax.axis_index("tp")


def slot_of(z, y, c):
    return z * 4 + y * 2 + c


def lay_blocks(view_ref, stack):
    half = view_ref.shape[2] // 2

    def row(i, carry):
        tile = view_ref[i].T
        stack[pl.ds(i, half, stride=BLOCK), :] = jnp.concatenate([tile[:half], tile[half:]], 1)
        return carry

    lax.fori_loop(0, BLOCK, row, 0, unroll=8)


def piece_shapes():
    return ((768, LANES), (64, 512), (1024, LANES), (LANES, 1024))


def both_halves(pair):
    low = lax.broadcasted_iota(jnp.int32, pair.shape, 1) < HALF
    turned = pltpu.roll(pair, HALF, 1)
    return jnp.where(low, pair, turned), jnp.where(low, turned, pair)


def update_kernel(
    scale,
    sum_q,
    sum_o,
    sum_i,
    sum_d,
    root_l,
    root_r,
    vec_g,
    vecs,
    vec_m,
    vec_s,
    mixed,
    input_grad,
    w,
    m,
    sl,
    sr,
    out_g,
    out_sl,
    out_sr,
    out_m,
    out_w,
    out_vg,
    out_vs,
    out_vm,
    out_v,
    out_mixed,
    out_input_grad,
    grads,
    first,
    second,
):
    count = w.shape[2]
    bf, f32 = jnp.bfloat16, jnp.float32
    out_mixed[...] = mixed[...]
    out_input_grad[...] = input_grad[...]

    @pl.when(pl.program_id(0) == 0)
    def _():
        total = vec_g[...]
        out_vg[...] = total
        scaled = total * scale
        fresh = VEC_DECAY * vec_s[...] + (1.0 - VEC_DECAY) * scaled * scaled
        out_vs[...] = fresh
        momentum = BETA * vec_m[...] + scaled * lax.rsqrt(fresh + VEC_EPS)
        out_vm[...] = momentum
        out_v[...] = vecs[...] - VEC_RATE * momentum
        rows = sum_q.shape[0]
        grads[0:rows, 0:HALF] = sum_q[:, 0:HALF]
        grads[rows : 2 * rows, 0:HALF] = sum_q[:, HALF:LANES]
        base = 2 * rows
        for b in range(8):
            grads[base + b * 64 : base + b * 64 + 64, 0:HALF] = sum_o[:, b * HALF : (b + 1) * HALF]
        base += 512
        grads[base : base + D, 0:HALF] = sum_i[:, 0:HALF]
        grads[0:D, HALF:LANES] = sum_i[:, HALF:LANES]
        for r in range(2):
            for b in range(16):
                at = D + (r * 16 + b) * 64
                grads[at : at + 64, HALF:LANES] = sum_d[r * 64 : r * 64 + 64, b * HALF : (b + 1) * HALF]

        row_id = lax.broadcasted_iota(jnp.int32, (256, 256), 0)
        col_id = lax.broadcasted_iota(jnp.int32, (256, 256), 1)
        mask = lax.shift_right_logical(row_id, 6) == lax.shift_right_logical(col_id, 6)
        low = lax.broadcasted_iota(jnp.int32, (256, LANES), 1) < HALF

        def spread(v):
            return jnp.where(mask, jnp.concatenate([v, v], 1), 0.0).astype(bf)

        def eight(k, carry):
            at = pl.ds(pl.multiple_of(k * 256, 256), 256)
            fours = zip(both_halves(grads[at, :]), both_halves(root_l[at, :]), both_halves(root_r[at, :]))
            for side, (grad, left, right) in enumerate(fours):
                to = pl.ds(pl.multiple_of(k * 256 + side * (count // 2 * BLOCK), 256), 256)
                s32 = grad * scale
                s = s32.astype(bf)
                outer = lax.dot_general(s[:, 0:HALF], s[:, 0:HALF], (((1,), (1,)), ((), ())), preferred_element_type=f32)
                kept = jnp.where(mask, outer, 0.0)
                kept = kept[:, :LANES] + kept[:, LANES:]
                outer = kept + pltpu.roll(kept, HALF, 1)
                inner = lax.dot_general(spread(s32), s, (((0,), (0,)), ((), ())), preferred_element_type=f32)
                shaped = jnp.dot(spread(left), s, preferred_element_type=f32)
                shaped = jnp.dot(spread(shaped), right.astype(bf), preferred_element_type=f32)
                first[to, :] = jnp.where(low, grad, outer)
                second[to, :] = jnp.where(low, inner, shaped)
            return carry

        lax.fori_loop(0, count // 8, eight, 0, unroll=2)

    i0 = pl.program_id(0) * w.shape[0]

    def rows_out(ii, carry):
        at = pl.ds(i0 + ii, count, stride=BLOCK)
        one = first[at, :].T
        two = second[at, :].T
        out_g[ii] = one[0:HALF]
        out_sl[ii] = DECAY * sl[ii] + (1.0 - DECAY) * one[HALF:LANES]
        out_sr[ii] = DECAY * sr[ii] + (1.0 - DECAY) * two[0:HALF]
        fresh = BETA * m[ii] + two[HALF:LANES]
        out_m[ii] = fresh
        out_w[ii] = w[ii] - RATE * fresh
        return carry

    lax.fori_loop(0, w.shape[0], rows_out, 0, unroll=True)


def update_blocks(sums, roots, blocks, vec_grads, vecs, results, token_total):
    views = [jnp.transpose(a, (1, 2, 0)) for a in blocks]
    count = blocks[0].shape[0]
    rows = 8
    whole = pl.BlockSpec(memory_space=pltpu.VMEM)
    steps = BLOCK // rows
    some = pl.BlockSpec((results[0].shape[0] // steps, results[0].shape[1]), lambda i: (i, 0))
    part = pl.BlockSpec((rows, BLOCK, count), lambda i: (i, 0, 0))
    vec = jax.ShapeDtypeStruct(vec_grads.shape, jnp.float32)
    outs = pl.pallas_call(
        functools.partial(update_kernel, token_total ** (-0.5)),
        grid=(steps,),
        out_shape=[jax.ShapeDtypeStruct((BLOCK, BLOCK, count), jnp.float32)] * 5
        + [vec] * 4
        + [jax.ShapeDtypeStruct(a.shape, a.dtype) for a in results],
        in_specs=[whole] * 10 + [some] * 2 + [part] * 4,
        out_specs=[part] * 5 + [whole] * 4 + [some] * 2,
        scratch_shapes=[
            pltpu.VMEM((count // 2 * BLOCK, LANES), jnp.float32),
            pltpu.VMEM((count * BLOCK, LANES), jnp.float32),
            pltpu.VMEM((count * BLOCK, LANES), jnp.float32),
        ],
        compiler_params=pltpu.CompilerParams(vmem_limit_bytes=VMEM_LIMIT),
        name="update_blocks",
    )(*sums, *roots, vec_grads, *vecs, *results, *views)
    return [jnp.transpose(a, (2, 0, 1)) for a in outs[:5]], outs[5:9], outs[9:]


DEPTH = 4


def layer_kernel(
    lengths,
    order,
    view,
    root_l,
    root_r,
    tokens,
    cot,
    vecs,
    mixed,
    input_grad,
    sum_q,
    sum_o,
    sum_i,
    sum_d,
    vec_grads,
    stack_l,
    stack_r,
    gq,
    go,
    gi,
    gd,
    wqkv,
    cq,
    co,
    ci,
    cd,
    yq,
    yo,
    yi,
    yd,
    yv,
    zq,
    zo,
    zi,
    zd,
    zv,
    rows_one,
    rows_two,
    rows_t,
    grad_rows,
    grad_attn,
    probs,
    qkv,
    ctx,
    gctx,
    far,
    inx,
    go_x,
    ctx_x,
    macc,
    nacc,
    act,
    gin,
    bias_sum,
    qkv_bias,
    qv_sum,
    vin,
    vout,
    late,
    late_sum,
    late_in,
    recv,
    send_y,
    send_c,
    send_z,
    rc_recv,
    rc_send,
    ry_recv,
    ry_send,
    rz_recv,
    rz_send,
    x_send,
    x_recv,
    v_send,
    v_recv,
    l_send,
    l_recv,
    copy_sem,
):
    bf, f32 = jnp.bfloat16, jnp.float32
    z, y, c, t = place()
    me = slot_of(z, y, c)
    x_peer = (me, 1 - t)
    y_peer = (slot_of(z, 1 - y, c), t)
    c_peer = (slot_of(z, y, 1 - c), t)
    rows = tokens.shape[0]
    own = pl.ds(pl.multiple_of(t * rows, rows), rows)
    other = pl.ds(pl.multiple_of((1 - t) * rows, rows), rows)

    def lanes(start, size, unit):
        return pl.ds(pl.multiple_of(start, unit), size)

    gathered, core_in = (gq, go, gi, gd), (cq, co, ci, cd)
    y_in, z_in = (yq, yo, yi, yd, yv), (zq, zo, zi, zd, zv)
    sums = (sum_q, sum_o, sum_i, sum_d)
    Q, O, I, W, V = range(5)

    def dot(a, b):
        return jnp.dot(a, b, preferred_element_type=f32)

    def dot_nt(a, b):
        return lax.dot_general(a, b, (((1,), (1,)), ((), ())), preferred_element_type=f32)

    def dot_tn(a, b):
        return lax.dot_general(a, b, (((0,), (0,)), ((), ())), preferred_element_type=f32)

    def piece(k, zz, yy, cc):
        if k == O:
            return go.at[zz * 2 + yy, :, pl.ds(pl.multiple_of(cc * 512, 512), 512)]
        return gathered[k].at[slot_of(zz, yy, cc)]

    def near(s):
        return lax.rem(z + (1 - 2 * lax.div(z, 2)) * s + DEPTH, DEPTH)

    def ag_piece(k, zz, yy, cc):
        if k == W:
            return gd.at[slot_of(zz, yy, cc), 0:HALF]
        if k == V:
            return gd.at[slot_of(zz, yy, cc), HALF:LANES]
        return piece(k, zz, yy, cc)

    def ag_copy(k, zz, yy, way):
        src = ag_piece(k, zz, yy, c)
        sem = recv.at[k, slot_of(zz, yy, c)]
        if way == "up":
            return remote(src, src, send_z.at[k, 0, yy * DEPTH + zz], sem, (slot_of(z + 1, y, c), t))
        if way == "down":
            return remote(src, src, send_z.at[k, 1, yy * DEPTH + zz], sem, (slot_of(z - 1, y, c), t))
        if way == "y":
            return remote(src, src, send_y.at[k, zz], sem, y_peer)
        return remote(src, src, send_c.at[k, yy * DEPTH + zz], sem, c_peer)

    def ag_wait(k, zz, yy, cc):
        ref = ag_piece(k, zz, yy, cc)
        remote(ref, ref, send_y.at[k, 0], recv.at[k, slot_of(zz, yy, cc)], y_peer).wait_recv()

    def own_sends_z(k):
        @pl.when(z < DEPTH - 1)
        def _():
            ag_copy(k, z, y, "up").start()

        @pl.when(z > 0)
        def _():
            ag_copy(k, z, y, "down").start()

        ag_copy(k, z, y, "core").start()

    def own_sends_y(k):
        ag_copy(k, z, y, "y").start()

    def z_arrival(kinds, dist):
        @pl.when(z >= dist)
        def _():
            for k in kinds:
                ag_wait(k, z - dist, y, c)

                @pl.when(z < DEPTH - 1)
                def _():
                    ag_copy(k, z - dist, y, "up").start()

                ag_copy(k, z - dist, y, "y").start()
                ag_copy(k, z - dist, y, "core").start()

        @pl.when(z + dist < DEPTH)
        def _():
            for k in kinds:
                ag_wait(k, z + dist, y, c)

                @pl.when(z > 0)
                def _():
                    ag_copy(k, z + dist, y, "down").start()

                ag_copy(k, z + dist, y, "y").start()
                ag_copy(k, z + dist, y, "core").start()

    def y_arrival(kinds, dist):
        def one(zz):
            for k in kinds:
                ag_wait(k, zz, 1 - y, c)
                ag_copy(k, zz, 1 - y, "core").start()

        if dist == 0:
            one(z)
            return

        @pl.when(z >= dist)
        def _():
            one(z - dist)

        @pl.when(z + dist < DEPTH)
        def _():
            one(z + dist)

    def v_forward(zz, yy):
        ag_wait(V, zz, yy, c)

        @pl.when((zz <= z) & (z < DEPTH - 1))
        def _():
            ag_copy(V, zz, yy, "up").start()

        @pl.when((zz >= z) & (z > 0))
        def _():
            ag_copy(V, zz, yy, "down").start()

        ag_copy(V, zz, yy, "core").start()

    def v_arrival(dist):
        for yy in (y, 1 - y):

            @pl.when(z >= dist)
            def _():
                v_forward(z - dist, yy)

            @pl.when(z + dist < DEPTH)
            def _():
                v_forward(z + dist, yy)

    def drain(k, zz, yy):
        ag_copy(k, zz, yy, "core").wait_send()
        if k == V:

            @pl.when((yy == y) & (zz == z))
            def _():
                ag_copy(k, zz, yy, "y").wait_send()

            @pl.when((zz <= z) & (z < DEPTH - 1))
            def _():
                ag_copy(k, zz, yy, "up").wait_send()

            @pl.when((zz >= z) & (z > 0))
            def _():
                ag_copy(k, zz, yy, "down").wait_send()

            return

        @pl.when(yy == y)
        def _():
            ag_copy(k, zz, y, "y").wait_send()

            @pl.when((zz <= z) & (z < DEPTH - 1))
            def _():
                ag_copy(k, zz, y, "up").wait_send()

            @pl.when((zz >= z) & (z > 0))
            def _():
                ag_copy(k, zz, y, "down").wait_send()

    def add(dst, *terms):
        count, width = dst.shape
        step = min(count, 256 * LANES // width)

        def body(i, carry):
            at = pl.ds(pl.multiple_of(i * step, 16), step)
            total = terms[0][at, :].astype(f32)
            for term in terms[1:]:
                total = total + term[at, :].astype(f32)
            dst[at, :] = total.astype(dst.dtype)
            return carry

        lax.fori_loop(0, count // step, body, 0)

    side = lax.div(z, 2)
    end_z, inner_z = 3 * side, 1 + side
    is_end = z == end_z

    def rc_copy(k, zz, yy):
        at = zz * 2 + yy
        return remote(piece(k, zz, yy, 1 - c), core_in[k].at[at], rc_send.at[k, at], rc_recv.at[k, at], c_peer)

    def ry_copy(k, zz):
        if k == V:
            return remote(ag_piece(V, z, 1 - y, c), y_in[V].at[0], ry_send.at[V, 0], ry_recv.at[V, 0], y_peer)
        return remote(ag_piece(k, zz, 1 - y, c), y_in[k].at[zz], ry_send.at[k, zz], ry_recv.at[k, zz], y_peer)

    def z_slot(k, slot, yy):
        return z_in[k].at[slot * 2 + yy if k == V else slot]

    def z_sem(slot, yy):
        return slot * 2 + yy

    def rz_copy(k, s, yy, from_end):
        slot = s - 1 if from_end else {3: 0, 2: 1, 1: 3}[s]
        to = inner_z if from_end else {3: end_z, 2: 3 - end_z, 1: 3 - inner_z}[s]
        sent, landed = rz_send.at[k, (s - 1) * 2 + yy], rz_recv.at[k, z_sem(slot, yy)]
        return remote(ag_piece(k, near(s), yy, c), z_slot(k, slot, yy), sent, landed, (slot_of(to, y, c), t))

    def z_landed(k, slot, yy):
        ref = z_slot(k, slot, yy)
        remote(ref, ref, rz_send.at[k, 0], rz_recv.at[k, z_sem(slot, yy)], y_peer).wait_recv()
        return ref

    def y_landed(k, zz):
        ref = y_in[k].at[0 if k == V else zz]
        remote(ref, ref, ry_send.at[k, 0], ry_recv.at[k, 0 if k == V else zz], y_peer).wait_recv()
        return ref

    def rc_add(k, zz, yy):
        at = zz * 2 + yy
        remote(core_in[k].at[at], core_in[k].at[at], rc_send.at[k, 0], rc_recv.at[k, at], c_peer).wait_recv()
        mine = piece(k, zz, yy, c)
        add(mine, mine, core_in[k].at[at])

        @pl.when(yy != y)
        def _():
            ry_copy(k, zz).start()

    def z_step(k, s, yy, *terms):
        mine = ag_piece(k, near(s), yy, c)
        if terms:
            add(mine, mine, *terms)

        @pl.when(is_end)
        def _():
            rz_copy(k, s, yy, True).start()

        if s == 3:

            @pl.when(jnp.logical_not(is_end))
            def _():
                rz_copy(k, s, yy, False).start()

    def z_merge(k, s, yy):
        @pl.when(jnp.logical_not(is_end))
        def _():
            mine = ag_piece(k, near(s), yy, c)
            add(mine, mine, z_landed(k, s, yy))
            rz_copy(k, s, yy, False).start()

    def ry_add(k, s):
        z_step(k, s, y, y_landed(k, near(s)))

    def ry_merge(k, s):
        z_merge(k, s, y)

    def total_of(k):
        return sum_d.at[(k - W) * HALF : (k - W + 1) * HALF] if k >= W else sums[k]

    def z_total(k, yy, dst, *terms):
        mine = ag_piece(k, z, yy, c)
        first = z_landed(k, 0, yy)

        @pl.when(is_end)
        def _():
            add(dst, mine, first, z_landed(k, 1, yy), *terms)

        @pl.when(jnp.logical_not(is_end))
        def _():
            add(dst, mine, first, z_landed(k, 3, yy), *terms)

    def own_total(k):
        z_total(k, y, total_of(k), y_landed(k, z))

    def v_cross():
        mine = ag_piece(V, z, 1 - y, c)
        z_total(V, 1 - y, mine)
        ry_copy(V, z).start()

    def x_rows(ref, index):
        return remote(ref.at[own], ref.at[own], x_send.at[index], x_recv.at[index], x_peer)

    def x_rows_wait(ref, index):
        remote(ref.at[other], ref.at[other], x_send.at[index], x_recv.at[index], x_peer).wait_recv()

    def x_part(index):
        slot = 1 if index == 2 else 0
        return remote(far.at[slot], inx.at[slot], x_send.at[5 + index], x_recv.at[5 + index], x_peer)

    def by_rows(body, step=64):
        def run(i, carry):
            body(pl.multiple_of(i * step, step), step)
            return carry

        lax.fori_loop(0, rows // step, run, 0)

    def norm(value):
        average = jnp.mean(value, -1, keepdims=True)
        centred = value - average
        inverse = lax.rsqrt(jnp.mean(centred * centred, -1, keepdims=True) + EPS)
        return centred * inverse, inverse

    def norm_grad(grad, unit, inverse, gain):
        scaled = grad * gain
        return inverse * (
            scaled - jnp.mean(scaled, -1, keepdims=True) - unit * jnp.mean(scaled * unit, -1, keepdims=True)
        )

    def x_out():
        half = (slice(None), slice(None), lanes(c * 512, 512, 512))
        return remote(go.at[half], go_x.at[half], x_send.at[4], x_recv.at[4], x_peer)

    def x_out_core(cc):
        half = (slice(None), slice(None), lanes(cc * 512, 512, 512))
        return remote(go_x.at[half], go_x.at[half], x_send.at[9], x_recv.at[9], c_peer)

    def x_grad_context():
        return remote(ctx_x, gctx.at[own], x_send.at[10], x_recv.at[10], x_peer)

    def x_grad_context_wait():
        remote(gctx.at[other], gctx.at[other], x_send.at[10], x_recv.at[10], x_peer).wait_recv()

    stages = (x_peer, c_peer, y_peer)

    def v_copy(stage):
        return remote(vout.at[1 + stage], vin.at[stage], v_send.at[stage], v_recv.at[stage], stages[stage])

    def vz_copy(step):
        peer = (slot_of(lax.rem(z + step, DEPTH), y, c), t)
        return remote(vout.at[4], vin.at[3 + z], v_send.at[2 + step], v_recv.at[3 + z], peer)

    def early_rows(hop):
        if hop == 0:
            vout[1] = vout[0]
        else:
            v_copy(hop - 1).wait_recv()
            vout[1 + hop] = vout[hop] + vin[hop - 1]
        if hop < 3:
            v_copy(hop).start()
        else:
            for step in range(1, DEPTH):
                vz_copy(step).start()
            vin[3 + z] = vout[4]

    def late_turn(turn):
        dx, dy, dc = turn // 4, turn // 2 % 2, turn % 2
        xx, yy, cc = (1 - t if dx else t), (1 - y if dy else y), (1 - c if dc else c)
        return (slot_of(z, yy, cc), xx), xx * 4 + yy * 2 + cc

    def late_copy(turn):
        here = t * 4 + y * 2 + c
        return remote(late, late_in.at[here], l_send.at[turn], l_recv.at[here], late_turn(turn)[0])

    def late_wait(index):
        remote(late_in.at[index], late_in.at[index], l_send.at[0], l_recv.at[index], y_peer).wait_recv()

    def late_z(step):
        peer = (slot_of(lax.rem(z + step, DEPTH), y, c), t)
        return remote(late_sum, late_in.at[8 + z], l_send.at[7 + step], l_recv.at[8 + z], peer)

    barrier = pltpu.get_barrier_semaphore()
    z_peers = [(slot_of(lax.rem(z + step, DEPTH), y, c), t) for step in range(1, DEPTH)]
    everyone = [late_turn(turn)[0] for turn in range(1, 8)] + z_peers
    for device in everyone:
        pl.semaphore_signal(barrier, inc=1, device_id=device, device_id_type=MESH_ID)

    def prepare(held, stack):
        load = pltpu.make_async_copy(view, held, copy_sem.at[0])
        load.start()

        def first_norm(at, step):
            unit, inverse = norm(tokens[pl.ds(at, step), :])
            to = pl.ds(pl.multiple_of(t * rows + at, step), step)
            rows_one[to, :] = (unit * vecs[0:1, :] + vecs[1:2, :]).astype(bf)
            grad_rows[to, :] = cot[pl.ds(at, step), :].astype(bf)

        load.wait()
        lay_blocks(held, stack)

        def pair(left, right, count, left_high=False, right_high=False):
            first, second = stack[left : left + count, :], stack[right : right + count, :]
            first = pltpu.roll(first, HALF, 1) if left_high else first
            second = second if right_high else pltpu.roll(second, HALF, 1)
            lane = lax.broadcasted_iota(jnp.int32, (count, LANES), 1)
            return jnp.where(lane < HALF, first, second).astype(bf)

        n = gq.shape[1]
        gq[me] = pair(0, n, n)
        base = 2 * n
        wide = [pair(base + b * 64, base + b * 64 + 64, 64) for b in range(0, 8, 2)]
        go[z * 2 + y, :, lanes(c * 512, 512, 512)] = jnp.concatenate(wide, 1)
        pl.semaphore_wait(barrier, len(everyone))
        for k in (Q, O):
            own_sends_y(k)
            own_sends_z(k)
        by_rows(first_norm)
        x_rows(rows_one, 0).start()
        base += 512
        gi[me] = pair(base, 0, D, right_high=True)
        for r in range(2):
            for b in range(0, 16, 2):
                at = D + (r * 16 + b) * 64
                gd[me, r * 64 : r * 64 + 64, b * HALF : b * HALF + LANES] = pair(at, at + 64, 64, True, True)

        x_rows(grad_rows, 1).start()
        z_arrival((Q, O), 1)
        y_arrival((Q, O), 0)
        z_arrival((Q, O), 2)
        for k in (I, W, V):
            own_sends_z(k)
        own_sends_y(I)
        y_arrival((Q, O), 1)
        load = pltpu.make_async_copy(root_l, held, copy_sem.at[0])
        load.start()
        load.wait()
        lay_blocks(held, stack)
        load = pltpu.make_async_copy(root_r, held, copy_sem.at[0])
        load.start()
        store = pltpu.make_async_copy(stack, stack_l, copy_sem.at[1])
        store.start()
        load.wait()
        store.wait()
        lay_blocks(held, stack)
        store = pltpu.make_async_copy(stack, stack_r, copy_sem.at[1])
        store.start()
        x_rows_wait(rows_one, 0)
        store.wait()

    pl.run_scoped(
        prepare,
        pltpu.VMEM(view.shape, f32),
        pltpu.VMEM((view.shape[2] // 2 * BLOCK, LANES), f32),
    )

    def core_waits(kinds, zz):
        for k in kinds:
            for yy in (y, 1 - y):
                ag_wait(k, zz, yy, 1 - c)

    ends = []
    for p in range(ARTICLES):
        length = 0
        for a in range(ARTICLES):
            length = length + jnp.where(order[0, p] == a, lengths[0, a], 0)
        ends.append(length + ends[-1] if p else length)

    def allowed(first, count):
        ids = lax.broadcasted_iota(jnp.int32, (rows, 1), 0) + first
        start = jnp.zeros((rows, 1), jnp.int32)
        for end in ends:
            start = jnp.where(ids >= end, end, start)
        start = jnp.where(ids >= ends[-1], ids, start)
        keys = lax.broadcasted_iota(jnp.int32, (rows, count), 1)
        return (keys <= ids) & (keys >= start)

    scale = HD ** (-0.5)
    strip = 1024

    def assemble(h):
        for yy in range(2):
            even, odd = gq.at[slot_of(h, yy, 0)], gq.at[slot_of(h, yy, 1)]
            at = yy * 192
            wqkv[h, 0:768, at : at + 64] = even[:, 0:64]
            wqkv[h, 768:1024, at : at + 64] = even[0:256, 64:128]
            wqkv[h, 0:512, at + 64 : at + 128] = even[256:768, 64:128]
            wqkv[h, 512:1024, at + 64 : at + 128] = odd[0:512, 0:64]
            wqkv[h, 0:256, at + 128 : at + 192] = odd[512:768, 0:64]
            wqkv[h, 256:1024, at + 128 : at + 192] = odd[:, 64:128]

    def disassemble(h, value):
        for yy in range(2):
            even, odd = gq.at[slot_of(h, yy, 0)], gq.at[slot_of(h, yy, 1)]
            at = yy * 192
            even[:, 0:64] = value[0:768, at : at + 64]
            even[0:256, 64:128] = value[768:1024, at : at + 64]
            even[256:768, 64:128] = value[0:512, at + 64 : at + 128]
            odd[0:512, 0:64] = value[512:1024, at + 64 : at + 128]
            odd[512:768, 0:64] = value[0:256, at + 128 : at + 192]
            odd[:, 64:128] = value[256:1024, at + 128 : at + 192]

    qv = vecs[pl.ds(6 + t, 1), :]
    for h in range(DEPTH):
        none = jnp.zeros((1, HD), f32)
        qkv_bias[h] = jnp.concatenate([qv[:, h * 256 : h * 256 + 128], none, qv[:, h * 256 + 128 : h * 256 + 256]], 1)

    def head(h):
        core_waits((Q,), h)
        assemble(h)
        qkv[h] = (dot(rows_one[...], wqkv[h]) + qkv_bias[h]).astype(bf)
        for block in range(2):
            at, seen = slice(block * rows, (block + 1) * rows), (block + 1) * rows
            scores = dot_nt(qkv[h, at, 0:128], qkv[h, 0:seen, 128:256]) * scale
            scores = jnp.where(allowed(block * rows, seen), scores, NEG)
            expo = jnp.exp(scores - jnp.max(scores, -1, keepdims=True))
            low = (expo / jnp.sum(expo, -1, keepdims=True)).astype(bf)
            probs[h, at, 0:seen] = low
            ctx[at, lanes(h * HD, HD, HD)] = dot(low, qkv[h, 0:seen, 256:384]).astype(bf)

    head(near(0))
    z_arrival((Q, O), 3)
    own_sends_y(W)
    own_sends_y(V)
    head(near(1))
    y_arrival((Q, O), 2)
    head(near(2))
    y_arrival((Q, O), 3)
    z_arrival((I, W), 1)
    head(near(3))
    y_arrival((I, W), 0)
    v_forward(z, 1 - y)
    for zz in range(DEPTH):
        core_waits((O,), zz)

    def w_out(ref):
        return ref[...].reshape(DEPTH * HD, D)

    far[0] = dot(ctx[other, :], w_out(go)).astype(bf)
    x_part(0).start()
    mixed[...] = tokens[...] + dot(ctx[own, :], w_out(go)) + vecs[4:5, :]
    z_arrival((I, W), 2)
    y_arrival((I, W), 1)
    x_part(0).wait_recv()

    def second_norm(at, step):
        value = mixed[pl.ds(at, step), :] + inx[0, pl.ds(at, step), :].astype(f32)
        mixed[pl.ds(at, step), :] = value
        unit, inverse = norm(value)
        to = pl.ds(pl.multiple_of(t * rows + at, step), step)
        rows_two[to, :] = (unit * vecs[2:3, :] + vecs[3:4, :]).astype(bf)

    by_rows(second_norm)
    x_rows(rows_two, 2).start()
    z_arrival((I, W), 3)
    macc[...] = jnp.zeros_like(macc)
    nacc[...] = jnp.zeros_like(nacc)
    vout[...] = jnp.zeros_like(vout)
    x_rows_wait(grad_rows, 1)

    def ffn(half, zz):
        first = 4 * zz
        at = pl.ds(pl.multiple_of(lax.rem(t + half, 2) * rows, rows), rows)
        units = lanes(zz * 512, 512, 512)
        bias_row = vecs[pl.ds(8 + 2 * t + lax.div(zz, 2), 1), lanes(lax.rem(zz, 2) * 512, 512, 512)]

        def w_in(start, count):
            return jnp.concatenate([gi[first + j, start : start + count, :] for j in range(4)], 1)

        def w_down(start, count):
            return gd[pl.ds(first, 4), :, start : start + count].reshape(512, count)

        inner = dot(rows_two[at, :], w_in(0, D)) + bias_row
        square = inner * inner
        bent = jnp.tanh(GELU_A * inner * (1.0 + GELU_B * square))
        act[at, units] = (0.5 * inner * (1.0 + bent)).astype(bf)
        slope = 0.5 * (1.0 + bent) + 0.5 * inner * (1.0 - bent * bent) * (GELU_A * (1.0 + 3.0 * GELU_B * square))
        gin[at, units] = (dot_nt(grad_rows[at, :], w_down(0, D)) * slope).astype(bf)
        for nb in range(4):
            out = slice(nb * 256, nb * 256 + 256)
            nacc[at, out] += dot_nt(gin[at, units], w_in(nb * 256, 256))
            macc[at, out] += dot(act[at, units], w_down(nb * 256, 256))

    def ffn_grads(zz):
        first = 4 * zz
        units = lanes(zz * 512, 512, 512)
        for k in (I, W, V):
            for yy in range(2):
                drain(k, zz, yy)
        bias_sum[zz] = jnp.sum(gin[:, units].astype(f32), 0, keepdims=True)
        for nb in range(4):
            out = slice(nb * 256, nb * 256 + 256)
            part = dot(rows_t[out, :], gin[:, units]).astype(bf)
            for j in range(4):
                gi[first + j, out, :] = part[:, j * LANES : (j + 1) * LANES]
        for yy in (1 - y, y):
            rc_copy(I, zz, yy).start()
        act_t = act[:, units].T
        for nb in range(4):
            out = slice(nb * 256, nb * 256 + 256)
            part = dot(act_t, grad_rows[:, out]).astype(bf)
            gd[pl.ds(first, 4), :, out] = part.reshape(4, LANES, 256)
        for yy in (1 - y, y):
            rc_copy(W, zz, yy).start()

    def reduce_core(zz):
        for yy in (1 - y, y):
            for k in (I, W):
                rc_add(k, zz, yy)

    def v_step(s):
        for yy in (1 - y, y):
            z_step(V, s, yy)

    def v_merge(s):
        for yy in (1 - y, y):
            z_merge(V, s, yy)

    core_waits((I, W, V), z)
    ffn(0, z)
    v_arrival(1)
    y_arrival((I, W), 2)
    core_waits((I, W, V), near(1))
    ffn(0, near(1))
    v_arrival(2)
    x_rows_wait(rows_two, 2)
    x_out().start()
    rows_t[...] = rows_two[...].T

    def by_z(s, carry):
        @pl.when(s == 2)
        def _():
            v_arrival(3)
            y_arrival((I, W), 3)

        @pl.when(s >= 2)
        def _():
            core_waits((I, W, V), near(s))
            ffn(0, near(s))

        ffn(1, near(s))

        @pl.when(s == DEPTH - 1)
        def _():
            x_part(0).wait_send()
            far[0] = nacc[other, :].astype(bf)
            x_part(1).start()

        ffn_grads(near(s))

        @pl.when(s > 0)
        def _():
            reduce_core(near(s - 1))

        for before in (1, 2):

            @pl.when(s == before + 1)
            def _():
                v_step(before)

        return carry

    lax.fori_loop(0, DEPTH, by_z, 0)
    x_out().wait_recv()
    x_out_core(c).start()
    reduce_core(near(3))
    v_step(3)
    v_merge(1)
    for zz in range(DEPTH):
        for side in range(2):
            row, start = 8 + 2 * side + zz // 2, zz % 2 * 512
            vout[0, row : row + 1, start : start + 512] = jnp.where(t == side, bias_sum[zz], 0.0)
    rows_t[...] = rows_one[...].T
    x_part(1).wait_recv()

    def row_sum(row, value):
        vout[0, row : row + 1, :] += jnp.sum(value, 0, keepdims=True)

    def second_back(at, step):
        here = pl.ds(at, step)
        in_group = pl.ds(pl.multiple_of(t * rows + at, step), step)
        grad = nacc[in_group, :] + inx[0, here, :].astype(f32)
        unit, inverse = norm(mixed[here, :])
        back = cot[here, :] + norm_grad(grad, unit, inverse, vecs[2:3, :])
        input_grad[here, :] = back
        grad_attn[in_group, :] = back.astype(bf)
        row_sum(2, grad * unit)
        row_sum(3, grad)
        row_sum(4, back)
        row_sum(5, cot[here, :])

    by_rows(second_back)
    early_rows(0)
    x_out_core(1 - c).wait_recv()
    ctx_x[...] = dot_nt(grad_attn[own, :], w_out(go_x)).astype(bf)
    x_grad_context().start()
    gctx[own, :] = dot_nt(grad_attn[own, :], w_out(go)).astype(bf)
    for s in (1, 2):
        for k in (I, W):
            ry_add(k, s)
    v_merge(2)
    for zz in range(DEPTH):
        for yy in range(2):
            drain(O, zz, yy)
            drain(Q, zz, yy)
    def mixed_out(at, step):
        here = pl.ds(at, step)
        in_group = pl.ds(pl.multiple_of(t * rows + at, step), step)
        mixed[here, :] = mixed[here, :] + macc[in_group, :] + inx[1, here, :].astype(f32) + vecs[5:6, :]

    x_out().wait_send()
    x_grad_context_wait()
    x_rows(grad_attn, 3).start()
    far[1] = macc[other, :].astype(bf)

    def out_grads():
        x_rows_wait(grad_attn, 3)
        ctx_t = ctx[...].T
        for nb in range(4):
            at = slice(nb * 256, nb * 256 + 256)
            go[:, :, at] = dot(ctx_t, grad_attn[:, at]).astype(bf).reshape(8, 64, 256)
        for zz in range(DEPTH):
            for yy in range(2):
                rc_copy(O, zz, yy).start()

    def head_back(h, turn):
        q0, q1 = qkv[h, 0:rows, 0:128], qkv[h, rows : 2 * rows, 0:128]
        grads = []
        for block in range(2):
            at, seen = slice(block * rows, (block + 1) * rows), (block + 1) * rows
            low = probs[h, at, 0:seen]
            given = gctx[at, lanes(h * HD, HD, HD)]
            prob = low.astype(f32)
            grad_probs = dot_nt(given, qkv[h, 0:seen, 256:384])
            delta = jnp.sum(prob * grad_probs, -1, keepdims=True)
            grad_scores = (prob * (grad_probs - delta)).astype(bf)
            grad_q = dot(grad_scores, qkv[h, 0:seen, 128:256]) * scale
            grad_k = dot_tn(grad_scores, q1 if block else q0) * scale
            grad_v = dot_tn(low, given)
            grads.append((grad_q, grad_k, grad_v))
        (gq0, gk0, gv0), (gq1, gk1, gv1) = grads
        top = jnp.concatenate([gq0, gk0 + gk1[0:rows], gv0 + gv1[0:rows]], 1).astype(bf)
        low_half = jnp.concatenate([gq1, gk1[rows:], gv1[rows:]], 1).astype(bf)
        qkv[h, 0:rows, :] = top
        qkv[h, rows : 2 * rows, :] = low_half
        total = jnp.sum(top.astype(f32), 0, keepdims=True) + jnp.sum(low_half.astype(f32), 0, keepdims=True)
        qv_sum[h] = total
        for half in (other, own):
            product = dot_nt(qkv[h, half, :], wqkv[h])
            if turn == 0:
                nacc[half, :] = product
            else:
                nacc[half, :] += product
            if turn == DEPTH - 1 and half is other:
                x_part(1).wait_send()
                far[0] = nacc[other, :].astype(bf)
                x_part(3).start()
        part = dot(rows_t[...], qkv[h]).astype(bf)
        disassemble(h, part)
        for yy in (1 - y, y):
            rc_copy(Q, h, yy).start()

    for turn in range(DEPTH):
        head_back(near(DEPTH - 1 - turn), turn)
        if turn < 3:
            early_rows(turn + 1)
        if turn > 0:
            for yy in (1 - y, y):
                rc_add(Q, near(DEPTH - turn), yy)
        if turn == 0:
            for k in (I, W):
                ry_add(k, 3)
            v_cross()
        if turn == 1:
            for k in (I, W):
                ry_merge(k, 1)
            out_grads()
            x_part(2).start()
        if turn == 2:
            for k in (I, W):
                ry_merge(k, 2)
            for yy in (1 - y, y):
                for s in (3, 2, 1, 0):
                    rc_add(O, near(s), yy)
            ry_add(Q, 3)
    for yy in (1 - y, y):
        rc_add(Q, z, yy)
    ry_add(Q, 2)
    ry_merge(Q, 2)
    for k in (I, W):
        own_total(k)
    for s in (3, 2, 1):
        ry_add(O, s)
    x_part(2).wait_recv()
    by_rows(mixed_out)
    x_part(3).wait_recv()

    def first_back(at, step):
        here = pl.ds(at, step)
        in_group = pl.ds(pl.multiple_of(t * rows + at, step), step)
        grad = nacc[in_group, :] + inx[0, here, :].astype(f32)
        unit, inverse = norm(tokens[here, :])
        input_grad[here, :] = input_grad[here, :] + norm_grad(grad, unit, inverse, vecs[0:1, :])
        row_sum(0, grad * unit)
        row_sum(1, grad)

    by_rows(first_back)

    for h in range(DEPTH):
        for row in range(2):
            total = jnp.where(t == row, qv_sum[h], 0.0)
            vout[0, 6 + row : 7 + row, h * 256 : h * 256 + 128] = total[:, 0:128]
            vout[0, 6 + row : 7 + row, h * 256 + 128 : h * 256 + 256] = total[:, 256:384]
    for row in range(4):
        for j in range(8):
            late[row * 8 + j : row * 8 + j + 1, :] = vout[0, (0, 1, 6, 7)[row] : (0, 1, 6, 7)[row] + 1, j * LANES : (j + 1) * LANES]
    here = t * 4 + y * 2 + c
    late_in[here] = late[...]
    for turn in range(1, 8):
        late_copy(turn).start()
    ry_add(Q, 1)
    ry_merge(O, 2)
    ry_merge(Q, 1)
    ry_merge(O, 1)
    z_total(V, y, total_of(V), y_landed(V, z))
    for turn in range(1, 8):
        late_wait(late_turn(turn)[1])
    total = late_in[0]
    for index in range(1, 8):
        total = total + late_in[index]
    late_sum[...] = total
    late_in[8 + z] = total
    for step in range(1, DEPTH):
        late_z(step).start()
    own_total(O)
    own_total(Q)
    for step in range(1, DEPTH):
        late_wait(8 + lax.rem(z + step, DEPTH))
    total = ((late_in[8] + late_in[9]) + late_in[10]) + late_in[11]
    for step in range(1, DEPTH):
        zz = lax.rem(z + step, DEPTH)
        remote(vin.at[3 + zz], vin.at[3 + zz], v_send.at[0], v_recv.at[3 + zz], y_peer).wait_recv()
    early = ((vin[3] + vin[4]) + vin[5]) + vin[6]
    vec_grads[...] = early[0 : vec_grads.shape[0]]
    for row in range(4):
        for j in range(8):
            vec_grads[(0, 1, 6, 7)[row] : (0, 1, 6, 7)[row] + 1, j * LANES : (j + 1) * LANES] = total[row * 8 + j : row * 8 + j + 1, :]

    for stage in range(3):
        v_copy(stage).wait_send()
    for turn in range(1, 8):
        late_copy(turn).wait_send()
    for step in range(1, DEPTH):
        vz_copy(step).wait_send()
        late_z(step).wait_send()
    for index, ref in enumerate((rows_one, grad_rows, rows_two, grad_attn)):
        x_rows(ref, index).wait_send()
    for index in (2, 3):
        x_part(index).wait_send()
    x_out_core(c).wait_send()
    x_grad_context().wait_send()
    for k in range(4):
        for zz in range(DEPTH):
            for yy in range(2):
                rc_copy(k, zz, yy).wait_send()
            ry_copy(k, zz).wait_send()
        for s in range(1, DEPTH):
            rz_copy(k, s, y, True).wait_send()
    ry_copy(V, z).wait_send()
    for yy in range(2):
        for s in range(1, DEPTH):
            rz_copy(V, s, yy, True).wait_send()


def run_layer(tokens, cotangent, lengths, order, weights, roots, vec_params):
    bf, f32 = jnp.bfloat16, jnp.float32
    rows = tokens.shape[0]
    group = 2 * rows
    owners = 16
    shapes = piece_shapes()
    views = [jnp.transpose(a, (1, 2, 0)) for a in (weights, *roots)]
    stack = jax.ShapeDtypeStruct((weights.shape[0] // 2 * BLOCK, LANES), f32)
    there = pl.BlockSpec(memory_space=pl.ANY)
    vmem = pl.BlockSpec(memory_space=pltpu.VMEM)
    smem = pl.BlockSpec(memory_space=pltpu.SMEM)

    halved = shapes[:3] + ((HALF, D),)

    def many(count, kinds):
        return [pltpu.VMEM((count,) + s, bf) for s in kinds]

    full = pltpu.VMEM((group, D), bf)
    dma = pltpu.SemaphoreType.DMA
    return pl.pallas_call(
        layer_kernel,
        out_shape=[jax.ShapeDtypeStruct((rows, D), f32)] * 2
        + [jax.ShapeDtypeStruct(s, f32) for s in shapes]
        + [jax.ShapeDtypeStruct(vec_params.shape, f32)]
        + [stack] * 2,
        in_specs=[smem, smem] + [there] * 3 + [vmem] * 3,
        out_specs=[vmem] * 7 + [there] * 2,
        scratch_shapes=[
            pltpu.VMEM((owners,) + shapes[0], bf),
            pltpu.VMEM((owners // 2, BLOCK, D), bf),
            pltpu.VMEM((owners,) + shapes[2], bf),
            pltpu.VMEM((owners,) + shapes[3], bf),
            pltpu.VMEM((DEPTH, D, 3 * HD), bf),
        ]
        + many(2 * DEPTH, shapes)
        + many(DEPTH, halved)
        + many(1, halved[3:])
        + many(DEPTH, halved)
        + many(2 * DEPTH, halved[3:])
        + [
            full,
            full,
            pltpu.VMEM((D, group), bf),
            full,
            full,
            pltpu.VMEM((DEPTH, group, group), bf),
            pltpu.VMEM((DEPTH, group, 3 * HD), bf),
            pltpu.VMEM((group, DEPTH * HD), bf),
            pltpu.VMEM((group, DEPTH * HD), bf),
            pltpu.VMEM((2, rows, D), bf),
            pltpu.VMEM((2, rows, D), bf),
            pltpu.VMEM((owners // 2, BLOCK, D), bf),
            pltpu.VMEM((rows, DEPTH * HD), bf),
            pltpu.VMEM((group, D), f32),
            pltpu.VMEM((group, D), f32),
            pltpu.VMEM((group, 2 * D), bf),
            pltpu.VMEM((group, 2 * D), bf),
            pltpu.VMEM((DEPTH, 1, 512), f32),
            pltpu.VMEM((DEPTH, 1, 3 * HD), f32),
            pltpu.VMEM((DEPTH, 1, 3 * HD), f32),
            pltpu.VMEM((7, 16, D), f32),
            pltpu.VMEM((5, 16, D), f32),
            pltpu.VMEM((32, LANES), f32),
            pltpu.VMEM((32, LANES), f32),
            pltpu.VMEM((12, 32, LANES), f32),
            dma((5, owners)),
            dma((5, DEPTH)),
            dma((5, 2 * DEPTH)),
            dma((5, 2, 2 * DEPTH)),
            dma((4, 2 * DEPTH)),
            dma((4, 2 * DEPTH)),
            dma((5, DEPTH)),
            dma((5, DEPTH)),
            dma((5, 2 * DEPTH)),
            dma((5, 2 * DEPTH)),
            dma((11,)),
            dma((11,)),
            dma((6,)),
            dma((7,)),
            dma((11,)),
            dma((12,)),
            dma((2,)),
        ],
        compiler_params=pltpu.CompilerParams(
            collective_id=0, has_side_effects=True, vmem_limit_bytes=VMEM_LIMIT
        ),
        name="layer",
    )(lengths, order, *views, tokens, cotangent, vec_params)


def per_device(
    grp_count,
    tp_count,
    tokens,
    cotangent,
    lengths,
    order,
    weights,
    momentum,
    stat_left,
    stat_right,
    root_left,
    root_right,
    vec_params,
    vec_momentum,
    vec_second,
):
    fits = grp_count == 4 * DEPTH and tp_count == 2 and tokens.shape[0] == 256
    if not fits or lengths.shape[1] != ARTICLES:
        return per_device_general(
            tokens,
            cotangent,
            lengths,
            order,
            weights,
            momentum,
            stat_left,
            stat_right,
            root_left,
            root_right,
            vec_params,
            vec_momentum,
            vec_second,
        )
    token_total = tokens.shape[0] * tp_count * grp_count
    mixed, input_grad, *sums, vec_grads, stack_l, stack_r = run_layer(
        tokens, cotangent, lengths, order, weights, (root_left, root_right), vec_params
    )
    blocks, vecs, results = update_blocks(
        sums,
        (stack_l, stack_r),
        (weights, momentum, stat_left, stat_right),
        vec_grads,
        (vec_params, vec_momentum, vec_second),
        (mixed, input_grad),
        token_total,
    )
    return (*results, *blocks, *vecs)


def solution(mesh):
    placed = (
        P(("grp", "tp"), None),
        P(("grp", "tp"), None),
        P("grp", None),
        P("grp", None),
        P(("tp", "grp"), None, None),
        P(("tp", "grp"), None, None),
        P(("tp", "grp"), None, None),
        P(("tp", "grp"), None, None),
        P(("tp", "grp"), None, None),
        P(("tp", "grp"), None, None),
        P(),
        P(),
        P(),
    )
    return jax.shard_map(
        functools.partial(per_device, mesh.shape["grp"], mesh.shape["tp"]),
        mesh=mesh,
        in_specs=placed,
        out_specs=(
            P(("grp", "tp"), None),
            P(("grp", "tp"), None),
            P(("tp", "grp"), None, None),
            P(("tp", "grp"), None, None),
            P(("tp", "grp"), None, None),
            P(("tp", "grp"), None, None),
            P(("tp", "grp"), None, None),
            P(),
            P(),
            P(),
            P(),
        ),
        check_vma=False,
    )
```

```python
import functools

import jax
import jax.numpy as jnp
from jax import lax
from jax.experimental import pallas as pl
from jax.experimental.pallas import tpu as pltpu
from jax.sharding import PartitionSpec as P

D = 1024
HEADS = 8
HD = 128
FF = 4096
BLOCK = 64


EPS = 1e-05
NEG = -1e30
DECAY = 0.9
BETA = 0.9
RATE = 0.05
VEC_DECAY = 0.9
VEC_RATE = 0.2
VEC_EPS = 1e-08


def norm_rows(value, gain, shift):
    average = jnp.mean(value, -1, keepdims=True)
    centred = value - average
    inverse = lax.rsqrt(jnp.mean(centred * centred, -1, keepdims=True) + EPS)
    normed = centred * inverse
    return (normed * gain + shift, normed, inverse)


def norm_back(grad_out, normed, inverse, gain):
    scaled = grad_out * gain
    return inverse * (
        scaled
        - jnp.mean(scaled, -1, keepdims=True)
        - normed * jnp.mean(scaled * normed, -1, keepdims=True)
    )


def segment_ids(lengths_row, order_row, group_rows):
    article_count = lengths_row.shape[0]
    slots = jnp.arange(article_count, dtype=jnp.int32)
    picks = (order_row[:, None] == slots[None, :]).astype(jnp.int32)
    packed = jnp.sum(picks * lengths_row[None, :], 1)
    ends = jnp.cumsum(packed)
    spots = jnp.arange(group_rows, dtype=jnp.int32)
    return jnp.sum((spots[:, None] >= ends[None, :]).astype(jnp.int32), 1)


def allowed_mask(row_ids, row_segs, segments, key_ids, article_count):
    causal = key_ids[None, :] <= row_ids[:, None]
    same = segments[None, :] == row_segs[:, None]
    alone = (row_segs[:, None] < article_count) | (key_ids[None, :] == row_ids[:, None])
    return causal & same & alone


def from_columns(tiles, row_total, col_total):
    return (
        tiles.reshape(col_total // BLOCK, row_total // BLOCK, BLOCK, BLOCK)
        .transpose(1, 2, 0, 3)
        .reshape(row_total, col_total)
    )


def from_rows(tiles, row_total, col_total):
    return (
        tiles.reshape(row_total // BLOCK, col_total // BLOCK, BLOCK, BLOCK)
        .transpose(0, 2, 1, 3)
        .reshape(row_total, col_total)
    )


def to_columns(matrix):
    row_total, col_total = matrix.shape
    return (
        matrix.reshape(row_total // BLOCK, BLOCK, col_total // BLOCK, BLOCK)
        .transpose(2, 0, 1, 3)
        .reshape(-1, BLOCK, BLOCK)
    )


def to_rows(matrix):
    row_total, col_total = matrix.shape
    return (
        matrix.reshape(row_total // BLOCK, BLOCK, col_total // BLOCK, BLOCK)
        .transpose(0, 2, 1, 3)
        .reshape(-1, BLOCK, BLOCK)
    )


def per_device_general(
    tokens,
    cotangent,
    lengths,
    order,
    weights,
    momentum,
    stat_left,
    stat_right,
    root_left,
    root_right,
    vec_params,
    vec_momentum,
    vec_second,
):
    groups = lax.axis_size("grp")
    tp_size = lax.axis_size("tp")
    tp_rank = lax.axis_index("tp")
    tok_rows = tokens.shape[0]
    group_rows = tok_rows * tp_size
    article_count = lengths.shape[1]
    owners = groups * tp_size
    block_area = BLOCK * BLOCK * owners
    qkv_count = 3 * D * D // block_area
    out_count = D * D // block_area
    in_count = D * FF // block_area
    owned_blocks = weights.shape[0]
    heads_here = HEADS // tp_size
    qkv_cols = 3 * D // tp_size
    feat_here = D // tp_size
    ff_here = FF // tp_size
    qv_width = 2 * D // tp_size
    token_total = group_rows * groups
    gathered = lax.all_gather(weights.astype(jnp.bfloat16), "grp", axis=0, tiled=True)
    per_owner = gathered.reshape(groups, owned_blocks, BLOCK, BLOCK)
    marks = [0, qkv_count, qkv_count + out_count, qkv_count + out_count + in_count, owned_blocks]
    pieces = [
        per_owner[:, marks[index] : marks[index + 1]].reshape(-1, BLOCK, BLOCK)
        for index in range(4)
    ]
    w_qkv = from_columns(pieces[0], D, qkv_cols)
    w_out = from_rows(pieces[1], feat_here, D)
    w_in = from_columns(pieces[2], D, ff_here)
    w_down = from_rows(pieces[3], ff_here, D)
    w_qkv_heads = w_qkv.reshape(D, heads_here, 3, HD)
    w_out_heads = w_out.reshape(heads_here, HD, D)
    segments = segment_ids(lengths[0], order[0], group_rows)
    gain_one = vec_params[0]
    shift_one = vec_params[1]
    gain_two = vec_params[2]
    shift_two = vec_params[3]
    bias_out = vec_params[4]
    bias_down = vec_params[5]
    qv_here = lax.dynamic_slice_in_dim(
        vec_params[6:8].reshape(2 * D), tp_rank * qv_width, qv_width
    ).reshape(heads_here, 2, HD)
    bias_heads = jnp.stack(
        [qv_here[:, 0], jnp.zeros((heads_here, HD), jnp.float32), qv_here[:, 1]], 0
    )[:, :, None, :]
    bias_in = lax.dynamic_slice_in_dim(vec_params[8:].reshape(FF), tp_rank * ff_here, ff_here)
    normed_one, unit_one, inverse_one = norm_rows(tokens, gain_one, shift_one)
    rows_one = lax.all_gather(normed_one.astype(jnp.bfloat16), "tp", axis=0, tiled=True)
    projected = (
        jnp.einsum("rx,xhcd->chrd", rows_one, w_qkv_heads, preferred_element_type=jnp.float32)
        + bias_heads
    ).astype(jnp.bfloat16)
    queries = projected[0]
    keys_all = projected[1]
    values_all = projected[2]
    span = min(512, group_rows)
    starts = jnp.arange(group_rows // span, dtype=jnp.int32) * span
    key_ids = jnp.arange(group_rows, dtype=jnp.int32)
    score_scale = HD ** (-0.5)

    def masked_scores(first_row):
        row_ids = first_row + jnp.arange(span, dtype=jnp.int32)
        row_segs = lax.dynamic_slice_in_dim(segments, first_row, span, 0)
        allowed = allowed_mask(row_ids, row_segs, segments, key_ids, article_count)
        query_rows = lax.dynamic_slice_in_dim(queries, first_row, span, 1)
        scores = (
            jnp.einsum("hqd,hkd->hqk", query_rows, keys_all, preferred_element_type=jnp.float32)
            * score_scale
        )
        return (jnp.where(allowed[None], scores, NEG), query_rows)

    def attend(context_buf, first_row):
        scores, query_rows = masked_scores(first_row)
        row_max = jnp.max(scores, -1, keepdims=True)
        expo = jnp.exp(scores - row_max)
        expsum = jnp.sum(expo, -1, keepdims=True)
        probs_low = (expo / expsum).astype(jnp.bfloat16)
        context = jnp.einsum(
            "hqk,hkd->hqd", probs_low, values_all, preferred_element_type=jnp.float32
        ).astype(jnp.bfloat16)
        context_buf = lax.dynamic_update_slice_in_dim(context_buf, context, first_row, 1)
        return (context_buf, (row_max + jnp.log(expsum))[:, :, 0])

    context_low, log_norm = lax.scan(
        attend, jnp.zeros((heads_here, group_rows, HD), jnp.bfloat16), starts
    )
    attn_sum = lax.psum_scatter(
        jnp.einsum(
            "hrd,hde->re", context_low, w_out_heads, preferred_element_type=jnp.float32
        ).astype(jnp.bfloat16),
        "tp",
        scatter_dimension=0,
        tiled=True,
    ).astype(jnp.float32)
    hidden = tokens + attn_sum + bias_out
    normed_two, unit_two, inverse_two = norm_rows(hidden, gain_two, shift_two)
    rows_two = lax.all_gather(normed_two.astype(jnp.bfloat16), "tp", axis=0, tiled=True)
    inner = jnp.dot(rows_two, w_in, preferred_element_type=jnp.float32) + bias_in
    activ, gelu_pull = jax.vjp(jax.nn.gelu, inner)
    activ_low = activ.astype(jnp.bfloat16)
    mixed = (
        hidden
        + lax.psum_scatter(
            jnp.dot(activ_low, w_down, preferred_element_type=jnp.float32).astype(jnp.bfloat16),
            "tp",
            scatter_dimension=0,
            tiled=True,
        ).astype(jnp.float32)
        + bias_down
    )
    grad_low = cotangent.astype(jnp.bfloat16)
    grad_rows = lax.all_gather(grad_low, "tp", axis=0, tiled=True)
    g_down = jnp.einsum("rf,rd->fd", activ_low, grad_rows, preferred_element_type=jnp.float32)
    grad_activ = jnp.einsum("rd,fd->rf", grad_rows, w_down, preferred_element_type=jnp.float32)
    grad_inner = gelu_pull(grad_activ)[0].astype(jnp.bfloat16)
    g_in = jnp.einsum("rd,rf->df", rows_two, grad_inner, preferred_element_type=jnp.float32)
    g_bias_in = jnp.sum(grad_inner.astype(jnp.float32), 0)
    ffn_blocks = jnp.concatenate(
        [
            to_columns(g_in).reshape(groups, in_count, BLOCK, BLOCK),
            to_rows(g_down).reshape(groups, in_count, BLOCK, BLOCK),
        ],
        1,
    )
    grad_normed_two = lax.psum_scatter(
        jnp.einsum("rf,df->rd", grad_inner, w_in, preferred_element_type=jnp.float32).astype(
            jnp.bfloat16
        ),
        "tp",
        scatter_dimension=0,
        tiled=True,
    ).astype(jnp.float32)
    grad_hidden = cotangent + norm_back(grad_normed_two, unit_two, inverse_two, gain_two)
    grad_attn_low = grad_hidden.astype(jnp.bfloat16)
    grad_attn_rows = lax.all_gather(grad_attn_low, "tp", axis=0, tiled=True)
    g_out = jnp.einsum(
        "hrd,re->hde", context_low, grad_attn_rows, preferred_element_type=jnp.float32
    ).reshape(feat_here, D)
    grad_context = jnp.einsum(
        "re,hde->hrd", grad_attn_rows, w_out_heads, preferred_element_type=jnp.float32
    ).astype(jnp.bfloat16)
    zero_heads = jnp.zeros((heads_here, group_rows, HD), jnp.float32)

    def attend_back(carry, inputs):
        grad_queries, grad_keys, grad_values = carry
        first_row, log_block = inputs
        scores, query_rows = masked_scores(first_row)
        probs = jnp.exp(scores - log_block[:, :, None])
        grad_ctx_rows = lax.dynamic_slice_in_dim(grad_context, first_row, span, 1)
        grad_probs = jnp.einsum(
            "hqd,hkd->hqk", grad_ctx_rows, values_all, preferred_element_type=jnp.float32
        )
        delta = jnp.sum(probs * grad_probs, -1, keepdims=True)
        grad_scores = (probs * (grad_probs - delta)).astype(jnp.bfloat16)
        query_part = (
            jnp.einsum("hqk,hkd->hqd", grad_scores, keys_all, preferred_element_type=jnp.float32)
            * score_scale
        )
        grad_queries = lax.dynamic_update_slice_in_dim(grad_queries, query_part, first_row, 1)
        grad_keys = (
            grad_keys
            + jnp.einsum(
                "hqk,hqd->hkd", grad_scores, query_rows, preferred_element_type=jnp.float32
            )
            * score_scale
        )
        grad_values = grad_values + jnp.einsum(
            "hqk,hqd->hkd",
            probs.astype(jnp.bfloat16),
            grad_ctx_rows,
            preferred_element_type=jnp.float32,
        )
        return ((grad_queries, grad_keys, grad_values), None)

    (grad_queries, grad_keys, grad_values), unused = lax.scan(
        attend_back, (zero_heads, zero_heads, zero_heads), (starts, log_norm)
    )
    grad_proj = jnp.stack([grad_queries, grad_keys, grad_values], 0).astype(jnp.bfloat16)
    proj_sums = jnp.sum(grad_proj.astype(jnp.float32), 2)
    g_bias_qv = jnp.stack([proj_sums[0], proj_sums[2]], 1).reshape(qv_width)
    g_qkv = jnp.einsum(
        "rx,chrd->xhcd", rows_one, grad_proj, preferred_element_type=jnp.float32
    ).reshape(D, qkv_cols)
    grad_normed_one = lax.psum_scatter(
        jnp.einsum(
            "chrd,xhcd->rx", grad_proj, w_qkv_heads, preferred_element_type=jnp.float32
        ).astype(jnp.bfloat16),
        "tp",
        scatter_dimension=0,
        tiled=True,
    ).astype(jnp.float32)
    input_grad = grad_hidden + norm_back(grad_normed_one, unit_one, inverse_one, gain_one)
    local_rows = jnp.stack(
        [
            jnp.sum(grad_normed_one * unit_one, 0),
            jnp.sum(grad_normed_one, 0),
            jnp.sum(grad_normed_two * unit_two, 0),
            jnp.sum(grad_normed_two, 0),
            jnp.sum(grad_hidden, 0),
            jnp.sum(cotangent, 0),
        ]
    )
    qv_rows = lax.dynamic_update_slice(
        jnp.zeros((2 * D,), jnp.float32), g_bias_qv, (tp_rank * qv_width,)
    ).reshape(2, D)
    in_rows = lax.dynamic_update_slice(
        jnp.zeros((FF,), jnp.float32), g_bias_in, (tp_rank * ff_here,)
    ).reshape(FF // D, D)
    vec_grads = lax.psum(jnp.concatenate([local_rows, qv_rows, in_rows], 0), ("grp", "tp"))
    attn_blocks = jnp.concatenate(
        [
            to_columns(g_qkv).reshape(groups, qkv_count, BLOCK, BLOCK),
            to_rows(g_out).reshape(groups, out_count, BLOCK, BLOCK),
        ],
        1,
    )
    every_block = jnp.concatenate([attn_blocks, ffn_blocks], 1).reshape(-1, BLOCK, BLOCK)
    weight_grads = lax.psum_scatter(
        every_block.astype(jnp.bfloat16), "grp", scatter_dimension=0, tiled=True
    ).astype(jnp.float32)
    scaled = weight_grads * token_total ** (-0.5)
    stat_left_new = DECAY * stat_left + (1.0 - DECAY) * jnp.einsum(
        "nij,nkj->nik", scaled, scaled, precision=lax.Precision.HIGHEST
    )
    stat_right_new = DECAY * stat_right + (1.0 - DECAY) * jnp.einsum(
        "nji,njk->nik", scaled, scaled, precision=lax.Precision.HIGHEST
    )
    shaped = jnp.einsum("nij,njk->nik", root_left, scaled, precision=lax.Precision.HIGHEST)
    shaped = jnp.einsum("nij,njk->nik", shaped, root_right, precision=lax.Precision.HIGHEST)
    momentum_new = BETA * momentum + shaped
    weights_new = weights - RATE * momentum_new
    vec_scaled = vec_grads * token_total ** (-0.5)
    vec_second_new = VEC_DECAY * vec_second + (1.0 - VEC_DECAY) * vec_scaled * vec_scaled
    vec_momentum_new = BETA * vec_momentum + vec_scaled * lax.rsqrt(vec_second_new + VEC_EPS)
    vec_new = vec_params - VEC_RATE * vec_momentum_new
    return (
        mixed,
        input_grad,
        weight_grads,
        stat_left_new,
        stat_right_new,
        momentum_new,
        weights_new,
        vec_grads,
        vec_second_new,
        vec_momentum_new,
        vec_new,
    )


MESH_ID = pl.DeviceIdType.MESH
LANES = 128
HALF = 64
VMEM_LIMIT = 62 * 2**20
ARTICLES = 4
GELU_A = (2.0 / 3.141592653589793) ** 0.5
GELU_B = 0.044715


def remote(src, dst, send_sem, recv_sem, device):
    return pltpu.make_async_remote_copy(
        src_ref=src,
        dst_ref=dst,
        send_sem=send_sem,
        recv_sem=recv_sem,
        device_id=device,
        device_id_type=MESH_ID,
    )


def place():
    grp = lax.axis_index("grp")
    return lax.div(grp, 4), lax.rem(lax.div(grp, 2), 2), lax.rem(grp, 2), lax.axis_index("tp")


def slot_of(z, y, c):
    return z * 4 + y * 2 + c


def lay_blocks(view_ref, stack):
    half = view_ref.shape[2] // 2

    def row(i, carry):
        tile = view_ref[i].T
        stack[pl.ds(i, half, stride=BLOCK), :] = jnp.concatenate([tile[:half], tile[half:]], 1)
        return carry

    lax.fori_loop(0, BLOCK, row, 0, unroll=8)


def piece_shapes():
    return ((768, LANES), (64, 512), (1024, LANES), (LANES, 1024))


def both_halves(pair):
    low = lax.broadcasted_iota(jnp.int32, pair.shape, 1) < HALF
    turned = pltpu.roll(pair, HALF, 1)
    return jnp.where(low, pair, turned), jnp.where(low, turned, pair)


def update_kernel(
    scale,
    sum_q,
    sum_o,
    sum_i,
    sum_d,
    root_l,
    root_r,
    vec_g,
    vecs,
    vec_m,
    vec_s,
    mixed,
    input_grad,
    w,
    m,
    sl,
    sr,
    out_g,
    out_sl,
    out_sr,
    out_m,
    out_w,
    out_vg,
    out_vs,
    out_vm,
    out_v,
    out_mixed,
    out_input_grad,
    grads,
    first,
    second,
):
    count = w.shape[2]
    bf, f32 = jnp.bfloat16, jnp.float32
    out_mixed[...] = mixed[...]
    out_input_grad[...] = input_grad[...]

    @pl.when(pl.program_id(0) == 0)
    def _():
        total = vec_g[...]
        out_vg[...] = total
        scaled = total * scale
        fresh = VEC_DECAY * vec_s[...] + (1.0 - VEC_DECAY) * scaled * scaled
        out_vs[...] = fresh
        momentum = BETA * vec_m[...] + scaled * lax.rsqrt(fresh + VEC_EPS)
        out_vm[...] = momentum
        out_v[...] = vecs[...] - VEC_RATE * momentum
        rows = sum_q.shape[0]
        grads[0:rows, 0:HALF] = sum_q[:, 0:HALF]
        grads[rows : 2 * rows, 0:HALF] = sum_q[:, HALF:LANES]
        base = 2 * rows
        for b in range(8):
            grads[base + b * 64 : base + b * 64 + 64, 0:HALF] = sum_o[:, b * HALF : (b + 1) * HALF]
        base += 512
        grads[base : base + D, 0:HALF] = sum_i[:, 0:HALF]
        grads[0:D, HALF:LANES] = sum_i[:, HALF:LANES]
        for r in range(2):
            for b in range(16):
                at = D + (r * 16 + b) * 64
                grads[at : at + 64, HALF:LANES] = sum_d[r * 64 : r * 64 + 64, b * HALF : (b + 1) * HALF]

        def row(i, carry):
            both = jnp.concatenate([root_l[i], root_r[i]], 0)
            second[pl.ds(i, count, stride=BLOCK), :] = both.T
            return carry

        lax.fori_loop(0, BLOCK, row, 0, unroll=8)
        row_id = lax.broadcasted_iota(jnp.int32, (256, 256), 0)
        col_id = lax.broadcasted_iota(jnp.int32, (256, 256), 1)
        mask = lax.shift_right_logical(row_id, 6) == lax.shift_right_logical(col_id, 6)
        low = lax.broadcasted_iota(jnp.int32, (256, LANES), 1) < HALF

        def spread(v):
            return jnp.where(mask, jnp.concatenate([v, v], 1), 0.0).astype(bf)

        def eight(k, carry):
            at = pl.ds(pl.multiple_of(k * 256, 256), 256)
            for side, grad in enumerate(both_halves(grads[at, :])):
                to = pl.ds(pl.multiple_of(k * 256 + side * (count // 2 * BLOCK), 256), 256)
                left, right = both_halves(second[to, :])
                s32 = grad * scale
                s = s32.astype(bf)
                outer = lax.dot_general(s[:, 0:HALF], s[:, 0:HALF], (((1,), (1,)), ((), ())), preferred_element_type=f32)
                kept = jnp.where(mask, outer, 0.0)
                kept = kept[:, :LANES] + kept[:, LANES:]
                outer = kept + pltpu.roll(kept, HALF, 1)
                inner = lax.dot_general(spread(s32), s, (((0,), (0,)), ((), ())), preferred_element_type=f32)
                shaped = jnp.dot(spread(left), s, preferred_element_type=f32)
                shaped = jnp.dot(spread(shaped), right.astype(bf), preferred_element_type=f32)
                first[to, :] = jnp.where(low, grad, outer)
                second[to, :] = jnp.where(low, inner, shaped)
            return carry

        lax.fori_loop(0, count // 8, eight, 0, unroll=2)

    i0 = pl.program_id(0) * w.shape[0]

    def rows_out(ii, carry):
        at = pl.ds(i0 + ii, count, stride=BLOCK)
        one = first[at, :].T
        two = second[at, :].T
        out_g[ii] = one[0:HALF]
        out_sl[ii] = DECAY * sl[ii] + (1.0 - DECAY) * one[HALF:LANES]
        out_sr[ii] = DECAY * sr[ii] + (1.0 - DECAY) * two[0:HALF]
        fresh = BETA * m[ii] + two[HALF:LANES]
        out_m[ii] = fresh
        out_w[ii] = w[ii] - RATE * fresh
        return carry

    lax.fori_loop(0, w.shape[0], rows_out, 0, unroll=True)


def update_blocks(sums, blocks, vec_grads, vecs, results, token_total):
    views = [jnp.transpose(a, (1, 2, 0)) for a in blocks]
    count = blocks[0].shape[0]
    rows = 8
    whole = pl.BlockSpec(memory_space=pltpu.VMEM)
    steps = BLOCK // rows
    some = pl.BlockSpec((results[0].shape[0] // steps, results[0].shape[1]), lambda i: (i, 0))
    part = pl.BlockSpec((rows, BLOCK, count), lambda i: (i, 0, 0))
    vec = jax.ShapeDtypeStruct(vec_grads.shape, jnp.float32)
    outs = pl.pallas_call(
        functools.partial(update_kernel, token_total ** (-0.5)),
        grid=(steps,),
        out_shape=[jax.ShapeDtypeStruct((BLOCK, BLOCK, count), jnp.float32)] * 5
        + [vec] * 4
        + [jax.ShapeDtypeStruct(a.shape, a.dtype) for a in results],
        in_specs=[whole] * 10 + [some] * 2 + [part] * 4,
        out_specs=[part] * 5 + [whole] * 4 + [some] * 2,
        scratch_shapes=[
            pltpu.VMEM((count // 2 * BLOCK, LANES), jnp.float32),
            pltpu.VMEM((count * BLOCK, LANES), jnp.float32),
            pltpu.VMEM((count * BLOCK, LANES), jnp.float32),
        ],
        compiler_params=pltpu.CompilerParams(vmem_limit_bytes=VMEM_LIMIT),
        name="update_blocks",
    )(*sums, *views[4:], vec_grads, *vecs, *results, *views[:4])
    return [jnp.transpose(a, (2, 0, 1)) for a in outs[:5]], outs[5:9], outs[9:]


DEPTH = 4


def layer_kernel(
    lengths,
    order,
    view,
    tokens,
    cot,
    vecs,
    mixed,
    input_grad,
    sum_q,
    sum_o,
    sum_i,
    sum_d,
    vec_grads,
    gq,
    go,
    gi,
    gd,
    wqkv,
    cq,
    co,
    ci,
    cd,
    yq,
    yo,
    yi,
    yd,
    yv,
    zq,
    zo,
    zi,
    zd,
    zv,
    rows_one,
    rows_two,
    rows_t,
    grad_rows,
    grad_attn,
    probs,
    qkv,
    ctx,
    gctx,
    far,
    inx,
    go_x,
    ctx_x,
    macc,
    nacc,
    act,
    gin,
    bias_sum,
    qkv_bias,
    qv_sum,
    vin,
    vout,
    late,
    late_sum,
    late_in,
    recv,
    send_y,
    send_c,
    send_z,
    rc_recv,
    rc_send,
    ry_recv,
    ry_send,
    rz_recv,
    rz_send,
    x_send,
    x_recv,
    v_send,
    v_recv,
    l_send,
    l_recv,
    copy_sem,
):
    bf, f32 = jnp.bfloat16, jnp.float32
    z, y, c, t = place()
    me = slot_of(z, y, c)
    x_peer = (me, 1 - t)
    y_peer = (slot_of(z, 1 - y, c), t)
    c_peer = (slot_of(z, y, 1 - c), t)
    rows = tokens.shape[0]
    own = pl.ds(pl.multiple_of(t * rows, rows), rows)
    other = pl.ds(pl.multiple_of((1 - t) * rows, rows), rows)

    def lanes(start, size, unit):
        return pl.ds(pl.multiple_of(start, unit), size)

    gathered, core_in = (gq, go, gi, gd), (cq, co, ci, cd)
    y_in, z_in = (yq, yo, yi, yd, yv), (zq, zo, zi, zd, zv)
    sums = (sum_q, sum_o, sum_i, sum_d)
    Q, O, I, W, V = range(5)

    def dot(a, b):
        return jnp.dot(a, b, preferred_element_type=f32)

    def dot_nt(a, b):
        return lax.dot_general(a, b, (((1,), (1,)), ((), ())), preferred_element_type=f32)

    def dot_tn(a, b):
        return lax.dot_general(a, b, (((0,), (0,)), ((), ())), preferred_element_type=f32)

    def piece(k, zz, yy, cc):
        if k == O:
            return go.at[zz * 2 + yy, :, pl.ds(pl.multiple_of(cc * 512, 512), 512)]
        return gathered[k].at[slot_of(zz, yy, cc)]

    def near(s):
        return lax.rem(z + (1 - 2 * lax.div(z, 2)) * s + DEPTH, DEPTH)

    def ag_piece(k, zz, yy, cc):
        if k == W:
            return gd.at[slot_of(zz, yy, cc), 0:HALF]
        if k == V:
            return gd.at[slot_of(zz, yy, cc), HALF:LANES]
        return piece(k, zz, yy, cc)

    def ag_copy(k, zz, yy, way):
        src = ag_piece(k, zz, yy, c)
        sem = recv.at[k, slot_of(zz, yy, c)]
        if way == "up":
            return remote(src, src, send_z.at[k, 0, yy * DEPTH + zz], sem, (slot_of(z + 1, y, c), t))
        if way == "down":
            return remote(src, src, send_z.at[k, 1, yy * DEPTH + zz], sem, (slot_of(z - 1, y, c), t))
        if way == "y":
            return remote(src, src, send_y.at[k, zz], sem, y_peer)
        return remote(src, src, send_c.at[k, yy * DEPTH + zz], sem, c_peer)

    def ag_wait(k, zz, yy, cc):
        ref = ag_piece(k, zz, yy, cc)
        remote(ref, ref, send_y.at[k, 0], recv.at[k, slot_of(zz, yy, cc)], y_peer).wait_recv()

    def own_sends_z(k):
        @pl.when(z < DEPTH - 1)
        def _():
            ag_copy(k, z, y, "up").start()

        @pl.when(z > 0)
        def _():
            ag_copy(k, z, y, "down").start()

        ag_copy(k, z, y, "core").start()

    def own_sends_y(k):
        ag_copy(k, z, y, "y").start()

    def z_arrival(kinds, dist):
        @pl.when(z >= dist)
        def _():
            for k in kinds:
                ag_wait(k, z - dist, y, c)

                @pl.when(z < DEPTH - 1)
                def _():
                    ag_copy(k, z - dist, y, "up").start()

                ag_copy(k, z - dist, y, "y").start()
                ag_copy(k, z - dist, y, "core").start()

        @pl.when(z + dist < DEPTH)
        def _():
            for k in kinds:
                ag_wait(k, z + dist, y, c)

                @pl.when(z > 0)
                def _():
                    ag_copy(k, z + dist, y, "down").start()

                ag_copy(k, z + dist, y, "y").start()
                ag_copy(k, z + dist, y, "core").start()

    def y_arrival(kinds, dist):
        def one(zz):
            for k in kinds:
                ag_wait(k, zz, 1 - y, c)
                ag_copy(k, zz, 1 - y, "core").start()

        if dist == 0:
            one(z)
            return

        @pl.when(z >= dist)
        def _():
            one(z - dist)

        @pl.when(z + dist < DEPTH)
        def _():
            one(z + dist)

    def v_forward(zz, yy):
        ag_wait(V, zz, yy, c)

        @pl.when((zz <= z) & (z < DEPTH - 1))
        def _():
            ag_copy(V, zz, yy, "up").start()

        @pl.when((zz >= z) & (z > 0))
        def _():
            ag_copy(V, zz, yy, "down").start()

        ag_copy(V, zz, yy, "core").start()

    def v_arrival(dist):
        for yy in (y, 1 - y):

            @pl.when(z >= dist)
            def _():
                v_forward(z - dist, yy)

            @pl.when(z + dist < DEPTH)
            def _():
                v_forward(z + dist, yy)

    def drain(k, zz, yy):
        ag_copy(k, zz, yy, "core").wait_send()
        if k == V:

            @pl.when((yy == y) & (zz == z))
            def _():
                ag_copy(k, zz, yy, "y").wait_send()

            @pl.when((zz <= z) & (z < DEPTH - 1))
            def _():
                ag_copy(k, zz, yy, "up").wait_send()

            @pl.when((zz >= z) & (z > 0))
            def _():
                ag_copy(k, zz, yy, "down").wait_send()

            return

        @pl.when(yy == y)
        def _():
            ag_copy(k, zz, y, "y").wait_send()

            @pl.when((zz <= z) & (z < DEPTH - 1))
            def _():
                ag_copy(k, zz, y, "up").wait_send()

            @pl.when((zz >= z) & (z > 0))
            def _():
                ag_copy(k, zz, y, "down").wait_send()

    def add(dst, *terms):
        count, width = dst.shape
        step = min(count, 256 * LANES // width)

        def body(i, carry):
            at = pl.ds(pl.multiple_of(i * step, 16), step)
            if len(terms) == 2 and dst.dtype == bf:
                dst[at, :] = terms[0][at, :] + terms[1][at, :]
                return carry
            total = terms[0][at, :].astype(f32)
            for term in terms[1:]:
                total = total + term[at, :].astype(f32)
            dst[at, :] = total.astype(dst.dtype)
            return carry

        lax.fori_loop(0, count // step, body, 0, unroll=2)

    side = lax.div(z, 2)
    end_z, inner_z = 3 * side, 1 + side
    is_end = z == end_z

    def rc_copy(k, zz, yy):
        at = zz * 2 + yy
        return remote(piece(k, zz, yy, 1 - c), core_in[k].at[at], rc_send.at[k, at], rc_recv.at[k, at], c_peer)

    def ry_copy(k, zz):
        if k == V:
            return remote(ag_piece(V, z, 1 - y, c), y_in[V].at[0], ry_send.at[V, 0], ry_recv.at[V, 0], y_peer)
        return remote(ag_piece(k, zz, 1 - y, c), y_in[k].at[zz], ry_send.at[k, zz], ry_recv.at[k, zz], y_peer)

    def z_slot(k, slot, yy):
        return z_in[k].at[slot * 2 + yy if k == V else slot]

    def z_sem(slot, yy):
        return slot * 2 + yy

    def rz_copy(k, s, yy, from_end):
        slot = s - 1 if from_end else {3: 0, 2: 1, 1: 3}[s]
        to = inner_z if from_end else {3: end_z, 2: 3 - end_z, 1: 3 - inner_z}[s]
        sent, landed = rz_send.at[k, (s - 1) * 2 + yy], rz_recv.at[k, z_sem(slot, yy)]
        return remote(ag_piece(k, near(s), yy, c), z_slot(k, slot, yy), sent, landed, (slot_of(to, y, c), t))

    def z_landed(k, slot, yy):
        ref = z_slot(k, slot, yy)
        remote(ref, ref, rz_send.at[k, 0], rz_recv.at[k, z_sem(slot, yy)], y_peer).wait_recv()
        return ref

    def y_landed(k, zz):
        ref = y_in[k].at[0 if k == V else zz]
        remote(ref, ref, ry_send.at[k, 0], ry_recv.at[k, 0 if k == V else zz], y_peer).wait_recv()
        return ref

    def rc_add(k, zz, yy):
        at = zz * 2 + yy
        remote(core_in[k].at[at], core_in[k].at[at], rc_send.at[k, 0], rc_recv.at[k, at], c_peer).wait_recv()
        mine = piece(k, zz, yy, c)
        add(mine, mine, core_in[k].at[at])

        @pl.when(yy != y)
        def _():
            ry_copy(k, zz).start()

    def z_step(k, s, yy, *terms):
        mine = ag_piece(k, near(s), yy, c)
        if terms:
            add(mine, mine, *terms)

        @pl.when(is_end)
        def _():
            rz_copy(k, s, yy, True).start()

        if s == 3:

            @pl.when(jnp.logical_not(is_end))
            def _():
                rz_copy(k, s, yy, False).start()

    def z_merge(k, s, yy):
        @pl.when(jnp.logical_not(is_end))
        def _():
            mine = ag_piece(k, near(s), yy, c)
            add(mine, mine, z_landed(k, s, yy))
            rz_copy(k, s, yy, False).start()

    def ry_add(k, s):
        z_step(k, s, y, y_landed(k, near(s)))

    def ry_merge(k, s):
        z_merge(k, s, y)

    def total_of(k):
        return sum_d.at[(k - W) * HALF : (k - W + 1) * HALF] if k >= W else sums[k]

    def z_total(k, yy, dst, *terms):
        mine = ag_piece(k, z, yy, c)
        first = z_landed(k, 0, yy)

        @pl.when(is_end)
        def _():
            add(dst, mine, first, z_landed(k, 1, yy), *terms)

        @pl.when(jnp.logical_not(is_end))
        def _():
            add(dst, mine, first, z_landed(k, 3, yy), *terms)

    def own_total(k):
        z_total(k, y, total_of(k), y_landed(k, z))

    def v_cross():
        mine = ag_piece(V, z, 1 - y, c)
        z_total(V, 1 - y, mine)
        ry_copy(V, z).start()

    def x_rows(ref, index):
        return remote(ref.at[own], ref.at[own], x_send.at[index], x_recv.at[index], x_peer)

    def x_rows_wait(ref, index):
        remote(ref.at[other], ref.at[other], x_send.at[index], x_recv.at[index], x_peer).wait_recv()

    def x_part(index):
        slot = 1 if index == 2 else 0
        return remote(far.at[slot], inx.at[slot], x_send.at[5 + index], x_recv.at[5 + index], x_peer)

    def by_rows(body, step=64):
        def run(i, carry):
            body(pl.multiple_of(i * step, step), step)
            return carry

        lax.fori_loop(0, rows // step, run, 0)

    def norm(value):
        average = jnp.mean(value, -1, keepdims=True)
        centred = value - average
        inverse = lax.rsqrt(jnp.mean(centred * centred, -1, keepdims=True) + EPS)
        return centred * inverse, inverse

    def norm_grad(grad, unit, inverse, gain):
        scaled = grad * gain
        return inverse * (
            scaled - jnp.mean(scaled, -1, keepdims=True) - unit * jnp.mean(scaled * unit, -1, keepdims=True)
        )

    def x_out():
        half = (slice(None), slice(None), lanes(c * 512, 512, 512))
        return remote(go.at[half], go_x.at[half], x_send.at[4], x_recv.at[4], x_peer)

    def x_out_core(cc):
        half = (slice(None), slice(None), lanes(cc * 512, 512, 512))
        return remote(go_x.at[half], go_x.at[half], x_send.at[9], x_recv.at[9], c_peer)

    def x_grad_context():
        return remote(ctx_x, gctx.at[own], x_send.at[10], x_recv.at[10], x_peer)

    def x_grad_context_wait():
        remote(gctx.at[other], gctx.at[other], x_send.at[10], x_recv.at[10], x_peer).wait_recv()

    stages = (x_peer, c_peer, y_peer)

    def v_copy(stage):
        return remote(vout.at[1 + stage], vin.at[stage], v_send.at[stage], v_recv.at[stage], stages[stage])

    def vz_copy(step):
        peer = (slot_of(lax.rem(z + step, DEPTH), y, c), t)
        return remote(vout.at[4], vin.at[3 + z], v_send.at[2 + step], v_recv.at[3 + z], peer)

    def early_rows(hop):
        if hop == 0:
            vout[1] = vout[0]
        else:
            v_copy(hop - 1).wait_recv()
            vout[1 + hop] = vout[hop] + vin[hop - 1]
        if hop < 3:
            v_copy(hop).start()
        else:
            for step in range(1, DEPTH):
                vz_copy(step).start()
            vin[3 + z] = vout[4]

    def late_turn(turn):
        dx, dy, dc = turn // 4, turn // 2 % 2, turn % 2
        xx, yy, cc = (1 - t if dx else t), (1 - y if dy else y), (1 - c if dc else c)
        return (slot_of(z, yy, cc), xx), xx * 4 + yy * 2 + cc

    def late_copy(turn):
        here = t * 4 + y * 2 + c
        return remote(late, late_in.at[here], l_send.at[turn], l_recv.at[here], late_turn(turn)[0])

    def late_wait(index):
        remote(late_in.at[index], late_in.at[index], l_send.at[0], l_recv.at[index], y_peer).wait_recv()

    def late_z(step):
        peer = (slot_of(lax.rem(z + step, DEPTH), y, c), t)
        return remote(late_sum, late_in.at[8 + z], l_send.at[7 + step], l_recv.at[8 + z], peer)

    barrier = pltpu.get_barrier_semaphore()
    z_peers = [(slot_of(lax.rem(z + step, DEPTH), y, c), t) for step in range(1, DEPTH)]
    everyone = [late_turn(turn)[0] for turn in range(1, 8)] + z_peers
    for device in everyone:
        pl.semaphore_signal(barrier, inc=1, device_id=device, device_id_type=MESH_ID)

    def prepare(held, stack):
        load = pltpu.make_async_copy(view, held, copy_sem.at[0])
        load.start()

        def first_norm(at, step):
            unit, inverse = norm(tokens[pl.ds(at, step), :])
            to = pl.ds(pl.multiple_of(t * rows + at, step), step)
            rows_one[to, :] = (unit * vecs[0:1, :] + vecs[1:2, :]).astype(bf)
            grad_rows[to, :] = cot[pl.ds(at, step), :].astype(bf)

        load.wait()
        lay_blocks(held, stack)

        def pair(left, right, count, left_high=False, right_high=False):
            first, second = stack[left : left + count, :], stack[right : right + count, :]
            first = pltpu.roll(first, HALF, 1) if left_high else first
            second = second if right_high else pltpu.roll(second, HALF, 1)
            lane = lax.broadcasted_iota(jnp.int32, (count, LANES), 1)
            return jnp.where(lane < HALF, first, second).astype(bf)

        n = gq.shape[1]
        gq[me] = pair(0, n, n)
        base = 2 * n
        wide = [pair(base + b * 64, base + b * 64 + 64, 64) for b in range(0, 8, 2)]
        go[z * 2 + y, :, lanes(c * 512, 512, 512)] = jnp.concatenate(wide, 1)
        pl.semaphore_wait(barrier, len(everyone))
        for k in (Q, O):
            own_sends_y(k)
            own_sends_z(k)
        by_rows(first_norm)
        x_rows(rows_one, 0).start()
        base += 512
        gi[me] = pair(base, 0, D, right_high=True)
        for r in range(2):
            for b in range(0, 16, 2):
                at = D + (r * 16 + b) * 64
                gd[me, r * 64 : r * 64 + 64, b * HALF : b * HALF + LANES] = pair(at, at + 64, 64, True, True)

    pl.run_scoped(
        prepare,
        pltpu.VMEM(view.shape, f32),
        pltpu.VMEM((view.shape[2] // 2 * BLOCK, LANES), f32),
    )
    x_rows(grad_rows, 1).start()
    z_arrival((Q, O), 1)
    y_arrival((Q, O), 0)
    z_arrival((Q, O), 2)
    for k in (I, W, V):
        own_sends_z(k)
    own_sends_y(I)
    y_arrival((Q, O), 1)

    def core_waits(kinds, zz):
        for k in kinds:
            for yy in (y, 1 - y):
                ag_wait(k, zz, yy, 1 - c)

    x_rows_wait(rows_one, 0)

    ends = []
    for p in range(ARTICLES):
        length = 0
        for a in range(ARTICLES):
            length = length + jnp.where(order[0, p] == a, lengths[0, a], 0)
        ends.append(length + ends[-1] if p else length)

    def allowed(first, count):
        ids = lax.broadcasted_iota(jnp.int32, (rows, 1), 0) + first
        start = jnp.zeros((rows, 1), jnp.int32)
        for end in ends:
            start = jnp.where(ids >= end, end, start)
        start = jnp.where(ids >= ends[-1], ids, start)
        keys = lax.broadcasted_iota(jnp.int32, (rows, count), 1)
        return (keys <= ids) & (keys >= start)

    scale = HD ** (-0.5)
    strip = 1024

    def assemble(h):
        for yy in range(2):
            even, odd = gq.at[slot_of(h, yy, 0)], gq.at[slot_of(h, yy, 1)]
            at = yy * 192
            wqkv[h, 0:768, at : at + 64] = even[:, 0:64]
            wqkv[h, 768:1024, at : at + 64] = even[0:256, 64:128]
            wqkv[h, 0:512, at + 64 : at + 128] = even[256:768, 64:128]
            wqkv[h, 512:1024, at + 64 : at + 128] = odd[0:512, 0:64]
            wqkv[h, 0:256, at + 128 : at + 192] = odd[512:768, 0:64]
            wqkv[h, 256:1024, at + 128 : at + 192] = odd[:, 64:128]

    def disassemble(h, value):
        for yy in range(2):
            even, odd = gq.at[slot_of(h, yy, 0)], gq.at[slot_of(h, yy, 1)]
            at = yy * 192
            even[:, 0:64] = value[0:768, at : at + 64]
            even[0:256, 64:128] = value[768:1024, at : at + 64]
            even[256:768, 64:128] = value[0:512, at + 64 : at + 128]
            odd[0:512, 0:64] = value[512:1024, at + 64 : at + 128]
            odd[512:768, 0:64] = value[0:256, at + 128 : at + 192]
            odd[:, 64:128] = value[256:1024, at + 128 : at + 192]

    qv = vecs[pl.ds(6 + t, 1), :]
    for h in range(DEPTH):
        none = jnp.zeros((1, HD), f32)
        qkv_bias[h] = jnp.concatenate([qv[:, h * 256 : h * 256 + 128], none, qv[:, h * 256 + 128 : h * 256 + 256]], 1)

    def head(h):
        core_waits((Q,), h)
        assemble(h)
        qkv[h] = (dot(rows_one[...], wqkv[h]) + qkv_bias[h]).astype(bf)
        for block in range(2):
            at, seen = slice(block * rows, (block + 1) * rows), (block + 1) * rows
            scores = dot_nt(qkv[h, at, 0:128], qkv[h, 0:seen, 128:256]) * scale
            scores = jnp.where(allowed(block * rows, seen), scores, NEG)
            expo = jnp.exp(scores - jnp.max(scores, -1, keepdims=True))
            low = (expo * (1.0 / jnp.sum(expo, -1, keepdims=True))).astype(bf)
            probs[h, at, 0:seen] = low
            ctx[at, lanes(h * HD, HD, HD)] = dot(low, qkv[h, 0:seen, 256:384]).astype(bf)

    head(near(0))
    y_arrival((Q, O), 2)
    z_arrival((Q, O), 3)
    y_arrival((Q, O), 3)
    own_sends_y(W)
    head(near(1))
    own_sends_y(V)
    head(near(2))
    z_arrival((I, W), 1)
    head(near(3))
    y_arrival((I, W), 0)
    for zz in range(DEPTH):
        core_waits((O,), zz)
    def w_out(ref):
        return ref[...].reshape(DEPTH * HD, D)
    far[0] = dot(ctx[other, :], w_out(go)).astype(bf)
    x_part(0).start()
    mixed[...] = tokens[...] + dot(ctx[own, :], w_out(go)) + vecs[4:5, :]
    v_forward(z, 1 - y)
    z_arrival((I, W), 2)
    x_part(0).wait_recv()
    def second_norm(at, step):
        value = mixed[pl.ds(at, step), :] + inx[0, pl.ds(at, step), :].astype(f32)
        mixed[pl.ds(at, step), :] = value
        unit, inverse = norm(value)
        to = pl.ds(pl.multiple_of(t * rows + at, step), step)
        rows_two[to, :] = (unit * vecs[2:3, :] + vecs[3:4, :]).astype(bf)
    x_rows_wait(grad_rows, 1)
    by_rows(second_norm)
    x_rows(rows_two, 2).start()
    macc[...] = jnp.zeros_like(macc)
    y_arrival((I, W), 1)
    nacc[...] = jnp.zeros_like(nacc)
    z_arrival((I, W), 3)
    vout[...] = jnp.zeros_like(vout)
    def ffn(half, zz):
        first = 4 * zz
        at = pl.ds(pl.multiple_of(lax.rem(t + half, 2) * rows, rows), rows)
        units = lanes(zz * 512, 512, 512)
        bias_row = vecs[pl.ds(8 + 2 * t + lax.div(zz, 2), 1), lanes(lax.rem(zz, 2) * 512, 512, 512)]

        def w_in(start, count):
            return jnp.concatenate([gi[first + j, start : start + count, :] for j in range(4)], 1)

        def w_down(start, count):
            return gd[pl.ds(first, 4), :, start : start + count].reshape(512, count)

        inner = dot(rows_two[at, :], w_in(0, D)) + bias_row
        square = inner * inner
        bent = jnp.tanh(GELU_A * inner * (1.0 + GELU_B * square))
        act[at, units] = (0.5 * inner * (1.0 + bent)).astype(bf)
        slope = 0.5 * (1.0 + bent) + 0.5 * inner * (1.0 - bent * bent) * (GELU_A * (1.0 + 3.0 * GELU_B * square))
        gin[at, units] = (dot_nt(grad_rows[at, :], w_down(0, D)) * slope).astype(bf)
        for nb in range(4):
            out = slice(nb * 256, nb * 256 + 256)
            nacc[at, out] += dot_nt(gin[at, units], w_in(nb * 256, 256))
            macc[at, out] += dot(act[at, units], w_down(nb * 256, 256))
    def ffn_grads(zz):
        first = 4 * zz
        units = lanes(zz * 512, 512, 512)
        for k in (I, W, V):
            for yy in range(2):
                drain(k, zz, yy)
        bias_sum[zz] = jnp.sum(gin[:, units].astype(f32), 0, keepdims=True)
        for nb in range(4):
            out = slice(nb * 256, nb * 256 + 256)
            part = dot(rows_t[out, :], gin[:, units]).astype(bf)
            for j in range(4):
                gi[first + j, out, :] = part[:, j * LANES : (j + 1) * LANES]
        for yy in (1 - y, y):
            rc_copy(I, zz, yy).start()
        act_t = act[:, units].T
        for nb in range(4):
            out = slice(nb * 256, nb * 256 + 256)
            part = dot(act_t, grad_rows[:, out]).astype(bf)
            gd[pl.ds(first, 4), :, out] = part.reshape(4, LANES, 256)
        for yy in (1 - y, y):
            rc_copy(W, zz, yy).start()
    def each(kinds, step, *args):
        for k in kinds:
            step(k, *args)
    def reduce_out():
        for yy in (1 - y, y):
            for s in (3, 2, 1, 0):
                rc_add(O, near(s), yy)
    def reduce_head(zz):
        for yy in (1 - y, y):
            rc_add(Q, zz, yy)
    def reduce_core(zz):
        for yy in (1 - y, y):
            for k in (I, W):
                rc_add(k, zz, yy)
    def v_step(s):
        for yy in (1 - y, y):
            z_step(V, s, yy)
    v_arrival(1)
    def v_merge(s):
        for yy in (1 - y, y):
            z_merge(V, s, yy)
    core_waits((I, W, V), z)
    ffn(0, z)
    core_waits((I, W, V), near(1))
    ffn(0, near(1))
    x_rows_wait(rows_two, 2)
    x_out().start()
    v_arrival(2)
    y_arrival((I, W), 2)
    rows_t[...] = rows_two[...].T
    def by_z(s, carry):
        @pl.when(s == 2)
        def _():
            v_arrival(3)
            y_arrival((I, W), 3)

        @pl.when(s >= 2)
        def _():
            core_waits((I, W, V), near(s))
            ffn(0, near(s))

        ffn(1, near(s))

        @pl.when(s == DEPTH - 1)
        def _():
            x_part(0).wait_send()
            far[0] = nacc[other, :].astype(bf)
            x_part(1).start()

        ffn_grads(near(s))

        @pl.when(s > 0)
        def _():
            reduce_core(near(s - 1))

        for before in (1, 2):

            @pl.when(s == before + 1)
            def _():
                v_step(before)

        return carry
    lax.fori_loop(0, DEPTH, by_z, 0)
    x_out().wait_recv()
    x_out_core(c).start()
    reduce_core(near(3))
    v_step(3)
    for zz in range(DEPTH):
        for side in range(2):
            row, start = 8 + 2 * side + zz // 2, zz % 2 * 512
            vout[0, row : row + 1, start : start + 512] = jnp.where(t == side, bias_sum[zz], 0.0)
    rows_t[...] = rows_one[...].T
    x_part(1).wait_recv()
    v_merge(1)
    def row_sum(row, value):
        vout[0, row : row + 1, :] += jnp.sum(value, 0, keepdims=True)
    def second_back(at, step):
        here = pl.ds(at, step)
        in_group = pl.ds(pl.multiple_of(t * rows + at, step), step)
        grad = nacc[in_group, :] + inx[0, here, :].astype(f32)
        unit, inverse = norm(mixed[here, :])
        back = cot[here, :] + norm_grad(grad, unit, inverse, vecs[2:3, :])
        input_grad[here, :] = back
        grad_attn[in_group, :] = back.astype(bf)
        row_sum(2, grad * unit)
        row_sum(3, grad)
        row_sum(4, back)
        row_sum(5, cot[here, :])
    by_rows(second_back)
    early_rows(0)
    x_out_core(1 - c).wait_recv()
    ctx_x[...] = dot_nt(grad_attn[own, :], w_out(go_x)).astype(bf)
    x_grad_context().start()
    gctx[own, :] = dot_nt(grad_attn[own, :], w_out(go)).astype(bf)
    each((I, W), ry_add, 1)
    v_merge(2)
    each((I, W), ry_add, 2)
    for zz in range(DEPTH):
        for yy in range(2):
            drain(O, zz, yy)
            drain(Q, zz, yy)
    def mixed_out(at, step):
        here = pl.ds(at, step)
        in_group = pl.ds(pl.multiple_of(t * rows + at, step), step)
        mixed[here, :] = mixed[here, :] + macc[in_group, :] + inx[1, here, :].astype(f32) + vecs[5:6, :]
    x_out().wait_send()
    x_grad_context_wait()
    far[1] = macc[other, :].astype(bf)
    x_rows(grad_attn, 3).start()
    def out_grads():
        x_rows_wait(grad_attn, 3)
        ctx_t = ctx[...].T
        for nb in range(4):
            at = slice(nb * 256, nb * 256 + 256)
            go[:, :, at] = dot(ctx_t, grad_attn[:, at]).astype(bf).reshape(8, 64, 256)
        for zz in range(DEPTH):
            for yy in range(2):
                rc_copy(O, zz, yy).start()
    def first_back(at, step):
        here = pl.ds(at, step)
        in_group = pl.ds(pl.multiple_of(t * rows + at, step), step)
        grad = nacc[in_group, :] + inx[0, here, :].astype(f32)
        unit, inverse = norm(tokens[here, :])
        input_grad[here, :] = input_grad[here, :] + norm_grad(grad, unit, inverse, vecs[0:1, :])
        row_sum(0, grad * unit)
        row_sum(1, grad)
    def finish_mixed():
        x_part(2).wait_recv()
        by_rows(mixed_out)
    def finish_input():
        x_part(3).wait_recv()
        by_rows(first_back)
    v_cross()
    late_rows = (0, 1, 6, 7)
    def late_start():
        for h in range(DEPTH):
            for row in range(2):
                total = jnp.where(t == row, qv_sum[h], 0.0)
                vout[0, 6 + row : 7 + row, h * 256 : h * 256 + 128] = total[:, 0:128]
                vout[0, 6 + row : 7 + row, h * 256 + 128 : h * 256 + 256] = total[:, 256:384]
        for at, row in enumerate(late_rows):
            for j in range(8):
                late[at * 8 + j : at * 8 + j + 1, :] = vout[0, row : row + 1, j * LANES : (j + 1) * LANES]
        late_in[t * 4 + y * 2 + c] = late[...]
        for turn in range(1, 8):
            late_copy(turn).start()
    def late_cross():
        for turn in range(1, 8):
            late_wait(late_turn(turn)[1])
        total = late_in[0]
        for index in range(1, 8):
            total = total + late_in[index]
        late_sum[...] = total
        late_in[8 + z] = total
        for step in range(1, DEPTH):
            late_z(step).start()
    def vec_finish():
        for step in range(1, DEPTH):
            zz = lax.rem(z + step, DEPTH)
            late_wait(8 + zz)
            remote(vin.at[3 + zz], vin.at[3 + zz], v_send.at[0], v_recv.at[3 + zz], y_peer).wait_recv()
        total = ((late_in[8] + late_in[9]) + late_in[10]) + late_in[11]
        early = ((vin[3] + vin[4]) + vin[5]) + vin[6]
        vec_grads[...] = early[0 : vec_grads.shape[0]]
        for at, row in enumerate(late_rows):
            for j in range(8):
                vec_grads[row : row + 1, j * LANES : (j + 1) * LANES] = total[at * 8 + j : at * 8 + j + 1, :]
    def head_back(h, turn):
        q0, q1 = qkv[h, 0:rows, 0:128], qkv[h, rows : 2 * rows, 0:128]
        grads = []
        for block in range(2):
            at, seen = slice(block * rows, (block + 1) * rows), (block + 1) * rows
            low = probs[h, at, 0:seen]
            given = gctx[at, lanes(h * HD, HD, HD)]
            prob = low.astype(f32)
            grad_probs = dot_nt(given, qkv[h, 0:seen, 256:384])
            delta = jnp.sum(prob * grad_probs, -1, keepdims=True)
            grad_scores = (prob * (grad_probs - delta)).astype(bf)
            grad_q = dot(grad_scores, qkv[h, 0:seen, 128:256]) * scale
            grad_k = dot_tn(grad_scores, q1 if block else q0) * scale
            grad_v = dot_tn(low, given)
            grads.append((grad_q, grad_k, grad_v))
        (gq0, gk0, gv0), (gq1, gk1, gv1) = grads
        top = jnp.concatenate([gq0, gk0 + gk1[0:rows], gv0 + gv1[0:rows]], 1).astype(bf)
        low_half = jnp.concatenate([gq1, gk1[rows:], gv1[rows:]], 1).astype(bf)
        qkv[h, 0:rows, :] = top
        qkv[h, rows : 2 * rows, :] = low_half
        total = jnp.sum(top.astype(f32), 0, keepdims=True) + jnp.sum(low_half.astype(f32), 0, keepdims=True)
        qv_sum[h] = total
        for half in (other, own):
            product = dot_nt(qkv[h, half, :], wqkv[h])
            if turn == 0:
                nacc[half, :] = product
            else:
                nacc[half, :] += product
            if turn == DEPTH - 1 and half is other:
                x_part(1).wait_send()
                far[0] = nacc[other, :].astype(bf)
                x_part(3).start()
        part = dot(rows_t[...], qkv[h]).astype(bf)
        disassemble(h, part)
        for yy in (1 - y, y):
            rc_copy(Q, h, yy).start()
    early_rows(1)
    head_back(near(3), 0)
    early_rows(2)
    head_back(near(2), 1)
    early_rows(3)
    x_part(2).start()
    reduce_head(near(3))
    each((I, W), ry_add, 3)
    each((I, W), ry_merge, 1)
    out_grads()
    reduce_head(near(2))
    head_back(near(1), 2)
    reduce_out()
    each((I, W), ry_merge, 2)
    head_back(z, 3)
    ry_add(Q, 3)
    finish_mixed()
    reduce_head(near(1))
    ry_add(Q, 2)
    ry_add(O, 3)
    ry_add(O, 2)
    ry_add(Q, 1)
    ry_merge(Q, 2)
    reduce_head(z)
    ry_merge(Q, 1)
    ry_add(O, 1)
    own_total(W)
    finish_input()
    late_start()
    own_total(I)
    ry_merge(O, 2)
    late_cross()
    own_total(Q)
    ry_merge(O, 1)
    vec_finish()
    z_total(V, y, total_of(V), y_landed(V, z))
    own_total(O)

    for stage in range(3):
        v_copy(stage).wait_send()
    for turn in range(1, 8):
        late_copy(turn).wait_send()
    for step in range(1, DEPTH):
        vz_copy(step).wait_send()
        late_z(step).wait_send()
    for index, ref in enumerate((rows_one, grad_rows, rows_two, grad_attn)):
        x_rows(ref, index).wait_send()
    for index in (2, 3):
        x_part(index).wait_send()
    x_out_core(c).wait_send()
    x_grad_context().wait_send()
    for k in range(4):
        for zz in range(DEPTH):
            for yy in range(2):
                rc_copy(k, zz, yy).wait_send()
            ry_copy(k, zz).wait_send()
        for s in range(1, DEPTH):
            rz_copy(k, s, y, True).wait_send()
    ry_copy(V, z).wait_send()
    for yy in range(2):
        for s in range(1, DEPTH):
            rz_copy(V, s, yy, True).wait_send()


def run_layer(tokens, cotangent, lengths, order, weights, vec_params):
    bf, f32 = jnp.bfloat16, jnp.float32
    rows = tokens.shape[0]
    group = 2 * rows
    owners = 16
    shapes = piece_shapes()
    view = jnp.transpose(weights, (1, 2, 0))
    there = pl.BlockSpec(memory_space=pl.ANY)
    vmem = pl.BlockSpec(memory_space=pltpu.VMEM)
    smem = pl.BlockSpec(memory_space=pltpu.SMEM)

    halved = shapes[:3] + ((HALF, D),)

    def many(count, kinds):
        return [pltpu.VMEM((count,) + s, bf) for s in kinds]

    full = pltpu.VMEM((group, D), bf)
    dma = pltpu.SemaphoreType.DMA
    return pl.pallas_call(
        layer_kernel,
        out_shape=[jax.ShapeDtypeStruct((rows, D), f32)] * 2
        + [jax.ShapeDtypeStruct(s, f32) for s in shapes]
        + [jax.ShapeDtypeStruct(vec_params.shape, f32)],
        in_specs=[smem, smem, there] + [vmem] * 3,
        out_specs=[vmem] * 7,
        scratch_shapes=[
            pltpu.VMEM((owners,) + shapes[0], bf),
            pltpu.VMEM((owners // 2, BLOCK, D), bf),
            pltpu.VMEM((owners,) + shapes[2], bf),
            pltpu.VMEM((owners,) + shapes[3], bf),
            pltpu.VMEM((DEPTH, D, 3 * HD), bf),
        ]
        + many(2 * DEPTH, shapes)
        + many(DEPTH, halved)
        + many(1, halved[3:])
        + many(DEPTH, halved)
        + many(2 * DEPTH, halved[3:])
        + [
            full,
            full,
            pltpu.VMEM((D, group), bf),
            full,
            full,
            pltpu.VMEM((DEPTH, group, group), bf),
            pltpu.VMEM((DEPTH, group, 3 * HD), bf),
            pltpu.VMEM((group, DEPTH * HD), bf),
            pltpu.VMEM((group, DEPTH * HD), bf),
            pltpu.VMEM((2, rows, D), bf),
            pltpu.VMEM((2, rows, D), bf),
            pltpu.VMEM((owners // 2, BLOCK, D), bf),
            pltpu.VMEM((rows, DEPTH * HD), bf),
            pltpu.VMEM((group, D), f32),
            pltpu.VMEM((group, D), f32),
            pltpu.VMEM((group, 2 * D), bf),
            pltpu.VMEM((group, 2 * D), bf),
            pltpu.VMEM((DEPTH, 1, 512), f32),
            pltpu.VMEM((DEPTH, 1, 3 * HD), f32),
            pltpu.VMEM((DEPTH, 1, 3 * HD), f32),
            pltpu.VMEM((7, 16, D), f32),
            pltpu.VMEM((5, 16, D), f32),
            pltpu.VMEM((32, LANES), f32),
            pltpu.VMEM((32, LANES), f32),
            pltpu.VMEM((12, 32, LANES), f32),
            dma((5, owners)),
            dma((5, DEPTH)),
            dma((5, 2 * DEPTH)),
            dma((5, 2, 2 * DEPTH)),
            dma((4, 2 * DEPTH)),
            dma((4, 2 * DEPTH)),
            dma((5, DEPTH)),
            dma((5, DEPTH)),
            dma((5, 2 * DEPTH)),
            dma((5, 2 * DEPTH)),
            dma((11,)),
            dma((11,)),
            dma((6,)),
            dma((7,)),
            dma((11,)),
            dma((12,)),
            dma((1,)),
        ],
        compiler_params=pltpu.CompilerParams(
            collective_id=0, has_side_effects=True, vmem_limit_bytes=VMEM_LIMIT
        ),
        name="layer",
    )(lengths, order, view, tokens, cotangent, vec_params)


def per_device(
    grp_count,
    tp_count,
    tokens,
    cotangent,
    lengths,
    order,
    weights,
    momentum,
    stat_left,
    stat_right,
    root_left,
    root_right,
    vec_params,
    vec_momentum,
    vec_second,
):
    fits = grp_count == 4 * DEPTH and tp_count == 2 and tokens.shape[0] == 256
    if not fits or lengths.shape[1] != ARTICLES:
        return per_device_general(
            tokens,
            cotangent,
            lengths,
            order,
            weights,
            momentum,
            stat_left,
            stat_right,
            root_left,
            root_right,
            vec_params,
            vec_momentum,
            vec_second,
        )
    token_total = tokens.shape[0] * tp_count * grp_count
    mixed, input_grad, *sums, vec_grads = run_layer(tokens, cotangent, lengths, order, weights, vec_params)
    blocks, vecs, results = update_blocks(
        sums,
        (weights, momentum, stat_left, stat_right, root_left, root_right),
        vec_grads,
        (vec_params, vec_momentum, vec_second),
        (mixed, input_grad),
        token_total,
    )
    return (*results, *blocks, *vecs)


def solution(mesh):
    placed = (
        P(("grp", "tp"), None),
        P(("grp", "tp"), None),
        P("grp", None),
        P("grp", None),
        P(("tp", "grp"), None, None),
        P(("tp", "grp"), None, None),
        P(("tp", "grp"), None, None),
        P(("tp", "grp"), None, None),
        P(("tp", "grp"), None, None),
        P(("tp", "grp"), None, None),
        P(),
        P(),
        P(),
    )
    return jax.shard_map(
        functools.partial(per_device, mesh.shape["grp"], mesh.shape["tp"]),
        mesh=mesh,
        in_specs=placed,
        out_specs=(
            P(("grp", "tp"), None),
            P(("grp", "tp"), None),
            P(("tp", "grp"), None, None),
            P(("tp", "grp"), None, None),
            P(("tp", "grp"), None, None),
            P(("tp", "grp"), None, None),
            P(("tp", "grp"), None, None),
            P(),
            P(),
            P(),
            P(),
        ),
        check_vma=False,
    )
```

```python
import functools

import jax
import jax.numpy as jnp
from jax import lax
from jax.experimental import pallas as pl
from jax.experimental.pallas import tpu as pltpu
from jax.sharding import PartitionSpec as P

D = 1024
HEADS = 8
HD = 128
FF = 4096
BLOCK = 64


EPS = 1e-05
NEG = -1e30
DECAY = 0.9
BETA = 0.9
RATE = 0.05
VEC_DECAY = 0.9
VEC_RATE = 0.2
VEC_EPS = 1e-08


def norm_rows(value, gain, shift):
    average = jnp.mean(value, -1, keepdims=True)
    centred = value - average
    inverse = lax.rsqrt(jnp.mean(centred * centred, -1, keepdims=True) + EPS)
    normed = centred * inverse
    return (normed * gain + shift, normed, inverse)


def norm_back(grad_out, normed, inverse, gain):
    scaled = grad_out * gain
    return inverse * (
        scaled
        - jnp.mean(scaled, -1, keepdims=True)
        - normed * jnp.mean(scaled * normed, -1, keepdims=True)
    )


def segment_ids(lengths_row, order_row, group_rows):
    article_count = lengths_row.shape[0]
    slots = jnp.arange(article_count, dtype=jnp.int32)
    picks = (order_row[:, None] == slots[None, :]).astype(jnp.int32)
    packed = jnp.sum(picks * lengths_row[None, :], 1)
    ends = jnp.cumsum(packed)
    spots = jnp.arange(group_rows, dtype=jnp.int32)
    return jnp.sum((spots[:, None] >= ends[None, :]).astype(jnp.int32), 1)


def allowed_mask(row_ids, row_segs, segments, key_ids, article_count):
    causal = key_ids[None, :] <= row_ids[:, None]
    same = segments[None, :] == row_segs[:, None]
    alone = (row_segs[:, None] < article_count) | (key_ids[None, :] == row_ids[:, None])
    return causal & same & alone


def from_columns(tiles, row_total, col_total):
    return (
        tiles.reshape(col_total // BLOCK, row_total // BLOCK, BLOCK, BLOCK)
        .transpose(1, 2, 0, 3)
        .reshape(row_total, col_total)
    )


def from_rows(tiles, row_total, col_total):
    return (
        tiles.reshape(row_total // BLOCK, col_total // BLOCK, BLOCK, BLOCK)
        .transpose(0, 2, 1, 3)
        .reshape(row_total, col_total)
    )


def to_columns(matrix):
    row_total, col_total = matrix.shape
    return (
        matrix.reshape(row_total // BLOCK, BLOCK, col_total // BLOCK, BLOCK)
        .transpose(2, 0, 1, 3)
        .reshape(-1, BLOCK, BLOCK)
    )


def to_rows(matrix):
    row_total, col_total = matrix.shape
    return (
        matrix.reshape(row_total // BLOCK, BLOCK, col_total // BLOCK, BLOCK)
        .transpose(0, 2, 1, 3)
        .reshape(-1, BLOCK, BLOCK)
    )


def per_device_general(
    tokens,
    cotangent,
    lengths,
    order,
    weights,
    momentum,
    stat_left,
    stat_right,
    root_left,
    root_right,
    vec_params,
    vec_momentum,
    vec_second,
):
    groups = lax.axis_size("grp")
    tp_size = lax.axis_size("tp")
    tp_rank = lax.axis_index("tp")
    tok_rows = tokens.shape[0]
    group_rows = tok_rows * tp_size
    article_count = lengths.shape[1]
    owners = groups * tp_size
    block_area = BLOCK * BLOCK * owners
    qkv_count = 3 * D * D // block_area
    out_count = D * D // block_area
    in_count = D * FF // block_area
    owned_blocks = weights.shape[0]
    heads_here = HEADS // tp_size
    qkv_cols = 3 * D // tp_size
    feat_here = D // tp_size
    ff_here = FF // tp_size
    qv_width = 2 * D // tp_size
    token_total = group_rows * groups
    gathered = lax.all_gather(weights.astype(jnp.bfloat16), "grp", axis=0, tiled=True)
    per_owner = gathered.reshape(groups, owned_blocks, BLOCK, BLOCK)
    marks = [0, qkv_count, qkv_count + out_count, qkv_count + out_count + in_count, owned_blocks]
    pieces = [
        per_owner[:, marks[index] : marks[index + 1]].reshape(-1, BLOCK, BLOCK)
        for index in range(4)
    ]
    w_qkv = from_columns(pieces[0], D, qkv_cols)
    w_out = from_rows(pieces[1], feat_here, D)
    w_in = from_columns(pieces[2], D, ff_here)
    w_down = from_rows(pieces[3], ff_here, D)
    w_qkv_heads = w_qkv.reshape(D, heads_here, 3, HD)
    w_out_heads = w_out.reshape(heads_here, HD, D)
    segments = segment_ids(lengths[0], order[0], group_rows)
    gain_one = vec_params[0]
    shift_one = vec_params[1]
    gain_two = vec_params[2]
    shift_two = vec_params[3]
    bias_out = vec_params[4]
    bias_down = vec_params[5]
    qv_here = lax.dynamic_slice_in_dim(
        vec_params[6:8].reshape(2 * D), tp_rank * qv_width, qv_width
    ).reshape(heads_here, 2, HD)
    bias_heads = jnp.stack(
        [qv_here[:, 0], jnp.zeros((heads_here, HD), jnp.float32), qv_here[:, 1]], 0
    )[:, :, None, :]
    bias_in = lax.dynamic_slice_in_dim(vec_params[8:].reshape(FF), tp_rank * ff_here, ff_here)
    normed_one, unit_one, inverse_one = norm_rows(tokens, gain_one, shift_one)
    rows_one = lax.all_gather(normed_one.astype(jnp.bfloat16), "tp", axis=0, tiled=True)
    projected = (
        jnp.einsum("rx,xhcd->chrd", rows_one, w_qkv_heads, preferred_element_type=jnp.float32)
        + bias_heads
    ).astype(jnp.bfloat16)
    queries = projected[0]
    keys_all = projected[1]
    values_all = projected[2]
    span = min(512, group_rows)
    starts = jnp.arange(group_rows // span, dtype=jnp.int32) * span
    key_ids = jnp.arange(group_rows, dtype=jnp.int32)
    score_scale = HD ** (-0.5)

    def masked_scores(first_row):
        row_ids = first_row + jnp.arange(span, dtype=jnp.int32)
        row_segs = lax.dynamic_slice_in_dim(segments, first_row, span, 0)
        allowed = allowed_mask(row_ids, row_segs, segments, key_ids, article_count)
        query_rows = lax.dynamic_slice_in_dim(queries, first_row, span, 1)
        scores = (
            jnp.einsum("hqd,hkd->hqk", query_rows, keys_all, preferred_element_type=jnp.float32)
            * score_scale
        )
        return (jnp.where(allowed[None], scores, NEG), query_rows)

    def attend(context_buf, first_row):
        scores, query_rows = masked_scores(first_row)
        row_max = jnp.max(scores, -1, keepdims=True)
        expo = jnp.exp(scores - row_max)
        expsum = jnp.sum(expo, -1, keepdims=True)
        probs_low = (expo / expsum).astype(jnp.bfloat16)
        context = jnp.einsum(
            "hqk,hkd->hqd", probs_low, values_all, preferred_element_type=jnp.float32
        ).astype(jnp.bfloat16)
        context_buf = lax.dynamic_update_slice_in_dim(context_buf, context, first_row, 1)
        return (context_buf, (row_max + jnp.log(expsum))[:, :, 0])

    context_low, log_norm = lax.scan(
        attend, jnp.zeros((heads_here, group_rows, HD), jnp.bfloat16), starts
    )
    attn_sum = lax.psum_scatter(
        jnp.einsum(
            "hrd,hde->re", context_low, w_out_heads, preferred_element_type=jnp.float32
        ).astype(jnp.bfloat16),
        "tp",
        scatter_dimension=0,
        tiled=True,
    ).astype(jnp.float32)
    hidden = tokens + attn_sum + bias_out
    normed_two, unit_two, inverse_two = norm_rows(hidden, gain_two, shift_two)
    rows_two = lax.all_gather(normed_two.astype(jnp.bfloat16), "tp", axis=0, tiled=True)
    inner = jnp.dot(rows_two, w_in, preferred_element_type=jnp.float32) + bias_in
    activ, gelu_pull = jax.vjp(jax.nn.gelu, inner)
    activ_low = activ.astype(jnp.bfloat16)
    mixed = (
        hidden
        + lax.psum_scatter(
            jnp.dot(activ_low, w_down, preferred_element_type=jnp.float32).astype(jnp.bfloat16),
            "tp",
            scatter_dimension=0,
            tiled=True,
        ).astype(jnp.float32)
        + bias_down
    )
    grad_low = cotangent.astype(jnp.bfloat16)
    grad_rows = lax.all_gather(grad_low, "tp", axis=0, tiled=True)
    g_down = jnp.einsum("rf,rd->fd", activ_low, grad_rows, preferred_element_type=jnp.float32)
    grad_activ = jnp.einsum("rd,fd->rf", grad_rows, w_down, preferred_element_type=jnp.float32)
    grad_inner = gelu_pull(grad_activ)[0].astype(jnp.bfloat16)
    g_in = jnp.einsum("rd,rf->df", rows_two, grad_inner, preferred_element_type=jnp.float32)
    g_bias_in = jnp.sum(grad_inner.astype(jnp.float32), 0)
    ffn_blocks = jnp.concatenate(
        [
            to_columns(g_in).reshape(groups, in_count, BLOCK, BLOCK),
            to_rows(g_down).reshape(groups, in_count, BLOCK, BLOCK),
        ],
        1,
    )
    grad_normed_two = lax.psum_scatter(
        jnp.einsum("rf,df->rd", grad_inner, w_in, preferred_element_type=jnp.float32).astype(
            jnp.bfloat16
        ),
        "tp",
        scatter_dimension=0,
        tiled=True,
    ).astype(jnp.float32)
    grad_hidden = cotangent + norm_back(grad_normed_two, unit_two, inverse_two, gain_two)
    grad_attn_low = grad_hidden.astype(jnp.bfloat16)
    grad_attn_rows = lax.all_gather(grad_attn_low, "tp", axis=0, tiled=True)
    g_out = jnp.einsum(
        "hrd,re->hde", context_low, grad_attn_rows, preferred_element_type=jnp.float32
    ).reshape(feat_here, D)
    grad_context = jnp.einsum(
        "re,hde->hrd", grad_attn_rows, w_out_heads, preferred_element_type=jnp.float32
    ).astype(jnp.bfloat16)
    zero_heads = jnp.zeros((heads_here, group_rows, HD), jnp.float32)

    def attend_back(carry, inputs):
        grad_queries, grad_keys, grad_values = carry
        first_row, log_block = inputs
        scores, query_rows = masked_scores(first_row)
        probs = jnp.exp(scores - log_block[:, :, None])
        grad_ctx_rows = lax.dynamic_slice_in_dim(grad_context, first_row, span, 1)
        grad_probs = jnp.einsum(
            "hqd,hkd->hqk", grad_ctx_rows, values_all, preferred_element_type=jnp.float32
        )
        delta = jnp.sum(probs * grad_probs, -1, keepdims=True)
        grad_scores = (probs * (grad_probs - delta)).astype(jnp.bfloat16)
        query_part = (
            jnp.einsum("hqk,hkd->hqd", grad_scores, keys_all, preferred_element_type=jnp.float32)
            * score_scale
        )
        grad_queries = lax.dynamic_update_slice_in_dim(grad_queries, query_part, first_row, 1)
        grad_keys = (
            grad_keys
            + jnp.einsum(
                "hqk,hqd->hkd", grad_scores, query_rows, preferred_element_type=jnp.float32
            )
            * score_scale
        )
        grad_values = grad_values + jnp.einsum(
            "hqk,hqd->hkd",
            probs.astype(jnp.bfloat16),
            grad_ctx_rows,
            preferred_element_type=jnp.float32,
        )
        return ((grad_queries, grad_keys, grad_values), None)

    (grad_queries, grad_keys, grad_values), unused = lax.scan(
        attend_back, (zero_heads, zero_heads, zero_heads), (starts, log_norm)
    )
    grad_proj = jnp.stack([grad_queries, grad_keys, grad_values], 0).astype(jnp.bfloat16)
    proj_sums = jnp.sum(grad_proj.astype(jnp.float32), 2)
    g_bias_qv = jnp.stack([proj_sums[0], proj_sums[2]], 1).reshape(qv_width)
    g_qkv = jnp.einsum(
        "rx,chrd->xhcd", rows_one, grad_proj, preferred_element_type=jnp.float32
    ).reshape(D, qkv_cols)
    grad_normed_one = lax.psum_scatter(
        jnp.einsum(
            "chrd,xhcd->rx", grad_proj, w_qkv_heads, preferred_element_type=jnp.float32
        ).astype(jnp.bfloat16),
        "tp",
        scatter_dimension=0,
        tiled=True,
    ).astype(jnp.float32)
    input_grad = grad_hidden + norm_back(grad_normed_one, unit_one, inverse_one, gain_one)
    local_rows = jnp.stack(
        [
            jnp.sum(grad_normed_one * unit_one, 0),
            jnp.sum(grad_normed_one, 0),
            jnp.sum(grad_normed_two * unit_two, 0),
            jnp.sum(grad_normed_two, 0),
            jnp.sum(grad_hidden, 0),
            jnp.sum(cotangent, 0),
        ]
    )
    qv_rows = lax.dynamic_update_slice(
        jnp.zeros((2 * D,), jnp.float32), g_bias_qv, (tp_rank * qv_width,)
    ).reshape(2, D)
    in_rows = lax.dynamic_update_slice(
        jnp.zeros((FF,), jnp.float32), g_bias_in, (tp_rank * ff_here,)
    ).reshape(FF // D, D)
    vec_grads = lax.psum(jnp.concatenate([local_rows, qv_rows, in_rows], 0), ("grp", "tp"))
    attn_blocks = jnp.concatenate(
        [
            to_columns(g_qkv).reshape(groups, qkv_count, BLOCK, BLOCK),
            to_rows(g_out).reshape(groups, out_count, BLOCK, BLOCK),
        ],
        1,
    )
    every_block = jnp.concatenate([attn_blocks, ffn_blocks], 1).reshape(-1, BLOCK, BLOCK)
    weight_grads = lax.psum_scatter(
        every_block.astype(jnp.bfloat16), "grp", scatter_dimension=0, tiled=True
    ).astype(jnp.float32)
    scaled = weight_grads * token_total ** (-0.5)
    stat_left_new = DECAY * stat_left + (1.0 - DECAY) * jnp.einsum(
        "nij,nkj->nik", scaled, scaled, precision=lax.Precision.HIGHEST
    )
    stat_right_new = DECAY * stat_right + (1.0 - DECAY) * jnp.einsum(
        "nji,njk->nik", scaled, scaled, precision=lax.Precision.HIGHEST
    )
    shaped = jnp.einsum("nij,njk->nik", root_left, scaled, precision=lax.Precision.HIGHEST)
    shaped = jnp.einsum("nij,njk->nik", shaped, root_right, precision=lax.Precision.HIGHEST)
    momentum_new = BETA * momentum + shaped
    weights_new = weights - RATE * momentum_new
    vec_scaled = vec_grads * token_total ** (-0.5)
    vec_second_new = VEC_DECAY * vec_second + (1.0 - VEC_DECAY) * vec_scaled * vec_scaled
    vec_momentum_new = BETA * vec_momentum + vec_scaled * lax.rsqrt(vec_second_new + VEC_EPS)
    vec_new = vec_params - VEC_RATE * vec_momentum_new
    return (
        mixed,
        input_grad,
        weight_grads,
        stat_left_new,
        stat_right_new,
        momentum_new,
        weights_new,
        vec_grads,
        vec_second_new,
        vec_momentum_new,
        vec_new,
    )


MESH_ID = pl.DeviceIdType.MESH
LANES = 128
HALF = 64
VMEM_LIMIT = 62 * 2**20
ARTICLES = 4
GELU_A = (2.0 / 3.141592653589793) ** 0.5
GELU_B = 0.044715


def remote(src, dst, send_sem, recv_sem, device):
    return pltpu.make_async_remote_copy(
        src_ref=src,
        dst_ref=dst,
        send_sem=send_sem,
        recv_sem=recv_sem,
        device_id=device,
        device_id_type=MESH_ID,
    )


def place():
    grp = lax.axis_index("grp")
    return lax.div(grp, 4), lax.rem(lax.div(grp, 2), 2), lax.rem(grp, 2), lax.axis_index("tp")


def slot_of(z, y, c):
    return z * 4 + y * 2 + c


def lay_blocks(view_ref, stack):
    half = view_ref.shape[2] // 2

    def row(i, carry):
        tile = view_ref[i].T
        stack[pl.ds(i, half, stride=BLOCK), :] = jnp.concatenate([tile[:half], tile[half:]], 1)
        return carry

    lax.fori_loop(0, BLOCK, row, 0, unroll=8)


def piece_shapes():
    return ((768, LANES), (64, 512), (1024, LANES), (LANES, 1024))


def both_halves(pair):
    low = lax.broadcasted_iota(jnp.int32, pair.shape, 1) < HALF
    turned = pltpu.roll(pair, HALF, 1)
    return jnp.where(low, pair, turned), jnp.where(low, turned, pair)


def update_kernel(
    scale,
    sum_q,
    sum_o,
    sum_i,
    sum_d,
    root_l,
    root_r,
    vec_g,
    vecs,
    vec_m,
    vec_s,
    mixed,
    input_grad,
    w,
    m,
    sl,
    sr,
    out_g,
    out_sl,
    out_sr,
    out_m,
    out_w,
    out_vg,
    out_vs,
    out_vm,
    out_v,
    out_mixed,
    out_input_grad,
    grads,
    first,
    second,
    held_l,
    held_r,
    held_w,
    held_m,
    held_sl,
    held_sr,
    sems,
    block_sems,
):
    count = w.shape[2]
    step_rows = out_w.shape[0]
    bf, f32 = jnp.bfloat16, jnp.float32

    def loads(k):
        part = pl.ds(16 * k, 16)
        return [
            pltpu.make_async_copy(root.at[part], held.at[part], sems.at[k, side])
            for side, (root, held) in enumerate(((root_l, held_l), (root_r, held_r)))
        ]

    def block_loads(k):
        part = pl.ds(k * step_rows, step_rows)
        pairs = ((w, held_w), (m, held_m), (sl, held_sl), (sr, held_sr))
        return [pltpu.make_async_copy(a.at[part], b.at[part], block_sems.at[k, n]) for n, (a, b) in enumerate(pairs)]

    out_mixed[...] = mixed[...]
    out_input_grad[...] = input_grad[...]

    @pl.when(pl.program_id(0) == 0)
    def _():
        for k in range(4):
            for load in loads(k):
                load.start()
        for k in range(BLOCK // step_rows):
            for load in block_loads(k):
                load.start()
        total = vec_g[...]
        out_vg[...] = total
        scaled = total * scale
        fresh = VEC_DECAY * vec_s[...] + (1.0 - VEC_DECAY) * scaled * scaled
        out_vs[...] = fresh
        momentum = BETA * vec_m[...] + scaled * lax.rsqrt(fresh + VEC_EPS)
        out_vm[...] = momentum
        out_v[...] = vecs[...] - VEC_RATE * momentum
        rows = sum_q.shape[0]
        grads[0:rows, 0:HALF] = sum_q[:, 0:HALF]
        grads[rows : 2 * rows, 0:HALF] = sum_q[:, HALF:LANES]
        base = 2 * rows
        for b in range(8):
            grads[base + b * 64 : base + b * 64 + 64, 0:HALF] = sum_o[:, b * HALF : (b + 1) * HALF]
        base += 512
        grads[base : base + D, 0:HALF] = sum_i[:, 0:HALF]
        grads[0:D, HALF:LANES] = sum_i[:, HALF:LANES]
        for r in range(2):
            for b in range(16):
                at = D + (r * 16 + b) * 64
                grads[at : at + 64, HALF:LANES] = sum_d[r * 64 : r * 64 + 64, b * HALF : (b + 1) * HALF]

        def row(i, carry):
            both = jnp.concatenate([held_l[i], held_r[i]], 0)
            second[pl.ds(i, count, stride=BLOCK), :] = both.T
            return carry

        for k in range(4):
            for load in loads(k):
                load.wait()
            lax.fori_loop(16 * k, 16 * k + 16, row, 0, unroll=8)
        row_id = lax.broadcasted_iota(jnp.int32, (256, 256), 0)
        col_id = lax.broadcasted_iota(jnp.int32, (256, 256), 1)
        mask = lax.shift_right_logical(row_id, 6) == lax.shift_right_logical(col_id, 6)
        low = lax.broadcasted_iota(jnp.int32, (256, LANES), 1) < HALF

        def spread(v):
            return jnp.where(mask, jnp.concatenate([v, v], 1), 0.0).astype(bf)

        def eight(k, carry):
            at = pl.ds(pl.multiple_of(k * 256, 256), 256)
            for side, grad in enumerate(both_halves(grads[at, :])):
                to = pl.ds(pl.multiple_of(k * 256 + side * (count // 2 * BLOCK), 256), 256)
                left, right = both_halves(second[to, :])
                s32 = grad * scale
                s = s32.astype(bf)
                outer = lax.dot_general(s[:, 0:HALF], s[:, 0:HALF], (((1,), (1,)), ((), ())), preferred_element_type=f32)
                kept = jnp.where(mask, outer, 0.0)
                kept = kept[:, :LANES] + kept[:, LANES:]
                outer = kept + pltpu.roll(kept, HALF, 1)
                inner = lax.dot_general(spread(s32), s, (((0,), (0,)), ((), ())), preferred_element_type=f32)
                shaped = jnp.dot(spread(left), s, preferred_element_type=f32)
                shaped = jnp.dot(spread(shaped), right.astype(bf), preferred_element_type=f32)
                first[to, :] = jnp.where(low, grad, outer)
                second[to, :] = jnp.where(low, inner, shaped)
            return carry

        lax.fori_loop(0, count // 8, eight, 0, unroll=4)

    i0 = pl.program_id(0) * step_rows
    for load in block_loads(pl.program_id(0)):
        load.wait()
    unit = lax.broadcasted_iota(jnp.int32, (LANES, LANES), 0) == lax.broadcasted_iota(jnp.int32, (LANES, LANES), 1)
    unit = unit.astype(f32).astype(bf)

    def turned(tile):
        high = tile.astype(bf)
        rest = (tile - high.astype(f32)).astype(bf)
        over = (((1,), (1,)), ((), ()))
        return lax.dot_general(unit, high, over, preferred_element_type=f32) + lax.dot_general(
            unit, rest, over, preferred_element_type=f32
        )


    def rows_out(ii, carry):
        i = i0 + ii
        at = pl.ds(i, count, stride=BLOCK)
        one = first[at, :].T
        two = turned(second[at, :])
        out_g[ii] = one[0:HALF]
        out_sl[ii] = DECAY * held_sl[i] + (1.0 - DECAY) * one[HALF:LANES]
        out_sr[ii] = DECAY * held_sr[i] + (1.0 - DECAY) * two[0:HALF]
        fresh = BETA * held_m[i] + two[HALF:LANES]
        out_m[ii] = fresh
        out_w[ii] = held_w[i] - RATE * fresh
        return carry

    lax.fori_loop(0, step_rows, rows_out, 0, unroll=True)


def update_blocks(sums, blocks, vec_grads, vecs, results, token_total):
    views = [jnp.transpose(a, (1, 2, 0)) for a in blocks]
    count = blocks[0].shape[0]
    rows = 8
    whole = pl.BlockSpec(memory_space=pltpu.VMEM)
    steps = BLOCK // rows
    some = pl.BlockSpec((results[0].shape[0] // steps, results[0].shape[1]), lambda i: (i, 0))
    there = pl.BlockSpec(memory_space=pl.ANY)
    part = pl.BlockSpec((rows, BLOCK, count), lambda i: (i, 0, 0))
    vec = jax.ShapeDtypeStruct(vec_grads.shape, jnp.float32)
    outs = pl.pallas_call(
        functools.partial(update_kernel, token_total ** (-0.5)),
        grid=(steps,),
        out_shape=[jax.ShapeDtypeStruct((BLOCK, BLOCK, count), jnp.float32)] * 5
        + [vec] * 4
        + [jax.ShapeDtypeStruct(a.shape, a.dtype) for a in results],
        in_specs=[whole] * 4 + [there] * 2 + [whole] * 4 + [some] * 2 + [there] * 4,
        out_specs=[part] * 5 + [whole] * 4 + [some] * 2,
        scratch_shapes=[
            pltpu.VMEM((count // 2 * BLOCK, LANES), jnp.float32),
            pltpu.VMEM((count * BLOCK, LANES), jnp.float32),
            pltpu.VMEM((count * BLOCK, LANES), jnp.float32),
            *[pltpu.VMEM((BLOCK, BLOCK, count), jnp.float32)] * 6,
            pltpu.SemaphoreType.DMA((4, 2)),
            pltpu.SemaphoreType.DMA((BLOCK // rows, 4)),
        ],
        compiler_params=pltpu.CompilerParams(vmem_limit_bytes=VMEM_LIMIT),
        name="update_blocks",
    )(*sums, *views[4:], vec_grads, *vecs, *results, *views[:4])
    return [jnp.transpose(a, (2, 0, 1)) for a in outs[:5]], outs[5:9], outs[9:]


DEPTH = 4


def layer_kernel(
    lengths,
    order,
    view,
    tokens,
    cot,
    vecs,
    mixed,
    input_grad,
    sum_q,
    sum_o,
    sum_i,
    sum_d,
    vec_grads,
    gq,
    go,
    gi,
    gd,
    wqkv,
    cq,
    co,
    ci,
    cd,
    yq,
    yo,
    yi,
    yd,
    yv,
    zq,
    zo,
    zi,
    zd,
    zv,
    rows_one,
    rows_two,
    rows_t,
    grad_rows,
    grad_attn,
    probs,
    qkv,
    ctx,
    gctx,
    far,
    inx,
    go_x,
    ctx_x,
    macc,
    nacc,
    act,
    gin,
    bias_sum,
    qkv_bias,
    qv_sum,
    vin,
    vout,
    late,
    late_sum,
    late_in,
    recv,
    send_y,
    send_c,
    send_z,
    rc_recv,
    rc_send,
    ry_recv,
    ry_send,
    rz_recv,
    rz_send,
    x_send,
    x_recv,
    v_send,
    v_recv,
    l_send,
    l_recv,
    copy_sem,
):
    bf, f32 = jnp.bfloat16, jnp.float32
    z, y, c, t = place()
    me = slot_of(z, y, c)
    x_peer = (me, 1 - t)
    y_peer = (slot_of(z, 1 - y, c), t)
    c_peer = (slot_of(z, y, 1 - c), t)
    rows = tokens.shape[0]
    own = pl.ds(pl.multiple_of(t * rows, rows), rows)
    other = pl.ds(pl.multiple_of((1 - t) * rows, rows), rows)

    def lanes(start, size, unit):
        return pl.ds(pl.multiple_of(start, unit), size)

    gathered, core_in = (gq, go, gi, gd), (cq, co, ci, cd)
    y_in, z_in = (yq, yo, yi, yd, yv), (zq, zo, zi, zd, zv)
    sums = (sum_q, sum_o, sum_i, sum_d)
    Q, O, I, W, V = range(5)

    def dot(a, b):
        return jnp.dot(a, b, preferred_element_type=f32)

    def dot_nt(a, b):
        return lax.dot_general(a, b, (((1,), (1,)), ((), ())), preferred_element_type=f32)

    def dot_tn(a, b):
        return lax.dot_general(a, b, (((0,), (0,)), ((), ())), preferred_element_type=f32)

    def piece(k, zz, yy, cc):
        if k == O:
            return go.at[zz * 2 + yy, :, pl.ds(pl.multiple_of(cc * 512, 512), 512)]
        return gathered[k].at[slot_of(zz, yy, cc)]

    def near(s):
        return lax.rem(z + (1 - 2 * lax.div(z, 2)) * s + DEPTH, DEPTH)

    def ag_piece(k, zz, yy, cc):
        if k == W:
            return gd.at[slot_of(zz, yy, cc), 0:HALF]
        if k == V:
            return gd.at[slot_of(zz, yy, cc), HALF:LANES]
        return piece(k, zz, yy, cc)

    def ag_copy(k, zz, yy, way):
        src = ag_piece(k, zz, yy, c)
        sem = recv.at[k, slot_of(zz, yy, c)]
        if way == "up":
            return remote(src, src, send_z.at[k, 0, yy * DEPTH + zz], sem, (slot_of(z + 1, y, c), t))
        if way == "down":
            return remote(src, src, send_z.at[k, 1, yy * DEPTH + zz], sem, (slot_of(z - 1, y, c), t))
        if way == "y":
            return remote(src, src, send_y.at[k, zz], sem, y_peer)
        return remote(src, src, send_c.at[k, yy * DEPTH + zz], sem, c_peer)

    def ag_wait(k, zz, yy, cc):
        ref = ag_piece(k, zz, yy, cc)
        remote(ref, ref, send_y.at[k, 0], recv.at[k, slot_of(zz, yy, cc)], y_peer).wait_recv()

    def own_sends_z(k):
        @pl.when(z < DEPTH - 1)
        def _():
            ag_copy(k, z, y, "up").start()

        @pl.when(z > 0)
        def _():
            ag_copy(k, z, y, "down").start()

        ag_copy(k, z, y, "core").start()

    def own_sends_y(k):
        ag_copy(k, z, y, "y").start()

    def z_arrival(kinds, dist):
        @pl.when(z >= dist)
        def _():
            for k in kinds:
                ag_wait(k, z - dist, y, c)

                @pl.when(z < DEPTH - 1)
                def _():
                    ag_copy(k, z - dist, y, "up").start()

                ag_copy(k, z - dist, y, "y").start()
                ag_copy(k, z - dist, y, "core").start()

        @pl.when(z + dist < DEPTH)
        def _():
            for k in kinds:
                ag_wait(k, z + dist, y, c)

                @pl.when(z > 0)
                def _():
                    ag_copy(k, z + dist, y, "down").start()

                ag_copy(k, z + dist, y, "y").start()
                ag_copy(k, z + dist, y, "core").start()

    def y_arrival(kinds, dist):
        def one(zz):
            for k in kinds:
                ag_wait(k, zz, 1 - y, c)
                ag_copy(k, zz, 1 - y, "core").start()

        if dist == 0:
            one(z)
            return

        @pl.when(z >= dist)
        def _():
            one(z - dist)

        @pl.when(z + dist < DEPTH)
        def _():
            one(z + dist)

    def v_forward(zz, yy):
        ag_wait(V, zz, yy, c)

        @pl.when((zz <= z) & (z < DEPTH - 1))
        def _():
            ag_copy(V, zz, yy, "up").start()

        @pl.when((zz >= z) & (z > 0))
        def _():
            ag_copy(V, zz, yy, "down").start()

        ag_copy(V, zz, yy, "core").start()

    def v_arrival(dist):
        for yy in (y, 1 - y):

            @pl.when(z >= dist)
            def _():
                v_forward(z - dist, yy)

            @pl.when(z + dist < DEPTH)
            def _():
                v_forward(z + dist, yy)

    def drain(k, zz, yy):
        ag_copy(k, zz, yy, "core").wait_send()
        if k == V:

            @pl.when((yy == y) & (zz == z))
            def _():
                ag_copy(k, zz, yy, "y").wait_send()

            @pl.when((zz <= z) & (z < DEPTH - 1))
            def _():
                ag_copy(k, zz, yy, "up").wait_send()

            @pl.when((zz >= z) & (z > 0))
            def _():
                ag_copy(k, zz, yy, "down").wait_send()

            return

        @pl.when(yy == y)
        def _():
            ag_copy(k, zz, y, "y").wait_send()

            @pl.when((zz <= z) & (z < DEPTH - 1))
            def _():
                ag_copy(k, zz, y, "up").wait_send()

            @pl.when((zz >= z) & (z > 0))
            def _():
                ag_copy(k, zz, y, "down").wait_send()

    def add(dst, *terms):
        count, width = dst.shape
        step = min(count, 256 * LANES // width)

        def body(i, carry):
            at = pl.ds(pl.multiple_of(i * step, 16), step)
            if len(terms) == 2 and dst.dtype == bf:
                dst[at, :] = terms[0][at, :] + terms[1][at, :]
                return carry
            total = terms[0][at, :].astype(f32)
            for term in terms[1:]:
                total = total + term[at, :].astype(f32)
            dst[at, :] = total.astype(dst.dtype)
            return carry

        lax.fori_loop(0, count // step, body, 0, unroll=2)

    side = lax.div(z, 2)
    end_z, inner_z = 3 * side, 1 + side
    is_end = z == end_z

    def rc_copy(k, zz, yy):
        at = zz * 2 + yy
        return remote(piece(k, zz, yy, 1 - c), core_in[k].at[at], rc_send.at[k, at], rc_recv.at[k, at], c_peer)

    def ry_copy(k, zz):
        if k == V:
            return remote(ag_piece(V, z, 1 - y, c), y_in[V].at[0], ry_send.at[V, 0], ry_recv.at[V, 0], y_peer)
        return remote(ag_piece(k, zz, 1 - y, c), y_in[k].at[zz], ry_send.at[k, zz], ry_recv.at[k, zz], y_peer)

    def z_slot(k, slot, yy):
        return z_in[k].at[slot * 2 + yy if k == V else slot]

    def z_sem(slot, yy):
        return slot * 2 + yy

    def rz_copy(k, s, yy, from_end):
        slot = s - 1 if from_end else {3: 0, 2: 1, 1: 3}[s]
        to = inner_z if from_end else {3: end_z, 2: 3 - end_z, 1: 3 - inner_z}[s]
        sent, landed = rz_send.at[k, (s - 1) * 2 + yy], rz_recv.at[k, z_sem(slot, yy)]
        return remote(ag_piece(k, near(s), yy, c), z_slot(k, slot, yy), sent, landed, (slot_of(to, y, c), t))

    def z_landed(k, slot, yy):
        ref = z_slot(k, slot, yy)
        remote(ref, ref, rz_send.at[k, 0], rz_recv.at[k, z_sem(slot, yy)], y_peer).wait_recv()
        return ref

    def y_landed(k, zz):
        ref = y_in[k].at[0 if k == V else zz]
        remote(ref, ref, ry_send.at[k, 0], ry_recv.at[k, 0 if k == V else zz], y_peer).wait_recv()
        return ref

    def rc_add(k, zz, yy):
        at = zz * 2 + yy
        remote(core_in[k].at[at], core_in[k].at[at], rc_send.at[k, 0], rc_recv.at[k, at], c_peer).wait_recv()
        mine = piece(k, zz, yy, c)
        add(mine, mine, core_in[k].at[at])

        @pl.when(yy != y)
        def _():
            ry_copy(k, zz).start()

    def z_step(k, s, yy, *terms):
        mine = ag_piece(k, near(s), yy, c)
        if terms:
            add(mine, mine, *terms)

        @pl.when(is_end)
        def _():
            rz_copy(k, s, yy, True).start()

        if s == 3:

            @pl.when(jnp.logical_not(is_end))
            def _():
                rz_copy(k, s, yy, False).start()

    def z_merge(k, s, yy):
        @pl.when(jnp.logical_not(is_end))
        def _():
            mine = ag_piece(k, near(s), yy, c)
            add(mine, mine, z_landed(k, s, yy))
            rz_copy(k, s, yy, False).start()

    def ry_add(k, s):
        z_step(k, s, y, y_landed(k, near(s)))

    def ry_merge(k, s):
        z_merge(k, s, y)

    def total_of(k):
        return sum_d.at[(k - W) * HALF : (k - W + 1) * HALF] if k >= W else sums[k]

    def z_total(k, yy, dst, *terms):
        mine = ag_piece(k, z, yy, c)
        first = z_landed(k, 0, yy)

        @pl.when(is_end)
        def _():
            add(dst, mine, first, z_landed(k, 1, yy), *terms)

        @pl.when(jnp.logical_not(is_end))
        def _():
            add(dst, mine, first, z_landed(k, 3, yy), *terms)

    def own_total(k):
        z_total(k, y, total_of(k), y_landed(k, z))

    def v_cross():
        mine = ag_piece(V, z, 1 - y, c)
        z_total(V, 1 - y, mine)
        ry_copy(V, z).start()

    def x_rows(ref, index):
        return remote(ref.at[own], ref.at[own], x_send.at[index], x_recv.at[index], x_peer)

    def x_rows_wait(ref, index):
        remote(ref.at[other], ref.at[other], x_send.at[index], x_recv.at[index], x_peer).wait_recv()

    def x_part(index):
        slot = 1 if index == 2 else 0
        return remote(far.at[slot], inx.at[slot], x_send.at[5 + index], x_recv.at[5 + index], x_peer)

    def by_rows(body, step=64):
        def run(i, carry):
            body(pl.multiple_of(i * step, step), step)
            return carry

        lax.fori_loop(0, rows // step, run, 0)

    def norm(value):
        average = jnp.mean(value, -1, keepdims=True)
        centred = value - average
        inverse = lax.rsqrt(jnp.mean(centred * centred, -1, keepdims=True) + EPS)
        return centred * inverse, inverse

    def norm_grad(grad, unit, inverse, gain):
        scaled = grad * gain
        return inverse * (
            scaled - jnp.mean(scaled, -1, keepdims=True) - unit * jnp.mean(scaled * unit, -1, keepdims=True)
        )

    def x_out():
        half = (slice(None), slice(None), lanes(c * 512, 512, 512))
        return remote(go.at[half], go_x.at[half], x_send.at[4], x_recv.at[4], x_peer)

    def x_out_core(cc):
        half = (slice(None), slice(None), lanes(cc * 512, 512, 512))
        return remote(go_x.at[half], go_x.at[half], x_send.at[9], x_recv.at[9], c_peer)

    def x_grad_context():
        return remote(ctx_x, gctx.at[own], x_send.at[10], x_recv.at[10], x_peer)

    def x_grad_context_wait():
        remote(gctx.at[other], gctx.at[other], x_send.at[10], x_recv.at[10], x_peer).wait_recv()

    stages = (x_peer, c_peer, y_peer)

    def v_copy(stage):
        return remote(vout.at[1 + stage], vin.at[stage], v_send.at[stage], v_recv.at[stage], stages[stage])

    def vz_copy(step):
        peer = (slot_of(lax.rem(z + step, DEPTH), y, c), t)
        return remote(vout.at[4], vin.at[3 + z], v_send.at[2 + step], v_recv.at[3 + z], peer)

    def early_rows(hop):
        if hop == 0:
            vout[1] = vout[0]
        else:
            v_copy(hop - 1).wait_recv()
            vout[1 + hop] = vout[hop] + vin[hop - 1]
        if hop < 3:
            v_copy(hop).start()
        else:
            for step in range(1, DEPTH):
                vz_copy(step).start()
            vin[3 + z] = vout[4]

    def late_turn(turn):
        dx, dy, dc = turn // 4, turn // 2 % 2, turn % 2
        xx, yy, cc = (1 - t if dx else t), (1 - y if dy else y), (1 - c if dc else c)
        return (slot_of(z, yy, cc), xx), xx * 4 + yy * 2 + cc

    def late_copy(turn):
        here = t * 4 + y * 2 + c
        return remote(late, late_in.at[here], l_send.at[turn], l_recv.at[here], late_turn(turn)[0])

    def late_wait(index):
        remote(late_in.at[index], late_in.at[index], l_send.at[0], l_recv.at[index], y_peer).wait_recv()

    def late_z(step):
        peer = (slot_of(lax.rem(z + step, DEPTH), y, c), t)
        return remote(late_sum, late_in.at[8 + z], l_send.at[7 + step], l_recv.at[8 + z], peer)

    barrier = pltpu.get_barrier_semaphore()
    z_peers = [(slot_of(lax.rem(z + step, DEPTH), y, c), t) for step in range(1, DEPTH)]
    everyone = [late_turn(turn)[0] for turn in range(1, 8)] + z_peers
    for device in everyone:
        pl.semaphore_signal(barrier, inc=1, device_id=device, device_id_type=MESH_ID)

    def prepare(held, stack):
        load = pltpu.make_async_copy(view, held, copy_sem.at[0])
        load.start()

        def first_norm(at, step):
            unit, inverse = norm(tokens[pl.ds(at, step), :])
            to = pl.ds(pl.multiple_of(t * rows + at, step), step)
            rows_one[to, :] = (unit * vecs[0:1, :] + vecs[1:2, :]).astype(bf)
            grad_rows[to, :] = cot[pl.ds(at, step), :].astype(bf)

        load.wait()
        lay_blocks(held, stack)

        def pair(left, right, count, left_high=False, right_high=False):
            first, second = stack[left : left + count, :], stack[right : right + count, :]
            first = pltpu.roll(first, HALF, 1) if left_high else first
            second = second if right_high else pltpu.roll(second, HALF, 1)
            lane = lax.broadcasted_iota(jnp.int32, (count, LANES), 1)
            return jnp.where(lane < HALF, first, second).astype(bf)

        n = gq.shape[1]
        gq[me] = pair(0, n, n)
        base = 2 * n
        wide = [pair(base + b * 64, base + b * 64 + 64, 64) for b in range(0, 8, 2)]
        go[z * 2 + y, :, lanes(c * 512, 512, 512)] = jnp.concatenate(wide, 1)
        pl.semaphore_wait(barrier, len(everyone))
        for k in (Q, O):
            own_sends_y(k)
            own_sends_z(k)
        by_rows(first_norm)
        x_rows(rows_one, 0).start()
        base += 512
        gi[me] = pair(base, 0, D, right_high=True)
        for r in range(2):
            for b in range(0, 16, 2):
                at = D + (r * 16 + b) * 64
                gd[me, r * 64 : r * 64 + 64, b * HALF : b * HALF + LANES] = pair(at, at + 64, 64, True, True)

    pl.run_scoped(
        prepare,
        pltpu.VMEM(view.shape, f32),
        pltpu.VMEM((view.shape[2] // 2 * BLOCK, LANES), f32),
    )
    x_rows(grad_rows, 1).start()
    z_arrival((Q, O), 1)
    y_arrival((Q, O), 0)
    z_arrival((Q, O), 2)
    for k in (I, W, V):
        own_sends_z(k)
    own_sends_y(I)
    y_arrival((Q, O), 1)

    def core_waits(kinds, zz):
        for k in kinds:
            for yy in (y, 1 - y):
                ag_wait(k, zz, yy, 1 - c)

    x_rows_wait(rows_one, 0)

    ends = []
    for p in range(ARTICLES):
        length = 0
        for a in range(ARTICLES):
            length = length + jnp.where(order[0, p] == a, lengths[0, a], 0)
        ends.append(length + ends[-1] if p else length)

    def allowed(first, count):
        ids = lax.broadcasted_iota(jnp.int32, (rows, 1), 0) + first
        start = jnp.zeros((rows, 1), jnp.int32)
        for end in ends:
            start = jnp.where(ids >= end, end, start)
        start = jnp.where(ids >= ends[-1], ids, start)
        keys = lax.broadcasted_iota(jnp.int32, (rows, count), 1)
        return (keys <= ids) & (keys >= start)

    scale = HD ** (-0.5)
    strip = 1024

    def assemble(h):
        for yy in range(2):
            even, odd = gq.at[slot_of(h, yy, 0)], gq.at[slot_of(h, yy, 1)]
            at = yy * 192
            wqkv[h, 0:768, at : at + 64] = even[:, 0:64]
            wqkv[h, 768:1024, at : at + 64] = even[0:256, 64:128]
            wqkv[h, 0:512, at + 64 : at + 128] = even[256:768, 64:128]
            wqkv[h, 512:1024, at + 64 : at + 128] = odd[0:512, 0:64]
            wqkv[h, 0:256, at + 128 : at + 192] = odd[512:768, 0:64]
            wqkv[h, 256:1024, at + 128 : at + 192] = odd[:, 64:128]

    def disassemble(h, value):
        for yy in range(2):
            even, odd = gq.at[slot_of(h, yy, 0)], gq.at[slot_of(h, yy, 1)]
            at = yy * 192
            even[:, 0:64] = value[0:768, at : at + 64]
            even[0:256, 64:128] = value[768:1024, at : at + 64]
            even[256:768, 64:128] = value[0:512, at + 64 : at + 128]
            odd[0:512, 0:64] = value[512:1024, at + 64 : at + 128]
            odd[512:768, 0:64] = value[0:256, at + 128 : at + 192]
            odd[:, 64:128] = value[256:1024, at + 128 : at + 192]

    qv = vecs[pl.ds(6 + t, 1), :]
    for h in range(DEPTH):
        none = jnp.zeros((1, HD), f32)
        qkv_bias[h] = jnp.concatenate([qv[:, h * 256 : h * 256 + 128], none, qv[:, h * 256 + 128 : h * 256 + 256]], 1)

    def head(h):
        core_waits((Q,), h)
        assemble(h)
        qkv[h] = (dot(rows_one[...], wqkv[h]) + qkv_bias[h]).astype(bf)
        for block in range(2):
            at, seen = slice(block * rows, (block + 1) * rows), (block + 1) * rows
            scores = dot_nt(qkv[h, at, 0:128], qkv[h, 0:seen, 128:256]) * scale
            scores = jnp.where(allowed(block * rows, seen), scores, NEG)
            expo = jnp.exp(scores - jnp.max(scores, -1, keepdims=True))
            low = (expo * (1.0 / jnp.sum(expo, -1, keepdims=True))).astype(bf)
            probs[h, at, 0:seen] = low
            ctx[at, lanes(h * HD, HD, HD)] = dot(low, qkv[h, 0:seen, 256:384]).astype(bf)

    head(near(0))
    y_arrival((Q, O), 2)
    z_arrival((Q, O), 3)
    y_arrival((Q, O), 3)
    own_sends_y(W)
    head(near(1))
    own_sends_y(V)
    head(near(2))
    z_arrival((I, W), 1)
    head(near(3))
    y_arrival((I, W), 0)
    for zz in range(DEPTH):
        core_waits((O,), zz)
    def w_out(ref):
        return ref[...].reshape(DEPTH * HD, D)
    far[0] = dot(ctx[other, :], w_out(go)).astype(bf)
    x_part(0).start()
    mixed[...] = tokens[...] + dot(ctx[own, :], w_out(go)) + vecs[4:5, :]
    z_arrival((I, W), 2)
    x_part(0).wait_recv()
    def second_norm(at, step):
        value = mixed[pl.ds(at, step), :] + inx[0, pl.ds(at, step), :].astype(f32)
        mixed[pl.ds(at, step), :] = value
        unit, inverse = norm(value)
        to = pl.ds(pl.multiple_of(t * rows + at, step), step)
        rows_two[to, :] = (unit * vecs[2:3, :] + vecs[3:4, :]).astype(bf)
    x_rows_wait(grad_rows, 1)
    by_rows(second_norm)
    x_rows(rows_two, 2).start()
    v_forward(z, 1 - y)
    macc[...] = jnp.zeros_like(macc)
    y_arrival((I, W), 1)
    nacc[...] = jnp.zeros_like(nacc)
    vout[...] = jnp.zeros_like(vout)
    z_arrival((I, W), 3)
    def ffn(half, zz):
        first = 4 * zz
        at = pl.ds(pl.multiple_of(lax.rem(t + half, 2) * rows, rows), rows)
        units = lanes(zz * 512, 512, 512)
        bias_row = vecs[pl.ds(8 + 2 * t + lax.div(zz, 2), 1), lanes(lax.rem(zz, 2) * 512, 512, 512)]

        def w_in(start, count):
            return jnp.concatenate([gi[first + j, start : start + count, :] for j in range(4)], 1)

        def w_down(start, count):
            return gd[pl.ds(first, 4), :, start : start + count].reshape(512, count)

        inner = dot(rows_two[at, :], w_in(0, D)) + bias_row
        square = inner * inner
        bent = jnp.tanh(GELU_A * inner * (1.0 + GELU_B * square))
        act[at, units] = (0.5 * inner * (1.0 + bent)).astype(bf)
        slope = 0.5 * (1.0 + bent) + 0.5 * inner * (1.0 - bent * bent) * (GELU_A * (1.0 + 3.0 * GELU_B * square))
        gin[at, units] = (dot_nt(grad_rows[at, :], w_down(0, D)) * slope).astype(bf)
        for nb in range(4):
            out = slice(nb * 256, nb * 256 + 256)
            nacc[at, out] += dot_nt(gin[at, units], w_in(nb * 256, 256))
            macc[at, out] += dot(act[at, units], w_down(nb * 256, 256))
    def ffn_grads(zz):
        first = 4 * zz
        units = lanes(zz * 512, 512, 512)
        for k in (I, W, V):
            for yy in range(2):
                drain(k, zz, yy)
        bias_sum[zz] = jnp.sum(gin[:, units].astype(f32), 0, keepdims=True)
        for nb in range(4):
            out = slice(nb * 256, nb * 256 + 256)
            part = dot(rows_t[out, :], gin[:, units]).astype(bf)
            for j in range(4):
                gi[first + j, out, :] = part[:, j * LANES : (j + 1) * LANES]
        for yy in (1 - y, y):
            rc_copy(I, zz, yy).start()
        act_t = act[:, units].T
        for nb in range(4):
            out = slice(nb * 256, nb * 256 + 256)
            part = dot(act_t, grad_rows[:, out]).astype(bf)
            gd[pl.ds(first, 4), :, out] = part.reshape(4, LANES, 256)
        for yy in (1 - y, y):
            rc_copy(W, zz, yy).start()
    def each(kinds, step, *args):
        for k in kinds:
            step(k, *args)
    def reduce_out():
        for yy in (1 - y, y):
            for s in (3, 2, 1, 0):
                rc_add(O, near(s), yy)
    def reduce_head(zz):
        for yy in (1 - y, y):
            rc_add(Q, zz, yy)
    v_arrival(1)
    def reduce_core(zz):
        for yy in (1 - y, y):
            for k in (I, W):
                rc_add(k, zz, yy)
    def v_step(s):
        for yy in (1 - y, y):
            z_step(V, s, yy)
    def v_merge(s):
        for yy in (1 - y, y):
            z_merge(V, s, yy)
    core_waits((I, W, V), z)
    ffn(0, z)
    core_waits((I, W, V), near(1))
    ffn(0, near(1))
    x_rows_wait(rows_two, 2)
    x_out().start()
    v_arrival(2)
    rows_t[...] = rows_two[...].T
    y_arrival((I, W), 2)
    def by_z(s, carry):
        @pl.when(s == 2)
        def _():
            v_arrival(3)
            y_arrival((I, W), 3)

        @pl.when(s >= 2)
        def _():
            core_waits((I, W, V), near(s))
            ffn(0, near(s))

        ffn(1, near(s))

        @pl.when(s == DEPTH - 1)
        def _():
            x_part(0).wait_send()
            far[0] = nacc[other, :].astype(bf)
            x_part(1).start()

        ffn_grads(near(s))

        @pl.when(s > 0)
        def _():
            reduce_core(near(s - 1))

        for before in (1, 2):

            @pl.when(s == before + 1)
            def _():
                v_step(before)

        return carry
    lax.fori_loop(0, DEPTH, by_z, 0)
    x_out().wait_recv()
    reduce_core(near(3))
    x_out_core(c).start()
    v_step(3)
    rows_t[...] = rows_one[...].T
    for zz in range(DEPTH):
        for side in range(2):
            row, start = 8 + 2 * side + zz // 2, zz % 2 * 512
            vout[0, row : row + 1, start : start + 512] = jnp.where(t == side, bias_sum[zz], 0.0)
    v_merge(1)
    x_part(1).wait_recv()
    def row_sum(row, value):
        vout[0, row : row + 1, :] += jnp.sum(value, 0, keepdims=True)
    def second_back(at, step):
        here = pl.ds(at, step)
        in_group = pl.ds(pl.multiple_of(t * rows + at, step), step)
        grad = nacc[in_group, :] + inx[0, here, :].astype(f32)
        unit, inverse = norm(mixed[here, :])
        back = cot[here, :] + norm_grad(grad, unit, inverse, vecs[2:3, :])
        input_grad[here, :] = back
        grad_attn[in_group, :] = back.astype(bf)
        row_sum(2, grad * unit)
        row_sum(3, grad)
        row_sum(4, back)
        row_sum(5, cot[here, :])
    by_rows(second_back)
    early_rows(0)
    x_out_core(1 - c).wait_recv()
    ctx_x[...] = dot_nt(grad_attn[own, :], w_out(go_x)).astype(bf)
    x_grad_context().start()
    gctx[own, :] = dot_nt(grad_attn[own, :], w_out(go)).astype(bf)
    each((I, W), ry_add, 1)
    v_merge(2)
    each((I, W), ry_add, 2)
    for zz in range(DEPTH):
        for yy in range(2):
            drain(O, zz, yy)
            drain(Q, zz, yy)
    def mixed_out(at, step):
        here = pl.ds(at, step)
        in_group = pl.ds(pl.multiple_of(t * rows + at, step), step)
        mixed[here, :] = mixed[here, :] + macc[in_group, :] + inx[1, here, :].astype(f32) + vecs[5:6, :]
    x_out().wait_send()
    x_grad_context_wait()
    far[1] = macc[other, :].astype(bf)
    x_rows(grad_attn, 3).start()
    def out_grads():
        x_rows_wait(grad_attn, 3)
        ctx_t = ctx[...].T
        for nb in range(4):
            at = slice(nb * 256, nb * 256 + 256)
            go[:, :, at] = dot(ctx_t, grad_attn[:, at]).astype(bf).reshape(8, 64, 256)
        for zz in range(DEPTH):
            for yy in range(2):
                rc_copy(O, zz, yy).start()
    def first_back(at, step):
        here = pl.ds(at, step)
        in_group = pl.ds(pl.multiple_of(t * rows + at, step), step)
        grad = nacc[in_group, :] + inx[0, here, :].astype(f32)
        unit, inverse = norm(tokens[here, :])
        input_grad[here, :] = input_grad[here, :] + norm_grad(grad, unit, inverse, vecs[0:1, :])
        row_sum(0, grad * unit)
        row_sum(1, grad)
    def finish_mixed():
        x_part(2).wait_recv()
        by_rows(mixed_out)
    def finish_input():
        x_part(3).wait_recv()
        by_rows(first_back)
    late_rows = (0, 1, 6, 7)
    v_cross()
    def late_start():
        for h in range(DEPTH):
            for row in range(2):
                total = jnp.where(t == row, qv_sum[h], 0.0)
                vout[0, 6 + row : 7 + row, h * 256 : h * 256 + 128] = total[:, 0:128]
                vout[0, 6 + row : 7 + row, h * 256 + 128 : h * 256 + 256] = total[:, 256:384]
        for at, row in enumerate(late_rows):
            for j in range(8):
                late[at * 8 + j : at * 8 + j + 1, :] = vout[0, row : row + 1, j * LANES : (j + 1) * LANES]
        late_in[t * 4 + y * 2 + c] = late[...]
        for turn in range(1, 8):
            late_copy(turn).start()
    def late_cross():
        for turn in range(1, 8):
            late_wait(late_turn(turn)[1])
        total = late_in[0]
        for index in range(1, 8):
            total = total + late_in[index]
        late_sum[...] = total
        late_in[8 + z] = total
        for step in range(1, DEPTH):
            late_z(step).start()
    def vec_finish():
        for step in range(1, DEPTH):
            zz = lax.rem(z + step, DEPTH)
            late_wait(8 + zz)
            remote(vin.at[3 + zz], vin.at[3 + zz], v_send.at[0], v_recv.at[3 + zz], y_peer).wait_recv()
        total = ((late_in[8] + late_in[9]) + late_in[10]) + late_in[11]
        early = ((vin[3] + vin[4]) + vin[5]) + vin[6]
        vec_grads[...] = early[0 : vec_grads.shape[0]]
        for at, row in enumerate(late_rows):
            for j in range(8):
                vec_grads[row : row + 1, j * LANES : (j + 1) * LANES] = total[at * 8 + j : at * 8 + j + 1, :]
    def head_back(h, turn):
        q0, q1 = qkv[h, 0:rows, 0:128], qkv[h, rows : 2 * rows, 0:128]
        grads = []
        for block in range(2):
            at, seen = slice(block * rows, (block + 1) * rows), (block + 1) * rows
            low = probs[h, at, 0:seen]
            given = gctx[at, lanes(h * HD, HD, HD)]
            prob = low.astype(f32)
            grad_probs = dot_nt(given, qkv[h, 0:seen, 256:384])
            delta = jnp.sum(prob * grad_probs, -1, keepdims=True)
            grad_scores = (prob * (grad_probs - delta)).astype(bf)
            grad_q = dot(grad_scores, qkv[h, 0:seen, 128:256]) * scale
            grad_k = dot_tn(grad_scores, q1 if block else q0) * scale
            grad_v = dot_tn(low, given)
            grads.append((grad_q, grad_k, grad_v))
        (gq0, gk0, gv0), (gq1, gk1, gv1) = grads
        top = jnp.concatenate([gq0, gk0 + gk1[0:rows], gv0 + gv1[0:rows]], 1).astype(bf)
        low_half = jnp.concatenate([gq1, gk1[rows:], gv1[rows:]], 1).astype(bf)
        qkv[h, 0:rows, :] = top
        qkv[h, rows : 2 * rows, :] = low_half
        total = jnp.sum(top.astype(f32), 0, keepdims=True) + jnp.sum(low_half.astype(f32), 0, keepdims=True)
        qv_sum[h] = total
        for half in (other, own):
            product = dot_nt(qkv[h, half, :], wqkv[h])
            if turn == 0:
                nacc[half, :] = product
            else:
                nacc[half, :] += product
            if turn == DEPTH - 1 and half is other:
                x_part(1).wait_send()
                far[0] = nacc[other, :].astype(bf)
                x_part(3).start()
        part = dot(rows_t[...], qkv[h]).astype(bf)
        disassemble(h, part)
        for yy in (1 - y, y):
            rc_copy(Q, h, yy).start()
    early_rows(1)
    head_back(near(3), 0)
    early_rows(2)
    head_back(near(2), 1)
    early_rows(3)
    x_part(2).start()
    reduce_head(near(3))
    each((I, W), ry_add, 3)
    each((I, W), ry_merge, 1)
    out_grads()
    reduce_head(near(2))
    head_back(near(1), 2)
    reduce_out()
    each((I, W), ry_merge, 2)
    head_back(z, 3)
    ry_add(Q, 3)
    finish_mixed()
    reduce_head(near(1))
    ry_add(Q, 2)
    ry_add(O, 3)
    ry_add(Q, 1)
    ry_add(O, 2)
    ry_merge(Q, 2)
    reduce_head(z)
    ry_merge(Q, 1)
    ry_add(O, 1)
    own_total(W)
    finish_input()
    late_start()
    ry_merge(O, 2)
    late_cross()
    z_total(V, y, total_of(V), y_landed(V, z))
    ry_merge(O, 1)
    own_total(Q)
    own_total(I)
    vec_finish()
    own_total(O)

    for stage in range(3):
        v_copy(stage).wait_send()
    for turn in range(1, 8):
        late_copy(turn).wait_send()
    for step in range(1, DEPTH):
        vz_copy(step).wait_send()
        late_z(step).wait_send()
    for index, ref in enumerate((rows_one, grad_rows, rows_two, grad_attn)):
        x_rows(ref, index).wait_send()
    for index in (2, 3):
        x_part(index).wait_send()
    x_out_core(c).wait_send()
    x_grad_context().wait_send()
    for k in range(4):
        for zz in range(DEPTH):
            for yy in range(2):
                rc_copy(k, zz, yy).wait_send()
            ry_copy(k, zz).wait_send()
        for s in range(1, DEPTH):
            rz_copy(k, s, y, True).wait_send()
    ry_copy(V, z).wait_send()
    for yy in range(2):
        for s in range(1, DEPTH):
            rz_copy(V, s, yy, True).wait_send()


def run_layer(tokens, cotangent, lengths, order, weights, vec_params):
    bf, f32 = jnp.bfloat16, jnp.float32
    rows = tokens.shape[0]
    group = 2 * rows
    owners = 16
    shapes = piece_shapes()
    view = jnp.transpose(weights, (1, 2, 0))
    there = pl.BlockSpec(memory_space=pl.ANY)
    vmem = pl.BlockSpec(memory_space=pltpu.VMEM)
    smem = pl.BlockSpec(memory_space=pltpu.SMEM)

    halved = shapes[:3] + ((HALF, D),)

    def many(count, kinds):
        return [pltpu.VMEM((count,) + s, bf) for s in kinds]

    full = pltpu.VMEM((group, D), bf)
    dma = pltpu.SemaphoreType.DMA
    return pl.pallas_call(
        layer_kernel,
        out_shape=[jax.ShapeDtypeStruct((rows, D), f32)] * 2
        + [jax.ShapeDtypeStruct(s, f32) for s in shapes]
        + [jax.ShapeDtypeStruct(vec_params.shape, f32)],
        in_specs=[smem, smem, there] + [vmem] * 3,
        out_specs=[vmem] * 7,
        scratch_shapes=[
            pltpu.VMEM((owners,) + shapes[0], bf),
            pltpu.VMEM((owners // 2, BLOCK, D), bf),
            pltpu.VMEM((owners,) + shapes[2], bf),
            pltpu.VMEM((owners,) + shapes[3], bf),
            pltpu.VMEM((DEPTH, D, 3 * HD), bf),
        ]
        + many(2 * DEPTH, shapes)
        + many(DEPTH, halved)
        + many(1, halved[3:])
        + many(DEPTH, halved)
        + many(2 * DEPTH, halved[3:])
        + [
            full,
            full,
            pltpu.VMEM((D, group), bf),
            full,
            full,
            pltpu.VMEM((DEPTH, group, group), bf),
            pltpu.VMEM((DEPTH, group, 3 * HD), bf),
            pltpu.VMEM((group, DEPTH * HD), bf),
            pltpu.VMEM((group, DEPTH * HD), bf),
            pltpu.VMEM((2, rows, D), bf),
            pltpu.VMEM((2, rows, D), bf),
            pltpu.VMEM((owners // 2, BLOCK, D), bf),
            pltpu.VMEM((rows, DEPTH * HD), bf),
            pltpu.VMEM((group, D), f32),
            pltpu.VMEM((group, D), f32),
            pltpu.VMEM((group, 2 * D), bf),
            pltpu.VMEM((group, 2 * D), bf),
            pltpu.VMEM((DEPTH, 1, 512), f32),
            pltpu.VMEM((DEPTH, 1, 3 * HD), f32),
            pltpu.VMEM((DEPTH, 1, 3 * HD), f32),
            pltpu.VMEM((7, 16, D), f32),
            pltpu.VMEM((5, 16, D), f32),
            pltpu.VMEM((32, LANES), f32),
            pltpu.VMEM((32, LANES), f32),
            pltpu.VMEM((12, 32, LANES), f32),
            dma((5, owners)),
            dma((5, DEPTH)),
            dma((5, 2 * DEPTH)),
            dma((5, 2, 2 * DEPTH)),
            dma((4, 2 * DEPTH)),
            dma((4, 2 * DEPTH)),
            dma((5, DEPTH)),
            dma((5, DEPTH)),
            dma((5, 2 * DEPTH)),
            dma((5, 2 * DEPTH)),
            dma((11,)),
            dma((11,)),
            dma((6,)),
            dma((7,)),
            dma((11,)),
            dma((12,)),
            dma((1,)),
        ],
        compiler_params=pltpu.CompilerParams(
            collective_id=0, has_side_effects=True, vmem_limit_bytes=VMEM_LIMIT
        ),
        name="layer",
    )(lengths, order, view, tokens, cotangent, vec_params)


def per_device(
    grp_count,
    tp_count,
    tokens,
    cotangent,
    lengths,
    order,
    weights,
    momentum,
    stat_left,
    stat_right,
    root_left,
    root_right,
    vec_params,
    vec_momentum,
    vec_second,
):
    fits = grp_count == 4 * DEPTH and tp_count == 2 and tokens.shape[0] == 256
    if not fits or lengths.shape[1] != ARTICLES:
        return per_device_general(
            tokens,
            cotangent,
            lengths,
            order,
            weights,
            momentum,
            stat_left,
            stat_right,
            root_left,
            root_right,
            vec_params,
            vec_momentum,
            vec_second,
        )
    token_total = tokens.shape[0] * tp_count * grp_count
    mixed, input_grad, *sums, vec_grads = run_layer(tokens, cotangent, lengths, order, weights, vec_params)
    blocks, vecs, results = update_blocks(
        sums,
        (weights, momentum, stat_left, stat_right, root_left, root_right),
        vec_grads,
        (vec_params, vec_momentum, vec_second),
        (mixed, input_grad),
        token_total,
    )
    return (*results, *blocks, *vecs)


def solution(mesh):
    placed = (
        P(("grp", "tp"), None),
        P(("grp", "tp"), None),
        P("grp", None),
        P("grp", None),
        P(("tp", "grp"), None, None),
        P(("tp", "grp"), None, None),
        P(("tp", "grp"), None, None),
        P(("tp", "grp"), None, None),
        P(("tp", "grp"), None, None),
        P(("tp", "grp"), None, None),
        P(),
        P(),
        P(),
    )
    return jax.shard_map(
        functools.partial(per_device, mesh.shape["grp"], mesh.shape["tp"]),
        mesh=mesh,
        in_specs=placed,
        out_specs=(
            P(("grp", "tp"), None),
            P(("grp", "tp"), None),
            P(("tp", "grp"), None, None),
            P(("tp", "grp"), None, None),
            P(("tp", "grp"), None, None),
            P(("tp", "grp"), None, None),
            P(("tp", "grp"), None, None),
            P(),
            P(),
            P(),
            P(),
        ),
        check_vma=False,
    )
```

```python
import functools

import jax
import jax.numpy as jnp
from jax import lax
from jax.experimental import pallas as pl
from jax.experimental.pallas import tpu as pltpu
from jax.sharding import PartitionSpec as P

D = 1024
HEADS = 8
HD = 128
FF = 4096
BLOCK = 64


EPS = 1e-05
NEG = -1e30
DECAY = 0.9
BETA = 0.9
RATE = 0.05
VEC_DECAY = 0.9
VEC_RATE = 0.2
VEC_EPS = 1e-08


def norm_rows(value, gain, shift):
    average = jnp.mean(value, -1, keepdims=True)
    centred = value - average
    inverse = lax.rsqrt(jnp.mean(centred * centred, -1, keepdims=True) + EPS)
    normed = centred * inverse
    return (normed * gain + shift, normed, inverse)


def norm_back(grad_out, normed, inverse, gain):
    scaled = grad_out * gain
    return inverse * (
        scaled
        - jnp.mean(scaled, -1, keepdims=True)
        - normed * jnp.mean(scaled * normed, -1, keepdims=True)
    )


def segment_ids(lengths_row, order_row, group_rows):
    article_count = lengths_row.shape[0]
    slots = jnp.arange(article_count, dtype=jnp.int32)
    picks = (order_row[:, None] == slots[None, :]).astype(jnp.int32)
    packed = jnp.sum(picks * lengths_row[None, :], 1)
    ends = jnp.cumsum(packed)
    spots = jnp.arange(group_rows, dtype=jnp.int32)
    return jnp.sum((spots[:, None] >= ends[None, :]).astype(jnp.int32), 1)


def allowed_mask(row_ids, row_segs, segments, key_ids, article_count):
    causal = key_ids[None, :] <= row_ids[:, None]
    same = segments[None, :] == row_segs[:, None]
    alone = (row_segs[:, None] < article_count) | (key_ids[None, :] == row_ids[:, None])
    return causal & same & alone


def from_columns(tiles, row_total, col_total):
    return (
        tiles.reshape(col_total // BLOCK, row_total // BLOCK, BLOCK, BLOCK)
        .transpose(1, 2, 0, 3)
        .reshape(row_total, col_total)
    )


def from_rows(tiles, row_total, col_total):
    return (
        tiles.reshape(row_total // BLOCK, col_total // BLOCK, BLOCK, BLOCK)
        .transpose(0, 2, 1, 3)
        .reshape(row_total, col_total)
    )


def to_columns(matrix):
    row_total, col_total = matrix.shape
    return (
        matrix.reshape(row_total // BLOCK, BLOCK, col_total // BLOCK, BLOCK)
        .transpose(2, 0, 1, 3)
        .reshape(-1, BLOCK, BLOCK)
    )


def to_rows(matrix):
    row_total, col_total = matrix.shape
    return (
        matrix.reshape(row_total // BLOCK, BLOCK, col_total // BLOCK, BLOCK)
        .transpose(0, 2, 1, 3)
        .reshape(-1, BLOCK, BLOCK)
    )


def per_device_general(
    tokens,
    cotangent,
    lengths,
    order,
    weights,
    momentum,
    stat_left,
    stat_right,
    root_left,
    root_right,
    vec_params,
    vec_momentum,
    vec_second,
):
    groups = lax.axis_size("grp")
    tp_size = lax.axis_size("tp")
    tp_rank = lax.axis_index("tp")
    tok_rows = tokens.shape[0]
    group_rows = tok_rows * tp_size
    article_count = lengths.shape[1]
    owners = groups * tp_size
    block_area = BLOCK * BLOCK * owners
    qkv_count = 3 * D * D // block_area
    out_count = D * D // block_area
    in_count = D * FF // block_area
    owned_blocks = weights.shape[0]
    heads_here = HEADS // tp_size
    qkv_cols = 3 * D // tp_size
    feat_here = D // tp_size
    ff_here = FF // tp_size
    qv_width = 2 * D // tp_size
    token_total = group_rows * groups
    gathered = lax.all_gather(weights.astype(jnp.bfloat16), "grp", axis=0, tiled=True)
    per_owner = gathered.reshape(groups, owned_blocks, BLOCK, BLOCK)
    marks = [0, qkv_count, qkv_count + out_count, qkv_count + out_count + in_count, owned_blocks]
    pieces = [
        per_owner[:, marks[index] : marks[index + 1]].reshape(-1, BLOCK, BLOCK)
        for index in range(4)
    ]
    w_qkv = from_columns(pieces[0], D, qkv_cols)
    w_out = from_rows(pieces[1], feat_here, D)
    w_in = from_columns(pieces[2], D, ff_here)
    w_down = from_rows(pieces[3], ff_here, D)
    w_qkv_heads = w_qkv.reshape(D, heads_here, 3, HD)
    w_out_heads = w_out.reshape(heads_here, HD, D)
    segments = segment_ids(lengths[0], order[0], group_rows)
    gain_one = vec_params[0]
    shift_one = vec_params[1]
    gain_two = vec_params[2]
    shift_two = vec_params[3]
    bias_out = vec_params[4]
    bias_down = vec_params[5]
    qv_here = lax.dynamic_slice_in_dim(
        vec_params[6:8].reshape(2 * D), tp_rank * qv_width, qv_width
    ).reshape(heads_here, 2, HD)
    bias_heads = jnp.stack(
        [qv_here[:, 0], jnp.zeros((heads_here, HD), jnp.float32), qv_here[:, 1]], 0
    )[:, :, None, :]
    bias_in = lax.dynamic_slice_in_dim(vec_params[8:].reshape(FF), tp_rank * ff_here, ff_here)
    normed_one, unit_one, inverse_one = norm_rows(tokens, gain_one, shift_one)
    rows_one = lax.all_gather(normed_one.astype(jnp.bfloat16), "tp", axis=0, tiled=True)
    projected = (
        jnp.einsum("rx,xhcd->chrd", rows_one, w_qkv_heads, preferred_element_type=jnp.float32)
        + bias_heads
    ).astype(jnp.bfloat16)
    queries = projected[0]
    keys_all = projected[1]
    values_all = projected[2]
    span = min(512, group_rows)
    starts = jnp.arange(group_rows // span, dtype=jnp.int32) * span
    key_ids = jnp.arange(group_rows, dtype=jnp.int32)
    score_scale = HD ** (-0.5)

    def masked_scores(first_row):
        row_ids = first_row + jnp.arange(span, dtype=jnp.int32)
        row_segs = lax.dynamic_slice_in_dim(segments, first_row, span, 0)
        allowed = allowed_mask(row_ids, row_segs, segments, key_ids, article_count)
        query_rows = lax.dynamic_slice_in_dim(queries, first_row, span, 1)
        scores = (
            jnp.einsum("hqd,hkd->hqk", query_rows, keys_all, preferred_element_type=jnp.float32)
            * score_scale
        )
        return (jnp.where(allowed[None], scores, NEG), query_rows)

    def attend(context_buf, first_row):
        scores, query_rows = masked_scores(first_row)
        row_max = jnp.max(scores, -1, keepdims=True)
        expo = jnp.exp(scores - row_max)
        expsum = jnp.sum(expo, -1, keepdims=True)
        probs_low = (expo / expsum).astype(jnp.bfloat16)
        context = jnp.einsum(
            "hqk,hkd->hqd", probs_low, values_all, preferred_element_type=jnp.float32
        ).astype(jnp.bfloat16)
        context_buf = lax.dynamic_update_slice_in_dim(context_buf, context, first_row, 1)
        return (context_buf, (row_max + jnp.log(expsum))[:, :, 0])

    context_low, log_norm = lax.scan(
        attend, jnp.zeros((heads_here, group_rows, HD), jnp.bfloat16), starts
    )
    attn_sum = lax.psum_scatter(
        jnp.einsum(
            "hrd,hde->re", context_low, w_out_heads, preferred_element_type=jnp.float32
        ).astype(jnp.bfloat16),
        "tp",
        scatter_dimension=0,
        tiled=True,
    ).astype(jnp.float32)
    hidden = tokens + attn_sum + bias_out
    normed_two, unit_two, inverse_two = norm_rows(hidden, gain_two, shift_two)
    rows_two = lax.all_gather(normed_two.astype(jnp.bfloat16), "tp", axis=0, tiled=True)
    inner = jnp.dot(rows_two, w_in, preferred_element_type=jnp.float32) + bias_in
    activ, gelu_pull = jax.vjp(jax.nn.gelu, inner)
    activ_low = activ.astype(jnp.bfloat16)
    mixed = (
        hidden
        + lax.psum_scatter(
            jnp.dot(activ_low, w_down, preferred_element_type=jnp.float32).astype(jnp.bfloat16),
            "tp",
            scatter_dimension=0,
            tiled=True,
        ).astype(jnp.float32)
        + bias_down
    )
    grad_low = cotangent.astype(jnp.bfloat16)
    grad_rows = lax.all_gather(grad_low, "tp", axis=0, tiled=True)
    g_down = jnp.einsum("rf,rd->fd", activ_low, grad_rows, preferred_element_type=jnp.float32)
    grad_activ = jnp.einsum("rd,fd->rf", grad_rows, w_down, preferred_element_type=jnp.float32)
    grad_inner = gelu_pull(grad_activ)[0].astype(jnp.bfloat16)
    g_in = jnp.einsum("rd,rf->df", rows_two, grad_inner, preferred_element_type=jnp.float32)
    g_bias_in = jnp.sum(grad_inner.astype(jnp.float32), 0)
    ffn_blocks = jnp.concatenate(
        [
            to_columns(g_in).reshape(groups, in_count, BLOCK, BLOCK),
            to_rows(g_down).reshape(groups, in_count, BLOCK, BLOCK),
        ],
        1,
    )
    grad_normed_two = lax.psum_scatter(
        jnp.einsum("rf,df->rd", grad_inner, w_in, preferred_element_type=jnp.float32).astype(
            jnp.bfloat16
        ),
        "tp",
        scatter_dimension=0,
        tiled=True,
    ).astype(jnp.float32)
    grad_hidden = cotangent + norm_back(grad_normed_two, unit_two, inverse_two, gain_two)
    grad_attn_low = grad_hidden.astype(jnp.bfloat16)
    grad_attn_rows = lax.all_gather(grad_attn_low, "tp", axis=0, tiled=True)
    g_out = jnp.einsum(
        "hrd,re->hde", context_low, grad_attn_rows, preferred_element_type=jnp.float32
    ).reshape(feat_here, D)
    grad_context = jnp.einsum(
        "re,hde->hrd", grad_attn_rows, w_out_heads, preferred_element_type=jnp.float32
    ).astype(jnp.bfloat16)
    zero_heads = jnp.zeros((heads_here, group_rows, HD), jnp.float32)

    def attend_back(carry, inputs):
        grad_queries, grad_keys, grad_values = carry
        first_row, log_block = inputs
        scores, query_rows = masked_scores(first_row)
        probs = jnp.exp(scores - log_block[:, :, None])
        grad_ctx_rows = lax.dynamic_slice_in_dim(grad_context, first_row, span, 1)
        grad_probs = jnp.einsum(
            "hqd,hkd->hqk", grad_ctx_rows, values_all, preferred_element_type=jnp.float32
        )
        delta = jnp.sum(probs * grad_probs, -1, keepdims=True)
        grad_scores = (probs * (grad_probs - delta)).astype(jnp.bfloat16)
        query_part = (
            jnp.einsum("hqk,hkd->hqd", grad_scores, keys_all, preferred_element_type=jnp.float32)
            * score_scale
        )
        grad_queries = lax.dynamic_update_slice_in_dim(grad_queries, query_part, first_row, 1)
        grad_keys = (
            grad_keys
            + jnp.einsum(
                "hqk,hqd->hkd", grad_scores, query_rows, preferred_element_type=jnp.float32
            )
            * score_scale
        )
        grad_values = grad_values + jnp.einsum(
            "hqk,hqd->hkd",
            probs.astype(jnp.bfloat16),
            grad_ctx_rows,
            preferred_element_type=jnp.float32,
        )
        return ((grad_queries, grad_keys, grad_values), None)

    (grad_queries, grad_keys, grad_values), unused = lax.scan(
        attend_back, (zero_heads, zero_heads, zero_heads), (starts, log_norm)
    )
    grad_proj = jnp.stack([grad_queries, grad_keys, grad_values], 0).astype(jnp.bfloat16)
    proj_sums = jnp.sum(grad_proj.astype(jnp.float32), 2)
    g_bias_qv = jnp.stack([proj_sums[0], proj_sums[2]], 1).reshape(qv_width)
    g_qkv = jnp.einsum(
        "rx,chrd->xhcd", rows_one, grad_proj, preferred_element_type=jnp.float32
    ).reshape(D, qkv_cols)
    grad_normed_one = lax.psum_scatter(
        jnp.einsum(
            "chrd,xhcd->rx", grad_proj, w_qkv_heads, preferred_element_type=jnp.float32
        ).astype(jnp.bfloat16),
        "tp",
        scatter_dimension=0,
        tiled=True,
    ).astype(jnp.float32)
    input_grad = grad_hidden + norm_back(grad_normed_one, unit_one, inverse_one, gain_one)
    local_rows = jnp.stack(
        [
            jnp.sum(grad_normed_one * unit_one, 0),
            jnp.sum(grad_normed_one, 0),
            jnp.sum(grad_normed_two * unit_two, 0),
            jnp.sum(grad_normed_two, 0),
            jnp.sum(grad_hidden, 0),
            jnp.sum(cotangent, 0),
        ]
    )
    qv_rows = lax.dynamic_update_slice(
        jnp.zeros((2 * D,), jnp.float32), g_bias_qv, (tp_rank * qv_width,)
    ).reshape(2, D)
    in_rows = lax.dynamic_update_slice(
        jnp.zeros((FF,), jnp.float32), g_bias_in, (tp_rank * ff_here,)
    ).reshape(FF // D, D)
    vec_grads = lax.psum(jnp.concatenate([local_rows, qv_rows, in_rows], 0), ("grp", "tp"))
    attn_blocks = jnp.concatenate(
        [
            to_columns(g_qkv).reshape(groups, qkv_count, BLOCK, BLOCK),
            to_rows(g_out).reshape(groups, out_count, BLOCK, BLOCK),
        ],
        1,
    )
    every_block = jnp.concatenate([attn_blocks, ffn_blocks], 1).reshape(-1, BLOCK, BLOCK)
    weight_grads = lax.psum_scatter(
        every_block.astype(jnp.bfloat16), "grp", scatter_dimension=0, tiled=True
    ).astype(jnp.float32)
    scaled = weight_grads * token_total ** (-0.5)
    stat_left_new = DECAY * stat_left + (1.0 - DECAY) * jnp.einsum(
        "nij,nkj->nik", scaled, scaled, precision=lax.Precision.HIGHEST
    )
    stat_right_new = DECAY * stat_right + (1.0 - DECAY) * jnp.einsum(
        "nji,njk->nik", scaled, scaled, precision=lax.Precision.HIGHEST
    )
    shaped = jnp.einsum("nij,njk->nik", root_left, scaled, precision=lax.Precision.HIGHEST)
    shaped = jnp.einsum("nij,njk->nik", shaped, root_right, precision=lax.Precision.HIGHEST)
    momentum_new = BETA * momentum + shaped
    weights_new = weights - RATE * momentum_new
    vec_scaled = vec_grads * token_total ** (-0.5)
    vec_second_new = VEC_DECAY * vec_second + (1.0 - VEC_DECAY) * vec_scaled * vec_scaled
    vec_momentum_new = BETA * vec_momentum + vec_scaled * lax.rsqrt(vec_second_new + VEC_EPS)
    vec_new = vec_params - VEC_RATE * vec_momentum_new
    return (
        mixed,
        input_grad,
        weight_grads,
        stat_left_new,
        stat_right_new,
        momentum_new,
        weights_new,
        vec_grads,
        vec_second_new,
        vec_momentum_new,
        vec_new,
    )


MESH_ID = pl.DeviceIdType.MESH
LANES = 128
HALF = 64
VMEM_LIMIT = 62 * 2**20
ARTICLES = 4
GELU_A = (2.0 / 3.141592653589793) ** 0.5
GELU_B = 0.044715


def remote(src, dst, send_sem, recv_sem, device):
    return pltpu.make_async_remote_copy(
        src_ref=src,
        dst_ref=dst,
        send_sem=send_sem,
        recv_sem=recv_sem,
        device_id=device,
        device_id_type=MESH_ID,
    )


def place():
    grp = lax.axis_index("grp")
    return lax.div(grp, 4), lax.rem(lax.div(grp, 2), 2), lax.rem(grp, 2), lax.axis_index("tp")


def slot_of(z, y, c):
    return z * 4 + y * 2 + c


def lay_blocks(view_ref, stack, first, last):
    half = view_ref.shape[2] // 2

    def row(i, carry):
        tile = view_ref[i].T
        stack[pl.ds(i, half, stride=BLOCK), :] = jnp.concatenate([tile[:half], tile[half:]], 1)
        return carry

    lax.fori_loop(first, last, row, 0, unroll=8)


def piece_shapes():
    return ((768, LANES), (64, 512), (1024, LANES), (LANES, 1024))


def both_halves(pair):
    low = lax.broadcasted_iota(jnp.int32, pair.shape, 1) < HALF
    turned = pltpu.roll(pair, HALF, 1)
    return jnp.where(low, pair, turned), jnp.where(low, turned, pair)


def update_kernel(
    scale,
    in_q,
    in_o,
    in_i,
    in_d,
    root_l,
    root_r,
    vec_g,
    vecs,
    vec_m,
    vec_s,
    mixed,
    input_grad,
    w,
    m,
    sl,
    sr,
    out_g,
    out_sl,
    out_sr,
    out_m,
    out_w,
    out_vg,
    out_vs,
    out_vm,
    out_v,
    out_mixed,
    out_input_grad,
    grads,
    first,
    second,
    held_l,
    held_r,
    held_w,
    held_m,
    held_sl,
    held_sr,
    sum_q,
    sum_o,
    sum_i,
    sum_d,
    sems,
    block_sems,
    sum_sems,
):
    count = w.shape[2]
    step_rows = out_w.shape[0]
    bf, f32 = jnp.bfloat16, jnp.float32

    def loads(k):
        part = pl.ds(16 * k, 16)
        return [
            pltpu.make_async_copy(root.at[part], held.at[part], sems.at[k, side])
            for side, (root, held) in enumerate(((root_l, held_l), (root_r, held_r)))
        ]

    def block_loads(k):
        part = pl.ds(k * step_rows, step_rows)
        pairs = ((w, held_w), (m, held_m), (sl, held_sl), (sr, held_sr))
        return [pltpu.make_async_copy(a.at[part], b.at[part], block_sems.at[k, n]) for n, (a, b) in enumerate(pairs)]

    out_mixed[...] = mixed[...]
    out_input_grad[...] = input_grad[...]

    @pl.when(pl.program_id(0) == 0)
    def _():
        for k in range(4):
            for load in loads(k):
                load.start()
        sum_loads = [
            pltpu.make_async_copy(a, b, sum_sems.at[n])
            for n, (a, b) in enumerate(((in_q, sum_q), (in_o, sum_o), (in_i, sum_i), (in_d, sum_d)))
        ]
        for load in sum_loads:
            load.start()
        for k in range(BLOCK // step_rows):
            for load in block_loads(k):
                load.start()
        total = vec_g[...]
        out_vg[...] = total
        scaled = total * scale
        fresh = VEC_DECAY * vec_s[...] + (1.0 - VEC_DECAY) * scaled * scaled
        out_vs[...] = fresh
        momentum = BETA * vec_m[...] + scaled * lax.rsqrt(fresh + VEC_EPS)
        out_vm[...] = momentum
        out_v[...] = vecs[...] - VEC_RATE * momentum
        def row(i, carry):
            both = jnp.concatenate([held_l[i], held_r[i]], 0)
            second[pl.ds(i, count, stride=BLOCK), :] = both.T
            return carry

        for k in range(4):
            for load in loads(k):
                load.wait()
            lax.fori_loop(16 * k, 16 * k + 16, row, 0, unroll=8)
        for load in sum_loads:
            load.wait()
        rows = sum_q.shape[0]
        grads[0:rows, 0:HALF] = sum_q[:, 0:HALF]
        grads[rows : 2 * rows, 0:HALF] = sum_q[:, HALF:LANES]
        base = 2 * rows
        for b in range(8):
            grads[base + b * 64 : base + b * 64 + 64, 0:HALF] = sum_o[:, b * HALF : (b + 1) * HALF]
        base += 512
        grads[base : base + D, 0:HALF] = sum_i[:, 0:HALF]
        grads[0:D, HALF:LANES] = sum_i[:, HALF:LANES]
        for r in range(2):
            for b in range(16):
                at = D + (r * 16 + b) * 64
                grads[at : at + 64, HALF:LANES] = sum_d[r * 64 : r * 64 + 64, b * HALF : (b + 1) * HALF]

        row_id = lax.broadcasted_iota(jnp.int32, (256, 256), 0)
        col_id = lax.broadcasted_iota(jnp.int32, (256, 256), 1)
        mask = lax.shift_right_logical(row_id, 6) == lax.shift_right_logical(col_id, 6)
        low = lax.broadcasted_iota(jnp.int32, (256, LANES), 1) < HALF

        def spread(v):
            return jnp.where(mask, jnp.concatenate([v, v], 1), 0.0).astype(bf)

        def eight(k, carry):
            at = pl.ds(pl.multiple_of(k * 256, 256), 256)
            for side, grad in enumerate(both_halves(grads[at, :])):
                to = pl.ds(pl.multiple_of(k * 256 + side * (count // 2 * BLOCK), 256), 256)
                left, right = both_halves(second[to, :])
                s32 = grad * scale
                s = s32.astype(bf)
                outer = lax.dot_general(s[:, 0:HALF], s[:, 0:HALF], (((1,), (1,)), ((), ())), preferred_element_type=f32)
                kept = jnp.where(mask, outer, 0.0)
                kept = kept[:, :LANES] + kept[:, LANES:]
                outer = kept + pltpu.roll(kept, HALF, 1)
                inner = lax.dot_general(spread(s32), s, (((0,), (0,)), ((), ())), preferred_element_type=f32)
                shaped = jnp.dot(spread(left), s, preferred_element_type=f32)
                shaped = jnp.dot(spread(shaped), right.astype(bf), preferred_element_type=f32)
                first[to, :] = jnp.where(low, grad, outer)
                second[to, :] = jnp.where(low, inner, shaped)
            return carry

        lax.fori_loop(0, count // 8, eight, 0, unroll=4)

    i0 = pl.program_id(0) * step_rows
    for load in block_loads(pl.program_id(0)):
        load.wait()
    unit = lax.broadcasted_iota(jnp.int32, (LANES, LANES), 0) == lax.broadcasted_iota(jnp.int32, (LANES, LANES), 1)
    unit = unit.astype(f32).astype(bf)

    def turned(tile):
        high = tile.astype(bf)
        rest = (tile - high.astype(f32)).astype(bf)
        over = (((1,), (1,)), ((), ()))
        return lax.dot_general(unit, high, over, preferred_element_type=f32) + lax.dot_general(
            unit, rest, over, preferred_element_type=f32
        )


    def rows_out(ii, carry):
        i = i0 + ii
        at = pl.ds(i, count, stride=BLOCK)
        one = first[at, :].T
        two = turned(second[at, :])
        out_g[ii] = one[0:HALF]
        out_sl[ii] = DECAY * held_sl[i] + (1.0 - DECAY) * one[HALF:LANES]
        out_sr[ii] = DECAY * held_sr[i] + (1.0 - DECAY) * two[0:HALF]
        fresh = BETA * held_m[i] + two[HALF:LANES]
        out_m[ii] = fresh
        out_w[ii] = held_w[i] - RATE * fresh
        return carry

    lax.fori_loop(0, step_rows, rows_out, 0, unroll=True)


def update_blocks(sums, blocks, vec_grads, vecs, results, token_total):
    views = [jnp.transpose(a, (1, 2, 0)) for a in blocks]
    count = blocks[0].shape[0]
    rows = 16
    whole = pl.BlockSpec(memory_space=pltpu.VMEM)
    steps = BLOCK // rows
    some = pl.BlockSpec((results[0].shape[0] // steps, results[0].shape[1]), lambda i: (i, 0))
    there = pl.BlockSpec(memory_space=pl.ANY)
    part = pl.BlockSpec((rows, BLOCK, count), lambda i: (i, 0, 0))
    vec = jax.ShapeDtypeStruct(vec_grads.shape, jnp.float32)
    outs = pl.pallas_call(
        functools.partial(update_kernel, token_total ** (-0.5)),
        grid=(steps,),
        out_shape=[jax.ShapeDtypeStruct((BLOCK, BLOCK, count), jnp.float32)] * 5
        + [vec] * 4
        + [jax.ShapeDtypeStruct(a.shape, a.dtype) for a in results],
        in_specs=[there] * 6 + [whole] * 4 + [some] * 2 + [there] * 4,
        out_specs=[part] * 5 + [whole] * 4 + [some] * 2,
        scratch_shapes=[
            pltpu.VMEM((count // 2 * BLOCK, LANES), jnp.float32),
            pltpu.VMEM((count * BLOCK, LANES), jnp.float32),
            pltpu.VMEM((count * BLOCK, LANES), jnp.float32),
            *[pltpu.VMEM((BLOCK, BLOCK, count), jnp.float32)] * 6,
            *[pltpu.VMEM(a.shape, a.dtype) for a in sums],
            pltpu.SemaphoreType.DMA((4, 2)),
            pltpu.SemaphoreType.DMA((BLOCK // rows, 4)),
            pltpu.SemaphoreType.DMA((4,)),
        ],
        compiler_params=pltpu.CompilerParams(vmem_limit_bytes=VMEM_LIMIT),
        name="update_blocks",
    )(*sums, *views[4:], vec_grads, *vecs, *results, *views[:4])
    return [jnp.transpose(a, (2, 0, 1)) for a in outs[:5]], outs[5:9], outs[9:]


DEPTH = 4


def layer_kernel(
    lengths,
    order,
    view,
    tokens_in,
    cot_in,
    vecs,
    mixed_there,
    input_grad_there,
    out_q,
    out_o,
    out_i,
    out_d,
    vec_grads,
    tokens,
    cot,
    mixed,
    input_grad,
    sum_q,
    sum_o,
    sum_i,
    sum_d,
    gq,
    go,
    gi,
    gd,
    wqkv,
    cq,
    co,
    ci,
    cd,
    yq,
    yo,
    yi,
    yd,
    yv,
    zq,
    zo,
    zi,
    zd,
    zv,
    rows_one,
    rows_two,
    rows_t,
    grad_rows,
    grad_attn,
    probs,
    qkv,
    ctx,
    gctx,
    far,
    inx,
    go_x,
    ctx_x,
    macc,
    nacc,
    act,
    gin,
    bias_sum,
    qkv_bias,
    qv_sum,
    vin,
    vout,
    late,
    late_sum,
    late_in,
    recv,
    send_y,
    send_c,
    send_z,
    rc_recv,
    rc_send,
    ry_recv,
    ry_send,
    rz_recv,
    rz_send,
    x_send,
    x_recv,
    v_send,
    v_recv,
    l_send,
    l_recv,
    copy_sem,
):
    bf, f32 = jnp.bfloat16, jnp.float32
    z, y, c, t = place()
    me = slot_of(z, y, c)
    x_peer = (me, 1 - t)
    y_peer = (slot_of(z, 1 - y, c), t)
    c_peer = (slot_of(z, y, 1 - c), t)
    rows = tokens.shape[0]
    own = pl.ds(pl.multiple_of(t * rows, rows), rows)
    other = pl.ds(pl.multiple_of((1 - t) * rows, rows), rows)

    def lanes(start, size, unit):
        return pl.ds(pl.multiple_of(start, unit), size)

    gathered, core_in = (gq, go, gi, gd), (cq, co, ci, cd)
    y_in, z_in = (yq, yo, yi, yd, yv), (zq, zo, zi, zd, zv)
    sums = (sum_q, sum_o, sum_i, sum_d)
    Q, O, I, W, V = range(5)

    def dot(a, b):
        return jnp.dot(a, b, preferred_element_type=f32)

    def dot_nt(a, b):
        return lax.dot_general(a, b, (((1,), (1,)), ((), ())), preferred_element_type=f32)

    def dot_tn(a, b):
        return lax.dot_general(a, b, (((0,), (0,)), ((), ())), preferred_element_type=f32)

    def piece(k, zz, yy, cc):
        if k == O:
            return go.at[zz * 2 + yy, :, pl.ds(pl.multiple_of(cc * 512, 512), 512)]
        return gathered[k].at[slot_of(zz, yy, cc)]

    def near(s):
        return lax.rem(z + (1 - 2 * lax.div(z, 2)) * s + DEPTH, DEPTH)

    def ag_piece(k, zz, yy, cc):
        if k == W:
            return gd.at[slot_of(zz, yy, cc), 0:HALF]
        if k == V:
            return gd.at[slot_of(zz, yy, cc), HALF:LANES]
        return piece(k, zz, yy, cc)

    def ag_copy(k, zz, yy, way):
        src = ag_piece(k, zz, yy, c)
        sem = recv.at[k, slot_of(zz, yy, c)]
        if way == "up":
            return remote(src, src, send_z.at[k, 0, yy * DEPTH + zz], sem, (slot_of(z + 1, y, c), t))
        if way == "down":
            return remote(src, src, send_z.at[k, 1, yy * DEPTH + zz], sem, (slot_of(z - 1, y, c), t))
        if way == "y":
            return remote(src, src, send_y.at[k, zz], sem, y_peer)
        return remote(src, src, send_c.at[k, yy * DEPTH + zz], sem, c_peer)

    def ag_wait(k, zz, yy, cc):
        ref = ag_piece(k, zz, yy, cc)
        remote(ref, ref, send_y.at[k, 0], recv.at[k, slot_of(zz, yy, cc)], y_peer).wait_recv()

    def own_sends_z(k):
        @pl.when(z < DEPTH - 1)
        def _():
            ag_copy(k, z, y, "up").start()

        @pl.when(z > 0)
        def _():
            ag_copy(k, z, y, "down").start()

        ag_copy(k, z, y, "core").start()

    def own_sends_y(k):
        ag_copy(k, z, y, "y").start()

    def z_arrival(kinds, dist):
        @pl.when(z >= dist)
        def _():
            for k in kinds:
                ag_wait(k, z - dist, y, c)

                @pl.when(z < DEPTH - 1)
                def _():
                    ag_copy(k, z - dist, y, "up").start()

                ag_copy(k, z - dist, y, "y").start()
                ag_copy(k, z - dist, y, "core").start()

        @pl.when(z + dist < DEPTH)
        def _():
            for k in kinds:
                ag_wait(k, z + dist, y, c)

                @pl.when(z > 0)
                def _():
                    ag_copy(k, z + dist, y, "down").start()

                ag_copy(k, z + dist, y, "y").start()
                ag_copy(k, z + dist, y, "core").start()

    def y_arrival(kinds, dist):
        def one(zz):
            for k in kinds:
                ag_wait(k, zz, 1 - y, c)
                ag_copy(k, zz, 1 - y, "core").start()

        if dist == 0:
            one(z)
            return

        @pl.when(z >= dist)
        def _():
            one(z - dist)

        @pl.when(z + dist < DEPTH)
        def _():
            one(z + dist)

    def v_forward(zz, yy):
        ag_wait(V, zz, yy, c)

        @pl.when((zz <= z) & (z < DEPTH - 1))
        def _():
            ag_copy(V, zz, yy, "up").start()

        @pl.when((zz >= z) & (z > 0))
        def _():
            ag_copy(V, zz, yy, "down").start()

        ag_copy(V, zz, yy, "core").start()

    def v_arrival(dist):
        for yy in (y, 1 - y):

            @pl.when(z >= dist)
            def _():
                v_forward(z - dist, yy)

            @pl.when(z + dist < DEPTH)
            def _():
                v_forward(z + dist, yy)

    def drain(k, zz, yy):
        ag_copy(k, zz, yy, "core").wait_send()
        if k == V:

            @pl.when((yy == y) & (zz == z))
            def _():
                ag_copy(k, zz, yy, "y").wait_send()

            @pl.when((zz <= z) & (z < DEPTH - 1))
            def _():
                ag_copy(k, zz, yy, "up").wait_send()

            @pl.when((zz >= z) & (z > 0))
            def _():
                ag_copy(k, zz, yy, "down").wait_send()

            return

        @pl.when(yy == y)
        def _():
            ag_copy(k, zz, y, "y").wait_send()

            @pl.when((zz <= z) & (z < DEPTH - 1))
            def _():
                ag_copy(k, zz, y, "up").wait_send()

            @pl.when((zz >= z) & (z > 0))
            def _():
                ag_copy(k, zz, y, "down").wait_send()

    def add(dst, *terms):
        count, width = dst.shape
        step = min(count, 256 * LANES // width)

        def body(i, carry):
            at = pl.ds(pl.multiple_of(i * step, 16), step)
            if len(terms) == 2 and dst.dtype == bf:
                dst[at, :] = terms[0][at, :] + terms[1][at, :]
                return carry
            total = terms[0][at, :].astype(f32)
            for term in terms[1:]:
                total = total + term[at, :].astype(f32)
            dst[at, :] = total.astype(dst.dtype)
            return carry

        lax.fori_loop(0, count // step, body, 0, unroll=2)

    side = lax.div(z, 2)
    end_z, inner_z = 3 * side, 1 + side
    is_end = z == end_z

    def rc_copy(k, zz, yy):
        at = zz * 2 + yy
        return remote(piece(k, zz, yy, 1 - c), core_in[k].at[at], rc_send.at[k, at], rc_recv.at[k, at], c_peer)

    def ry_copy(k, zz):
        if k == V:
            return remote(ag_piece(V, z, 1 - y, c), y_in[V].at[0], ry_send.at[V, 0], ry_recv.at[V, 0], y_peer)
        return remote(ag_piece(k, zz, 1 - y, c), y_in[k].at[zz], ry_send.at[k, zz], ry_recv.at[k, zz], y_peer)

    def z_slot(k, slot, yy):
        return z_in[k].at[slot * 2 + yy if k == V else slot]

    def z_sem(slot, yy):
        return slot * 2 + yy

    def rz_copy(k, s, yy, from_end):
        slot = s - 1 if from_end else {3: 0, 2: 1, 1: 3}[s]
        to = inner_z if from_end else {3: end_z, 2: 3 - end_z, 1: 3 - inner_z}[s]
        sent, landed = rz_send.at[k, (s - 1) * 2 + yy], rz_recv.at[k, z_sem(slot, yy)]
        return remote(ag_piece(k, near(s), yy, c), z_slot(k, slot, yy), sent, landed, (slot_of(to, y, c), t))

    def z_landed(k, slot, yy):
        ref = z_slot(k, slot, yy)
        remote(ref, ref, rz_send.at[k, 0], rz_recv.at[k, z_sem(slot, yy)], y_peer).wait_recv()
        return ref

    def y_landed(k, zz):
        ref = y_in[k].at[0 if k == V else zz]
        remote(ref, ref, ry_send.at[k, 0], ry_recv.at[k, 0 if k == V else zz], y_peer).wait_recv()
        return ref

    def rc_add(k, zz, yy):
        at = zz * 2 + yy
        remote(core_in[k].at[at], core_in[k].at[at], rc_send.at[k, 0], rc_recv.at[k, at], c_peer).wait_recv()
        mine = piece(k, zz, yy, c)
        add(mine, mine, core_in[k].at[at])

        @pl.when(yy != y)
        def _():
            ry_copy(k, zz).start()

    def z_step(k, s, yy, *terms):
        mine = ag_piece(k, near(s), yy, c)
        if terms:
            add(mine, mine, *terms)

        @pl.when(is_end)
        def _():
            rz_copy(k, s, yy, True).start()

        if s == 3:

            @pl.when(jnp.logical_not(is_end))
            def _():
                rz_copy(k, s, yy, False).start()

    def z_merge(k, s, yy):
        @pl.when(jnp.logical_not(is_end))
        def _():
            mine = ag_piece(k, near(s), yy, c)
            add(mine, mine, z_landed(k, s, yy))
            rz_copy(k, s, yy, False).start()

    def ry_add(k, s):
        z_step(k, s, y, y_landed(k, near(s)))

    def ry_merge(k, s):
        z_merge(k, s, y)

    def total_of(k):
        return sum_d.at[(k - W) * HALF : (k - W + 1) * HALF] if k >= W else sums[k]

    def z_total(k, yy, dst, *terms):
        mine = ag_piece(k, z, yy, c)
        first = z_landed(k, 0, yy)

        @pl.when(is_end)
        def _():
            add(dst, mine, first, z_landed(k, 1, yy), *terms)

        @pl.when(jnp.logical_not(is_end))
        def _():
            add(dst, mine, first, z_landed(k, 3, yy), *terms)

    def own_total(k):
        z_total(k, y, total_of(k), y_landed(k, z))

    def v_cross():
        mine = ag_piece(V, z, 1 - y, c)
        z_total(V, 1 - y, mine)
        ry_copy(V, z).start()

    def x_rows(ref, index):
        return remote(ref.at[own], ref.at[own], x_send.at[index], x_recv.at[index], x_peer)

    def x_rows_wait(ref, index):
        remote(ref.at[other], ref.at[other], x_send.at[index], x_recv.at[index], x_peer).wait_recv()

    def x_part(index):
        slot = 1 if index == 2 else 0
        return remote(far.at[slot], inx.at[slot], x_send.at[5 + index], x_recv.at[5 + index], x_peer)

    def by_rows(body, step=64):
        def run(i, carry):
            body(pl.multiple_of(i * step, step), step)
            return carry

        lax.fori_loop(0, rows // step, run, 0)

    def norm(value):
        average = jnp.mean(value, -1, keepdims=True)
        centred = value - average
        inverse = lax.rsqrt(jnp.mean(centred * centred, -1, keepdims=True) + EPS)
        return centred * inverse, inverse

    def norm_grad(grad, unit, inverse, gain):
        scaled = grad * gain
        return inverse * (
            scaled - jnp.mean(scaled, -1, keepdims=True) - unit * jnp.mean(scaled * unit, -1, keepdims=True)
        )

    def x_out():
        half = (slice(None), slice(None), lanes(c * 512, 512, 512))
        return remote(go.at[half], go_x.at[half], x_send.at[4], x_recv.at[4], x_peer)

    def x_out_core(cc):
        half = (slice(None), slice(None), lanes(cc * 512, 512, 512))
        return remote(go_x.at[half], go_x.at[half], x_send.at[9], x_recv.at[9], c_peer)

    def x_grad_context():
        return remote(ctx_x, gctx.at[own], x_send.at[10], x_recv.at[10], x_peer)

    def x_grad_context_wait():
        remote(gctx.at[other], gctx.at[other], x_send.at[10], x_recv.at[10], x_peer).wait_recv()

    stages = (x_peer, c_peer, y_peer)

    def v_copy(stage):
        return remote(vout.at[1 + stage], vin.at[stage], v_send.at[stage], v_recv.at[stage], stages[stage])

    def vz_copy(step):
        peer = (slot_of(lax.rem(z + step, DEPTH), y, c), t)
        return remote(vout.at[4], vin.at[3 + z], v_send.at[2 + step], v_recv.at[3 + z], peer)

    def early_rows(hop):
        if hop == 0:
            vout[1] = vout[0]
        else:
            v_copy(hop - 1).wait_recv()
            vout[1 + hop] = vout[hop] + vin[hop - 1]
        if hop < 3:
            v_copy(hop).start()
        else:
            for step in range(1, DEPTH):
                vz_copy(step).start()
            vin[3 + z] = vout[4]

    def late_turn(turn):
        dx, dy, dc = turn // 4, turn // 2 % 2, turn % 2
        xx, yy, cc = (1 - t if dx else t), (1 - y if dy else y), (1 - c if dc else c)
        return (slot_of(z, yy, cc), xx), xx * 4 + yy * 2 + cc

    def late_copy(turn):
        here = t * 4 + y * 2 + c
        return remote(late, late_in.at[here], l_send.at[turn], l_recv.at[here], late_turn(turn)[0])

    def late_wait(index):
        remote(late_in.at[index], late_in.at[index], l_send.at[0], l_recv.at[index], y_peer).wait_recv()

    def late_z(step):
        peer = (slot_of(lax.rem(z + step, DEPTH), y, c), t)
        return remote(late_sum, late_in.at[8 + z], l_send.at[7 + step], l_recv.at[8 + z], peer)

    stores = [
        pltpu.make_async_copy(a, b, copy_sem.at[6 + n])
        for n, (a, b) in enumerate(
            (
                (sum_q, out_q),
                (sum_o, out_o),
                (sum_i, out_i),
                (sum_d, out_d),
                (mixed, mixed_there),
                (input_grad, input_grad_there),
            )
        )
    ]

    barrier = pltpu.get_barrier_semaphore()
    z_peers = [(slot_of(lax.rem(z + step, DEPTH), y, c), t) for step in range(1, DEPTH)]
    everyone = [late_turn(turn)[0] for turn in range(1, 8)] + z_peers
    for device in everyone:
        pl.semaphore_signal(barrier, inc=1, device_id=device, device_id_type=MESH_ID)

    row_loads = [pltpu.make_async_copy(tokens_in, tokens, copy_sem.at[4]), pltpu.make_async_copy(cot_in, cot, copy_sem.at[5])]

    def prepare(held, stack):
        parts = [pl.ds(16 * k, 16) for k in range(4)]
        loads = [pltpu.make_async_copy(view.at[part], held.at[part], copy_sem.at[k]) for k, part in enumerate(parts)]
        for load in loads:
            load.start()
        for load in row_loads:
            load.start()

        def first_norm(at, step):
            unit, inverse = norm(tokens[pl.ds(at, step), :])
            to = pl.ds(pl.multiple_of(t * rows + at, step), step)
            rows_one[to, :] = (unit * vecs[0:1, :] + vecs[1:2, :]).astype(bf)
            grad_rows[to, :] = cot[pl.ds(at, step), :].astype(bf)

        for k, load in enumerate(loads):
            load.wait()
            lay_blocks(held, stack, 16 * k, 16 * k + 16)

        def pair(left, right, count, left_high=False, right_high=False):
            first, second = stack[left : left + count, :], stack[right : right + count, :]
            first = pltpu.roll(first, HALF, 1) if left_high else first
            second = second if right_high else pltpu.roll(second, HALF, 1)
            lane = lax.broadcasted_iota(jnp.int32, (count, LANES), 1)
            return jnp.where(lane < HALF, first, second).astype(bf)

        n = gq.shape[1]
        gq[me] = pair(0, n, n)
        base = 2 * n
        wide = [pair(base + b * 64, base + b * 64 + 64, 64) for b in range(0, 8, 2)]
        go[z * 2 + y, :, lanes(c * 512, 512, 512)] = jnp.concatenate(wide, 1)
        pl.semaphore_wait(barrier, len(everyone))
        for k in (Q, O):
            own_sends_y(k)
            own_sends_z(k)
        for load in row_loads:
            load.wait()
        by_rows(first_norm)
        x_rows(rows_one, 0).start()
        base += 512
        gi[me] = pair(base, 0, D, right_high=True)
        for r in range(2):
            for b in range(0, 16, 2):
                at = D + (r * 16 + b) * 64
                gd[me, r * 64 : r * 64 + 64, b * HALF : b * HALF + LANES] = pair(at, at + 64, 64, True, True)

    pl.run_scoped(
        prepare,
        pltpu.VMEM(view.shape, f32),
        pltpu.VMEM((view.shape[2] // 2 * BLOCK, LANES), f32),
    )
    x_rows(grad_rows, 1).start()
    z_arrival((Q, O), 1)
    y_arrival((Q, O), 0)
    z_arrival((Q, O), 2)
    for k in (I, W, V):
        own_sends_z(k)
    own_sends_y(I)
    y_arrival((Q, O), 1)

    def core_waits(kinds, zz):
        for k in kinds:
            for yy in (y, 1 - y):
                ag_wait(k, zz, yy, 1 - c)

    x_rows_wait(rows_one, 0)

    ends = []
    for p in range(ARTICLES):
        length = 0
        for a in range(ARTICLES):
            length = length + jnp.where(order[0, p] == a, lengths[0, a], 0)
        ends.append(length + ends[-1] if p else length)

    def allowed(first, count):
        ids = lax.broadcasted_iota(jnp.int32, (rows, 1), 0) + first
        start = jnp.zeros((rows, 1), jnp.int32)
        for end in ends:
            start = jnp.where(ids >= end, end, start)
        start = jnp.where(ids >= ends[-1], ids, start)
        keys = lax.broadcasted_iota(jnp.int32, (rows, count), 1)
        return (keys <= ids) & (keys >= start)

    scale = HD ** (-0.5)
    strip = 1024

    def assemble(h):
        for yy in range(2):
            even, odd = gq.at[slot_of(h, yy, 0)], gq.at[slot_of(h, yy, 1)]
            at = yy * 192
            wqkv[h, 0:768, at : at + 64] = even[:, 0:64]
            wqkv[h, 768:1024, at : at + 64] = even[0:256, 64:128]
            wqkv[h, 0:512, at + 64 : at + 128] = even[256:768, 64:128]
            wqkv[h, 512:1024, at + 64 : at + 128] = odd[0:512, 0:64]
            wqkv[h, 0:256, at + 128 : at + 192] = odd[512:768, 0:64]
            wqkv[h, 256:1024, at + 128 : at + 192] = odd[:, 64:128]

    def disassemble(h, value):
        for yy in range(2):
            even, odd = gq.at[slot_of(h, yy, 0)], gq.at[slot_of(h, yy, 1)]
            at = yy * 192
            even[:, 0:64] = value[0:768, at : at + 64]
            even[0:256, 64:128] = value[768:1024, at : at + 64]
            even[256:768, 64:128] = value[0:512, at + 64 : at + 128]
            odd[0:512, 0:64] = value[512:1024, at + 64 : at + 128]
            odd[512:768, 0:64] = value[0:256, at + 128 : at + 192]
            odd[:, 64:128] = value[256:1024, at + 128 : at + 192]

    qv = vecs[pl.ds(6 + t, 1), :]
    for h in range(DEPTH):
        none = jnp.zeros((1, HD), f32)
        qkv_bias[h] = jnp.concatenate([qv[:, h * 256 : h * 256 + 128], none, qv[:, h * 256 + 128 : h * 256 + 256]], 1)

    def head(h):
        core_waits((Q,), h)
        assemble(h)
        qkv[h] = (dot(rows_one[...], wqkv[h]) + qkv_bias[h]).astype(bf)
        for block in range(2):
            at, seen = slice(block * rows, (block + 1) * rows), (block + 1) * rows
            scores = dot_nt(qkv[h, at, 0:128], qkv[h, 0:seen, 128:256]) * scale
            scores = jnp.where(allowed(block * rows, seen), scores, NEG)
            expo = jnp.exp(scores - jnp.max(scores, -1, keepdims=True))
            low = (expo * (1.0 / jnp.sum(expo, -1, keepdims=True))).astype(bf)
            probs[h, at, 0:seen] = low
            ctx[at, lanes(h * HD, HD, HD)] = dot(low, qkv[h, 0:seen, 256:384]).astype(bf)

    head(near(0))
    y_arrival((Q, O), 2)
    z_arrival((Q, O), 3)
    y_arrival((Q, O), 3)
    own_sends_y(W)
    head(near(1))
    own_sends_y(V)
    head(near(2))
    z_arrival((I, W), 1)
    head(near(3))
    y_arrival((I, W), 0)
    for zz in range(DEPTH):
        core_waits((O,), zz)
    def w_out(ref):
        return ref[...].reshape(DEPTH * HD, D)
    far[0] = dot(ctx[other, :], w_out(go)).astype(bf)
    x_part(0).start()
    mixed[...] = tokens[...] + dot(ctx[own, :], w_out(go)) + vecs[4:5, :]
    z_arrival((I, W), 2)
    x_part(0).wait_recv()
    def second_norm(at, step):
        value = mixed[pl.ds(at, step), :] + inx[0, pl.ds(at, step), :].astype(f32)
        mixed[pl.ds(at, step), :] = value
        unit, inverse = norm(value)
        to = pl.ds(pl.multiple_of(t * rows + at, step), step)
        rows_two[to, :] = (unit * vecs[2:3, :] + vecs[3:4, :]).astype(bf)
    x_rows_wait(grad_rows, 1)
    by_rows(second_norm)
    x_rows(rows_two, 2).start()
    v_forward(z, 1 - y)
    macc[...] = jnp.zeros_like(macc)
    y_arrival((I, W), 1)
    nacc[...] = jnp.zeros_like(nacc)
    vout[...] = jnp.zeros_like(vout)
    z_arrival((I, W), 3)
    def ffn(half, zz):
        first = 4 * zz
        at = pl.ds(pl.multiple_of(lax.rem(t + half, 2) * rows, rows), rows)
        units = lanes(zz * 512, 512, 512)
        bias_row = vecs[pl.ds(8 + 2 * t + lax.div(zz, 2), 1), lanes(lax.rem(zz, 2) * 512, 512, 512)]

        def w_in(start, count):
            return jnp.concatenate([gi[first + j, start : start + count, :] for j in range(4)], 1)

        def w_down(start, count):
            return gd[pl.ds(first, 4), :, start : start + count].reshape(512, count)

        inner = dot(rows_two[at, :], w_in(0, D)) + bias_row
        square = inner * inner
        bent = jnp.tanh(GELU_A * inner * (1.0 + GELU_B * square))
        act[at, units] = (0.5 * inner * (1.0 + bent)).astype(bf)
        slope = 0.5 * (1.0 + bent) + 0.5 * inner * (1.0 - bent * bent) * (GELU_A * (1.0 + 3.0 * GELU_B * square))
        gin[at, units] = (dot_nt(grad_rows[at, :], w_down(0, D)) * slope).astype(bf)
        for nb in range(4):
            out = slice(nb * 256, nb * 256 + 256)
            nacc[at, out] += dot_nt(gin[at, units], w_in(nb * 256, 256))
            macc[at, out] += dot(act[at, units], w_down(nb * 256, 256))
    def ffn_grads(zz):
        first = 4 * zz
        units = lanes(zz * 512, 512, 512)
        for k in (I, W, V):
            for yy in range(2):
                drain(k, zz, yy)
        bias_sum[zz] = jnp.sum(gin[:, units].astype(f32), 0, keepdims=True)
        for nb in range(4):
            out = slice(nb * 256, nb * 256 + 256)
            part = dot(rows_t[out, :], gin[:, units]).astype(bf)
            for j in range(4):
                gi[first + j, out, :] = part[:, j * LANES : (j + 1) * LANES]
        for yy in (1 - y, y):
            rc_copy(I, zz, yy).start()
        act_t = act[:, units].T
        for nb in range(4):
            out = slice(nb * 256, nb * 256 + 256)
            part = dot(act_t, grad_rows[:, out]).astype(bf)
            gd[pl.ds(first, 4), :, out] = part.reshape(4, LANES, 256)
        for yy in (1 - y, y):
            rc_copy(W, zz, yy).start()
    def each(kinds, step, *args):
        for k in kinds:
            step(k, *args)
    def reduce_out():
        for yy in (1 - y, y):
            for s in (3, 2, 1, 0):
                rc_add(O, near(s), yy)
    def reduce_head(zz):
        for yy in (1 - y, y):
            rc_add(Q, zz, yy)
    v_arrival(1)
    def reduce_core(zz):
        for yy in (1 - y, y):
            for k in (I, W):
                rc_add(k, zz, yy)
    def v_step(s):
        for yy in (1 - y, y):
            z_step(V, s, yy)
    def v_merge(s):
        for yy in (1 - y, y):
            z_merge(V, s, yy)
    core_waits((I, W, V), z)
    ffn(0, z)
    core_waits((I, W, V), near(1))
    ffn(0, near(1))
    x_rows_wait(rows_two, 2)
    x_out().start()
    v_arrival(2)
    rows_t[...] = rows_two[...].T
    y_arrival((I, W), 2)
    def by_z(s, carry):
        @pl.when(s == 2)
        def _():
            v_arrival(3)
            y_arrival((I, W), 3)

        @pl.when(s >= 2)
        def _():
            core_waits((I, W, V), near(s))
            ffn(0, near(s))

        ffn(1, near(s))

        @pl.when(s == DEPTH - 1)
        def _():
            x_part(0).wait_send()
            far[0] = nacc[other, :].astype(bf)
            x_part(1).start()

        ffn_grads(near(s))

        @pl.when(s > 0)
        def _():
            reduce_core(near(s - 1))

        for before in (1, 2):

            @pl.when(s == before + 1)
            def _():
                v_step(before)

        return carry
    lax.fori_loop(0, DEPTH, by_z, 0)
    x_out().wait_recv()
    reduce_core(near(3))
    x_out_core(c).start()
    v_step(3)
    rows_t[...] = rows_one[...].T
    for zz in range(DEPTH):
        for side in range(2):
            row, start = 8 + 2 * side + zz // 2, zz % 2 * 512
            vout[0, row : row + 1, start : start + 512] = jnp.where(t == side, bias_sum[zz], 0.0)
    v_merge(1)
    x_part(1).wait_recv()
    def row_sum(row, value):
        vout[0, row : row + 1, :] += jnp.sum(value, 0, keepdims=True)
    def second_back(at, step):
        here = pl.ds(at, step)
        in_group = pl.ds(pl.multiple_of(t * rows + at, step), step)
        grad = nacc[in_group, :] + inx[0, here, :].astype(f32)
        unit, inverse = norm(mixed[here, :])
        back = cot[here, :] + norm_grad(grad, unit, inverse, vecs[2:3, :])
        input_grad[here, :] = back
        grad_attn[in_group, :] = back.astype(bf)
        row_sum(2, grad * unit)
        row_sum(3, grad)
        row_sum(4, back)
        row_sum(5, cot[here, :])
    by_rows(second_back)
    early_rows(0)
    x_out_core(1 - c).wait_recv()
    ctx_x[...] = dot_nt(grad_attn[own, :], w_out(go_x)).astype(bf)
    x_grad_context().start()
    gctx[own, :] = dot_nt(grad_attn[own, :], w_out(go)).astype(bf)
    each((I, W), ry_add, 1)
    v_merge(2)
    each((I, W), ry_add, 2)
    for zz in range(DEPTH):
        for yy in range(2):
            drain(O, zz, yy)
            drain(Q, zz, yy)
    def mixed_out(at, step):
        here = pl.ds(at, step)
        in_group = pl.ds(pl.multiple_of(t * rows + at, step), step)
        mixed[here, :] = mixed[here, :] + macc[in_group, :] + inx[1, here, :].astype(f32) + vecs[5:6, :]
    x_out().wait_send()
    x_grad_context_wait()
    far[1] = macc[other, :].astype(bf)
    x_rows(grad_attn, 3).start()
    def out_grads():
        x_rows_wait(grad_attn, 3)
        ctx_t = ctx[...].T
        for nb in range(4):
            at = slice(nb * 256, nb * 256 + 256)
            go[:, :, at] = dot(ctx_t, grad_attn[:, at]).astype(bf).reshape(8, 64, 256)
        for zz in range(DEPTH):
            for yy in range(2):
                rc_copy(O, zz, yy).start()
    def first_back(at, step):
        here = pl.ds(at, step)
        in_group = pl.ds(pl.multiple_of(t * rows + at, step), step)
        grad = nacc[in_group, :] + inx[0, here, :].astype(f32)
        unit, inverse = norm(tokens[here, :])
        input_grad[here, :] = input_grad[here, :] + norm_grad(grad, unit, inverse, vecs[0:1, :])
        row_sum(0, grad * unit)
        row_sum(1, grad)
    def finish_mixed():
        x_part(2).wait_recv()
        by_rows(mixed_out)
        stores[4].start()
    def finish_input():
        x_part(3).wait_recv()
        by_rows(first_back)
        stores[5].start()
    late_rows = (0, 1, 6, 7)
    v_cross()
    def late_start():
        for h in range(DEPTH):
            for row in range(2):
                total = jnp.where(t == row, qv_sum[h], 0.0)
                vout[0, 6 + row : 7 + row, h * 256 : h * 256 + 128] = total[:, 0:128]
                vout[0, 6 + row : 7 + row, h * 256 + 128 : h * 256 + 256] = total[:, 256:384]
        for at, row in enumerate(late_rows):
            for j in range(8):
                late[at * 8 + j : at * 8 + j + 1, :] = vout[0, row : row + 1, j * LANES : (j + 1) * LANES]
        late_in[t * 4 + y * 2 + c] = late[...]
        for turn in range(1, 8):
            late_copy(turn).start()
    def late_cross():
        for turn in range(1, 8):
            late_wait(late_turn(turn)[1])
        total = late_in[0]
        for index in range(1, 8):
            total = total + late_in[index]
        late_sum[...] = total
        late_in[8 + z] = total
        for step in range(1, DEPTH):
            late_z(step).start()
    def vec_finish():
        for step in range(1, DEPTH):
            zz = lax.rem(z + step, DEPTH)
            late_wait(8 + zz)
            remote(vin.at[3 + zz], vin.at[3 + zz], v_send.at[0], v_recv.at[3 + zz], y_peer).wait_recv()
        total = ((late_in[8] + late_in[9]) + late_in[10]) + late_in[11]
        early = ((vin[3] + vin[4]) + vin[5]) + vin[6]
        vec_grads[...] = early[0 : vec_grads.shape[0]]
        for at, row in enumerate(late_rows):
            for j in range(8):
                vec_grads[row : row + 1, j * LANES : (j + 1) * LANES] = total[at * 8 + j : at * 8 + j + 1, :]
    def head_back(h, turn):
        q0, q1 = qkv[h, 0:rows, 0:128], qkv[h, rows : 2 * rows, 0:128]
        grads = []
        for block in range(2):
            at, seen = slice(block * rows, (block + 1) * rows), (block + 1) * rows
            low = probs[h, at, 0:seen]
            given = gctx[at, lanes(h * HD, HD, HD)]
            prob = low.astype(f32)
            grad_probs = dot_nt(given, qkv[h, 0:seen, 256:384])
            delta = jnp.sum(prob * grad_probs, -1, keepdims=True)
            grad_scores = (prob * (grad_probs - delta)).astype(bf)
            grad_q = dot(grad_scores, qkv[h, 0:seen, 128:256]) * scale
            grad_k = dot_tn(grad_scores, q1 if block else q0) * scale
            grad_v = dot_tn(low, given)
            grads.append((grad_q, grad_k, grad_v))
        (gq0, gk0, gv0), (gq1, gk1, gv1) = grads
        top = jnp.concatenate([gq0, gk0 + gk1[0:rows], gv0 + gv1[0:rows]], 1).astype(bf)
        low_half = jnp.concatenate([gq1, gk1[rows:], gv1[rows:]], 1).astype(bf)
        qkv[h, 0:rows, :] = top
        qkv[h, rows : 2 * rows, :] = low_half
        total = jnp.sum(top.astype(f32), 0, keepdims=True) + jnp.sum(low_half.astype(f32), 0, keepdims=True)
        qv_sum[h] = total
        for half in (other, own):
            product = dot_nt(qkv[h, half, :], wqkv[h])
            if turn == 0:
                nacc[half, :] = product
            else:
                nacc[half, :] += product
            if turn == DEPTH - 1 and half is other:
                x_part(1).wait_send()
                far[0] = nacc[other, :].astype(bf)
                x_part(3).start()
        part = dot(rows_t[...], qkv[h]).astype(bf)
        disassemble(h, part)
        for yy in (1 - y, y):
            rc_copy(Q, h, yy).start()
    early_rows(1)
    head_back(near(3), 0)
    early_rows(2)
    head_back(near(2), 1)
    early_rows(3)
    x_part(2).start()
    reduce_head(near(3))
    each((I, W), ry_add, 3)
    each((I, W), ry_merge, 1)
    out_grads()
    reduce_head(near(2))
    head_back(near(1), 2)
    reduce_out()
    each((I, W), ry_merge, 2)
    head_back(z, 3)
    ry_add(Q, 3)
    finish_mixed()
    reduce_head(near(1))
    ry_add(Q, 2)
    ry_add(O, 3)
    ry_add(Q, 1)
    ry_add(O, 2)
    ry_merge(Q, 2)
    reduce_head(z)
    ry_merge(Q, 1)
    ry_add(O, 1)
    own_total(W)
    finish_input()
    late_start()
    ry_merge(O, 2)
    late_cross()
    z_total(V, y, total_of(V), y_landed(V, z))
    ry_merge(O, 1)
    own_total(Q)
    stores[Q].start()
    own_total(I)
    stores[I].start()
    vec_finish()
    own_total(O)
    stores[O].start()

    stores[W].start()
    for stage in range(3):
        v_copy(stage).wait_send()
    for turn in range(1, 8):
        late_copy(turn).wait_send()
    for step in range(1, DEPTH):
        vz_copy(step).wait_send()
        late_z(step).wait_send()
    for index, ref in enumerate((rows_one, grad_rows, rows_two, grad_attn)):
        x_rows(ref, index).wait_send()
    for index in (2, 3):
        x_part(index).wait_send()
    x_out_core(c).wait_send()
    x_grad_context().wait_send()
    for k in range(4):
        for zz in range(DEPTH):
            for yy in range(2):
                rc_copy(k, zz, yy).wait_send()
            ry_copy(k, zz).wait_send()
        for s in range(1, DEPTH):
            rz_copy(k, s, y, True).wait_send()
    for store in stores:
        store.wait()
    ry_copy(V, z).wait_send()
    for yy in range(2):
        for s in range(1, DEPTH):
            rz_copy(V, s, yy, True).wait_send()


def run_layer(tokens, cotangent, lengths, order, weights, vec_params):
    bf, f32 = jnp.bfloat16, jnp.float32
    rows = tokens.shape[0]
    group = 2 * rows
    owners = 16
    shapes = piece_shapes()
    view = jnp.transpose(weights, (1, 2, 0))
    there = pl.BlockSpec(memory_space=pl.ANY)
    vmem = pl.BlockSpec(memory_space=pltpu.VMEM)
    smem = pl.BlockSpec(memory_space=pltpu.SMEM)

    halved = shapes[:3] + ((HALF, D),)

    def many(count, kinds):
        return [pltpu.VMEM((count,) + s, bf) for s in kinds]

    full = pltpu.VMEM((group, D), bf)
    dma = pltpu.SemaphoreType.DMA
    return pl.pallas_call(
        layer_kernel,
        out_shape=[jax.ShapeDtypeStruct((rows, D), f32)] * 2
        + [jax.ShapeDtypeStruct(s, f32) for s in shapes]
        + [jax.ShapeDtypeStruct(vec_params.shape, f32)],
        in_specs=[smem, smem] + [there] * 3 + [vmem],
        out_specs=[there] * 6 + [vmem],
        scratch_shapes=[pltpu.VMEM((rows, D), f32)] * 4
        + [pltpu.VMEM(s, f32) for s in shapes]
        + [
            pltpu.VMEM((owners,) + shapes[0], bf),
            pltpu.VMEM((owners // 2, BLOCK, D), bf),
            pltpu.VMEM((owners,) + shapes[2], bf),
            pltpu.VMEM((owners,) + shapes[3], bf),
            pltpu.VMEM((DEPTH, D, 3 * HD), bf),
        ]
        + many(2 * DEPTH, shapes)
        + many(DEPTH, halved)
        + many(1, halved[3:])
        + many(DEPTH, halved)
        + many(2 * DEPTH, halved[3:])
        + [
            full,
            full,
            pltpu.VMEM((D, group), bf),
            full,
            full,
            pltpu.VMEM((DEPTH, group, group), bf),
            pltpu.VMEM((DEPTH, group, 3 * HD), bf),
            pltpu.VMEM((group, DEPTH * HD), bf),
            pltpu.VMEM((group, DEPTH * HD), bf),
            pltpu.VMEM((2, rows, D), bf),
            pltpu.VMEM((2, rows, D), bf),
            pltpu.VMEM((owners // 2, BLOCK, D), bf),
            pltpu.VMEM((rows, DEPTH * HD), bf),
            pltpu.VMEM((group, D), f32),
            pltpu.VMEM((group, D), f32),
            pltpu.VMEM((group, 2 * D), bf),
            pltpu.VMEM((group, 2 * D), bf),
            pltpu.VMEM((DEPTH, 1, 512), f32),
            pltpu.VMEM((DEPTH, 1, 3 * HD), f32),
            pltpu.VMEM((DEPTH, 1, 3 * HD), f32),
            pltpu.VMEM((7, 16, D), f32),
            pltpu.VMEM((5, 16, D), f32),
            pltpu.VMEM((32, LANES), f32),
            pltpu.VMEM((32, LANES), f32),
            pltpu.VMEM((12, 32, LANES), f32),
            dma((5, owners)),
            dma((5, DEPTH)),
            dma((5, 2 * DEPTH)),
            dma((5, 2, 2 * DEPTH)),
            dma((4, 2 * DEPTH)),
            dma((4, 2 * DEPTH)),
            dma((5, DEPTH)),
            dma((5, DEPTH)),
            dma((5, 2 * DEPTH)),
            dma((5, 2 * DEPTH)),
            dma((11,)),
            dma((11,)),
            dma((6,)),
            dma((7,)),
            dma((11,)),
            dma((12,)),
            dma((12,)),
        ],
        compiler_params=pltpu.CompilerParams(
            collective_id=0, has_side_effects=True, vmem_limit_bytes=VMEM_LIMIT
        ),
        name="layer",
    )(lengths, order, view, tokens, cotangent, vec_params)


def per_device(
    grp_count,
    tp_count,
    tokens,
    cotangent,
    lengths,
    order,
    weights,
    momentum,
    stat_left,
    stat_right,
    root_left,
    root_right,
    vec_params,
    vec_momentum,
    vec_second,
):
    fits = grp_count == 4 * DEPTH and tp_count == 2 and tokens.shape[0] == 256
    if not fits or lengths.shape[1] != ARTICLES:
        return per_device_general(
            tokens,
            cotangent,
            lengths,
            order,
            weights,
            momentum,
            stat_left,
            stat_right,
            root_left,
            root_right,
            vec_params,
            vec_momentum,
            vec_second,
        )
    token_total = tokens.shape[0] * tp_count * grp_count
    mixed, input_grad, *sums, vec_grads = run_layer(tokens, cotangent, lengths, order, weights, vec_params)
    blocks, vecs, results = update_blocks(
        sums,
        (weights, momentum, stat_left, stat_right, root_left, root_right),
        vec_grads,
        (vec_params, vec_momentum, vec_second),
        (mixed, input_grad),
        token_total,
    )
    return (*results, *blocks, *vecs)


def solution(mesh):
    placed = (
        P(("grp", "tp"), None),
        P(("grp", "tp"), None),
        P("grp", None),
        P("grp", None),
        P(("tp", "grp"), None, None),
        P(("tp", "grp"), None, None),
        P(("tp", "grp"), None, None),
        P(("tp", "grp"), None, None),
        P(("tp", "grp"), None, None),
        P(("tp", "grp"), None, None),
        P(),
        P(),
        P(),
    )
    return jax.shard_map(
        functools.partial(per_device, mesh.shape["grp"], mesh.shape["tp"]),
        mesh=mesh,
        in_specs=placed,
        out_specs=(
            P(("grp", "tp"), None),
            P(("grp", "tp"), None),
            P(("tp", "grp"), None, None),
            P(("tp", "grp"), None, None),
            P(("tp", "grp"), None, None),
            P(("tp", "grp"), None, None),
            P(("tp", "grp"), None, None),
            P(),
            P(),
            P(),
            P(),
        ),
        check_vma=False,
    )
```

```python
import functools

import jax
import jax.numpy as jnp
from jax import lax
from jax.experimental import pallas as pl
from jax.experimental.pallas import tpu as pltpu
from jax.sharding import PartitionSpec as P

D = 1024
HEADS = 8
HD = 128
FF = 4096
BLOCK = 64


EPS = 1e-05
NEG = -1e30
DECAY = 0.9
BETA = 0.9
RATE = 0.05
VEC_DECAY = 0.9
VEC_RATE = 0.2
VEC_EPS = 1e-08


def norm_rows(value, gain, shift):
    average = jnp.mean(value, -1, keepdims=True)
    centred = value - average
    inverse = lax.rsqrt(jnp.mean(centred * centred, -1, keepdims=True) + EPS)
    normed = centred * inverse
    return (normed * gain + shift, normed, inverse)


def norm_back(grad_out, normed, inverse, gain):
    scaled = grad_out * gain
    return inverse * (
        scaled
        - jnp.mean(scaled, -1, keepdims=True)
        - normed * jnp.mean(scaled * normed, -1, keepdims=True)
    )


def segment_ids(lengths_row, order_row, group_rows):
    article_count = lengths_row.shape[0]
    slots = jnp.arange(article_count, dtype=jnp.int32)
    picks = (order_row[:, None] == slots[None, :]).astype(jnp.int32)
    packed = jnp.sum(picks * lengths_row[None, :], 1)
    ends = jnp.cumsum(packed)
    spots = jnp.arange(group_rows, dtype=jnp.int32)
    return jnp.sum((spots[:, None] >= ends[None, :]).astype(jnp.int32), 1)


def allowed_mask(row_ids, row_segs, segments, key_ids, article_count):
    causal = key_ids[None, :] <= row_ids[:, None]
    same = segments[None, :] == row_segs[:, None]
    alone = (row_segs[:, None] < article_count) | (key_ids[None, :] == row_ids[:, None])
    return causal & same & alone


def from_columns(tiles, row_total, col_total):
    return (
        tiles.reshape(col_total // BLOCK, row_total // BLOCK, BLOCK, BLOCK)
        .transpose(1, 2, 0, 3)
        .reshape(row_total, col_total)
    )


def from_rows(tiles, row_total, col_total):
    return (
        tiles.reshape(row_total // BLOCK, col_total // BLOCK, BLOCK, BLOCK)
        .transpose(0, 2, 1, 3)
        .reshape(row_total, col_total)
    )


def to_columns(matrix):
    row_total, col_total = matrix.shape
    return (
        matrix.reshape(row_total // BLOCK, BLOCK, col_total // BLOCK, BLOCK)
        .transpose(2, 0, 1, 3)
        .reshape(-1, BLOCK, BLOCK)
    )


def to_rows(matrix):
    row_total, col_total = matrix.shape
    return (
        matrix.reshape(row_total // BLOCK, BLOCK, col_total // BLOCK, BLOCK)
        .transpose(0, 2, 1, 3)
        .reshape(-1, BLOCK, BLOCK)
    )


def per_device_general(
    tokens,
    cotangent,
    lengths,
    order,
    weights,
    momentum,
    stat_left,
    stat_right,
    root_left,
    root_right,
    vec_params,
    vec_momentum,
    vec_second,
):
    groups = lax.axis_size("grp")
    tp_size = lax.axis_size("tp")
    tp_rank = lax.axis_index("tp")
    tok_rows = tokens.shape[0]
    group_rows = tok_rows * tp_size
    article_count = lengths.shape[1]
    owners = groups * tp_size
    block_area = BLOCK * BLOCK * owners
    qkv_count = 3 * D * D // block_area
    out_count = D * D // block_area
    in_count = D * FF // block_area
    owned_blocks = weights.shape[0]
    heads_here = HEADS // tp_size
    qkv_cols = 3 * D // tp_size
    feat_here = D // tp_size
    ff_here = FF // tp_size
    qv_width = 2 * D // tp_size
    token_total = group_rows * groups
    gathered = lax.all_gather(weights.astype(jnp.bfloat16), "grp", axis=0, tiled=True)
    per_owner = gathered.reshape(groups, owned_blocks, BLOCK, BLOCK)
    marks = [0, qkv_count, qkv_count + out_count, qkv_count + out_count + in_count, owned_blocks]
    pieces = [
        per_owner[:, marks[index] : marks[index + 1]].reshape(-1, BLOCK, BLOCK)
        for index in range(4)
    ]
    w_qkv = from_columns(pieces[0], D, qkv_cols)
    w_out = from_rows(pieces[1], feat_here, D)
    w_in = from_columns(pieces[2], D, ff_here)
    w_down = from_rows(pieces[3], ff_here, D)
    w_qkv_heads = w_qkv.reshape(D, heads_here, 3, HD)
    w_out_heads = w_out.reshape(heads_here, HD, D)
    segments = segment_ids(lengths[0], order[0], group_rows)
    gain_one = vec_params[0]
    shift_one = vec_params[1]
    gain_two = vec_params[2]
    shift_two = vec_params[3]
    bias_out = vec_params[4]
    bias_down = vec_params[5]
    qv_here = lax.dynamic_slice_in_dim(
        vec_params[6:8].reshape(2 * D), tp_rank * qv_width, qv_width
    ).reshape(heads_here, 2, HD)
    bias_heads = jnp.stack(
        [qv_here[:, 0], jnp.zeros((heads_here, HD), jnp.float32), qv_here[:, 1]], 0
    )[:, :, None, :]
    bias_in = lax.dynamic_slice_in_dim(vec_params[8:].reshape(FF), tp_rank * ff_here, ff_here)
    normed_one, unit_one, inverse_one = norm_rows(tokens, gain_one, shift_one)
    rows_one = lax.all_gather(normed_one.astype(jnp.bfloat16), "tp", axis=0, tiled=True)
    projected = (
        jnp.einsum("rx,xhcd->chrd", rows_one, w_qkv_heads, preferred_element_type=jnp.float32)
        + bias_heads
    ).astype(jnp.bfloat16)
    queries = projected[0]
    keys_all = projected[1]
    values_all = projected[2]
    span = min(512, group_rows)
    starts = jnp.arange(group_rows // span, dtype=jnp.int32) * span
    key_ids = jnp.arange(group_rows, dtype=jnp.int32)
    score_scale = HD ** (-0.5)

    def masked_scores(first_row):
        row_ids = first_row + jnp.arange(span, dtype=jnp.int32)
        row_segs = lax.dynamic_slice_in_dim(segments, first_row, span, 0)
        allowed = allowed_mask(row_ids, row_segs, segments, key_ids, article_count)
        query_rows = lax.dynamic_slice_in_dim(queries, first_row, span, 1)
        scores = (
            jnp.einsum("hqd,hkd->hqk", query_rows, keys_all, preferred_element_type=jnp.float32)
            * score_scale
        )
        return (jnp.where(allowed[None], scores, NEG), query_rows)

    def attend(context_buf, first_row):
        scores, query_rows = masked_scores(first_row)
        row_max = jnp.max(scores, -1, keepdims=True)
        expo = jnp.exp(scores - row_max)
        expsum = jnp.sum(expo, -1, keepdims=True)
        probs_low = (expo / expsum).astype(jnp.bfloat16)
        context = jnp.einsum(
            "hqk,hkd->hqd", probs_low, values_all, preferred_element_type=jnp.float32
        ).astype(jnp.bfloat16)
        context_buf = lax.dynamic_update_slice_in_dim(context_buf, context, first_row, 1)
        return (context_buf, (row_max + jnp.log(expsum))[:, :, 0])

    context_low, log_norm = lax.scan(
        attend, jnp.zeros((heads_here, group_rows, HD), jnp.bfloat16), starts
    )
    attn_sum = lax.psum_scatter(
        jnp.einsum(
            "hrd,hde->re", context_low, w_out_heads, preferred_element_type=jnp.float32
        ).astype(jnp.bfloat16),
        "tp",
        scatter_dimension=0,
        tiled=True,
    ).astype(jnp.float32)
    hidden = tokens + attn_sum + bias_out
    normed_two, unit_two, inverse_two = norm_rows(hidden, gain_two, shift_two)
    rows_two = lax.all_gather(normed_two.astype(jnp.bfloat16), "tp", axis=0, tiled=True)
    inner = jnp.dot(rows_two, w_in, preferred_element_type=jnp.float32) + bias_in
    activ, gelu_pull = jax.vjp(jax.nn.gelu, inner)
    activ_low = activ.astype(jnp.bfloat16)
    mixed = (
        hidden
        + lax.psum_scatter(
            jnp.dot(activ_low, w_down, preferred_element_type=jnp.float32).astype(jnp.bfloat16),
            "tp",
            scatter_dimension=0,
            tiled=True,
        ).astype(jnp.float32)
        + bias_down
    )
    grad_low = cotangent.astype(jnp.bfloat16)
    grad_rows = lax.all_gather(grad_low, "tp", axis=0, tiled=True)
    g_down = jnp.einsum("rf,rd->fd", activ_low, grad_rows, preferred_element_type=jnp.float32)
    grad_activ = jnp.einsum("rd,fd->rf", grad_rows, w_down, preferred_element_type=jnp.float32)
    grad_inner = gelu_pull(grad_activ)[0].astype(jnp.bfloat16)
    g_in = jnp.einsum("rd,rf->df", rows_two, grad_inner, preferred_element_type=jnp.float32)
    g_bias_in = jnp.sum(grad_inner.astype(jnp.float32), 0)
    ffn_blocks = jnp.concatenate(
        [
            to_columns(g_in).reshape(groups, in_count, BLOCK, BLOCK),
            to_rows(g_down).reshape(groups, in_count, BLOCK, BLOCK),
        ],
        1,
    )
    grad_normed_two = lax.psum_scatter(
        jnp.einsum("rf,df->rd", grad_inner, w_in, preferred_element_type=jnp.float32).astype(
            jnp.bfloat16
        ),
        "tp",
        scatter_dimension=0,
        tiled=True,
    ).astype(jnp.float32)
    grad_hidden = cotangent + norm_back(grad_normed_two, unit_two, inverse_two, gain_two)
    grad_attn_low = grad_hidden.astype(jnp.bfloat16)
    grad_attn_rows = lax.all_gather(grad_attn_low, "tp", axis=0, tiled=True)
    g_out = jnp.einsum(
        "hrd,re->hde", context_low, grad_attn_rows, preferred_element_type=jnp.float32
    ).reshape(feat_here, D)
    grad_context = jnp.einsum(
        "re,hde->hrd", grad_attn_rows, w_out_heads, preferred_element_type=jnp.float32
    ).astype(jnp.bfloat16)
    zero_heads = jnp.zeros((heads_here, group_rows, HD), jnp.float32)

    def attend_back(carry, inputs):
        grad_queries, grad_keys, grad_values = carry
        first_row, log_block = inputs
        scores, query_rows = masked_scores(first_row)
        probs = jnp.exp(scores - log_block[:, :, None])
        grad_ctx_rows = lax.dynamic_slice_in_dim(grad_context, first_row, span, 1)
        grad_probs = jnp.einsum(
            "hqd,hkd->hqk", grad_ctx_rows, values_all, preferred_element_type=jnp.float32
        )
        delta = jnp.sum(probs * grad_probs, -1, keepdims=True)
        grad_scores = (probs * (grad_probs - delta)).astype(jnp.bfloat16)
        query_part = (
            jnp.einsum("hqk,hkd->hqd", grad_scores, keys_all, preferred_element_type=jnp.float32)
            * score_scale
        )
        grad_queries = lax.dynamic_update_slice_in_dim(grad_queries, query_part, first_row, 1)
        grad_keys = (
            grad_keys
            + jnp.einsum(
                "hqk,hqd->hkd", grad_scores, query_rows, preferred_element_type=jnp.float32
            )
            * score_scale
        )
        grad_values = grad_values + jnp.einsum(
            "hqk,hqd->hkd",
            probs.astype(jnp.bfloat16),
            grad_ctx_rows,
            preferred_element_type=jnp.float32,
        )
        return ((grad_queries, grad_keys, grad_values), None)

    (grad_queries, grad_keys, grad_values), unused = lax.scan(
        attend_back, (zero_heads, zero_heads, zero_heads), (starts, log_norm)
    )
    grad_proj = jnp.stack([grad_queries, grad_keys, grad_values], 0).astype(jnp.bfloat16)
    proj_sums = jnp.sum(grad_proj.astype(jnp.float32), 2)
    g_bias_qv = jnp.stack([proj_sums[0], proj_sums[2]], 1).reshape(qv_width)
    g_qkv = jnp.einsum(
        "rx,chrd->xhcd", rows_one, grad_proj, preferred_element_type=jnp.float32
    ).reshape(D, qkv_cols)
    grad_normed_one = lax.psum_scatter(
        jnp.einsum(
            "chrd,xhcd->rx", grad_proj, w_qkv_heads, preferred_element_type=jnp.float32
        ).astype(jnp.bfloat16),
        "tp",
        scatter_dimension=0,
        tiled=True,
    ).astype(jnp.float32)
    input_grad = grad_hidden + norm_back(grad_normed_one, unit_one, inverse_one, gain_one)
    local_rows = jnp.stack(
        [
            jnp.sum(grad_normed_one * unit_one, 0),
            jnp.sum(grad_normed_one, 0),
            jnp.sum(grad_normed_two * unit_two, 0),
            jnp.sum(grad_normed_two, 0),
            jnp.sum(grad_hidden, 0),
            jnp.sum(cotangent, 0),
        ]
    )
    qv_rows = lax.dynamic_update_slice(
        jnp.zeros((2 * D,), jnp.float32), g_bias_qv, (tp_rank * qv_width,)
    ).reshape(2, D)
    in_rows = lax.dynamic_update_slice(
        jnp.zeros((FF,), jnp.float32), g_bias_in, (tp_rank * ff_here,)
    ).reshape(FF // D, D)
    vec_grads = lax.psum(jnp.concatenate([local_rows, qv_rows, in_rows], 0), ("grp", "tp"))
    attn_blocks = jnp.concatenate(
        [
            to_columns(g_qkv).reshape(groups, qkv_count, BLOCK, BLOCK),
            to_rows(g_out).reshape(groups, out_count, BLOCK, BLOCK),
        ],
        1,
    )
    every_block = jnp.concatenate([attn_blocks, ffn_blocks], 1).reshape(-1, BLOCK, BLOCK)
    weight_grads = lax.psum_scatter(
        every_block.astype(jnp.bfloat16), "grp", scatter_dimension=0, tiled=True
    ).astype(jnp.float32)
    scaled = weight_grads * token_total ** (-0.5)
    stat_left_new = DECAY * stat_left + (1.0 - DECAY) * jnp.einsum(
        "nij,nkj->nik", scaled, scaled, precision=lax.Precision.HIGHEST
    )
    stat_right_new = DECAY * stat_right + (1.0 - DECAY) * jnp.einsum(
        "nji,njk->nik", scaled, scaled, precision=lax.Precision.HIGHEST
    )
    shaped = jnp.einsum("nij,njk->nik", root_left, scaled, precision=lax.Precision.HIGHEST)
    shaped = jnp.einsum("nij,njk->nik", shaped, root_right, precision=lax.Precision.HIGHEST)
    momentum_new = BETA * momentum + shaped
    weights_new = weights - RATE * momentum_new
    vec_scaled = vec_grads * token_total ** (-0.5)
    vec_second_new = VEC_DECAY * vec_second + (1.0 - VEC_DECAY) * vec_scaled * vec_scaled
    vec_momentum_new = BETA * vec_momentum + vec_scaled * lax.rsqrt(vec_second_new + VEC_EPS)
    vec_new = vec_params - VEC_RATE * vec_momentum_new
    return (
        mixed,
        input_grad,
        weight_grads,
        stat_left_new,
        stat_right_new,
        momentum_new,
        weights_new,
        vec_grads,
        vec_second_new,
        vec_momentum_new,
        vec_new,
    )


MESH_ID = pl.DeviceIdType.MESH
LANES = 128
HALF = 64
VMEM_LIMIT = 62 * 2**20
ARTICLES = 4
GELU_A = (2.0 / 3.141592653589793) ** 0.5
GELU_B = 0.044715


def remote(src, dst, send_sem, recv_sem, device):
    return pltpu.make_async_remote_copy(
        src_ref=src,
        dst_ref=dst,
        send_sem=send_sem,
        recv_sem=recv_sem,
        device_id=device,
        device_id_type=MESH_ID,
    )


def place():
    grp = lax.axis_index("grp")
    return lax.div(grp, 4), lax.rem(lax.div(grp, 2), 2), lax.rem(grp, 2), lax.axis_index("tp")


def slot_of(z, y, c):
    return z * 4 + y * 2 + c


def lay_blocks(view_ref, stack, first, last):
    half = view_ref.shape[2] // 2

    def row(i, carry):
        tile = view_ref[i].T
        stack[pl.ds(i, half, stride=BLOCK), :] = jnp.concatenate([tile[:half], tile[half:]], 1)
        return carry

    lax.fori_loop(first, last, row, 0, unroll=8)


def piece_shapes():
    return ((768, LANES), (64, 512), (1024, LANES), (LANES, 1024))


def both_halves(pair):
    low = lax.broadcasted_iota(jnp.int32, pair.shape, 1) < HALF
    turned = pltpu.roll(pair, HALF, 1)
    return jnp.where(low, pair, turned), jnp.where(low, turned, pair)


def update_kernel(
    scale,
    in_q,
    in_o,
    in_i,
    in_d,
    root_l,
    root_r,
    vec_g,
    vecs,
    vec_m,
    vec_s,
    mixed,
    input_grad,
    w,
    m,
    sl,
    sr,
    out_g,
    out_sl,
    out_sr,
    out_m,
    out_w,
    out_vg,
    out_vs,
    out_vm,
    out_v,
    out_mixed,
    out_input_grad,
    grads,
    first,
    second,
    held_l,
    held_r,
    held_w,
    held_m,
    held_sl,
    held_sr,
    new_g,
    new_sl,
    new_sr,
    new_m,
    new_w,
    sum_q,
    sum_o,
    sum_i,
    sum_d,
    held_mixed,
    held_input_grad,
    root_sems,
    sum_sems,
    block_sems,
    out_sems,
    pass_sems,
):
    count = w.shape[2]
    bf, f32 = jnp.bfloat16, jnp.float32
    chunk = 8
    chunks = BLOCK // chunk

    def copies(pairs, part, sems):
        return [pltpu.make_async_copy(a.at[part], b.at[part], sems.at[n]) for n, (a, b) in enumerate(pairs)]

    def root_loads(k):
        return copies(((root_l, held_l), (root_r, held_r)), pl.ds(16 * k, 16), root_sems.at[k])

    def block_loads(k):
        pairs = ((w, held_w), (m, held_m), (sl, held_sl), (sr, held_sr))
        return copies(pairs, pl.ds(chunk * k, chunk), block_sems.at[k])

    def block_stores(k):
        pairs = ((new_g, out_g), (new_sl, out_sl), (new_sr, out_sr), (new_m, out_m), (new_w, out_w))
        return copies(pairs, pl.ds(chunk * k, chunk), out_sems.at[k])

    everything = pl.ds(0, mixed.shape[0])
    sum_loads = [
        pltpu.make_async_copy(a, b, sum_sems.at[n])
        for n, (a, b) in enumerate(((in_q, sum_q), (in_o, sum_o), (in_i, sum_i), (in_d, sum_d)))
    ]
    pass_in = copies(((mixed, held_mixed), (input_grad, held_input_grad)), everything, pass_sems.at[0])
    pass_out = copies(((held_mixed, out_mixed), (held_input_grad, out_input_grad)), everything, pass_sems.at[1])
    for k in range(4):
        for load in root_loads(k):
            load.start()
    for load in sum_loads:
        load.start()
    for k in range(chunks):
        for load in block_loads(k):
            load.start()
    for load in pass_in:
        load.start()

    total = vec_g[...]
    out_vg[...] = total
    scaled = total * scale
    fresh = VEC_DECAY * vec_s[...] + (1.0 - VEC_DECAY) * scaled * scaled
    out_vs[...] = fresh
    momentum = BETA * vec_m[...] + scaled * lax.rsqrt(fresh + VEC_EPS)
    out_vm[...] = momentum
    out_v[...] = vecs[...] - VEC_RATE * momentum

    def row(i, carry):
        both = jnp.concatenate([held_l[i], held_r[i]], 0)
        second[pl.ds(i, count, stride=BLOCK), :] = both.T
        return carry

    for k in range(4):
        for load in root_loads(k):
            load.wait()
        lax.fori_loop(16 * k, 16 * k + 16, row, 0, unroll=8)
    for load in sum_loads:
        load.wait()
    rows = sum_q.shape[0]
    grads[0:rows, 0:HALF] = sum_q[:, 0:HALF]
    grads[rows : 2 * rows, 0:HALF] = sum_q[:, HALF:LANES]
    base = 2 * rows
    for b in range(8):
        grads[base + b * 64 : base + b * 64 + 64, 0:HALF] = sum_o[:, b * HALF : (b + 1) * HALF]
    base += 512
    grads[base : base + D, 0:HALF] = sum_i[:, 0:HALF]
    grads[0:D, HALF:LANES] = sum_i[:, HALF:LANES]
    for r in range(2):
        for b in range(16):
            at = D + (r * 16 + b) * 64
            grads[at : at + 64, HALF:LANES] = sum_d[r * 64 : r * 64 + 64, b * HALF : (b + 1) * HALF]

    row_id = lax.broadcasted_iota(jnp.int32, (256, 256), 0)
    col_id = lax.broadcasted_iota(jnp.int32, (256, 256), 1)
    mask = lax.shift_right_logical(row_id, 6) == lax.shift_right_logical(col_id, 6)
    low = lax.broadcasted_iota(jnp.int32, (256, LANES), 1) < HALF

    def spread(v):
        return jnp.where(mask, jnp.concatenate([v, v], 1), 0.0).astype(bf)

    def eight(k, carry):
        at = pl.ds(pl.multiple_of(k * 256, 256), 256)
        for side, grad in enumerate(both_halves(grads[at, :])):
            to = pl.ds(pl.multiple_of(k * 256 + side * (count // 2 * BLOCK), 256), 256)
            left, right = both_halves(second[to, :])
            s32 = grad * scale
            s = s32.astype(bf)
            outer = lax.dot_general(s[:, 0:HALF], s[:, 0:HALF], (((1,), (1,)), ((), ())), preferred_element_type=f32)
            kept = jnp.where(mask, outer, 0.0)
            kept = kept[:, :LANES] + kept[:, LANES:]
            outer = kept + pltpu.roll(kept, HALF, 1)
            inner = lax.dot_general(spread(s32), s, (((0,), (0,)), ((), ())), preferred_element_type=f32)
            shaped = jnp.dot(spread(left), s, preferred_element_type=f32)
            shaped = jnp.dot(spread(shaped), right.astype(bf), preferred_element_type=f32)
            first[to, :] = jnp.where(low, grad, outer)
            second[to, :] = jnp.where(low, inner, shaped)
        return carry

    lax.fori_loop(0, count // 8, eight, 0, unroll=4)

    for load, store in zip(pass_in, pass_out):
        load.wait()
        store.start()
    unit = lax.broadcasted_iota(jnp.int32, (LANES, LANES), 0) == lax.broadcasted_iota(jnp.int32, (LANES, LANES), 1)
    unit = unit.astype(f32).astype(bf)

    def turned(tile):
        high = tile.astype(bf)
        rest = (tile - high.astype(f32)).astype(bf)
        over = (((1,), (1,)), ((), ()))
        return lax.dot_general(unit, high, over, preferred_element_type=f32) + lax.dot_general(
            unit, rest, over, preferred_element_type=f32
        )

    def rows_out(i, carry):
        at = pl.ds(i, count, stride=BLOCK)
        one = first[at, :].T
        two = turned(second[at, :])
        new_g[i] = one[0:HALF]
        new_sl[i] = DECAY * held_sl[i] + (1.0 - DECAY) * one[HALF:LANES]
        new_sr[i] = DECAY * held_sr[i] + (1.0 - DECAY) * two[0:HALF]
        fresh = BETA * held_m[i] + two[HALF:LANES]
        new_m[i] = fresh
        new_w[i] = held_w[i] - RATE * fresh
        return carry

    for k in range(chunks):
        for load in block_loads(k):
            load.wait()
        lax.fori_loop(chunk * k, chunk * k + chunk, rows_out, 0, unroll=8)
        for store in block_stores(k):
            store.start()
    for k in range(chunks):
        for store in block_stores(k):
            store.wait()
    for store in pass_out:
        store.wait()


def update_blocks(sums, blocks, vec_grads, vecs, results, token_total):
    views = [jnp.transpose(a, (1, 2, 0)) for a in blocks]
    count = blocks[0].shape[0]
    whole = pl.BlockSpec(memory_space=pltpu.VMEM)
    there = pl.BlockSpec(memory_space=pl.ANY)
    vec = jax.ShapeDtypeStruct(vec_grads.shape, jnp.float32)
    block = jax.ShapeDtypeStruct((BLOCK, BLOCK, count), jnp.float32)
    stack = pltpu.VMEM((count * BLOCK, LANES), jnp.float32)
    dma = pltpu.SemaphoreType.DMA
    outs = pl.pallas_call(
        functools.partial(update_kernel, token_total ** (-0.5)),
        out_shape=[block] * 5 + [vec] * 4 + [jax.ShapeDtypeStruct(a.shape, a.dtype) for a in results],
        in_specs=[there] * 6 + [whole] * 4 + [there] * 6,
        out_specs=[there] * 5 + [whole] * 4 + [there] * 2,
        scratch_shapes=[
            pltpu.VMEM((count // 2 * BLOCK, LANES), jnp.float32),
            stack,
            stack,
            *[pltpu.VMEM(block.shape, block.dtype)] * 11,
            *[pltpu.VMEM(a.shape, a.dtype) for a in (*sums, *results)],
            dma((4, 2)),
            dma((4,)),
            dma((8, 4)),
            dma((8, 5)),
            dma((2, 2)),
        ],
        compiler_params=pltpu.CompilerParams(vmem_limit_bytes=VMEM_LIMIT),
        name="update_blocks",
    )(*sums, *views[4:], vec_grads, *vecs, *results, *views[:4])
    return [jnp.transpose(a, (2, 0, 1)) for a in outs[:5]], outs[5:9], outs[9:]


DEPTH = 4


def layer_kernel(
    lengths,
    order,
    view,
    tokens_in,
    cot_in,
    vecs,
    mixed_there,
    input_grad_there,
    out_q,
    out_o,
    out_i,
    out_d,
    vec_grads,
    tokens,
    cot,
    mixed,
    input_grad,
    sum_q,
    sum_o,
    sum_i,
    sum_d,
    gq,
    go,
    gi,
    gd,
    wqkv,
    cq,
    co,
    ci,
    cd,
    yq,
    yo,
    yi,
    yd,
    yv,
    zq,
    zo,
    zi,
    zd,
    zv,
    rows_one,
    rows_two,
    rows_t,
    grad_rows,
    grad_attn,
    probs,
    qkv,
    ctx,
    gctx,
    far,
    inx,
    go_x,
    ctx_x,
    macc,
    nacc,
    act,
    gin,
    bias_sum,
    qkv_bias,
    qv_sum,
    vin,
    vout,
    late,
    late_sum,
    late_in,
    recv,
    send_y,
    send_c,
    send_z,
    rc_recv,
    rc_send,
    ry_recv,
    ry_send,
    rz_recv,
    rz_send,
    x_send,
    x_recv,
    v_send,
    v_recv,
    l_send,
    l_recv,
    copy_sem,
):
    bf, f32 = jnp.bfloat16, jnp.float32
    z, y, c, t = place()
    me = slot_of(z, y, c)
    x_peer = (me, 1 - t)
    y_peer = (slot_of(z, 1 - y, c), t)
    c_peer = (slot_of(z, y, 1 - c), t)
    rows = tokens.shape[0]
    own = pl.ds(pl.multiple_of(t * rows, rows), rows)
    other = pl.ds(pl.multiple_of((1 - t) * rows, rows), rows)

    def lanes(start, size, unit):
        return pl.ds(pl.multiple_of(start, unit), size)

    gathered, core_in = (gq, go, gi, gd), (cq, co, ci, cd)
    y_in, z_in = (yq, yo, yi, yd, yv), (zq, zo, zi, zd, zv)
    sums = (sum_q, sum_o, sum_i, sum_d)
    Q, O, I, W, V = range(5)

    def dot(a, b):
        return jnp.dot(a, b, preferred_element_type=f32)

    def dot_nt(a, b):
        return lax.dot_general(a, b, (((1,), (1,)), ((), ())), preferred_element_type=f32)

    def dot_tn(a, b):
        return lax.dot_general(a, b, (((0,), (0,)), ((), ())), preferred_element_type=f32)

    def piece(k, zz, yy, cc):
        if k == O:
            return go.at[zz * 2 + yy, :, pl.ds(pl.multiple_of(cc * 512, 512), 512)]
        return gathered[k].at[slot_of(zz, yy, cc)]

    def near(s):
        return lax.rem(z + (1 - 2 * lax.div(z, 2)) * s + DEPTH, DEPTH)

    def ag_piece(k, zz, yy, cc):
        if k == W:
            return gd.at[slot_of(zz, yy, cc), 0:HALF]
        if k == V:
            return gd.at[slot_of(zz, yy, cc), HALF:LANES]
        return piece(k, zz, yy, cc)

    def ag_copy(k, zz, yy, way):
        src = ag_piece(k, zz, yy, c)
        sem = recv.at[k, slot_of(zz, yy, c)]
        if way == "up":
            return remote(src, src, send_z.at[k, 0, yy * DEPTH + zz], sem, (slot_of(z + 1, y, c), t))
        if way == "down":
            return remote(src, src, send_z.at[k, 1, yy * DEPTH + zz], sem, (slot_of(z - 1, y, c), t))
        if way == "y":
            return remote(src, src, send_y.at[k, zz], sem, y_peer)
        return remote(src, src, send_c.at[k, yy * DEPTH + zz], sem, c_peer)

    def ag_wait(k, zz, yy, cc):
        ref = ag_piece(k, zz, yy, cc)
        remote(ref, ref, send_y.at[k, 0], recv.at[k, slot_of(zz, yy, cc)], y_peer).wait_recv()

    def own_sends_z(k):
        @pl.when(z < DEPTH - 1)
        def _():
            ag_copy(k, z, y, "up").start()

        @pl.when(z > 0)
        def _():
            ag_copy(k, z, y, "down").start()

        ag_copy(k, z, y, "core").start()

    def own_sends_y(k):
        ag_copy(k, z, y, "y").start()

    def z_arrival(kinds, dist):
        @pl.when(z >= dist)
        def _():
            for k in kinds:
                ag_wait(k, z - dist, y, c)

                @pl.when(z < DEPTH - 1)
                def _():
                    ag_copy(k, z - dist, y, "up").start()

                ag_copy(k, z - dist, y, "y").start()
                ag_copy(k, z - dist, y, "core").start()

        @pl.when(z + dist < DEPTH)
        def _():
            for k in kinds:
                ag_wait(k, z + dist, y, c)

                @pl.when(z > 0)
                def _():
                    ag_copy(k, z + dist, y, "down").start()

                ag_copy(k, z + dist, y, "y").start()
                ag_copy(k, z + dist, y, "core").start()

    def y_arrival(kinds, dist):
        def one(zz):
            for k in kinds:
                ag_wait(k, zz, 1 - y, c)
                ag_copy(k, zz, 1 - y, "core").start()

        if dist == 0:
            one(z)
            return

        @pl.when(z >= dist)
        def _():
            one(z - dist)

        @pl.when(z + dist < DEPTH)
        def _():
            one(z + dist)

    def v_forward(zz, yy):
        ag_wait(V, zz, yy, c)

        @pl.when((zz <= z) & (z < DEPTH - 1))
        def _():
            ag_copy(V, zz, yy, "up").start()

        @pl.when((zz >= z) & (z > 0))
        def _():
            ag_copy(V, zz, yy, "down").start()

        ag_copy(V, zz, yy, "core").start()

    def v_arrival(dist):
        for yy in (y, 1 - y):

            @pl.when(z >= dist)
            def _():
                v_forward(z - dist, yy)

            @pl.when(z + dist < DEPTH)
            def _():
                v_forward(z + dist, yy)

    def drain(k, zz, yy):
        ag_copy(k, zz, yy, "core").wait_send()
        if k == V:

            @pl.when((yy == y) & (zz == z))
            def _():
                ag_copy(k, zz, yy, "y").wait_send()

            @pl.when((zz <= z) & (z < DEPTH - 1))
            def _():
                ag_copy(k, zz, yy, "up").wait_send()

            @pl.when((zz >= z) & (z > 0))
            def _():
                ag_copy(k, zz, yy, "down").wait_send()

            return

        @pl.when(yy == y)
        def _():
            ag_copy(k, zz, y, "y").wait_send()

            @pl.when((zz <= z) & (z < DEPTH - 1))
            def _():
                ag_copy(k, zz, y, "up").wait_send()

            @pl.when((zz >= z) & (z > 0))
            def _():
                ag_copy(k, zz, y, "down").wait_send()

    def add(dst, *terms):
        count, width = dst.shape
        step = min(count, 256 * LANES // width)

        def body(i, carry):
            at = pl.ds(pl.multiple_of(i * step, 16), step)
            if len(terms) == 2 and dst.dtype == bf:
                dst[at, :] = terms[0][at, :] + terms[1][at, :]
                return carry
            total = terms[0][at, :].astype(f32)
            for term in terms[1:]:
                total = total + term[at, :].astype(f32)
            dst[at, :] = total.astype(dst.dtype)
            return carry

        lax.fori_loop(0, count // step, body, 0, unroll=2)

    side = lax.div(z, 2)
    end_z, inner_z = 3 * side, 1 + side
    is_end = z == end_z

    def rc_copy(k, zz, yy):
        at = zz * 2 + yy
        return remote(piece(k, zz, yy, 1 - c), core_in[k].at[at], rc_send.at[k, at], rc_recv.at[k, at], c_peer)

    def ry_copy(k, zz):
        if k == V:
            return remote(ag_piece(V, z, 1 - y, c), y_in[V].at[0], ry_send.at[V, 0], ry_recv.at[V, 0], y_peer)
        return remote(ag_piece(k, zz, 1 - y, c), y_in[k].at[zz], ry_send.at[k, zz], ry_recv.at[k, zz], y_peer)

    def z_slot(k, slot, yy):
        return z_in[k].at[slot * 2 + yy if k == V else slot]

    def z_sem(slot, yy):
        return slot * 2 + yy

    def rz_copy(k, s, yy, from_end):
        slot = s - 1 if from_end else {3: 0, 2: 1, 1: 3}[s]
        to = inner_z if from_end else {3: end_z, 2: 3 - end_z, 1: 3 - inner_z}[s]
        sent, landed = rz_send.at[k, (s - 1) * 2 + yy], rz_recv.at[k, z_sem(slot, yy)]
        return remote(ag_piece(k, near(s), yy, c), z_slot(k, slot, yy), sent, landed, (slot_of(to, y, c), t))

    def z_landed(k, slot, yy):
        ref = z_slot(k, slot, yy)
        remote(ref, ref, rz_send.at[k, 0], rz_recv.at[k, z_sem(slot, yy)], y_peer).wait_recv()
        return ref

    def y_landed(k, zz):
        ref = y_in[k].at[0 if k == V else zz]
        remote(ref, ref, ry_send.at[k, 0], ry_recv.at[k, 0 if k == V else zz], y_peer).wait_recv()
        return ref

    def rc_add(k, zz, yy):
        at = zz * 2 + yy
        remote(core_in[k].at[at], core_in[k].at[at], rc_send.at[k, 0], rc_recv.at[k, at], c_peer).wait_recv()
        mine = piece(k, zz, yy, c)
        add(mine, mine, core_in[k].at[at])

        @pl.when(yy != y)
        def _():
            ry_copy(k, zz).start()

    def z_step(k, s, yy, *terms):
        mine = ag_piece(k, near(s), yy, c)
        if terms:
            add(mine, mine, *terms)

        @pl.when(is_end)
        def _():
            rz_copy(k, s, yy, True).start()

        if s == 3:

            @pl.when(jnp.logical_not(is_end))
            def _():
                rz_copy(k, s, yy, False).start()

    def z_merge(k, s, yy):
        @pl.when(jnp.logical_not(is_end))
        def _():
            mine = ag_piece(k, near(s), yy, c)
            add(mine, mine, z_landed(k, s, yy))
            rz_copy(k, s, yy, False).start()

    def ry_add(k, s):
        z_step(k, s, y, y_landed(k, near(s)))

    def ry_merge(k, s):
        z_merge(k, s, y)

    def total_of(k):
        return sum_d.at[(k - W) * HALF : (k - W + 1) * HALF] if k >= W else sums[k]

    def z_total(k, yy, dst, *terms):
        mine = ag_piece(k, z, yy, c)
        first = z_landed(k, 0, yy)

        @pl.when(is_end)
        def _():
            add(dst, mine, first, z_landed(k, 1, yy), *terms)

        @pl.when(jnp.logical_not(is_end))
        def _():
            add(dst, mine, first, z_landed(k, 3, yy), *terms)

    def own_total(k):
        z_total(k, y, total_of(k), y_landed(k, z))

    def v_cross():
        mine = ag_piece(V, z, 1 - y, c)
        z_total(V, 1 - y, mine)
        ry_copy(V, z).start()

    def x_rows(ref, index):
        return remote(ref.at[own], ref.at[own], x_send.at[index], x_recv.at[index], x_peer)

    def x_rows_wait(ref, index):
        remote(ref.at[other], ref.at[other], x_send.at[index], x_recv.at[index], x_peer).wait_recv()

    def x_part(index):
        slot = 1 if index == 2 else 0
        return remote(far.at[slot], inx.at[slot], x_send.at[5 + index], x_recv.at[5 + index], x_peer)

    def by_rows(body, step=64):
        def run(i, carry):
            body(pl.multiple_of(i * step, step), step)
            return carry

        lax.fori_loop(0, rows // step, run, 0)

    def norm(value):
        average = jnp.mean(value, -1, keepdims=True)
        centred = value - average
        inverse = lax.rsqrt(jnp.mean(centred * centred, -1, keepdims=True) + EPS)
        return centred * inverse, inverse

    def norm_grad(grad, unit, inverse, gain):
        scaled = grad * gain
        return inverse * (
            scaled - jnp.mean(scaled, -1, keepdims=True) - unit * jnp.mean(scaled * unit, -1, keepdims=True)
        )

    def x_out():
        half = (slice(None), slice(None), lanes(c * 512, 512, 512))
        return remote(go.at[half], go_x.at[half], x_send.at[4], x_recv.at[4], x_peer)

    def x_out_core(cc):
        half = (slice(None), slice(None), lanes(cc * 512, 512, 512))
        return remote(go_x.at[half], go_x.at[half], x_send.at[9], x_recv.at[9], c_peer)

    def x_grad_context():
        return remote(ctx_x, gctx.at[own], x_send.at[10], x_recv.at[10], x_peer)

    def x_grad_context_wait():
        remote(gctx.at[other], gctx.at[other], x_send.at[10], x_recv.at[10], x_peer).wait_recv()

    stages = (x_peer, c_peer, y_peer)

    def v_copy(stage):
        return remote(vout.at[1 + stage], vin.at[stage], v_send.at[stage], v_recv.at[stage], stages[stage])

    def vz_copy(step):
        peer = (slot_of(lax.rem(z + step, DEPTH), y, c), t)
        return remote(vout.at[4], vin.at[3 + z], v_send.at[2 + step], v_recv.at[3 + z], peer)

    def early_rows(hop):
        if hop == 0:
            vout[1] = vout[0]
        else:
            v_copy(hop - 1).wait_recv()
            vout[1 + hop] = vout[hop] + vin[hop - 1]
        if hop < 3:
            v_copy(hop).start()
        else:
            for step in range(1, DEPTH):
                vz_copy(step).start()
            vin[3 + z] = vout[4]

    def late_turn(turn):
        dx, dy, dc = turn // 4, turn // 2 % 2, turn % 2
        xx, yy, cc = (1 - t if dx else t), (1 - y if dy else y), (1 - c if dc else c)
        return (slot_of(z, yy, cc), xx), xx * 4 + yy * 2 + cc

    def late_copy(turn):
        here = t * 4 + y * 2 + c
        return remote(late, late_in.at[here], l_send.at[turn], l_recv.at[here], late_turn(turn)[0])

    def late_wait(index):
        remote(late_in.at[index], late_in.at[index], l_send.at[0], l_recv.at[index], y_peer).wait_recv()

    def late_z(step):
        peer = (slot_of(lax.rem(z + step, DEPTH), y, c), t)
        return remote(late_sum, late_in.at[8 + z], l_send.at[7 + step], l_recv.at[8 + z], peer)

    stores = [
        pltpu.make_async_copy(a, b, copy_sem.at[6 + n])
        for n, (a, b) in enumerate(
            (
                (sum_q, out_q),
                (sum_o, out_o),
                (sum_i, out_i),
                (sum_d, out_d),
                (mixed, mixed_there),
                (input_grad, input_grad_there),
            )
        )
    ]

    barrier = pltpu.get_barrier_semaphore()
    z_peers = [(slot_of(lax.rem(z + step, DEPTH), y, c), t) for step in range(1, DEPTH)]
    everyone = [late_turn(turn)[0] for turn in range(1, 8)] + z_peers
    for device in everyone:
        pl.semaphore_signal(barrier, inc=1, device_id=device, device_id_type=MESH_ID)

    row_loads = [pltpu.make_async_copy(tokens_in, tokens, copy_sem.at[4]), pltpu.make_async_copy(cot_in, cot, copy_sem.at[5])]

    def prepare(held, stack):
        parts = [pl.ds(16 * k, 16) for k in range(4)]
        loads = [pltpu.make_async_copy(view.at[part], held.at[part], copy_sem.at[k]) for k, part in enumerate(parts)]
        for load in loads:
            load.start()
        for load in row_loads:
            load.start()

        def first_norm(at, step):
            unit, inverse = norm(tokens[pl.ds(at, step), :])
            to = pl.ds(pl.multiple_of(t * rows + at, step), step)
            rows_one[to, :] = (unit * vecs[0:1, :] + vecs[1:2, :]).astype(bf)
            grad_rows[to, :] = cot[pl.ds(at, step), :].astype(bf)

        for k, load in enumerate(loads):
            load.wait()
            lay_blocks(held, stack, 16 * k, 16 * k + 16)

        def pair(left, right, count, left_high=False, right_high=False):
            first, second = stack[left : left + count, :], stack[right : right + count, :]
            first = pltpu.roll(first, HALF, 1) if left_high else first
            second = second if right_high else pltpu.roll(second, HALF, 1)
            lane = lax.broadcasted_iota(jnp.int32, (count, LANES), 1)
            return jnp.where(lane < HALF, first, second).astype(bf)

        n = gq.shape[1]
        gq[me] = pair(0, n, n)
        base = 2 * n
        wide = [pair(base + b * 64, base + b * 64 + 64, 64) for b in range(0, 8, 2)]
        go[z * 2 + y, :, lanes(c * 512, 512, 512)] = jnp.concatenate(wide, 1)
        pl.semaphore_wait(barrier, len(everyone))
        for k in (Q, O):
            own_sends_y(k)
            own_sends_z(k)
        for load in row_loads:
            load.wait()
        by_rows(first_norm)
        x_rows(rows_one, 0).start()
        base += 512
        gi[me] = pair(base, 0, D, right_high=True)
        for r in range(2):
            for b in range(0, 16, 2):
                at = D + (r * 16 + b) * 64
                gd[me, r * 64 : r * 64 + 64, b * HALF : b * HALF + LANES] = pair(at, at + 64, 64, True, True)

    pl.run_scoped(
        prepare,
        pltpu.VMEM(view.shape, f32),
        pltpu.VMEM((view.shape[2] // 2 * BLOCK, LANES), f32),
    )
    x_rows(grad_rows, 1).start()
    z_arrival((Q, O), 1)
    y_arrival((Q, O), 0)
    z_arrival((Q, O), 2)
    for k in (I, W, V):
        own_sends_z(k)
    own_sends_y(I)
    y_arrival((Q, O), 1)

    def core_waits(kinds, zz):
        for k in kinds:
            for yy in (y, 1 - y):
                ag_wait(k, zz, yy, 1 - c)

    x_rows_wait(rows_one, 0)

    ends = []
    for p in range(ARTICLES):
        length = 0
        for a in range(ARTICLES):
            length = length + jnp.where(order[0, p] == a, lengths[0, a], 0)
        ends.append(length + ends[-1] if p else length)

    def allowed(first, count):
        ids = lax.broadcasted_iota(jnp.int32, (rows, 1), 0) + first
        start = jnp.zeros((rows, 1), jnp.int32)
        for end in ends:
            start = jnp.where(ids >= end, end, start)
        start = jnp.where(ids >= ends[-1], ids, start)
        keys = lax.broadcasted_iota(jnp.int32, (rows, count), 1)
        return (keys <= ids) & (keys >= start)

    scale = HD ** (-0.5)

    def assemble(h):
        for yy in range(2):
            even, odd = gq.at[slot_of(h, yy, 0)], gq.at[slot_of(h, yy, 1)]
            at = yy * 192
            wqkv[h, 0:768, at : at + 64] = even[:, 0:64]
            wqkv[h, 768:1024, at : at + 64] = even[0:256, 64:128]
            wqkv[h, 0:512, at + 64 : at + 128] = even[256:768, 64:128]
            wqkv[h, 512:1024, at + 64 : at + 128] = odd[0:512, 0:64]
            wqkv[h, 0:256, at + 128 : at + 192] = odd[512:768, 0:64]
            wqkv[h, 256:1024, at + 128 : at + 192] = odd[:, 64:128]

    def disassemble(h, value):
        for yy in range(2):
            even, odd = gq.at[slot_of(h, yy, 0)], gq.at[slot_of(h, yy, 1)]
            at = yy * 192
            even[:, 0:64] = value[0:768, at : at + 64]
            even[0:256, 64:128] = value[768:1024, at : at + 64]
            even[256:768, 64:128] = value[0:512, at + 64 : at + 128]
            odd[0:512, 0:64] = value[512:1024, at + 64 : at + 128]
            odd[512:768, 0:64] = value[0:256, at + 128 : at + 192]
            odd[:, 64:128] = value[256:1024, at + 128 : at + 192]

    qv = vecs[pl.ds(6 + t, 1), :]
    for h in range(DEPTH):
        none = jnp.zeros((1, HD), f32)
        qkv_bias[h] = jnp.concatenate([qv[:, h * 256 : h * 256 + 128], none, qv[:, h * 256 + 128 : h * 256 + 256]], 1)

    def head(h):
        core_waits((Q,), h)
        assemble(h)
        qkv[h] = (dot(rows_one[...], wqkv[h]) + qkv_bias[h]).astype(bf)
        for block in range(2):
            at, seen = slice(block * rows, (block + 1) * rows), (block + 1) * rows
            scores = dot_nt(qkv[h, at, 0:128], qkv[h, 0:seen, 128:256]) * scale
            scores = jnp.where(allowed(block * rows, seen), scores, NEG)
            expo = jnp.exp(scores - jnp.max(scores, -1, keepdims=True))
            low = (expo * (1.0 / jnp.sum(expo, -1, keepdims=True))).astype(bf)
            probs[h, at, 0:seen] = low
            ctx[at, lanes(h * HD, HD, HD)] = dot(low, qkv[h, 0:seen, 256:384]).astype(bf)

    head(near(0))
    y_arrival((Q, O), 2)
    z_arrival((Q, O), 3)
    y_arrival((Q, O), 3)
    own_sends_y(W)
    head(near(1))
    own_sends_y(V)
    head(near(2))
    z_arrival((I, W), 1)
    head(near(3))
    y_arrival((I, W), 0)
    for zz in range(DEPTH):
        core_waits((O,), zz)
    def w_out(ref):
        return ref[...].reshape(DEPTH * HD, D)
    far[0] = dot(ctx[other, :], w_out(go)).astype(bf)
    x_part(0).start()
    mixed[...] = tokens[...] + dot(ctx[own, :], w_out(go)) + vecs[4:5, :]
    z_arrival((I, W), 2)
    x_part(0).wait_recv()
    def second_norm(at, step):
        value = mixed[pl.ds(at, step), :] + inx[0, pl.ds(at, step), :].astype(f32)
        mixed[pl.ds(at, step), :] = value
        unit, inverse = norm(value)
        to = pl.ds(pl.multiple_of(t * rows + at, step), step)
        rows_two[to, :] = (unit * vecs[2:3, :] + vecs[3:4, :]).astype(bf)
    x_rows_wait(grad_rows, 1)
    by_rows(second_norm)
    x_rows(rows_two, 2).start()
    v_forward(z, 1 - y)
    macc[...] = jnp.zeros_like(macc)
    y_arrival((I, W), 1)
    nacc[...] = jnp.zeros_like(nacc)
    vout[...] = jnp.zeros_like(vout)
    z_arrival((I, W), 3)
    def ffn(half, zz):
        first = 4 * zz
        at = pl.ds(pl.multiple_of(lax.rem(t + half, 2) * rows, rows), rows)
        units = lanes(zz * 512, 512, 512)
        bias_row = vecs[pl.ds(8 + 2 * t + lax.div(zz, 2), 1), lanes(lax.rem(zz, 2) * 512, 512, 512)]

        def w_in(start, count):
            return jnp.concatenate([gi[first + j, start : start + count, :] for j in range(4)], 1)

        def w_down(start, count):
            return gd[pl.ds(first, 4), :, start : start + count].reshape(512, count)

        inner = dot(rows_two[at, :], w_in(0, D)) + bias_row
        square = inner * inner
        bent = jnp.tanh(GELU_A * inner * (1.0 + GELU_B * square))
        act[at, units] = (0.5 * inner * (1.0 + bent)).astype(bf)
        slope = 0.5 * (1.0 + bent) + 0.5 * inner * (1.0 - bent * bent) * (GELU_A * (1.0 + 3.0 * GELU_B * square))
        gin[at, units] = (dot_nt(grad_rows[at, :], w_down(0, D)) * slope).astype(bf)
        for nb in range(4):
            out = slice(nb * 256, nb * 256 + 256)
            nacc[at, out] += dot_nt(gin[at, units], w_in(nb * 256, 256))
            macc[at, out] += dot(act[at, units], w_down(nb * 256, 256))
    def ffn_grads(zz):
        first = 4 * zz
        units = lanes(zz * 512, 512, 512)
        for k in (I, W, V):
            for yy in range(2):
                drain(k, zz, yy)
        bias_sum[zz] = jnp.sum(gin[:, units].astype(f32), 0, keepdims=True)
        for nb in range(4):
            out = slice(nb * 256, nb * 256 + 256)
            part = dot(rows_t[out, :], gin[:, units]).astype(bf)
            for j in range(4):
                gi[first + j, out, :] = part[:, j * LANES : (j + 1) * LANES]
        for yy in (1 - y, y):
            rc_copy(I, zz, yy).start()
        act_t = act[:, units].T
        for nb in range(4):
            out = slice(nb * 256, nb * 256 + 256)
            part = dot(act_t, grad_rows[:, out]).astype(bf)
            gd[pl.ds(first, 4), :, out] = part.reshape(4, LANES, 256)
        for yy in (1 - y, y):
            rc_copy(W, zz, yy).start()
    def each(kinds, step, *args):
        for k in kinds:
            step(k, *args)
    def reduce_out():
        for yy in (1 - y, y):
            for s in (3, 2, 1, 0):
                rc_add(O, near(s), yy)
    def reduce_head(zz):
        for yy in (1 - y, y):
            rc_add(Q, zz, yy)
    v_arrival(1)
    def reduce_core(zz):
        for yy in (1 - y, y):
            for k in (I, W):
                rc_add(k, zz, yy)
    def v_step(s):
        for yy in (1 - y, y):
            z_step(V, s, yy)
    def v_merge(s):
        for yy in (1 - y, y):
            z_merge(V, s, yy)
    core_waits((I, W, V), z)
    ffn(0, z)
    core_waits((I, W, V), near(1))
    ffn(0, near(1))
    x_rows_wait(rows_two, 2)
    x_out().start()
    v_arrival(2)
    rows_t[...] = rows_two[...].T
    y_arrival((I, W), 2)
    def by_z(s, carry):
        @pl.when(s == 2)
        def _():
            v_arrival(3)
            y_arrival((I, W), 3)

        @pl.when(s >= 2)
        def _():
            core_waits((I, W, V), near(s))
            ffn(0, near(s))

        ffn(1, near(s))

        @pl.when(s == DEPTH - 1)
        def _():
            x_part(0).wait_send()
            far[0] = nacc[other, :].astype(bf)
            x_part(1).start()

        ffn_grads(near(s))

        @pl.when(s > 0)
        def _():
            reduce_core(near(s - 1))

        for before in (1, 2):

            @pl.when(s == before + 1)
            def _():
                v_step(before)

        return carry
    lax.fori_loop(0, DEPTH, by_z, 0)
    x_out().wait_recv()
    reduce_core(near(3))
    x_out_core(c).start()
    v_step(3)
    rows_t[...] = rows_one[...].T
    for zz in range(DEPTH):
        for side in range(2):
            row, start = 8 + 2 * side + zz // 2, zz % 2 * 512
            vout[0, row : row + 1, start : start + 512] = jnp.where(t == side, bias_sum[zz], 0.0)
    v_merge(1)
    x_part(1).wait_recv()
    def row_sum(row, value):
        vout[0, row : row + 1, :] += jnp.sum(value, 0, keepdims=True)
    def second_back(at, step):
        here = pl.ds(at, step)
        in_group = pl.ds(pl.multiple_of(t * rows + at, step), step)
        grad = nacc[in_group, :] + inx[0, here, :].astype(f32)
        unit, inverse = norm(mixed[here, :])
        back = cot[here, :] + norm_grad(grad, unit, inverse, vecs[2:3, :])
        input_grad[here, :] = back
        grad_attn[in_group, :] = back.astype(bf)
        row_sum(2, grad * unit)
        row_sum(3, grad)
        row_sum(4, back)
        row_sum(5, cot[here, :])
    by_rows(second_back)
    early_rows(0)
    x_out_core(1 - c).wait_recv()
    ctx_x[...] = dot_nt(grad_attn[own, :], w_out(go_x)).astype(bf)
    x_grad_context().start()
    gctx[own, :] = dot_nt(grad_attn[own, :], w_out(go)).astype(bf)
    each((I, W), ry_add, 1)
    v_merge(2)
    each((I, W), ry_add, 2)
    for zz in range(DEPTH):
        for yy in range(2):
            drain(O, zz, yy)
            drain(Q, zz, yy)
    def mixed_out(at, step):
        here = pl.ds(at, step)
        in_group = pl.ds(pl.multiple_of(t * rows + at, step), step)
        mixed[here, :] = mixed[here, :] + macc[in_group, :] + inx[1, here, :].astype(f32) + vecs[5:6, :]
    x_out().wait_send()
    x_grad_context_wait()
    far[1] = macc[other, :].astype(bf)
    x_rows(grad_attn, 3).start()
    def out_grads():
        x_rows_wait(grad_attn, 3)
        ctx_t = ctx[...].T
        for nb in range(4):
            at = slice(nb * 256, nb * 256 + 256)
            go[:, :, at] = dot(ctx_t, grad_attn[:, at]).astype(bf).reshape(8, 64, 256)
        for zz in range(DEPTH):
            for yy in range(2):
                rc_copy(O, zz, yy).start()
    def first_back(at, step):
        here = pl.ds(at, step)
        in_group = pl.ds(pl.multiple_of(t * rows + at, step), step)
        grad = nacc[in_group, :] + inx[0, here, :].astype(f32)
        unit, inverse = norm(tokens[here, :])
        input_grad[here, :] = input_grad[here, :] + norm_grad(grad, unit, inverse, vecs[0:1, :])
        row_sum(0, grad * unit)
        row_sum(1, grad)
    def finish_mixed():
        x_part(2).wait_recv()
        by_rows(mixed_out)
        stores[4].start()
    def finish_input():
        x_part(3).wait_recv()
        by_rows(first_back)
        stores[5].start()
    late_rows = (0, 1, 6, 7)
    v_cross()
    def late_start():
        for h in range(DEPTH):
            for row in range(2):
                total = jnp.where(t == row, qv_sum[h], 0.0)
                vout[0, 6 + row : 7 + row, h * 256 : h * 256 + 128] = total[:, 0:128]
                vout[0, 6 + row : 7 + row, h * 256 + 128 : h * 256 + 256] = total[:, 256:384]
        for at, row in enumerate(late_rows):
            for j in range(8):
                late[at * 8 + j : at * 8 + j + 1, :] = vout[0, row : row + 1, j * LANES : (j + 1) * LANES]
        late_in[t * 4 + y * 2 + c] = late[...]
        for turn in range(1, 8):
            late_copy(turn).start()
    def late_cross():
        for turn in range(1, 8):
            late_wait(late_turn(turn)[1])
        total = late_in[0]
        for index in range(1, 8):
            total = total + late_in[index]
        late_sum[...] = total
        late_in[8 + z] = total
        for step in range(1, DEPTH):
            late_z(step).start()
    def vec_finish():
        for step in range(1, DEPTH):
            zz = lax.rem(z + step, DEPTH)
            late_wait(8 + zz)
            remote(vin.at[3 + zz], vin.at[3 + zz], v_send.at[0], v_recv.at[3 + zz], y_peer).wait_recv()
        total = ((late_in[8] + late_in[9]) + late_in[10]) + late_in[11]
        early = ((vin[3] + vin[4]) + vin[5]) + vin[6]
        vec_grads[...] = early[0 : vec_grads.shape[0]]
        for at, row in enumerate(late_rows):
            for j in range(8):
                vec_grads[row : row + 1, j * LANES : (j + 1) * LANES] = total[at * 8 + j : at * 8 + j + 1, :]
    def head_back(h, turn):
        q0, q1 = qkv[h, 0:rows, 0:128], qkv[h, rows : 2 * rows, 0:128]
        grads = []
        for block in range(2):
            at, seen = slice(block * rows, (block + 1) * rows), (block + 1) * rows
            low = probs[h, at, 0:seen]
            given = gctx[at, lanes(h * HD, HD, HD)]
            prob = low.astype(f32)
            grad_probs = dot_nt(given, qkv[h, 0:seen, 256:384])
            delta = jnp.sum(prob * grad_probs, -1, keepdims=True)
            grad_scores = (prob * (grad_probs - delta)).astype(bf)
            grad_q = dot(grad_scores, qkv[h, 0:seen, 128:256]) * scale
            grad_k = dot_tn(grad_scores, q1 if block else q0) * scale
            grad_v = dot_tn(low, given)
            grads.append((grad_q, grad_k, grad_v))
        (gq0, gk0, gv0), (gq1, gk1, gv1) = grads
        top = jnp.concatenate([gq0, gk0 + gk1[0:rows], gv0 + gv1[0:rows]], 1).astype(bf)
        low_half = jnp.concatenate([gq1, gk1[rows:], gv1[rows:]], 1).astype(bf)
        qkv[h, 0:rows, :] = top
        qkv[h, rows : 2 * rows, :] = low_half
        total = jnp.sum(top.astype(f32), 0, keepdims=True) + jnp.sum(low_half.astype(f32), 0, keepdims=True)
        qv_sum[h] = total
        for half in (other, own):
            product = dot_nt(qkv[h, half, :], wqkv[h])
            if turn == 0:
                nacc[half, :] = product
            else:
                nacc[half, :] += product
            if turn == DEPTH - 1 and half is other:
                x_part(1).wait_send()
                far[0] = nacc[other, :].astype(bf)
                x_part(3).start()
        part = dot(rows_t[...], qkv[h]).astype(bf)
        disassemble(h, part)
        for yy in (1 - y, y):
            rc_copy(Q, h, yy).start()
    early_rows(1)
    head_back(near(3), 0)
    early_rows(2)
    head_back(near(2), 1)
    early_rows(3)
    x_part(2).start()
    reduce_head(near(3))
    each((I, W), ry_add, 3)
    each((I, W), ry_merge, 1)
    out_grads()
    reduce_head(near(2))
    head_back(near(1), 2)
    reduce_out()
    each((I, W), ry_merge, 2)
    head_back(z, 3)
    ry_add(Q, 3)
    finish_mixed()
    reduce_head(near(1))
    ry_add(Q, 2)
    ry_add(O, 3)
    ry_add(Q, 1)
    ry_add(O, 2)
    ry_merge(Q, 2)
    reduce_head(z)
    ry_merge(Q, 1)
    ry_add(O, 1)
    own_total(W)
    finish_input()
    late_start()
    ry_merge(O, 2)
    late_cross()
    z_total(V, y, total_of(V), y_landed(V, z))
    ry_merge(O, 1)
    own_total(Q)
    stores[Q].start()
    own_total(I)
    stores[I].start()
    vec_finish()
    own_total(O)
    stores[O].start()

    stores[W].start()
    for stage in range(3):
        v_copy(stage).wait_send()
    for turn in range(1, 8):
        late_copy(turn).wait_send()
    for step in range(1, DEPTH):
        vz_copy(step).wait_send()
        late_z(step).wait_send()
    for index, ref in enumerate((rows_one, grad_rows, rows_two, grad_attn)):
        x_rows(ref, index).wait_send()
    for index in (2, 3):
        x_part(index).wait_send()
    x_out_core(c).wait_send()
    x_grad_context().wait_send()
    for k in range(4):
        for zz in range(DEPTH):
            for yy in range(2):
                rc_copy(k, zz, yy).wait_send()
            ry_copy(k, zz).wait_send()
        for s in range(1, DEPTH):
            rz_copy(k, s, y, True).wait_send()
    for store in stores:
        store.wait()
    ry_copy(V, z).wait_send()
    for yy in range(2):
        for s in range(1, DEPTH):
            rz_copy(V, s, yy, True).wait_send()


def run_layer(tokens, cotangent, lengths, order, weights, vec_params):
    bf, f32 = jnp.bfloat16, jnp.float32
    rows = tokens.shape[0]
    group = 2 * rows
    owners = 16
    shapes = piece_shapes()
    view = jnp.transpose(weights, (1, 2, 0))
    there = pl.BlockSpec(memory_space=pl.ANY)
    vmem = pl.BlockSpec(memory_space=pltpu.VMEM)
    smem = pl.BlockSpec(memory_space=pltpu.SMEM)

    halved = shapes[:3] + ((HALF, D),)

    def many(count, kinds):
        return [pltpu.VMEM((count,) + s, bf) for s in kinds]

    full = pltpu.VMEM((group, D), bf)
    dma = pltpu.SemaphoreType.DMA
    return pl.pallas_call(
        layer_kernel,
        out_shape=[jax.ShapeDtypeStruct((rows, D), f32)] * 2
        + [jax.ShapeDtypeStruct(s, f32) for s in shapes]
        + [jax.ShapeDtypeStruct(vec_params.shape, f32)],
        in_specs=[smem, smem] + [there] * 3 + [vmem],
        out_specs=[there] * 6 + [vmem],
        scratch_shapes=[pltpu.VMEM((rows, D), f32)] * 4
        + [pltpu.VMEM(s, f32) for s in shapes]
        + [
            pltpu.VMEM((owners,) + shapes[0], bf),
            pltpu.VMEM((owners // 2, BLOCK, D), bf),
            pltpu.VMEM((owners,) + shapes[2], bf),
            pltpu.VMEM((owners,) + shapes[3], bf),
            pltpu.VMEM((DEPTH, D, 3 * HD), bf),
        ]
        + many(2 * DEPTH, shapes)
        + many(DEPTH, halved)
        + many(1, halved[3:])
        + many(DEPTH, halved)
        + many(2 * DEPTH, halved[3:])
        + [
            full,
            full,
            pltpu.VMEM((D, group), bf),
            full,
            full,
            pltpu.VMEM((DEPTH, group, group), bf),
            pltpu.VMEM((DEPTH, group, 3 * HD), bf),
            pltpu.VMEM((group, DEPTH * HD), bf),
            pltpu.VMEM((group, DEPTH * HD), bf),
            pltpu.VMEM((2, rows, D), bf),
            pltpu.VMEM((2, rows, D), bf),
            pltpu.VMEM((owners // 2, BLOCK, D), bf),
            pltpu.VMEM((rows, DEPTH * HD), bf),
            pltpu.VMEM((group, D), f32),
            pltpu.VMEM((group, D), f32),
            pltpu.VMEM((group, 2 * D), bf),
            pltpu.VMEM((group, 2 * D), bf),
            pltpu.VMEM((DEPTH, 1, 512), f32),
            pltpu.VMEM((DEPTH, 1, 3 * HD), f32),
            pltpu.VMEM((DEPTH, 1, 3 * HD), f32),
            pltpu.VMEM((7, 16, D), f32),
            pltpu.VMEM((5, 16, D), f32),
            pltpu.VMEM((32, LANES), f32),
            pltpu.VMEM((32, LANES), f32),
            pltpu.VMEM((12, 32, LANES), f32),
            dma((5, owners)),
            dma((5, DEPTH)),
            dma((5, 2 * DEPTH)),
            dma((5, 2, 2 * DEPTH)),
            dma((4, 2 * DEPTH)),
            dma((4, 2 * DEPTH)),
            dma((5, DEPTH)),
            dma((5, DEPTH)),
            dma((5, 2 * DEPTH)),
            dma((5, 2 * DEPTH)),
            dma((11,)),
            dma((11,)),
            dma((6,)),
            dma((7,)),
            dma((11,)),
            dma((12,)),
            dma((12,)),
        ],
        compiler_params=pltpu.CompilerParams(
            collective_id=0, has_side_effects=True, vmem_limit_bytes=VMEM_LIMIT
        ),
        name="layer",
    )(lengths, order, view, tokens, cotangent, vec_params)


def per_device(
    grp_count,
    tp_count,
    tokens,
    cotangent,
    lengths,
    order,
    weights,
    momentum,
    stat_left,
    stat_right,
    root_left,
    root_right,
    vec_params,
    vec_momentum,
    vec_second,
):
    fits = grp_count == 4 * DEPTH and tp_count == 2 and tokens.shape[0] == 256
    if not fits or lengths.shape[1] != ARTICLES:
        return per_device_general(
            tokens,
            cotangent,
            lengths,
            order,
            weights,
            momentum,
            stat_left,
            stat_right,
            root_left,
            root_right,
            vec_params,
            vec_momentum,
            vec_second,
        )
    token_total = tokens.shape[0] * tp_count * grp_count
    mixed, input_grad, *sums, vec_grads = run_layer(tokens, cotangent, lengths, order, weights, vec_params)
    blocks, vecs, results = update_blocks(
        sums,
        (weights, momentum, stat_left, stat_right, root_left, root_right),
        vec_grads,
        (vec_params, vec_momentum, vec_second),
        (mixed, input_grad),
        token_total,
    )
    return (*results, *blocks, *vecs)


def solution(mesh):
    placed = (
        P(("grp", "tp"), None),
        P(("grp", "tp"), None),
        P("grp", None),
        P("grp", None),
        P(("tp", "grp"), None, None),
        P(("tp", "grp"), None, None),
        P(("tp", "grp"), None, None),
        P(("tp", "grp"), None, None),
        P(("tp", "grp"), None, None),
        P(("tp", "grp"), None, None),
        P(),
        P(),
        P(),
    )
    return jax.shard_map(
        functools.partial(per_device, mesh.shape["grp"], mesh.shape["tp"]),
        mesh=mesh,
        in_specs=placed,
        out_specs=(
            P(("grp", "tp"), None),
            P(("grp", "tp"), None),
            P(("tp", "grp"), None, None),
            P(("tp", "grp"), None, None),
            P(("tp", "grp"), None, None),
            P(("tp", "grp"), None, None),
            P(("tp", "grp"), None, None),
            P(),
            P(),
            P(),
            P(),
        ),
        check_vma=False,
    )
```

```python
import functools

import jax
import jax.numpy as jnp
from jax import lax
from jax.experimental import pallas as pl
from jax.experimental.pallas import tpu as pltpu
from jax.sharding import PartitionSpec as P

D = 1024
HEADS = 8
HD = 128
FF = 4096
BLOCK = 64


EPS = 1e-05
NEG = -1e30
DECAY = 0.9
BETA = 0.9
RATE = 0.05
VEC_DECAY = 0.9
VEC_RATE = 0.2
VEC_EPS = 1e-08


def norm_rows(value, gain, shift):
    average = jnp.mean(value, -1, keepdims=True)
    centred = value - average
    inverse = lax.rsqrt(jnp.mean(centred * centred, -1, keepdims=True) + EPS)
    normed = centred * inverse
    return (normed * gain + shift, normed, inverse)


def norm_back(grad_out, normed, inverse, gain):
    scaled = grad_out * gain
    return inverse * (
        scaled
        - jnp.mean(scaled, -1, keepdims=True)
        - normed * jnp.mean(scaled * normed, -1, keepdims=True)
    )


def segment_ids(lengths_row, order_row, group_rows):
    article_count = lengths_row.shape[0]
    slots = jnp.arange(article_count, dtype=jnp.int32)
    picks = (order_row[:, None] == slots[None, :]).astype(jnp.int32)
    packed = jnp.sum(picks * lengths_row[None, :], 1)
    ends = jnp.cumsum(packed)
    spots = jnp.arange(group_rows, dtype=jnp.int32)
    return jnp.sum((spots[:, None] >= ends[None, :]).astype(jnp.int32), 1)


def allowed_mask(row_ids, row_segs, segments, key_ids, article_count):
    causal = key_ids[None, :] <= row_ids[:, None]
    same = segments[None, :] == row_segs[:, None]
    alone = (row_segs[:, None] < article_count) | (key_ids[None, :] == row_ids[:, None])
    return causal & same & alone


def from_columns(tiles, row_total, col_total):
    return (
        tiles.reshape(col_total // BLOCK, row_total // BLOCK, BLOCK, BLOCK)
        .transpose(1, 2, 0, 3)
        .reshape(row_total, col_total)
    )


def from_rows(tiles, row_total, col_total):
    return (
        tiles.reshape(row_total // BLOCK, col_total // BLOCK, BLOCK, BLOCK)
        .transpose(0, 2, 1, 3)
        .reshape(row_total, col_total)
    )


def to_columns(matrix):
    row_total, col_total = matrix.shape
    return (
        matrix.reshape(row_total // BLOCK, BLOCK, col_total // BLOCK, BLOCK)
        .transpose(2, 0, 1, 3)
        .reshape(-1, BLOCK, BLOCK)
    )


def to_rows(matrix):
    row_total, col_total = matrix.shape
    return (
        matrix.reshape(row_total // BLOCK, BLOCK, col_total // BLOCK, BLOCK)
        .transpose(0, 2, 1, 3)
        .reshape(-1, BLOCK, BLOCK)
    )


def per_device_general(
    tokens,
    cotangent,
    lengths,
    order,
    weights,
    momentum,
    stat_left,
    stat_right,
    root_left,
    root_right,
    vec_params,
    vec_momentum,
    vec_second,
):
    groups = lax.axis_size("grp")
    tp_size = lax.axis_size("tp")
    tp_rank = lax.axis_index("tp")
    tok_rows = tokens.shape[0]
    group_rows = tok_rows * tp_size
    article_count = lengths.shape[1]
    owners = groups * tp_size
    block_area = BLOCK * BLOCK * owners
    qkv_count = 3 * D * D // block_area
    out_count = D * D // block_area
    in_count = D * FF // block_area
    owned_blocks = weights.shape[0]
    heads_here = HEADS // tp_size
    qkv_cols = 3 * D // tp_size
    feat_here = D // tp_size
    ff_here = FF // tp_size
    qv_width = 2 * D // tp_size
    token_total = group_rows * groups
    gathered = lax.all_gather(weights.astype(jnp.bfloat16), "grp", axis=0, tiled=True)
    per_owner = gathered.reshape(groups, owned_blocks, BLOCK, BLOCK)
    marks = [0, qkv_count, qkv_count + out_count, qkv_count + out_count + in_count, owned_blocks]
    pieces = [
        per_owner[:, marks[index] : marks[index + 1]].reshape(-1, BLOCK, BLOCK)
        for index in range(4)
    ]
    w_qkv = from_columns(pieces[0], D, qkv_cols)
    w_out = from_rows(pieces[1], feat_here, D)
    w_in = from_columns(pieces[2], D, ff_here)
    w_down = from_rows(pieces[3], ff_here, D)
    w_qkv_heads = w_qkv.reshape(D, heads_here, 3, HD)
    w_out_heads = w_out.reshape(heads_here, HD, D)
    segments = segment_ids(lengths[0], order[0], group_rows)
    gain_one = vec_params[0]
    shift_one = vec_params[1]
    gain_two = vec_params[2]
    shift_two = vec_params[3]
    bias_out = vec_params[4]
    bias_down = vec_params[5]
    qv_here = lax.dynamic_slice_in_dim(
        vec_params[6:8].reshape(2 * D), tp_rank * qv_width, qv_width
    ).reshape(heads_here, 2, HD)
    bias_heads = jnp.stack(
        [qv_here[:, 0], jnp.zeros((heads_here, HD), jnp.float32), qv_here[:, 1]], 0
    )[:, :, None, :]
    bias_in = lax.dynamic_slice_in_dim(vec_params[8:].reshape(FF), tp_rank * ff_here, ff_here)
    normed_one, unit_one, inverse_one = norm_rows(tokens, gain_one, shift_one)
    rows_one = lax.all_gather(normed_one.astype(jnp.bfloat16), "tp", axis=0, tiled=True)
    projected = (
        jnp.einsum("rx,xhcd->chrd", rows_one, w_qkv_heads, preferred_element_type=jnp.float32)
        + bias_heads
    ).astype(jnp.bfloat16)
    queries = projected[0]
    keys_all = projected[1]
    values_all = projected[2]
    span = min(512, group_rows)
    starts = jnp.arange(group_rows // span, dtype=jnp.int32) * span
    key_ids = jnp.arange(group_rows, dtype=jnp.int32)
    score_scale = HD ** (-0.5)

    def masked_scores(first_row):
        row_ids = first_row + jnp.arange(span, dtype=jnp.int32)
        row_segs = lax.dynamic_slice_in_dim(segments, first_row, span, 0)
        allowed = allowed_mask(row_ids, row_segs, segments, key_ids, article_count)
        query_rows = lax.dynamic_slice_in_dim(queries, first_row, span, 1)
        scores = (
            jnp.einsum("hqd,hkd->hqk", query_rows, keys_all, preferred_element_type=jnp.float32)
            * score_scale
        )
        return (jnp.where(allowed[None], scores, NEG), query_rows)

    def attend(context_buf, first_row):
        scores, query_rows = masked_scores(first_row)
        row_max = jnp.max(scores, -1, keepdims=True)
        expo = jnp.exp(scores - row_max)
        expsum = jnp.sum(expo, -1, keepdims=True)
        probs_low = (expo / expsum).astype(jnp.bfloat16)
        context = jnp.einsum(
            "hqk,hkd->hqd", probs_low, values_all, preferred_element_type=jnp.float32
        ).astype(jnp.bfloat16)
        context_buf = lax.dynamic_update_slice_in_dim(context_buf, context, first_row, 1)
        return (context_buf, (row_max + jnp.log(expsum))[:, :, 0])

    context_low, log_norm = lax.scan(
        attend, jnp.zeros((heads_here, group_rows, HD), jnp.bfloat16), starts
    )
    attn_sum = lax.psum_scatter(
        jnp.einsum(
            "hrd,hde->re", context_low, w_out_heads, preferred_element_type=jnp.float32
        ).astype(jnp.bfloat16),
        "tp",
        scatter_dimension=0,
        tiled=True,
    ).astype(jnp.float32)
    hidden = tokens + attn_sum + bias_out
    normed_two, unit_two, inverse_two = norm_rows(hidden, gain_two, shift_two)
    rows_two = lax.all_gather(normed_two.astype(jnp.bfloat16), "tp", axis=0, tiled=True)
    inner = jnp.dot(rows_two, w_in, preferred_element_type=jnp.float32) + bias_in
    activ, gelu_pull = jax.vjp(jax.nn.gelu, inner)
    activ_low = activ.astype(jnp.bfloat16)
    mixed = (
        hidden
        + lax.psum_scatter(
            jnp.dot(activ_low, w_down, preferred_element_type=jnp.float32).astype(jnp.bfloat16),
            "tp",
            scatter_dimension=0,
            tiled=True,
        ).astype(jnp.float32)
        + bias_down
    )
    grad_low = cotangent.astype(jnp.bfloat16)
    grad_rows = lax.all_gather(grad_low, "tp", axis=0, tiled=True)
    g_down = jnp.einsum("rf,rd->fd", activ_low, grad_rows, preferred_element_type=jnp.float32)
    grad_activ = jnp.einsum("rd,fd->rf", grad_rows, w_down, preferred_element_type=jnp.float32)
    grad_inner = gelu_pull(grad_activ)[0].astype(jnp.bfloat16)
    g_in = jnp.einsum("rd,rf->df", rows_two, grad_inner, preferred_element_type=jnp.float32)
    g_bias_in = jnp.sum(grad_inner.astype(jnp.float32), 0)
    ffn_blocks = jnp.concatenate(
        [
            to_columns(g_in).reshape(groups, in_count, BLOCK, BLOCK),
            to_rows(g_down).reshape(groups, in_count, BLOCK, BLOCK),
        ],
        1,
    )
    grad_normed_two = lax.psum_scatter(
        jnp.einsum("rf,df->rd", grad_inner, w_in, preferred_element_type=jnp.float32).astype(
            jnp.bfloat16
        ),
        "tp",
        scatter_dimension=0,
        tiled=True,
    ).astype(jnp.float32)
    grad_hidden = cotangent + norm_back(grad_normed_two, unit_two, inverse_two, gain_two)
    grad_attn_low = grad_hidden.astype(jnp.bfloat16)
    grad_attn_rows = lax.all_gather(grad_attn_low, "tp", axis=0, tiled=True)
    g_out = jnp.einsum(
        "hrd,re->hde", context_low, grad_attn_rows, preferred_element_type=jnp.float32
    ).reshape(feat_here, D)
    grad_context = jnp.einsum(
        "re,hde->hrd", grad_attn_rows, w_out_heads, preferred_element_type=jnp.float32
    ).astype(jnp.bfloat16)
    zero_heads = jnp.zeros((heads_here, group_rows, HD), jnp.float32)

    def attend_back(carry, inputs):
        grad_queries, grad_keys, grad_values = carry
        first_row, log_block = inputs
        scores, query_rows = masked_scores(first_row)
        probs = jnp.exp(scores - log_block[:, :, None])
        grad_ctx_rows = lax.dynamic_slice_in_dim(grad_context, first_row, span, 1)
        grad_probs = jnp.einsum(
            "hqd,hkd->hqk", grad_ctx_rows, values_all, preferred_element_type=jnp.float32
        )
        delta = jnp.sum(probs * grad_probs, -1, keepdims=True)
        grad_scores = (probs * (grad_probs - delta)).astype(jnp.bfloat16)
        query_part = (
            jnp.einsum("hqk,hkd->hqd", grad_scores, keys_all, preferred_element_type=jnp.float32)
            * score_scale
        )
        grad_queries = lax.dynamic_update_slice_in_dim(grad_queries, query_part, first_row, 1)
        grad_keys = (
            grad_keys
            + jnp.einsum(
                "hqk,hqd->hkd", grad_scores, query_rows, preferred_element_type=jnp.float32
            )
            * score_scale
        )
        grad_values = grad_values + jnp.einsum(
            "hqk,hqd->hkd",
            probs.astype(jnp.bfloat16),
            grad_ctx_rows,
            preferred_element_type=jnp.float32,
        )
        return ((grad_queries, grad_keys, grad_values), None)

    (grad_queries, grad_keys, grad_values), unused = lax.scan(
        attend_back, (zero_heads, zero_heads, zero_heads), (starts, log_norm)
    )
    grad_proj = jnp.stack([grad_queries, grad_keys, grad_values], 0).astype(jnp.bfloat16)
    proj_sums = jnp.sum(grad_proj.astype(jnp.float32), 2)
    g_bias_qv = jnp.stack([proj_sums[0], proj_sums[2]], 1).reshape(qv_width)
    g_qkv = jnp.einsum(
        "rx,chrd->xhcd", rows_one, grad_proj, preferred_element_type=jnp.float32
    ).reshape(D, qkv_cols)
    grad_normed_one = lax.psum_scatter(
        jnp.einsum(
            "chrd,xhcd->rx", grad_proj, w_qkv_heads, preferred_element_type=jnp.float32
        ).astype(jnp.bfloat16),
        "tp",
        scatter_dimension=0,
        tiled=True,
    ).astype(jnp.float32)
    input_grad = grad_hidden + norm_back(grad_normed_one, unit_one, inverse_one, gain_one)
    local_rows = jnp.stack(
        [
            jnp.sum(grad_normed_one * unit_one, 0),
            jnp.sum(grad_normed_one, 0),
            jnp.sum(grad_normed_two * unit_two, 0),
            jnp.sum(grad_normed_two, 0),
            jnp.sum(grad_hidden, 0),
            jnp.sum(cotangent, 0),
        ]
    )
    qv_rows = lax.dynamic_update_slice(
        jnp.zeros((2 * D,), jnp.float32), g_bias_qv, (tp_rank * qv_width,)
    ).reshape(2, D)
    in_rows = lax.dynamic_update_slice(
        jnp.zeros((FF,), jnp.float32), g_bias_in, (tp_rank * ff_here,)
    ).reshape(FF // D, D)
    vec_grads = lax.psum(jnp.concatenate([local_rows, qv_rows, in_rows], 0), ("grp", "tp"))
    attn_blocks = jnp.concatenate(
        [
            to_columns(g_qkv).reshape(groups, qkv_count, BLOCK, BLOCK),
            to_rows(g_out).reshape(groups, out_count, BLOCK, BLOCK),
        ],
        1,
    )
    every_block = jnp.concatenate([attn_blocks, ffn_blocks], 1).reshape(-1, BLOCK, BLOCK)
    weight_grads = lax.psum_scatter(
        every_block.astype(jnp.bfloat16), "grp", scatter_dimension=0, tiled=True
    ).astype(jnp.float32)
    scaled = weight_grads * token_total ** (-0.5)
    stat_left_new = DECAY * stat_left + (1.0 - DECAY) * jnp.einsum(
        "nij,nkj->nik", scaled, scaled, precision=lax.Precision.HIGHEST
    )
    stat_right_new = DECAY * stat_right + (1.0 - DECAY) * jnp.einsum(
        "nji,njk->nik", scaled, scaled, precision=lax.Precision.HIGHEST
    )
    shaped = jnp.einsum("nij,njk->nik", root_left, scaled, precision=lax.Precision.HIGHEST)
    shaped = jnp.einsum("nij,njk->nik", shaped, root_right, precision=lax.Precision.HIGHEST)
    momentum_new = BETA * momentum + shaped
    weights_new = weights - RATE * momentum_new
    vec_scaled = vec_grads * token_total ** (-0.5)
    vec_second_new = VEC_DECAY * vec_second + (1.0 - VEC_DECAY) * vec_scaled * vec_scaled
    vec_momentum_new = BETA * vec_momentum + vec_scaled * lax.rsqrt(vec_second_new + VEC_EPS)
    vec_new = vec_params - VEC_RATE * vec_momentum_new
    return (
        mixed,
        input_grad,
        weight_grads,
        stat_left_new,
        stat_right_new,
        momentum_new,
        weights_new,
        vec_grads,
        vec_second_new,
        vec_momentum_new,
        vec_new,
    )


MESH_ID = pl.DeviceIdType.MESH
LANES = 128
HALF = 64
VMEM_LIMIT = 62 * 2**20
ARTICLES = 4
GELU_A = (2.0 / 3.141592653589793) ** 0.5
GELU_B = 0.044715


def remote(src, dst, send_sem, recv_sem, device):
    return pltpu.make_async_remote_copy(
        src_ref=src,
        dst_ref=dst,
        send_sem=send_sem,
        recv_sem=recv_sem,
        device_id=device,
        device_id_type=MESH_ID,
    )


def place():
    grp = lax.axis_index("grp")
    return lax.div(grp, 4), lax.rem(lax.div(grp, 2), 2), lax.rem(grp, 2), lax.axis_index("tp")


def slot_of(z, y, c):
    return z * 4 + y * 2 + c


def lay_blocks(view_ref, stack, first, last):
    half = view_ref.shape[2] // 2

    def row(i, carry):
        tile = view_ref[i].T
        stack[pl.ds(i, half, stride=BLOCK), :] = jnp.concatenate([tile[:half], tile[half:]], 1)
        return carry

    lax.fori_loop(first, last, row, 0, unroll=8)


def piece_shapes():
    return ((768, LANES), (64, 512), (1024, LANES), (LANES, 1024))


def both_halves(pair):
    low = lax.broadcasted_iota(jnp.int32, pair.shape, 1) < HALF
    turned = pltpu.roll(pair, HALF, 1)
    return jnp.where(low, pair, turned), jnp.where(low, turned, pair)


def update_kernel(
    scale,
    in_q,
    in_o,
    in_i,
    in_d,
    root_l,
    root_r,
    vec_g,
    vecs,
    vec_m,
    vec_s,
    mixed,
    input_grad,
    w,
    m,
    sl,
    sr,
    out_g,
    out_sl,
    out_sr,
    out_m,
    out_w,
    out_vg,
    out_vs,
    out_vm,
    out_v,
    out_mixed,
    out_input_grad,
    grads,
    first,
    second,
    held_l,
    held_r,
    held_w,
    held_m,
    held_sl,
    held_sr,
    sum_q,
    sum_o,
    sum_i,
    sum_d,
    sems,
    block_sems,
    sum_sems,
):
    count = w.shape[2]
    step_rows = out_w.shape[0]
    bf, f32 = jnp.bfloat16, jnp.float32

    def loads(k):
        part = pl.ds(16 * k, 16)
        return [
            pltpu.make_async_copy(root.at[part], held.at[part], sems.at[k, side])
            for side, (root, held) in enumerate(((root_l, held_l), (root_r, held_r)))
        ]

    def block_loads(k):
        part = pl.ds(k * step_rows, step_rows)
        pairs = ((w, held_w), (m, held_m), (sl, held_sl), (sr, held_sr))
        return [pltpu.make_async_copy(a.at[part], b.at[part], block_sems.at[k, n]) for n, (a, b) in enumerate(pairs)]

    out_mixed[...] = mixed[...]
    out_input_grad[...] = input_grad[...]

    @pl.when(pl.program_id(0) == 0)
    def _():
        for k in range(4):
            for load in loads(k):
                load.start()
        sum_loads = [
            pltpu.make_async_copy(a, b, sum_sems.at[n])
            for n, (a, b) in enumerate(((in_q, sum_q), (in_o, sum_o), (in_i, sum_i), (in_d, sum_d)))
        ]
        for load in sum_loads:
            load.start()
        for k in range(BLOCK // step_rows):
            for load in block_loads(k):
                load.start()
        total = vec_g[...]
        out_vg[...] = total
        scaled = total * scale
        fresh = VEC_DECAY * vec_s[...] + (1.0 - VEC_DECAY) * scaled * scaled
        out_vs[...] = fresh
        momentum = BETA * vec_m[...] + scaled * lax.rsqrt(fresh + VEC_EPS)
        out_vm[...] = momentum
        out_v[...] = vecs[...] - VEC_RATE * momentum
        def row(i, carry):
            both = jnp.concatenate([held_l[i], held_r[i]], 0)
            second[pl.ds(i, count, stride=BLOCK), :] = both.T
            return carry

        for k in range(4):
            for load in loads(k):
                load.wait()
            lax.fori_loop(16 * k, 16 * k + 16, row, 0, unroll=8)
        for load in sum_loads:
            load.wait()
        rows = sum_q.shape[0]
        grads[0:rows, 0:HALF] = sum_q[:, 0:HALF]
        grads[rows : 2 * rows, 0:HALF] = sum_q[:, HALF:LANES]
        base = 2 * rows
        for b in range(8):
            grads[base + b * 64 : base + b * 64 + 64, 0:HALF] = sum_o[:, b * HALF : (b + 1) * HALF]
        base += 512
        grads[base : base + D, 0:HALF] = sum_i[:, 0:HALF]
        grads[0:D, HALF:LANES] = sum_i[:, HALF:LANES]
        for r in range(2):
            for b in range(16):
                at = D + (r * 16 + b) * 64
                grads[at : at + 64, HALF:LANES] = sum_d[r * 64 : r * 64 + 64, b * HALF : (b + 1) * HALF]

        row_id = lax.broadcasted_iota(jnp.int32, (256, 256), 0)
        col_id = lax.broadcasted_iota(jnp.int32, (256, 256), 1)
        mask = lax.shift_right_logical(row_id, 6) == lax.shift_right_logical(col_id, 6)
        low = lax.broadcasted_iota(jnp.int32, (256, LANES), 1) < HALF

        def spread(v):
            return jnp.where(mask, jnp.concatenate([v, v], 1), 0.0).astype(bf)

        def eight(k, carry):
            at = pl.ds(pl.multiple_of(k * 256, 256), 256)
            for side, grad in enumerate(both_halves(grads[at, :])):
                to = pl.ds(pl.multiple_of(k * 256 + side * (count // 2 * BLOCK), 256), 256)
                left, right = both_halves(second[to, :])
                s32 = grad * scale
                s = s32.astype(bf)
                outer = lax.dot_general(s[:, 0:HALF], s[:, 0:HALF], (((1,), (1,)), ((), ())), preferred_element_type=f32)
                kept = jnp.where(mask, outer, 0.0)
                kept = kept[:, :LANES] + kept[:, LANES:]
                outer = kept + pltpu.roll(kept, HALF, 1)
                inner = lax.dot_general(spread(s32), s, (((0,), (0,)), ((), ())), preferred_element_type=f32)
                shaped = jnp.dot(spread(left), s, preferred_element_type=f32)
                shaped = jnp.dot(spread(shaped), right.astype(bf), preferred_element_type=f32)
                first[to, :] = jnp.where(low, grad, outer)
                second[to, :] = jnp.where(low, inner, shaped)
            return carry

        lax.fori_loop(0, count // 8, eight, 0, unroll=4)

    i0 = pl.program_id(0) * step_rows
    for load in block_loads(pl.program_id(0)):
        load.wait()
    unit = lax.broadcasted_iota(jnp.int32, (LANES, LANES), 0) == lax.broadcasted_iota(jnp.int32, (LANES, LANES), 1)
    unit = unit.astype(f32).astype(bf)

    def turned(tile):
        high = tile.astype(bf)
        rest = (tile - high.astype(f32)).astype(bf)
        over = (((1,), (1,)), ((), ()))
        return lax.dot_general(unit, high, over, preferred_element_type=f32) + lax.dot_general(
            unit, rest, over, preferred_element_type=f32
        )


    def rows_out(ii, carry):
        i = i0 + ii
        at = pl.ds(i, count, stride=BLOCK)
        one = first[at, :].T
        two = turned(second[at, :])
        out_g[ii] = one[0:HALF]
        out_sl[ii] = DECAY * held_sl[i] + (1.0 - DECAY) * one[HALF:LANES]
        out_sr[ii] = DECAY * held_sr[i] + (1.0 - DECAY) * two[0:HALF]
        fresh = BETA * held_m[i] + two[HALF:LANES]
        out_m[ii] = fresh
        out_w[ii] = held_w[i] - RATE * fresh
        return carry

    lax.fori_loop(0, step_rows, rows_out, 0, unroll=True)


def update_blocks(sums, blocks, vec_grads, vecs, results, token_total):
    views = [jnp.transpose(a, (1, 2, 0)) for a in blocks]
    count = blocks[0].shape[0]
    rows = 16
    whole = pl.BlockSpec(memory_space=pltpu.VMEM)
    steps = BLOCK // rows
    some = pl.BlockSpec((results[0].shape[0] // steps, results[0].shape[1]), lambda i: (i, 0))
    there = pl.BlockSpec(memory_space=pl.ANY)
    part = pl.BlockSpec((rows, BLOCK, count), lambda i: (i, 0, 0))
    vec = jax.ShapeDtypeStruct(vec_grads.shape, jnp.float32)
    outs = pl.pallas_call(
        functools.partial(update_kernel, token_total ** (-0.5)),
        grid=(steps,),
        out_shape=[jax.ShapeDtypeStruct((BLOCK, BLOCK, count), jnp.float32)] * 5
        + [vec] * 4
        + [jax.ShapeDtypeStruct(a.shape, a.dtype) for a in results],
        in_specs=[there] * 6 + [whole] * 4 + [some] * 2 + [there] * 4,
        out_specs=[part] * 5 + [whole] * 4 + [some] * 2,
        scratch_shapes=[
            pltpu.VMEM((count // 2 * BLOCK, LANES), jnp.float32),
            pltpu.VMEM((count * BLOCK, LANES), jnp.float32),
            pltpu.VMEM((count * BLOCK, LANES), jnp.float32),
            *[pltpu.VMEM((BLOCK, BLOCK, count), jnp.float32)] * 6,
            *[pltpu.VMEM(a.shape, a.dtype) for a in sums],
            pltpu.SemaphoreType.DMA((4, 2)),
            pltpu.SemaphoreType.DMA((BLOCK // rows, 4)),
            pltpu.SemaphoreType.DMA((4,)),
        ],
        compiler_params=pltpu.CompilerParams(vmem_limit_bytes=VMEM_LIMIT),
        name="update_blocks",
    )(*sums, *views[4:], vec_grads, *vecs, *results, *views[:4])
    return [jnp.transpose(a, (2, 0, 1)) for a in outs[:5]], outs[5:9], outs[9:]


DEPTH = 4


def layer_kernel(
    lengths,
    order,
    view,
    tokens_in,
    cot_in,
    vecs,
    mixed_there,
    input_grad_there,
    out_q,
    out_o,
    out_i,
    out_d,
    vec_grads,
    tokens,
    cot,
    mixed,
    input_grad,
    sum_q,
    sum_o,
    sum_i,
    sum_d,
    gq,
    go,
    gi,
    gd,
    wqkv,
    cq,
    co,
    ci,
    cd,
    yq,
    yo,
    yi,
    yd,
    yv,
    zq,
    zo,
    zi,
    zd,
    zv,
    rows_one,
    rows_two,
    rows_t,
    grad_rows,
    grad_attn,
    probs,
    qkv,
    ctx,
    gctx,
    far,
    inx,
    go_x,
    ctx_x,
    macc,
    nacc,
    act,
    gin,
    bias_sum,
    qkv_bias,
    qv_sum,
    vin,
    vout,
    late,
    late_sum,
    late_in,
    recv,
    send_y,
    send_c,
    send_z,
    rc_recv,
    rc_send,
    ry_recv,
    ry_send,
    rz_recv,
    rz_send,
    x_send,
    x_recv,
    v_send,
    v_recv,
    l_send,
    l_recv,
    copy_sem,
):
    bf, f32 = jnp.bfloat16, jnp.float32
    z, y, c, t = place()
    me = slot_of(z, y, c)
    x_peer = (me, 1 - t)
    y_peer = (slot_of(z, 1 - y, c), t)
    c_peer = (slot_of(z, y, 1 - c), t)
    rows = tokens.shape[0]
    own = pl.ds(pl.multiple_of(t * rows, rows), rows)
    other = pl.ds(pl.multiple_of((1 - t) * rows, rows), rows)

    def lanes(start, size, unit):
        return pl.ds(pl.multiple_of(start, unit), size)

    gathered, core_in = (gq, go, gi, gd), (cq, co, ci, cd)
    y_in, z_in = (yq, yo, yi, yd, yv), (zq, zo, zi, zd, zv)
    sums = (sum_q, sum_o, sum_i, sum_d)
    Q, O, I, W, V = range(5)

    def dot(a, b):
        return jnp.dot(a, b, preferred_element_type=f32)

    def dot_nt(a, b):
        return lax.dot_general(a, b, (((1,), (1,)), ((), ())), preferred_element_type=f32)

    def dot_tn(a, b):
        return lax.dot_general(a, b, (((0,), (0,)), ((), ())), preferred_element_type=f32)

    def piece(k, zz, yy, cc):
        if k == O:
            return go.at[zz * 2 + yy, :, pl.ds(pl.multiple_of(cc * 512, 512), 512)]
        return gathered[k].at[slot_of(zz, yy, cc)]

    def near(s):
        return lax.rem(z + (1 - 2 * lax.div(z, 2)) * s + DEPTH, DEPTH)

    def ag_piece(k, zz, yy, cc):
        if k == W:
            return gd.at[slot_of(zz, yy, cc), 0:HALF]
        if k == V:
            return gd.at[slot_of(zz, yy, cc), HALF:LANES]
        return piece(k, zz, yy, cc)

    def ag_copy(k, zz, yy, way):
        src = ag_piece(k, zz, yy, c)
        sem = recv.at[k, slot_of(zz, yy, c)]
        if way == "up":
            return remote(src, src, send_z.at[k, 0, yy * DEPTH + zz], sem, (slot_of(z + 1, y, c), t))
        if way == "down":
            return remote(src, src, send_z.at[k, 1, yy * DEPTH + zz], sem, (slot_of(z - 1, y, c), t))
        if way == "y":
            return remote(src, src, send_y.at[k, zz], sem, y_peer)
        return remote(src, src, send_c.at[k, yy * DEPTH + zz], sem, c_peer)

    def ag_wait(k, zz, yy, cc):
        ref = ag_piece(k, zz, yy, cc)
        remote(ref, ref, send_y.at[k, 0], recv.at[k, slot_of(zz, yy, cc)], y_peer).wait_recv()

    def own_sends_z(k):
        @pl.when(z < DEPTH - 1)
        def _():
            ag_copy(k, z, y, "up").start()

        @pl.when(z > 0)
        def _():
            ag_copy(k, z, y, "down").start()

        ag_copy(k, z, y, "core").start()

    def own_sends_y(k):
        ag_copy(k, z, y, "y").start()

    def z_arrival(kinds, dist):
        @pl.when(z >= dist)
        def _():
            for k in kinds:
                ag_wait(k, z - dist, y, c)

                @pl.when(z < DEPTH - 1)
                def _():
                    ag_copy(k, z - dist, y, "up").start()

                ag_copy(k, z - dist, y, "y").start()
                ag_copy(k, z - dist, y, "core").start()

        @pl.when(z + dist < DEPTH)
        def _():
            for k in kinds:
                ag_wait(k, z + dist, y, c)

                @pl.when(z > 0)
                def _():
                    ag_copy(k, z + dist, y, "down").start()

                ag_copy(k, z + dist, y, "y").start()
                ag_copy(k, z + dist, y, "core").start()

    def y_arrival(kinds, dist):
        def one(zz):
            for k in kinds:
                ag_wait(k, zz, 1 - y, c)
                ag_copy(k, zz, 1 - y, "core").start()

        if dist == 0:
            one(z)
            return

        @pl.when(z >= dist)
        def _():
            one(z - dist)

        @pl.when(z + dist < DEPTH)
        def _():
            one(z + dist)

    def v_forward(zz, yy):
        ag_wait(V, zz, yy, c)

        @pl.when((zz <= z) & (z < DEPTH - 1))
        def _():
            ag_copy(V, zz, yy, "up").start()

        @pl.when((zz >= z) & (z > 0))
        def _():
            ag_copy(V, zz, yy, "down").start()

        ag_copy(V, zz, yy, "core").start()

    def v_arrival(dist):
        for yy in (y, 1 - y):

            @pl.when(z >= dist)
            def _():
                v_forward(z - dist, yy)

            @pl.when(z + dist < DEPTH)
            def _():
                v_forward(z + dist, yy)

    def drain(k, zz, yy):
        ag_copy(k, zz, yy, "core").wait_send()
        if k == V:

            @pl.when((yy == y) & (zz == z))
            def _():
                ag_copy(k, zz, yy, "y").wait_send()

            @pl.when((zz <= z) & (z < DEPTH - 1))
            def _():
                ag_copy(k, zz, yy, "up").wait_send()

            @pl.when((zz >= z) & (z > 0))
            def _():
                ag_copy(k, zz, yy, "down").wait_send()

            return

        @pl.when(yy == y)
        def _():
            ag_copy(k, zz, y, "y").wait_send()

            @pl.when((zz <= z) & (z < DEPTH - 1))
            def _():
                ag_copy(k, zz, y, "up").wait_send()

            @pl.when((zz >= z) & (z > 0))
            def _():
                ag_copy(k, zz, y, "down").wait_send()

    def add(dst, *terms):
        count, width = dst.shape
        step = min(count, 256 * LANES // width)

        def body(i, carry):
            at = pl.ds(pl.multiple_of(i * step, 16), step)
            if len(terms) == 2 and dst.dtype == bf:
                dst[at, :] = terms[0][at, :] + terms[1][at, :]
                return carry
            total = terms[0][at, :].astype(f32)
            for term in terms[1:]:
                total = total + term[at, :].astype(f32)
            dst[at, :] = total.astype(dst.dtype)
            return carry

        lax.fori_loop(0, count // step, body, 0, unroll=2)

    side = lax.div(z, 2)
    end_z, inner_z = 3 * side, 1 + side
    is_end = z == end_z

    def rc_copy(k, zz, yy):
        at = zz * 2 + yy
        return remote(piece(k, zz, yy, 1 - c), core_in[k].at[at], rc_send.at[k, at], rc_recv.at[k, at], c_peer)

    def ry_copy(k, zz):
        if k == V:
            return remote(ag_piece(V, z, 1 - y, c), y_in[V].at[0], ry_send.at[V, 0], ry_recv.at[V, 0], y_peer)
        return remote(ag_piece(k, zz, 1 - y, c), y_in[k].at[zz], ry_send.at[k, zz], ry_recv.at[k, zz], y_peer)

    def z_slot(k, slot, yy):
        return z_in[k].at[slot * 2 + yy if k == V else slot]

    def z_sem(slot, yy):
        return slot * 2 + yy

    def rz_copy(k, s, yy, from_end):
        slot = s - 1 if from_end else {3: 0, 2: 1, 1: 3}[s]
        to = inner_z if from_end else {3: end_z, 2: 3 - end_z, 1: 3 - inner_z}[s]
        sent, landed = rz_send.at[k, (s - 1) * 2 + yy], rz_recv.at[k, z_sem(slot, yy)]
        return remote(ag_piece(k, near(s), yy, c), z_slot(k, slot, yy), sent, landed, (slot_of(to, y, c), t))

    def z_landed(k, slot, yy):
        ref = z_slot(k, slot, yy)
        remote(ref, ref, rz_send.at[k, 0], rz_recv.at[k, z_sem(slot, yy)], y_peer).wait_recv()
        return ref

    def y_landed(k, zz):
        ref = y_in[k].at[0 if k == V else zz]
        remote(ref, ref, ry_send.at[k, 0], ry_recv.at[k, 0 if k == V else zz], y_peer).wait_recv()
        return ref

    def rc_add(k, zz, yy):
        at = zz * 2 + yy
        remote(core_in[k].at[at], core_in[k].at[at], rc_send.at[k, 0], rc_recv.at[k, at], c_peer).wait_recv()
        mine = piece(k, zz, yy, c)
        add(mine, mine, core_in[k].at[at])

        @pl.when(yy != y)
        def _():
            ry_copy(k, zz).start()

    def z_step(k, s, yy, *terms):
        mine = ag_piece(k, near(s), yy, c)
        if terms:
            add(mine, mine, *terms)

        @pl.when(is_end)
        def _():
            rz_copy(k, s, yy, True).start()

        if s == 3:

            @pl.when(jnp.logical_not(is_end))
            def _():
                rz_copy(k, s, yy, False).start()

    def z_merge(k, s, yy):
        @pl.when(jnp.logical_not(is_end))
        def _():
            mine = ag_piece(k, near(s), yy, c)
            add(mine, mine, z_landed(k, s, yy))
            rz_copy(k, s, yy, False).start()

    def ry_add(k, s):
        z_step(k, s, y, y_landed(k, near(s)))

    def ry_merge(k, s):
        z_merge(k, s, y)

    def total_of(k):
        return sum_d.at[(k - W) * HALF : (k - W + 1) * HALF] if k >= W else sums[k]

    def z_total(k, yy, dst, *terms):
        mine = ag_piece(k, z, yy, c)
        first = z_landed(k, 0, yy)

        @pl.when(is_end)
        def _():
            add(dst, mine, first, z_landed(k, 1, yy), *terms)

        @pl.when(jnp.logical_not(is_end))
        def _():
            add(dst, mine, first, z_landed(k, 3, yy), *terms)

    def own_total(k):
        z_total(k, y, total_of(k), y_landed(k, z))

    def v_cross():
        mine = ag_piece(V, z, 1 - y, c)
        z_total(V, 1 - y, mine)
        ry_copy(V, z).start()

    def x_rows(ref, index):
        return remote(ref.at[own], ref.at[own], x_send.at[index], x_recv.at[index], x_peer)

    def x_rows_wait(ref, index):
        remote(ref.at[other], ref.at[other], x_send.at[index], x_recv.at[index], x_peer).wait_recv()

    def x_part(index):
        slot = 1 if index == 2 else 0
        return remote(far.at[slot], inx.at[slot], x_send.at[5 + index], x_recv.at[5 + index], x_peer)

    def by_rows(body, step=64):
        def run(i, carry):
            body(pl.multiple_of(i * step, step), step)
            return carry

        lax.fori_loop(0, rows // step, run, 0, unroll=2)

    def norm(value):
        average = jnp.mean(value, -1, keepdims=True)
        centred = value - average
        inverse = lax.rsqrt(jnp.mean(centred * centred, -1, keepdims=True) + EPS)
        return centred * inverse, inverse

    def norm_grad(grad, unit, inverse, gain):
        scaled = grad * gain
        return inverse * (
            scaled - jnp.mean(scaled, -1, keepdims=True) - unit * jnp.mean(scaled * unit, -1, keepdims=True)
        )

    def x_out():
        half = (slice(None), slice(None), lanes(c * 512, 512, 512))
        return remote(go.at[half], go_x.at[half], x_send.at[4], x_recv.at[4], x_peer)

    def x_out_core(cc):
        half = (slice(None), slice(None), lanes(cc * 512, 512, 512))
        return remote(go_x.at[half], go_x.at[half], x_send.at[9], x_recv.at[9], c_peer)

    def x_grad_context():
        return remote(ctx_x, gctx.at[own], x_send.at[10], x_recv.at[10], x_peer)

    def x_grad_context_wait():
        remote(gctx.at[other], gctx.at[other], x_send.at[10], x_recv.at[10], x_peer).wait_recv()

    stages = (x_peer, c_peer, y_peer)

    def v_copy(stage):
        return remote(vout.at[1 + stage], vin.at[stage], v_send.at[stage], v_recv.at[stage], stages[stage])

    def vz_copy(step):
        peer = (slot_of(lax.rem(z + step, DEPTH), y, c), t)
        return remote(vout.at[4], vin.at[3 + z], v_send.at[2 + step], v_recv.at[3 + z], peer)

    def early_rows(hop):
        if hop == 0:
            vout[1] = vout[0]
        else:
            v_copy(hop - 1).wait_recv()
            vout[1 + hop] = vout[hop] + vin[hop - 1]
        if hop < 3:
            v_copy(hop).start()
        else:
            for step in range(1, DEPTH):
                vz_copy(step).start()
            vin[3 + z] = vout[4]

    def late_turn(turn):
        dx, dy, dc = turn // 4, turn // 2 % 2, turn % 2
        xx, yy, cc = (1 - t if dx else t), (1 - y if dy else y), (1 - c if dc else c)
        return (slot_of(z, yy, cc), xx), xx * 4 + yy * 2 + cc

    def late_copy(turn):
        here = t * 4 + y * 2 + c
        return remote(late, late_in.at[here], l_send.at[turn], l_recv.at[here], late_turn(turn)[0])

    def late_wait(index):
        remote(late_in.at[index], late_in.at[index], l_send.at[0], l_recv.at[index], y_peer).wait_recv()

    def late_z(step):
        peer = (slot_of(lax.rem(z + step, DEPTH), y, c), t)
        return remote(late_sum, late_in.at[8 + z], l_send.at[7 + step], l_recv.at[8 + z], peer)

    stores = [
        pltpu.make_async_copy(a, b, copy_sem.at[6 + n])
        for n, (a, b) in enumerate(
            (
                (sum_q, out_q),
                (sum_o, out_o),
                (sum_i, out_i),
                (sum_d, out_d),
                (mixed, mixed_there),
                (input_grad, input_grad_there),
            )
        )
    ]

    barrier = pltpu.get_barrier_semaphore()
    z_peers = [(slot_of(lax.rem(z + step, DEPTH), y, c), t) for step in range(1, DEPTH)]
    everyone = [late_turn(turn)[0] for turn in range(1, 8)] + z_peers
    for device in everyone:
        pl.semaphore_signal(barrier, inc=1, device_id=device, device_id_type=MESH_ID)

    row_loads = [pltpu.make_async_copy(tokens_in, tokens, copy_sem.at[4]), pltpu.make_async_copy(cot_in, cot, copy_sem.at[5])]

    def prepare(held, stack):
        parts = [pl.ds(16 * k, 16) for k in range(4)]
        loads = [pltpu.make_async_copy(view.at[part], held.at[part], copy_sem.at[k]) for k, part in enumerate(parts)]
        for load in loads:
            load.start()
        for load in row_loads:
            load.start()

        def first_norm(at, step):
            unit, inverse = norm(tokens[pl.ds(at, step), :])
            to = pl.ds(pl.multiple_of(t * rows + at, step), step)
            rows_one[to, :] = (unit * vecs[0:1, :] + vecs[1:2, :]).astype(bf)
            grad_rows[to, :] = cot[pl.ds(at, step), :].astype(bf)

        for k, load in enumerate(loads):
            load.wait()
            lay_blocks(held, stack, 16 * k, 16 * k + 16)

        def pair(left, right, count, left_high=False, right_high=False):
            first, second = stack[left : left + count, :], stack[right : right + count, :]
            first = pltpu.roll(first, HALF, 1) if left_high else first
            second = second if right_high else pltpu.roll(second, HALF, 1)
            lane = lax.broadcasted_iota(jnp.int32, (count, LANES), 1)
            return jnp.where(lane < HALF, first, second).astype(bf)

        n = gq.shape[1]
        gq[me] = pair(0, n, n)
        base = 2 * n
        wide = [pair(base + b * 64, base + b * 64 + 64, 64) for b in range(0, 8, 2)]
        go[z * 2 + y, :, lanes(c * 512, 512, 512)] = jnp.concatenate(wide, 1)
        pl.semaphore_wait(barrier, len(everyone))
        for k in (Q, O):
            own_sends_y(k)
            own_sends_z(k)
        for load in row_loads:
            load.wait()
        by_rows(first_norm)
        x_rows(rows_one, 0).start()
        base += 512
        gi[me] = pair(base, 0, D, right_high=True)
        for r in range(2):
            for b in range(0, 16, 2):
                at = D + (r * 16 + b) * 64
                gd[me, r * 64 : r * 64 + 64, b * HALF : b * HALF + LANES] = pair(at, at + 64, 64, True, True)

    pl.run_scoped(
        prepare,
        pltpu.VMEM(view.shape, f32),
        pltpu.VMEM((view.shape[2] // 2 * BLOCK, LANES), f32),
    )
    x_rows(grad_rows, 1).start()
    z_arrival((Q, O), 1)
    y_arrival((Q, O), 0)
    z_arrival((Q, O), 2)
    for k in (I, W, V):
        own_sends_z(k)
    own_sends_y(I)
    y_arrival((Q, O), 1)

    def core_waits(kinds, zz):
        for k in kinds:
            for yy in (y, 1 - y):
                ag_wait(k, zz, yy, 1 - c)

    x_rows_wait(rows_one, 0)

    ends = []
    for p in range(ARTICLES):
        length = 0
        for a in range(ARTICLES):
            length = length + jnp.where(order[0, p] == a, lengths[0, a], 0)
        ends.append(length + ends[-1] if p else length)

    def allowed(first, count):
        ids = lax.broadcasted_iota(jnp.int32, (rows, 1), 0) + first
        start = jnp.zeros((rows, 1), jnp.int32)
        for end in ends:
            start = jnp.where(ids >= end, end, start)
        start = jnp.where(ids >= ends[-1], ids, start)
        keys = lax.broadcasted_iota(jnp.int32, (rows, count), 1)
        return (keys <= ids) & (keys >= start)

    scale = HD ** (-0.5)

    def assemble(h):
        for yy in range(2):
            even, odd = gq.at[slot_of(h, yy, 0)], gq.at[slot_of(h, yy, 1)]
            at = yy * 192
            wqkv[h, 0:768, at : at + 64] = even[:, 0:64]
            wqkv[h, 768:1024, at : at + 64] = even[0:256, 64:128]
            wqkv[h, 0:512, at + 64 : at + 128] = even[256:768, 64:128]
            wqkv[h, 512:1024, at + 64 : at + 128] = odd[0:512, 0:64]
            wqkv[h, 0:256, at + 128 : at + 192] = odd[512:768, 0:64]
            wqkv[h, 256:1024, at + 128 : at + 192] = odd[:, 64:128]

    def disassemble(h, value):
        for yy in range(2):
            even, odd = gq.at[slot_of(h, yy, 0)], gq.at[slot_of(h, yy, 1)]
            at = yy * 192
            even[:, 0:64] = value[0:768, at : at + 64]
            even[0:256, 64:128] = value[768:1024, at : at + 64]
            even[256:768, 64:128] = value[0:512, at + 64 : at + 128]
            odd[0:512, 0:64] = value[512:1024, at + 64 : at + 128]
            odd[512:768, 0:64] = value[0:256, at + 128 : at + 192]
            odd[:, 64:128] = value[256:1024, at + 128 : at + 192]

    qv = vecs[pl.ds(6 + t, 1), :]
    for h in range(DEPTH):
        none = jnp.zeros((1, HD), f32)
        qkv_bias[h] = jnp.concatenate([qv[:, h * 256 : h * 256 + 128], none, qv[:, h * 256 + 128 : h * 256 + 256]], 1)

    def head(h):
        core_waits((Q,), h)
        assemble(h)
        qkv[h] = (dot(rows_one[...], wqkv[h]) + qkv_bias[h]).astype(bf)
        for block in range(2):
            at, seen = slice(block * rows, (block + 1) * rows), (block + 1) * rows
            scores = dot_nt(qkv[h, at, 0:128], qkv[h, 0:seen, 128:256]) * scale
            scores = jnp.where(allowed(block * rows, seen), scores, NEG)
            expo = jnp.exp(scores - jnp.max(scores, -1, keepdims=True))
            low = (expo * (1.0 / jnp.sum(expo, -1, keepdims=True))).astype(bf)
            probs[h, at, 0:seen] = low
            ctx[at, lanes(h * HD, HD, HD)] = dot(low, qkv[h, 0:seen, 256:384]).astype(bf)

    head(near(0))
    y_arrival((Q, O), 2)
    z_arrival((Q, O), 3)
    y_arrival((Q, O), 3)
    own_sends_y(W)
    head(near(1))
    own_sends_y(V)
    head(near(2))
    z_arrival((I, W), 1)
    head(near(3))
    y_arrival((I, W), 0)
    for zz in range(DEPTH):
        core_waits((O,), zz)
    def w_out(ref):
        return ref[...].reshape(DEPTH * HD, D)
    far[0] = dot(ctx[other, :], w_out(go)).astype(bf)
    x_part(0).start()
    mixed[...] = tokens[...] + dot(ctx[own, :], w_out(go)) + vecs[4:5, :]
    z_arrival((I, W), 2)
    x_part(0).wait_recv()
    def second_norm(at, step):
        value = mixed[pl.ds(at, step), :] + inx[0, pl.ds(at, step), :].astype(f32)
        mixed[pl.ds(at, step), :] = value
        unit, inverse = norm(value)
        to = pl.ds(pl.multiple_of(t * rows + at, step), step)
        rows_two[to, :] = (unit * vecs[2:3, :] + vecs[3:4, :]).astype(bf)
    x_rows_wait(grad_rows, 1)
    by_rows(second_norm)
    x_rows(rows_two, 2).start()
    v_forward(z, 1 - y)
    macc[...] = jnp.zeros_like(macc)
    y_arrival((I, W), 1)
    nacc[...] = jnp.zeros_like(nacc)
    vout[...] = jnp.zeros_like(vout)
    z_arrival((I, W), 3)
    def ffn(half, zz):
        first = 4 * zz
        at = pl.ds(pl.multiple_of(lax.rem(t + half, 2) * rows, rows), rows)
        units = lanes(zz * 512, 512, 512)
        bias_row = vecs[pl.ds(8 + 2 * t + lax.div(zz, 2), 1), lanes(lax.rem(zz, 2) * 512, 512, 512)]

        def w_in(start, count):
            return jnp.concatenate([gi[first + j, start : start + count, :] for j in range(4)], 1)

        def w_down(start, count):
            return gd[pl.ds(first, 4), :, start : start + count].reshape(512, count)

        inner = dot(rows_two[at, :], w_in(0, D)) + bias_row
        square = inner * inner
        bent = jnp.tanh(GELU_A * inner * (1.0 + GELU_B * square))
        act[at, units] = (0.5 * inner * (1.0 + bent)).astype(bf)
        slope = 0.5 * (1.0 + bent) + 0.5 * inner * (1.0 - bent * bent) * (GELU_A * (1.0 + 3.0 * GELU_B * square))
        gin[at, units] = (dot_nt(grad_rows[at, :], w_down(0, D)) * slope).astype(bf)
        for nb in range(4):
            out = slice(nb * 256, nb * 256 + 256)
            nacc[at, out] += dot_nt(gin[at, units], w_in(nb * 256, 256))
            macc[at, out] += dot(act[at, units], w_down(nb * 256, 256))
    def ffn_grads(zz):
        first = 4 * zz
        units = lanes(zz * 512, 512, 512)
        for k in (I, W, V):
            for yy in range(2):
                drain(k, zz, yy)
        bias_sum[zz] = jnp.sum(gin[:, units].astype(f32), 0, keepdims=True)
        for nb in range(4):
            out = slice(nb * 256, nb * 256 + 256)
            part = dot(rows_t[out, :], gin[:, units]).astype(bf)
            for j in range(4):
                gi[first + j, out, :] = part[:, j * LANES : (j + 1) * LANES]
        for yy in (1 - y, y):
            rc_copy(I, zz, yy).start()
        act_t = act[:, units].T
        for nb in range(4):
            out = slice(nb * 256, nb * 256 + 256)
            part = dot(act_t, grad_rows[:, out]).astype(bf)
            gd[pl.ds(first, 4), :, out] = part.reshape(4, LANES, 256)
        for yy in (1 - y, y):
            rc_copy(W, zz, yy).start()
    def each(kinds, step, *args):
        for k in kinds:
            step(k, *args)
    def reduce_out():
        for yy in (1 - y, y):
            for s in (3, 2, 1, 0):
                rc_add(O, near(s), yy)
    def reduce_head(zz):
        for yy in (1 - y, y):
            rc_add(Q, zz, yy)
    v_arrival(1)
    def reduce_core(zz):
        for yy in (1 - y, y):
            for k in (I, W):
                rc_add(k, zz, yy)
    def v_step(s):
        for yy in (1 - y, y):
            z_step(V, s, yy)
    def v_merge(s):
        for yy in (1 - y, y):
            z_merge(V, s, yy)
    core_waits((I, W, V), z)
    ffn(0, z)
    core_waits((I, W, V), near(1))
    ffn(0, near(1))
    x_rows_wait(rows_two, 2)
    x_out().start()
    v_arrival(2)
    rows_t[...] = rows_two[...].T
    y_arrival((I, W), 2)
    def by_z(s, carry):
        @pl.when(s == 2)
        def _():
            v_arrival(3)
            y_arrival((I, W), 3)

        @pl.when(s >= 2)
        def _():
            core_waits((I, W, V), near(s))
            ffn(0, near(s))

        ffn(1, near(s))

        @pl.when(s == DEPTH - 1)
        def _():
            x_part(0).wait_send()
            far[0] = nacc[other, :].astype(bf)
            x_part(1).start()

        ffn_grads(near(s))

        @pl.when(s > 0)
        def _():
            reduce_core(near(s - 1))

        for before in (1, 2):

            @pl.when(s == before + 1)
            def _():
                v_step(before)

        return carry
    lax.fori_loop(0, DEPTH, by_z, 0)
    x_out().wait_recv()
    reduce_core(near(3))
    x_out_core(c).start()
    v_step(3)
    rows_t[...] = rows_one[...].T
    for zz in range(DEPTH):
        for side in range(2):
            row, start = 8 + 2 * side + zz // 2, zz % 2 * 512
            vout[0, row : row + 1, start : start + 512] = jnp.where(t == side, bias_sum[zz], 0.0)
    v_merge(1)
    x_part(1).wait_recv()
    def row_sum(row, value):
        vout[0, row : row + 1, :] += jnp.sum(value, 0, keepdims=True)
    def second_back(at, step):
        here = pl.ds(at, step)
        in_group = pl.ds(pl.multiple_of(t * rows + at, step), step)
        grad = nacc[in_group, :] + inx[0, here, :].astype(f32)
        unit, inverse = norm(mixed[here, :])
        back = cot[here, :] + norm_grad(grad, unit, inverse, vecs[2:3, :])
        input_grad[here, :] = back
        grad_attn[in_group, :] = back.astype(bf)
        row_sum(2, grad * unit)
        row_sum(3, grad)
        row_sum(4, back)
        row_sum(5, cot[here, :])
    by_rows(second_back)
    early_rows(0)
    x_out_core(1 - c).wait_recv()
    ctx_x[...] = dot_nt(grad_attn[own, :], w_out(go_x)).astype(bf)
    x_grad_context().start()
    gctx[own, :] = dot_nt(grad_attn[own, :], w_out(go)).astype(bf)
    each((I, W), ry_add, 1)
    v_merge(2)
    each((I, W), ry_add, 2)
    for zz in range(DEPTH):
        for yy in range(2):
            drain(O, zz, yy)
            drain(Q, zz, yy)
    def mixed_out(at, step):
        here = pl.ds(at, step)
        in_group = pl.ds(pl.multiple_of(t * rows + at, step), step)
        mixed[here, :] = mixed[here, :] + macc[in_group, :] + inx[1, here, :].astype(f32) + vecs[5:6, :]
    x_out().wait_send()
    x_grad_context_wait()
    far[1] = macc[other, :].astype(bf)
    x_rows(grad_attn, 3).start()
    def out_grads():
        x_rows_wait(grad_attn, 3)
        ctx_t = ctx[...].T
        for nb in range(4):
            at = slice(nb * 256, nb * 256 + 256)
            go[:, :, at] = dot(ctx_t, grad_attn[:, at]).astype(bf).reshape(8, 64, 256)
        for zz in range(DEPTH):
            for yy in range(2):
                rc_copy(O, zz, yy).start()
    def first_back(at, step):
        here = pl.ds(at, step)
        in_group = pl.ds(pl.multiple_of(t * rows + at, step), step)
        grad = nacc[in_group, :] + inx[0, here, :].astype(f32)
        unit, inverse = norm(tokens[here, :])
        input_grad[here, :] = input_grad[here, :] + norm_grad(grad, unit, inverse, vecs[0:1, :])
        row_sum(0, grad * unit)
        row_sum(1, grad)
    def finish_mixed():
        x_part(2).wait_recv()
        by_rows(mixed_out)
        stores[4].start()
    def finish_input():
        x_part(3).wait_recv()
        by_rows(first_back)
        stores[5].start()
    late_rows = (0, 1, 6, 7)
    v_cross()
    def late_start():
        for h in range(DEPTH):
            for row in range(2):
                total = jnp.where(t == row, qv_sum[h], 0.0)
                vout[0, 6 + row : 7 + row, h * 256 : h * 256 + 128] = total[:, 0:128]
                vout[0, 6 + row : 7 + row, h * 256 + 128 : h * 256 + 256] = total[:, 256:384]
        for at, row in enumerate(late_rows):
            for j in range(8):
                late[at * 8 + j : at * 8 + j + 1, :] = vout[0, row : row + 1, j * LANES : (j + 1) * LANES]
        late_in[t * 4 + y * 2 + c] = late[...]
        for turn in range(1, 8):
            late_copy(turn).start()
    def late_cross():
        for turn in range(1, 8):
            late_wait(late_turn(turn)[1])
        total = late_in[0]
        for index in range(1, 8):
            total = total + late_in[index]
        late_sum[...] = total
        late_in[8 + z] = total
        for step in range(1, DEPTH):
            late_z(step).start()
    def vec_finish():
        for step in range(1, DEPTH):
            zz = lax.rem(z + step, DEPTH)
            late_wait(8 + zz)
            remote(vin.at[3 + zz], vin.at[3 + zz], v_send.at[0], v_recv.at[3 + zz], y_peer).wait_recv()
        total = ((late_in[8] + late_in[9]) + late_in[10]) + late_in[11]
        early = ((vin[3] + vin[4]) + vin[5]) + vin[6]
        vec_grads[...] = early[0 : vec_grads.shape[0]]
        for at, row in enumerate(late_rows):
            for j in range(8):
                vec_grads[row : row + 1, j * LANES : (j + 1) * LANES] = total[at * 8 + j : at * 8 + j + 1, :]
    def head_back(h, turn):
        q0, q1 = qkv[h, 0:rows, 0:128], qkv[h, rows : 2 * rows, 0:128]
        grads = []
        for block in range(2):
            at, seen = slice(block * rows, (block + 1) * rows), (block + 1) * rows
            low = probs[h, at, 0:seen]
            given = gctx[at, lanes(h * HD, HD, HD)]
            prob = low.astype(f32)
            grad_probs = dot_nt(given, qkv[h, 0:seen, 256:384])
            delta = jnp.sum(prob * grad_probs, -1, keepdims=True)
            grad_scores = (prob * (grad_probs - delta)).astype(bf)
            grad_q = dot(grad_scores, qkv[h, 0:seen, 128:256]) * scale
            grad_k = dot_tn(grad_scores, q1 if block else q0) * scale
            grad_v = dot_tn(low, given)
            grads.append((grad_q, grad_k, grad_v))
        (gq0, gk0, gv0), (gq1, gk1, gv1) = grads
        top = jnp.concatenate([gq0, gk0 + gk1[0:rows], gv0 + gv1[0:rows]], 1).astype(bf)
        low_half = jnp.concatenate([gq1, gk1[rows:], gv1[rows:]], 1).astype(bf)
        qkv[h, 0:rows, :] = top
        qkv[h, rows : 2 * rows, :] = low_half
        total = jnp.sum(top.astype(f32), 0, keepdims=True) + jnp.sum(low_half.astype(f32), 0, keepdims=True)
        qv_sum[h] = total
        for half in (other, own):
            product = dot_nt(qkv[h, half, :], wqkv[h])
            if turn == 0:
                nacc[half, :] = product
            else:
                nacc[half, :] += product
            if turn == DEPTH - 1 and half is other:
                x_part(1).wait_send()
                far[0] = nacc[other, :].astype(bf)
                x_part(3).start()
        part = dot(rows_t[...], qkv[h]).astype(bf)
        disassemble(h, part)
        for yy in (1 - y, y):
            rc_copy(Q, h, yy).start()
    early_rows(1)
    head_back(near(3), 0)
    early_rows(2)
    head_back(near(2), 1)
    early_rows(3)
    x_part(2).start()
    reduce_head(near(3))
    each((I, W), ry_add, 3)
    each((I, W), ry_merge, 1)
    out_grads()
    reduce_head(near(2))
    head_back(near(1), 2)
    reduce_out()
    each((I, W), ry_merge, 2)
    head_back(z, 3)
    ry_add(Q, 3)
    finish_mixed()
    reduce_head(near(1))
    ry_add(Q, 2)
    ry_add(O, 3)
    ry_add(Q, 1)
    ry_add(O, 2)
    ry_merge(Q, 2)
    reduce_head(z)
    ry_merge(Q, 1)
    ry_add(O, 1)
    own_total(W)
    finish_input()
    late_start()
    ry_merge(O, 2)
    late_cross()
    z_total(V, y, total_of(V), y_landed(V, z))
    ry_merge(O, 1)
    own_total(Q)
    stores[Q].start()
    own_total(I)
    stores[I].start()
    vec_finish()
    own_total(O)
    stores[O].start()

    stores[W].start()
    for stage in range(3):
        v_copy(stage).wait_send()
    for turn in range(1, 8):
        late_copy(turn).wait_send()
    for step in range(1, DEPTH):
        vz_copy(step).wait_send()
        late_z(step).wait_send()
    for index, ref in enumerate((rows_one, grad_rows, rows_two, grad_attn)):
        x_rows(ref, index).wait_send()
    for index in (2, 3):
        x_part(index).wait_send()
    x_out_core(c).wait_send()
    x_grad_context().wait_send()
    for k in range(4):
        for zz in range(DEPTH):
            for yy in range(2):
                rc_copy(k, zz, yy).wait_send()
            ry_copy(k, zz).wait_send()
        for s in range(1, DEPTH):
            rz_copy(k, s, y, True).wait_send()
    for store in stores:
        store.wait()
    ry_copy(V, z).wait_send()
    for yy in range(2):
        for s in range(1, DEPTH):
            rz_copy(V, s, yy, True).wait_send()


def run_layer(tokens, cotangent, lengths, order, weights, vec_params):
    bf, f32 = jnp.bfloat16, jnp.float32
    rows = tokens.shape[0]
    group = 2 * rows
    owners = 16
    shapes = piece_shapes()
    view = jnp.transpose(weights, (1, 2, 0))
    there = pl.BlockSpec(memory_space=pl.ANY)
    vmem = pl.BlockSpec(memory_space=pltpu.VMEM)
    smem = pl.BlockSpec(memory_space=pltpu.SMEM)

    halved = shapes[:3] + ((HALF, D),)

    def many(count, kinds):
        return [pltpu.VMEM((count,) + s, bf) for s in kinds]

    full = pltpu.VMEM((group, D), bf)
    dma = pltpu.SemaphoreType.DMA
    return pl.pallas_call(
        layer_kernel,
        out_shape=[jax.ShapeDtypeStruct((rows, D), f32)] * 2
        + [jax.ShapeDtypeStruct(s, f32) for s in shapes]
        + [jax.ShapeDtypeStruct(vec_params.shape, f32)],
        in_specs=[smem, smem] + [there] * 3 + [vmem],
        out_specs=[there] * 6 + [vmem],
        scratch_shapes=[pltpu.VMEM((rows, D), f32)] * 4
        + [pltpu.VMEM(s, f32) for s in shapes]
        + [
            pltpu.VMEM((owners,) + shapes[0], bf),
            pltpu.VMEM((owners // 2, BLOCK, D), bf),
            pltpu.VMEM((owners,) + shapes[2], bf),
            pltpu.VMEM((owners,) + shapes[3], bf),
            pltpu.VMEM((DEPTH, D, 3 * HD), bf),
        ]
        + many(2 * DEPTH, shapes)
        + many(DEPTH, halved)
        + many(1, halved[3:])
        + many(DEPTH, halved)
        + many(2 * DEPTH, halved[3:])
        + [
            full,
            full,
            pltpu.VMEM((D, group), bf),
            full,
            full,
            pltpu.VMEM((DEPTH, group, group), bf),
            pltpu.VMEM((DEPTH, group, 3 * HD), bf),
            pltpu.VMEM((group, DEPTH * HD), bf),
            pltpu.VMEM((group, DEPTH * HD), bf),
            pltpu.VMEM((2, rows, D), bf),
            pltpu.VMEM((2, rows, D), bf),
            pltpu.VMEM((owners // 2, BLOCK, D), bf),
            pltpu.VMEM((rows, DEPTH * HD), bf),
            pltpu.VMEM((group, D), f32),
            pltpu.VMEM((group, D), f32),
            pltpu.VMEM((group, 2 * D), bf),
            pltpu.VMEM((group, 2 * D), bf),
            pltpu.VMEM((DEPTH, 1, 512), f32),
            pltpu.VMEM((DEPTH, 1, 3 * HD), f32),
            pltpu.VMEM((DEPTH, 1, 3 * HD), f32),
            pltpu.VMEM((7, 16, D), f32),
            pltpu.VMEM((5, 16, D), f32),
            pltpu.VMEM((32, LANES), f32),
            pltpu.VMEM((32, LANES), f32),
            pltpu.VMEM((12, 32, LANES), f32),
            dma((5, owners)),
            dma((5, DEPTH)),
            dma((5, 2 * DEPTH)),
            dma((5, 2, 2 * DEPTH)),
            dma((4, 2 * DEPTH)),
            dma((4, 2 * DEPTH)),
            dma((5, DEPTH)),
            dma((5, DEPTH)),
            dma((5, 2 * DEPTH)),
            dma((5, 2 * DEPTH)),
            dma((11,)),
            dma((11,)),
            dma((6,)),
            dma((7,)),
            dma((11,)),
            dma((12,)),
            dma((12,)),
        ],
        compiler_params=pltpu.CompilerParams(
            collective_id=0, has_side_effects=True, vmem_limit_bytes=VMEM_LIMIT
        ),
        name="layer",
    )(lengths, order, view, tokens, cotangent, vec_params)


def per_device(
    grp_count,
    tp_count,
    tokens,
    cotangent,
    lengths,
    order,
    weights,
    momentum,
    stat_left,
    stat_right,
    root_left,
    root_right,
    vec_params,
    vec_momentum,
    vec_second,
):
    fits = grp_count == 4 * DEPTH and tp_count == 2 and tokens.shape[0] == 256
    if not fits or lengths.shape[1] != ARTICLES:
        return per_device_general(
            tokens,
            cotangent,
            lengths,
            order,
            weights,
            momentum,
            stat_left,
            stat_right,
            root_left,
            root_right,
            vec_params,
            vec_momentum,
            vec_second,
        )
    token_total = tokens.shape[0] * tp_count * grp_count
    mixed, input_grad, *sums, vec_grads = run_layer(tokens, cotangent, lengths, order, weights, vec_params)
    blocks, vecs, results = update_blocks(
        sums,
        (weights, momentum, stat_left, stat_right, root_left, root_right),
        vec_grads,
        (vec_params, vec_momentum, vec_second),
        (mixed, input_grad),
        token_total,
    )
    return (*results, *blocks, *vecs)


def solution(mesh):
    placed = (
        P(("grp", "tp"), None),
        P(("grp", "tp"), None),
        P("grp", None),
        P("grp", None),
        P(("tp", "grp"), None, None),
        P(("tp", "grp"), None, None),
        P(("tp", "grp"), None, None),
        P(("tp", "grp"), None, None),
        P(("tp", "grp"), None, None),
        P(("tp", "grp"), None, None),
        P(),
        P(),
        P(),
    )
    return jax.shard_map(
        functools.partial(per_device, mesh.shape["grp"], mesh.shape["tp"]),
        mesh=mesh,
        in_specs=placed,
        out_specs=(
            P(("grp", "tp"), None),
            P(("grp", "tp"), None),
            P(("tp", "grp"), None, None),
            P(("tp", "grp"), None, None),
            P(("tp", "grp"), None, None),
            P(("tp", "grp"), None, None),
            P(("tp", "grp"), None, None),
            P(),
            P(),
            P(),
            P(),
        ),
        check_vma=False,
    )
```
